32 devices in a mesh: pipe: 2 (over y), dp: 16 (over z, x, core).
Axes of the slice: x: 2, y: 2, z: 4, core: 2. Of those that a mesh axis runs over, the one named last changes fastest.
Arguments:
- history_codes: int32 [1024, 80], P('dp'), may hold values from 0 to 255
- user_ids: int32 [1024], P('dp'), may hold values from 0 to 1999
- targets: int32 [1024, 4], P('dp'), may hold values from 0 to 255
- domains: int32 [1024], P('dp'), may hold values from 0 to 2
- mixer: float32 [2, 128, 2304], P('pipe'), may hold values from -0.5 to 0.5
- mixer_moment: float32 [2, 128, 2304], P('pipe'), may hold values from -0.00024414062 to 0.00024414062
- mixer_square: float32 [2, 128, 2304], P('pipe'), may hold values from 1.6639334e-10 to 6.655734e-10
- feed: float32 [2, 128, 2048], P('pipe'), may hold values from -0.5 to 0.5
- feed_moment: float32 [2, 128, 2048], P('pipe'), may hold values from -0.00024414062 to 0.00024414062
- feed_square: float32 [2, 128, 2048], P('pipe'), may hold values from 1.6639334e-10 to 6.655734e-10
- embedding: float32 [3024, 128], replicated, may hold values from -0.6 to 0.6
- embedding_moment: float32 [3024, 128], replicated, may hold values from -0.00024414062 to 0.00024414062
- embedding_square: float32 [3024, 128], replicated, may hold values from 1.6639334e-10 to 6.655734e-10
- gains: float32 [7, 128], replicated, may hold values from 0.5 to 1.5
- gains_moment: float32 [7, 128], replicated, may hold values from -0.0014648438 to 0.0014648438
- gains_square: float32 [7, 128], replicated, may hold values from 4.1598334e-09 to 1.6639333e-08
- position_bias: float32 [2, 32, 6], replicated, may hold values from -3 to 3
- bias_moment: float32 [2, 32, 6], replicated, may hold values from -0.00024414062 to 0.00024414062
- bias_square: float32 [2, 32, 6], replicated, may hold values from 1.3311467e-10 to 5.324587e-10
Outputs:
- loss: float32 [], replicated
- gradient_norm: float32 [], replicated
- section_norms: float32 [2], replicated
- histograms: float32 [4, 256], replicated
- new_mixer: float32 [2, 128, 2304], P('pipe')
- new_mixer_moment: float32 [2, 128, 2304], P('pipe')
- new_mixer_square: float32 [2, 128, 2304], P('pipe')
- new_feed: float32 [2, 128, 2048], P('pipe')
- new_feed_moment: float32 [2, 128, 2048], P('pipe')
- new_feed_square: float32 [2, 128, 2048], P('pipe')
- new_embedding: float32 [3024, 128], replicated
- new_embedding_moment: float32 [3024, 128], replicated
- new_embedding_square: float32 [3024, 128], replicated
- new_gains: float32 [7, 128], replicated
- new_gains_moment: float32 [7, 128], replicated
- new_gains_square: float32 [7, 128], replicated
- new_bias: float32 [2, 32, 6], replicated
- new_bias_moment: float32 [2, 32, 6], replicated
- new_bias_square: float32 [2, 32, 6], replicated
- mixer_copy: bfloat16 [2, 128, 2304], P('pipe')
- feed_copy: bfloat16 [2, 128, 2048], P('pipe')
- embedding_copy: bfloat16 [3024, 128], replicated
The draws below stay inside these ranges and needn't reach their ends.
All inputs are finite; a program needn't handle non-finite values.
Results may differ from the reference program's by a relative error of at most 0.03.
Values may be sent and summed in bfloat16 or wider, within the bound.
A program may use at most 384 MiB of HBM per device.

```python
import math
import jax
import jax.numpy as jnp
import numpy as np
from jax import lax

D = 128
HEADS = 6
HEAD_DIM = 64
FF = 1024
CODEBOOK = 256
USERS = 2000
LEVELS = 4
BUCKETS = 32
DOMAINS = 3
HIST_LEN = 81
STEP = 5
MIXW = 2304
CODES = 1024
VOCAB = 3024
HIST_DEV = 64
HISTORIES = 1024
PARAMS = 1502464


def draw_domains(key, part):
    places = jnp.arange(HISTORIES)
    share = 20 + 40 * places // HISTORIES
    roll = jax.random.randint(key, (HISTORIES,), 0, 100)
    return jnp.where(roll < share, 0, jnp.where(roll < 80, 1, 2)).astype(jnp.int32)


def place_ends(entries, key, least, top_value):
    longest = entries.shape.index(max(entries.shape))
    spots = []
    for shift in (0, 1):
        where = [jax.random.randint(jax.random.fold_in(key, axis), (), 0, length) for axis, length in enumerate(entries.shape)]
        where[longest] = (where[longest] + shift) % entries.shape[longest]
        spots.append(tuple(where))
    return entries.at[spots[0]].set(least).at[spots[1]].set(top_value)


def level_of(own_key, extent, pieces, low, high):
    loudness, own = 1.0, jax.random.fold_in(own_key, 6)
    for dim, parts in pieces:
        draws = jnp.exp(jax.random.uniform(jax.random.fold_in(own, dim), (parts,), jnp.float32, low / len(pieces), high / len(pieces)))
        loudness = loudness * jnp.repeat(draws, extent[dim] // parts).reshape([-1 if axis == dim else 1 for axis in range(len(extent))])
    return loudness


def rank_table(count, skew):
    portions = [(1 << 20) // math.isqrt(rank ** skew) + 1 for rank in range(1, count + 1)]
    scale = 1 + sum(portions) // (1 << 30)
    return np.cumsum(np.array([max(1, weight // scale) for weight in portions]))


def ranked_ids(stream_key, extent, count, lean):
    table = rank_table(count, lean)
    lot = jax.random.randint(jax.random.fold_in(stream_key, 1), extent, 0, int(table[count - 1]))
    rank = jnp.searchsorted(jnp.asarray(table, jnp.int32), lot, side="right")
    return jax.random.permutation(jax.random.fold_in(stream_key, 2), count)[rank].astype(jnp.int32)


def bell_draw(own_key, dims, scale, limit, pieces=(), dtype=jnp.bfloat16):
    values = jax.random.normal(own_key, dims, jnp.float32) * scale
    if len(pieces) > 0:
        values = level_of(own_key, dims, pieces, -0.22, 0.18) * values
    return jnp.clip(values, min=-limit, max=limit).astype(dtype)


def setup_inputs(seed: int = 0) -> dict:
    key_of = jax.random.split(jax.random.key(seed), 20)
    return {
        "history_codes": place_ends(ranked_ids(key_of[0], (HISTORIES, HIST_LEN - 1), CODEBOOK, 2), jax.random.fold_in(key_of[0], 3), 0, CODEBOOK - 1).astype(jnp.int32),
        "user_ids": place_ends(jax.random.randint(key_of[1], (HISTORIES,), 0, USERS), jax.random.fold_in(key_of[1], 1), 0, USERS - 1).astype(jnp.int32),
        "targets": place_ends(ranked_ids(key_of[2], (HISTORIES, LEVELS), CODEBOOK, 1), jax.random.fold_in(key_of[2], 3), 0, CODEBOOK - 1).astype(jnp.int32),
        "domains": draw_domains(jax.random.fold_in(key_of[19], 71), 0),
        "mixer": bell_draw(key_of[4], (2, D, MIXW), D ** -0.5, 0.5, ((0, 2),), jnp.float32),
        "mixer_moment": bell_draw(key_of[5], (2, D, MIXW), (0.0555 / PARAMS ** 0.5), 0.00024414062, ((0, 2),), jnp.float32),
        "mixer_square": jnp.clip(jnp.exp(math.log(6.655733741922631e-10) - 1.3862944 * jax.random.uniform(key_of[6], (2, D, MIXW), jnp.float32) ** level_of(key_of[6], (2, D, MIXW), ((0, 2),), -0.2, 0.2)), 1.6639334354806579e-10, 6.655733741922631e-10),
        "feed": bell_draw(key_of[7], (2, D, 2 * FF), D ** -0.5, 0.5, ((0, 2),), jnp.float32),
        "feed_moment": bell_draw(key_of[8], (2, D, 2 * FF), (0.0555 / PARAMS ** 0.5), 0.00024414062, ((0, 2),), jnp.float32),
        "feed_square": jnp.clip(jnp.exp(math.log(6.655733741922631e-10) - 1.3862944 * jax.random.uniform(key_of[9], (2, D, 2 * FF), jnp.float32) ** level_of(key_of[9], (2, D, 2 * FF), ((0, 2),), -0.2, 0.2)), 1.6639334354806579e-10, 6.655733741922631e-10),
        "embedding": bell_draw(key_of[10], (VOCAB, D), 0.1, 0.6, (), jnp.float32),
        "embedding_moment": bell_draw(key_of[11], (VOCAB, D), (0.0555 / PARAMS ** 0.5), 0.00024414062, (), jnp.float32),
        "embedding_square": jnp.clip(jnp.exp(jax.random.uniform(key_of[12], (VOCAB, D), jnp.float32, math.log(1.6639334354806579e-10), math.log(6.655733741922631e-10))), 1.6639334354806579e-10, 6.655733741922631e-10),
        "gains": jnp.clip(1.0 + 0.1 * jax.random.normal(key_of[13], (7, D), jnp.float32), 0.5, 1.5),
        "gains_moment": bell_draw(key_of[14], (7, D), (0.2775 / PARAMS ** 0.5), 0.0014648438, (), jnp.float32),
        "gains_square": jnp.clip(jnp.exp(jax.random.uniform(key_of[15], (7, D), jnp.float32, math.log(4.15983336665704e-09), math.log(1.663933346662816e-08))), 4.15983336665704e-09, 1.663933346662816e-08),
        "position_bias": bell_draw(key_of[16], (2, BUCKETS, HEADS), 0.5, 3.0, (), jnp.float32),
        "bias_moment": bell_draw(key_of[17], (2, BUCKETS, HEADS), (0.05 / PARAMS ** 0.5), 0.00024414062, (), jnp.float32),
        "bias_square": jnp.clip(jnp.exp(jax.random.uniform(key_of[18], (2, BUCKETS, HEADS), jnp.float32, math.log(1.3311467206289507e-10), math.log(5.324586882515803e-10))), 1.3311467206289507e-10, 5.324586882515803e-10),
    }


@jax.custom_vjp
def low(v):
    return lax.optimization_barrier(v.astype(jnp.bfloat16)).astype(jnp.float32)

@jax.custom_vjp
def low_back(v):
    return v

def low_keep(v):
    return (low(v), None)

def low_pass(kept, grad):
    return (grad,)

def back_keep(v):
    return (v, None)

def back_low(kept, grad):
    return (low(grad),)
low.defvjp(low_keep, low_pass)
low_back.defvjp(back_keep, back_low)
highest = lax.Precision.HIGHEST
norm_eps = 1e-06
beta_one = 0.9
beta_two = 0.999
adam_eps = 1e-08
clip_norm = 0.5
rate_matrix = 0.04
rate_gain = 0.8
rate_small = 0.3
decay_matrix = 0.01

def rms(rows, gain):
    return rows * lax.rsqrt(lax.optimization_barrier(jnp.mean(rows * rows, -1, keepdims=True)) + norm_eps) * gain

def encoder_buckets():
    places = jnp.arange(HIST_LEN)
    offset = places[None, :] - places[:, None]
    distance = jnp.abs(offset)
    remote = jnp.zeros_like(distance)
    for edge in (12, 16, 23, 32, 46, 64, 91):
        remote = remote + (distance >= edge).astype(jnp.int32)
    nearby = jnp.minimum(jnp.where(distance < 8, distance, 8 + remote), 15)
    return (nearby + 16 * (offset > 0).astype(jnp.int32)).astype(jnp.int32)

def history_ids(codes, users):
    level = jnp.arange(codes.shape[1]) % LEVELS
    return jnp.concatenate([CODES + users[:, None], level[None, :] * CODEBOOK + codes], 1).reshape(-1).astype(jnp.int32)

def split_heads(table, count):
    return table.reshape(count, -1, HEADS, HEAD_DIM)

def attend(query, keys, values, bias, mask):
    scores = HEAD_DIM ** (-0.5) * jnp.einsum('nqhd,nkhd->nhqk', query, keys, precision=highest) + bias
    scores = low_back(scores)
    if mask is not None:
        scores = jnp.where(mask, scores, -1e+30)
    chance = low(jax.nn.softmax(scores, -1))
    return low_back(jnp.einsum('nhqk,nkhd->nqhd', chance, values, precision=highest))

def attention_layer(rows, gain, w_in, w_out, bias, mask, count, memory):
    normed = low(rms(rows, gain))
    projected = low(low_back(jnp.dot(normed, w_in, precision=highest)))
    width = w_out.shape[1]
    query = split_heads(projected[:, :width], count)
    if memory is None:
        keys = split_heads(projected[:, width:2 * width], count)
        values = split_heads(projected[:, 2 * width:], count)
    else:
        keys = split_heads(memory[:, :width], count)
        values = split_heads(memory[:, width:], count)
    mixed = low(attend(query, keys, values, bias, mask).reshape(rows.shape[0], width))
    return rows + low_back(jnp.dot(mixed, w_out.T, precision=highest))

def feed_layer(rows, gain, w_up, w_down):
    normed = low(rms(rows, gain))
    lifted = low_back(jnp.dot(normed, w_up, precision=highest))
    active = low(jnp.maximum(lifted, 0.0))
    return rows + low_back(jnp.dot(active, w_down.T, precision=highest))

def block_loss(embed_w, gain_w, mix_low, feed_low, table, enc_bias, dec_bias, codes, users, goal, weight):
    count = codes.shape[0]
    width = HEADS * HEAD_DIM
    rows = embed_w[history_ids(codes, users)]
    rows = attention_layer(rows, gain_w[0], mix_low[0][:, :3 * width], mix_low[0][:, 3 * width:4 * width], enc_bias, None, count, None)
    rows = feed_layer(rows, gain_w[1], feed_low[0][:, :FF], feed_low[0][:, FF:])
    final = low(rms(rows, gain_w[2]))
    memory = low(low_back(jnp.dot(final, mix_low[0][:, 4 * width:], precision=highest)))
    start_ids = jnp.concatenate([jnp.zeros((count, 1), jnp.int32), goal[:, :-1]], 1).reshape(-1)
    places = jnp.arange(LEVELS)
    causal = places[:, None] >= places[None, :]
    decoded = embed_w[start_ids]
    decoded = attention_layer(decoded, gain_w[3], mix_low[1][:, :3 * width], mix_low[1][:, 3 * width:4 * width], dec_bias, causal, count, None)
    decoded = attention_layer(decoded, gain_w[4], mix_low[1][:, 4 * width:5 * width], mix_low[1][:, 5 * width:], 0.0, None, count, memory)
    decoded = feed_layer(decoded, gain_w[5], feed_low[1][:, :FF], feed_low[1][:, FF:])
    final_dec = low(rms(decoded, gain_w[6]))
    logits = low_back(jnp.dot(final_dec, table.T, precision=highest))
    log_total = jax.nn.logsumexp(logits, -1)
    match = goal.reshape(-1)[:, None] == jnp.arange(CODES)[None, :]
    picked = lax.optimization_barrier(jnp.sum(jnp.where(match, logits, 0.0), -1))
    return jnp.sum(weight.reshape(-1) * (log_total - picked))

def adam_step(weight, moment, square, slope, rate, decay):
    moment = beta_one * moment + (1 - beta_one) * slope
    square = beta_two * square + (1 - beta_two) * slope * slope
    unbiased_moment = moment / (1 - beta_one ** STEP)
    unbiased_square = square / (1 - beta_two ** STEP)
    return (weight - rate * (unbiased_moment / (jnp.sqrt(unbiased_square) + adam_eps) + decay * weight), moment, square)

def reference(history_codes, user_ids, targets, domains, mixer, mixer_moment, mixer_square, feed, feed_moment, feed_square, embedding, embedding_moment, embedding_square, gains, gains_moment, gains_square, position_bias, bias_moment, bias_square):
    hits = (domains[:, None] == jnp.arange(DOMAINS)[None, :]).astype(jnp.float32)
    counts = LEVELS * lax.optimization_barrier(jnp.sum(hits, 0))
    share = 1.0 / (DOMAINS * jnp.maximum(counts, 1.0))
    token_weight = jnp.broadcast_to(share[domains][:, None], (HISTORIES, LEVELS))
    histograms = lax.optimization_barrier(jnp.sum((targets[:, :, None] == jnp.arange(CODEBOOK)[None, None, :]).astype(jnp.float32), 0))
    goal = (jnp.arange(LEVELS)[None, :] * CODEBOOK + targets).astype(jnp.int32)
    blocks = HISTORIES // HIST_DEV
    inputs = (history_codes.reshape(blocks, HIST_DEV, HIST_LEN - 1), user_ids.reshape(blocks, HIST_DEV), goal.reshape(blocks, HIST_DEV, LEVELS), token_weight.reshape(blocks, HIST_DEV, LEVELS))
    places = jnp.arange(LEVELS)
    spacing = jnp.maximum(places[:, None] - places[None, :], 0)

    def total_loss(embed_w, gain_w, bias_w, mixer_w, feed_w):
        mix_low = low(mixer_w)
        feed_low = low(feed_w)
        table = low(embed_w[:CODES])
        enc_bias = jnp.transpose(bias_w[0][encoder_buckets()], (2, 0, 1))
        dec_bias = jnp.transpose(bias_w[1][spacing], (2, 0, 1))
        checked = jax.checkpoint(block_loss)

        def step(total, block):
            return (total + checked(embed_w, gain_w, mix_low, feed_low, table, enc_bias, dec_bias, *block), None)
        total, unused = lax.scan(step, jnp.zeros((), jnp.float32), inputs)
        return total
    loss, pull = jax.vjp(total_loss, embedding, gains, position_bias, mixer, feed)
    slopes = pull(jnp.ones((), jnp.float32))
    section_squares = lax.optimization_barrier(jnp.sum(slopes[3] * slopes[3], (1, 2))) + lax.optimization_barrier(jnp.sum(slopes[4] * slopes[4], (1, 2)))
    section_norms = jnp.sqrt(section_squares)
    small_squares = jnp.sum(slopes[0] * slopes[0]) + jnp.sum(slopes[1] * slopes[1]) + jnp.sum(slopes[2] * slopes[2])
    gradient_norm = jnp.sqrt(jnp.sum(section_squares) + small_squares)
    factor = jnp.minimum(1.0, clip_norm / (gradient_norm + 1e-06))
    embed_slope, gain_slope, bias_slope, mixer_slope, feed_slope = [factor * slope for slope in slopes]
    new_mixer, new_mixer_moment, new_mixer_square = adam_step(mixer, mixer_moment, mixer_square, mixer_slope, rate_matrix, decay_matrix)
    new_feed, new_feed_moment, new_feed_square = adam_step(feed, feed_moment, feed_square, feed_slope, rate_matrix, decay_matrix)
    new_embedding, new_embedding_moment, new_embedding_square = adam_step(embedding, embedding_moment, embedding_square, embed_slope, rate_matrix, decay_matrix)
    new_gains, new_gains_moment, new_gains_square = adam_step(gains, gains_moment, gains_square, gain_slope, rate_gain, 0.0)
    new_bias, new_bias_moment, new_bias_square = adam_step(position_bias, bias_moment, bias_square, bias_slope, rate_small, 0.0)
    return (loss, gradient_norm, section_norms, histograms, new_mixer, new_mixer_moment, new_mixer_square, new_feed, new_feed_moment, new_feed_square, new_embedding, new_embedding_moment, new_embedding_square, new_gains, new_gains_moment, new_gains_square, new_bias, new_bias_moment, new_bias_square, new_mixer.astype(jnp.bfloat16), new_feed.astype(jnp.bfloat16), new_embedding.astype(jnp.bfloat16))
```

```python
import functools

import jax
import jax.numpy as jnp
from jax import lax
from jax.experimental import pallas as pl
from jax.experimental.pallas import tpu as pltpu
from jax.sharding import PartitionSpec as P

D = 128
HEADS = 6
HEAD_DIM = 64
FF = 1024
CODEBOOK = 256
LEVELS = 4
BUCKETS = 32
DOMAINS = 3
HIST_LEN = 81
STEP = 5
CODES = 1024
LANES = 128
WIDTH = HEADS * HEAD_DIM
MIXW = 6 * WIDTH
COLS = MIXW + 2 * FF
BLOCKS = COLS // LANES
KEYS = 96
PAIRS = HEADS // 2
ROWS = 32

norm_eps = 1e-06
beta_one = 0.9
beta_two = 0.999
adam_eps = 1e-08
clip_norm = 0.5
rate_matrix = 0.04
rate_gain = 0.8
rate_small = 0.3
decay_matrix = 0.01

f32 = jnp.float32
bf16 = jnp.bfloat16


def iota(shape, axis):
    return lax.broadcasted_iota(jnp.int32, shape, axis)


def mul(left, right):
    return jnp.dot(left, right, preferred_element_type=f32)


def mul_t(left, right):
    return lax.dot_general(left, right, (((1,), (1,)), ((), ())), preferred_element_type=f32)


def mul_exact(left, right):
    return jnp.dot(left, right, preferred_element_type=f32, precision=lax.Precision.HIGHEST)


def onehot(ids, rows):
    return jnp.where(iota((rows, ids.shape[1]), 0) == ids, 1.0, 0.0).astype(bf16)


def inverse_rms(x):
    return lax.rsqrt(jnp.mean(x * x, axis=0, keepdims=True) + norm_eps)


def norm_low(x, inverse, gain):
    return (x * inverse * gain).astype(bf16)


def norm_back(x, inverse, gain, upstream):
    scaled = x * inverse
    inner = upstream * gain
    back = inverse * (inner - scaled * jnp.mean(inner * scaled, axis=0, keepdims=True))
    return back, upstream * scaled


def block_diag(pair):
    zero = jnp.zeros((HEAD_DIM, LANES), pair.dtype)
    left = jnp.concatenate([pair[:HEAD_DIM], zero], 0)
    right = jnp.concatenate([zero, pair[HEAD_DIM:]], 0)
    return jnp.concatenate([left, right], 1)


def diagonal(both):
    return jnp.concatenate([both[:HEAD_DIM, :LANES], both[HEAD_DIM:, LANES:]], 0)


def pad_keys(table):
    if table.shape[0] == LANES:
        return table
    zero = jnp.zeros((LANES - table.shape[0], table.shape[1]), table.dtype)
    return jnp.concatenate([table, zero], 0)


def attend(keys, query, values, bias):
    scores = mul(keys, block_diag(query)) + bias
    top = jnp.max(scores, axis=0, keepdims=True)
    chance = jnp.exp(scores - top)
    total = jnp.sum(chance, axis=0, keepdims=True)
    chance = (chance * (1.0 / total)).astype(bf16)
    mixed = diagonal(mul(values, pad_keys(chance))).astype(bf16)
    return chance, mixed


def attend_back(keys_t, query, values, back_mixed, chance):
    exact = chance.astype(f32)
    spread = block_diag(back_mixed)
    back_chance = mul(values, spread)
    inner = jnp.sum(back_chance * exact, axis=0, keepdims=True)
    back_scores = exact * (back_chance - inner)
    low = pad_keys(back_scores.astype(bf16))
    back_query = diagonal(mul(keys_t, low)).astype(bf16)
    back_keys = mul_t(block_diag(query), low).astype(bf16)
    back_values = mul_t(spread, pad_keys(chance)).astype(bf16)
    return back_query, back_keys, back_values, back_scores


def add_blocks(ref, first, value):
    for block in range(value.shape[1] // LANES):
        ref[first + block] += value[:, block * LANES : (block + 1) * LANES]


def put_blocks(ref, first, value):
    for block in range(value.shape[1] // LANES):
        rows = slice((first + block) * D, (first + block + 1) * D)
        ref[1, rows, :] = value[:, block * LANES : (block + 1) * LANES].astype(ref.dtype)


def split_low(x):
    high = x.astype(bf16)
    return jnp.concatenate([high, (x - high.astype(f32)).astype(bf16)], 0)


def compute_kernel(
    n,
    users_ref,
    bias_ref,
    ids_ref,
    start_ref,
    goal_ref,
    domain_ref,
    count_ref,
    gains_ref,
    embed_ref,
    wn_s,
    grad_ref,
    grad_embed_ref,
    grad_user_ref,
    small_ref,
    x0_s,
    x1_s,
    x2_s,
    qkv_s,
    p_s,
    o_s,
    r_s,
    mem_s,
    dz_s,
    wt_s,
    ext_s,
    table_s,
    gain_s,
    ebias_s,
    dbias_s,
    g0_s,
    ge_s,
    gbias_s,
    ggain_s,
    rows_s,
    user_s,
    qbd_s,
    qbdt_s,
    dobd_s,
    dobdt_s,
    pc_s,
    oc_s,
):
    chunks = n // 2
    groups = n // 4
    wide = 2 * LANES
    eye = jnp.where(iota((LANES, LANES), 0) == iota((LANES, LANES), 1), 1.0, 0.0).astype(bf16)

    for section in range(2):
        for block in range(BLOCKS):
            place = slice(block * LANES, (block + 1) * LANES)
            wt_s[section, place, :] = mul_t(eye, wn_s[section, :, place]).astype(bf16)

    def fetch(i, carry):
        user_s[pl.ds(i, 1), :] = embed_ref[pl.ds(CODES + users_ref[i], 1), :]
        return carry

    lax.fori_loop(0, n, fetch, 0)
    for block in range(CODES // LANES + 1):
        if block < CODES // LANES:
            rows = embed_ref[block * LANES : (block + 1) * LANES, :]
            table_s[block * LANES : (block + 1) * LANES, :] = rows.astype(bf16)
            span = LANES
        else:
            rows = user_s[...]
            span = n
        high = rows.astype(bf16)
        rest = (rows - high.astype(f32)).astype(bf16)
        place = slice(block * LANES, block * LANES + span)
        ext_s[:D, place] = mul_t(eye, high).astype(bf16)
        ext_s[D:, place] = mul_t(eye, rest).astype(bf16)

    for g in range(7):
        gain_s[g] = jnp.broadcast_to(gains_ref[g : g + 1, :], (LANES, LANES)).T

    key, query = iota((KEYS, LANES), 0), iota((KEYS, LANES), 1)
    distance = jnp.abs(query - key)
    remote = jnp.zeros_like(distance)
    for edge in (12, 16, 23, 32, 46, 64, 91):
        remote = remote + (distance >= edge).astype(jnp.int32)
    nearby = jnp.minimum(jnp.where(distance < 8, distance, 8 + remote), 15)
    buckets = nearby + jnp.where(key > query, 16, 0)
    for head in range(HEADS):
        lanes = slice((head % 2) * LANES, (head % 2 + 1) * LANES)

        def choose(b, table):
            return jnp.where(buckets == b, bias_ref[b, head], table)

        table = lax.fori_loop(0, BUCKETS, choose, jnp.zeros((KEYS, LANES), f32))
        ebias_s[head // 2, :, lanes] = jnp.where(key < HIST_LEN, table, -1e30)
    key, query = iota((LANES, LANES), 0), iota((LANES, LANES), 1)
    offset = query - key
    seen = ((key >> 2) == (query >> 2)) & (offset >= 0)
    for head in range(HEADS):
        lanes = slice((head % 2) * LANES, (head % 2 + 1) * LANES)
        table = jnp.full((LANES, LANES), -1e30, f32)
        for b in range(LEVELS):
            table = jnp.where(seen & (offset == b), bias_ref[BUCKETS + b, head], table)
        dbias_s[head // 2, :, lanes] = table

    def gain(g, width):
        column = gain_s[g]
        return column if width == LANES else jnp.concatenate([column] * (width // LANES), 1)

    def encode(c, carry):
        hot = onehot(ids_ref[c], CODES + n)
        both = mul(ext_s[...], hot)
        x0 = both[:D] + both[D:]
        x0_s[c] = x0
        h = norm_low(x0, inverse_rms(x0), gain(0, wide))
        for j in range(3):
            qkv_s[c, j * WIDTH : (j + 1) * WIDTH, :] = mul(
                wt_s[0, j * WIDTH : (j + 1) * WIDTH, :], h
            ).astype(bf16)
        for i in range(2):
            lanes = slice(i * LANES, (i + 1) * LANES)
            natural = mul_t(eye, h[:, lanes]).astype(bf16)[:KEYS]
            keys = mul(natural, wn_s[0, :, WIDTH : 2 * WIDTH]).astype(bf16)
            for j in range(PAIRS):
                part = slice(j * LANES, (j + 1) * LANES)
                chance, mixed = attend(
                    keys[:, part],
                    qkv_s[c, part, lanes],
                    qkv_s[c, 2 * WIDTH + j * LANES : 2 * WIDTH + (j + 1) * LANES, lanes],
                    ebias_s[j],
                )
                p_s[2 * c + i, j] = chance
                o_s[c, part, lanes] = mixed
        x1 = x0 + mul(wn_s[0, :, 3 * WIDTH : 4 * WIDTH], o_s[c])
        x1_s[c] = x1
        h = norm_low(x1, inverse_rms(x1), gain(1, wide))
        for j in range(2):
            part = slice(j * FF // 2, (j + 1) * FF // 2)
            lifted = mul(wt_s[0, MIXW + j * FF // 2 : MIXW + (j + 1) * FF // 2, :], h)
            r_s[c, part, :] = jnp.maximum(lifted, 0.0).astype(bf16)
        x2 = x1 + mul(wn_s[0, :, MIXW + FF :], r_s[c])
        x2_s[c] = x2
        e = norm_low(x2, inverse_rms(x2), gain(2, wide))
        for j in range(2):
            part = slice(j * WIDTH, (j + 1) * WIDTH)
            mem_s[c, part, :] = mul(
                wt_s[0, 4 * WIDTH + j * WIDTH : 4 * WIDTH + (j + 1) * WIDTH, :], e
            ).astype(bf16)
        return carry

    lax.fori_loop(0, chunks, encode, 0)

    start = onehot(start_ref[...], CODES)
    both = mul(ext_s[:, :CODES], start)
    y0 = both[:D] + both[D:]
    inverse0 = inverse_rms(y0)
    h0 = norm_low(y0, inverse0, gain(3, LANES))
    dz_s[:, :LANES] = mul(wt_s[1, : 3 * WIDTH, :], h0).astype(bf16)
    both = mul(mul_t(eye, h0).astype(bf16), wn_s[1, :, WIDTH : 3 * WIDTH]).astype(bf16)
    self_chance = []
    mixed_parts = []
    for j in range(PAIRS):
        part = slice(j * LANES, (j + 1) * LANES)
        chance, mixed = attend(
            both[:, part],
            dz_s[part, :LANES],
            dz_s[2 * WIDTH + j * LANES : 2 * WIDTH + (j + 1) * LANES, :LANES],
            dbias_s[j],
        )
        self_chance.append(chance)
        mixed_parts.append(mixed)
    self_values = both[:, WIDTH:]
    self_mixed = jnp.concatenate(mixed_parts, 0)
    y1 = y0 + mul(wn_s[1, :, 3 * WIDTH : 4 * WIDTH], self_mixed)
    inverse1 = inverse_rms(y1)
    h1 = norm_low(y1, inverse1, gain(4, LANES))
    cross_query = mul(wt_s[1, 4 * WIDTH : 5 * WIDTH, :], h1).astype(bf16)

    def spread_rows(table, ref, ref_t):
        for g in range(groups):
            shape = (LANES, LANES)
            row, token = g * LANES + iota(shape, 0), iota(shape, 1)
            rep = jnp.where(token == 4 * (row >> 5) + (row & 3), 1.0, 0.0).astype(bf16)
            rows = mul_t(rep, table)
            mask = (iota(rows.shape, 1) >> 6) == ((iota(rows.shape, 0) & 31) >> 2)
            ref[g] = jnp.where(mask, rows, 0.0).astype(bf16)
            token, row = iota(shape, 0), g * LANES + iota(shape, 1)
            rep = jnp.where(token == 4 * (row >> 5) + (row & 3), 1.0, 0.0).astype(bf16)
            rows = mul(table, rep)
            ref_t[g] = jnp.where(head_mask(rows.shape), rows, 0.0).astype(bf16)

    def head_mask(shape):
        return (iota(shape, 0) >> 6) == ((iota(shape, 1) & 31) >> 2)

    def gather_rows(ref):
        total = jnp.zeros((WIDTH, LANES), f32)
        for g in range(groups):
            row, token = g * LANES + iota((LANES, LANES), 0), iota((LANES, LANES), 1)
            rep = jnp.where(token == 4 * (row >> 5) + (row & 3), 1.0, 0.0).astype(bf16)
            total = total + mul(ref[g], rep)
        return total.astype(bf16)

    def blocks_of(table, half):
        owner = iota(table.shape, 0) >> 5
        zero = jnp.zeros_like(table)
        return jnp.concatenate(
            [
                jnp.where(owner == 2 * half, table, zero),
                jnp.where(owner == 2 * half + 1, table, zero),
            ],
            1,
        )

    spread_rows(cross_query, qbd_s, qbdt_s)

    def cross(g, carry):
        parts = []
        for j in range(4):
            parts.append(
                mul(
                    qbd_s[g, 32 * j : 32 * j + 32, :],
                    mem_s[2 * g + j // 2, :WIDTH, (j % 2) * LANES : (j % 2 + 1) * LANES],
                )
            )
        scores = jnp.concatenate(parts, 0)
        scores = jnp.where(iota(scores.shape, 1) < HIST_LEN, scores, -1e30)
        chance = jnp.exp(scores - jnp.max(scores, axis=1, keepdims=True))
        chance = chance * (1.0 / jnp.sum(chance, axis=1, keepdims=True))
        pc_s[g] = chance
        mixed = jnp.zeros((WIDTH, LANES), f32)
        for half in range(2):
            mixed = mixed + mul_t(
                mem_s[2 * g + half, WIDTH:, :], blocks_of(chance, half).astype(bf16)
            )
        oc_s[g] = jnp.where(head_mask(mixed.shape), mixed, 0.0).astype(bf16)
        return carry

    lax.fori_loop(0, groups, cross, 0)
    cross_mixed = gather_rows(oc_s)
    y2 = y1 + mul(wn_s[1, :, 5 * WIDTH : 6 * WIDTH], cross_mixed)
    inverse2 = inverse_rms(y2)
    h2 = norm_low(y2, inverse2, gain(5, LANES))
    lifted = mul(wt_s[1, MIXW : MIXW + FF, :], h2)
    active = jnp.maximum(lifted, 0.0).astype(bf16)
    y3 = y2 + mul(wn_s[1, :, MIXW + FF :], active)
    inverse3 = inverse_rms(y3)
    final = norm_low(y3, inverse3, gain(6, LANES))
    logits = mul(table_s[...], final)
    top = jnp.max(logits, axis=0, keepdims=True)
    log_total = top + jnp.log(jnp.sum(jnp.exp(logits - top), axis=0, keepdims=True))
    goal = goal_ref[...]
    match = iota(logits.shape, 0) == goal
    picked = jnp.sum(jnp.where(match, logits, 0.0), axis=0, keepdims=True)
    weight = jnp.zeros((1, LANES), f32)
    for d in range(DOMAINS):
        share = 1.0 / (DOMAINS * jnp.maximum(count_ref[d : d + 1, :], 1.0))
        weight = weight + jnp.where(domain_ref[...] == d, share, 0.0)
    loss = jnp.sum(weight * (log_total - picked), axis=1, keepdims=True)
    back_logits = (
        weight * (jnp.exp(logits - log_total) - jnp.where(match, 1.0, 0.0))
    ).astype(bf16)
    back_final = mul(ext_s[:D, :CODES], back_logits)
    table_grad = mul_t(back_logits, final)
    back, gain_grad = norm_back(y3, inverse3, gain(6, LANES), back_final)
    ggain_s[6] = gain_grad
    low = back.astype(bf16)
    put_blocks(grad_ref, 26, mul_t(low, active))
    back_lifted = jnp.where(lifted > 0, mul(wt_s[1, MIXW + FF :, :], low), 0.0).astype(bf16)
    put_blocks(grad_ref, 18, mul_t(h2, back_lifted))
    more, gain_grad = norm_back(
        y2, inverse2, gain(5, LANES), mul(wn_s[1, :, MIXW : MIXW + FF], back_lifted)
    )
    ggain_s[5] = gain_grad
    back = back + more
    low = back.astype(bf16)
    put_blocks(grad_ref, 15, mul_t(low, cross_mixed))
    spread_rows(mul(wt_s[1, 5 * WIDTH : 6 * WIDTH, :], low).astype(bf16), dobd_s, dobdt_s)

    def cross_back(g, carry):
        parts = []
        for j in range(4):
            parts.append(
                mul(
                    dobd_s[g, 32 * j : 32 * j + 32, :],
                    mem_s[2 * g + j // 2, WIDTH:, (j % 2) * LANES : (j % 2 + 1) * LANES],
                )
            )
        back_chance = jnp.concatenate(parts, 0)
        chance = pc_s[g]
        inner = jnp.sum(back_chance * chance, axis=1, keepdims=True)
        back_scores = chance * (back_chance - inner)
        total = jnp.zeros((WIDTH, LANES), f32)
        for half in range(2):
            spread = blocks_of(back_scores, half).astype(bf16)
            total = total + mul_t(mem_s[2 * g + half, :WIDTH, :], spread)
            mem_s[2 * g + half, :WIDTH, :] = mul(qbdt_s[g], spread).astype(bf16)
            spread = blocks_of(chance, half).astype(bf16)
            mem_s[2 * g + half, WIDTH:, :] = mul(dobdt_s[g], spread).astype(bf16)
        oc_s[g] = jnp.where(head_mask(total.shape), total, 0.0).astype(bf16)
        return carry

    lax.fori_loop(0, groups, cross_back, 0)
    back_query = gather_rows(oc_s)
    put_blocks(grad_ref, 12, mul_t(h1, back_query) * HEAD_DIM**-0.5)
    more, gain_grad = norm_back(
        y1, inverse1, gain(4, LANES), mul(wn_s[1, :, 4 * WIDTH : 5 * WIDTH], back_query)
    )
    ggain_s[4] = gain_grad
    back = back + more
    low = back.astype(bf16)
    put_blocks(grad_ref, 9, mul_t(low, self_mixed))
    back_mixed = mul(wt_s[1, 3 * WIDTH : 4 * WIDTH, :], low).astype(bf16)
    self_scores = []
    for j in range(PAIRS):
        part = slice(j * LANES, (j + 1) * LANES)
        keys = slice(WIDTH + j * LANES, WIDTH + (j + 1) * LANES)
        values = slice(2 * WIDTH + j * LANES, 2 * WIDTH + (j + 1) * LANES)
        one, two, three, scores = attend_back(
            dz_s[keys, :LANES],
            dz_s[part, :LANES],
            self_values[:, part],
            back_mixed[part],
            self_chance[j],
        )
        dz_s[part, LANES:] = one
        dz_s[keys, LANES:] = two
        dz_s[values, LANES:] = three
        self_scores.append(scores)
    put_blocks(grad_ref, 0, mul_t(h0, dz_s[:WIDTH, LANES:]) * HEAD_DIM**-0.5)
    put_blocks(grad_ref, 3, mul_t(h0, dz_s[WIDTH:, LANES:]))
    more, gain_grad = norm_back(
        y0, inverse0, gain(3, LANES), mul(wn_s[1, :, : 3 * WIDTH], dz_s[:, LANES:])
    )
    ggain_s[3] = gain_grad
    back = back + more
    spread = mul_t(onehot(start_ref[...], CODES), split_low(back))
    ge_s[:CODES, :] = table_grad + spread[:, :D] + spread[:, D:]
    ge_s[CODES:, :] = jnp.zeros((n, D), f32)

    g0_s[...] = jnp.zeros_like(g0_s)
    gbias_s[...] = jnp.zeros_like(gbias_s)
    for g in range(3):
        ggain_s[g] = jnp.zeros((D, LANES), f32)

    def fold(x):
        return x[:, :LANES] + x[:, LANES:]

    def encode_back(c, carry):
        x2 = x2_s[c]
        inverse = inverse_rms(x2)
        back_memory = mem_s[c]
        add_blocks(g0_s, 12, mul_t(norm_low(x2, inverse, gain(2, wide)), back_memory))
        back, gain_grad = norm_back(
            x2, inverse, gain(2, wide), mul(wn_s[0, :, 4 * WIDTH : 6 * WIDTH], back_memory)
        )
        ggain_s[2] += fold(gain_grad)
        low = back.astype(bf16)
        active = r_s[c]
        add_blocks(g0_s, 26, mul_t(low, active))
        back_active = mul(wt_s[0, MIXW + FF :, :], low)
        back_lifted = jnp.where(active.astype(f32) > 0, back_active, 0.0).astype(bf16)
        x1 = x1_s[c]
        inverse = inverse_rms(x1)
        add_blocks(g0_s, 18, mul_t(norm_low(x1, inverse, gain(1, wide)), back_lifted))
        more, gain_grad = norm_back(
            x1, inverse, gain(1, wide), mul(wn_s[0, :, MIXW : MIXW + FF], back_lifted)
        )
        ggain_s[1] += fold(gain_grad)
        back = back + more
        low = back.astype(bf16)
        add_blocks(g0_s, 9, mul_t(low, o_s[c]))
        back_mixed = mul(wt_s[0, 3 * WIDTH : 4 * WIDTH, :], low).astype(bf16)
        for i in range(2):
            lanes = slice(i * LANES, (i + 1) * LANES)
            for j in range(PAIRS):
                part = slice(j * LANES, (j + 1) * LANES)
                keys = slice(WIDTH + j * LANES, WIDTH + (j + 1) * LANES)
                values = slice(2 * WIDTH + j * LANES, 2 * WIDTH + (j + 1) * LANES)
                one, two, three, scores = attend_back(
                    qkv_s[c, keys, lanes],
                    qkv_s[c, part, lanes],
                    mul_t(eye, qkv_s[c, values, lanes]).astype(bf16)[:KEYS],
                    back_mixed[part, lanes],
                    p_s[2 * c + i, j],
                )
                dz_s[part, lanes] = one
                dz_s[keys, lanes] = two
                dz_s[values, lanes] = three
                gbias_s[j] += scores
        x0 = x0_s[c]
        inverse = inverse_rms(x0)
        add_blocks(g0_s, 0, mul_t(norm_low(x0, inverse, gain(0, wide)), dz_s[...]))
        more, gain_grad = norm_back(
            x0, inverse, gain(0, wide), mul(wn_s[0, :, : 3 * WIDTH], dz_s[...])
        )
        ggain_s[0] += fold(gain_grad)
        spread = mul_t(onehot(ids_ref[c], CODES + n), split_low(back + more))
        ge_s[...] += spread[:, :D] + spread[:, D:]
        return carry

    lax.fori_loop(0, chunks, encode_back, 0)

    for block in range(BLOCKS):
        value = g0_s[block]
        if block < 3:
            value = value * HEAD_DIM**-0.5
        grad_ref[0, block * D : (block + 1) * D, :] = value.astype(bf16)
    grad_embed_ref[...] = ge_s[:CODES, :].astype(bf16)
    grad_user_ref[...] = ge_s[CODES:, :].astype(bf16)

    ones = jnp.ones((8, LANES), f32)
    for g in range(7):
        small_ref[g : g + 1, :] = mul_exact(ones, ggain_s[g].T)[:1]
    small_ref[7:8, :] = jnp.broadcast_to(loss, (1, LANES))

    rows_s[...] = jnp.zeros_like(rows_s)

    def bucket_sums(b, carry):
        for head in range(HEADS):
            lanes = slice((head % 2) * LANES, (head % 2 + 1) * LANES)
            hit = jnp.where(buckets == b, gbias_s[head // 2, :, lanes], 0.0)
            rows_s[head, pl.ds(b, 1), :] = jnp.sum(hit, axis=0, keepdims=True)
        return carry

    lax.fori_loop(0, BUCKETS, bucket_sums, 0)
    for head in range(HEADS):
        lanes = slice((head % 2) * LANES, (head % 2 + 1) * LANES)
        for b in range(LEVELS):
            hit = jnp.where(offset == b, self_scores[head // 2][:, lanes], 0.0)
            rows_s[head, BUCKETS + b : BUCKETS + b + 1, :] = jnp.sum(hit, axis=0, keepdims=True)
    total = jnp.zeros((2 * BUCKETS, LANES), f32)
    for head in range(HEADS):
        pick = jnp.where(iota((LANES, LANES), 1) == head, 1.0, 0.0)
        total = total + mul_exact(rows_s[head], pick)
    small_ref[8:, :] = total


def compute(users, bias, ids, start, goal, domain, count, gains, embedding, weights):
    n = users.shape[0]
    chunks, groups = n // 2, n // 4
    wide = 2 * LANES
    vmem = pl.BlockSpec(memory_space=pltpu.VMEM)
    smem = pl.BlockSpec(memory_space=pltpu.SMEM)
    return pl.pallas_call(
        functools.partial(compute_kernel, n),
        out_shape=(
            jax.ShapeDtypeStruct((2, COLS, D), bf16),
            jax.ShapeDtypeStruct((CODES, D), bf16),
            jax.ShapeDtypeStruct((n, D), bf16),
            jax.ShapeDtypeStruct((8 + 2 * BUCKETS, LANES), f32),
        ),
        in_specs=[smem, smem] + [vmem] * 8,
        out_specs=(vmem,) * 4,
        scratch_shapes=[
            pltpu.VMEM((chunks, D, wide), f32),
            pltpu.VMEM((chunks, D, wide), f32),
            pltpu.VMEM((chunks, D, wide), f32),
            pltpu.VMEM((chunks, 3 * WIDTH, wide), bf16),
            pltpu.VMEM((n, PAIRS, KEYS, wide), bf16),
            pltpu.VMEM((chunks, WIDTH, wide), bf16),
            pltpu.VMEM((chunks, FF, wide), bf16),
            pltpu.VMEM((chunks, 2 * WIDTH, wide), bf16),
            pltpu.VMEM((3 * WIDTH, wide), bf16),
            pltpu.VMEM((2, COLS, D), bf16),
            pltpu.VMEM((2 * D, CODES + n), bf16),
            pltpu.VMEM((CODES, D), bf16),
            pltpu.VMEM((7, D, LANES), f32),
            pltpu.VMEM((PAIRS, KEYS, wide), f32),
            pltpu.VMEM((PAIRS, LANES, wide), f32),
            pltpu.VMEM((BLOCKS, D, LANES), f32),
            pltpu.VMEM((CODES + n, D), f32),
            pltpu.VMEM((PAIRS, KEYS, wide), f32),
            pltpu.VMEM((7, D, LANES), f32),
            pltpu.VMEM((HEADS, 2 * BUCKETS, LANES), f32),
            pltpu.VMEM((n, D), f32),
            pltpu.VMEM((groups, LANES, WIDTH), bf16),
            pltpu.VMEM((groups, WIDTH, LANES), bf16),
            pltpu.VMEM((groups, LANES, WIDTH), bf16),
            pltpu.VMEM((groups, WIDTH, LANES), bf16),
            pltpu.VMEM((groups, LANES, LANES), f32),
            pltpu.VMEM((groups, WIDTH, LANES), bf16),
        ],
        compiler_params=pltpu.CompilerParams(vmem_limit_bytes=62 * 2**20),
        name="gradients",
    )(users, bias, ids, start, goal, domain, count, gains, embedding, weights)


MESH = pl.DeviceIdType.MESH


def stages(dp):
    order = [("dp", 1), ("pipe", 1)]
    bit = 2
    while bit < dp:
        order.append(("dp", bit))
        bit *= 2
    return order


def side_of(axis, bit):
    return lax.rem(lax.div(lax.axis_index(axis), bit), 2)


def partner_of(axis, bit):
    place = lax.axis_index(axis)
    return {axis: place + bit * (1 - 2 * side_of(axis, bit))}


def greet(order):
    barrier = pltpu.get_barrier_semaphore()
    for axis, bit in order:
        pl.semaphore_signal(barrier, inc=1, device_id=partner_of(axis, bit), device_id_type=MESH)
    pl.semaphore_wait(barrier, len(order))


def remote(source, target, sends, recvs, index, stage):
    return pltpu.make_async_remote_copy(
        src_ref=source,
        dst_ref=target,
        send_sem=sends.at[index],
        recv_sem=recvs.at[index],
        device_id=partner_of(*stage),
        device_id_type=MESH,
    )


def begin_kernel(
    dp, mixer_ref, feed_ref, domain_ref, goal_ref, w_ref, stat_ref, stat_s, land_s, sends, recvs
):
    order = stages(dp)
    section = lax.axis_index("pipe")
    core = side_of("dp", 1)
    half = D // 2
    greet(order)

    scale = HEAD_DIM**-0.5
    cross = jnp.where(section == 1, scale, 1.0).astype(f32)
    own = w_ref.at[section]
    for start, width, ref, factor in (
        (0, WIDTH, mixer_ref, scale),
        (WIDTH, 3 * WIDTH, mixer_ref, None),
        (4 * WIDTH, WIDTH, mixer_ref, cross),
        (5 * WIDTH, WIDTH, mixer_ref, None),
        (MIXW, 2 * FF, feed_ref, None),
    ):
        first = start if ref is mixer_ref else 0
        value = ref[0, :, first : first + width]
        if factor is not None:
            value = value * factor
        own[:, start : start + width] = value.astype(bf16)
    rows = pl.ds(pl.multiple_of(core * half, half), half)
    across = remote(
        w_ref.at[section, rows], w_ref.at[section, rows], sends, recvs, 0, ("pipe", 1)
    )
    across.start()

    counts = [
        jnp.sum(jnp.where(domain_ref[...] == d, 1.0, 0.0), axis=1, keepdims=True)
        for d in range(DOMAINS)
    ]
    counts += [jnp.zeros((1, 1), f32)] * (8 - DOMAINS)
    stat_s[0, :, CODES:] = jnp.broadcast_to(jnp.concatenate(counts, 0), (8, LANES))
    stat_s[0, :, :CODES] = mul_t(jnp.ones((8, LANES), bf16), onehot(goal_ref[...], CODES))
    for k, stage in enumerate(order):
        copy = remote(stat_s.at[k], land_s.at[k], sends, recvs, 2 + k, stage)
        copy.start()
        copy.wait()
        stat_s[k + 1] = stat_s[k] + land_s[k]
    stat_ref[...] = stat_s[len(order)]

    across.wait()
    other = w_ref.at[1 - section, rows]
    share = remote(other, other, sends, recvs, 1, ("dp", 1))
    share.start()
    share.wait()


def begin(dp, mixer, feed, domain, goal):
    count = len(stages(dp))
    vmem = pl.BlockSpec(memory_space=pltpu.VMEM)
    stat = (8, CODES + LANES)
    return pl.pallas_call(
        functools.partial(begin_kernel, dp),
        out_shape=(
            jax.ShapeDtypeStruct((2, D, COLS), bf16),
            jax.ShapeDtypeStruct(stat, f32),
        ),
        in_specs=[vmem] * 4,
        out_specs=(vmem,) * 2,
        scratch_shapes=[
            pltpu.VMEM((count + 1,) + stat, f32),
            pltpu.VMEM((count,) + stat, f32),
            pltpu.SemaphoreType.DMA((2 + count,)),
            pltpu.SemaphoreType.DMA((2 + count,)),
        ],
        compiler_params=pltpu.CompilerParams(
            collective_id=0, has_side_effects=True, vmem_limit_bytes=32 * 2**20
        ),
        name="begin",
    )(mixer, feed, domain, goal)


def plan(dp):
    section_rows, code_rows = COLS, CODES
    steps = []
    for axis, bit in stages(dp):
        halve_section = axis == "dp" and section_rows % 32 == 0
        halve_codes = code_rows % 32 == 0
        steps.append((axis, bit, halve_section, halve_codes, section_rows, code_rows))
        section_rows = section_rows // 2 if halve_section else section_rows
        code_rows = code_rows // 2 if halve_codes else code_rows
    return steps, section_rows, code_rows


def reduce_kernel(
    dp,
    n,
    grad_ref,
    embed_ref,
    user_ref,
    small_ref,
    ids_ref,
    out_ref,
    out_embed_ref,
    out_user_ref,
    out_small_ref,
    out_ids_ref,
    out_square_ref,
    *scratch,
):
    steps, section_rows, code_rows = plan(dp)
    count = len(steps)
    land, land_embed = scratch[:count], scratch[count : 2 * count]
    sums, sums_embed = scratch[2 * count : 3 * count], scratch[3 * count : 4 * count]
    small_s, land_small, sends, recvs = scratch[4 * count :]
    pipe = lax.axis_index("pipe")
    greet([(step[0], step[1]) for step in steps])

    rising, falling = 0, 0
    for k, step in enumerate(steps):
        side = side_of(step[0], step[1])
        rising = rising + side * 2**k
        falling = falling + side * 2 ** (count - 1 - k)
    out_user_ref[pl.ds(pl.multiple_of(rising * n, n), n), :] = user_ref[...]
    fit = LANES // n
    owner = iota((8, LANES), 1) // n
    out_ids_ref[rising] = jnp.where(owner == lax.rem(rising, fit), ids_ref[...], 0)
    small_s[0] = small_ref[...]

    current, current_embed = grad_ref, embed_ref
    offset, offset_embed = 0, 0
    for k, (axis, bit, halve, halve_codes, rows, codes) in enumerate(steps):
        side = side_of(axis, bit)
        stage = (axis, bit)
        copies = []

        def send(source, target, index):
            copy = remote(source, target, sends, recvs, 5 * k + index, stage)
            copy.start()
            copies.append(copy)

        if axis == "pipe":
            keep = current.at[pipe]
            send(current.at[1 - pipe], land[k], 0)
        elif k == 0:
            part = rows // 2
            keep = current.at[:, pl.ds(pl.multiple_of(side * part, part), part)]
            send(current.at[:, pl.ds(pl.multiple_of((1 - side) * part, part), part)], land[k], 0)
        elif halve:
            part = rows // 2
            keep = current.at[pl.ds(pl.multiple_of(side * part, part), part)]
            send(current.at[pl.ds(pl.multiple_of((1 - side) * part, part), part)], land[k], 0)
        else:
            keep = current
            send(current, land[k], 0)
        if halve:
            offset = offset + side * (rows // 2)
        if halve_codes:
            part = codes // 2
            keep_embed = current_embed.at[pl.ds(pl.multiple_of(side * part, part), part)]
            source = current_embed.at[pl.ds(pl.multiple_of((1 - side) * part, part), part)]
            offset_embed = offset_embed + side * part
        else:
            keep_embed = source = current_embed
        send(source, land_embed[k], 1)
        slots = 2**k
        first = (rising // slots) * slots
        span = pl.ds(pl.multiple_of(first * n, n), slots * n)
        send(out_user_ref.at[span], out_user_ref.at[span], 2)
        span = pl.ds(first, slots)
        send(out_ids_ref.at[span], out_ids_ref.at[span], 3)
        send(small_s.at[k], land_small.at[k], 4)
        for copy in copies:
            copy.wait()
        sums[k][...] = (keep[...].astype(f32) + land[k][...].astype(f32)).astype(bf16)
        sums_embed[k][...] = (
            keep_embed[...].astype(f32) + land_embed[k][...].astype(f32)
        ).astype(bf16)
        small_s[k + 1] = small_s[k] + land_small[k]
        current, current_embed = sums[k], sums_embed[k]
    out_small_ref[...] = small_s[count]

    mine = pl.ds(pl.multiple_of(offset, section_rows), section_rows)
    mine_embed = pl.ds(pl.multiple_of(offset_embed, code_rows), code_rows)
    value = current[...]
    out_ref[mine, :] = value
    value = value.astype(f32)
    code_value = current_embed[...]
    out_embed_ref[mine_embed, :] = code_value
    code_value = code_value.astype(f32)
    copies_held = (2 ** (count - 1)) * section_rows // COLS
    code_copies_held = (2**count) * code_rows // CODES
    squares = jnp.sum(value * value, axis=0, keepdims=True) / copies_held
    code_squares = jnp.sum(code_value * code_value, axis=0, keepdims=True) / code_copies_held
    out_square_ref[falling] = jnp.concatenate(
        [squares, code_squares, jnp.zeros((6, LANES), f32)], 0
    )

    rows, codes = section_rows, code_rows
    for j, (axis, bit, halve, halve_codes, _, _) in enumerate(reversed(steps)):
        side = side_of(axis, bit)
        stage = (axis, bit)
        base = 5 * count + 3 * j
        copies = []
        if halve:
            span = pl.ds(pl.multiple_of(offset, section_rows), rows)
            copies.append(remote(out_ref.at[span], out_ref.at[span], sends, recvs, base, stage))
            offset = offset - side * rows
            rows = rows * 2
        if halve_codes:
            span = pl.ds(pl.multiple_of(offset_embed, code_rows), codes)
            copies.append(
                remote(out_embed_ref.at[span], out_embed_ref.at[span], sends, recvs, base + 1, stage)
            )
            offset_embed = offset_embed - side * codes
            codes = codes * 2
        slots = 2**j
        span = pl.ds((falling // slots) * slots, slots)
        copies.append(
            remote(
                out_square_ref.at[span], out_square_ref.at[span], sends, recvs, base + 2, stage
            )
        )
        for copy in copies:
            copy.start()
        for copy in copies:
            copy.wait()


def reduce(dp, grads, embed, user, small, ids):
    steps, section_rows, code_rows = plan(dp)
    count = len(steps)
    n = user.shape[0]
    devices = 2 * dp
    vmem = pl.BlockSpec(memory_space=pltpu.VMEM)
    buffers, embed_buffers = [], []
    for k, (axis, bit, halve, halve_codes, rows, codes) in enumerate(steps):
        rows = rows // 2 if halve else rows
        buffers.append(pltpu.VMEM((2, rows, D) if k == 0 else (rows, D), bf16))
        embed_buffers.append(pltpu.VMEM((codes // 2 if halve_codes else codes, D), bf16))
    return pl.pallas_call(
        functools.partial(reduce_kernel, dp, n),
        out_shape=(
            jax.ShapeDtypeStruct((COLS, D), bf16),
            jax.ShapeDtypeStruct((CODES, D), bf16),
            jax.ShapeDtypeStruct((devices * n, D), bf16),
            jax.ShapeDtypeStruct(small.shape, f32),
            jax.ShapeDtypeStruct((devices, 8, LANES), jnp.int32),
            jax.ShapeDtypeStruct((devices, 8, LANES), f32),
        ),
        in_specs=[vmem] * 5,
        out_specs=(vmem,) * 6,
        scratch_shapes=buffers
        + embed_buffers
        + buffers
        + embed_buffers
        + [
            pltpu.VMEM((count + 1,) + small.shape, f32),
            pltpu.VMEM((count,) + small.shape, f32),
            pltpu.SemaphoreType.DMA((8 * count,)),
            pltpu.SemaphoreType.DMA((8 * count,)),
        ],
        compiler_params=pltpu.CompilerParams(
            collective_id=1, has_side_effects=True, vmem_limit_bytes=48 * 2**20
        ),
        name="reduce",
    )(grads, embed, user, small, ids)


def adam(weight, moment, square, slope, rate, decay):
    moment = beta_one * moment + (1 - beta_one) * slope
    square = beta_two * square + (1 - beta_two) * slope * slope
    unbiased_moment = moment * (1 / (1 - beta_one**STEP))
    unbiased_square = square * (1 / (1 - beta_two**STEP))
    step = unbiased_moment / (jnp.sqrt(unbiased_square) + adam_eps) + decay * weight
    return weight - rate * step, moment, square


USER_ROWS = 400


def update_kernel(
    grad_ref,
    code_ref,
    user_ref,
    ids_ref,
    square_ref,
    small_ref,
    stat_ref,
    *refs,
):
    big_in, small_in, refs = refs[:9], refs[9:15], refs[15:]
    loss_ref, norm_ref, section_ref, hist_ref = refs[:4]
    big_out, small_out, low_out, refs = refs[4:13], refs[13:19], refs[19:22], refs[22:]
    hold, low_hold, user_grad, in_sems, out_sems = refs[:9], refs[9:12], *refs[12:]
    loads = [pltpu.make_async_copy(big_in[i], hold[i], in_sems.at[i]) for i in range(9)]
    for load in loads:
        load.start()

    users = user_grad.shape[0]
    span = min(1024, user_ref.shape[0])
    slots = span // LANES * (ids_ref.shape[0] * LANES // user_ref.shape[0])
    fit = ids_ref.shape[0] * LANES // user_ref.shape[0]
    user_grad[...] = jnp.zeros_like(user_grad)

    def scatter(part, carry):
        rows = user_ref[pl.ds(pl.multiple_of(part * span, span), span), :]
        lanes = []
        for group in range(span // LANES):
            total = ids_ref[part * slots + group * fit, :1, :]
            for other in range(1, fit):
                total = total + ids_ref[part * slots + group * fit + other, :1, :]
            lanes.append(total)
        ids = jnp.concatenate(lanes, 1)
        for block in range(users // USER_ROWS):
            place = slice(block * USER_ROWS, (block + 1) * USER_ROWS)
            hit = iota((USER_ROWS, span), 0) + block * USER_ROWS == ids
            user_grad[place, :] += mul(jnp.where(hit, 1.0, 0.0).astype(bf16), rows)
        return carry

    lax.fori_loop(0, user_ref.shape[0] // span, scatter, 0)

    def total(x):
        return jnp.sum(jnp.sum(x, axis=0, keepdims=True), axis=1, keepdims=True)

    devices = square_ref.shape[0]
    slot = iota((devices, 8, LANES), 0)
    row = iota((devices, 8, LANES), 1)
    squares = square_ref[...]
    side = lax.rem(lax.div(slot, devices // 4), 2)
    section_squares = [
        total(jnp.sum(jnp.where((row == 0) & (side == s), squares, 0.0), axis=0)) for s in range(2)
    ]
    rest = total(jnp.sum(jnp.where(row == 1, squares, 0.0), axis=0))
    user_values = user_grad[...]
    rest = rest + total(user_values * user_values)
    small = small_ref[...]
    lane, line = iota(small.shape, 1), iota(small.shape, 0)
    counted = (line < 7) | ((line > 7) & (lane < HEADS))
    small_kept = jnp.where(counted, small, 0.0)
    rest = rest + total(small_kept * small_kept)
    norm = jnp.sqrt(section_squares[0] + section_squares[1] + rest)
    factor = jnp.minimum(1.0, clip_norm / (norm + 1e-06))
    loss_ref[0] = small[7, 0]
    norm_ref[0] = norm[0, 0]
    for s in range(2):
        section_ref[s] = jnp.sqrt(section_squares[s])[0, 0]
    for level in range(LEVELS):
        hist_ref[level : level + 1, :] = stat_ref[
            :1, level * CODEBOOK : (level + 1) * CODEBOOK
        ]

    outs = adam(
        small_in[0][...], small_in[1][...], small_in[2][...], factor * small[:7], rate_gain, 0.0
    )
    for ref, value in zip(small_out[:3], outs):
        ref[...] = value
    for s in range(2):
        slope = factor * small[8 + s * BUCKETS : 8 + (s + 1) * BUCKETS, :HEADS]
        outs = adam(
            small_in[3][s], small_in[4][s], small_in[5][s], slope, rate_small, 0.0
        )
        for ref, value in zip(small_out[3:], outs):
            ref[s] = value

    stores = []

    def store(kind, place):
        first = 3 * kind
        pieces = [(hold[first + i], big_out[first + i]) for i in range(3)]
        pieces.append((low_hold[kind], low_out[kind]))
        for source, target in pieces:
            copy = pltpu.make_async_copy(
                source.at[place], target.at[place], out_sems.at[len(stores)]
            )
            copy.start()
            stores.append(copy)

    def step(kind, place, slope):
        first = 3 * kind
        outs = adam(
            hold[first][place],
            hold[first + 1][place],
            hold[first + 2][place],
            factor * slope,
            rate_matrix,
            decay_matrix,
        )
        for i in range(3):
            hold[first + i][place] = outs[i]
        low_hold[kind][place] = outs[0].astype(bf16)

    for i in range(3):
        loads[i].wait()
    for part in range(6):
        for block in range(3 * part, 3 * part + 3):
            lanes = slice(block * LANES, (block + 1) * LANES)
            step(0, (0, slice(None), lanes), grad_ref[lanes, :].astype(f32))
        store(0, (0, slice(None), slice(3 * part * LANES, 3 * (part + 1) * LANES)))
    for i in range(3, 6):
        loads[i].wait()
    for part in range(4):
        for block in range(4 * part, 4 * part + 4):
            lanes = slice(block * LANES, (block + 1) * LANES)
            rows = slice(MIXW + block * LANES, MIXW + (block + 1) * LANES)
            step(1, (0, slice(None), lanes), grad_ref[rows, :].astype(f32))
        store(1, (0, slice(None), slice(4 * part * LANES, 4 * (part + 1) * LANES)))
    for i in range(6, 9):
        loads[i].wait()
    for part in range(4):
        rows = slice(part * CODEBOOK, (part + 1) * CODEBOOK)
        step(2, (rows, slice(None)), code_ref[rows, :].astype(f32))
        store(2, (rows, slice(None)))
    for part in range(users // USER_ROWS):
        rows = slice(part * USER_ROWS, (part + 1) * USER_ROWS)
        place = (slice(CODES + part * USER_ROWS, CODES + (part + 1) * USER_ROWS), slice(None))
        step(2, place, user_grad[rows, :])
        store(2, place)
    for copy in stores:
        copy.wait()


def update(reduced, stat, mixers, feeds, embeds, gains, biases):
    vmem = pl.BlockSpec(memory_space=pltpu.VMEM)
    smem = pl.BlockSpec(memory_space=pltpu.SMEM)
    hbm = pl.BlockSpec(memory_space=pl.ANY)
    big = [*mixers, *feeds, *embeds]
    small = [*gains, *biases]
    low = [jax.ShapeDtypeStruct(x[0].shape, bf16) for x in (mixers, feeds, embeds)]
    users = embeds[0].shape[0] - CODES
    pieces = 4 * (6 + 4 + 4 + users // USER_ROWS)
    return pl.pallas_call(
        update_kernel,
        out_shape=[
            jax.ShapeDtypeStruct((1,), f32),
            jax.ShapeDtypeStruct((1,), f32),
            jax.ShapeDtypeStruct((2,), f32),
            jax.ShapeDtypeStruct((LEVELS, CODEBOOK), f32),
        ]
        + [jax.ShapeDtypeStruct(x.shape, f32) for x in big + small]
        + low,
        in_specs=[vmem] * 7 + [hbm] * 9 + [vmem] * 6,
        out_specs=[smem] * 3 + [vmem] + [hbm] * 9 + [vmem] * 6 + [hbm] * 3,
        scratch_shapes=[pltpu.VMEM(x.shape, f32) for x in big]
        + [pltpu.VMEM(x.shape, bf16) for x in low]
        + [
            pltpu.VMEM((users, D), f32),
            pltpu.SemaphoreType.DMA((9,)),
            pltpu.SemaphoreType.DMA((pieces,)),
        ],
        compiler_params=pltpu.CompilerParams(vmem_limit_bytes=40 * 2**20),
        name="update",
    )(*reduced, stat, *big, *small)


def shards(
    history_codes,
    user_ids,
    targets,
    domains,
    mixer,
    mixer_moment,
    mixer_square,
    feed,
    feed_moment,
    feed_square,
    embedding,
    embedding_moment,
    embedding_square,
    gains,
    gains_moment,
    gains_square,
    position_bias,
    bias_moment,
    bias_square,
):
    dp = lax.axis_size("dp")
    n = history_codes.shape[0] // 2
    first = lax.axis_index("pipe") * n

    def own(table):
        return lax.dynamic_slice_in_dim(table, first, n)

    codes, users, goal = own(history_codes), own(user_ids), own(targets)
    level = jnp.arange(codes.shape[1]) % LEVELS
    ids = jnp.concatenate(
        [
            CODES + jnp.arange(n, dtype=jnp.int32)[:, None],
            level[None, :] * CODEBOOK + codes,
            jnp.full((n, LANES - HIST_LEN), -1, jnp.int32),
        ],
        1,
    ).reshape(n // 2, 1, 2 * LANES)
    goal = jnp.arange(LEVELS)[None, :] * CODEBOOK + goal
    start = jnp.concatenate([jnp.zeros((n, 1), jnp.int32), goal[:, :-1]], 1).reshape(1, -1)
    goal = goal.reshape(1, -1)
    domain = jnp.broadcast_to(own(domains)[:, None], (n, LEVELS)).reshape(1, -1)
    weights, stat = begin(dp, mixer, feed, domain, goal)
    grads, embed, user, small = compute(
        users,
        position_bias.reshape(2 * BUCKETS, HEADS),
        ids,
        start,
        goal,
        domain,
        stat[:, CODES:],
        gains,
        embedding,
        weights,
    )
    spread = jnp.broadcast_to(jnp.tile(users, LANES // n)[None, :], (8, LANES))
    out, out_embed, out_user, out_small, out_ids, out_square = reduce(
        dp, grads, embed, user, small, spread
    )
    outs = update(
        (out, out_embed, out_user, out_ids, out_square, out_small),
        stat,
        (mixer, mixer_moment, mixer_square),
        (feed, feed_moment, feed_square),
        (embedding, embedding_moment, embedding_square),
        (gains, gains_moment, gains_square),
        (position_bias, bias_moment, bias_square),
    )
    loss, norm, sections, histograms = outs[:4]
    return (loss.reshape(()), norm.reshape(()), sections, histograms, *outs[4:])


def solution(mesh):
    by_dp, by_pipe, copied = P("dp"), P("pipe"), P()
    return jax.shard_map(
        shards,
        mesh=mesh,
        in_specs=(by_dp,) * 4 + (by_pipe,) * 6 + (copied,) * 9,
        out_specs=(copied,) * 4 + (by_pipe,) * 6 + (copied,) * 9 + (by_pipe,) * 2 + (copied,),
        check_vma=False,
    )
```

```python
import functools

import jax
import jax.numpy as jnp
from jax import lax
from jax.experimental import pallas as pl
from jax.experimental.pallas import tpu as pltpu
from jax.sharding import PartitionSpec as P

D = 128
HEADS = 6
HEAD_DIM = 64
FF = 1024
CODEBOOK = 256
LEVELS = 4
BUCKETS = 32
DOMAINS = 3
HIST_LEN = 81
STEP = 5
CODES = 1024
LANES = 128
WIDTH = HEADS * HEAD_DIM
MIXW = 6 * WIDTH
COLS = MIXW + 2 * FF
BLOCKS = COLS // LANES
KEYS = 96
GROUP = 4
WIDE = GROUP * LANES
PAIRS = HEADS // 2
ROWS = 32

norm_eps = 1e-06
beta_one = 0.9
beta_two = 0.999
adam_eps = 1e-08
clip_norm = 0.5
rate_matrix = 0.04
rate_gain = 0.8
rate_small = 0.3
decay_matrix = 0.01

f32 = jnp.float32
bf16 = jnp.bfloat16


def iota(shape, axis):
    return lax.broadcasted_iota(jnp.int32, shape, axis)


def mul(left, right):
    return jnp.dot(left, right, preferred_element_type=f32)


def mul_t(left, right):
    return lax.dot_general(left, right, (((1,), (1,)), ((), ())), preferred_element_type=f32)


def mul_exact(left, right):
    return jnp.dot(left, right, preferred_element_type=f32, precision=lax.Precision.HIGHEST)


def onehot(ids, rows):
    return jnp.where(iota((rows, ids.shape[1]), 0) == ids, 1.0, 0.0).astype(bf16)


def inverse_rms(x):
    return lax.rsqrt(jnp.mean(x * x, axis=0, keepdims=True) + norm_eps)


def norm_low(x, inverse, gain):
    return (x * inverse * gain).astype(bf16)


def norm_back(x, inverse, gain, upstream):
    scaled = x * inverse
    inner = upstream * gain
    back = inverse * (inner - scaled * jnp.mean(inner * scaled, axis=0, keepdims=True))
    return back, upstream * scaled


def block_diag(pair):
    zero = jnp.zeros((HEAD_DIM, LANES), pair.dtype)
    left = jnp.concatenate([pair[:HEAD_DIM], zero], 0)
    right = jnp.concatenate([zero, pair[HEAD_DIM:]], 0)
    return jnp.concatenate([left, right], 1)


def diagonal(both):
    return jnp.concatenate([both[:HEAD_DIM, :LANES], both[HEAD_DIM:, LANES:]], 0)


def pad_keys(table):
    if table.shape[0] == LANES:
        return table
    zero = jnp.zeros((LANES - table.shape[0], table.shape[1]), table.dtype)
    return jnp.concatenate([table, zero], 0)


def attend(keys, query, values, bias):
    scores = mul(keys, block_diag(query)) + bias
    top = jnp.max(scores, axis=0, keepdims=True)
    chance = jnp.exp(scores - top)
    total = jnp.sum(chance, axis=0, keepdims=True)
    chance = (chance * (1.0 / total)).astype(bf16)
    mixed = diagonal(mul(values, pad_keys(chance))).astype(bf16)
    return chance, mixed


def attend_back(keys_t, query, values, back_mixed, chance):
    exact = chance.astype(f32)
    spread = block_diag(back_mixed)
    back_chance = mul(values, spread)
    inner = jnp.sum(back_chance * exact, axis=0, keepdims=True)
    back_scores = exact * (back_chance - inner)
    low = pad_keys(back_scores.astype(bf16))
    back_query = diagonal(mul(keys_t, low)).astype(bf16)
    back_keys = mul_t(block_diag(query), low).astype(bf16)
    back_values = mul_t(spread, pad_keys(chance)).astype(bf16)
    return back_query, back_keys, back_values, back_scores


def add_blocks(ref, first, value):
    for block in range(value.shape[1] // LANES):
        ref[first + block] += value[:, block * LANES : (block + 1) * LANES]


def put_blocks(ref, first, value):
    for block in range(value.shape[1] // LANES):
        rows = slice((first + block) * D, (first + block + 1) * D)
        ref[1, rows, :] = value[:, block * LANES : (block + 1) * LANES].astype(ref.dtype)


def split_low(x):
    high = x.astype(bf16)
    return jnp.concatenate([high, (x - high.astype(f32)).astype(bf16)], 0)


def compute_kernel(
    n,
    users_ref,
    bias_ref,
    ids_ref,
    start_ref,
    goal_ref,
    domain_ref,
    count_ref,
    gains_ref,
    embed_ref,
    wn_s,
    grad_ref,
    grad_embed_ref,
    grad_user_ref,
    small_ref,
    x0_s,
    x1_s,
    x2_s,
    qkv_s,
    p_s,
    o_s,
    r_s,
    mem_s,
    dz_s,
    wt_s,
    ext_s,
    table_s,
    gain_s,
    ebias_s,
    dbias_s,
    g0_s,
    ge_s,
    gbias_s,
    ggain_s,
    rows_s,
    user_s,
    cross_s,
    cross_back_s,
    pc_s,
    oc_s,
):
    chunks = n // GROUP
    eye = jnp.where(iota((LANES, LANES), 0) == iota((LANES, LANES), 1), 1.0, 0.0).astype(bf16)

    for section in range(2):
        for block in range(BLOCKS):
            place = slice(block * LANES, (block + 1) * LANES)
            wt_s[section, place, :] = mul_t(eye, wn_s[section, :, place]).astype(bf16)

    def fetch(i, carry):
        user_s[pl.ds(i, 1), :] = embed_ref[pl.ds(CODES + users_ref[i], 1), :]
        return carry

    lax.fori_loop(0, n, fetch, 0)
    for block in range(CODES // LANES + 1):
        if block < CODES // LANES:
            rows = embed_ref[block * LANES : (block + 1) * LANES, :]
            table_s[block * LANES : (block + 1) * LANES, :] = rows.astype(bf16)
            span = LANES
        else:
            rows = user_s[...]
            span = n
        high = rows.astype(bf16)
        rest = (rows - high.astype(f32)).astype(bf16)
        place = slice(block * LANES, block * LANES + span)
        ext_s[:D, place] = mul_t(eye, high).astype(bf16)
        ext_s[D:, place] = mul_t(eye, rest).astype(bf16)

    for g in range(7):
        gain_s[g] = jnp.broadcast_to(gains_ref[g : g + 1, :], (LANES, LANES)).T

    key, query = iota((KEYS, LANES), 0), iota((KEYS, LANES), 1)
    distance = jnp.abs(query - key)
    remote = jnp.zeros_like(distance)
    for edge in (12, 16, 23, 32, 46, 64, 91):
        remote = remote + (distance >= edge).astype(jnp.int32)
    nearby = jnp.minimum(jnp.where(distance < 8, distance, 8 + remote), 15)
    buckets = nearby + jnp.where(key > query, 16, 0)
    for head in range(HEADS):
        lanes = slice((head % 2) * LANES, (head % 2 + 1) * LANES)

        def choose(b, table):
            return jnp.where(buckets == b, bias_ref[b, head], table)

        table = lax.fori_loop(0, BUCKETS, choose, jnp.zeros((KEYS, LANES), f32))
        ebias_s[head // 2, :, lanes] = jnp.where(key < HIST_LEN, table, -1e30)
    key, query = iota((LANES, LANES), 0), iota((LANES, LANES), 1)
    offset = query - key
    seen = ((key >> 2) == (query >> 2)) & (offset >= 0)
    for head in range(HEADS):
        lanes = slice((head % 2) * LANES, (head % 2 + 1) * LANES)
        table = jnp.full((LANES, LANES), -1e30, f32)
        for b in range(LEVELS):
            table = jnp.where(seen & (offset == b), bias_ref[BUCKETS + b, head], table)
        dbias_s[head // 2, :, lanes] = table

    def gain(g, width):
        column = gain_s[g]
        return column if width == LANES else jnp.concatenate([column] * (width // LANES), 1)

    def encode(c, carry):
        hot = onehot(ids_ref[c], CODES + n)
        both = mul(ext_s[...], hot)
        x0 = both[:D] + both[D:]
        x0_s[c] = x0
        h = norm_low(x0, inverse_rms(x0), gain(0, WIDE))
        for j in range(3):
            qkv_s[c, j * WIDTH : (j + 1) * WIDTH, :] = mul(
                wt_s[0, j * WIDTH : (j + 1) * WIDTH, :], h
            ).astype(bf16)
        for i in range(GROUP):
            lanes = slice(i * LANES, (i + 1) * LANES)
            natural = mul_t(eye, h[:, lanes]).astype(bf16)[:KEYS]
            keys = mul(natural, wn_s[0, :, WIDTH : 2 * WIDTH]).astype(bf16)
            for j in range(PAIRS):
                part = slice(j * LANES, (j + 1) * LANES)
                chance, mixed = attend(
                    keys[:, part],
                    qkv_s[c, part, lanes],
                    qkv_s[c, 2 * WIDTH + j * LANES : 2 * WIDTH + (j + 1) * LANES, lanes],
                    ebias_s[j],
                )
                p_s[GROUP * c + i, j] = chance
                o_s[c, part, lanes] = mixed
        x1 = x0 + mul(wn_s[0, :, 3 * WIDTH : 4 * WIDTH], o_s[c])
        x1_s[c] = x1
        h = norm_low(x1, inverse_rms(x1), gain(1, WIDE))
        for j in range(2):
            part = slice(j * FF // 2, (j + 1) * FF // 2)
            lifted = mul(wt_s[0, MIXW + j * FF // 2 : MIXW + (j + 1) * FF // 2, :], h)
            r_s[c, part, :] = jnp.maximum(lifted, 0.0).astype(bf16)
        x2 = x1 + mul(wn_s[0, :, MIXW + FF :], r_s[c])
        x2_s[c] = x2
        e = norm_low(x2, inverse_rms(x2), gain(2, WIDE))
        for j in range(2):
            part = slice(j * WIDTH, (j + 1) * WIDTH)
            mem_s[c, part, :] = mul(
                wt_s[0, 4 * WIDTH + j * WIDTH : 4 * WIDTH + (j + 1) * WIDTH, :], e
            ).astype(bf16)
        return carry

    lax.fori_loop(0, chunks, encode, 0)

    start = onehot(start_ref[...], CODES)
    both = mul(ext_s[:, :CODES], start)
    y0 = both[:D] + both[D:]
    inverse0 = inverse_rms(y0)
    h0 = norm_low(y0, inverse0, gain(3, LANES))
    dz_s[:, :LANES] = mul(wt_s[1, : 3 * WIDTH, :], h0).astype(bf16)
    both = mul(mul_t(eye, h0).astype(bf16), wn_s[1, :, WIDTH : 3 * WIDTH]).astype(bf16)
    self_chance = []
    mixed_parts = []
    for j in range(PAIRS):
        part = slice(j * LANES, (j + 1) * LANES)
        chance, mixed = attend(
            both[:, part],
            dz_s[part, :LANES],
            dz_s[2 * WIDTH + j * LANES : 2 * WIDTH + (j + 1) * LANES, :LANES],
            dbias_s[j],
        )
        self_chance.append(chance)
        mixed_parts.append(mixed)
    self_values = both[:, WIDTH:]
    self_mixed = jnp.concatenate(mixed_parts, 0)
    y1 = y0 + mul(wn_s[1, :, 3 * WIDTH : 4 * WIDTH], self_mixed)
    inverse1 = inverse_rms(y1)
    h1 = norm_low(y1, inverse1, gain(4, LANES))
    cross_s[...] = mul(wt_s[1, 4 * WIDTH : 5 * WIDTH, :], h1).astype(bf16)

    def rows_of(g, table):
        row, token = iota((LANES, LANES), 0), iota((LANES, LANES), 1)
        rep = jnp.where(token == 16 * g + 4 * (row >> 5) + (row & 3), 1.0, 0.0).astype(bf16)
        rows = mul_t(rep, table)
        mask = (iota(rows.shape, 1) >> 6) == ((iota(rows.shape, 0) & 31) >> 2)
        return jnp.where(mask, rows, 0.0).astype(bf16)

    def rows_t_of(g, table):
        token, row = iota((LANES, LANES), 0), iota((LANES, LANES), 1)
        rep = jnp.where(token == 16 * g + 4 * (row >> 5) + (row & 3), 1.0, 0.0).astype(bf16)
        rows = mul(table, rep)
        return jnp.where(head_mask(rows.shape), rows, 0.0).astype(bf16)

    def head_mask(shape):
        return (iota(shape, 0) >> 6) == ((iota(shape, 1) & 31) >> 2)

    def gather_rows(ref):
        total = jnp.zeros((WIDTH, LANES), f32)
        for g in range(chunks):
            row, token = iota((LANES, LANES), 0), iota((LANES, LANES), 1)
            rep = jnp.where(token == 16 * g + 4 * (row >> 5) + (row & 3), 1.0, 0.0).astype(bf16)
            total = total + mul(ref[g], rep)
        return total.astype(bf16)

    def blocks_of(table):
        owner = iota(table.shape, 0) >> 5
        zero = jnp.zeros_like(table)
        return jnp.concatenate(
            [jnp.where(owner == j, table, zero) for j in range(GROUP)], 1
        ).astype(bf16)

    def cross(g, carry):
        queries = rows_of(g, cross_s[...])
        parts = []
        for j in range(GROUP):
            parts.append(
                mul(
                    queries[32 * j : 32 * j + 32],
                    mem_s[g, :WIDTH, j * LANES : (j + 1) * LANES],
                )
            )
        scores = jnp.concatenate(parts, 0)
        scores = jnp.where(iota(scores.shape, 1) < HIST_LEN, scores, -1e30)
        chance = jnp.exp(scores - jnp.max(scores, axis=1, keepdims=True))
        chance = chance * (1.0 / jnp.sum(chance, axis=1, keepdims=True))
        pc_s[g] = chance
        mixed = mul_t(mem_s[g, WIDTH:, :], blocks_of(chance))
        oc_s[g] = jnp.where(head_mask(mixed.shape), mixed, 0.0).astype(bf16)
        return carry

    lax.fori_loop(0, chunks, cross, 0)
    cross_mixed = gather_rows(oc_s)
    y2 = y1 + mul(wn_s[1, :, 5 * WIDTH : 6 * WIDTH], cross_mixed)
    inverse2 = inverse_rms(y2)
    h2 = norm_low(y2, inverse2, gain(5, LANES))
    lifted = mul(wt_s[1, MIXW : MIXW + FF, :], h2)
    active = jnp.maximum(lifted, 0.0).astype(bf16)
    y3 = y2 + mul(wn_s[1, :, MIXW + FF :], active)
    inverse3 = inverse_rms(y3)
    final = norm_low(y3, inverse3, gain(6, LANES))
    logits = mul(table_s[...], final)
    top = jnp.max(logits, axis=0, keepdims=True)
    log_total = top + jnp.log(jnp.sum(jnp.exp(logits - top), axis=0, keepdims=True))
    goal = goal_ref[...]
    match = iota(logits.shape, 0) == goal
    picked = jnp.sum(jnp.where(match, logits, 0.0), axis=0, keepdims=True)
    weight = jnp.zeros((1, LANES), f32)
    for d in range(DOMAINS):
        share = 1.0 / (DOMAINS * jnp.maximum(count_ref[d : d + 1, :], 1.0))
        weight = weight + jnp.where(domain_ref[...] == d, share, 0.0)
    loss = jnp.sum(weight * (log_total - picked), axis=1, keepdims=True)
    back_logits = (
        weight * (jnp.exp(logits - log_total) - jnp.where(match, 1.0, 0.0))
    ).astype(bf16)
    back_final = mul(ext_s[:D, :CODES], back_logits)
    table_grad = mul_t(back_logits, final)
    back, gain_grad = norm_back(y3, inverse3, gain(6, LANES), back_final)
    ggain_s[6] = gain_grad
    low = back.astype(bf16)
    put_blocks(grad_ref, 26, mul_t(low, active))
    back_lifted = jnp.where(lifted > 0, mul(wt_s[1, MIXW + FF :, :], low), 0.0).astype(bf16)
    put_blocks(grad_ref, 18, mul_t(h2, back_lifted))
    more, gain_grad = norm_back(
        y2, inverse2, gain(5, LANES), mul(wn_s[1, :, MIXW : MIXW + FF], back_lifted)
    )
    ggain_s[5] = gain_grad
    back = back + more
    low = back.astype(bf16)
    put_blocks(grad_ref, 15, mul_t(low, cross_mixed))
    cross_back_s[...] = mul(wt_s[1, 5 * WIDTH : 6 * WIDTH, :], low).astype(bf16)

    def cross_back(g, carry):
        mixed_rows = rows_of(g, cross_back_s[...])
        parts = []
        for j in range(GROUP):
            parts.append(
                mul(
                    mixed_rows[32 * j : 32 * j + 32],
                    mem_s[g, WIDTH:, j * LANES : (j + 1) * LANES],
                )
            )
        back_chance = jnp.concatenate(parts, 0)
        chance = pc_s[g]
        inner = jnp.sum(back_chance * chance, axis=1, keepdims=True)
        spread = blocks_of(chance * (back_chance - inner))
        total = mul_t(mem_s[g, :WIDTH, :], spread)
        mem_s[g, :WIDTH, :] = mul(rows_t_of(g, cross_s[...]), spread).astype(bf16)
        mem_s[g, WIDTH:, :] = mul(rows_t_of(g, cross_back_s[...]), blocks_of(chance)).astype(bf16)
        oc_s[g] = jnp.where(head_mask(total.shape), total, 0.0).astype(bf16)
        return carry

    lax.fori_loop(0, chunks, cross_back, 0)
    back_query = gather_rows(oc_s)
    put_blocks(grad_ref, 12, mul_t(h1, back_query) * HEAD_DIM**-0.5)
    more, gain_grad = norm_back(
        y1, inverse1, gain(4, LANES), mul(wn_s[1, :, 4 * WIDTH : 5 * WIDTH], back_query)
    )
    ggain_s[4] = gain_grad
    back = back + more
    low = back.astype(bf16)
    put_blocks(grad_ref, 9, mul_t(low, self_mixed))
    back_mixed = mul(wt_s[1, 3 * WIDTH : 4 * WIDTH, :], low).astype(bf16)
    self_scores = []
    for j in range(PAIRS):
        part = slice(j * LANES, (j + 1) * LANES)
        keys = slice(WIDTH + j * LANES, WIDTH + (j + 1) * LANES)
        values = slice(2 * WIDTH + j * LANES, 2 * WIDTH + (j + 1) * LANES)
        one, two, three, scores = attend_back(
            dz_s[keys, :LANES],
            dz_s[part, :LANES],
            self_values[:, part],
            back_mixed[part],
            self_chance[j],
        )
        dz_s[part, LANES : 2 * LANES] = one
        dz_s[keys, LANES : 2 * LANES] = two
        dz_s[values, LANES : 2 * LANES] = three
        self_scores.append(scores)
    put_blocks(grad_ref, 0, mul_t(h0, dz_s[:WIDTH, LANES : 2 * LANES]) * HEAD_DIM**-0.5)
    put_blocks(grad_ref, 3, mul_t(h0, dz_s[WIDTH:, LANES : 2 * LANES]))
    more, gain_grad = norm_back(
        y0, inverse0, gain(3, LANES), mul(wn_s[1, :, : 3 * WIDTH], dz_s[:, LANES : 2 * LANES])
    )
    ggain_s[3] = gain_grad
    back = back + more
    spread = mul_t(onehot(start_ref[...], CODES), split_low(back))
    ge_s[:CODES, :] = table_grad + spread[:, :D] + spread[:, D:]
    ge_s[CODES:, :] = jnp.zeros((n, D), f32)

    g0_s[...] = jnp.zeros_like(g0_s)
    gbias_s[...] = jnp.zeros_like(gbias_s)
    for g in range(3):
        ggain_s[g] = jnp.zeros((D, LANES), f32)

    def fold(x):
        return sum(x[:, i * LANES : (i + 1) * LANES] for i in range(GROUP))

    def encode_back(c, carry):
        x2 = x2_s[c]
        inverse = inverse_rms(x2)
        back_memory = mem_s[c]
        add_blocks(g0_s, 12, mul_t(norm_low(x2, inverse, gain(2, WIDE)), back_memory))
        back, gain_grad = norm_back(
            x2, inverse, gain(2, WIDE), mul(wn_s[0, :, 4 * WIDTH : 6 * WIDTH], back_memory)
        )
        ggain_s[2] += fold(gain_grad)
        low = back.astype(bf16)
        active = r_s[c]
        add_blocks(g0_s, 26, mul_t(low, active))
        back_active = mul(wt_s[0, MIXW + FF :, :], low)
        back_lifted = jnp.where(active.astype(f32) > 0, back_active, 0.0).astype(bf16)
        x1 = x1_s[c]
        inverse = inverse_rms(x1)
        add_blocks(g0_s, 18, mul_t(norm_low(x1, inverse, gain(1, WIDE)), back_lifted))
        more, gain_grad = norm_back(
            x1, inverse, gain(1, WIDE), mul(wn_s[0, :, MIXW : MIXW + FF], back_lifted)
        )
        ggain_s[1] += fold(gain_grad)
        back = back + more
        low = back.astype(bf16)
        add_blocks(g0_s, 9, mul_t(low, o_s[c]))
        back_mixed = mul(wt_s[0, 3 * WIDTH : 4 * WIDTH, :], low).astype(bf16)
        for i in range(GROUP):
            lanes = slice(i * LANES, (i + 1) * LANES)
            for j in range(PAIRS):
                part = slice(j * LANES, (j + 1) * LANES)
                keys = slice(WIDTH + j * LANES, WIDTH + (j + 1) * LANES)
                values = slice(2 * WIDTH + j * LANES, 2 * WIDTH + (j + 1) * LANES)
                one, two, three, scores = attend_back(
                    qkv_s[c, keys, lanes],
                    qkv_s[c, part, lanes],
                    mul_t(eye, qkv_s[c, values, lanes]).astype(bf16)[:KEYS],
                    back_mixed[part, lanes],
                    p_s[GROUP * c + i, j],
                )
                dz_s[part, lanes] = one
                dz_s[keys, lanes] = two
                dz_s[values, lanes] = three
                gbias_s[j] += scores
        x0 = x0_s[c]
        inverse = inverse_rms(x0)
        add_blocks(g0_s, 0, mul_t(norm_low(x0, inverse, gain(0, WIDE)), dz_s[...]))
        more, gain_grad = norm_back(
            x0, inverse, gain(0, WIDE), mul(wn_s[0, :, : 3 * WIDTH], dz_s[...])
        )
        ggain_s[0] += fold(gain_grad)
        spread = mul_t(onehot(ids_ref[c], CODES + n), split_low(back + more))
        ge_s[...] += spread[:, :D] + spread[:, D:]
        return carry

    lax.fori_loop(0, chunks, encode_back, 0)

    for block in range(BLOCKS):
        value = g0_s[block]
        if block < 3:
            value = value * HEAD_DIM**-0.5
        grad_ref[0, block * D : (block + 1) * D, :] = value.astype(bf16)
    grad_embed_ref[...] = ge_s[:CODES, :].astype(bf16)
    grad_user_ref[...] = ge_s[CODES:, :].astype(bf16)

    ones = jnp.ones((8, LANES), f32)
    for g in range(7):
        small_ref[g : g + 1, :] = mul_exact(ones, ggain_s[g].T)[:1]
    small_ref[7:8, :] = jnp.broadcast_to(loss, (1, LANES))

    rows_s[...] = jnp.zeros_like(rows_s)

    def bucket_sums(b, carry):
        for head in range(HEADS):
            lanes = slice((head % 2) * LANES, (head % 2 + 1) * LANES)
            hit = jnp.where(buckets == b, gbias_s[head // 2, :, lanes], 0.0)
            rows_s[head, pl.ds(b, 1), :] = jnp.sum(hit, axis=0, keepdims=True)
        return carry

    lax.fori_loop(0, BUCKETS, bucket_sums, 0)
    for head in range(HEADS):
        lanes = slice((head % 2) * LANES, (head % 2 + 1) * LANES)
        for b in range(LEVELS):
            hit = jnp.where(offset == b, self_scores[head // 2][:, lanes], 0.0)
            rows_s[head, BUCKETS + b : BUCKETS + b + 1, :] = jnp.sum(hit, axis=0, keepdims=True)
    total = jnp.zeros((2 * BUCKETS, LANES), f32)
    for head in range(HEADS):
        pick = jnp.where(iota((LANES, LANES), 1) == head, 1.0, 0.0)
        total = total + mul_exact(rows_s[head], pick)
    small_ref[8:, :] = total


def compute(users, bias, ids, start, goal, domain, count, gains, embedding, weights):
    n = users.shape[0]
    chunks = n // GROUP
    vmem = pl.BlockSpec(memory_space=pltpu.VMEM)
    smem = pl.BlockSpec(memory_space=pltpu.SMEM)
    return pl.pallas_call(
        functools.partial(compute_kernel, n),
        out_shape=(
            jax.ShapeDtypeStruct((2, COLS, D), bf16),
            jax.ShapeDtypeStruct((CODES, D), bf16),
            jax.ShapeDtypeStruct((n, D), bf16),
            jax.ShapeDtypeStruct((8 + 2 * BUCKETS, LANES), f32),
        ),
        in_specs=[smem, smem] + [vmem] * 8,
        out_specs=(vmem,) * 4,
        scratch_shapes=[
            pltpu.VMEM((chunks, D, WIDE), f32),
            pltpu.VMEM((chunks, D, WIDE), f32),
            pltpu.VMEM((chunks, D, WIDE), f32),
            pltpu.VMEM((chunks, 3 * WIDTH, WIDE), bf16),
            pltpu.VMEM((n, PAIRS, KEYS, 2 * LANES), bf16),
            pltpu.VMEM((chunks, WIDTH, WIDE), bf16),
            pltpu.VMEM((chunks, FF, WIDE), bf16),
            pltpu.VMEM((chunks, 2 * WIDTH, WIDE), bf16),
            pltpu.VMEM((3 * WIDTH, WIDE), bf16),
            pltpu.VMEM((2, COLS, D), bf16),
            pltpu.VMEM((2 * D, CODES + n), bf16),
            pltpu.VMEM((CODES, D), bf16),
            pltpu.VMEM((7, D, LANES), f32),
            pltpu.VMEM((PAIRS, KEYS, 2 * LANES), f32),
            pltpu.VMEM((PAIRS, LANES, 2 * LANES), f32),
            pltpu.VMEM((BLOCKS, D, LANES), f32),
            pltpu.VMEM((CODES + n, D), f32),
            pltpu.VMEM((PAIRS, KEYS, 2 * LANES), f32),
            pltpu.VMEM((7, D, LANES), f32),
            pltpu.VMEM((HEADS, 2 * BUCKETS, LANES), f32),
            pltpu.VMEM((n, D), f32),
            pltpu.VMEM((WIDTH, LANES), bf16),
            pltpu.VMEM((WIDTH, LANES), bf16),
            pltpu.VMEM((chunks, LANES, LANES), f32),
            pltpu.VMEM((chunks, WIDTH, LANES), bf16),
        ],
        compiler_params=pltpu.CompilerParams(vmem_limit_bytes=62 * 2**20),
        name="gradients",
    )(users, bias, ids, start, goal, domain, count, gains, embedding, weights)


MESH = pl.DeviceIdType.MESH


def stages(dp):
    order = [("dp", 1), ("pipe", 1)]
    bit = 2
    while bit < dp:
        order.append(("dp", bit))
        bit *= 2
    return order


def side_of(axis, bit):
    return lax.rem(lax.div(lax.axis_index(axis), bit), 2)


def partner_of(axis, bit):
    place = lax.axis_index(axis)
    return {axis: place + bit * (1 - 2 * side_of(axis, bit))}


def greet(order):
    barrier = pltpu.get_barrier_semaphore()
    for axis, bit in order:
        pl.semaphore_signal(barrier, inc=1, device_id=partner_of(axis, bit), device_id_type=MESH)
    pl.semaphore_wait(barrier, len(order))


def remote(source, target, sends, recvs, index, stage):
    return pltpu.make_async_remote_copy(
        src_ref=source,
        dst_ref=target,
        send_sem=sends.at[index],
        recv_sem=recvs.at[index],
        device_id=partner_of(*stage),
        device_id_type=MESH,
    )


def begin_kernel(
    dp, mixer_ref, feed_ref, domain_ref, goal_ref, w_ref, stat_ref, stat_s, land_s, sends, recvs
):
    order = stages(dp)
    section = lax.axis_index("pipe")
    core = side_of("dp", 1)
    half = D // 2
    greet(order)

    scale = HEAD_DIM**-0.5
    cross = jnp.where(section == 1, scale, 1.0).astype(f32)
    own = w_ref.at[section]
    for start, width, ref, factor in (
        (0, WIDTH, mixer_ref, scale),
        (WIDTH, 3 * WIDTH, mixer_ref, None),
        (4 * WIDTH, WIDTH, mixer_ref, cross),
        (5 * WIDTH, WIDTH, mixer_ref, None),
        (MIXW, 2 * FF, feed_ref, None),
    ):
        first = start if ref is mixer_ref else 0
        value = ref[0, :, first : first + width]
        if factor is not None:
            value = value * factor
        own[:, start : start + width] = value.astype(bf16)
    rows = pl.ds(pl.multiple_of(core * half, half), half)
    across = remote(
        w_ref.at[section, rows], w_ref.at[section, rows], sends, recvs, 0, ("pipe", 1)
    )
    across.start()

    counts = [
        jnp.sum(jnp.where(domain_ref[...] == d, 1.0, 0.0), axis=1, keepdims=True)
        for d in range(DOMAINS)
    ]
    counts += [jnp.zeros((1, 1), f32)] * (8 - DOMAINS)
    stat_s[0, :, CODES:] = jnp.broadcast_to(jnp.concatenate(counts, 0), (8, LANES))
    stat_s[0, :, :CODES] = mul_t(jnp.ones((8, LANES), bf16), onehot(goal_ref[...], CODES))
    for k, stage in enumerate(order):
        copy = remote(stat_s.at[k], land_s.at[k], sends, recvs, 2 + k, stage)
        copy.start()
        copy.wait()
        stat_s[k + 1] = stat_s[k] + land_s[k]
    stat_ref[...] = stat_s[len(order)]

    across.wait()
    other = w_ref.at[1 - section, rows]
    share = remote(other, other, sends, recvs, 1, ("dp", 1))
    share.start()
    share.wait()


def begin(dp, mixer, feed, domain, goal):
    count = len(stages(dp))
    vmem = pl.BlockSpec(memory_space=pltpu.VMEM)
    stat = (8, CODES + LANES)
    return pl.pallas_call(
        functools.partial(begin_kernel, dp),
        out_shape=(
            jax.ShapeDtypeStruct((2, D, COLS), bf16),
            jax.ShapeDtypeStruct(stat, f32),
        ),
        in_specs=[vmem] * 4,
        out_specs=(vmem,) * 2,
        scratch_shapes=[
            pltpu.VMEM((count + 1,) + stat, f32),
            pltpu.VMEM((count,) + stat, f32),
            pltpu.SemaphoreType.DMA((2 + count,)),
            pltpu.SemaphoreType.DMA((2 + count,)),
        ],
        compiler_params=pltpu.CompilerParams(
            collective_id=0, has_side_effects=True, vmem_limit_bytes=32 * 2**20
        ),
        name="begin",
    )(mixer, feed, domain, goal)


def plan(dp):
    section_rows, code_rows = COLS, CODES
    steps = []
    for axis, bit in stages(dp):
        halve_section = axis == "dp" and section_rows % 32 == 0
        halve_codes = code_rows % 32 == 0
        steps.append((axis, bit, halve_section, halve_codes, section_rows, code_rows))
        section_rows = section_rows // 2 if halve_section else section_rows
        code_rows = code_rows // 2 if halve_codes else code_rows
    return steps, section_rows, code_rows


def reduce_kernel(
    dp,
    n,
    grad_ref,
    embed_ref,
    user_ref,
    small_ref,
    ids_ref,
    out_ref,
    out_embed_ref,
    out_user_ref,
    out_small_ref,
    out_ids_ref,
    out_square_ref,
    *scratch,
):
    steps, section_rows, code_rows = plan(dp)
    count = len(steps)
    land, land_embed = scratch[:count], scratch[count : 2 * count]
    sums, sums_embed = scratch[2 * count : 3 * count], scratch[3 * count : 4 * count]
    small_s, land_small, sends, recvs = scratch[4 * count :]
    pipe = lax.axis_index("pipe")
    greet([(step[0], step[1]) for step in steps])

    rising, falling = 0, 0
    for k, step in enumerate(steps):
        side = side_of(step[0], step[1])
        rising = rising + side * 2**k
        falling = falling + side * 2 ** (count - 1 - k)
    out_user_ref[pl.ds(pl.multiple_of(rising * n, n), n), :] = user_ref[...]
    fit = LANES // n
    owner = iota((8, LANES), 1) // n
    out_ids_ref[rising] = jnp.where(owner == lax.rem(rising, fit), ids_ref[...], 0)
    small_s[0] = small_ref[...]

    current, current_embed = grad_ref, embed_ref
    offset, offset_embed = 0, 0
    for k, (axis, bit, halve, halve_codes, rows, codes) in enumerate(steps):
        side = side_of(axis, bit)
        stage = (axis, bit)
        copies = []

        def send(source, target, index):
            copy = remote(source, target, sends, recvs, 5 * k + index, stage)
            copy.start()
            copies.append(copy)

        if axis == "pipe":
            keep = current.at[pipe]
            send(current.at[1 - pipe], land[k], 0)
        elif k == 0:
            part = rows // 2
            keep = current.at[:, pl.ds(pl.multiple_of(side * part, part), part)]
            send(current.at[:, pl.ds(pl.multiple_of((1 - side) * part, part), part)], land[k], 0)
        elif halve:
            part = rows // 2
            keep = current.at[pl.ds(pl.multiple_of(side * part, part), part)]
            send(current.at[pl.ds(pl.multiple_of((1 - side) * part, part), part)], land[k], 0)
        else:
            keep = current
            send(current, land[k], 0)
        if halve:
            offset = offset + side * (rows // 2)
        if halve_codes:
            part = codes // 2
            keep_embed = current_embed.at[pl.ds(pl.multiple_of(side * part, part), part)]
            source = current_embed.at[pl.ds(pl.multiple_of((1 - side) * part, part), part)]
            offset_embed = offset_embed + side * part
        else:
            keep_embed = source = current_embed
        send(source, land_embed[k], 1)
        slots = 2**k
        first = (rising // slots) * slots
        span = pl.ds(pl.multiple_of(first * n, n), slots * n)
        send(out_user_ref.at[span], out_user_ref.at[span], 2)
        span = pl.ds(first, slots)
        send(out_ids_ref.at[span], out_ids_ref.at[span], 3)
        send(small_s.at[k], land_small.at[k], 4)
        for copy in copies:
            copy.wait()
        sums[k][...] = (keep[...].astype(f32) + land[k][...].astype(f32)).astype(bf16)
        sums_embed[k][...] = (
            keep_embed[...].astype(f32) + land_embed[k][...].astype(f32)
        ).astype(bf16)
        small_s[k + 1] = small_s[k] + land_small[k]
        current, current_embed = sums[k], sums_embed[k]
    out_small_ref[...] = small_s[count]

    mine = pl.ds(pl.multiple_of(offset, section_rows), section_rows)
    mine_embed = pl.ds(pl.multiple_of(offset_embed, code_rows), code_rows)
    value = current[...]
    out_ref[mine, :] = value
    value = value.astype(f32)
    code_value = current_embed[...]
    out_embed_ref[mine_embed, :] = code_value
    code_value = code_value.astype(f32)
    copies_held = (2 ** (count - 1)) * section_rows // COLS
    code_copies_held = (2**count) * code_rows // CODES
    squares = jnp.sum(value * value, axis=0, keepdims=True) / copies_held
    code_squares = jnp.sum(code_value * code_value, axis=0, keepdims=True) / code_copies_held
    out_square_ref[falling] = jnp.concatenate(
        [squares, code_squares, jnp.zeros((6, LANES), f32)], 0
    )

    rows, codes = section_rows, code_rows
    for j, (axis, bit, halve, halve_codes, _, _) in enumerate(reversed(steps)):
        side = side_of(axis, bit)
        stage = (axis, bit)
        base = 5 * count + 3 * j
        copies = []
        if halve:
            span = pl.ds(pl.multiple_of(offset, section_rows), rows)
            copies.append(remote(out_ref.at[span], out_ref.at[span], sends, recvs, base, stage))
            offset = offset - side * rows
            rows = rows * 2
        if halve_codes:
            span = pl.ds(pl.multiple_of(offset_embed, code_rows), codes)
            copies.append(
                remote(out_embed_ref.at[span], out_embed_ref.at[span], sends, recvs, base + 1, stage)
            )
            offset_embed = offset_embed - side * codes
            codes = codes * 2
        slots = 2**j
        span = pl.ds((falling // slots) * slots, slots)
        copies.append(
            remote(
                out_square_ref.at[span], out_square_ref.at[span], sends, recvs, base + 2, stage
            )
        )
        for copy in copies:
            copy.start()
        for copy in copies:
            copy.wait()


def reduce(dp, grads, embed, user, small, ids):
    steps, section_rows, code_rows = plan(dp)
    count = len(steps)
    n = user.shape[0]
    devices = 2 * dp
    vmem = pl.BlockSpec(memory_space=pltpu.VMEM)
    buffers, embed_buffers = [], []
    for k, (axis, bit, halve, halve_codes, rows, codes) in enumerate(steps):
        rows = rows // 2 if halve else rows
        buffers.append(pltpu.VMEM((2, rows, D) if k == 0 else (rows, D), bf16))
        embed_buffers.append(pltpu.VMEM((codes // 2 if halve_codes else codes, D), bf16))
    return pl.pallas_call(
        functools.partial(reduce_kernel, dp, n),
        out_shape=(
            jax.ShapeDtypeStruct((COLS, D), bf16),
            jax.ShapeDtypeStruct((CODES, D), bf16),
            jax.ShapeDtypeStruct((devices * n, D), bf16),
            jax.ShapeDtypeStruct(small.shape, f32),
            jax.ShapeDtypeStruct((devices, 8, LANES), jnp.int32),
            jax.ShapeDtypeStruct((devices, 8, LANES), f32),
        ),
        in_specs=[vmem] * 5,
        out_specs=(vmem,) * 6,
        scratch_shapes=buffers
        + embed_buffers
        + buffers
        + embed_buffers
        + [
            pltpu.VMEM((count + 1,) + small.shape, f32),
            pltpu.VMEM((count,) + small.shape, f32),
            pltpu.SemaphoreType.DMA((8 * count,)),
            pltpu.SemaphoreType.DMA((8 * count,)),
        ],
        compiler_params=pltpu.CompilerParams(
            collective_id=1, has_side_effects=True, vmem_limit_bytes=48 * 2**20
        ),
        name="reduce",
    )(grads, embed, user, small, ids)


def adam(weight, moment, square, slope, rate, decay):
    moment = beta_one * moment + (1 - beta_one) * slope
    square = beta_two * square + (1 - beta_two) * slope * slope
    unbiased_moment = moment * (1 / (1 - beta_one**STEP))
    unbiased_square = square * (1 / (1 - beta_two**STEP))
    step = unbiased_moment / (jnp.sqrt(unbiased_square) + adam_eps) + decay * weight
    return weight - rate * step, moment, square


USER_ROWS = 400


def update_kernel(*refs):
    parts_in, big_in, small_in, refs = refs[:7], refs[7:16], refs[16:22], refs[22:]
    loss_ref, norm_ref, section_ref, hist_ref = refs[:4]
    big_out, small_out, low_out, refs = refs[4:13], refs[13:19], refs[19:22], refs[22:]
    parts, hold, low_hold = refs[:7], refs[7:16], refs[16:19]
    user_grad, part_sems, in_sems, out_sems = refs[19:]
    grad_ref, code_ref, user_ref, ids_ref, square_ref, small_ref, stat_ref = parts
    arrivals = [pltpu.make_async_copy(parts_in[i], parts[i], part_sems.at[i]) for i in range(7)]
    loads = [pltpu.make_async_copy(big_in[i], hold[i], in_sems.at[i]) for i in range(9)]
    for load in arrivals[1:] + arrivals[:1] + loads:
        load.start()
    for arrival in arrivals:
        arrival.wait()

    users = user_grad.shape[0]
    span = min(1024, user_ref.shape[0])
    slots = span // LANES * (ids_ref.shape[0] * LANES // user_ref.shape[0])
    fit = ids_ref.shape[0] * LANES // user_ref.shape[0]
    user_grad[...] = jnp.zeros_like(user_grad)

    def scatter(part, carry):
        rows = user_ref[pl.ds(pl.multiple_of(part * span, span), span), :]
        lanes = []
        for group in range(span // LANES):
            total = ids_ref[part * slots + group * fit, :1, :]
            for other in range(1, fit):
                total = total + ids_ref[part * slots + group * fit + other, :1, :]
            lanes.append(total)
        ids = jnp.concatenate(lanes, 1)
        for block in range(users // USER_ROWS):
            place = slice(block * USER_ROWS, (block + 1) * USER_ROWS)
            hit = iota((USER_ROWS, span), 0) + block * USER_ROWS == ids
            user_grad[place, :] += mul(jnp.where(hit, 1.0, 0.0).astype(bf16), rows)
        return carry

    lax.fori_loop(0, user_ref.shape[0] // span, scatter, 0)

    def total(x):
        return jnp.sum(jnp.sum(x, axis=0, keepdims=True), axis=1, keepdims=True)

    devices = square_ref.shape[0]
    slot = iota((devices, 8, LANES), 0)
    row = iota((devices, 8, LANES), 1)
    squares = square_ref[...]
    side = lax.rem(lax.div(slot, devices // 4), 2)
    section_squares = [
        total(jnp.sum(jnp.where((row == 0) & (side == s), squares, 0.0), axis=0)) for s in range(2)
    ]
    rest = total(jnp.sum(jnp.where(row == 1, squares, 0.0), axis=0))
    user_values = user_grad[...]
    rest = rest + total(user_values * user_values)
    small = small_ref[...]
    lane, line = iota(small.shape, 1), iota(small.shape, 0)
    counted = (line < 7) | ((line > 7) & (lane < HEADS))
    small_kept = jnp.where(counted, small, 0.0)
    rest = rest + total(small_kept * small_kept)
    norm = jnp.sqrt(section_squares[0] + section_squares[1] + rest)
    factor = jnp.minimum(1.0, clip_norm / (norm + 1e-06))
    loss_ref[0] = small[7, 0]
    norm_ref[0] = norm[0, 0]
    for s in range(2):
        section_ref[s] = jnp.sqrt(section_squares[s])[0, 0]
    for level in range(LEVELS):
        hist_ref[level : level + 1, :] = stat_ref[
            :1, level * CODEBOOK : (level + 1) * CODEBOOK
        ]

    outs = adam(
        small_in[0][...], small_in[1][...], small_in[2][...], factor * small[:7], rate_gain, 0.0
    )
    for ref, value in zip(small_out[:3], outs):
        ref[...] = value
    for s in range(2):
        slope = factor * small[8 + s * BUCKETS : 8 + (s + 1) * BUCKETS, :HEADS]
        outs = adam(
            small_in[3][s], small_in[4][s], small_in[5][s], slope, rate_small, 0.0
        )
        for ref, value in zip(small_out[3:], outs):
            ref[s] = value

    stores = []

    def store(kind, place):
        first = 3 * kind
        pieces = [(hold[first + i], big_out[first + i]) for i in range(3)]
        pieces.append((low_hold[kind], low_out[kind]))
        for source, target in pieces:
            copy = pltpu.make_async_copy(
                source.at[place], target.at[place], out_sems.at[len(stores)]
            )
            copy.start()
            stores.append(copy)

    def step(kind, place, slope):
        first = 3 * kind
        outs = adam(
            hold[first][place],
            hold[first + 1][place],
            hold[first + 2][place],
            factor * slope,
            rate_matrix,
            decay_matrix,
        )
        for i in range(3):
            hold[first + i][place] = outs[i]
        low_hold[kind][place] = outs[0].astype(bf16)

    for i in range(3):
        loads[i].wait()
    for part in range(6):
        for block in range(3 * part, 3 * part + 3):
            lanes = slice(block * LANES, (block + 1) * LANES)
            step(0, (0, slice(None), lanes), grad_ref[lanes, :].astype(f32))
        store(0, (0, slice(None), slice(3 * part * LANES, 3 * (part + 1) * LANES)))
    for i in range(3, 6):
        loads[i].wait()
    for part in range(4):
        for block in range(4 * part, 4 * part + 4):
            lanes = slice(block * LANES, (block + 1) * LANES)
            rows = slice(MIXW + block * LANES, MIXW + (block + 1) * LANES)
            step(1, (0, slice(None), lanes), grad_ref[rows, :].astype(f32))
        store(1, (0, slice(None), slice(4 * part * LANES, 4 * (part + 1) * LANES)))
    for i in range(6, 9):
        loads[i].wait()
    for part in range(4):
        rows = slice(part * CODEBOOK, (part + 1) * CODEBOOK)
        step(2, (rows, slice(None)), code_ref[rows, :].astype(f32))
        store(2, (rows, slice(None)))
    for part in range(users // USER_ROWS):
        rows = slice(part * USER_ROWS, (part + 1) * USER_ROWS)
        place = (slice(CODES + part * USER_ROWS, CODES + (part + 1) * USER_ROWS), slice(None))
        step(2, place, user_grad[rows, :])
        store(2, place)
    for copy in stores:
        copy.wait()


def update(reduced, stat, mixers, feeds, embeds, gains, biases):
    vmem = pl.BlockSpec(memory_space=pltpu.VMEM)
    smem = pl.BlockSpec(memory_space=pltpu.SMEM)
    hbm = pl.BlockSpec(memory_space=pl.ANY)
    big = [*mixers, *feeds, *embeds]
    small = [*gains, *biases]
    low = [jax.ShapeDtypeStruct(x[0].shape, bf16) for x in (mixers, feeds, embeds)]
    users = embeds[0].shape[0] - CODES
    pieces = 4 * (6 + 4 + 4 + users // USER_ROWS)
    return pl.pallas_call(
        update_kernel,
        out_shape=[
            jax.ShapeDtypeStruct((1,), f32),
            jax.ShapeDtypeStruct((1,), f32),
            jax.ShapeDtypeStruct((2,), f32),
            jax.ShapeDtypeStruct((LEVELS, CODEBOOK), f32),
        ]
        + [jax.ShapeDtypeStruct(x.shape, f32) for x in big + small]
        + low,
        in_specs=[hbm] * 16 + [vmem] * 6,
        out_specs=[smem] * 3 + [vmem] + [hbm] * 9 + [vmem] * 6 + [hbm] * 3,
        scratch_shapes=[pltpu.VMEM(x.shape, x.dtype) for x in (*reduced, stat)]
        + [pltpu.VMEM(x.shape, f32) for x in big]
        + [pltpu.VMEM(x.shape, bf16) for x in low]
        + [
            pltpu.VMEM((users, D), f32),
            pltpu.SemaphoreType.DMA((7,)),
            pltpu.SemaphoreType.DMA((9,)),
            pltpu.SemaphoreType.DMA((pieces,)),
        ],
        compiler_params=pltpu.CompilerParams(vmem_limit_bytes=40 * 2**20),
        name="update",
    )(*reduced, stat, *big, *small)


def shards(
    history_codes,
    user_ids,
    targets,
    domains,
    mixer,
    mixer_moment,
    mixer_square,
    feed,
    feed_moment,
    feed_square,
    embedding,
    embedding_moment,
    embedding_square,
    gains,
    gains_moment,
    gains_square,
    position_bias,
    bias_moment,
    bias_square,
):
    dp = lax.axis_size("dp")
    n = history_codes.shape[0] // 2
    first = lax.axis_index("pipe") * n

    def own(table):
        return lax.dynamic_slice_in_dim(table, first, n)

    codes, users, goal = own(history_codes), own(user_ids), own(targets)
    level = jnp.arange(codes.shape[1]) % LEVELS
    ids = jnp.concatenate(
        [
            CODES + jnp.arange(n, dtype=jnp.int32)[:, None],
            level[None, :] * CODEBOOK + codes,
            jnp.full((n, LANES - HIST_LEN), -1, jnp.int32),
        ],
        1,
    ).reshape(n // GROUP, 1, WIDE)
    goal = jnp.arange(LEVELS)[None, :] * CODEBOOK + goal
    start = jnp.concatenate([jnp.zeros((n, 1), jnp.int32), goal[:, :-1]], 1).reshape(1, -1)
    goal = goal.reshape(1, -1)
    domain = jnp.broadcast_to(own(domains)[:, None], (n, LEVELS)).reshape(1, -1)
    weights, stat = begin(dp, mixer, feed, domain, goal)
    grads, embed, user, small = compute(
        users,
        position_bias.reshape(2 * BUCKETS, HEADS),
        ids,
        start,
        goal,
        domain,
        stat[:, CODES:],
        gains,
        embedding,
        weights,
    )
    spread = jnp.broadcast_to(jnp.tile(users, LANES // n)[None, :], (8, LANES))
    out, out_embed, out_user, out_small, out_ids, out_square = reduce(
        dp, grads, embed, user, small, spread
    )
    outs = update(
        (out, out_embed, out_user, out_ids, out_square, out_small),
        stat,
        (mixer, mixer_moment, mixer_square),
        (feed, feed_moment, feed_square),
        (embedding, embedding_moment, embedding_square),
        (gains, gains_moment, gains_square),
        (position_bias, bias_moment, bias_square),
    )
    loss, norm, sections, histograms = outs[:4]
    return (loss.reshape(()), norm.reshape(()), sections, histograms, *outs[4:])


def solution(mesh):
    by_dp, by_pipe, copied = P("dp"), P("pipe"), P()
    return jax.shard_map(
        shards,
        mesh=mesh,
        in_specs=(by_dp,) * 4 + (by_pipe,) * 6 + (copied,) * 9,
        out_specs=(copied,) * 4 + (by_pipe,) * 6 + (copied,) * 9 + (by_pipe,) * 2 + (copied,),
        check_vma=False,
    )
```

```python
import functools

import jax
import jax.numpy as jnp
from jax import lax
from jax.experimental import pallas as pl
from jax.experimental.pallas import tpu as pltpu
from jax.sharding import PartitionSpec as P

D = 128
HEADS = 6
HEAD_DIM = 64
FF = 1024
CODEBOOK = 256
LEVELS = 4
BUCKETS = 32
DOMAINS = 3
HIST_LEN = 81
STEP = 5
CODES = 1024
LANES = 128
WIDTH = HEADS * HEAD_DIM
MIXW = 6 * WIDTH
COLS = MIXW + 2 * FF
BLOCKS = COLS // LANES
KEYS = 96
GROUP = 4
WIDE = GROUP * LANES
PAIRS = HEADS // 2
FIRST = 4 * WIDTH
REST = COLS - FIRST
USER_ROWS = 400
MESH = pl.DeviceIdType.MESH

norm_eps = 1e-06
beta_one = 0.9
beta_two = 0.999
adam_eps = 1e-08
clip_norm = 0.5
rate_matrix = 0.04
rate_gain = 0.8
rate_small = 0.3
decay_matrix = 0.01

f32 = jnp.float32
bf16 = jnp.bfloat16


def iota(shape, axis):
    return lax.broadcasted_iota(jnp.int32, shape, axis)


def mul(left, right):
    return jnp.dot(left, right, preferred_element_type=f32)


def mul_t(left, right):
    return lax.dot_general(left, right, (((1,), (1,)), ((), ())), preferred_element_type=f32)


def mul_exact(left, right):
    return jnp.dot(left, right, preferred_element_type=f32, precision=lax.Precision.HIGHEST)


def onehot(ids, rows):
    return jnp.where(iota((rows, ids.shape[1]), 0) == ids, 1.0, 0.0).astype(bf16)


def inverse_rms(x):
    return lax.rsqrt(jnp.mean(x * x, axis=0, keepdims=True) + norm_eps)


def norm_low(x, inverse, gain):
    return (x * inverse * gain).astype(bf16)


def norm_back(x, inverse, gain, upstream):
    scaled = x * inverse
    inner = upstream * gain
    back = inverse * (inner - scaled * jnp.mean(inner * scaled, axis=0, keepdims=True))
    return back, upstream * scaled


def block_diag(pair):
    zero = jnp.zeros((HEAD_DIM, LANES), pair.dtype)
    left = jnp.concatenate([pair[:HEAD_DIM], zero], 0)
    right = jnp.concatenate([zero, pair[HEAD_DIM:]], 0)
    return jnp.concatenate([left, right], 1)


def diagonal(both):
    return jnp.concatenate([both[:HEAD_DIM, :LANES], both[HEAD_DIM:, LANES:]], 0)


def pad_keys(table):
    if table.shape[0] == LANES:
        return table
    zero = jnp.zeros((LANES - table.shape[0], table.shape[1]), table.dtype)
    return jnp.concatenate([table, zero], 0)


def attend(keys, query, values, bias):
    scores = mul(keys, block_diag(query)) + bias
    top = jnp.max(scores, axis=0, keepdims=True)
    chance = jnp.exp(scores - top)
    total = jnp.sum(chance, axis=0, keepdims=True)
    chance = (chance * (1.0 / total)).astype(bf16)
    mixed = diagonal(mul(values, pad_keys(chance))).astype(bf16)
    return chance, mixed


def attend_back(keys_t, query, values, back_mixed, chance):
    exact = chance.astype(f32)
    spread = block_diag(back_mixed)
    back_chance = mul(values, spread)
    inner = jnp.sum(back_chance * exact, axis=0, keepdims=True)
    back_scores = exact * (back_chance - inner)
    low = pad_keys(back_scores.astype(bf16))
    back_query = diagonal(mul(keys_t, low)).astype(bf16)
    back_keys = mul_t(block_diag(query), low).astype(bf16)
    back_values = mul_t(spread, pad_keys(chance)).astype(bf16)
    return back_query, back_keys, back_values, back_scores


def split_low(x):
    high = x.astype(bf16)
    return jnp.concatenate([high, (x - high.astype(f32)).astype(bf16)], 0)


def stages(dp):
    order = []
    bit = 1
    while bit < dp:
        order.append(("dp", bit))
        bit *= 2
    return order + [("pipe", 1)]


def side_of(stage):
    axis, bit = stage
    return lax.rem(lax.div(lax.axis_index(axis), bit), 2)


def partner_of(stage):
    axis, bit = stage
    return {axis: lax.axis_index(axis) + bit * (1 - 2 * side_of(stage))}


def shares(order, rows):
    held = [rows]
    for stage in order:
        held.append(held[-1] // 2 if held[-1] % 32 == 0 else held[-1])
    return held


def span(start, size):
    return pl.ds(pl.multiple_of(start, 16), size)


def step_kernel(n, dp, *refs):
    codes_ref, users_ref, user_row_ref, targets_ref, domains_ref, bias_ref, gains_ref = refs[:7]
    mixer_ref, feed_ref, embed_ref = refs[7:10]
    out_ref, out_user_ref, out_ids_ref, out_square_ref, out_small_ref, out_stat_ref = refs[10:16]
    x0_s, x1_s, x2_s, qkv_s, p_s, o_s, r_s, mem_s, dz_s, wn_s, wt_s, ext_s, table_s = refs[16:29]
    gain_s, ebias_s, dbias_s, g0_s, ge_s, gbias_s, ggain_s, rows_s, user_s, ids_s = refs[29:39]
    cross_s, cross_back_s, pc_s, oc_s, rest_s, first_s, codes_s, slot_s, user_low_s = refs[39:48]
    stat_s, stat_land, small_s, small_land, local_sems, sends, recvs = refs[48:55]
    lands = refs[55:]
    order = stages(dp)
    across = order[-1]
    depth = len(order)
    chunks = n // GROUP
    section = lax.axis_index("pipe")
    used = [0]

    def remote(source, target, stage):
        index = used[0]
        used[0] += 1
        return pltpu.make_async_remote_copy(
            src_ref=source,
            dst_ref=target,
            send_sem=sends.at[index],
            recv_sem=recvs.at[index],
            device_id=partner_of(stage),
            device_id_type=MESH,
        )

    locals_in = []
    for block in range(BLOCKS):
        lanes = slice(block * LANES, (block + 1) * LANES)
        if block < MIXW // LANES:
            source = mixer_ref.at[0, :, lanes]
        else:
            source = feed_ref.at[0, :, slice(lanes.start - MIXW, lanes.stop - MIXW)]
        locals_in.append(pltpu.make_async_copy(source, g0_s.at[block], local_sems.at[block]))
    vocabulary = embed_ref.shape[0]
    flat = x2_s.at[pl.ds(0, vocabulary)]
    load_embed = pltpu.make_async_copy(embed_ref, flat, local_sems.at[BLOCKS])
    for copy in locals_in:
        copy.start()
    load_embed.start()

    barrier = pltpu.get_barrier_semaphore()
    for stage in order:
        pl.semaphore_signal(barrier, inc=1, device_id=partner_of(stage), device_id_type=MESH)
    pl.semaphore_wait(barrier, depth)

    scale = HEAD_DIM**-0.5
    cross_scale = jnp.where(section == 1, scale, 1.0).astype(f32)
    for copy in locals_in:
        copy.wait()
    for block in range(BLOCKS):
        value = g0_s[block]
        if block < 3:
            value = value * scale
        elif 12 <= block < 15:
            value = value * cross_scale
        wn_s[section, :, block * LANES : (block + 1) * LANES] = value.astype(bf16)
    half = D // 2
    mine = span(side_of(order[0]) * half, half)
    over = remote(wn_s.at[section, mine], wn_s.at[section, mine], across)
    over.start()

    ids_s[:, : HIST_LEN - 1] = codes_ref[pl.ds(pl.multiple_of(section * n, 8), n), :]
    lane, row = iota((n, LANES), 1), iota((n, LANES), 0)
    ids = ids_s[...] + ((lane & 3) << 8)
    ids = jnp.where(lane < HIST_LEN - 1, ids, jnp.where(lane == HIST_LEN - 1, CODES + row, -1))
    ids_s[...] = ids
    count = targets_ref.shape[1]
    history, token = iota((count, LANES), 0), iota((count, LANES), 1)
    pick = jnp.where((token >> 2) + section * n == history, 1.0, 0.0)
    level, place = iota((LEVELS, LANES), 0), iota((LEVELS, LANES), 1) & 3
    target = mul(targets_ref[...].astype(f32), pick) + (level * CODEBOOK).astype(f32)
    goal = jnp.sum(jnp.where(level == place, target, 0.0), axis=0, keepdims=True).astype(jnp.int32)
    start_ids = jnp.sum(
        jnp.where(level == place - 1, target, 0.0), axis=0, keepdims=True
    ).astype(jnp.int32)
    domain = mul(domains_ref[...].astype(f32), pick)
    pick = jnp.where(lax.rem(token, n) + section * n == history, 1.0, 0.0)
    own_users = mul_exact(user_row_ref[...].astype(f32), pick)

    counts = [
        jnp.sum(jnp.where(domain == d, 1.0, 0.0), axis=1, keepdims=True) for d in range(DOMAINS)
    ]
    counts += [jnp.zeros((1, 1), f32)] * (8 - DOMAINS)
    stat_s[0, :, CODES:] = jnp.broadcast_to(jnp.concatenate(counts, 0), (8, LANES))
    stat_s[0, :, :CODES] = mul_t(jnp.ones((8, LANES), bf16), onehot(goal, CODES))
    slot = 0
    for k, stage in enumerate(order):
        slot = slot + side_of(stage) * 2 ** (depth - 1 - k)
    owner = iota((8, LANES), 1) // n
    own_users = jnp.broadcast_to(own_users, (8, LANES)).astype(jnp.int32)
    slot_s[...] = jnp.where(owner == lax.rem(slot, LANES // n), own_users, 0)
    store_ids = pltpu.make_async_copy(slot_s, out_ids_ref.at[slot], local_sems.at[BLOCKS + 1])
    store_ids.start()
    store_ids.wait()

    def slots_of(j):
        return pl.ds(lax.div(slot, 2**j) * 2**j, 2**j)

    early = []
    for j, stage in enumerate(reversed(order)):
        held = out_ids_ref.at[slots_of(j)]
        early.append(
            (
                remote(stat_s.at[j], stat_land.at[j], stage),
                remote(held, held, stage),
            )
        )

    def early_step(j):
        if j > 0:
            for copy in early[j - 1]:
                copy.wait()
            stat_s[j] = stat_s[j - 1] + stat_land[j - 1]
        if j < depth:
            for copy in early[j]:
                copy.start()

    eye = jnp.where(iota((LANES, LANES), 0) == iota((LANES, LANES), 1), 1.0, 0.0).astype(bf16)
    load_embed.wait()

    def fetch(i, carry):
        user_s[pl.ds(i, 1), :] = x2_s[pl.ds(CODES + users_ref[section * n + i], 1), :]
        return carry

    lax.fori_loop(0, n, fetch, 0)
    for block in range(CODES // LANES + 1):
        if block < CODES // LANES:
            rows = x2_s[block * LANES : (block + 1) * LANES, :]
            table_s[block * LANES : (block + 1) * LANES, :] = rows.astype(bf16)
            width = LANES
        else:
            rows = user_s[...]
            width = n
        high = rows.astype(bf16)
        low = (rows - high.astype(f32)).astype(bf16)
        lanes = slice(block * LANES, block * LANES + width)
        ext_s[:D, lanes] = mul_t(eye, high).astype(bf16)
        ext_s[D:, lanes] = mul_t(eye, low).astype(bf16)

    def lookup(c, carry):
        ids = jnp.concatenate([ids_s[pl.ds(GROUP * c + i, 1), :] for i in range(GROUP)], 1)
        both = mul(ext_s[...], onehot(ids, CODES + n))
        x0_s[c] = both[:D] + both[D:]
        return carry

    lax.fori_loop(0, chunks, lookup, 0)

    for g in range(7):
        gain_s[g] = jnp.broadcast_to(gains_ref[g : g + 1, :], (LANES, LANES)).T

    def positions(axis):
        index = iota((KEYS, LANES), axis)
        return jnp.where(index == HIST_LEN - 1, 0, index + 1)

    key, query = positions(0), positions(1)
    distance = jnp.abs(query - key)
    remoteness = jnp.zeros_like(distance)
    for edge in (12, 16, 23, 32, 46, 64, 91):
        remoteness = remoteness + (distance >= edge).astype(jnp.int32)
    nearby = jnp.minimum(jnp.where(distance < 8, distance, 8 + remoteness), 15)
    buckets = nearby + jnp.where(key > query, 16, 0)
    real = iota((KEYS, LANES), 0) < HIST_LEN
    for head in range(HEADS):
        lanes = slice((head % 2) * LANES, (head % 2 + 1) * LANES)

        def choose(b, table):
            return jnp.where(buckets == b, bias_ref[head, 0, b], table)

        table = lax.fori_loop(0, BUCKETS, choose, jnp.zeros((KEYS, LANES), f32))
        ebias_s[head // 2, :, lanes] = jnp.where(real, table, -1e30)
    key, query = iota((LANES, LANES), 0), iota((LANES, LANES), 1)
    offset = query - key
    seen = ((key >> 2) == (query >> 2)) & (offset >= 0)
    for head in range(HEADS):
        lanes = slice((head % 2) * LANES, (head % 2 + 1) * LANES)
        table = jnp.full((LANES, LANES), -1e30, f32)
        for b in range(LEVELS):
            table = jnp.where(seen & (offset == b), bias_ref[head, 1, b], table)
        dbias_s[head // 2, :, lanes] = table

    def transpose_weights(which):
        for block in range(BLOCKS):
            place = slice(block * LANES, (block + 1) * LANES)
            wt_s[which, place, :] = mul_t(eye, wn_s[which, :, place]).astype(bf16)

    transpose_weights(section)
    over.wait()
    came = wn_s.at[1 - section, mine]
    beside = remote(came, came, order[0])
    beside.start()
    beside.wait()
    transpose_weights(1 - section)

    def gain(g, width):
        column = gain_s[g]
        return column if width == LANES else jnp.concatenate([column] * (width // LANES), 1)

    def encode(c, carry):
        for j in range(depth + 1):
            pl.when(c == j)(functools.partial(early_step, j))
        x0 = x0_s[c]
        h = norm_low(x0, inverse_rms(x0), gain(0, WIDE))
        for j in range(3):
            part = slice(j * WIDTH, (j + 1) * WIDTH)
            qkv_s[c, part, :] = mul(wt_s[0, part, :], h).astype(bf16)
        for i in range(GROUP):
            lanes = slice(i * LANES, (i + 1) * LANES)
            natural = mul_t(eye, h[:, lanes]).astype(bf16)[:KEYS]
            keys = mul(natural, wn_s[0, :, WIDTH : 2 * WIDTH]).astype(bf16)
            for j in range(PAIRS):
                part = slice(j * LANES, (j + 1) * LANES)
                chance, mixed = attend(
                    keys[:, part],
                    qkv_s[c, part, lanes],
                    qkv_s[c, 2 * WIDTH + j * LANES : 2 * WIDTH + (j + 1) * LANES, lanes],
                    ebias_s[j],
                )
                p_s[GROUP * c + i, j] = chance
                o_s[c, part, lanes] = mixed
        x1 = x0 + mul(wn_s[0, :, 3 * WIDTH : 4 * WIDTH], o_s[c])
        x1_s[c] = x1
        h = norm_low(x1, inverse_rms(x1), gain(1, WIDE))
        for j in range(2):
            part = slice(j * FF // 2, (j + 1) * FF // 2)
            lifted = mul(wt_s[0, MIXW + j * FF // 2 : MIXW + (j + 1) * FF // 2, :], h)
            r_s[c, part, :] = jnp.maximum(lifted, 0.0).astype(bf16)
        x2 = x1 + mul(wn_s[0, :, MIXW + FF :], r_s[c])
        put_wide(x2_s, c, x2)
        e = norm_low(x2, inverse_rms(x2), gain(2, WIDE))
        for j in range(2):
            part = slice(j * WIDTH, (j + 1) * WIDTH)
            mem_s[c, part, :] = mul(
                wt_s[0, 4 * WIDTH + j * WIDTH : 4 * WIDTH + (j + 1) * WIDTH, :], e
            ).astype(bf16)
        return carry

    def put_wide(ref, c, value):
        for i in range(GROUP):
            ref[pl.ds(pl.multiple_of((GROUP * c + i) * D, D), D), :] = value[
                :, i * LANES : (i + 1) * LANES
            ]

    def get_wide(ref, c):
        return jnp.concatenate(
            [ref[pl.ds(pl.multiple_of((GROUP * c + i) * D, D), D), :] for i in range(GROUP)], 1
        )

    lax.fori_loop(0, chunks, encode, 0)
    for j in range(chunks, depth + 1):
        early_step(j)
    out_stat_ref[...] = stat_s[depth, :1, :CODES]

    def put_blocks(first, value):
        for index in range(value.shape[1] // LANES):
            block = first + index
            part = value[:, index * LANES : (index + 1) * LANES].astype(bf16)
            if block < FIRST // LANES:
                first_s[1, block * D : (block + 1) * D, :] = part
            else:
                block -= FIRST // LANES
                rest_s[1, block * D : (block + 1) * D, :] = part

    def add_blocks(first, value):
        for index in range(value.shape[1] // LANES):
            g0_s[first + index] += value[:, index * LANES : (index + 1) * LANES]

    start = onehot(start_ids, CODES)
    both = mul(ext_s[:, :CODES], start)
    y0 = both[:D] + both[D:]
    inverse0 = inverse_rms(y0)
    h0 = norm_low(y0, inverse0, gain(3, LANES))
    dz_s[:, :LANES] = mul(wt_s[1, : 3 * WIDTH, :], h0).astype(bf16)
    both = mul(mul_t(eye, h0).astype(bf16), wn_s[1, :, WIDTH : 3 * WIDTH]).astype(bf16)
    self_chance = []
    mixed_parts = []
    for j in range(PAIRS):
        part = slice(j * LANES, (j + 1) * LANES)
        chance, mixed = attend(
            both[:, part],
            dz_s[part, :LANES],
            dz_s[2 * WIDTH + j * LANES : 2 * WIDTH + (j + 1) * LANES, :LANES],
            dbias_s[j],
        )
        self_chance.append(chance)
        mixed_parts.append(mixed)
    self_values = both[:, WIDTH:]
    self_mixed = jnp.concatenate(mixed_parts, 0)
    y1 = y0 + mul(wn_s[1, :, 3 * WIDTH : 4 * WIDTH], self_mixed)
    inverse1 = inverse_rms(y1)
    h1 = norm_low(y1, inverse1, gain(4, LANES))
    cross_s[...] = mul(wt_s[1, 4 * WIDTH : 5 * WIDTH, :], h1).astype(bf16)

    def rows_of(g, table):
        row, token = iota((LANES, LANES), 0), iota((LANES, LANES), 1)
        rep = jnp.where(token == 16 * g + 4 * (row >> 5) + (row & 3), 1.0, 0.0).astype(bf16)
        rows = mul_t(rep, table)
        mask = (iota(rows.shape, 1) >> 6) == ((iota(rows.shape, 0) & 31) >> 2)
        return jnp.where(mask, rows, 0.0).astype(bf16)

    def head_mask(shape):
        return (iota(shape, 0) >> 6) == ((iota(shape, 1) & 31) >> 2)

    def rows_t_of(g, table):
        token, row = iota((LANES, LANES), 0), iota((LANES, LANES), 1)
        rep = jnp.where(token == 16 * g + 4 * (row >> 5) + (row & 3), 1.0, 0.0).astype(bf16)
        rows = mul(table, rep)
        return jnp.where(head_mask(rows.shape), rows, 0.0).astype(bf16)

    def gather_rows(ref):
        total = jnp.zeros((WIDTH, LANES), f32)
        for g in range(chunks):
            row, token = iota((LANES, LANES), 0), iota((LANES, LANES), 1)
            rep = jnp.where(token == 16 * g + 4 * (row >> 5) + (row & 3), 1.0, 0.0).astype(bf16)
            total = total + mul(ref[g], rep)
        return total.astype(bf16)

    def blocks_of(table):
        owner = iota(table.shape, 0) >> 5
        zero = jnp.zeros_like(table)
        return jnp.concatenate(
            [jnp.where(owner == j, table, zero) for j in range(GROUP)], 1
        ).astype(bf16)

    def cross(g, carry):
        queries = rows_of(g, cross_s[...])
        parts = []
        for j in range(GROUP):
            parts.append(
                mul(
                    queries[32 * j : 32 * j + 32],
                    mem_s[g, :WIDTH, j * LANES : (j + 1) * LANES],
                )
            )
        scores = jnp.concatenate(parts, 0)
        scores = jnp.where(iota(scores.shape, 1) < HIST_LEN, scores, -1e30)
        chance = jnp.exp(scores - jnp.max(scores, axis=1, keepdims=True))
        chance = chance * (1.0 / jnp.sum(chance, axis=1, keepdims=True))
        pc_s[g] = chance
        mixed = mul_t(mem_s[g, WIDTH:, :], blocks_of(chance))
        oc_s[g] = jnp.where(head_mask(mixed.shape), mixed, 0.0).astype(bf16)
        return carry

    lax.fori_loop(0, chunks, cross, 0)
    cross_mixed = gather_rows(oc_s)
    y2 = y1 + mul(wn_s[1, :, 5 * WIDTH : 6 * WIDTH], cross_mixed)
    inverse2 = inverse_rms(y2)
    h2 = norm_low(y2, inverse2, gain(5, LANES))
    lifted = mul(wt_s[1, MIXW : MIXW + FF, :], h2)
    active = jnp.maximum(lifted, 0.0).astype(bf16)
    y3 = y2 + mul(wn_s[1, :, MIXW + FF :], active)
    inverse3 = inverse_rms(y3)
    final = norm_low(y3, inverse3, gain(6, LANES))
    logits = mul(table_s[...], final)
    top = jnp.max(logits, axis=0, keepdims=True)
    log_total = top + jnp.log(jnp.sum(jnp.exp(logits - top), axis=0, keepdims=True))
    match = iota(logits.shape, 0) == goal
    picked = jnp.sum(jnp.where(match, logits, 0.0), axis=0, keepdims=True)
    weight = jnp.zeros((1, LANES), f32)
    for d in range(DOMAINS):
        share = 1.0 / (DOMAINS * jnp.maximum(stat_s[depth, d : d + 1, CODES:], 1.0))
        weight = weight + jnp.where(domain == d, share, 0.0)
    loss = jnp.sum(weight * (log_total - picked), axis=1, keepdims=True)
    back_logits = (
        weight * (jnp.exp(logits - log_total) - jnp.where(match, 1.0, 0.0))
    ).astype(bf16)
    back_final = mul(ext_s[:D, :CODES], back_logits)
    table_grad = mul_t(back_logits, final)
    back, gain_grad = norm_back(y3, inverse3, gain(6, LANES), back_final)
    ggain_s[6] = gain_grad
    low = back.astype(bf16)
    put_blocks(26, mul_t(low, active))
    back_lifted = jnp.where(lifted > 0, mul(wt_s[1, MIXW + FF :, :], low), 0.0).astype(bf16)
    put_blocks(18, mul_t(h2, back_lifted))
    more, gain_grad = norm_back(
        y2, inverse2, gain(5, LANES), mul(wn_s[1, :, MIXW : MIXW + FF], back_lifted)
    )
    ggain_s[5] = gain_grad
    back = back + more
    low = back.astype(bf16)
    put_blocks(15, mul_t(low, cross_mixed))
    cross_back_s[...] = mul(wt_s[1, 5 * WIDTH : 6 * WIDTH, :], low).astype(bf16)

    def cross_back(g, carry):
        mixed_rows = rows_of(g, cross_back_s[...])
        parts = []
        for j in range(GROUP):
            parts.append(
                mul(
                    mixed_rows[32 * j : 32 * j + 32],
                    mem_s[g, WIDTH:, j * LANES : (j + 1) * LANES],
                )
            )
        back_chance = jnp.concatenate(parts, 0)
        chance = pc_s[g]
        inner = jnp.sum(back_chance * chance, axis=1, keepdims=True)
        spread = blocks_of(chance * (back_chance - inner))
        total = mul_t(mem_s[g, :WIDTH, :], spread)
        mem_s[g, :WIDTH, :] = mul(rows_t_of(g, cross_s[...]), spread).astype(bf16)
        mem_s[g, WIDTH:, :] = mul(rows_t_of(g, cross_back_s[...]), blocks_of(chance)).astype(bf16)
        oc_s[g] = jnp.where(head_mask(total.shape), total, 0.0).astype(bf16)
        return carry

    lax.fori_loop(0, chunks, cross_back, 0)
    back_query = gather_rows(oc_s)
    put_blocks(12, mul_t(h1, back_query) * HEAD_DIM**-0.5)
    more, gain_grad = norm_back(
        y1, inverse1, gain(4, LANES), mul(wn_s[1, :, 4 * WIDTH : 5 * WIDTH], back_query)
    )
    ggain_s[4] = gain_grad
    back = back + more
    low = back.astype(bf16)
    put_blocks(9, mul_t(low, self_mixed))
    back_mixed = mul(wt_s[1, 3 * WIDTH : 4 * WIDTH, :], low).astype(bf16)
    self_scores = []
    for j in range(PAIRS):
        part = slice(j * LANES, (j + 1) * LANES)
        keys = slice(WIDTH + j * LANES, WIDTH + (j + 1) * LANES)
        values = slice(2 * WIDTH + j * LANES, 2 * WIDTH + (j + 1) * LANES)
        one, two, three, scores = attend_back(
            dz_s[keys, :LANES],
            dz_s[part, :LANES],
            self_values[:, part],
            back_mixed[part],
            self_chance[j],
        )
        dz_s[part, LANES : 2 * LANES] = one
        dz_s[keys, LANES : 2 * LANES] = two
        dz_s[values, LANES : 2 * LANES] = three
        self_scores.append(scores)
    put_blocks(0, mul_t(h0, dz_s[:WIDTH, LANES : 2 * LANES]) * HEAD_DIM**-0.5)
    put_blocks(3, mul_t(h0, dz_s[WIDTH:, LANES : 2 * LANES]))
    more, gain_grad = norm_back(
        y0, inverse0, gain(3, LANES), mul(wn_s[1, :, : 3 * WIDTH], dz_s[:, LANES : 2 * LANES])
    )
    ggain_s[3] = gain_grad
    back = back + more
    spread = mul_t(start, split_low(back))
    ge_s[:CODES, :] = table_grad + spread[:, :D] + spread[:, D:]
    ge_s[CODES:, :] = jnp.zeros((n, D), f32)
    rows_s[...] = jnp.zeros_like(rows_s)
    for head in range(HEADS):
        lanes = slice((head % 2) * LANES, (head % 2 + 1) * LANES)
        for b in range(LEVELS):
            hit = jnp.where(offset == b, self_scores[head // 2][:, lanes], 0.0)
            rows_s[head, BUCKETS + b : BUCKETS + b + 1, :] = jnp.sum(hit, axis=0, keepdims=True)

    def reducing(buffer, kept):
        steps, at = [], 0
        held = shares(order[:-1], buffer.shape[0])
        for k, stage in enumerate(order[:-1]):
            rows, left = held[k], held[k + 1]
            side = side_of(stage)
            if left < rows:
                source = buffer.at[span(at + (1 - side) * left, left)]
                at = at + side * left
            else:
                source = buffer.at[span(at, rows)]
            steps.append((remote(source, kept[k], stage), at, left))
        return steps, at, held

    def begin(steps, k):
        steps[k][0].start()

    def finish(steps, buffer, kept, k):
        copy, at, left = steps[k]
        copy.wait()
        place = span(at, left)
        total = buffer[place, :].astype(f32) + kept[k][...].astype(f32)
        buffer[place, :] = total.astype(bf16)

    flat_depth = depth - 1
    land = {}
    for index, name in enumerate(("rest0", "rest1", "first0", "first1", "codes")):
        land[name] = lands[index * flat_depth : (index + 1) * flat_depth]
    land_rest, land_first, land_codes = lands[5 * flat_depth :]
    rest1 = reducing(rest_s.at[1], land["rest1"])
    first1 = reducing(first_s.at[1], land["first1"])
    rest0 = reducing(rest_s.at[0], land["rest0"])
    first0 = reducing(first_s.at[0], land["first0"])
    codes = reducing(codes_s, land["codes"])

    def step1(k):
        if k > 0:
            finish(rest1[0], rest_s.at[1], land["rest1"], k - 1)
            finish(first1[0], first_s.at[1], land["first1"], k - 1)
        if k < flat_depth:
            begin(rest1[0], k)
            begin(first1[0], k)

    def crossing(buffer, target, at, rows):
        source = buffer.at[1 - section, span(at, rows)]
        return remote(source, target, across)

    cross_rest = crossing(rest_s, land_rest, rest1[1], rest1[2][-1])
    cross_first = crossing(first_s, land_first, first1[1], first1[2][-1])

    def settle(copy, buffer, landed, at, rows, base):
        copy.wait()
        value = (buffer[section, span(at, rows), :].astype(f32) + landed[...].astype(f32)).astype(
            bf16
        )
        out_ref[span(base + at, rows), :] = value
        value = value.astype(f32)
        return jnp.sum(value * value, axis=0, keepdims=True)

    def gathering(base, at, held):
        steps = []
        for k in reversed(range(flat_depth)):
            rows, left = held[k], held[k + 1]
            if left < rows:
                place = out_ref.at[span(base + at, left)]
                steps.append(remote(place, place, order[k]))
                at = at - side_of(order[k]) * left
            else:
                steps.append(None)
        return steps

    gather_rest = gathering(0, rest1[1], rest1[2])
    gather_first = gathering(REST, first1[1], first1[2])

    def step0(k):
        if k > 0 and k <= flat_depth:
            finish(rest0[0], rest_s.at[0], land["rest0"], k - 1)
        if k < flat_depth:
            begin(rest0[0], k)
        if k == flat_depth:
            cross_rest.start()
        if k == flat_depth + 1:
            squares = settle(cross_rest, rest_s, land_rest, rest1[1], rest1[2][-1], 0)
            out_square_ref[slot, 0:1, :] = squares / (dp * rest1[2][-1] // REST)
        if k > flat_depth + 1 and gather_rest[k - flat_depth - 2] is not None:
            gather_rest[k - flat_depth - 2].wait()
        if flat_depth < k < 2 * flat_depth + 1 and gather_rest[k - flat_depth - 1] is not None:
            gather_rest[k - flat_depth - 1].start()

    g0_s[...] = jnp.zeros_like(g0_s)
    gbias_s[...] = jnp.zeros_like(gbias_s)
    for g in range(3):
        ggain_s[g] = jnp.zeros((D, LANES), f32)

    def fold(x):
        return sum(x[:, i * LANES : (i + 1) * LANES] for i in range(GROUP))

    def back_rest(c, carry):
        for j in range(flat_depth + 1):
            pl.when(c == j)(functools.partial(step1, j))
        x2 = get_wide(x2_s, c)
        inverse = inverse_rms(x2)
        back_memory = mem_s[c]
        add_blocks(12, mul_t(norm_low(x2, inverse, gain(2, WIDE)), back_memory))
        back, gain_grad = norm_back(
            x2, inverse, gain(2, WIDE), mul(wn_s[0, :, 4 * WIDTH : 6 * WIDTH], back_memory)
        )
        ggain_s[2] += fold(gain_grad)
        low = back.astype(bf16)
        active = r_s[c]
        add_blocks(26, mul_t(low, active))
        back_active = mul(wt_s[0, MIXW + FF :, :], low)
        back_lifted = jnp.where(active.astype(f32) > 0, back_active, 0.0).astype(bf16)
        x1 = x1_s[c]
        inverse = inverse_rms(x1)
        add_blocks(18, mul_t(norm_low(x1, inverse, gain(1, WIDE)), back_lifted))
        more, gain_grad = norm_back(
            x1, inverse, gain(1, WIDE), mul(wn_s[0, :, MIXW : MIXW + FF], back_lifted)
        )
        ggain_s[1] += fold(gain_grad)
        put_wide(x2_s, c, back + more)
        return carry

    lax.fori_loop(0, chunks, back_rest, 0)
    for j in range(chunks, flat_depth + 1):
        step1(j)
    for block in range(REST // D):
        rest_s[0, block * D : (block + 1) * D, :] = g0_s[FIRST // D + block].astype(bf16)

    def back_first(c, carry):
        for j in range(min(chunks, 2 * flat_depth + 2)):
            pl.when(c == j)(functools.partial(step0, j))
        back = get_wide(x2_s, c)
        low = back.astype(bf16)
        add_blocks(9, mul_t(low, o_s[c]))
        back_mixed = mul(wt_s[0, 3 * WIDTH : 4 * WIDTH, :], low).astype(bf16)
        for i in range(GROUP):
            lanes = slice(i * LANES, (i + 1) * LANES)
            for j in range(PAIRS):
                part = slice(j * LANES, (j + 1) * LANES)
                keys = slice(WIDTH + j * LANES, WIDTH + (j + 1) * LANES)
                values = slice(2 * WIDTH + j * LANES, 2 * WIDTH + (j + 1) * LANES)
                one, two, three, scores = attend_back(
                    qkv_s[c, keys, lanes],
                    qkv_s[c, part, lanes],
                    mul_t(eye, qkv_s[c, values, lanes]).astype(bf16)[:KEYS],
                    back_mixed[part, lanes],
                    p_s[GROUP * c + i, j],
                )
                mem_s[c, part, lanes] = one
                mem_s[c, keys, lanes] = two
                r_s[c, part, lanes] = three
                gbias_s[j] += scores
        x0 = x0_s[c]
        inverse = inverse_rms(x0)
        h = norm_low(x0, inverse, gain(0, WIDE))
        add_blocks(0, mul_t(h, mem_s[c]))
        add_blocks(6, mul_t(h, r_s[c, :WIDTH, :]))
        back_normed = mul(wn_s[0, :, : 2 * WIDTH], mem_s[c])
        back_normed = back_normed + mul(wn_s[0, :, 2 * WIDTH : 3 * WIDTH], r_s[c, :WIDTH, :])
        more, gain_grad = norm_back(x0, inverse, gain(0, WIDE), back_normed)
        ggain_s[0] += fold(gain_grad)
        ids = jnp.concatenate([ids_s[pl.ds(GROUP * c + i, 1), :] for i in range(GROUP)], 1)
        spread = mul_t(onehot(ids, CODES + n), split_low(back + more))
        ge_s[...] += spread[:, :D] + spread[:, D:]
        return carry

    lax.fori_loop(0, chunks, back_first, 0)

    for block in range(FIRST // D):
        value = g0_s[block]
        if block < 3:
            value = value * HEAD_DIM**-0.5
        first_s[0, block * D : (block + 1) * D, :] = value.astype(bf16)
    codes_s[...] = ge_s[:CODES, :].astype(bf16)
    begin(first0[0], 0)
    begin(codes[0], 0)
    user_low_s[...] = ge_s[CODES:, :].astype(bf16)
    store_users = pltpu.make_async_copy(
        user_low_s, out_user_ref.at[span(slot * n, n)], local_sems.at[BLOCKS + 2]
    )
    store_users.start()

    ones = jnp.ones((8, LANES), f32)
    for g in range(7):
        small_s[0, g : g + 1, :] = mul_exact(ones, ggain_s[g].T)[:1]
    small_s[0, 7:8, :] = jnp.broadcast_to(loss, (1, LANES))

    def bucket_sums(b, carry):
        for head in range(HEADS):
            lanes = slice((head % 2) * LANES, (head % 2 + 1) * LANES)
            hit = jnp.where(buckets == b, gbias_s[head // 2, :, lanes], 0.0)
            rows_s[head, pl.ds(b, 1), :] = jnp.sum(hit, axis=0, keepdims=True)
        return carry

    lax.fori_loop(0, BUCKETS, bucket_sums, 0)
    for head in range(HEADS):
        small_s[0, 8 + head : 9 + head, :] = mul_exact(ones, rows_s[head].T)[:1]
    small_s[0, 8 + HEADS :, :] = jnp.zeros((8 - HEADS, LANES), f32)

    small_steps = [remote(small_s.at[k], small_land.at[k], stage) for k, stage in enumerate(order)]
    small_steps[0].start()
    done = min(chunks, 2 * flat_depth + 2)
    for k in range(flat_depth):
        finish(first0[0], first_s.at[0], land["first0"], k)
        finish(codes[0], codes_s, land["codes"], k)
        small_steps[k].wait()
        small_s[k + 1] = small_s[k] + small_land[k]
        small_steps[k + 1].start()
        if k + 1 < flat_depth:
            begin(first0[0], k + 1)
            begin(codes[0], k + 1)
        if done < 2 * flat_depth + 2:
            step0(done)
            done += 1
    while done < 2 * flat_depth + 2:
        step0(done)
        done += 1
    at, rows = codes[1], codes[2][-1]
    left = rows // 2 if rows % 32 == 0 else rows
    side = side_of(across)
    cross_first.start()
    if left < rows:
        source = codes_s.at[span(at + (1 - side) * left, left)]
        at = at + side * left
    else:
        source = codes_s.at[span(at, rows)]
    cross_codes = remote(source, land_codes, across)
    cross_codes.start()
    squares = settle(cross_first, first_s, land_first, first1[1], first1[2][-1], REST)
    out_square_ref[slot, 1:2, :] = squares / (dp * first1[2][-1] // FIRST)
    cross_codes.wait()
    value = codes_s[span(at, left), :].astype(f32) + land_codes[...].astype(f32)
    value = value.astype(bf16)
    out_ref[span(COLS + at, left), :] = value
    value = value.astype(f32)
    squares = jnp.sum(value * value, axis=0, keepdims=True)
    out_square_ref[slot, 2:3, :] = squares / (2 * dp * left // CODES)
    out_square_ref[slot, 3:, :] = jnp.zeros((5, LANES), f32)
    small_steps[depth - 1].wait()
    out_small_ref[...] = small_s[depth - 1] + small_land[depth - 1]

    store_users.wait()
    for j, stage in enumerate(reversed(order)):
        copies = []
        if j == 0:
            if left < rows:
                place = out_ref.at[span(COLS + at, left)]
                copies.append(remote(place, place, stage))
                at = at - side * left
        else:
            k = flat_depth - j
            rows, left = codes[2][k], codes[2][k + 1]
            if left < rows:
                place = out_ref.at[span(COLS + at, left)]
                copies.append(remote(place, place, stage))
                at = at - side_of(stage) * left
            if gather_first[j - 1] is not None:
                copies.append(gather_first[j - 1])
        held = out_square_ref.at[slots_of(j)]
        copies.append(remote(held, held, stage))
        start_row = lax.div(slot, 2**j) * 2**j * n
        held = out_user_ref.at[span(start_row, 2**j * n)]
        copies.append(remote(held, held, stage))
        for copy in copies:
            copy.start()
        for copy in copies:
            copy.wait()


def gradients(codes, users, targets, domains, bias, gains, mixer, feed, embedding, dp):
    n = users.shape[0] // 2
    chunks = n // GROUP
    order = stages(dp)
    depth = len(order)
    devices = 2 * dp
    vmem = pl.BlockSpec(memory_space=pltpu.VMEM)
    smem = pl.BlockSpec(memory_space=pltpu.SMEM)
    hbm = pl.BlockSpec(memory_space=pl.ANY)
    stat = (8, CODES + LANES)
    lands = []
    for rows in (REST, REST, FIRST, FIRST, CODES):
        held = shares(order[:-1], rows)
        lands += [pltpu.VMEM((left, D), bf16) for left in held[1:]]
    last = [shares(order[:-1], rows)[-1] for rows in (REST, FIRST)]
    last.append(shares(order, CODES)[-1])
    lands += [pltpu.VMEM((left, D), bf16) for left in last]
    copies = 16 * depth + 16
    return pl.pallas_call(
        functools.partial(step_kernel, n, dp),
        out_shape=(
            jax.ShapeDtypeStruct((COLS + CODES, D), bf16),
            jax.ShapeDtypeStruct((devices * n, D), bf16),
            jax.ShapeDtypeStruct((devices, 8, LANES), jnp.int32),
            jax.ShapeDtypeStruct((devices, 8, LANES), f32),
            jax.ShapeDtypeStruct((16, LANES), f32),
            jax.ShapeDtypeStruct((1, CODES), f32),
        ),
        in_specs=[vmem, smem, vmem, vmem, vmem, smem, vmem, hbm, hbm, hbm],
        out_specs=(vmem, hbm, hbm, vmem, vmem, vmem),
        scratch_shapes=[
            pltpu.VMEM((chunks, D, WIDE), f32),
            pltpu.VMEM((chunks, D, WIDE), f32),
            pltpu.VMEM((n * D, LANES), f32),
            pltpu.VMEM((chunks, 3 * WIDTH, WIDE), bf16),
            pltpu.VMEM((n, PAIRS, KEYS, 2 * LANES), bf16),
            pltpu.VMEM((chunks, WIDTH, WIDE), bf16),
            pltpu.VMEM((chunks, FF, WIDE), bf16),
            pltpu.VMEM((chunks, 2 * WIDTH, WIDE), bf16),
            pltpu.VMEM((3 * WIDTH, 2 * LANES), bf16),
            pltpu.VMEM((2, D, COLS), bf16),
            pltpu.VMEM((2, COLS, D), bf16),
            pltpu.VMEM((2 * D, CODES + n), bf16),
            pltpu.VMEM((CODES, D), bf16),
            pltpu.VMEM((7, D, LANES), f32),
            pltpu.VMEM((PAIRS, KEYS, 2 * LANES), f32),
            pltpu.VMEM((PAIRS, LANES, 2 * LANES), f32),
            pltpu.VMEM((BLOCKS, D, LANES), f32),
            pltpu.VMEM((CODES + n, D), f32),
            pltpu.VMEM((PAIRS, KEYS, 2 * LANES), f32),
            pltpu.VMEM((7, D, LANES), f32),
            pltpu.VMEM((HEADS, LANES, LANES), f32),
            pltpu.VMEM((n, D), f32),
            pltpu.VMEM((n, LANES), jnp.int32),
            pltpu.VMEM((WIDTH, LANES), bf16),
            pltpu.VMEM((WIDTH, LANES), bf16),
            pltpu.VMEM((chunks, LANES, LANES), f32),
            pltpu.VMEM((chunks, WIDTH, LANES), bf16),
            pltpu.VMEM((2, REST, D), bf16),
            pltpu.VMEM((2, FIRST, D), bf16),
            pltpu.VMEM((CODES, D), bf16),
            pltpu.VMEM((8, LANES), jnp.int32),
            pltpu.VMEM((n, D), bf16),
            pltpu.VMEM((depth + 1,) + stat, f32),
            pltpu.VMEM((depth,) + stat, f32),
            pltpu.VMEM((depth, 16, LANES), f32),
            pltpu.VMEM((depth, 16, LANES), f32),
            pltpu.SemaphoreType.DMA((BLOCKS + 3,)),
            pltpu.SemaphoreType.DMA((copies,)),
            pltpu.SemaphoreType.DMA((copies,)),
        ]
        + lands,
        compiler_params=pltpu.CompilerParams(
            collective_id=0, has_side_effects=True, vmem_limit_bytes=63 * 2**20
        ),
        name="gradients",
    )(codes, users, users.reshape(1, -1), targets, domains, bias, gains, mixer, feed, embedding)


def adam(weight, moment, square, slope, rate, decay):
    moment = beta_one * moment + (1 - beta_one) * slope
    square = beta_two * square + (1 - beta_two) * slope * slope
    unbiased_moment = moment * (1 / (1 - beta_one**STEP))
    unbiased_square = square * (1 / (1 - beta_two**STEP))
    step = unbiased_moment / (jnp.sqrt(unbiased_square) + adam_eps) + decay * weight
    return weight - rate * step, moment, square


def update_kernel(*refs):
    parts_in, big_in, small_in, refs = refs[:6], refs[6:15], refs[15:21], refs[21:]
    loss_ref, norm_ref, section_ref, hist_ref = refs[:4]
    big_out, small_out, low_out, refs = refs[4:13], refs[13:19], refs[19:22], refs[22:]
    parts, hold, low_hold = refs[:6], refs[6:15], refs[15:18]
    user_grad, part_sems, in_sems, out_sems = refs[18:]
    grad_ref, user_ref, ids_ref, square_ref, small_ref, stat_ref = parts
    arrivals = [pltpu.make_async_copy(parts_in[i], parts[i], part_sems.at[i]) for i in range(6)]
    loads = [pltpu.make_async_copy(big_in[i], hold[i], in_sems.at[i]) for i in range(9)]
    for load in arrivals[1:] + arrivals[:1] + loads:
        load.start()
    for arrival in arrivals:
        arrival.wait()

    users = user_grad.shape[0]
    span = min(1024, user_ref.shape[0])
    slots = span // LANES * (ids_ref.shape[0] * LANES // user_ref.shape[0])
    fit = ids_ref.shape[0] * LANES // user_ref.shape[0]
    user_grad[...] = jnp.zeros_like(user_grad)

    def scatter(part, carry):
        rows = user_ref[pl.ds(pl.multiple_of(part * span, span), span), :]
        lanes = []
        for group in range(span // LANES):
            total = ids_ref[part * slots + group * fit, :1, :]
            for other in range(1, fit):
                total = total + ids_ref[part * slots + group * fit + other, :1, :]
            lanes.append(total)
        ids = jnp.concatenate(lanes, 1)
        for block in range(users // USER_ROWS):
            place = slice(block * USER_ROWS, (block + 1) * USER_ROWS)
            hit = iota((USER_ROWS, span), 0) + block * USER_ROWS == ids
            user_grad[place, :] += mul(jnp.where(hit, 1.0, 0.0).astype(bf16), rows)
        return carry

    lax.fori_loop(0, user_ref.shape[0] // span, scatter, 0)

    def total(x):
        return jnp.sum(jnp.sum(x, axis=0, keepdims=True), axis=1, keepdims=True)

    devices = square_ref.shape[0]
    slot = iota((devices, 8, LANES), 0)
    row = iota((devices, 8, LANES), 1)
    squares = square_ref[...]
    side = lax.rem(slot, 2)
    section_squares = [
        total(jnp.sum(jnp.where((row < 2) & (side == s), squares, 0.0), axis=0)) for s in range(2)
    ]
    rest = total(jnp.sum(jnp.where(row == 2, squares, 0.0), axis=0))
    user_values = user_grad[...]
    rest = rest + total(user_values * user_values)
    small = small_ref[...]
    lane, line = iota(small.shape, 1), iota(small.shape, 0)
    counted = (line < 7) | ((line > 7) & (lane < 2 * BUCKETS))
    small_kept = jnp.where(counted, small, 0.0)
    rest = rest + total(small_kept * small_kept)
    norm = jnp.sqrt(section_squares[0] + section_squares[1] + rest)
    factor = jnp.minimum(1.0, clip_norm / (norm + 1e-06))
    loss_ref[0] = small[7, 0]
    norm_ref[0] = norm[0, 0]
    for s in range(2):
        section_ref[s] = jnp.sqrt(section_squares[s])[0, 0]
    for level in range(LEVELS):
        hist_ref[level : level + 1, :] = stat_ref[
            :1, level * CODEBOOK : (level + 1) * CODEBOOK
        ]

    outs = adam(
        small_in[0][...], small_in[1][...], small_in[2][...], factor * small[:7], rate_gain, 0.0
    )
    for ref, value in zip(small_out[:3], outs):
        ref[...] = value
    for head in range(HEADS):
        for s in range(2):
            slope = factor * small[8 + head : 9 + head, s * BUCKETS : (s + 1) * BUCKETS]
            one = slice(s, s + 1)
            outs = adam(
                small_in[3][head, one, :],
                small_in[4][head, one, :],
                small_in[5][head, one, :],
                slope,
                rate_small,
                0.0,
            )
            for ref, value in zip(small_out[3:], outs):
                ref[head, one, :] = value

    stores = []

    def store(kind, place):
        first = 3 * kind
        pieces = [(hold[first + i], big_out[first + i]) for i in range(3)]
        pieces.append((low_hold[kind], low_out[kind]))
        for source, target in pieces:
            copy = pltpu.make_async_copy(
                source.at[place], target.at[place], out_sems.at[len(stores)]
            )
            copy.start()
            stores.append(copy)

    def step(kind, place, slope):
        first = 3 * kind
        outs = adam(
            hold[first][place],
            hold[first + 1][place],
            hold[first + 2][place],
            factor * slope,
            rate_matrix,
            decay_matrix,
        )
        for i in range(3):
            hold[first + i][place] = outs[i]
        low_hold[kind][place] = outs[0].astype(bf16)

    def block_of(block):
        first = FIRST // D
        place = block - first if block >= first else REST // D + block
        return grad_ref[place * D : (place + 1) * D, :].astype(f32)

    for i in range(3):
        loads[i].wait()
    for part in range(6):
        for block in range(3 * part, 3 * part + 3):
            lanes = slice(block * LANES, (block + 1) * LANES)
            step(0, (0, slice(None), lanes), block_of(block))
        store(0, (0, slice(None), slice(3 * part * LANES, 3 * (part + 1) * LANES)))
    for i in range(3, 6):
        loads[i].wait()
    for part in range(4):
        for block in range(4 * part, 4 * part + 4):
            lanes = slice(block * LANES, (block + 1) * LANES)
            step(1, (0, slice(None), lanes), block_of(MIXW // LANES + block))
        store(1, (0, slice(None), slice(4 * part * LANES, 4 * (part + 1) * LANES)))
    for i in range(6, 9):
        loads[i].wait()
    for part in range(4):
        rows = slice(part * CODEBOOK, (part + 1) * CODEBOOK)
        step(2, (rows, slice(None)), grad_ref[COLS + rows.start : COLS + rows.stop, :].astype(f32))
        store(2, (rows, slice(None)))
    for part in range(users // USER_ROWS):
        rows = slice(part * USER_ROWS, (part + 1) * USER_ROWS)
        place = (slice(CODES + part * USER_ROWS, CODES + (part + 1) * USER_ROWS), slice(None))
        step(2, place, user_grad[rows, :])
        store(2, place)
    for copy in stores:
        copy.wait()


def update(reduced, mixers, feeds, embeds, gains, biases):
    vmem = pl.BlockSpec(memory_space=pltpu.VMEM)
    smem = pl.BlockSpec(memory_space=pltpu.SMEM)
    hbm = pl.BlockSpec(memory_space=pl.ANY)
    big = [*mixers, *feeds, *embeds]
    small = [*gains, *biases]
    low = [jax.ShapeDtypeStruct(x[0].shape, bf16) for x in (mixers, feeds, embeds)]
    users = embeds[0].shape[0] - CODES
    pieces = 4 * (6 + 4 + 4 + users // USER_ROWS)
    return pl.pallas_call(
        update_kernel,
        out_shape=[
            jax.ShapeDtypeStruct((1,), f32),
            jax.ShapeDtypeStruct((1,), f32),
            jax.ShapeDtypeStruct((2,), f32),
            jax.ShapeDtypeStruct((LEVELS, CODEBOOK), f32),
        ]
        + [jax.ShapeDtypeStruct(x.shape, f32) for x in big + small]
        + low,
        in_specs=[hbm] * 15 + [vmem] * 6,
        out_specs=[smem] * 3 + [vmem] + [hbm] * 9 + [vmem] * 6 + [hbm] * 3,
        scratch_shapes=[pltpu.VMEM(x.shape, x.dtype) for x in reduced]
        + [pltpu.VMEM(x.shape, f32) for x in big]
        + [pltpu.VMEM(x.shape, bf16) for x in low]
        + [
            pltpu.VMEM((users, D), f32),
            pltpu.SemaphoreType.DMA((6,)),
            pltpu.SemaphoreType.DMA((9,)),
            pltpu.SemaphoreType.DMA((pieces,)),
        ],
        compiler_params=pltpu.CompilerParams(vmem_limit_bytes=62 * 2**20),
        name="update",
    )(*reduced, *big, *small)


def shards(
    history_codes,
    user_ids,
    targets,
    domains,
    mixer,
    mixer_moment,
    mixer_square,
    feed,
    feed_moment,
    feed_square,
    embedding,
    embedding_moment,
    embedding_square,
    gains,
    gains_moment,
    gains_square,
    position_bias,
    bias_moment,
    bias_square,
):
    def turned(table):
        return jnp.transpose(table, (2, 0, 1))

    biases = [turned(x) for x in (position_bias, bias_moment, bias_square)]
    reduced = gradients(
        history_codes,
        user_ids,
        targets.T,
        domains.reshape(1, -1),
        biases[0],
        gains,
        mixer,
        feed,
        embedding,
        lax.axis_size("dp"),
    )
    outs = update(
        reduced,
        (mixer, mixer_moment, mixer_square),
        (feed, feed_moment, feed_square),
        (embedding, embedding_moment, embedding_square),
        (gains, gains_moment, gains_square),
        biases,
    )
    loss, norm, sections, histograms = outs[:4]
    back = [jnp.transpose(x, (1, 2, 0)) for x in outs[16:19]]
    return (
        loss.reshape(()),
        norm.reshape(()),
        sections,
        histograms,
        *outs[4:16],
        *back,
        *outs[19:],
    )


def solution(mesh):
    by_dp, by_pipe, copied = P("dp"), P("pipe"), P()
    return jax.shard_map(
        shards,
        mesh=mesh,
        in_specs=(by_dp,) * 4 + (by_pipe,) * 6 + (copied,) * 9,
        out_specs=(copied,) * 4 + (by_pipe,) * 6 + (copied,) * 9 + (by_pipe,) * 2 + (copied,),
        check_vma=False,
    )
```

```python
import functools

import jax
import jax.numpy as jnp
from jax import lax
from jax.experimental import pallas as pl
from jax.experimental.pallas import tpu as pltpu
from jax.sharding import PartitionSpec as P

D = 128
HEADS = 6
HEAD_DIM = 64
FF = 1024
CODEBOOK = 256
LEVELS = 4
BUCKETS = 32
DOMAINS = 3
HIST_LEN = 81
STEP = 5
CODES = 1024
LANES = 128
WIDTH = HEADS * HEAD_DIM
MIXW = 6 * WIDTH
COLS = MIXW + 2 * FF
BLOCKS = COLS // LANES
KEYS = 96
GROUP = 4
WIDE = GROUP * LANES
PAIRS = HEADS // 2
FIRST = 4 * WIDTH
REST = COLS - FIRST
USER_ROWS = 400
MESH = pl.DeviceIdType.MESH

norm_eps = 1e-06
beta_one = 0.9
beta_two = 0.999
adam_eps = 1e-08
clip_norm = 0.5
rate_matrix = 0.04
rate_gain = 0.8
rate_small = 0.3
decay_matrix = 0.01

f32 = jnp.float32
bf16 = jnp.bfloat16


def iota(shape, axis):
    return lax.broadcasted_iota(jnp.int32, shape, axis)


def mul(left, right):
    return jnp.dot(left, right, preferred_element_type=f32)


def mul_t(left, right):
    return lax.dot_general(left, right, (((1,), (1,)), ((), ())), preferred_element_type=f32)


def mul_exact(left, right):
    return jnp.dot(left, right, preferred_element_type=f32, precision=lax.Precision.HIGHEST)


def onehot(ids, rows):
    return jnp.where(iota((rows, ids.shape[1]), 0) == ids, 1.0, 0.0).astype(bf16)


def inverse_rms(x):
    return lax.rsqrt(jnp.mean(x * x, axis=0, keepdims=True) + norm_eps)


def norm_low(x, inverse, gain):
    return (x * inverse * gain).astype(bf16)


def norm_back(x, inverse, gain, upstream):
    scaled = x * inverse
    inner = upstream * gain
    back = inverse * (inner - scaled * jnp.mean(inner * scaled, axis=0, keepdims=True))
    return back, upstream * scaled


def block_diag(pair):
    zero = jnp.zeros((HEAD_DIM, LANES), pair.dtype)
    left = jnp.concatenate([pair[:HEAD_DIM], zero], 0)
    right = jnp.concatenate([zero, pair[HEAD_DIM:]], 0)
    return jnp.concatenate([left, right], 1)


def diagonal(both):
    return jnp.concatenate([both[:HEAD_DIM, :LANES], both[HEAD_DIM:, LANES:]], 0)


def pad_keys(table):
    if table.shape[0] == LANES:
        return table
    zero = jnp.zeros((LANES - table.shape[0], table.shape[1]), table.dtype)
    return jnp.concatenate([table, zero], 0)


def attend(keys, query, values, bias):
    scores = mul(keys, block_diag(query)) + bias
    top = jnp.max(scores, axis=0, keepdims=True)
    chance = jnp.exp(scores - top)
    total = jnp.sum(chance, axis=0, keepdims=True)
    chance = (chance * (1.0 / total)).astype(bf16)
    mixed = diagonal(mul(values, pad_keys(chance))).astype(bf16)
    return chance, mixed


def attend_back(keys_t, query, values, back_mixed, chance):
    exact = chance.astype(f32)
    spread = block_diag(back_mixed)
    back_chance = mul(values, spread)
    inner = jnp.sum(back_chance * exact, axis=0, keepdims=True)
    back_scores = exact * (back_chance - inner)
    low = pad_keys(back_scores.astype(bf16))
    back_query = diagonal(mul(keys_t, low)).astype(bf16)
    back_keys = mul_t(block_diag(query), low).astype(bf16)
    back_values = mul_t(spread, pad_keys(chance)).astype(bf16)
    return back_query, back_keys, back_values, back_scores


def split_low(x):
    high = x.astype(bf16)
    return jnp.concatenate([high, (x - high.astype(f32)).astype(bf16)], 0)


def stages(dp):
    order = []
    bit = 1
    while bit < dp:
        order.append(("dp", bit))
        bit *= 2
    return order + [("pipe", 1)]


def side_of(stage):
    axis, bit = stage
    return lax.rem(lax.div(lax.axis_index(axis), bit), 2)


def partner_of(stage):
    axis, bit = stage
    return {axis: lax.axis_index(axis) + bit * (1 - 2 * side_of(stage))}


def shares(order, rows):
    held = [rows]
    for stage in order:
        held.append(held[-1] // 2 if held[-1] % 32 == 0 else held[-1])
    return held


def span(start, size):
    return pl.ds(pl.multiple_of(start, 16), size)


def step_kernel(n, dp, *refs):
    codes_ref, users_ref, user_row_ref, targets_ref, domains_ref, bias_ref, gains_ref = refs[:7]
    mixer_ref, feed_ref, embed_ref = refs[7:10]
    out_ref, out_user_ref, out_ids_ref, out_square_ref, out_small_ref, out_stat_ref = refs[10:16]
    x0_s, x1_s, x2_s, qkv_s, p_s, o_s, r_s, mem_s, dz_s, wn_s, wt_s, ext_s, table_s = refs[16:29]
    gain_s, ebias_s, dbias_s, g0_s, ge_s, gbias_s, ggain_s, rows_s, user_s, ids_s = refs[29:39]
    cross_s, cross_back_s, pc_s, oc_s, rest_s, first_s, codes_s, slot_s, user_low_s = refs[39:48]
    stat_s, stat_land, small_s, small_land, local_sems, sends, recvs = refs[48:55]
    lands = refs[55:]
    order = stages(dp)
    across = order[-1]
    depth = len(order)
    chunks = n // GROUP
    section = lax.axis_index("pipe")
    used = [0]

    def remote(source, target, stage):
        index = used[0]
        used[0] += 1
        return pltpu.make_async_remote_copy(
            src_ref=source,
            dst_ref=target,
            send_sem=sends.at[index],
            recv_sem=recvs.at[index],
            device_id=partner_of(stage),
            device_id_type=MESH,
        )

    locals_in = []
    for block in range(BLOCKS):
        lanes = slice(block * LANES, (block + 1) * LANES)
        if block < MIXW // LANES:
            source = mixer_ref.at[0, :, lanes]
        else:
            source = feed_ref.at[0, :, slice(lanes.start - MIXW, lanes.stop - MIXW)]
        locals_in.append(pltpu.make_async_copy(source, g0_s.at[block], local_sems.at[block]))
    vocabulary = embed_ref.shape[0]
    flat = x2_s.at[pl.ds(0, vocabulary)]
    load_embed = pltpu.make_async_copy(embed_ref, flat, local_sems.at[BLOCKS])
    for copy in locals_in:
        copy.start()
    load_embed.start()

    barrier = pltpu.get_barrier_semaphore()
    for stage in order:
        pl.semaphore_signal(barrier, inc=1, device_id=partner_of(stage), device_id_type=MESH)
    pl.semaphore_wait(barrier, depth)

    scale = HEAD_DIM**-0.5
    cross_scale = jnp.where(section == 1, scale, 1.0).astype(f32)
    for copy in locals_in:
        copy.wait()
    for block in range(BLOCKS):
        value = g0_s[block]
        if block < 3:
            value = value * scale
        elif 12 <= block < 15:
            value = value * cross_scale
        wn_s[section, :, block * LANES : (block + 1) * LANES] = value.astype(bf16)
    half = D // 2
    mine = span(side_of(order[0]) * half, half)
    over = remote(wn_s.at[section, mine], wn_s.at[section, mine], across)
    over.start()

    ids_s[:, : HIST_LEN - 1] = codes_ref[pl.ds(pl.multiple_of(section * n, 8), n), :]
    lane, row = iota((n, LANES), 1), iota((n, LANES), 0)
    ids = ids_s[...] + ((lane & 3) << 8)
    ids = jnp.where(lane < HIST_LEN - 1, ids, jnp.where(lane == HIST_LEN - 1, CODES + row, -1))
    ids_s[...] = ids
    count = targets_ref.shape[1]
    history, token = iota((count, LANES), 0), iota((count, LANES), 1)
    pick = jnp.where((token >> 2) + section * n == history, 1.0, 0.0)
    level, place = iota((LEVELS, LANES), 0), iota((LEVELS, LANES), 1) & 3
    target = mul(targets_ref[...].astype(f32), pick) + (level * CODEBOOK).astype(f32)
    goal = jnp.sum(jnp.where(level == place, target, 0.0), axis=0, keepdims=True).astype(jnp.int32)
    start_ids = jnp.sum(
        jnp.where(level == place - 1, target, 0.0), axis=0, keepdims=True
    ).astype(jnp.int32)
    domain = mul(domains_ref[...].astype(f32), pick)
    pick = jnp.where(lax.rem(token, n) + section * n == history, 1.0, 0.0)
    own_users = mul_exact(user_row_ref[...].astype(f32), pick)

    counts = [
        jnp.sum(jnp.where(domain == d, 1.0, 0.0), axis=1, keepdims=True) for d in range(DOMAINS)
    ]
    counts += [jnp.zeros((1, 1), f32)] * (8 - DOMAINS)
    stat_s[0, :, CODES:] = jnp.broadcast_to(jnp.concatenate(counts, 0), (8, LANES))
    stat_s[0, :, :CODES] = mul_t(jnp.ones((8, LANES), bf16), onehot(goal, CODES))
    slot = 0
    for k, stage in enumerate(order):
        slot = slot + side_of(stage) * 2 ** (depth - 1 - k)
    owner = iota((8, LANES), 1) // n
    own_users = jnp.broadcast_to(own_users, (8, LANES)).astype(jnp.int32)
    slot_s[...] = jnp.where(owner == lax.rem(slot, LANES // n), own_users, 0)
    store_ids = pltpu.make_async_copy(slot_s, out_ids_ref.at[slot], local_sems.at[BLOCKS + 1])
    store_ids.start()
    store_ids.wait()

    def slots_of(j):
        return pl.ds(lax.div(slot, 2**j) * 2**j, 2**j)

    early = []
    for j, stage in enumerate(reversed(order)):
        held = out_ids_ref.at[slots_of(j)]
        early.append(
            (
                remote(stat_s.at[j], stat_land.at[j], stage),
                remote(held, held, stage),
            )
        )

    def early_step(j):
        if j > 0:
            for copy in early[j - 1]:
                copy.wait()
            stat_s[j] = stat_s[j - 1] + stat_land[j - 1]
        if j < depth:
            for copy in early[j]:
                copy.start()

    eye = jnp.where(iota((LANES, LANES), 0) == iota((LANES, LANES), 1), 1.0, 0.0).astype(bf16)
    load_embed.wait()

    def fetch(i, carry):
        user_s[pl.ds(i, 1), :] = x2_s[pl.ds(CODES + users_ref[section * n + i], 1), :]
        return carry

    lax.fori_loop(0, n, fetch, 0)
    for block in range(CODES // LANES + 1):
        if block < CODES // LANES:
            rows = x2_s[block * LANES : (block + 1) * LANES, :]
            table_s[block * LANES : (block + 1) * LANES, :] = rows.astype(bf16)
            width = LANES
        else:
            rows = user_s[...]
            width = n
        high = rows.astype(bf16)
        low = (rows - high.astype(f32)).astype(bf16)
        lanes = slice(block * LANES, block * LANES + width)
        ext_s[:D, lanes] = mul_t(eye, high).astype(bf16)
        ext_s[D:, lanes] = mul_t(eye, low).astype(bf16)

    def lookup(c, carry):
        ids = jnp.concatenate([ids_s[pl.ds(GROUP * c + i, 1), :] for i in range(GROUP)], 1)
        both = mul(ext_s[...], onehot(ids, CODES + n))
        x0_s[c] = both[:D] + both[D:]
        return carry

    lax.fori_loop(0, chunks, lookup, 0)

    for g in range(7):
        gain_s[g] = jnp.broadcast_to(gains_ref[g : g + 1, :], (LANES, LANES)).T

    def positions(axis):
        index = iota((KEYS, LANES), axis)
        return jnp.where(index == HIST_LEN - 1, 0, index + 1)

    key, query = positions(0), positions(1)
    distance = jnp.abs(query - key)
    remoteness = jnp.zeros_like(distance)
    for edge in (12, 16, 23, 32, 46, 64, 91):
        remoteness = remoteness + (distance >= edge).astype(jnp.int32)
    nearby = jnp.minimum(jnp.where(distance < 8, distance, 8 + remoteness), 15)
    buckets = nearby + jnp.where(key > query, 16, 0)
    real = iota((KEYS, LANES), 0) < HIST_LEN
    for head in range(HEADS):
        lanes = slice((head % 2) * LANES, (head % 2 + 1) * LANES)

        def choose(b, table):
            return jnp.where(buckets == b, bias_ref[head, 0, b], table)

        table = lax.fori_loop(0, BUCKETS, choose, jnp.zeros((KEYS, LANES), f32))
        ebias_s[head // 2, :, lanes] = jnp.where(real, table, -1e30)
    key, query = iota((LANES, LANES), 0), iota((LANES, LANES), 1)
    offset = query - key
    seen = ((key >> 2) == (query >> 2)) & (offset >= 0)
    for head in range(HEADS):
        lanes = slice((head % 2) * LANES, (head % 2 + 1) * LANES)
        table = jnp.full((LANES, LANES), -1e30, f32)
        for b in range(LEVELS):
            table = jnp.where(seen & (offset == b), bias_ref[head, 1, b], table)
        dbias_s[head // 2, :, lanes] = table

    def transpose_weights(which):
        for block in range(BLOCKS):
            place = slice(block * LANES, (block + 1) * LANES)
            wt_s[which, place, :] = mul_t(eye, wn_s[which, :, place]).astype(bf16)

    transpose_weights(section)
    over.wait()
    came = wn_s.at[1 - section, mine]
    beside = remote(came, came, order[0])
    beside.start()
    beside.wait()
    transpose_weights(1 - section)

    def gain(g, width):
        column = gain_s[g]
        return column if width == LANES else jnp.concatenate([column] * (width // LANES), 1)

    def encode(c, carry):
        for j in range(depth + 1):
            pl.when(c == j)(functools.partial(early_step, j))
        x0 = x0_s[c]
        h = norm_low(x0, inverse_rms(x0), gain(0, WIDE))
        for j in range(3):
            part = slice(j * WIDTH, (j + 1) * WIDTH)
            qkv_s[c, part, :] = mul(wt_s[0, part, :], h).astype(bf16)
        for i in range(GROUP):
            lanes = slice(i * LANES, (i + 1) * LANES)
            natural = mul_t(eye, h[:, lanes]).astype(bf16)[:KEYS]
            keys = mul(natural, wn_s[0, :, WIDTH : 2 * WIDTH]).astype(bf16)
            for j in range(PAIRS):
                part = slice(j * LANES, (j + 1) * LANES)
                chance, mixed = attend(
                    keys[:, part],
                    qkv_s[c, part, lanes],
                    qkv_s[c, 2 * WIDTH + j * LANES : 2 * WIDTH + (j + 1) * LANES, lanes],
                    ebias_s[j],
                )
                p_s[GROUP * c + i, j] = chance
                o_s[c, part, lanes] = mixed
        x1 = x0 + mul(wn_s[0, :, 3 * WIDTH : 4 * WIDTH], o_s[c])
        x1_s[c] = x1
        h = norm_low(x1, inverse_rms(x1), gain(1, WIDE))
        for j in range(2):
            part = slice(j * FF // 2, (j + 1) * FF // 2)
            lifted = mul(wt_s[0, MIXW + j * FF // 2 : MIXW + (j + 1) * FF // 2, :], h)
            r_s[c, part, :] = jnp.maximum(lifted, 0.0).astype(bf16)
        x2 = x1 + mul(wn_s[0, :, MIXW + FF :], r_s[c])
        put_wide(x2_s, c, x2)
        e = norm_low(x2, inverse_rms(x2), gain(2, WIDE))
        for j in range(2):
            part = slice(j * WIDTH, (j + 1) * WIDTH)
            mem_s[c, part, :] = mul(
                wt_s[0, 4 * WIDTH + j * WIDTH : 4 * WIDTH + (j + 1) * WIDTH, :], e
            ).astype(bf16)
        return carry

    def put_wide(ref, c, value):
        for i in range(GROUP):
            ref[pl.ds(pl.multiple_of((GROUP * c + i) * D, D), D), :] = value[
                :, i * LANES : (i + 1) * LANES
            ]

    def get_wide(ref, c):
        return jnp.concatenate(
            [ref[pl.ds(pl.multiple_of((GROUP * c + i) * D, D), D), :] for i in range(GROUP)], 1
        )

    lax.fori_loop(0, chunks, encode, 0)
    for j in range(chunks, depth + 1):
        early_step(j)
    out_stat_ref[...] = stat_s[depth, :1, :CODES]

    def put_blocks(first, value):
        for index in range(value.shape[1] // LANES):
            block = first + index
            part = value[:, index * LANES : (index + 1) * LANES].astype(bf16)
            if block < FIRST // LANES:
                first_s[1, block * D : (block + 1) * D, :] = part
            else:
                block -= FIRST // LANES
                rest_s[1, block * D : (block + 1) * D, :] = part

    def add_blocks(first, value):
        for index in range(value.shape[0] // LANES):
            g0_s[first + index] += value[index * LANES : (index + 1) * LANES, :]

    start = onehot(start_ids, CODES)
    both = mul(ext_s[:, :CODES], start)
    y0 = both[:D] + both[D:]
    inverse0 = inverse_rms(y0)
    h0 = norm_low(y0, inverse0, gain(3, LANES))
    dz_s[:, :LANES] = mul(wt_s[1, : 3 * WIDTH, :], h0).astype(bf16)
    both = mul(mul_t(eye, h0).astype(bf16), wn_s[1, :, WIDTH : 3 * WIDTH]).astype(bf16)
    self_chance = []
    mixed_parts = []
    for j in range(PAIRS):
        part = slice(j * LANES, (j + 1) * LANES)
        chance, mixed = attend(
            both[:, part],
            dz_s[part, :LANES],
            dz_s[2 * WIDTH + j * LANES : 2 * WIDTH + (j + 1) * LANES, :LANES],
            dbias_s[j],
        )
        self_chance.append(chance)
        mixed_parts.append(mixed)
    self_values = both[:, WIDTH:]
    self_mixed = jnp.concatenate(mixed_parts, 0)
    y1 = y0 + mul(wn_s[1, :, 3 * WIDTH : 4 * WIDTH], self_mixed)
    inverse1 = inverse_rms(y1)
    h1 = norm_low(y1, inverse1, gain(4, LANES))
    cross_s[...] = mul(wt_s[1, 4 * WIDTH : 5 * WIDTH, :], h1).astype(bf16)

    def rows_of(g, table):
        row, token = iota((LANES, LANES), 0), iota((LANES, LANES), 1)
        rep = jnp.where(token == 16 * g + 4 * (row >> 5) + (row & 3), 1.0, 0.0).astype(bf16)
        rows = mul_t(rep, table)
        mask = (iota(rows.shape, 1) >> 6) == ((iota(rows.shape, 0) & 31) >> 2)
        return jnp.where(mask, rows, 0.0).astype(bf16)

    def head_mask(shape):
        return (iota(shape, 0) >> 6) == ((iota(shape, 1) & 31) >> 2)

    def rows_t_of(g, table):
        token, row = iota((LANES, LANES), 0), iota((LANES, LANES), 1)
        rep = jnp.where(token == 16 * g + 4 * (row >> 5) + (row & 3), 1.0, 0.0).astype(bf16)
        rows = mul(table, rep)
        return jnp.where(head_mask(rows.shape), rows, 0.0).astype(bf16)

    def gather_rows(ref):
        total = jnp.zeros((WIDTH, LANES), f32)
        for g in range(chunks):
            row, token = iota((LANES, LANES), 0), iota((LANES, LANES), 1)
            rep = jnp.where(token == 16 * g + 4 * (row >> 5) + (row & 3), 1.0, 0.0).astype(bf16)
            total = total + mul(ref[g], rep)
        return total.astype(bf16)

    def blocks_of(table):
        owner = iota(table.shape, 0) >> 5
        zero = jnp.zeros_like(table)
        return jnp.concatenate(
            [jnp.where(owner == j, table, zero) for j in range(GROUP)], 1
        ).astype(bf16)

    def cross(g, carry):
        queries = rows_of(g, cross_s[...])
        parts = []
        for j in range(GROUP):
            parts.append(
                mul(
                    queries[32 * j : 32 * j + 32],
                    mem_s[g, :WIDTH, j * LANES : (j + 1) * LANES],
                )
            )
        scores = jnp.concatenate(parts, 0)
        scores = jnp.where(iota(scores.shape, 1) < HIST_LEN, scores, -1e30)
        chance = jnp.exp(scores - jnp.max(scores, axis=1, keepdims=True))
        chance = chance * (1.0 / jnp.sum(chance, axis=1, keepdims=True))
        pc_s[g] = chance
        mixed = mul_t(mem_s[g, WIDTH:, :], blocks_of(chance))
        oc_s[g] = jnp.where(head_mask(mixed.shape), mixed, 0.0).astype(bf16)
        return carry

    lax.fori_loop(0, chunks, cross, 0)
    cross_mixed = gather_rows(oc_s)
    y2 = y1 + mul(wn_s[1, :, 5 * WIDTH : 6 * WIDTH], cross_mixed)
    inverse2 = inverse_rms(y2)
    h2 = norm_low(y2, inverse2, gain(5, LANES))
    lifted = mul(wt_s[1, MIXW : MIXW + FF, :], h2)
    active = jnp.maximum(lifted, 0.0).astype(bf16)
    y3 = y2 + mul(wn_s[1, :, MIXW + FF :], active)
    inverse3 = inverse_rms(y3)
    final = norm_low(y3, inverse3, gain(6, LANES))
    logits = mul(table_s[...], final)
    top = jnp.max(logits, axis=0, keepdims=True)
    log_total = top + jnp.log(jnp.sum(jnp.exp(logits - top), axis=0, keepdims=True))
    match = iota(logits.shape, 0) == goal
    picked = jnp.sum(jnp.where(match, logits, 0.0), axis=0, keepdims=True)
    weight = jnp.zeros((1, LANES), f32)
    for d in range(DOMAINS):
        share = 1.0 / (DOMAINS * jnp.maximum(stat_s[depth, d : d + 1, CODES:], 1.0))
        weight = weight + jnp.where(domain == d, share, 0.0)
    loss = jnp.sum(weight * (log_total - picked), axis=1, keepdims=True)
    back_logits = (
        weight * (jnp.exp(logits - log_total) - jnp.where(match, 1.0, 0.0))
    ).astype(bf16)
    back_final = mul(ext_s[:D, :CODES], back_logits)
    table_grad = mul_t(back_logits, final)
    back, gain_grad = norm_back(y3, inverse3, gain(6, LANES), back_final)
    ggain_s[6] = gain_grad
    low = back.astype(bf16)
    put_blocks(26, mul_t(low, active))
    back_lifted = jnp.where(lifted > 0, mul(wt_s[1, MIXW + FF :, :], low), 0.0).astype(bf16)
    put_blocks(18, mul_t(h2, back_lifted))
    more, gain_grad = norm_back(
        y2, inverse2, gain(5, LANES), mul(wn_s[1, :, MIXW : MIXW + FF], back_lifted)
    )
    ggain_s[5] = gain_grad
    back = back + more
    low = back.astype(bf16)
    put_blocks(15, mul_t(low, cross_mixed))
    cross_back_s[...] = mul(wt_s[1, 5 * WIDTH : 6 * WIDTH, :], low).astype(bf16)

    def cross_back(g, carry):
        mixed_rows = rows_of(g, cross_back_s[...])
        parts = []
        for j in range(GROUP):
            parts.append(
                mul(
                    mixed_rows[32 * j : 32 * j + 32],
                    mem_s[g, WIDTH:, j * LANES : (j + 1) * LANES],
                )
            )
        back_chance = jnp.concatenate(parts, 0)
        chance = pc_s[g]
        inner = jnp.sum(back_chance * chance, axis=1, keepdims=True)
        spread = blocks_of(chance * (back_chance - inner))
        total = mul_t(mem_s[g, :WIDTH, :], spread)
        mem_s[g, :WIDTH, :] = mul(rows_t_of(g, cross_s[...]), spread).astype(bf16)
        mem_s[g, WIDTH:, :] = mul(rows_t_of(g, cross_back_s[...]), blocks_of(chance)).astype(bf16)
        oc_s[g] = jnp.where(head_mask(total.shape), total, 0.0).astype(bf16)
        return carry

    lax.fori_loop(0, chunks, cross_back, 0)
    back_query = gather_rows(oc_s)
    put_blocks(12, mul_t(h1, back_query) * HEAD_DIM**-0.5)
    more, gain_grad = norm_back(
        y1, inverse1, gain(4, LANES), mul(wn_s[1, :, 4 * WIDTH : 5 * WIDTH], back_query)
    )
    ggain_s[4] = gain_grad
    back = back + more
    low = back.astype(bf16)
    put_blocks(9, mul_t(low, self_mixed))
    back_mixed = mul(wt_s[1, 3 * WIDTH : 4 * WIDTH, :], low).astype(bf16)
    self_scores = []
    for j in range(PAIRS):
        part = slice(j * LANES, (j + 1) * LANES)
        keys = slice(WIDTH + j * LANES, WIDTH + (j + 1) * LANES)
        values = slice(2 * WIDTH + j * LANES, 2 * WIDTH + (j + 1) * LANES)
        one, two, three, scores = attend_back(
            dz_s[keys, :LANES],
            dz_s[part, :LANES],
            self_values[:, part],
            back_mixed[part],
            self_chance[j],
        )
        dz_s[part, LANES : 2 * LANES] = one
        dz_s[keys, LANES : 2 * LANES] = two
        dz_s[values, LANES : 2 * LANES] = three
        self_scores.append(scores)
    put_blocks(0, mul_t(h0, dz_s[:WIDTH, LANES : 2 * LANES]) * HEAD_DIM**-0.5)
    put_blocks(3, mul_t(h0, dz_s[WIDTH:, LANES : 2 * LANES]))
    more, gain_grad = norm_back(
        y0, inverse0, gain(3, LANES), mul(wn_s[1, :, : 3 * WIDTH], dz_s[:, LANES : 2 * LANES])
    )
    ggain_s[3] = gain_grad
    back = back + more
    spread = mul_t(start, split_low(back))
    ge_s[:CODES, :] = table_grad + spread[:, :D] + spread[:, D:]
    ge_s[CODES:, :] = jnp.zeros((n, D), f32)
    rows_s[...] = jnp.zeros_like(rows_s)
    for head in range(HEADS):
        lanes = slice((head % 2) * LANES, (head % 2 + 1) * LANES)
        for b in range(LEVELS):
            hit = jnp.where(offset == b, self_scores[head // 2][:, lanes], 0.0)
            rows_s[head, BUCKETS + b : BUCKETS + b + 1, :] = jnp.sum(hit, axis=0, keepdims=True)

    def reducing(buffer, kept):
        steps, at = [], 0
        held = shares(order[:-1], buffer.shape[0])
        for k, stage in enumerate(order[:-1]):
            rows, left = held[k], held[k + 1]
            side = side_of(stage)
            if left < rows:
                source = buffer.at[span(at + (1 - side) * left, left)]
                at = at + side * left
            else:
                source = buffer.at[span(at, rows)]
            steps.append((remote(source, kept[k], stage), at, left))
        return steps, at, held

    def begin(steps, k):
        steps[k][0].start()

    def finish(steps, buffer, kept, k):
        copy, at, left = steps[k]
        copy.wait()
        place = span(at, left)
        total = buffer[place, :].astype(f32) + kept[k][...].astype(f32)
        buffer[place, :] = total.astype(bf16)

    flat_depth = depth - 1
    land = {}
    for index, name in enumerate(("rest0", "rest1", "first0", "first1", "codes")):
        land[name] = lands[index * flat_depth : (index + 1) * flat_depth]
    land_rest, land_first, land_codes = lands[5 * flat_depth :]
    rest1 = reducing(rest_s.at[1], land["rest1"])
    first1 = reducing(first_s.at[1], land["first1"])
    rest0 = reducing(rest_s.at[0], land["rest0"])
    first0 = reducing(first_s.at[0], land["first0"])
    codes = reducing(codes_s, land["codes"])

    def step1(k):
        if k > 0:
            finish(rest1[0], rest_s.at[1], land["rest1"], k - 1)
            finish(first1[0], first_s.at[1], land["first1"], k - 1)
        if k < flat_depth:
            begin(rest1[0], k)
            begin(first1[0], k)

    def crossing(buffer, target, at, rows):
        source = buffer.at[1 - section, span(at, rows)]
        return remote(source, target, across)

    cross_rest = crossing(rest_s, land_rest, rest1[1], rest1[2][-1])
    cross_first = crossing(first_s, land_first, first1[1], first1[2][-1])

    def settle(copy, buffer, landed, at, rows, base):
        copy.wait()
        value = (buffer[section, span(at, rows), :].astype(f32) + landed[...].astype(f32)).astype(
            bf16
        )
        out_ref[span(base + at, rows), :] = value
        value = value.astype(f32)
        return jnp.sum(value * value, axis=0, keepdims=True)

    def gathering(base, at, held):
        steps = []
        for k in reversed(range(flat_depth)):
            rows, left = held[k], held[k + 1]
            if left < rows:
                place = out_ref.at[span(base + at, left)]
                steps.append(remote(place, place, order[k]))
                at = at - side_of(order[k]) * left
            else:
                steps.append(None)
        return steps

    gather_rest = gathering(0, rest1[1], rest1[2])
    gather_first = gathering(REST, first1[1], first1[2])

    def step0(k):
        if k > 0 and k <= flat_depth:
            finish(rest0[0], rest_s.at[0], land["rest0"], k - 1)
        if k < flat_depth:
            begin(rest0[0], k)
        if k == flat_depth:
            cross_rest.start()
        if k == flat_depth + 1:
            squares = settle(cross_rest, rest_s, land_rest, rest1[1], rest1[2][-1], 0)
            out_square_ref[slot, 0:1, :] = squares / (dp * rest1[2][-1] // REST)
        if k > flat_depth + 1 and gather_rest[k - flat_depth - 2] is not None:
            gather_rest[k - flat_depth - 2].wait()
        if flat_depth < k < 2 * flat_depth + 1 and gather_rest[k - flat_depth - 1] is not None:
            gather_rest[k - flat_depth - 1].start()

    g0_s[...] = jnp.zeros_like(g0_s)
    gbias_s[...] = jnp.zeros_like(gbias_s)
    for g in range(3):
        ggain_s[g] = jnp.zeros((D, LANES), f32)

    def fold(x):
        return sum(x[:, i * LANES : (i + 1) * LANES] for i in range(GROUP))

    def back_rest(c, carry):
        for j in range(flat_depth + 1):
            pl.when(c == j)(functools.partial(step1, j))
        x2 = get_wide(x2_s, c)
        inverse = inverse_rms(x2)
        back_memory = mem_s[c]
        add_blocks(12, mul_t(back_memory, norm_low(x2, inverse, gain(2, WIDE))))
        back, gain_grad = norm_back(
            x2, inverse, gain(2, WIDE), mul(wn_s[0, :, 4 * WIDTH : 6 * WIDTH], back_memory)
        )
        ggain_s[2] += fold(gain_grad)
        low = back.astype(bf16)
        active = r_s[c]
        add_blocks(26, mul_t(active, low))
        back_active = mul(wt_s[0, MIXW + FF :, :], low)
        back_lifted = jnp.where(active.astype(f32) > 0, back_active, 0.0).astype(bf16)
        x1 = x1_s[c]
        inverse = inverse_rms(x1)
        add_blocks(18, mul_t(back_lifted, norm_low(x1, inverse, gain(1, WIDE))))
        more, gain_grad = norm_back(
            x1, inverse, gain(1, WIDE), mul(wn_s[0, :, MIXW : MIXW + FF], back_lifted)
        )
        ggain_s[1] += fold(gain_grad)
        put_wide(x2_s, c, back + more)
        return carry

    lax.fori_loop(0, chunks, back_rest, 0)
    for j in range(chunks, flat_depth + 1):
        step1(j)
    for block in range(REST // D):
        turned = mul_t(eye, g0_s[FIRST // D + block].astype(bf16)).astype(bf16)
        rest_s[0, block * D : (block + 1) * D, :] = turned

    def back_first(c, carry):
        for j in range(min(chunks, 2 * flat_depth + 2)):
            pl.when(c == j)(functools.partial(step0, j))
        back = get_wide(x2_s, c)
        low = back.astype(bf16)
        add_blocks(9, mul_t(o_s[c], low))
        back_mixed = mul(wt_s[0, 3 * WIDTH : 4 * WIDTH, :], low).astype(bf16)
        for i in range(GROUP):
            lanes = slice(i * LANES, (i + 1) * LANES)
            for j in range(PAIRS):
                part = slice(j * LANES, (j + 1) * LANES)
                keys = slice(WIDTH + j * LANES, WIDTH + (j + 1) * LANES)
                values = slice(2 * WIDTH + j * LANES, 2 * WIDTH + (j + 1) * LANES)
                one, two, three, scores = attend_back(
                    qkv_s[c, keys, lanes],
                    qkv_s[c, part, lanes],
                    mul_t(eye, qkv_s[c, values, lanes]).astype(bf16)[:KEYS],
                    back_mixed[part, lanes],
                    p_s[GROUP * c + i, j],
                )
                mem_s[c, part, lanes] = one
                mem_s[c, keys, lanes] = two
                r_s[c, part, lanes] = three
                gbias_s[j] += scores
        x0 = x0_s[c]
        inverse = inverse_rms(x0)
        h = norm_low(x0, inverse, gain(0, WIDE))
        add_blocks(0, mul_t(mem_s[c], h))
        add_blocks(6, mul_t(r_s[c, :WIDTH, :], h))
        back_normed = mul(wn_s[0, :, : 2 * WIDTH], mem_s[c])
        back_normed = back_normed + mul(wn_s[0, :, 2 * WIDTH : 3 * WIDTH], r_s[c, :WIDTH, :])
        more, gain_grad = norm_back(x0, inverse, gain(0, WIDE), back_normed)
        ggain_s[0] += fold(gain_grad)
        ids = jnp.concatenate([ids_s[pl.ds(GROUP * c + i, 1), :] for i in range(GROUP)], 1)
        spread = mul_t(onehot(ids, CODES + n), split_low(back + more))
        ge_s[...] += spread[:, :D] + spread[:, D:]
        return carry

    lax.fori_loop(0, chunks, back_first, 0)

    for block in range(FIRST // D):
        value = g0_s[block]
        if block < 3:
            value = value * HEAD_DIM**-0.5
        turned = mul_t(eye, value.astype(bf16)).astype(bf16)
        first_s[0, block * D : (block + 1) * D, :] = turned
    codes_s[...] = ge_s[:CODES, :].astype(bf16)
    begin(first0[0], 0)
    begin(codes[0], 0)
    user_low_s[...] = ge_s[CODES:, :].astype(bf16)
    store_users = pltpu.make_async_copy(
        user_low_s, out_user_ref.at[span(slot * n, n)], local_sems.at[BLOCKS + 2]
    )
    store_users.start()

    ones = jnp.ones((8, LANES), f32)
    for g in range(7):
        small_s[0, g : g + 1, :] = mul_exact(ones, ggain_s[g].T)[:1]
    small_s[0, 7:8, :] = jnp.broadcast_to(loss, (1, LANES))

    def bucket_sums(b, carry):
        for head in range(HEADS):
            lanes = slice((head % 2) * LANES, (head % 2 + 1) * LANES)
            hit = jnp.where(buckets == b, gbias_s[head // 2, :, lanes], 0.0)
            rows_s[head, pl.ds(b, 1), :] = jnp.sum(hit, axis=0, keepdims=True)
        return carry

    lax.fori_loop(0, BUCKETS, bucket_sums, 0)
    for head in range(HEADS):
        small_s[0, 8 + head : 9 + head, :] = mul_exact(ones, rows_s[head].T)[:1]
    small_s[0, 8 + HEADS :, :] = jnp.zeros((8 - HEADS, LANES), f32)

    small_steps = [remote(small_s.at[k], small_land.at[k], stage) for k, stage in enumerate(order)]
    small_steps[0].start()
    done = min(chunks, 2 * flat_depth + 2)
    for k in range(flat_depth):
        finish(first0[0], first_s.at[0], land["first0"], k)
        finish(codes[0], codes_s, land["codes"], k)
        small_steps[k].wait()
        small_s[k + 1] = small_s[k] + small_land[k]
        small_steps[k + 1].start()
        if k + 1 < flat_depth:
            begin(first0[0], k + 1)
            begin(codes[0], k + 1)
        if done < 2 * flat_depth + 2:
            step0(done)
            done += 1
    while done < 2 * flat_depth + 2:
        step0(done)
        done += 1
    at, rows = codes[1], codes[2][-1]
    left = rows // 2 if rows % 32 == 0 else rows
    side = side_of(across)
    cross_first.start()
    if left < rows:
        source = codes_s.at[span(at + (1 - side) * left, left)]
        at = at + side * left
    else:
        source = codes_s.at[span(at, rows)]
    cross_codes = remote(source, land_codes, across)
    cross_codes.start()
    squares = settle(cross_first, first_s, land_first, first1[1], first1[2][-1], REST)
    out_square_ref[slot, 1:2, :] = squares / (dp * first1[2][-1] // FIRST)
    cross_codes.wait()
    value = codes_s[span(at, left), :].astype(f32) + land_codes[...].astype(f32)
    value = value.astype(bf16)
    out_ref[span(COLS + at, left), :] = value
    value = value.astype(f32)
    squares = jnp.sum(value * value, axis=0, keepdims=True)
    out_square_ref[slot, 2:3, :] = squares / (2 * dp * left // CODES)
    out_square_ref[slot, 3:, :] = jnp.zeros((5, LANES), f32)
    small_steps[depth - 1].wait()
    out_small_ref[...] = small_s[depth - 1] + small_land[depth - 1]

    store_users.wait()
    for j, stage in enumerate(reversed(order)):
        copies = []
        if j == 0:
            if left < rows:
                place = out_ref.at[span(COLS + at, left)]
                copies.append(remote(place, place, stage))
                at = at - side * left
        else:
            k = flat_depth - j
            rows, left = codes[2][k], codes[2][k + 1]
            if left < rows:
                place = out_ref.at[span(COLS + at, left)]
                copies.append(remote(place, place, stage))
                at = at - side_of(stage) * left
            if gather_first[j - 1] is not None:
                copies.append(gather_first[j - 1])
        held = out_square_ref.at[slots_of(j)]
        copies.append(remote(held, held, stage))
        start_row = lax.div(slot, 2**j) * 2**j * n
        held = out_user_ref.at[span(start_row, 2**j * n)]
        copies.append(remote(held, held, stage))
        for copy in copies:
            copy.start()
        for copy in copies:
            copy.wait()


def gradients(codes, users, targets, domains, bias, gains, mixer, feed, embedding, dp):
    n = users.shape[0] // 2
    chunks = n // GROUP
    order = stages(dp)
    depth = len(order)
    devices = 2 * dp
    vmem = pl.BlockSpec(memory_space=pltpu.VMEM)
    smem = pl.BlockSpec(memory_space=pltpu.SMEM)
    hbm = pl.BlockSpec(memory_space=pl.ANY)
    stat = (8, CODES + LANES)
    lands = []
    for rows in (REST, REST, FIRST, FIRST, CODES):
        held = shares(order[:-1], rows)
        lands += [pltpu.VMEM((left, D), bf16) for left in held[1:]]
    last = [shares(order[:-1], rows)[-1] for rows in (REST, FIRST)]
    last.append(shares(order, CODES)[-1])
    lands += [pltpu.VMEM((left, D), bf16) for left in last]
    copies = 16 * depth + 16
    return pl.pallas_call(
        functools.partial(step_kernel, n, dp),
        out_shape=(
            jax.ShapeDtypeStruct((COLS + CODES, D), bf16),
            jax.ShapeDtypeStruct((devices * n, D), bf16),
            jax.ShapeDtypeStruct((devices, 8, LANES), jnp.int32),
            jax.ShapeDtypeStruct((devices, 8, LANES), f32),
            jax.ShapeDtypeStruct((16, LANES), f32),
            jax.ShapeDtypeStruct((1, CODES), f32),
        ),
        in_specs=[vmem, smem, vmem, vmem, vmem, smem, vmem, hbm, hbm, hbm],
        out_specs=(vmem, hbm, hbm, vmem, vmem, vmem),
        scratch_shapes=[
            pltpu.VMEM((chunks, D, WIDE), f32),
            pltpu.VMEM((chunks, D, WIDE), f32),
            pltpu.VMEM((n * D, LANES), f32),
            pltpu.VMEM((chunks, 3 * WIDTH, WIDE), bf16),
            pltpu.VMEM((n, PAIRS, KEYS, 2 * LANES), bf16),
            pltpu.VMEM((chunks, WIDTH, WIDE), bf16),
            pltpu.VMEM((chunks, FF, WIDE), bf16),
            pltpu.VMEM((chunks, 2 * WIDTH, WIDE), bf16),
            pltpu.VMEM((3 * WIDTH, 2 * LANES), bf16),
            pltpu.VMEM((2, D, COLS), bf16),
            pltpu.VMEM((2, COLS, D), bf16),
            pltpu.VMEM((2 * D, CODES + n), bf16),
            pltpu.VMEM((CODES, D), bf16),
            pltpu.VMEM((7, D, LANES), f32),
            pltpu.VMEM((PAIRS, KEYS, 2 * LANES), f32),
            pltpu.VMEM((PAIRS, LANES, 2 * LANES), f32),
            pltpu.VMEM((BLOCKS, D, LANES), f32),
            pltpu.VMEM((CODES + n, D), f32),
            pltpu.VMEM((PAIRS, KEYS, 2 * LANES), f32),
            pltpu.VMEM((7, D, LANES), f32),
            pltpu.VMEM((HEADS, LANES, LANES), f32),
            pltpu.VMEM((n, D), f32),
            pltpu.VMEM((n, LANES), jnp.int32),
            pltpu.VMEM((WIDTH, LANES), bf16),
            pltpu.VMEM((WIDTH, LANES), bf16),
            pltpu.VMEM((chunks, LANES, LANES), f32),
            pltpu.VMEM((chunks, WIDTH, LANES), bf16),
            pltpu.VMEM((2, REST, D), bf16),
            pltpu.VMEM((2, FIRST, D), bf16),
            pltpu.VMEM((CODES, D), bf16),
            pltpu.VMEM((8, LANES), jnp.int32),
            pltpu.VMEM((n, D), bf16),
            pltpu.VMEM((depth + 1,) + stat, f32),
            pltpu.VMEM((depth,) + stat, f32),
            pltpu.VMEM((depth, 16, LANES), f32),
            pltpu.VMEM((depth, 16, LANES), f32),
            pltpu.SemaphoreType.DMA((BLOCKS + 3,)),
            pltpu.SemaphoreType.DMA((copies,)),
            pltpu.SemaphoreType.DMA((copies,)),
        ]
        + lands,
        compiler_params=pltpu.CompilerParams(
            collective_id=0, has_side_effects=True, vmem_limit_bytes=63 * 2**20
        ),
        name="gradients",
    )(codes, users, users.reshape(1, -1), targets, domains, bias, gains, mixer, feed, embedding)


def adam(weight, moment, square, slope, rate, decay):
    moment = beta_one * moment + (1 - beta_one) * slope
    square = beta_two * square + (1 - beta_two) * slope * slope
    unbiased_moment = moment * (1 / (1 - beta_one**STEP))
    unbiased_square = square * (1 / (1 - beta_two**STEP))
    root = unbiased_square * lax.rsqrt(unbiased_square)
    step = unbiased_moment / (root + adam_eps) + decay * weight
    return weight - rate * step, moment, square


def update_kernel(*refs):
    parts_in, big_in, small_in, refs = refs[:6], refs[6:15], refs[15:21], refs[21:]
    loss_ref, norm_ref, section_ref, hist_ref = refs[:4]
    big_out, small_out, low_out, refs = refs[4:13], refs[13:19], refs[19:22], refs[22:]
    parts, hold, low_hold = refs[:6], refs[6:15], refs[15:18]
    user_grad, part_sems, in_sems, out_sems = refs[18:]
    grad_ref, user_ref, ids_ref, square_ref, small_ref, stat_ref = parts
    arrivals = [pltpu.make_async_copy(parts_in[i], parts[i], part_sems.at[i]) for i in range(6)]
    loads = [pltpu.make_async_copy(big_in[i], hold[i], in_sems.at[i]) for i in range(9)]
    for load in arrivals[1:] + arrivals[:1] + loads:
        load.start()
    for arrival in arrivals:
        arrival.wait()

    users = user_grad.shape[0]
    span = min(1024, user_ref.shape[0])
    slots = span // LANES * (ids_ref.shape[0] * LANES // user_ref.shape[0])
    fit = ids_ref.shape[0] * LANES // user_ref.shape[0]
    user_grad[...] = jnp.zeros_like(user_grad)

    def scatter(part, carry):
        rows = user_ref[pl.ds(pl.multiple_of(part * span, span), span), :]
        lanes = []
        for group in range(span // LANES):
            total = ids_ref[part * slots + group * fit, :1, :]
            for other in range(1, fit):
                total = total + ids_ref[part * slots + group * fit + other, :1, :]
            lanes.append(total)
        ids = jnp.concatenate(lanes, 1)
        for block in range(users // USER_ROWS):
            place = slice(block * USER_ROWS, (block + 1) * USER_ROWS)
            hit = iota((USER_ROWS, span), 0) + block * USER_ROWS == ids
            user_grad[place, :] += mul(jnp.where(hit, 1.0, 0.0).astype(bf16), rows)
        return carry

    lax.fori_loop(0, user_ref.shape[0] // span, scatter, 0)

    def total(x):
        return jnp.sum(jnp.sum(x, axis=0, keepdims=True), axis=1, keepdims=True)

    devices = square_ref.shape[0]
    slot = iota((devices, 8, LANES), 0)
    row = iota((devices, 8, LANES), 1)
    squares = square_ref[...]
    side = lax.rem(slot, 2)
    section_squares = [
        total(jnp.sum(jnp.where((row < 2) & (side == s), squares, 0.0), axis=0)) for s in range(2)
    ]
    rest = total(jnp.sum(jnp.where(row == 2, squares, 0.0), axis=0))
    user_values = user_grad[...]
    rest = rest + total(user_values * user_values)
    small = small_ref[...]
    lane, line = iota(small.shape, 1), iota(small.shape, 0)
    counted = (line < 7) | ((line > 7) & (lane < 2 * BUCKETS))
    small_kept = jnp.where(counted, small, 0.0)
    rest = rest + total(small_kept * small_kept)
    norm = jnp.sqrt(section_squares[0] + section_squares[1] + rest)
    factor = jnp.minimum(1.0, clip_norm / (norm + 1e-06))
    loss_ref[0] = small[7, 0]
    norm_ref[0] = norm[0, 0]
    for s in range(2):
        section_ref[s] = jnp.sqrt(section_squares[s])[0, 0]
    for level in range(LEVELS):
        hist_ref[level : level + 1, :] = stat_ref[
            :1, level * CODEBOOK : (level + 1) * CODEBOOK
        ]

    outs = adam(
        small_in[0][...], small_in[1][...], small_in[2][...], factor * small[:7], rate_gain, 0.0
    )
    for ref, value in zip(small_out[:3], outs):
        ref[...] = value
    for head in range(HEADS):
        for s in range(2):
            slope = factor * small[8 + head : 9 + head, s * BUCKETS : (s + 1) * BUCKETS]
            one = slice(s, s + 1)
            outs = adam(
                small_in[3][head, one, :],
                small_in[4][head, one, :],
                small_in[5][head, one, :],
                slope,
                rate_small,
                0.0,
            )
            for ref, value in zip(small_out[3:], outs):
                ref[head, one, :] = value

    stores = []

    def store(kind, place):
        first = 3 * kind
        pieces = [(hold[first + i], big_out[first + i]) for i in range(3)]
        pieces.append((low_hold[kind], low_out[kind]))
        for source, target in pieces:
            copy = pltpu.make_async_copy(
                source.at[place], target.at[place], out_sems.at[len(stores)]
            )
            copy.start()
            stores.append(copy)

    def step(kind, place, slope):
        first = 3 * kind
        outs = adam(
            hold[first][place],
            hold[first + 1][place],
            hold[first + 2][place],
            factor * slope,
            rate_matrix,
            decay_matrix,
        )
        for i in range(3):
            hold[first + i][place] = outs[i]
        low_hold[kind][place] = outs[0].astype(bf16)

    def block_of(block):
        first = FIRST // D
        place = block - first if block >= first else REST // D + block
        return grad_ref[place * D : (place + 1) * D, :].astype(f32)

    for i in range(3):
        loads[i].wait()
    for part in range(6):
        for block in range(3 * part, 3 * part + 3):
            lanes = slice(block * LANES, (block + 1) * LANES)
            step(0, (0, slice(None), lanes), block_of(block))
        store(0, (0, slice(None), slice(3 * part * LANES, 3 * (part + 1) * LANES)))
    for i in range(3, 6):
        loads[i].wait()
    for part in range(4):
        for block in range(4 * part, 4 * part + 4):
            lanes = slice(block * LANES, (block + 1) * LANES)
            step(1, (0, slice(None), lanes), block_of(MIXW // LANES + block))
        store(1, (0, slice(None), slice(4 * part * LANES, 4 * (part + 1) * LANES)))
    for i in range(6, 9):
        loads[i].wait()
    for part in range(4):
        rows = slice(part * CODEBOOK, (part + 1) * CODEBOOK)
        step(2, (rows, slice(None)), grad_ref[COLS + rows.start : COLS + rows.stop, :].astype(f32))
        store(2, (rows, slice(None)))
    for part in range(users // USER_ROWS):
        rows = slice(part * USER_ROWS, (part + 1) * USER_ROWS)
        place = (slice(CODES + part * USER_ROWS, CODES + (part + 1) * USER_ROWS), slice(None))
        step(2, place, user_grad[rows, :])
        store(2, place)
    for copy in stores:
        copy.wait()


def update(reduced, mixers, feeds, embeds, gains, biases):
    vmem = pl.BlockSpec(memory_space=pltpu.VMEM)
    smem = pl.BlockSpec(memory_space=pltpu.SMEM)
    hbm = pl.BlockSpec(memory_space=pl.ANY)
    big = [*mixers, *feeds, *embeds]
    small = [*gains, *biases]
    low = [jax.ShapeDtypeStruct(x[0].shape, bf16) for x in (mixers, feeds, embeds)]
    users = embeds[0].shape[0] - CODES
    pieces = 4 * (6 + 4 + 4 + users // USER_ROWS)
    return pl.pallas_call(
        update_kernel,
        out_shape=[
            jax.ShapeDtypeStruct((1,), f32),
            jax.ShapeDtypeStruct((1,), f32),
            jax.ShapeDtypeStruct((2,), f32),
            jax.ShapeDtypeStruct((LEVELS, CODEBOOK), f32),
        ]
        + [jax.ShapeDtypeStruct(x.shape, f32) for x in big + small]
        + low,
        in_specs=[hbm] * 15 + [vmem] * 6,
        out_specs=[smem] * 3 + [vmem] + [hbm] * 9 + [vmem] * 6 + [hbm] * 3,
        scratch_shapes=[pltpu.VMEM(x.shape, x.dtype) for x in reduced]
        + [pltpu.VMEM(x.shape, f32) for x in big]
        + [pltpu.VMEM(x.shape, bf16) for x in low]
        + [
            pltpu.VMEM((users, D), f32),
            pltpu.SemaphoreType.DMA((6,)),
            pltpu.SemaphoreType.DMA((9,)),
            pltpu.SemaphoreType.DMA((pieces,)),
        ],
        compiler_params=pltpu.CompilerParams(vmem_limit_bytes=62 * 2**20),
        name="update",
    )(*reduced, *big, *small)


def shards(
    history_codes,
    user_ids,
    targets,
    domains,
    mixer,
    mixer_moment,
    mixer_square,
    feed,
    feed_moment,
    feed_square,
    embedding,
    embedding_moment,
    embedding_square,
    gains,
    gains_moment,
    gains_square,
    position_bias,
    bias_moment,
    bias_square,
):
    def turned(table):
        return jnp.transpose(table, (2, 0, 1))

    biases = [turned(x) for x in (position_bias, bias_moment, bias_square)]
    reduced = gradients(
        history_codes,
        user_ids,
        targets.T,
        domains.reshape(1, -1),
        biases[0],
        gains,
        mixer,
        feed,
        embedding,
        lax.axis_size("dp"),
    )
    outs = update(
        reduced,
        (mixer, mixer_moment, mixer_square),
        (feed, feed_moment, feed_square),
        (embedding, embedding_moment, embedding_square),
        (gains, gains_moment, gains_square),
        biases,
    )
    loss, norm, sections, histograms = outs[:4]
    back = [jnp.transpose(x, (1, 2, 0)) for x in outs[16:19]]
    return (
        loss.reshape(()),
        norm.reshape(()),
        sections,
        histograms,
        *outs[4:16],
        *back,
        *outs[19:],
    )


def solution(mesh):
    by_dp, by_pipe, copied = P("dp"), P("pipe"), P()
    return jax.shard_map(
        shards,
        mesh=mesh,
        in_specs=(by_dp,) * 4 + (by_pipe,) * 6 + (copied,) * 9,
        out_specs=(copied,) * 4 + (by_pipe,) * 6 + (copied,) * 9 + (by_pipe,) * 2 + (copied,),
        check_vma=False,
    )
```

```python
import functools

import jax
import jax.numpy as jnp
from jax import lax
from jax.experimental import pallas as pl
from jax.experimental.pallas import tpu as pltpu
from jax.sharding import PartitionSpec as P

D = 128
HEADS = 6
HEAD_DIM = 64
FF = 1024
CODEBOOK = 256
LEVELS = 4
BUCKETS = 32
DOMAINS = 3
HIST_LEN = 81
STEP = 5
CODES = 1024
LANES = 128
WIDTH = HEADS * HEAD_DIM
MIXW = 6 * WIDTH
COLS = MIXW + 2 * FF
BLOCKS = COLS // LANES
KEYS = 96
GROUP = 4
WIDE = GROUP * LANES
PAIRS = HEADS // 2
FIRST = 4 * WIDTH
REST = COLS - FIRST
USER_ROWS = 400
MESH = pl.DeviceIdType.MESH

norm_eps = 1e-06
beta_one = 0.9
beta_two = 0.999
adam_eps = 1e-08
clip_norm = 0.5
rate_matrix = 0.04
rate_gain = 0.8
rate_small = 0.3
decay_matrix = 0.01

f32 = jnp.float32
bf16 = jnp.bfloat16


def iota(shape, axis):
    return lax.broadcasted_iota(jnp.int32, shape, axis)


def mul(left, right):
    return jnp.dot(left, right, preferred_element_type=f32)


def mul_t(left, right):
    return lax.dot_general(left, right, (((1,), (1,)), ((), ())), preferred_element_type=f32)


def mul_exact(left, right):
    return jnp.dot(left, right, preferred_element_type=f32, precision=lax.Precision.HIGHEST)


def onehot(ids, rows):
    return jnp.where(iota((rows, ids.shape[1]), 0) == ids, 1.0, 0.0).astype(bf16)


def inverse_rms(x):
    return lax.rsqrt(jnp.mean(x * x, axis=0, keepdims=True) + norm_eps)


def norm_low(x, inverse, gain):
    return (x * inverse * gain).astype(bf16)


def norm_back(x, inverse, gain, upstream):
    scaled = x * inverse
    inner = upstream * gain
    back = inverse * (inner - scaled * jnp.mean(inner * scaled, axis=0, keepdims=True))
    return back, upstream * scaled


def block_diag(pair):
    zero = jnp.zeros((HEAD_DIM, LANES), pair.dtype)
    left = jnp.concatenate([pair[:HEAD_DIM], zero], 0)
    right = jnp.concatenate([zero, pair[HEAD_DIM:]], 0)
    return jnp.concatenate([left, right], 1)


def diagonal(both):
    return jnp.concatenate([both[:HEAD_DIM, :LANES], both[HEAD_DIM:, LANES:]], 0)


def stack(both):
    return jnp.concatenate([both[:, :LANES], both[:, LANES:]], 0)


def pad_keys(table):
    if table.shape[0] == LANES:
        return table
    zero = jnp.zeros((LANES - table.shape[0], table.shape[1]), table.dtype)
    return jnp.concatenate([table, zero], 0)


def attend(keys, query, values, bias):
    scores = mul(keys, block_diag(query)) + bias
    top = jnp.max(scores, axis=0, keepdims=True)
    chance = jnp.exp(scores - top)
    total = jnp.sum(chance, axis=0, keepdims=True)
    chance = (chance * (1.0 / total)).astype(bf16)
    mixed = diagonal(mul(values, pad_keys(chance))).astype(bf16)
    return chance, mixed


def attend_back(keys_t, query, values, back_mixed, chance):
    exact = chance.astype(f32)
    spread = block_diag(back_mixed)
    back_chance = mul(values, spread)
    inner = jnp.sum(back_chance * exact, axis=0, keepdims=True)
    back_scores = exact * (back_chance - inner)
    low = pad_keys(back_scores.astype(bf16))
    back_query = diagonal(mul(keys_t, low)).astype(bf16)
    back_keys = diagonal(mul_t(query, stack(low))).astype(bf16)
    back_values = diagonal(mul_t(back_mixed, stack(pad_keys(chance)))).astype(bf16)
    return back_query, back_keys, back_values, back_scores


def split_low(x):
    high = x.astype(bf16)
    return jnp.concatenate([high, (x - high.astype(f32)).astype(bf16)], 0)


def stages(dp):
    order = []
    bit = 1
    while bit < dp:
        order.append(("dp", bit))
        bit *= 2
    return order + [("pipe", 1)]


def side_of(stage):
    axis, bit = stage
    return lax.rem(lax.div(lax.axis_index(axis), bit), 2)


def partner_of(stage):
    axis, bit = stage
    return {axis: lax.axis_index(axis) + bit * (1 - 2 * side_of(stage))}


def shares(order, rows):
    held = [rows]
    for stage in order:
        held.append(held[-1] // 2 if held[-1] % 32 == 0 else held[-1])
    return held


def span(start, size):
    return pl.ds(pl.multiple_of(start, 16), size)


def step_kernel(n, dp, *refs):
    codes_ref, users_ref, user_row_ref, targets_ref, domains_ref, bias_ref, gains_ref = refs[:7]
    mixer_ref, feed_ref, embed_ref = refs[7:10]
    out_ref, out_user_ref, out_ids_ref, out_square_ref, out_small_ref, out_stat_ref = refs[10:16]
    x0_s, x1_s, x2_s, qkv_s, p_s, o_s, r_s, mem_s, dz_s, wn_s, wt_s, ext_s, table_s = refs[16:29]
    gain_s, ebias_s, dbias_s, g0_s, ge_s, gbias_s, ggain_s, rows_s, user_s, ids_s = refs[29:39]
    cross_s, cross_back_s, pc_s, oc_s, rest_s, first_s, codes_s, slot_s, user_low_s = refs[39:48]
    stat_s, stat_land, small_s, small_land, local_sems, sends, recvs = refs[48:55]
    lands = refs[55:]
    order = stages(dp)
    across = order[-1]
    depth = len(order)
    chunks = n // GROUP
    section = lax.axis_index("pipe")
    used = [0]

    def remote(source, target, stage):
        index = used[0]
        used[0] += 1
        return pltpu.make_async_remote_copy(
            src_ref=source,
            dst_ref=target,
            send_sem=sends.at[index],
            recv_sem=recvs.at[index],
            device_id=partner_of(stage),
            device_id_type=MESH,
        )

    locals_in = []
    for block in range(BLOCKS):
        lanes = slice(block * LANES, (block + 1) * LANES)
        if block < MIXW // LANES:
            source = mixer_ref.at[0, :, lanes]
        else:
            source = feed_ref.at[0, :, slice(lanes.start - MIXW, lanes.stop - MIXW)]
        locals_in.append(pltpu.make_async_copy(source, g0_s.at[block], local_sems.at[block]))
    vocabulary = embed_ref.shape[0]
    flat = x2_s.at[pl.ds(0, vocabulary)]
    load_embed = pltpu.make_async_copy(embed_ref, flat, local_sems.at[BLOCKS])
    for copy in locals_in:
        copy.start()
    load_embed.start()

    barrier = pltpu.get_barrier_semaphore()
    for stage in order:
        pl.semaphore_signal(barrier, inc=1, device_id=partner_of(stage), device_id_type=MESH)
    pl.semaphore_wait(barrier, depth)

    scale = HEAD_DIM**-0.5
    cross_scale = jnp.where(section == 1, scale, 1.0).astype(f32)
    for copy in locals_in:
        copy.wait()
    for block in range(BLOCKS):
        value = g0_s[block]
        if block < 3:
            value = value * scale
        elif 12 <= block < 15:
            value = value * cross_scale
        wn_s[section, :, block * LANES : (block + 1) * LANES] = value.astype(bf16)
    half = D // 2
    mine = span(side_of(order[0]) * half, half)
    pieces = (slice(0, FIRST), slice(FIRST, COLS))
    over = [
        remote(wn_s.at[section, mine, piece], wn_s.at[section, mine, piece], across)
        for piece in pieces
    ]
    for copy in over:
        copy.start()

    ids_s[:, : HIST_LEN - 1] = codes_ref[pl.ds(pl.multiple_of(section * n, 8), n), :]
    lane, row = iota((n, LANES), 1), iota((n, LANES), 0)
    ids = ids_s[...] + ((lane & 3) << 8)
    ids = jnp.where(lane < HIST_LEN - 1, ids, jnp.where(lane == HIST_LEN - 1, CODES + row, -1))
    ids_s[...] = ids
    count = targets_ref.shape[1]
    history, token = iota((count, LANES), 0), iota((count, LANES), 1)
    pick = jnp.where((token >> 2) + section * n == history, 1.0, 0.0)
    level, place = iota((LEVELS, LANES), 0), iota((LEVELS, LANES), 1) & 3
    target = mul(targets_ref[...].astype(f32), pick) + (level * CODEBOOK).astype(f32)
    goal = jnp.sum(jnp.where(level == place, target, 0.0), axis=0, keepdims=True).astype(jnp.int32)
    start_ids = jnp.sum(
        jnp.where(level == place - 1, target, 0.0), axis=0, keepdims=True
    ).astype(jnp.int32)
    domain = mul(domains_ref[...].astype(f32), pick)
    pick = jnp.where(lax.rem(token, n) + section * n == history, 1.0, 0.0)
    own_users = mul_exact(user_row_ref[...].astype(f32), pick)

    counts = [
        jnp.sum(jnp.where(domain == d, 1.0, 0.0), axis=1, keepdims=True) for d in range(DOMAINS)
    ]
    counts += [jnp.zeros((1, 1), f32)] * (8 - DOMAINS)
    stat_s[0, :, CODES:] = jnp.broadcast_to(jnp.concatenate(counts, 0), (8, LANES))
    stat_s[0, :, :CODES] = mul_t(jnp.ones((8, LANES), bf16), onehot(goal, CODES))
    slot = 0
    for k, stage in enumerate(order):
        slot = slot + side_of(stage) * 2 ** (depth - 1 - k)
    owner = iota((8, LANES), 1) // n
    own_users = jnp.broadcast_to(own_users, (8, LANES)).astype(jnp.int32)
    slot_s[...] = jnp.where(owner == lax.rem(slot, LANES // n), own_users, 0)
    store_ids = pltpu.make_async_copy(slot_s, out_ids_ref.at[slot], local_sems.at[BLOCKS + 1])
    store_ids.start()
    store_ids.wait()

    def slots_of(j):
        return pl.ds(lax.div(slot, 2**j) * 2**j, 2**j)

    early = []
    for j, stage in enumerate(reversed(order)):
        held = out_ids_ref.at[slots_of(j)]
        early.append(
            (
                remote(stat_s.at[j], stat_land.at[j], stage),
                remote(held, held, stage),
            )
        )

    def early_step(j):
        if j > 0:
            for copy in early[j - 1]:
                copy.wait()
            stat_s[j] = stat_s[j - 1] + stat_land[j - 1]
        if j < depth:
            for copy in early[j]:
                copy.start()

    eye = jnp.where(iota((LANES, LANES), 0) == iota((LANES, LANES), 1), 1.0, 0.0).astype(bf16)
    load_embed.wait()

    def fetch(i, carry):
        user_s[pl.ds(i, 1), :] = x2_s[pl.ds(CODES + users_ref[section * n + i], 1), :]
        return carry

    lax.fori_loop(0, n, fetch, 0)
    for block in range(CODES // LANES + 1):
        if block < CODES // LANES:
            rows = x2_s[block * LANES : (block + 1) * LANES, :]
            table_s[block * LANES : (block + 1) * LANES, :] = rows.astype(bf16)
            width = LANES
        else:
            rows = user_s[...]
            width = n
        high = rows.astype(bf16)
        low = (rows - high.astype(f32)).astype(bf16)
        lanes = slice(block * LANES, block * LANES + width)
        ext_s[:D, lanes] = mul_t(eye, high).astype(bf16)
        ext_s[D:, lanes] = mul_t(eye, low).astype(bf16)

    def lookup(c, carry):
        ids = jnp.concatenate([ids_s[pl.ds(GROUP * c + i, 1), :] for i in range(GROUP)], 1)
        both = mul(ext_s[...], onehot(ids, CODES + n))
        x0_s[c] = both[:D] + both[D:]
        return carry

    lax.fori_loop(0, chunks, lookup, 0)

    for g in range(7):
        gain_s[g] = jnp.broadcast_to(gains_ref[g : g + 1, :], (LANES, LANES)).T

    def positions(axis):
        index = iota((KEYS, LANES), axis)
        return jnp.where(index == HIST_LEN - 1, 0, index + 1)

    key, query = positions(0), positions(1)
    distance = jnp.abs(query - key)
    remoteness = jnp.zeros_like(distance)
    for edge in (12, 16, 23, 32, 46, 64, 91):
        remoteness = remoteness + (distance >= edge).astype(jnp.int32)
    nearby = jnp.minimum(jnp.where(distance < 8, distance, 8 + remoteness), 15)
    buckets = nearby + jnp.where(key > query, 16, 0)
    real = iota((KEYS, LANES), 0) < HIST_LEN
    for head in range(HEADS):
        lanes = slice((head % 2) * LANES, (head % 2 + 1) * LANES)

        def choose(b, table):
            return jnp.where(buckets == b, bias_ref[head, 0, b], table)

        table = lax.fori_loop(0, BUCKETS, choose, jnp.zeros((KEYS, LANES), f32))
        ebias_s[head // 2, :, lanes] = jnp.where(real, table, -1e30)
    key, query = iota((LANES, LANES), 0), iota((LANES, LANES), 1)
    offset = query - key
    seen = ((key >> 2) == (query >> 2)) & (offset >= 0)
    for head in range(HEADS):
        lanes = slice((head % 2) * LANES, (head % 2 + 1) * LANES)
        table = jnp.full((LANES, LANES), -1e30, f32)
        for b in range(LEVELS):
            table = jnp.where(seen & (offset == b), bias_ref[head, 1, b], table)
        dbias_s[head // 2, :, lanes] = table

    def transpose_weights(which, first, last):
        for block in range(first, last):
            place = slice(block * LANES, (block + 1) * LANES)
            wt_s[which, place, :] = wn_s[which, :, place].T

    beside = []
    for piece in pieces:
        came = wn_s.at[1 - section, mine, piece]
        beside.append(remote(came, came, order[0]))
    over[0].wait()
    beside[0].start()
    transpose_weights(section, 0, BLOCKS)
    beside[0].wait()
    transpose_weights(1 - section, 0, FIRST // LANES)

    def rest_arrives():
        over[1].wait()
        beside[1].start()
        beside[1].wait()
        transpose_weights(1 - section, FIRST // LANES, BLOCKS)

    def gain(g, width):
        column = gain_s[g]
        return column if width == LANES else jnp.concatenate([column] * (width // LANES), 1)

    def encode(c, carry):
        for j in range(depth + 1):
            pl.when(c == j)(functools.partial(early_step, j))
        x0 = x0_s[c]
        h = norm_low(x0, inverse_rms(x0), gain(0, WIDE))
        for j in range(3):
            part = slice(j * WIDTH, (j + 1) * WIDTH)
            qkv_s[c, part, :] = mul(wt_s[0, part, :], h).astype(bf16)
        for i in range(GROUP):
            lanes = slice(i * LANES, (i + 1) * LANES)
            for j in range(PAIRS):
                part = slice(j * LANES, (j + 1) * LANES)
                keys = slice(WIDTH + j * LANES, WIDTH + (j + 1) * LANES)
                chance, mixed = attend(
                    qkv_s[c, keys, lanes].T[:KEYS],
                    qkv_s[c, part, lanes],
                    qkv_s[c, 2 * WIDTH + j * LANES : 2 * WIDTH + (j + 1) * LANES, lanes],
                    ebias_s[j],
                )
                p_s[GROUP * c + i, j] = chance
                o_s[c, part, lanes] = mixed
        x1 = x0 + mul(wn_s[0, :, 3 * WIDTH : 4 * WIDTH], o_s[c])
        x1_s[c] = x1
        pl.when(c == 0)(rest_arrives)
        h = norm_low(x1, inverse_rms(x1), gain(1, WIDE))
        for j in range(2):
            part = slice(j * FF // 2, (j + 1) * FF // 2)
            lifted = mul(wt_s[0, MIXW + j * FF // 2 : MIXW + (j + 1) * FF // 2, :], h)
            r_s[c, part, :] = jnp.maximum(lifted, 0.0).astype(bf16)
        x2 = x1 + mul(wn_s[0, :, MIXW + FF :], r_s[c])
        put_wide(x2_s, c, x2)
        e = norm_low(x2, inverse_rms(x2), gain(2, WIDE))
        for j in range(2):
            part = slice(j * WIDTH, (j + 1) * WIDTH)
            mem_s[c, part, :] = mul(
                wt_s[0, 4 * WIDTH + j * WIDTH : 4 * WIDTH + (j + 1) * WIDTH, :], e
            ).astype(bf16)
        return carry

    def put_wide(ref, c, value):
        for i in range(GROUP):
            ref[pl.ds(pl.multiple_of((GROUP * c + i) * D, D), D), :] = value[
                :, i * LANES : (i + 1) * LANES
            ]

    def get_wide(ref, c):
        return jnp.concatenate(
            [ref[pl.ds(pl.multiple_of((GROUP * c + i) * D, D), D), :] for i in range(GROUP)], 1
        )

    lax.fori_loop(0, chunks, encode, 0)
    for j in range(chunks, depth + 1):
        early_step(j)
    out_stat_ref[...] = stat_s[depth, :1, :CODES]

    def put_blocks(first, value):
        for index in range(value.shape[1] // LANES):
            block = first + index
            part = value[:, index * LANES : (index + 1) * LANES].astype(bf16)
            if block < FIRST // LANES:
                first_s[1, block * D : (block + 1) * D, :] = part
            else:
                block -= FIRST // LANES
                rest_s[1, block * D : (block + 1) * D, :] = part

    def add_blocks(first, value):
        for index in range(value.shape[1] // LANES):
            g0_s[first + index] += value[:, index * LANES : (index + 1) * LANES]

    start = onehot(start_ids, CODES)
    both = mul(ext_s[:, :CODES], start)
    y0 = both[:D] + both[D:]
    inverse0 = inverse_rms(y0)
    h0 = norm_low(y0, inverse0, gain(3, LANES))
    dz_s[:, :LANES] = mul(wt_s[1, : 3 * WIDTH, :], h0).astype(bf16)
    both = mul(mul_t(eye, h0).astype(bf16), wn_s[1, :, WIDTH : 3 * WIDTH]).astype(bf16)
    self_chance = []
    mixed_parts = []
    for j in range(PAIRS):
        part = slice(j * LANES, (j + 1) * LANES)
        chance, mixed = attend(
            both[:, part],
            dz_s[part, :LANES],
            dz_s[2 * WIDTH + j * LANES : 2 * WIDTH + (j + 1) * LANES, :LANES],
            dbias_s[j],
        )
        self_chance.append(chance)
        mixed_parts.append(mixed)
    self_values = both[:, WIDTH:]
    self_mixed = jnp.concatenate(mixed_parts, 0)
    y1 = y0 + mul(wn_s[1, :, 3 * WIDTH : 4 * WIDTH], self_mixed)
    inverse1 = inverse_rms(y1)
    h1 = norm_low(y1, inverse1, gain(4, LANES))
    cross_s[...] = mul(wt_s[1, 4 * WIDTH : 5 * WIDTH, :], h1).astype(bf16)

    def rows_of(g, table):
        row, token = iota((LANES, LANES), 0), iota((LANES, LANES), 1)
        rep = jnp.where(token == 16 * g + 4 * (row >> 5) + (row & 3), 1.0, 0.0).astype(bf16)
        rows = mul_t(rep, table)
        mask = (iota(rows.shape, 1) >> 6) == ((iota(rows.shape, 0) & 31) >> 2)
        return jnp.where(mask, rows, 0.0).astype(bf16)

    def head_mask(shape):
        return (iota(shape, 0) >> 6) == ((iota(shape, 1) & 31) >> 2)

    def rows_t_of(g, table):
        token, row = iota((LANES, LANES), 0), iota((LANES, LANES), 1)
        rep = jnp.where(token == 16 * g + 4 * (row >> 5) + (row & 3), 1.0, 0.0).astype(bf16)
        rows = mul(table, rep)
        return jnp.where(head_mask(rows.shape), rows, 0.0).astype(bf16)

    def gather_rows(ref):
        total = jnp.zeros((WIDTH, LANES), f32)
        for g in range(chunks):
            row, token = iota((LANES, LANES), 0), iota((LANES, LANES), 1)
            rep = jnp.where(token == 16 * g + 4 * (row >> 5) + (row & 3), 1.0, 0.0).astype(bf16)
            total = total + mul(ref[g], rep)
        return total.astype(bf16)

    def blocks_of(table):
        owner = iota(table.shape, 0) >> 5
        zero = jnp.zeros_like(table)
        return jnp.concatenate(
            [jnp.where(owner == j, table, zero) for j in range(GROUP)], 1
        ).astype(bf16)

    def row_products(rows, ref, g, first):
        parts = []
        for j in range(0, GROUP, 2):
            pair = slice(j * LANES, (j + 2) * LANES)
            both = mul(rows[32 * j : 32 * j + 64], ref[g, first : first + WIDTH, pair])
            parts += [both[:32, :LANES], both[32:, LANES:]]
        return jnp.concatenate(parts, 0)

    def cross(g, carry):
        queries = rows_of(g, cross_s[...])
        scores = row_products(queries, mem_s, g, 0)
        scores = jnp.where(iota(scores.shape, 1) < HIST_LEN, scores, -1e30)
        chance = jnp.exp(scores - jnp.max(scores, axis=1, keepdims=True))
        chance = chance * (1.0 / jnp.sum(chance, axis=1, keepdims=True))
        pc_s[g] = chance
        mixed = mul_t(mem_s[g, WIDTH:, :], blocks_of(chance))
        oc_s[g] = jnp.where(head_mask(mixed.shape), mixed, 0.0).astype(bf16)
        return carry

    lax.fori_loop(0, chunks, cross, 0)
    cross_mixed = gather_rows(oc_s)
    y2 = y1 + mul(wn_s[1, :, 5 * WIDTH : 6 * WIDTH], cross_mixed)
    inverse2 = inverse_rms(y2)
    h2 = norm_low(y2, inverse2, gain(5, LANES))
    lifted = mul(wt_s[1, MIXW : MIXW + FF, :], h2)
    active = jnp.maximum(lifted, 0.0).astype(bf16)
    y3 = y2 + mul(wn_s[1, :, MIXW + FF :], active)
    inverse3 = inverse_rms(y3)
    final = norm_low(y3, inverse3, gain(6, LANES))
    logits = mul(table_s[...], final)
    top = jnp.max(logits, axis=0, keepdims=True)
    log_total = top + jnp.log(jnp.sum(jnp.exp(logits - top), axis=0, keepdims=True))
    match = iota(logits.shape, 0) == goal
    picked = jnp.sum(jnp.where(match, logits, 0.0), axis=0, keepdims=True)
    weight = jnp.zeros((1, LANES), f32)
    for d in range(DOMAINS):
        share = 1.0 / (DOMAINS * jnp.maximum(stat_s[depth, d : d + 1, CODES:], 1.0))
        weight = weight + jnp.where(domain == d, share, 0.0)
    loss = jnp.sum(weight * (log_total - picked), axis=1, keepdims=True)
    back_logits = (
        weight * (jnp.exp(logits - log_total) - jnp.where(match, 1.0, 0.0))
    ).astype(bf16)
    back_final = mul(ext_s[:D, :CODES], back_logits)
    table_grad = mul_t(back_logits, final)
    back, gain_grad = norm_back(y3, inverse3, gain(6, LANES), back_final)
    ggain_s[6] = gain_grad
    low = back.astype(bf16)
    put_blocks(26, mul_t(low, active))
    back_lifted = jnp.where(lifted > 0, mul(wt_s[1, MIXW + FF :, :], low), 0.0).astype(bf16)
    put_blocks(18, mul_t(h2, back_lifted))
    more, gain_grad = norm_back(
        y2, inverse2, gain(5, LANES), mul(wn_s[1, :, MIXW : MIXW + FF], back_lifted)
    )
    ggain_s[5] = gain_grad
    back = back + more
    low = back.astype(bf16)
    put_blocks(15, mul_t(low, cross_mixed))
    cross_back_s[...] = mul(wt_s[1, 5 * WIDTH : 6 * WIDTH, :], low).astype(bf16)

    def cross_back(g, carry):
        mixed_rows = rows_of(g, cross_back_s[...])
        back_chance = row_products(mixed_rows, mem_s, g, WIDTH)
        chance = pc_s[g]
        inner = jnp.sum(back_chance * chance, axis=1, keepdims=True)
        spread = blocks_of(chance * (back_chance - inner))
        total = mul_t(mem_s[g, :WIDTH, :], spread)
        mem_s[g, :WIDTH, :] = mul(rows_t_of(g, cross_s[...]), spread).astype(bf16)
        mem_s[g, WIDTH:, :] = mul(rows_t_of(g, cross_back_s[...]), blocks_of(chance)).astype(bf16)
        oc_s[g] = jnp.where(head_mask(total.shape), total, 0.0).astype(bf16)
        return carry

    lax.fori_loop(0, chunks, cross_back, 0)
    back_query = gather_rows(oc_s)
    put_blocks(12, mul_t(h1, back_query) * HEAD_DIM**-0.5)
    more, gain_grad = norm_back(
        y1, inverse1, gain(4, LANES), mul(wn_s[1, :, 4 * WIDTH : 5 * WIDTH], back_query)
    )
    ggain_s[4] = gain_grad
    back = back + more
    low = back.astype(bf16)
    put_blocks(9, mul_t(low, self_mixed))
    back_mixed = mul(wt_s[1, 3 * WIDTH : 4 * WIDTH, :], low).astype(bf16)
    self_scores = []
    for j in range(PAIRS):
        part = slice(j * LANES, (j + 1) * LANES)
        keys = slice(WIDTH + j * LANES, WIDTH + (j + 1) * LANES)
        values = slice(2 * WIDTH + j * LANES, 2 * WIDTH + (j + 1) * LANES)
        one, two, three, scores = attend_back(
            dz_s[keys, :LANES],
            dz_s[part, :LANES],
            self_values[:, part],
            back_mixed[part],
            self_chance[j],
        )
        dz_s[part, LANES : 2 * LANES] = one
        dz_s[keys, LANES : 2 * LANES] = two
        dz_s[values, LANES : 2 * LANES] = three
        self_scores.append(scores)
    put_blocks(0, mul_t(h0, dz_s[:WIDTH, LANES : 2 * LANES]) * HEAD_DIM**-0.5)
    put_blocks(3, mul_t(h0, dz_s[WIDTH:, LANES : 2 * LANES]))
    more, gain_grad = norm_back(
        y0, inverse0, gain(3, LANES), mul(wn_s[1, :, : 3 * WIDTH], dz_s[:, LANES : 2 * LANES])
    )
    ggain_s[3] = gain_grad
    back = back + more
    spread = mul_t(start, split_low(back))
    ge_s[:CODES, :] = table_grad + spread[:, :D] + spread[:, D:]
    ge_s[CODES:, :] = jnp.zeros((n, D), f32)
    rows_s[...] = jnp.zeros_like(rows_s)
    for head in range(HEADS):
        lanes = slice((head % 2) * LANES, (head % 2 + 1) * LANES)
        for b in range(LEVELS):
            hit = jnp.where(offset == b, self_scores[head // 2][:, lanes], 0.0)
            rows_s[head, BUCKETS + b : BUCKETS + b + 1, :] = jnp.sum(hit, axis=0, keepdims=True)

    def reducing(buffer, kept):
        steps, at = [], 0
        held = shares(order[:-1], buffer.shape[0])
        for k, stage in enumerate(order[:-1]):
            rows, left = held[k], held[k + 1]
            side = side_of(stage)
            if left < rows:
                source = buffer.at[span(at + (1 - side) * left, left)]
                at = at + side * left
            else:
                source = buffer.at[span(at, rows)]
            steps.append((remote(source, kept[k], stage), at, left))
        return steps, at, held

    def begin(steps, k):
        steps[k][0].start()

    def finish(steps, buffer, kept, k):
        copy, at, left = steps[k]
        copy.wait()
        place = span(at, left)
        total = buffer[place, :].astype(f32) + kept[k][...].astype(f32)
        buffer[place, :] = total.astype(bf16)

    flat_depth = depth - 1
    land = {}
    for index, name in enumerate(("rest0", "rest1", "first0", "first1", "codes")):
        land[name] = lands[index * flat_depth : (index + 1) * flat_depth]
    land_rest, land_first, land_codes = lands[5 * flat_depth :]
    rest1 = reducing(rest_s.at[1], land["rest1"])
    first1 = reducing(first_s.at[1], land["first1"])
    rest0 = reducing(rest_s.at[0], land["rest0"])
    first0 = reducing(first_s.at[0], land["first0"])
    codes = reducing(codes_s, land["codes"])

    def step1(k):
        if k > 0:
            finish(rest1[0], rest_s.at[1], land["rest1"], k - 1)
            finish(first1[0], first_s.at[1], land["first1"], k - 1)
        if k < flat_depth:
            begin(rest1[0], k)
            begin(first1[0], k)

    def crossing(buffer, target, at, rows):
        source = buffer.at[1 - section, span(at, rows)]
        return remote(source, target, across)

    cross_rest = crossing(rest_s, land_rest, rest1[1], rest1[2][-1])
    cross_first = crossing(first_s, land_first, first1[1], first1[2][-1])

    def settle(copy, buffer, landed, at, rows, base):
        copy.wait()
        value = (buffer[section, span(at, rows), :].astype(f32) + landed[...].astype(f32)).astype(
            bf16
        )
        out_ref[span(base + at, rows), :] = value
        value = value.astype(f32)
        return jnp.sum(value * value, axis=0, keepdims=True)

    def gathering(base, at, held):
        steps = []
        for k in reversed(range(flat_depth)):
            rows, left = held[k], held[k + 1]
            if left < rows:
                place = out_ref.at[span(base + at, left)]
                steps.append(remote(place, place, order[k]))
                at = at - side_of(order[k]) * left
            else:
                steps.append(None)
        return steps

    gather_rest = gathering(0, rest1[1], rest1[2])
    gather_first = gathering(REST, first1[1], first1[2])

    def step0(k):
        if k > 0 and k <= flat_depth:
            finish(rest0[0], rest_s.at[0], land["rest0"], k - 1)
        if k < flat_depth:
            begin(rest0[0], k)
        if k == flat_depth:
            cross_rest.start()
        if k == flat_depth + 1:
            squares = settle(cross_rest, rest_s, land_rest, rest1[1], rest1[2][-1], 0)
            out_square_ref[slot, 0:1, :] = squares / (dp * rest1[2][-1] // REST)
        if k > flat_depth + 1 and gather_rest[k - flat_depth - 2] is not None:
            gather_rest[k - flat_depth - 2].wait()
        if flat_depth < k < 2 * flat_depth + 1 and gather_rest[k - flat_depth - 1] is not None:
            gather_rest[k - flat_depth - 1].start()

    g0_s[...] = jnp.zeros_like(g0_s)
    gbias_s[...] = jnp.zeros_like(gbias_s)
    for g in range(3):
        ggain_s[g] = jnp.zeros((D, LANES), f32)

    def fold(x):
        return sum(x[:, i * LANES : (i + 1) * LANES] for i in range(GROUP))

    def back_rest(c, carry):
        for j in range(flat_depth + 1):
            pl.when(c == j)(functools.partial(step1, j))
        x2 = get_wide(x2_s, c)
        inverse = inverse_rms(x2)
        back_memory = mem_s[c]
        add_blocks(12, mul_t(norm_low(x2, inverse, gain(2, WIDE)), back_memory))
        back, gain_grad = norm_back(
            x2, inverse, gain(2, WIDE), mul(wn_s[0, :, 4 * WIDTH : 6 * WIDTH], back_memory)
        )
        ggain_s[2] += fold(gain_grad)
        low = back.astype(bf16)
        active = r_s[c]
        add_blocks(26, mul_t(low, active))
        back_active = mul(wt_s[0, MIXW + FF :, :], low)
        back_lifted = jnp.where(active.astype(f32) > 0, back_active, 0.0).astype(bf16)
        x1 = x1_s[c]
        inverse = inverse_rms(x1)
        add_blocks(18, mul_t(norm_low(x1, inverse, gain(1, WIDE)), back_lifted))
        more, gain_grad = norm_back(
            x1, inverse, gain(1, WIDE), mul(wn_s[0, :, MIXW : MIXW + FF], back_lifted)
        )
        ggain_s[1] += fold(gain_grad)
        put_wide(x2_s, c, back + more)
        return carry

    lax.fori_loop(0, chunks, back_rest, 0)
    for j in range(chunks, flat_depth + 1):
        step1(j)
    for block in range(REST // D):
        rest_s[0, block * D : (block + 1) * D, :] = g0_s[FIRST // D + block].astype(bf16)

    def back_first(c, carry):
        for j in range(min(chunks, 2 * flat_depth + 2)):
            pl.when(c == j)(functools.partial(step0, j))
        back = get_wide(x2_s, c)
        low = back.astype(bf16)
        add_blocks(9, mul_t(low, o_s[c]))
        back_mixed = mul(wt_s[0, 3 * WIDTH : 4 * WIDTH, :], low).astype(bf16)
        for i in range(GROUP):
            lanes = slice(i * LANES, (i + 1) * LANES)
            for j in range(PAIRS):
                part = slice(j * LANES, (j + 1) * LANES)
                keys = slice(WIDTH + j * LANES, WIDTH + (j + 1) * LANES)
                values = slice(2 * WIDTH + j * LANES, 2 * WIDTH + (j + 1) * LANES)
                one, two, three, scores = attend_back(
                    qkv_s[c, keys, lanes],
                    qkv_s[c, part, lanes],
                    qkv_s[c, values, lanes].T[:KEYS],
                    back_mixed[part, lanes],
                    p_s[GROUP * c + i, j],
                )
                mem_s[c, part, lanes] = one
                mem_s[c, keys, lanes] = two
                r_s[c, part, lanes] = three
                gbias_s[j] += scores
        x0 = x0_s[c]
        inverse = inverse_rms(x0)
        h = norm_low(x0, inverse, gain(0, WIDE))
        add_blocks(0, mul_t(h, mem_s[c]))
        add_blocks(6, mul_t(h, r_s[c, :WIDTH, :]))
        back_normed = mul(wn_s[0, :, : 2 * WIDTH], mem_s[c])
        back_normed = back_normed + mul(wn_s[0, :, 2 * WIDTH : 3 * WIDTH], r_s[c, :WIDTH, :])
        more, gain_grad = norm_back(x0, inverse, gain(0, WIDE), back_normed)
        ggain_s[0] += fold(gain_grad)
        ids = jnp.concatenate([ids_s[pl.ds(GROUP * c + i, 1), :] for i in range(GROUP)], 1)
        spread = mul_t(onehot(ids, CODES + n), split_low(back + more))
        ge_s[...] += spread[:, :D] + spread[:, D:]
        return carry

    lax.fori_loop(0, chunks, back_first, 0)

    for block in range(FIRST // D):
        value = g0_s[block]
        if block < 3:
            value = value * HEAD_DIM**-0.5
        first_s[0, block * D : (block + 1) * D, :] = value.astype(bf16)
    codes_s[...] = ge_s[:CODES, :].astype(bf16)
    begin(first0[0], 0)
    begin(codes[0], 0)
    user_low_s[...] = ge_s[CODES:, :].astype(bf16)
    store_users = pltpu.make_async_copy(
        user_low_s, out_user_ref.at[span(slot * n, n)], local_sems.at[BLOCKS + 2]
    )
    store_users.start()

    ones = jnp.ones((8, LANES), f32)
    for g in range(7):
        small_s[0, g : g + 1, :] = mul_exact(ones, ggain_s[g].T)[:1]
    small_s[0, 7:8, :] = jnp.broadcast_to(loss, (1, LANES))

    def bucket_sums(b, carry):
        for head in range(HEADS):
            lanes = slice((head % 2) * LANES, (head % 2 + 1) * LANES)
            hit = jnp.where(buckets == b, gbias_s[head // 2, :, lanes], 0.0)
            rows_s[head, pl.ds(b, 1), :] = jnp.sum(hit, axis=0, keepdims=True)
        return carry

    lax.fori_loop(0, BUCKETS, bucket_sums, 0)
    for head in range(HEADS):
        small_s[0, 8 + head : 9 + head, :] = mul_exact(ones, rows_s[head].T)[:1]
    small_s[0, 8 + HEADS :, :] = jnp.zeros((8 - HEADS, LANES), f32)

    small_steps = [remote(small_s.at[k], small_land.at[k], stage) for k, stage in enumerate(order)]
    small_steps[0].start()
    done = min(chunks, 2 * flat_depth + 2)
    for k in range(flat_depth):
        finish(first0[0], first_s.at[0], land["first0"], k)
        finish(codes[0], codes_s, land["codes"], k)
        small_steps[k].wait()
        small_s[k + 1] = small_s[k] + small_land[k]
        small_steps[k + 1].start()
        if k + 1 < flat_depth:
            begin(first0[0], k + 1)
            begin(codes[0], k + 1)
        if done < 2 * flat_depth + 2:
            step0(done)
            done += 1
    while done < 2 * flat_depth + 2:
        step0(done)
        done += 1
    at, rows = codes[1], codes[2][-1]
    left = rows // 2 if rows % 32 == 0 else rows
    side = side_of(across)
    cross_first.start()
    if left < rows:
        source = codes_s.at[span(at + (1 - side) * left, left)]
        at = at + side * left
    else:
        source = codes_s.at[span(at, rows)]
    cross_codes = remote(source, land_codes, across)
    cross_codes.start()
    squares = settle(cross_first, first_s, land_first, first1[1], first1[2][-1], REST)
    out_square_ref[slot, 1:2, :] = squares / (dp * first1[2][-1] // FIRST)
    cross_codes.wait()
    value = codes_s[span(at, left), :].astype(f32) + land_codes[...].astype(f32)
    value = value.astype(bf16)
    out_ref[span(COLS + at, left), :] = value
    value = value.astype(f32)
    squares = jnp.sum(value * value, axis=0, keepdims=True)
    out_square_ref[slot, 2:3, :] = squares / (2 * dp * left // CODES)
    out_square_ref[slot, 3:, :] = jnp.zeros((5, LANES), f32)
    small_steps[depth - 1].wait()
    out_small_ref[...] = small_s[depth - 1] + small_land[depth - 1]

    store_users.wait()
    for j, stage in enumerate(reversed(order)):
        copies = []
        if j == 0:
            if left < rows:
                place = out_ref.at[span(COLS + at, left)]
                copies.append(remote(place, place, stage))
                at = at - side * left
        else:
            k = flat_depth - j
            rows, left = codes[2][k], codes[2][k + 1]
            if left < rows:
                place = out_ref.at[span(COLS + at, left)]
                copies.append(remote(place, place, stage))
                at = at - side_of(stage) * left
            if gather_first[j - 1] is not None:
                copies.append(gather_first[j - 1])
        held = out_square_ref.at[slots_of(j)]
        copies.append(remote(held, held, stage))
        start_row = lax.div(slot, 2**j) * 2**j * n
        held = out_user_ref.at[span(start_row, 2**j * n)]
        copies.append(remote(held, held, stage))
        for copy in copies:
            copy.start()
        for copy in copies:
            copy.wait()


def gradients(codes, users, targets, domains, bias, gains, mixer, feed, embedding, dp):
    n = users.shape[0] // 2
    chunks = n // GROUP
    order = stages(dp)
    depth = len(order)
    devices = 2 * dp
    vmem = pl.BlockSpec(memory_space=pltpu.VMEM)
    smem = pl.BlockSpec(memory_space=pltpu.SMEM)
    hbm = pl.BlockSpec(memory_space=pl.ANY)
    stat = (8, CODES + LANES)
    lands = []
    for rows in (REST, REST, FIRST, FIRST, CODES):
        held = shares(order[:-1], rows)
        lands += [pltpu.VMEM((left, D), bf16) for left in held[1:]]
    last = [shares(order[:-1], rows)[-1] for rows in (REST, FIRST)]
    last.append(shares(order, CODES)[-1])
    lands += [pltpu.VMEM((left, D), bf16) for left in last]
    copies = 16 * depth + 16
    return pl.pallas_call(
        functools.partial(step_kernel, n, dp),
        out_shape=(
            jax.ShapeDtypeStruct((COLS + CODES, D), bf16),
            jax.ShapeDtypeStruct((devices * n, D), bf16),
            jax.ShapeDtypeStruct((devices, 8, LANES), jnp.int32),
            jax.ShapeDtypeStruct((devices, 8, LANES), f32),
            jax.ShapeDtypeStruct((16, LANES), f32),
            jax.ShapeDtypeStruct((1, CODES), f32),
        ),
        in_specs=[vmem, smem, vmem, vmem, vmem, smem, vmem, hbm, hbm, hbm],
        out_specs=(vmem, hbm, hbm, vmem, vmem, vmem),
        scratch_shapes=[
            pltpu.VMEM((chunks, D, WIDE), f32),
            pltpu.VMEM((chunks, D, WIDE), f32),
            pltpu.VMEM((n * D, LANES), f32),
            pltpu.VMEM((chunks, 3 * WIDTH, WIDE), bf16),
            pltpu.VMEM((n, PAIRS, KEYS, 2 * LANES), bf16),
            pltpu.VMEM((chunks, WIDTH, WIDE), bf16),
            pltpu.VMEM((chunks, FF, WIDE), bf16),
            pltpu.VMEM((chunks, 2 * WIDTH, WIDE), bf16),
            pltpu.VMEM((3 * WIDTH, 2 * LANES), bf16),
            pltpu.VMEM((2, D, COLS), bf16),
            pltpu.VMEM((2, COLS, D), bf16),
            pltpu.VMEM((2 * D, CODES + n), bf16),
            pltpu.VMEM((CODES, D), bf16),
            pltpu.VMEM((7, D, LANES), f32),
            pltpu.VMEM((PAIRS, KEYS, 2 * LANES), f32),
            pltpu.VMEM((PAIRS, LANES, 2 * LANES), f32),
            pltpu.VMEM((BLOCKS, D, LANES), f32),
            pltpu.VMEM((CODES + n, D), f32),
            pltpu.VMEM((PAIRS, KEYS, 2 * LANES), f32),
            pltpu.VMEM((7, D, LANES), f32),
            pltpu.VMEM((HEADS, LANES, LANES), f32),
            pltpu.VMEM((n, D), f32),
            pltpu.VMEM((n, LANES), jnp.int32),
            pltpu.VMEM((WIDTH, LANES), bf16),
            pltpu.VMEM((WIDTH, LANES), bf16),
            pltpu.VMEM((chunks, LANES, LANES), f32),
            pltpu.VMEM((chunks, WIDTH, LANES), bf16),
            pltpu.VMEM((2, REST, D), bf16),
            pltpu.VMEM((2, FIRST, D), bf16),
            pltpu.VMEM((CODES, D), bf16),
            pltpu.VMEM((8, LANES), jnp.int32),
            pltpu.VMEM((n, D), bf16),
            pltpu.VMEM((depth + 1,) + stat, f32),
            pltpu.VMEM((depth,) + stat, f32),
            pltpu.VMEM((depth, 16, LANES), f32),
            pltpu.VMEM((depth, 16, LANES), f32),
            pltpu.SemaphoreType.DMA((BLOCKS + 3,)),
            pltpu.SemaphoreType.DMA((copies,)),
            pltpu.SemaphoreType.DMA((copies,)),
        ]
        + lands,
        compiler_params=pltpu.CompilerParams(
            collective_id=0, has_side_effects=True, vmem_limit_bytes=63 * 2**20
        ),
        name="gradients",
    )(codes, users, users.reshape(1, -1), targets, domains, bias, gains, mixer, feed, embedding)


def adam(weight, moment, square, slope, rate, decay):
    moment = beta_one * moment + (1 - beta_one) * slope
    square = beta_two * square + (1 - beta_two) * slope * slope
    unbiased_moment = moment * (1 / (1 - beta_one**STEP))
    unbiased_square = square * (1 / (1 - beta_two**STEP))
    root = unbiased_square * lax.rsqrt(unbiased_square)
    step = unbiased_moment / (root + adam_eps) + decay * weight
    return weight - rate * step, moment, square


def update_kernel(*refs):
    parts_in, big_in, small_in, refs = refs[:6], refs[6:15], refs[15:21], refs[21:]
    loss_ref, norm_ref, section_ref, hist_ref = refs[:4]
    big_out, small_out, low_out, refs = refs[4:13], refs[13:19], refs[19:22], refs[22:]
    parts, hold, low_hold = refs[:6], refs[6:15], refs[15:18]
    user_grad, part_sems, in_sems, out_sems = refs[18:]
    grad_ref, user_ref, ids_ref, square_ref, small_ref, stat_ref = parts
    arrivals = [pltpu.make_async_copy(parts_in[i], parts[i], part_sems.at[i]) for i in range(6)]
    loads = [pltpu.make_async_copy(big_in[i], hold[i], in_sems.at[i]) for i in range(9)]
    for load in arrivals[1:] + arrivals[:1] + loads:
        load.start()
    for arrival in arrivals:
        arrival.wait()

    users = user_grad.shape[0]
    span = min(1024, user_ref.shape[0])
    slots = span // LANES * (ids_ref.shape[0] * LANES // user_ref.shape[0])
    fit = ids_ref.shape[0] * LANES // user_ref.shape[0]
    user_grad[...] = jnp.zeros_like(user_grad)

    def scatter(part, carry):
        rows = user_ref[pl.ds(pl.multiple_of(part * span, span), span), :]
        lanes = []
        for group in range(span // LANES):
            total = ids_ref[part * slots + group * fit, :1, :]
            for other in range(1, fit):
                total = total + ids_ref[part * slots + group * fit + other, :1, :]
            lanes.append(total)
        ids = jnp.concatenate(lanes, 1)
        for block in range(users // USER_ROWS):
            place = slice(block * USER_ROWS, (block + 1) * USER_ROWS)
            hit = iota((USER_ROWS, span), 0) + block * USER_ROWS == ids
            user_grad[place, :] += mul(jnp.where(hit, 1.0, 0.0).astype(bf16), rows)
        return carry

    lax.fori_loop(0, user_ref.shape[0] // span, scatter, 0)

    def total(x):
        return jnp.sum(jnp.sum(x, axis=0, keepdims=True), axis=1, keepdims=True)

    devices = square_ref.shape[0]
    slot = iota((devices, 8, LANES), 0)
    row = iota((devices, 8, LANES), 1)
    squares = square_ref[...]
    side = lax.rem(slot, 2)
    section_squares = [
        total(jnp.sum(jnp.where((row < 2) & (side == s), squares, 0.0), axis=0)) for s in range(2)
    ]
    rest = total(jnp.sum(jnp.where(row == 2, squares, 0.0), axis=0))
    user_values = user_grad[...]
    rest = rest + total(user_values * user_values)
    small = small_ref[...]
    lane, line = iota(small.shape, 1), iota(small.shape, 0)
    counted = (line < 7) | ((line > 7) & (lane < 2 * BUCKETS))
    small_kept = jnp.where(counted, small, 0.0)
    rest = rest + total(small_kept * small_kept)
    norm = jnp.sqrt(section_squares[0] + section_squares[1] + rest)
    factor = jnp.minimum(1.0, clip_norm / (norm + 1e-06))
    loss_ref[0] = small[7, 0]
    norm_ref[0] = norm[0, 0]
    for s in range(2):
        section_ref[s] = jnp.sqrt(section_squares[s])[0, 0]
    for level in range(LEVELS):
        hist_ref[level : level + 1, :] = stat_ref[
            :1, level * CODEBOOK : (level + 1) * CODEBOOK
        ]

    outs = adam(
        small_in[0][...], small_in[1][...], small_in[2][...], factor * small[:7], rate_gain, 0.0
    )
    for ref, value in zip(small_out[:3], outs):
        ref[...] = value
    for head in range(HEADS):
        for s in range(2):
            slope = factor * small[8 + head : 9 + head, s * BUCKETS : (s + 1) * BUCKETS]
            one = slice(s, s + 1)
            outs = adam(
                small_in[3][head, one, :],
                small_in[4][head, one, :],
                small_in[5][head, one, :],
                slope,
                rate_small,
                0.0,
            )
            for ref, value in zip(small_out[3:], outs):
                ref[head, one, :] = value

    stores = []

    def store(kind, place):
        first = 3 * kind
        pieces = [(hold[first + i], big_out[first + i]) for i in range(3)]
        pieces.append((low_hold[kind], low_out[kind]))
        for source, target in pieces:
            copy = pltpu.make_async_copy(
                source.at[place], target.at[place], out_sems.at[len(stores)]
            )
            copy.start()
            stores.append(copy)

    def step(kind, place, slope):
        first = 3 * kind
        outs = adam(
            hold[first][place],
            hold[first + 1][place],
            hold[first + 2][place],
            factor * slope,
            rate_matrix,
            decay_matrix,
        )
        for i in range(3):
            hold[first + i][place] = outs[i]
        low_hold[kind][place] = outs[0].astype(bf16)

    def block_of(block):
        first = FIRST // D
        place = block - first if block >= first else REST // D + block
        return grad_ref[place * D : (place + 1) * D, :].astype(f32)

    for i in range(3):
        loads[i].wait()
    for part in range(6):
        for block in range(3 * part, 3 * part + 3):
            lanes = slice(block * LANES, (block + 1) * LANES)
            step(0, (0, slice(None), lanes), block_of(block))
        store(0, (0, slice(None), slice(3 * part * LANES, 3 * (part + 1) * LANES)))
    for i in range(3, 6):
        loads[i].wait()
    for part in range(4):
        for block in range(4 * part, 4 * part + 4):
            lanes = slice(block * LANES, (block + 1) * LANES)
            step(1, (0, slice(None), lanes), block_of(MIXW // LANES + block))
        store(1, (0, slice(None), slice(4 * part * LANES, 4 * (part + 1) * LANES)))
    for i in range(6, 9):
        loads[i].wait()
    for part in range(4):
        rows = slice(part * CODEBOOK, (part + 1) * CODEBOOK)
        step(2, (rows, slice(None)), grad_ref[COLS + rows.start : COLS + rows.stop, :].astype(f32))
        store(2, (rows, slice(None)))
    for part in range(users // USER_ROWS):
        rows = slice(part * USER_ROWS, (part + 1) * USER_ROWS)
        place = (slice(CODES + part * USER_ROWS, CODES + (part + 1) * USER_ROWS), slice(None))
        step(2, place, user_grad[rows, :])
        store(2, place)
    for copy in stores:
        copy.wait()


def update(reduced, mixers, feeds, embeds, gains, biases):
    vmem = pl.BlockSpec(memory_space=pltpu.VMEM)
    smem = pl.BlockSpec(memory_space=pltpu.SMEM)
    hbm = pl.BlockSpec(memory_space=pl.ANY)
    big = [*mixers, *feeds, *embeds]
    small = [*gains, *biases]
    low = [jax.ShapeDtypeStruct(x[0].shape, bf16) for x in (mixers, feeds, embeds)]
    users = embeds[0].shape[0] - CODES
    pieces = 4 * (6 + 4 + 4 + users // USER_ROWS)
    return pl.pallas_call(
        update_kernel,
        out_shape=[
            jax.ShapeDtypeStruct((1,), f32),
            jax.ShapeDtypeStruct((1,), f32),
            jax.ShapeDtypeStruct((2,), f32),
            jax.ShapeDtypeStruct((LEVELS, CODEBOOK), f32),
        ]
        + [jax.ShapeDtypeStruct(x.shape, f32) for x in big + small]
        + low,
        in_specs=[hbm] * 15 + [vmem] * 6,
        out_specs=[smem] * 3 + [vmem] + [hbm] * 9 + [vmem] * 6 + [hbm] * 3,
        scratch_shapes=[pltpu.VMEM(x.shape, x.dtype) for x in reduced]
        + [pltpu.VMEM(x.shape, f32) for x in big]
        + [pltpu.VMEM(x.shape, bf16) for x in low]
        + [
            pltpu.VMEM((users, D), f32),
            pltpu.SemaphoreType.DMA((6,)),
            pltpu.SemaphoreType.DMA((9,)),
            pltpu.SemaphoreType.DMA((pieces,)),
        ],
        compiler_params=pltpu.CompilerParams(vmem_limit_bytes=62 * 2**20),
        name="update",
    )(*reduced, *big, *small)


def shards(
    history_codes,
    user_ids,
    targets,
    domains,
    mixer,
    mixer_moment,
    mixer_square,
    feed,
    feed_moment,
    feed_square,
    embedding,
    embedding_moment,
    embedding_square,
    gains,
    gains_moment,
    gains_square,
    position_bias,
    bias_moment,
    bias_square,
):
    def turned(table):
        return jnp.transpose(table, (2, 0, 1))

    biases = [turned(x) for x in (position_bias, bias_moment, bias_square)]
    reduced = gradients(
        history_codes,
        user_ids,
        targets.T,
        domains.reshape(1, -1),
        biases[0],
        gains,
        mixer,
        feed,
        embedding,
        lax.axis_size("dp"),
    )
    outs = update(
        reduced,
        (mixer, mixer_moment, mixer_square),
        (feed, feed_moment, feed_square),
        (embedding, embedding_moment, embedding_square),
        (gains, gains_moment, gains_square),
        biases,
    )
    loss, norm, sections, histograms = outs[:4]
    back = [jnp.transpose(x, (1, 2, 0)) for x in outs[16:19]]
    return (
        loss.reshape(()),
        norm.reshape(()),
        sections,
        histograms,
        *outs[4:16],
        *back,
        *outs[19:],
    )


def solution(mesh):
    by_dp, by_pipe, copied = P("dp"), P("pipe"), P()
    return jax.shard_map(
        shards,
        mesh=mesh,
        in_specs=(by_dp,) * 4 + (by_pipe,) * 6 + (copied,) * 9,
        out_specs=(copied,) * 4 + (by_pipe,) * 6 + (copied,) * 9 + (by_pipe,) * 2 + (copied,),
        check_vma=False,
    )
```

```python
import functools

import jax
import jax.numpy as jnp
from jax import lax
from jax.experimental import pallas as pl
from jax.experimental.pallas import tpu as pltpu
from jax.sharding import PartitionSpec as P

D = 128
HEADS = 6
HEAD_DIM = 64
FF = 1024
CODEBOOK = 256
LEVELS = 4
BUCKETS = 32
DOMAINS = 3
HIST_LEN = 81
STEP = 5
CODES = 1024
LANES = 128
WIDTH = HEADS * HEAD_DIM
MIXW = 6 * WIDTH
COLS = MIXW + 2 * FF
BLOCKS = COLS // LANES
KEYS = 96
GROUP = 4
WIDE = GROUP * LANES
PAIRS = HEADS // 2
FIRST = 4 * WIDTH
REST = COLS - FIRST
USER_ROWS = 400
MESH = pl.DeviceIdType.MESH

norm_eps = 1e-06
beta_one = 0.9
beta_two = 0.999
adam_eps = 1e-08
clip_norm = 0.5
rate_matrix = 0.04
rate_gain = 0.8
rate_small = 0.3
decay_matrix = 0.01

f32 = jnp.float32
bf16 = jnp.bfloat16


def iota(shape, axis):
    return lax.broadcasted_iota(jnp.int32, shape, axis)


def mul(left, right):
    return jnp.dot(left, right, preferred_element_type=f32)


def mul_t(left, right):
    return lax.dot_general(left, right, (((1,), (1,)), ((), ())), preferred_element_type=f32)


def mul_exact(left, right):
    return jnp.dot(left, right, preferred_element_type=f32, precision=lax.Precision.HIGHEST)


def mul_exact_t(left, right):
    return lax.dot_general(
        left,
        right,
        (((1,), (1,)), ((), ())),
        preferred_element_type=f32,
        precision=lax.Precision.HIGHEST,
    )


def onehot(ids, rows):
    return jnp.where(iota((rows, ids.shape[1]), 0) == ids, 1.0, 0.0).astype(bf16)


def inverse_rms(x):
    return lax.rsqrt(jnp.mean(x * x, axis=0, keepdims=True) + norm_eps)


def norm_low(x, inverse, gain):
    return (x * inverse * gain).astype(bf16)


def norm_back(x, inverse, gain, upstream):
    scaled = x * inverse
    inner = upstream * gain
    back = inverse * (inner - scaled * jnp.mean(inner * scaled, axis=0, keepdims=True))
    return back, upstream * scaled


def block_diag(pair):
    zero = jnp.zeros((HEAD_DIM, LANES), pair.dtype)
    left = jnp.concatenate([pair[:HEAD_DIM], zero], 0)
    right = jnp.concatenate([zero, pair[HEAD_DIM:]], 0)
    return jnp.concatenate([left, right], 1)


def diagonal(both):
    return jnp.concatenate([both[:HEAD_DIM, :LANES], both[HEAD_DIM:, LANES:]], 0)


def stack(both):
    return jnp.concatenate([both[:, :LANES], both[:, LANES:]], 0)


def pad_keys(table):
    if table.shape[0] == LANES:
        return table
    zero = jnp.zeros((LANES - table.shape[0], table.shape[1]), table.dtype)
    return jnp.concatenate([table, zero], 0)


def attend(keys, query, values, bias):
    scores = mul(keys, block_diag(query)) + bias
    top = jnp.max(scores, axis=0, keepdims=True)
    chance = jnp.exp(scores - top)
    total = jnp.sum(chance, axis=0, keepdims=True)
    chance = (chance * (1.0 / total)).astype(bf16)
    mixed = diagonal(mul(values, pad_keys(chance))).astype(bf16)
    return chance, mixed


def attend_back(keys_t, query, values, back_mixed, chance):
    exact = chance.astype(f32)
    spread = block_diag(back_mixed)
    back_chance = mul(values, spread)
    inner = jnp.sum(back_chance * exact, axis=0, keepdims=True)
    back_scores = exact * (back_chance - inner)
    low = pad_keys(back_scores.astype(bf16))
    back_query = diagonal(mul(keys_t, low)).astype(bf16)
    back_keys = diagonal(mul_t(query, stack(low))).astype(bf16)
    back_values = diagonal(mul_t(back_mixed, stack(pad_keys(chance)))).astype(bf16)
    return back_query, back_keys, back_values, back_scores


def split_low(x):
    high = x.astype(bf16)
    return jnp.concatenate([high, (x - high.astype(f32)).astype(bf16)], 0)


def stages(dp):
    bits = [2**k for k in range(dp.bit_length() - 1)]
    near = bits[1:4]
    return [("dp", bit) for bit in bits[:1] + bits[4:] + near] + [("pipe", 1)]


def side_of(stage):
    axis, bit = stage
    return lax.rem(lax.div(lax.axis_index(axis), bit), 2)


def partner_of(stage):
    axis, bit = stage
    return {axis: lax.axis_index(axis) + bit * (1 - 2 * side_of(stage))}


def shares(dp, rows, across=0):
    held = [rows]
    depth = len(stages(dp)) - 1
    for k in range(depth + across):
        later = min(3, depth - 1 - k) + across if k < depth else 0
        half = held[-1] // 2
        held.append(half if half % (16 * 2**later) == 0 else held[-1])
    return held


def span(start, size):
    return pl.ds(pl.multiple_of(start, 16), size)


def step_kernel(n, dp, *refs):
    codes_ref, users_ref, user_row_ref, targets_ref, domains_ref, bias_ref, gains_ref = refs[:7]
    mixer_ref, feed_ref, embed_ref = refs[7:10]
    out_ref, out_user_ref, out_ids_ref, out_slot_ref, out_stat_ref = refs[10:15]
    x0_s, x1_s, x2_s, qkv_s, p_s, o_s, r_s, mem_s, dz_s, wn_s, wt_s, ext_s = refs[15:27]
    gain_s, ebias_s, dbias_s, g0_s, ge_s, gbias_s, ggain_s, rows_s, user_s, ids_s = refs[27:37]
    cross_s, cross_back_s, pc_s, oc_s, rest_s, first_s, codes_s, slot_s, user_low_s, own_slot_s = refs[37:47]
    stat_s, stat_land, near_first, near_codes, local_sems, sends, recvs = refs[47:54]
    lands = refs[54:]
    order = stages(dp)
    across = order[-1]
    depth = len(order)
    chunks = n // GROUP
    section = lax.axis_index("pipe")
    used = [0]

    def remote_to(source, target, device):
        index = used[0]
        used[0] += 1
        return pltpu.make_async_remote_copy(
            src_ref=source,
            dst_ref=target,
            send_sem=sends.at[index],
            recv_sem=recvs.at[index],
            device_id=device,
            device_id_type=MESH,
        )

    def remote(source, target, stage):
        return remote_to(source, target, partner_of(stage))

    near, far = order[-4:], order[:-4]
    masks = range(1, 2 ** len(near))

    def device_of(mask):
        place = {"dp": lax.axis_index("dp"), "pipe": lax.axis_index("pipe")}
        for i, (axis, bit) in enumerate(near):
            if mask >> i & 1:
                place[axis] = place[axis] + bit * (1 - 2 * side_of((axis, bit)))
        return place

    def shift_of(mask, lefts):
        total = 0
        for i, left in enumerate(lefts):
            side = side_of(near[i])
            total = total + (1 - side if mask >> i & 1 else side) * left
        return total

    locals_in = []
    for block in range(BLOCKS):
        lanes = slice(block * LANES, (block + 1) * LANES)
        if block < MIXW // LANES:
            source = mixer_ref.at[0, :, lanes]
        else:
            source = feed_ref.at[0, :, slice(lanes.start - MIXW, lanes.stop - MIXW)]
        locals_in.append(pltpu.make_async_copy(source, g0_s.at[block], local_sems.at[block]))
    vocabulary = embed_ref.shape[0]
    flat = x2_s.at[pl.ds(0, vocabulary)]
    load_embed = pltpu.make_async_copy(embed_ref, flat, local_sems.at[BLOCKS])
    for copy in locals_in:
        copy.start()
    load_embed.start()

    barrier = pltpu.get_barrier_semaphore()
    for stage in far:
        pl.semaphore_signal(barrier, inc=1, device_id=partner_of(stage), device_id_type=MESH)
    for mask in masks:
        pl.semaphore_signal(barrier, inc=1, device_id=device_of(mask), device_id_type=MESH)
    pl.semaphore_wait(barrier, len(far) + len(masks))

    scale = HEAD_DIM**-0.5
    cross_scale = jnp.where(section == 1, scale, 1.0).astype(f32)
    for copy in locals_in:
        copy.wait()
    for block in range(BLOCKS):
        value = g0_s[block]
        if block < 3:
            value = value * scale
        elif 12 <= block < 15:
            value = value * cross_scale
        wn_s[section, :, block * LANES : (block + 1) * LANES] = value.astype(bf16)
    half = D // 2
    mine = span(side_of(order[0]) * half, half)
    pieces = (slice(0, FIRST), slice(FIRST, COLS))
    over = [
        remote(wn_s.at[section, mine, piece], wn_s.at[section, mine, piece], across)
        for piece in pieces
    ]
    for copy in over:
        copy.start()

    ids_s[:, : HIST_LEN - 1] = codes_ref[pl.ds(pl.multiple_of(section * n, 8), n), :]
    lane, row = iota((n, LANES), 1), iota((n, LANES), 0)
    ids = ids_s[...] + ((lane & 3) << 8)
    ids = jnp.where(lane < HIST_LEN - 1, ids, jnp.where(lane == HIST_LEN - 1, CODES + row, -1))
    ids_s[...] = ids
    count = targets_ref.shape[1]
    history, token = iota((count, LANES), 0), iota((count, LANES), 1)
    pick = jnp.where((token >> 2) + section * n == history, 1.0, 0.0)
    level, place = iota((LEVELS, LANES), 0), iota((LEVELS, LANES), 1) & 3
    target = mul(targets_ref[...].astype(f32), pick) + (level * CODEBOOK).astype(f32)
    goal = jnp.sum(jnp.where(level == place, target, 0.0), axis=0, keepdims=True).astype(jnp.int32)
    start_ids = jnp.sum(
        jnp.where(level == place - 1, target, 0.0), axis=0, keepdims=True
    ).astype(jnp.int32)
    domain = mul(domains_ref[...].astype(f32), pick)
    pick = jnp.where(lax.rem(token, n) + section * n == history, 1.0, 0.0)
    own_users = mul_exact(user_row_ref[...].astype(f32), pick)

    counts = [
        jnp.sum(jnp.where(domain == d, 1.0, 0.0), axis=1, keepdims=True) for d in range(DOMAINS)
    ]
    counts += [jnp.zeros((1, 1), f32)] * (8 - DOMAINS)
    stat_s[0, 8:, :] = jnp.broadcast_to(jnp.concatenate(counts, 0), (8, LANES))
    histogram = mul_t(jnp.ones((8, LANES), bf16), onehot(goal, CODES))
    for r in range(8):
        stat_s[0, r : r + 1, :] = histogram[:1, r * LANES : (r + 1) * LANES]
    slot = 0
    for k, stage in enumerate(order):
        slot = slot + side_of(stage) * 2 ** (depth - 1 - k)
    owner = iota((8, LANES), 1) // n
    own_users = jnp.broadcast_to(own_users, (8, LANES)).astype(jnp.int32)
    slot_s[...] = jnp.where(owner == lax.rem(slot, LANES // n), own_users, 0)
    store_ids = pltpu.make_async_copy(slot_s, out_ids_ref.at[slot], local_sems.at[BLOCKS + 1])
    store_ids.start()
    store_ids.wait()

    def slots_of(j):
        return pl.ds(lax.div(slot, 2**j) * 2**j, 2**j)

    early = []
    for j, stage in enumerate(reversed(order)):
        held = out_ids_ref.at[slots_of(j)]
        early.append(
            (
                remote(stat_s.at[j], stat_land.at[j], stage),
                remote(held, held, stage),
            )
        )

    def early_step(j):
        if j > 0:
            for copy in early[j - 1]:
                copy.wait()
            stat_s[j] = stat_s[j - 1] + stat_land[j - 1]
        if j < depth:
            for copy in early[j]:
                copy.start()

    eye = jnp.where(iota((LANES, LANES), 0) == iota((LANES, LANES), 1), 1.0, 0.0).astype(bf16)
    load_embed.wait()

    def fetch(i, carry):
        user_s[pl.ds(i, 1), :] = x2_s[pl.ds(CODES + users_ref[section * n + i], 1), :]
        return carry

    lax.fori_loop(0, n, fetch, 0)
    for block in range(CODES // LANES + 1):
        if block < CODES // LANES:
            rows = x2_s[block * LANES : (block + 1) * LANES, :]
            codes_s[block * LANES : (block + 1) * LANES, :] = rows.astype(bf16)
            width = LANES
        else:
            rows = user_s[...]
            width = n
        high = rows.astype(bf16)
        low = (rows - high.astype(f32)).astype(bf16)
        lanes = slice(block * LANES, block * LANES + width)
        ext_s[:D, lanes] = mul_t(eye, high).astype(bf16)
        ext_s[D:, lanes] = mul_t(eye, low).astype(bf16)

    def lookup(c, carry):
        ids = jnp.concatenate([ids_s[pl.ds(GROUP * c + i, 1), :] for i in range(GROUP)], 1)
        both = mul(ext_s[...], onehot(ids, CODES + n))
        x0_s[c] = both[:D] + both[D:]
        return carry

    lax.fori_loop(0, chunks, lookup, 0)

    for g in range(7):
        gain_s[g] = jnp.broadcast_to(gains_ref[g : g + 1, :], (LANES, LANES)).T

    def positions(axis):
        index = iota((KEYS, LANES), axis)
        return jnp.where(index == HIST_LEN - 1, 0, index + 1)

    key, query = positions(0), positions(1)
    distance = jnp.abs(query - key)
    remoteness = jnp.zeros_like(distance)
    for edge in (12, 16, 23, 32, 46, 64, 91):
        remoteness = remoteness + (distance >= edge).astype(jnp.int32)
    nearby = jnp.minimum(jnp.where(distance < 8, distance, 8 + remoteness), 15)
    buckets = nearby + jnp.where(key > query, 16, 0)
    real = iota((KEYS, LANES), 0) < HIST_LEN
    for head in range(HEADS):
        lanes = slice((head % 2) * LANES, (head % 2 + 1) * LANES)

        def choose(b, table):
            return jnp.where(buckets == b, bias_ref[head, 0, b], table)

        table = lax.fori_loop(0, BUCKETS, choose, jnp.zeros((KEYS, LANES), f32))
        ebias_s[head // 2, :, lanes] = jnp.where(real, table, -1e30)
    key, query = iota((LANES, LANES), 0), iota((LANES, LANES), 1)
    offset = query - key
    seen = ((key >> 2) == (query >> 2)) & (offset >= 0)
    for head in range(HEADS):
        lanes = slice((head % 2) * LANES, (head % 2 + 1) * LANES)
        table = jnp.full((LANES, LANES), -1e30, f32)
        for b in range(LEVELS):
            table = jnp.where(seen & (offset == b), bias_ref[head, 1, b], table)
        dbias_s[head // 2, :, lanes] = table

    def transpose_weights(which, first, last):
        for block in range(first, last):
            place = slice(block * LANES, (block + 1) * LANES)
            wt_s[which, place, :] = wn_s[which, :, place].T

    beside = []
    for piece in pieces:
        came = wn_s.at[1 - section, mine, piece]
        beside.append(remote(came, came, order[0]))
    over[0].wait()
    beside[0].start()
    transpose_weights(section, 0, BLOCKS)
    beside[0].wait()
    transpose_weights(1 - section, 0, FIRST // LANES)

    def rest_arrives():
        over[1].wait()
        beside[1].start()
        beside[1].wait()
        transpose_weights(1 - section, FIRST // LANES, BLOCKS)

    def gain(g, width):
        column = gain_s[g]
        return column if width == LANES else jnp.concatenate([column] * (width // LANES), 1)

    def encode(c, carry):
        for j in range(depth + 1):
            pl.when(c == j)(functools.partial(early_step, j))
        x0 = x0_s[c]
        h = norm_low(x0, inverse_rms(x0), gain(0, WIDE))
        for j in range(3):
            part = slice(j * WIDTH, (j + 1) * WIDTH)
            qkv_s[c, part, :] = mul(wt_s[0, part, :], h).astype(bf16)
        for i in range(GROUP):
            lanes = slice(i * LANES, (i + 1) * LANES)
            for j in range(PAIRS):
                part = slice(j * LANES, (j + 1) * LANES)
                keys = slice(WIDTH + j * LANES, WIDTH + (j + 1) * LANES)
                chance, mixed = attend(
                    qkv_s[c, keys, lanes].T[:KEYS],
                    qkv_s[c, part, lanes],
                    qkv_s[c, 2 * WIDTH + j * LANES : 2 * WIDTH + (j + 1) * LANES, lanes],
                    ebias_s[j],
                )
                p_s[GROUP * c + i, j] = chance
                o_s[c, part, lanes] = mixed
        x1 = x0 + mul(wn_s[0, :, 3 * WIDTH : 4 * WIDTH], o_s[c])
        x1_s[c] = x1
        pl.when(c == 0)(rest_arrives)
        h = norm_low(x1, inverse_rms(x1), gain(1, WIDE))
        for j in range(2):
            part = slice(j * FF // 2, (j + 1) * FF // 2)
            lifted = mul(wt_s[0, MIXW + j * FF // 2 : MIXW + (j + 1) * FF // 2, :], h)
            r_s[c, part, :] = jnp.maximum(lifted, 0.0).astype(bf16)
        x2 = x1 + mul(wn_s[0, :, MIXW + FF :], r_s[c])
        put_wide(x2_s, c, x2)
        e = norm_low(x2, inverse_rms(x2), gain(2, WIDE))
        for j in range(2):
            part = slice(j * WIDTH, (j + 1) * WIDTH)
            mem_s[c, part, :] = mul(
                wt_s[0, 4 * WIDTH + j * WIDTH : 4 * WIDTH + (j + 1) * WIDTH, :], e
            ).astype(bf16)
        return carry

    def put_wide(ref, c, value):
        for i in range(GROUP):
            ref[pl.ds(pl.multiple_of((GROUP * c + i) * D, D), D), :] = value[
                :, i * LANES : (i + 1) * LANES
            ]

    def get_wide(ref, c):
        return jnp.concatenate(
            [ref[pl.ds(pl.multiple_of((GROUP * c + i) * D, D), D), :] for i in range(GROUP)], 1
        )

    lax.fori_loop(0, chunks, encode, 0)
    for j in range(chunks, depth + 1):
        early_step(j)
    out_stat_ref[...] = stat_s[depth, :8, :]

    def put_blocks(first, value):
        for index in range(value.shape[1] // LANES):
            block = first + index
            part = value[:, index * LANES : (index + 1) * LANES].astype(bf16)
            if block < FIRST // LANES:
                first_s[1, block * D : (block + 1) * D, :] = part
            else:
                block -= FIRST // LANES
                rest_s[1, block * D : (block + 1) * D, :] = part

    def add_blocks(first, value):
        for index in range(value.shape[1] // LANES):
            g0_s[first + index] += value[:, index * LANES : (index + 1) * LANES]

    start = onehot(start_ids, CODES)
    both = mul(ext_s[:, :CODES], start)
    y0 = both[:D] + both[D:]
    inverse0 = inverse_rms(y0)
    h0 = norm_low(y0, inverse0, gain(3, LANES))
    dz_s[:, :LANES] = mul(wt_s[1, : 3 * WIDTH, :], h0).astype(bf16)
    both = mul(mul_t(eye, h0).astype(bf16), wn_s[1, :, WIDTH : 3 * WIDTH]).astype(bf16)
    self_chance = []
    mixed_parts = []
    for j in range(PAIRS):
        part = slice(j * LANES, (j + 1) * LANES)
        chance, mixed = attend(
            both[:, part],
            dz_s[part, :LANES],
            dz_s[2 * WIDTH + j * LANES : 2 * WIDTH + (j + 1) * LANES, :LANES],
            dbias_s[j],
        )
        self_chance.append(chance)
        mixed_parts.append(mixed)
    self_values = both[:, WIDTH:]
    self_mixed = jnp.concatenate(mixed_parts, 0)
    y1 = y0 + mul(wn_s[1, :, 3 * WIDTH : 4 * WIDTH], self_mixed)
    inverse1 = inverse_rms(y1)
    h1 = norm_low(y1, inverse1, gain(4, LANES))
    cross_s[...] = mul(wt_s[1, 4 * WIDTH : 5 * WIDTH, :], h1).astype(bf16)

    def rows_of(g, table):
        row, token = iota((LANES, LANES), 0), iota((LANES, LANES), 1)
        rep = jnp.where(token == 16 * g + 4 * (row >> 5) + (row & 3), 1.0, 0.0).astype(bf16)
        rows = mul_t(rep, table)
        mask = (iota(rows.shape, 1) >> 6) == ((iota(rows.shape, 0) & 31) >> 2)
        return jnp.where(mask, rows, 0.0).astype(bf16)

    def head_mask(shape):
        return (iota(shape, 0) >> 6) == ((iota(shape, 1) & 31) >> 2)

    def rows_t_of(g, table):
        token, row = iota((LANES, LANES), 0), iota((LANES, LANES), 1)
        rep = jnp.where(token == 16 * g + 4 * (row >> 5) + (row & 3), 1.0, 0.0).astype(bf16)
        rows = mul(table, rep)
        return jnp.where(head_mask(rows.shape), rows, 0.0).astype(bf16)

    def gather_rows(ref):
        total = jnp.zeros((WIDTH, LANES), f32)
        for g in range(chunks):
            row, token = iota((LANES, LANES), 0), iota((LANES, LANES), 1)
            rep = jnp.where(token == 16 * g + 4 * (row >> 5) + (row & 3), 1.0, 0.0).astype(bf16)
            total = total + mul(ref[g], rep)
        return total.astype(bf16)

    def blocks_of(table):
        owner = iota(table.shape, 0) >> 5
        zero = jnp.zeros_like(table)
        return jnp.concatenate(
            [jnp.where(owner == j, table, zero) for j in range(GROUP)], 1
        ).astype(bf16)

    def row_products(rows, ref, g, first):
        parts = []
        for j in range(0, GROUP, 2):
            pair = slice(j * LANES, (j + 2) * LANES)
            both = mul(rows[32 * j : 32 * j + 64], ref[g, first : first + WIDTH, pair])
            parts += [both[:32, :LANES], both[32:, LANES:]]
        return jnp.concatenate(parts, 0)

    def cross(g, carry):
        queries = rows_of(g, cross_s[...])
        scores = row_products(queries, mem_s, g, 0)
        scores = jnp.where(iota(scores.shape, 1) < HIST_LEN, scores, -1e30)
        chance = jnp.exp(scores - jnp.max(scores, axis=1, keepdims=True))
        chance = chance * (1.0 / jnp.sum(chance, axis=1, keepdims=True))
        pc_s[g] = chance
        mixed = mul_t(mem_s[g, WIDTH:, :], blocks_of(chance))
        oc_s[g] = jnp.where(head_mask(mixed.shape), mixed, 0.0).astype(bf16)
        return carry

    lax.fori_loop(0, chunks, cross, 0)
    cross_mixed = gather_rows(oc_s)
    y2 = y1 + mul(wn_s[1, :, 5 * WIDTH : 6 * WIDTH], cross_mixed)
    inverse2 = inverse_rms(y2)
    h2 = norm_low(y2, inverse2, gain(5, LANES))
    lifted = mul(wt_s[1, MIXW : MIXW + FF, :], h2)
    active = jnp.maximum(lifted, 0.0).astype(bf16)
    y3 = y2 + mul(wn_s[1, :, MIXW + FF :], active)
    inverse3 = inverse_rms(y3)
    final = norm_low(y3, inverse3, gain(6, LANES))
    logits = mul(codes_s[...], final)
    top = jnp.max(logits, axis=0, keepdims=True)
    log_total = top + jnp.log(jnp.sum(jnp.exp(logits - top), axis=0, keepdims=True))
    match = iota(logits.shape, 0) == goal
    picked = jnp.sum(jnp.where(match, logits, 0.0), axis=0, keepdims=True)
    weight = jnp.zeros((1, LANES), f32)
    for d in range(DOMAINS):
        share = 1.0 / (DOMAINS * jnp.maximum(stat_s[depth, 8 + d : 9 + d, :], 1.0))
        weight = weight + jnp.where(domain == d, share, 0.0)
    loss = jnp.sum(weight * (log_total - picked), axis=1, keepdims=True)
    back_logits = (
        weight * (jnp.exp(logits - log_total) - jnp.where(match, 1.0, 0.0))
    ).astype(bf16)
    back_final = mul(ext_s[:D, :CODES], back_logits)
    table_grad = mul_t(back_logits, final)
    back, gain_grad = norm_back(y3, inverse3, gain(6, LANES), back_final)
    ggain_s[6] = gain_grad
    low = back.astype(bf16)
    put_blocks(26, mul_t(low, active))
    back_lifted = jnp.where(lifted > 0, mul(wt_s[1, MIXW + FF :, :], low), 0.0).astype(bf16)
    put_blocks(18, mul_t(h2, back_lifted))
    more, gain_grad = norm_back(
        y2, inverse2, gain(5, LANES), mul(wn_s[1, :, MIXW : MIXW + FF], back_lifted)
    )
    ggain_s[5] = gain_grad
    back = back + more
    low = back.astype(bf16)
    put_blocks(15, mul_t(low, cross_mixed))
    cross_back_s[...] = mul(wt_s[1, 5 * WIDTH : 6 * WIDTH, :], low).astype(bf16)

    def cross_back(g, carry):
        mixed_rows = rows_of(g, cross_back_s[...])
        back_chance = row_products(mixed_rows, mem_s, g, WIDTH)
        chance = pc_s[g]
        inner = jnp.sum(back_chance * chance, axis=1, keepdims=True)
        spread = blocks_of(chance * (back_chance - inner))
        total = mul_t(mem_s[g, :WIDTH, :], spread)
        mem_s[g, :WIDTH, :] = mul(rows_t_of(g, cross_s[...]), spread).astype(bf16)
        mem_s[g, WIDTH:, :] = mul(rows_t_of(g, cross_back_s[...]), blocks_of(chance)).astype(bf16)
        oc_s[g] = jnp.where(head_mask(total.shape), total, 0.0).astype(bf16)
        return carry

    lax.fori_loop(0, chunks, cross_back, 0)
    back_query = gather_rows(oc_s)
    put_blocks(12, mul_t(h1, back_query) * HEAD_DIM**-0.5)
    more, gain_grad = norm_back(
        y1, inverse1, gain(4, LANES), mul(wn_s[1, :, 4 * WIDTH : 5 * WIDTH], back_query)
    )
    ggain_s[4] = gain_grad
    back = back + more
    low = back.astype(bf16)
    put_blocks(9, mul_t(low, self_mixed))
    back_mixed = mul(wt_s[1, 3 * WIDTH : 4 * WIDTH, :], low).astype(bf16)
    self_scores = []
    for j in range(PAIRS):
        part = slice(j * LANES, (j + 1) * LANES)
        keys = slice(WIDTH + j * LANES, WIDTH + (j + 1) * LANES)
        values = slice(2 * WIDTH + j * LANES, 2 * WIDTH + (j + 1) * LANES)
        one, two, three, scores = attend_back(
            dz_s[keys, :LANES],
            dz_s[part, :LANES],
            self_values[:, part],
            back_mixed[part],
            self_chance[j],
        )
        dz_s[part, LANES : 2 * LANES] = one
        dz_s[keys, LANES : 2 * LANES] = two
        dz_s[values, LANES : 2 * LANES] = three
        self_scores.append(scores)
    put_blocks(0, mul_t(h0, dz_s[:WIDTH, LANES : 2 * LANES]) * HEAD_DIM**-0.5)
    put_blocks(3, mul_t(h0, dz_s[WIDTH:, LANES : 2 * LANES]))
    more, gain_grad = norm_back(
        y0, inverse0, gain(3, LANES), mul(wn_s[1, :, : 3 * WIDTH], dz_s[:, LANES : 2 * LANES])
    )
    ggain_s[3] = gain_grad
    back = back + more
    spread = mul_t(start, split_low(back))
    ge_s[:CODES, :] = table_grad + spread[:, :D] + spread[:, D:]
    ge_s[CODES:, :] = jnp.zeros((n, D), f32)
    rows_s[...] = jnp.zeros_like(rows_s)
    for head in range(HEADS):
        lanes = slice((head % 2) * LANES, (head % 2 + 1) * LANES)
        for b in range(LEVELS):
            hit = jnp.where(offset == b, self_scores[head // 2][:, lanes], 0.0)
            rows_s[head, BUCKETS + b : BUCKETS + b + 1, :] = jnp.sum(hit, axis=0, keepdims=True)

    def reducing(buffer, kept, held, upto):
        steps, at = [], 0
        for k, stage in enumerate(order[:upto]):
            rows, left = held[k], held[k + 1]
            side = side_of(stage)
            if left < rows:
                source = buffer.at[span(at + (1 - side) * left, left)]
                at = at + side * left
            else:
                source = buffer.at[span(at, rows)]
            steps.append((remote(source, kept[k], stage), at, left))
        return steps, at, held

    def begin(steps, k):
        steps[k][0].start()

    def finish(steps, buffer, kept, k):
        copy, at, left = steps[k]
        copy.wait()
        place = span(at, left)
        total = buffer[place, :].astype(f32) + kept[k][...].astype(f32)
        buffer[place, :] = total.astype(bf16)

    flat_depth = depth - 1
    held_rest, held_first, held_codes = shares(dp, REST), shares(dp, FIRST), shares(dp, CODES, 1)
    land, rest = {}, lands
    for name, number in (
        ("rest0", flat_depth),
        ("rest1", flat_depth),
        ("first1", flat_depth),
        ("first0", len(far)),
        ("codes", len(far)),
    ):
        land[name], rest = rest[:number], rest[number:]
    land_rest, land_first = rest
    rest1 = reducing(rest_s.at[1], land["rest1"], held_rest, flat_depth)
    first1 = reducing(first_s.at[1], land["first1"], held_first, flat_depth)
    rest0 = reducing(rest_s.at[0], land["rest0"], held_rest, flat_depth)
    first0 = reducing(first_s.at[0], land["first0"], held_first, len(far))
    codes = reducing(codes_s, land["codes"], held_codes, len(far))

    def step1(k):
        if k > 0:
            finish(rest1[0], rest_s.at[1], land["rest1"], k - 1)
            finish(first1[0], first_s.at[1], land["first1"], k - 1)
        if k < flat_depth:
            begin(rest1[0], k)
            begin(first1[0], k)

    def crossing(buffer, target, at, rows):
        source = buffer.at[1 - section, span(at, rows)]
        return remote(source, target, across)

    cross_rest = crossing(rest_s, land_rest, rest1[1], rest1[2][-1])
    cross_first = crossing(first_s, land_first, first1[1], first1[2][-1])

    def settle(copy, buffer, landed, at, rows, base):
        copy.wait()
        value = (buffer[section, span(at, rows), :].astype(f32) + landed[...].astype(f32)).astype(
            bf16
        )
        out_ref[span(base + at, rows), :] = value
        value = value.astype(f32)
        return jnp.sum(value * value, axis=0, keepdims=True)

    def gathering(base, at, held):
        steps = []
        for k in reversed(range(flat_depth)):
            rows, left = held[k], held[k + 1]
            if left < rows:
                place = out_ref.at[span(base + at, left)]
                steps.append(remote(place, place, order[k]))
                at = at - side_of(order[k]) * left
            else:
                steps.append(None)
        return steps

    gather_rest = gathering(0, rest1[1], rest1[2])

    def step0(k):
        if k > 0 and k <= flat_depth:
            finish(rest0[0], rest_s.at[0], land["rest0"], k - 1)
        if k < flat_depth:
            begin(rest0[0], k)
        if k == flat_depth:
            cross_rest.start()
        if k == flat_depth + 1:
            squares = settle(cross_rest, rest_s, land_rest, rest1[1], rest1[2][-1], 0)
            own_slot_s[16:17, :] = squares / (dp * rest1[2][-1] // REST)
        if k > flat_depth + 1 and gather_rest[k - flat_depth - 2] is not None:
            gather_rest[k - flat_depth - 2].wait()
        if flat_depth < k < 2 * flat_depth + 1 and gather_rest[k - flat_depth - 1] is not None:
            gather_rest[k - flat_depth - 1].start()

    g0_s[...] = jnp.zeros_like(g0_s)
    gbias_s[...] = jnp.zeros_like(gbias_s)
    for g in range(3):
        ggain_s[g] = jnp.zeros((D, LANES), f32)

    def fold(x):
        return sum(x[:, i * LANES : (i + 1) * LANES] for i in range(GROUP))

    def back_rest(c, carry):
        for j in range(flat_depth + 1):
            pl.when(c == j)(functools.partial(step1, j))
        x2 = get_wide(x2_s, c)
        inverse = inverse_rms(x2)
        back_memory = mem_s[c]
        add_blocks(12, mul_t(norm_low(x2, inverse, gain(2, WIDE)), back_memory))
        back, gain_grad = norm_back(
            x2, inverse, gain(2, WIDE), mul(wn_s[0, :, 4 * WIDTH : 6 * WIDTH], back_memory)
        )
        ggain_s[2] += fold(gain_grad)
        low = back.astype(bf16)
        active = r_s[c]
        add_blocks(26, mul_t(low, active))
        back_active = mul(wt_s[0, MIXW + FF :, :], low)
        back_lifted = jnp.where(active.astype(f32) > 0, back_active, 0.0).astype(bf16)
        x1 = x1_s[c]
        inverse = inverse_rms(x1)
        add_blocks(18, mul_t(norm_low(x1, inverse, gain(1, WIDE)), back_lifted))
        more, gain_grad = norm_back(
            x1, inverse, gain(1, WIDE), mul(wn_s[0, :, MIXW : MIXW + FF], back_lifted)
        )
        ggain_s[1] += fold(gain_grad)
        put_wide(x2_s, c, back + more)
        return carry

    lax.fori_loop(0, chunks, back_rest, 0)
    for j in range(chunks, flat_depth + 1):
        step1(j)
    for block in range(REST // D):
        rest_s[0, block * D : (block + 1) * D, :] = g0_s[FIRST // D + block].astype(bf16)

    def back_first(c, carry):
        for j in range(min(chunks, 2 * flat_depth + 2)):
            pl.when(c == j)(functools.partial(step0, j))
        back = get_wide(x2_s, c)
        low = back.astype(bf16)
        add_blocks(9, mul_t(low, o_s[c]))
        back_mixed = mul(wt_s[0, 3 * WIDTH : 4 * WIDTH, :], low).astype(bf16)
        for i in range(GROUP):
            lanes = slice(i * LANES, (i + 1) * LANES)
            for j in range(PAIRS):
                part = slice(j * LANES, (j + 1) * LANES)
                keys = slice(WIDTH + j * LANES, WIDTH + (j + 1) * LANES)
                values = slice(2 * WIDTH + j * LANES, 2 * WIDTH + (j + 1) * LANES)
                one, two, three, scores = attend_back(
                    qkv_s[c, keys, lanes],
                    qkv_s[c, part, lanes],
                    qkv_s[c, values, lanes].T[:KEYS],
                    back_mixed[part, lanes],
                    p_s[GROUP * c + i, j],
                )
                mem_s[c, part, lanes] = one
                mem_s[c, keys, lanes] = two
                r_s[c, part, lanes] = three
                gbias_s[j] += scores
        x0 = x0_s[c]
        inverse = inverse_rms(x0)
        h = norm_low(x0, inverse, gain(0, WIDE))
        add_blocks(0, mul_t(h, mem_s[c]))
        add_blocks(6, mul_t(h, r_s[c, :WIDTH, :]))
        back_normed = mul(wn_s[0, :, : 2 * WIDTH], mem_s[c])
        back_normed = back_normed + mul(wn_s[0, :, 2 * WIDTH : 3 * WIDTH], r_s[c, :WIDTH, :])
        more, gain_grad = norm_back(x0, inverse, gain(0, WIDE), back_normed)
        ggain_s[0] += fold(gain_grad)
        ids = jnp.concatenate([ids_s[pl.ds(GROUP * c + i, 1), :] for i in range(GROUP)], 1)
        spread = mul_t(onehot(ids, CODES + n), split_low(back + more))
        ge_s[...] += spread[:, :D] + spread[:, D:]
        return carry

    lax.fori_loop(0, chunks, back_first, 0)

    for block in range(FIRST // D):
        value = g0_s[block]
        if block < 3:
            value = value * HEAD_DIM**-0.5
        first_s[0, block * D : (block + 1) * D, :] = value.astype(bf16)
    codes_s[...] = ge_s[:CODES, :].astype(bf16)
    begin(first0[0], 0)
    begin(codes[0], 0)
    user_low_s[...] = ge_s[CODES:, :].astype(bf16)
    store_users = pltpu.make_async_copy(
        user_low_s, out_user_ref.at[span(slot * n, n)], local_sems.at[BLOCKS + 2]
    )
    store_users.start()
    late = list(range(min(chunks, 2 * flat_depth + 2), 2 * flat_depth + 2))
    if late:
        step0(late.pop(0))

    ones = jnp.ones((8, LANES), f32)
    own_slot_s[8:16, :] = jnp.zeros((8, LANES), f32)
    for g in range(7):
        own_slot_s[g : g + 1, :] = mul_exact_t(ones, ggain_s[g])[:1]
    own_slot_s[7:8, :] = jnp.broadcast_to(loss, (1, LANES))

    def bucket_sums(b, carry):
        for head in range(HEADS):
            lanes = slice((head % 2) * LANES, (head % 2 + 1) * LANES)
            hit = jnp.where(buckets == b, gbias_s[head // 2, :, lanes], 0.0)
            rows_s[head, pl.ds(b, 1), :] = jnp.sum(hit, axis=0, keepdims=True)
        return carry

    lax.fori_loop(0, BUCKETS, bucket_sums, 0)
    for head in range(HEADS):
        sums = mul_exact_t(ones, rows_s[head])
        own_slot_s[8 + head : 9 + head, : 2 * BUCKETS] = sums[:1]
    own_slot_s[19:, :] = jnp.zeros((5, LANES), f32)

    for k in range(len(far)):
        finish(first0[0], first_s.at[0], land["first0"], k)
        finish(codes[0], codes_s, land["codes"], k)
        if k + 1 < len(far):
            begin(first0[0], k + 1)
            begin(codes[0], k + 1)

    first_at, first_left = first0[1], held_first[len(far) + 1 :]
    codes_at, codes_left = codes[1], held_codes[len(far) + 1 :]
    size, code_size = first_left[-1], codes_left[-1]
    mine_first = first_at + shift_of(0, first_left)
    mine_codes = codes_at + shift_of(0, codes_left)
    inside, crossing_first, everyone = [], [], []
    for mask in masks:
        source = first_s.at[0, span(first_at + shift_of(mask, first_left), size)]
        copy = remote_to(source, near_first.at[mask], device_of(mask))
        (crossing_first if mask >> 3 else inside).append(copy)
    for mask in masks:
        source = codes_s.at[span(codes_at + shift_of(mask, codes_left), code_size)]
        everyone.append(remote_to(source, near_codes.at[mask], device_of(mask)))
    store_users.wait()
    held = out_user_ref.at[span(slot * n, n)]
    users_out = [remote_to(held, held, device_of(mask)) for mask in masks]

    @pl.when(section == 0)
    def _():
        for copy in inside:
            copy.start()
        cross_first.start()

    @pl.when(section == 1)
    def _():
        for copy in crossing_first:
            copy.start()

    for copy in everyone + users_out:
        copy.start()
    for step in late:
        step0(step)

    def keep_first(value):
        value = value.astype(bf16)
        out_ref[span(REST + mine_first, size), :] = value
        value = value.astype(f32)
        squares = jnp.sum(value * value, axis=0, keepdims=True)
        own_slot_s[17:18, :] = squares / (dp * size // FIRST)

    @pl.when(section == 0)
    def _():
        for copy in inside:
            copy.wait()
        for copy in crossing_first:
            copy.wait_recv()
        cross_first.wait_send()
        value = first_s[0, span(mine_first, size), :].astype(f32)
        for mask in masks:
            value = value + near_first[mask].astype(f32)
        keep_first(value)

    @pl.when(section == 1)
    def _():
        for copy in crossing_first:
            copy.wait_send()
        cross_first.wait_recv()
        value = first_s[1, span(mine_first, size), :].astype(f32)
        keep_first(value + land_first[...].astype(f32))

    for copy in everyone:
        copy.wait()
    value = codes_s[span(mine_codes, code_size), :].astype(f32)
    for mask in masks:
        value = value + near_codes[mask].astype(f32)
    value = value.astype(bf16)
    out_ref[span(COLS + mine_codes, code_size), :] = value
    value = value.astype(f32)
    squares = jnp.sum(value * value, axis=0, keepdims=True)
    own_slot_s[18:19, :] = squares / (2 * dp * code_size // CODES)

    store_slot = pltpu.make_async_copy(
        own_slot_s, out_slot_ref.at[slot], local_sems.at[BLOCKS + 3]
    )
    store_slot.start()

    copies = []
    place = out_ref.at[span(REST + mine_first, size)]
    code_place = out_ref.at[span(COLS + mine_codes, code_size)]
    for mask in masks:
        device = device_of(mask)
        if not mask >> 3:
            copies.append(remote_to(place, place, device))
        copies.append(remote_to(code_place, code_place, device))
    for copy in copies:
        copy.start()
    store_slot.wait()
    held = out_slot_ref.at[slot]
    slots_out = [remote_to(held, held, device_of(mask)) for mask in masks]
    for copy in slots_out:
        copy.start()
    copies += slots_out
    for copy in copies + users_out:
        copy.wait()
    for j, k in enumerate(reversed(range(len(far)))):
        stage = far[k]
        copies = []
        if held_first[k + 1] < held_first[k]:
            place = out_ref.at[span(REST + first_at, held_first[k + 1])]
            copies.append(remote(place, place, stage))
            first_at = first_at - side_of(stage) * held_first[k + 1]
        if held_codes[k + 1] < held_codes[k]:
            place = out_ref.at[span(COLS + codes_at, held_codes[k + 1])]
            copies.append(remote(place, place, stage))
            codes_at = codes_at - side_of(stage) * held_codes[k + 1]
        slots = 16 * 2**j
        first_slot = lax.div(slot, slots) * slots
        held = out_slot_ref.at[pl.ds(first_slot, slots)]
        copies.append(remote(held, held, stage))
        held = out_user_ref.at[span(first_slot * n, slots * n)]
        copies.append(remote(held, held, stage))
        for copy in copies:
            copy.start()
        for copy in copies:
            copy.wait()


def gradients(codes, users, targets, domains, bias, gains, mixer, feed, embedding, dp):
    n = users.shape[0] // 2
    chunks = n // GROUP
    order = stages(dp)
    depth = len(order)
    devices = 2 * dp
    vmem = pl.BlockSpec(memory_space=pltpu.VMEM)
    smem = pl.BlockSpec(memory_space=pltpu.SMEM)
    hbm = pl.BlockSpec(memory_space=pl.ANY)
    stat = (16, LANES)
    held_rest, held_first, held_codes = shares(dp, REST), shares(dp, FIRST), shares(dp, CODES, 1)
    plane, far = depth - 1, depth - 4
    sizes = [*held_rest[1:] * 2, *held_first[1:]]
    sizes += [*held_first[1 : far + 1], *held_codes[1 : far + 1], held_rest[-1], held_first[-1]]
    lands = [pltpu.VMEM((rows, D), bf16) for rows in sizes]
    copies = 128 + 16 * depth
    return pl.pallas_call(
        functools.partial(step_kernel, n, dp),
        out_shape=(
            jax.ShapeDtypeStruct((COLS + CODES, D), bf16),
            jax.ShapeDtypeStruct((devices * n, D), bf16),
            jax.ShapeDtypeStruct((devices, 8, LANES), jnp.int32),
            jax.ShapeDtypeStruct((devices, 24, LANES), f32),
            jax.ShapeDtypeStruct((8, LANES), f32),
        ),
        in_specs=[vmem, smem, vmem, vmem, vmem, smem, vmem, hbm, hbm, hbm],
        out_specs=(vmem, hbm, hbm, hbm, vmem),
        scratch_shapes=[
            pltpu.VMEM((chunks, D, WIDE), f32),
            pltpu.VMEM((chunks, D, WIDE), f32),
            pltpu.VMEM((n * D, LANES), f32),
            pltpu.VMEM((chunks, 3 * WIDTH, WIDE), bf16),
            pltpu.VMEM((n, PAIRS, KEYS, 2 * LANES), bf16),
            pltpu.VMEM((chunks, WIDTH, WIDE), bf16),
            pltpu.VMEM((chunks, FF, WIDE), bf16),
            pltpu.VMEM((chunks, 2 * WIDTH, WIDE), bf16),
            pltpu.VMEM((3 * WIDTH, 2 * LANES), bf16),
            pltpu.VMEM((2, D, COLS), bf16),
            pltpu.VMEM((2, COLS, D), bf16),
            pltpu.VMEM((2 * D, CODES + n), bf16),
            pltpu.VMEM((7, D, LANES), f32),
            pltpu.VMEM((PAIRS, KEYS, 2 * LANES), f32),
            pltpu.VMEM((PAIRS, LANES, 2 * LANES), f32),
            pltpu.VMEM((BLOCKS, D, LANES), f32),
            pltpu.VMEM((CODES + n, D), f32),
            pltpu.VMEM((PAIRS, KEYS, 2 * LANES), f32),
            pltpu.VMEM((7, D, LANES), f32),
            pltpu.VMEM((HEADS, 2 * BUCKETS, LANES), f32),
            pltpu.VMEM((n, D), f32),
            pltpu.VMEM((n, LANES), jnp.int32),
            pltpu.VMEM((WIDTH, LANES), bf16),
            pltpu.VMEM((WIDTH, LANES), bf16),
            pltpu.VMEM((chunks, LANES, LANES), f32),
            pltpu.VMEM((chunks, WIDTH, LANES), bf16),
            pltpu.VMEM((2, REST, D), bf16),
            pltpu.VMEM((2, FIRST, D), bf16),
            pltpu.VMEM((CODES, D), bf16),
            pltpu.VMEM((8, LANES), jnp.int32),
            pltpu.VMEM((n, D), bf16),
            pltpu.VMEM((24, LANES), f32),
            pltpu.VMEM((depth + 1,) + stat, f32),
            pltpu.VMEM((depth,) + stat, f32),
            pltpu.VMEM((16, held_first[-1], D), bf16),
            pltpu.VMEM((16, held_codes[-1], D), bf16),
            pltpu.SemaphoreType.DMA((BLOCKS + 4,)),
            pltpu.SemaphoreType.DMA((copies,)),
            pltpu.SemaphoreType.DMA((copies,)),
        ]
        + lands,
        compiler_params=pltpu.CompilerParams(
            collective_id=0, has_side_effects=True, vmem_limit_bytes=63 * 2**20
        ),
        name="gradients",
    )(codes, users, users.reshape(1, -1), targets, domains, bias, gains, mixer, feed, embedding)


def adam(weight, moment, square, slope, rate, decay):
    moment = beta_one * moment + (1 - beta_one) * slope
    square = beta_two * square + (1 - beta_two) * slope * slope
    unbiased_moment = moment * (1 / (1 - beta_one**STEP))
    unbiased_square = square * (1 / (1 - beta_two**STEP))
    root = unbiased_square * lax.rsqrt(unbiased_square)
    step = unbiased_moment / (root + adam_eps) + decay * weight
    return weight - rate * step, moment, square


def update_kernel(*refs):
    parts_in, big_in, small_in, refs = refs[:5], refs[5:14], refs[14:20], refs[20:]
    loss_ref, norm_ref, section_ref, hist_ref = refs[:4]
    big_out, small_out, low_out, refs = refs[4:13], refs[13:19], refs[19:22], refs[22:]
    parts, hold, low_hold = refs[:5], refs[5:14], refs[14:17]
    user_grad, part_sems, in_sems, out_sems = refs[17:]
    grad_ref, user_ref, ids_ref, slot_ref, stat_ref = parts
    arrivals = [pltpu.make_async_copy(parts_in[i], parts[i], part_sems.at[i]) for i in range(5)]
    loads = [pltpu.make_async_copy(big_in[i], hold[i], in_sems.at[i]) for i in range(9)]
    for load in arrivals[1:] + arrivals[:1] + loads:
        load.start()
    for arrival in arrivals:
        arrival.wait()

    users = user_grad.shape[0]
    span = min(1024, user_ref.shape[0])
    slots = span // LANES * (ids_ref.shape[0] * LANES // user_ref.shape[0])
    fit = ids_ref.shape[0] * LANES // user_ref.shape[0]
    user_grad[...] = jnp.zeros_like(user_grad)

    def scatter(part, carry):
        rows = user_ref[pl.ds(pl.multiple_of(part * span, span), span), :]
        lanes = []
        for group in range(span // LANES):
            total = ids_ref[part * slots + group * fit, :1, :]
            for other in range(1, fit):
                total = total + ids_ref[part * slots + group * fit + other, :1, :]
            lanes.append(total)
        ids = jnp.concatenate(lanes, 1)
        for block in range(users // USER_ROWS):
            place = slice(block * USER_ROWS, (block + 1) * USER_ROWS)
            hit = iota((USER_ROWS, span), 0) + block * USER_ROWS == ids
            user_grad[place, :] += mul(jnp.where(hit, 1.0, 0.0).astype(bf16), rows)
        return carry

    lax.fori_loop(0, user_ref.shape[0] // span, scatter, 0)

    def total(x):
        return jnp.sum(jnp.sum(x, axis=0, keepdims=True), axis=1, keepdims=True)

    def slot_sum(first):
        def add(i, value):
            return value + slot_ref[2 * i + first]

        zero = jnp.zeros(slot_ref.shape[1:], f32)
        return lax.fori_loop(0, slot_ref.shape[0] // 2, add, zero)

    even, odd = slot_sum(0), slot_sum(1)
    section_squares = [total(x[16:17] + x[17:18]) for x in (even, odd)]
    small = even[:16] + odd[:16]
    rest = total(even[18:19] + odd[18:19])
    user_values = user_grad[...]
    rest = rest + total(user_values * user_values)
    lane, line = iota(small.shape, 1), iota(small.shape, 0)
    counted = (line < 7) | ((line > 7) & (lane < 2 * BUCKETS))
    small_kept = jnp.where(counted, small, 0.0)
    rest = rest + total(small_kept * small_kept)
    norm = jnp.sqrt(section_squares[0] + section_squares[1] + rest)
    factor = jnp.minimum(1.0, clip_norm / (norm + 1e-06))
    loss_ref[0] = small[7, 0]
    norm_ref[0] = norm[0, 0]
    for s in range(2):
        section_ref[s] = jnp.sqrt(section_squares[s])[0, 0]
    for row in range(8):
        lanes = slice((row % 2) * LANES, (row % 2 + 1) * LANES)
        hist_ref[row // 2 : row // 2 + 1, lanes] = stat_ref[row : row + 1, :]

    outs = adam(
        small_in[0][...], small_in[1][...], small_in[2][...], factor * small[:7], rate_gain, 0.0
    )
    for ref, value in zip(small_out[:3], outs):
        ref[...] = value
    for head in range(HEADS):
        for s in range(2):
            slope = factor * small[8 + head : 9 + head, s * BUCKETS : (s + 1) * BUCKETS]
            one = slice(s, s + 1)
            outs = adam(
                small_in[3][head, one, :],
                small_in[4][head, one, :],
                small_in[5][head, one, :],
                slope,
                rate_small,
                0.0,
            )
            for ref, value in zip(small_out[3:], outs):
                ref[head, one, :] = value

    stores = []

    def store(kind, place):
        first = 3 * kind
        pieces = [(hold[first + i], big_out[first + i]) for i in range(3)]
        pieces.append((low_hold[kind], low_out[kind]))
        for source, target in pieces:
            copy = pltpu.make_async_copy(
                source.at[place], target.at[place], out_sems.at[len(stores)]
            )
            copy.start()
            stores.append(copy)

    def step(kind, place, slope):
        first = 3 * kind
        outs = adam(
            hold[first][place],
            hold[first + 1][place],
            hold[first + 2][place],
            factor * slope,
            rate_matrix,
            decay_matrix,
        )
        for i in range(3):
            hold[first + i][place] = outs[i]
        low_hold[kind][place] = outs[0].astype(bf16)

    def block_of(block):
        first = FIRST // D
        place = block - first if block >= first else REST // D + block
        return grad_ref[place * D : (place + 1) * D, :].astype(f32)

    for i in range(3):
        loads[i].wait()
    for part in range(6):
        for block in range(3 * part, 3 * part + 3):
            lanes = slice(block * LANES, (block + 1) * LANES)
            step(0, (0, slice(None), lanes), block_of(block))
        store(0, (0, slice(None), slice(3 * part * LANES, 3 * (part + 1) * LANES)))
    for i in range(3, 6):
        loads[i].wait()
    for part in range(4):
        for block in range(4 * part, 4 * part + 4):
            lanes = slice(block * LANES, (block + 1) * LANES)
            step(1, (0, slice(None), lanes), block_of(MIXW // LANES + block))
        store(1, (0, slice(None), slice(4 * part * LANES, 4 * (part + 1) * LANES)))
    for i in range(6, 9):
        loads[i].wait()
    for part in range(4):
        rows = slice(part * CODEBOOK, (part + 1) * CODEBOOK)
        step(2, (rows, slice(None)), grad_ref[COLS + rows.start : COLS + rows.stop, :].astype(f32))
        store(2, (rows, slice(None)))
    for part in range(users // USER_ROWS):
        rows = slice(part * USER_ROWS, (part + 1) * USER_ROWS)
        place = (slice(CODES + part * USER_ROWS, CODES + (part + 1) * USER_ROWS), slice(None))
        step(2, place, user_grad[rows, :])
        store(2, place)
    for copy in stores:
        copy.wait()


def update(reduced, mixers, feeds, embeds, gains, biases):
    vmem = pl.BlockSpec(memory_space=pltpu.VMEM)
    smem = pl.BlockSpec(memory_space=pltpu.SMEM)
    hbm = pl.BlockSpec(memory_space=pl.ANY)
    big = [*mixers, *feeds, *embeds]
    small = [*gains, *biases]
    low = [jax.ShapeDtypeStruct(x[0].shape, bf16) for x in (mixers, feeds, embeds)]
    users = embeds[0].shape[0] - CODES
    pieces = 4 * (6 + 4 + 4 + users // USER_ROWS)
    return pl.pallas_call(
        update_kernel,
        out_shape=[
            jax.ShapeDtypeStruct((1,), f32),
            jax.ShapeDtypeStruct((1,), f32),
            jax.ShapeDtypeStruct((2,), f32),
            jax.ShapeDtypeStruct((LEVELS, CODEBOOK), f32),
        ]
        + [jax.ShapeDtypeStruct(x.shape, f32) for x in big + small]
        + low,
        in_specs=[hbm] * 14 + [vmem] * 6,
        out_specs=[smem] * 3 + [vmem] + [hbm] * 9 + [vmem] * 6 + [hbm] * 3,
        scratch_shapes=[pltpu.VMEM(x.shape, x.dtype) for x in reduced]
        + [pltpu.VMEM(x.shape, f32) for x in big]
        + [pltpu.VMEM(x.shape, bf16) for x in low]
        + [
            pltpu.VMEM((users, D), f32),
            pltpu.SemaphoreType.DMA((5,)),
            pltpu.SemaphoreType.DMA((9,)),
            pltpu.SemaphoreType.DMA((pieces,)),
        ],
        compiler_params=pltpu.CompilerParams(vmem_limit_bytes=62 * 2**20),
        name="update",
    )(*reduced, *big, *small)


def shards(
    history_codes,
    user_ids,
    targets,
    domains,
    mixer,
    mixer_moment,
    mixer_square,
    feed,
    feed_moment,
    feed_square,
    embedding,
    embedding_moment,
    embedding_square,
    gains,
    gains_moment,
    gains_square,
    position_bias,
    bias_moment,
    bias_square,
):
    def turned(table):
        return jnp.transpose(table, (2, 0, 1))

    biases = [turned(x) for x in (position_bias, bias_moment, bias_square)]
    reduced = gradients(
        history_codes,
        user_ids,
        targets.T,
        domains.reshape(1, -1),
        biases[0],
        gains,
        mixer,
        feed,
        embedding,
        lax.axis_size("dp"),
    )
    outs = update(
        reduced,
        (mixer, mixer_moment, mixer_square),
        (feed, feed_moment, feed_square),
        (embedding, embedding_moment, embedding_square),
        (gains, gains_moment, gains_square),
        biases,
    )
    loss, norm, sections, histograms = outs[:4]
    back = [jnp.transpose(x, (1, 2, 0)) for x in outs[16:19]]
    return (
        loss.reshape(()),
        norm.reshape(()),
        sections,
        histograms,
        *outs[4:16],
        *back,
        *outs[19:],
    )


def solution(mesh):
    by_dp, by_pipe, copied = P("dp"), P("pipe"), P()
    return jax.shard_map(
        shards,
        mesh=mesh,
        in_specs=(by_dp,) * 4 + (by_pipe,) * 6 + (copied,) * 9,
        out_specs=(copied,) * 4 + (by_pipe,) * 6 + (copied,) * 9 + (by_pipe,) * 2 + (copied,),
        check_vma=False,
    )
```

```python
import functools

import jax
import jax.numpy as jnp
from jax import lax
from jax.experimental import pallas as pl
from jax.experimental.pallas import tpu as pltpu
from jax.sharding import PartitionSpec as P

D = 128
HEADS = 6
HEAD_DIM = 64
FF = 1024
CODEBOOK = 256
LEVELS = 4
BUCKETS = 32
DOMAINS = 3
HIST_LEN = 81
STEP = 5
CODES = 1024
LANES = 128
WIDTH = HEADS * HEAD_DIM
MIXW = 6 * WIDTH
COLS = MIXW + 2 * FF
BLOCKS = COLS // LANES
KEYS = 96
GROUP = 8
PACK = 96
WIDE = GROUP * PACK
SPAN = GROUP * LANES
COLUMNS = WIDE // LANES
PAIRS = HEADS // 2
FIRST = 4 * WIDTH
REST = COLS - FIRST
USER_ROWS = 400
MESH = pl.DeviceIdType.MESH

norm_eps = 1e-06
beta_one = 0.9
beta_two = 0.999
adam_eps = 1e-08
clip_norm = 0.5
rate_matrix = 0.04
rate_gain = 0.8
rate_small = 0.3
decay_matrix = 0.01

f32 = jnp.float32
bf16 = jnp.bfloat16


def iota(shape, axis):
    return lax.broadcasted_iota(jnp.int32, shape, axis)


def mul(left, right):
    return jnp.dot(left, right, preferred_element_type=f32)


def mul_t(left, right):
    return lax.dot_general(left, right, (((1,), (1,)), ((), ())), preferred_element_type=f32)


def mul_exact(left, right):
    return jnp.dot(left, right, preferred_element_type=f32, precision=lax.Precision.HIGHEST)


def mul_exact_t(left, right):
    return lax.dot_general(
        left,
        right,
        (((1,), (1,)), ((), ())),
        preferred_element_type=f32,
        precision=lax.Precision.HIGHEST,
    )


def onehot(ids, rows):
    return jnp.where(iota((rows, ids.shape[1]), 0) == ids, 1.0, 0.0).astype(bf16)


def inverse_rms(x):
    return lax.rsqrt(jnp.mean(x * x, axis=0, keepdims=True) + norm_eps)


def norm_low(x, inverse, gain):
    return (x * inverse * gain).astype(bf16)


def norm_back(x, inverse, gain, upstream):
    scaled = x * inverse
    inner = upstream * gain
    back = inverse * (inner - scaled * jnp.mean(inner * scaled, axis=0, keepdims=True))
    return back, upstream * scaled


def block_diag(pair):
    zero = jnp.zeros((HEAD_DIM, LANES), pair.dtype)
    left = jnp.concatenate([pair[:HEAD_DIM], zero], 0)
    right = jnp.concatenate([zero, pair[HEAD_DIM:]], 0)
    return jnp.concatenate([left, right], 1)


def diagonal(both):
    return jnp.concatenate([both[:HEAD_DIM, :LANES], both[HEAD_DIM:, LANES:]], 0)


def turn(x, shift):
    return x if shift % LANES == 0 else pltpu.roll(x, shift % LANES, 1)


def pack(tables):
    lane = iota(tables[0].shape, 1)
    columns = []
    for first in range(0, len(tables), 4):
        turned = [turn(tables[first + i], PACK * i) for i in range(4)]
        for i in range(3):
            columns.append(jnp.where(lane < PACK - 32 * i, turned[i], turned[i + 1]))
    return jnp.concatenate(columns, 1)


def unpack(x):
    lane = iota((x.shape[0], LANES), 1)
    tables = []
    for first in range(0, x.shape[1] // LANES, 3):
        a, b, c = [x[:, (first + i) * LANES : (first + i + 1) * LANES] for i in range(3)]
        tables.append(a)
        tables.append(jnp.where(lane < 32, turn(a, 32), turn(b, 32)))
        tables.append(jnp.where(lane < 64, turn(b, 64), turn(c, 64)))
        tables.append(turn(c, 96))
    return tables


def stack(both):
    return jnp.concatenate([both[:, :LANES], both[:, LANES:]], 0)


def pad_keys(table):
    if table.shape[0] == LANES:
        return table
    zero = jnp.zeros((LANES - table.shape[0], table.shape[1]), table.dtype)
    return jnp.concatenate([table, zero], 0)


def attend(keys, query, values, bias):
    scores = mul(keys, block_diag(query)) + bias
    top = jnp.max(scores, axis=0, keepdims=True)
    chance = jnp.exp(scores - top)
    total = jnp.sum(chance, axis=0, keepdims=True)
    chance = (chance * (1.0 / total)).astype(bf16)
    mixed = diagonal(mul(values, pad_keys(chance))).astype(bf16)
    return chance, mixed


def attend_back(keys_t, query, values, back_mixed, chance):
    exact = chance.astype(f32)
    spread = block_diag(back_mixed)
    back_chance = mul(values, spread)
    inner = jnp.sum(back_chance * exact, axis=0, keepdims=True)
    back_scores = exact * (back_chance - inner)
    low = pad_keys(back_scores.astype(bf16))
    back_query = diagonal(mul(keys_t, low)).astype(bf16)
    back_keys = diagonal(mul_t(query, stack(low))).astype(bf16)
    back_values = diagonal(mul_t(back_mixed, stack(pad_keys(chance)))).astype(bf16)
    return back_query, back_keys, back_values, back_scores


def split_low(x):
    high = x.astype(bf16)
    return jnp.concatenate([high, (x - high.astype(f32)).astype(bf16)], 0)


def stages(dp):
    bits = [2**k for k in range(dp.bit_length() - 1)]
    near = bits[1:4]
    return [("dp", bit) for bit in bits[:1] + bits[4:] + near] + [("pipe", 1)]


def side_of(stage):
    axis, bit = stage
    return lax.rem(lax.div(lax.axis_index(axis), bit), 2)


def partner_of(stage):
    axis, bit = stage
    return {axis: lax.axis_index(axis) + bit * (1 - 2 * side_of(stage))}


def shares(dp, rows, across=0):
    held = [rows]
    depth = len(stages(dp)) - 1
    for k in range(depth + across):
        later = min(3, depth - 1 - k) + across if k < depth else 0
        half = held[-1] // 2
        held.append(half if half % (16 * 2**later) == 0 else held[-1])
    return held


def span(start, size):
    return pl.ds(pl.multiple_of(start, 16), size)


def step_kernel(n, dp, *refs):
    codes_ref, users_ref, user_row_ref, targets_ref, domains_ref, bias_ref, gains_ref = refs[:7]
    mixer_ref, feed_ref, embed_ref = refs[7:10]
    out_ref, out_user_ref, out_ids_ref, out_slot_ref, out_stat_ref = refs[10:15]
    x0_s, x1_s, x2_s, qkv_s, p_s, o_s, r_s, mem_s, dz_s, wn_s, wt_s, ext_s = refs[15:27]
    gain_s, ebias_s, dbias_s, g0_s, ge_s, gbias_s, ggain_s, rows_s, user_s, ids_s = refs[27:37]
    cross_s, cross_back_s, pc_s, oc_s, rest_s, first_s, codes_s, slot_s, user_low_s, own_slot_s, id_rows_s, hot_s = refs[37:49]
    stat_s, stat_land, near_first, near_codes, local_sems, sends, recvs = refs[49:56]
    lands = refs[56:]
    order = stages(dp)
    across = order[-1]
    depth = len(order)
    chunks = n // GROUP
    section = lax.axis_index("pipe")
    used = [0]

    def remote_to(source, target, device):
        index = used[0]
        used[0] += 1
        return pltpu.make_async_remote_copy(
            src_ref=source,
            dst_ref=target,
            send_sem=sends.at[index],
            recv_sem=recvs.at[index],
            device_id=device,
            device_id_type=MESH,
        )

    def remote(source, target, stage):
        return remote_to(source, target, partner_of(stage))

    near, far = order[-4:], order[:-4]
    masks = range(1, 2 ** len(near))

    def device_of(mask):
        place = {"dp": lax.axis_index("dp"), "pipe": lax.axis_index("pipe")}
        for i, (axis, bit) in enumerate(near):
            if mask >> i & 1:
                place[axis] = place[axis] + bit * (1 - 2 * side_of((axis, bit)))
        return place

    def shift_of(mask, lefts):
        total = 0
        for i, left in enumerate(lefts):
            side = side_of(near[i])
            total = total + (1 - side if mask >> i & 1 else side) * left
        return total

    locals_in = []
    for block in range(BLOCKS):
        lanes = slice(block * LANES, (block + 1) * LANES)
        if block < MIXW // LANES:
            source = mixer_ref.at[0, :, lanes]
        else:
            source = feed_ref.at[0, :, slice(lanes.start - MIXW, lanes.stop - MIXW)]
        locals_in.append(pltpu.make_async_copy(source, g0_s.at[block], local_sems.at[block]))
    vocabulary = embed_ref.shape[0]
    flat = x2_s.at[pl.ds(0, vocabulary)]
    load_embed = pltpu.make_async_copy(embed_ref, flat, local_sems.at[BLOCKS])
    for copy in locals_in:
        copy.start()
    load_embed.start()

    barrier = pltpu.get_barrier_semaphore()
    for stage in far:
        pl.semaphore_signal(barrier, inc=1, device_id=partner_of(stage), device_id_type=MESH)
    for mask in masks:
        pl.semaphore_signal(barrier, inc=1, device_id=device_of(mask), device_id_type=MESH)
    pl.semaphore_wait(barrier, len(far) + len(masks))

    scale = HEAD_DIM**-0.5
    cross_scale = jnp.where(section == 1, scale, 1.0).astype(f32)
    for copy in locals_in:
        copy.wait()
    for block in range(BLOCKS):
        value = g0_s[block]
        if block < 3:
            value = value * scale
        elif 12 <= block < 15:
            value = value * cross_scale
        wn_s[section, :, block * LANES : (block + 1) * LANES] = value.astype(bf16)
    half = D // 2
    mine = span(side_of(order[0]) * half, half)
    pieces = (slice(0, FIRST), slice(FIRST, COLS))
    over = [
        remote(wn_s.at[section, mine, piece], wn_s.at[section, mine, piece], across)
        for piece in pieces
    ]
    for copy in over:
        copy.start()

    ids_s[:, : HIST_LEN - 1] = codes_ref[pl.ds(pl.multiple_of(section * n, 8), n), :]
    lane, row = iota((n, LANES), 1), iota((n, LANES), 0)
    ids = ids_s[...] + ((lane & 3) << 8)
    ids = jnp.where(lane < HIST_LEN - 1, ids, jnp.where(lane == HIST_LEN - 1, CODES + row, -1))
    ids_s[...] = ids
    packed = []
    for i in range(GROUP):
        rows = [ids_s[c * GROUP + i : c * GROUP + i + 1, :] for c in range(chunks)]
        rows += [jnp.zeros((8 - chunks, LANES), jnp.int32)]
        packed.append(jnp.concatenate(rows, 0))
    id_rows_s[...] = pack(packed)
    count = targets_ref.shape[1]
    history, token = iota((count, LANES), 0), iota((count, LANES), 1)
    pick = jnp.where((token >> 2) + section * n == history, 1.0, 0.0)
    level, place = iota((LEVELS, LANES), 0), iota((LEVELS, LANES), 1) & 3
    target = mul(targets_ref[...].astype(f32), pick) + (level * CODEBOOK).astype(f32)
    goal = jnp.sum(jnp.where(level == place, target, 0.0), axis=0, keepdims=True).astype(jnp.int32)
    start_ids = jnp.sum(
        jnp.where(level == place - 1, target, 0.0), axis=0, keepdims=True
    ).astype(jnp.int32)
    domain = mul(domains_ref[...].astype(f32), pick)
    pick = jnp.where(lax.rem(token, n) + section * n == history, 1.0, 0.0)
    own_users = mul_exact(user_row_ref[...].astype(f32), pick)

    counts = [
        jnp.sum(jnp.where(domain == d, 1.0, 0.0), axis=1, keepdims=True) for d in range(DOMAINS)
    ]
    counts += [jnp.zeros((1, 1), f32)] * (8 - DOMAINS)
    stat_s[0, 8:, :] = jnp.broadcast_to(jnp.concatenate(counts, 0), (8, LANES))
    histogram = mul_t(jnp.ones((8, LANES), bf16), onehot(goal, CODES))
    for r in range(8):
        stat_s[0, r : r + 1, :] = histogram[:1, r * LANES : (r + 1) * LANES]
    slot = 0
    for k, stage in enumerate(order):
        slot = slot + side_of(stage) * 2 ** (depth - 1 - k)
    owner = iota((8, LANES), 1) // n
    own_users = jnp.broadcast_to(own_users, (8, LANES)).astype(jnp.int32)
    slot_s[...] = jnp.where(owner == lax.rem(slot, LANES // n), own_users, 0)
    store_ids = pltpu.make_async_copy(slot_s, out_ids_ref.at[slot], local_sems.at[BLOCKS + 1])
    store_ids.start()
    store_ids.wait()

    def slots_of(j):
        return pl.ds(lax.div(slot, 2**j) * 2**j, 2**j)

    early = []
    for j, stage in enumerate(reversed(order)):
        held = out_ids_ref.at[slots_of(j)]
        early.append(
            (
                remote(stat_s.at[j], stat_land.at[j], stage),
                remote(held, held, stage),
            )
        )

    def early_step(j):
        if j > 0:
            for copy in early[j - 1]:
                copy.wait()
            stat_s[j] = stat_s[j - 1] + stat_land[j - 1]
        if j < depth:
            for copy in early[j]:
                copy.start()

    eye = jnp.where(iota((LANES, LANES), 0) == iota((LANES, LANES), 1), 1.0, 0.0).astype(bf16)
    load_embed.wait()

    def fetch(i, carry):
        user_s[pl.ds(i, 1), :] = x2_s[pl.ds(CODES + users_ref[section * n + i], 1), :]
        return carry

    lax.fori_loop(0, n, fetch, 0)
    for block in range(CODES // LANES + 1):
        if block < CODES // LANES:
            rows = x2_s[block * LANES : (block + 1) * LANES, :]
            codes_s[block * LANES : (block + 1) * LANES, :] = rows.astype(bf16)
            width = LANES
        else:
            rows = user_s[...]
            width = n
        high = rows.astype(bf16)
        low = (rows - high.astype(f32)).astype(bf16)
        lanes = slice(block * LANES, block * LANES + width)
        ext_s[:D, lanes] = mul_t(eye, high).astype(bf16)
        ext_s[D:, lanes] = mul_t(eye, low).astype(bf16)

    def find(c):
        ids = id_rows_s[pl.ds(c, 1), :]
        for first in range(0, CODES + n, LANES):
            rows = min(LANES, CODES + n - first)
            hot_s[first : first + rows, :] = onehot(ids - first, rows)

    def lookup(c, carry):
        find(c)
        both = mul(ext_s[...], hot_s[...])
        x0_s[c] = both[:D] + both[D:]
        return carry

    lax.fori_loop(0, chunks, lookup, 0)

    for g in range(7):
        gain_s[g] = jnp.broadcast_to(gains_ref[g : g + 1, :], (LANES, LANES)).T

    def positions(axis):
        index = iota((KEYS, LANES), axis)
        return jnp.where(index == HIST_LEN - 1, 0, index + 1)

    key, query = positions(0), positions(1)
    distance = jnp.abs(query - key)
    remoteness = jnp.zeros_like(distance)
    for edge in (12, 16, 23, 32, 46, 64, 91):
        remoteness = remoteness + (distance >= edge).astype(jnp.int32)
    nearby = jnp.minimum(jnp.where(distance < 8, distance, 8 + remoteness), 15)
    buckets = nearby + jnp.where(key > query, 16, 0)
    real = iota((KEYS, LANES), 0) < HIST_LEN
    for head in range(HEADS):
        lanes = slice((head % 2) * LANES, (head % 2 + 1) * LANES)

        def choose(b, table):
            return jnp.where(buckets == b, bias_ref[head, 0, b], table)

        table = lax.fori_loop(0, BUCKETS, choose, jnp.zeros((KEYS, LANES), f32))
        ebias_s[head // 2, :, lanes] = jnp.where(real, table, -1e30)
    key, query = iota((LANES, LANES), 0), iota((LANES, LANES), 1)
    offset = query - key
    seen = ((key >> 2) == (query >> 2)) & (offset >= 0)
    for head in range(HEADS):
        lanes = slice((head % 2) * LANES, (head % 2 + 1) * LANES)
        table = jnp.full((LANES, LANES), -1e30, f32)
        for b in range(LEVELS):
            table = jnp.where(seen & (offset == b), bias_ref[head, 1, b], table)
        dbias_s[head // 2, :, lanes] = table

    def transpose_weights(which, first, last):
        for block in range(first, last):
            place = slice(block * LANES, (block + 1) * LANES)
            wt_s[which, place, :] = wn_s[which, :, place].T

    beside = []
    for piece in pieces:
        came = wn_s.at[1 - section, mine, piece]
        beside.append(remote(came, came, order[0]))
    over[0].wait()
    beside[0].start()
    transpose_weights(section, 0, BLOCKS)
    beside[0].wait()
    transpose_weights(1 - section, 0, FIRST // LANES)

    def rest_arrives():
        over[1].wait()
        beside[1].start()
        beside[1].wait()
        transpose_weights(1 - section, FIRST // LANES, BLOCKS)

    def gain(g, width):
        column = gain_s[g]
        return column if width == LANES else jnp.concatenate([column] * (width // LANES), 1)

    def at_chunk(c, step, point, points, count):
        for j in range(point, count, points):
            pl.when(c == j // points)(functools.partial(step, j))

    def spread_low(x):
        return jnp.concatenate([part.astype(bf16) for part in unpack(x)], 1)

    def packed(x):
        return pack([x[:, i * LANES : (i + 1) * LANES] for i in range(GROUP)])

    def encode(c, carry):
        at_chunk(c, early_step, 0, 2, depth + 1)
        x0 = x0_s[c]
        h = spread_low(x0 * inverse_rms(x0) * gain(0, WIDE))
        for j in range(3):
            part = slice(j * WIDTH, (j + 1) * WIDTH)
            qkv_s[c, part, :] = mul(wt_s[0, part, :], h).astype(bf16)
        for i in range(GROUP):
            lanes = slice(i * LANES, (i + 1) * LANES)
            for j in range(PAIRS):
                part = slice(j * LANES, (j + 1) * LANES)
                keys = slice(WIDTH + j * LANES, WIDTH + (j + 1) * LANES)
                chance, mixed = attend(
                    qkv_s[c, keys, lanes].T[:KEYS],
                    qkv_s[c, part, lanes],
                    qkv_s[c, 2 * WIDTH + j * LANES : 2 * WIDTH + (j + 1) * LANES, lanes],
                    ebias_s[j],
                )
                p_s[GROUP * c + i, j] = chance
                o_s[c, part, lanes] = mixed
        x1 = x0 + packed(mul(wn_s[0, :, 3 * WIDTH : 4 * WIDTH], o_s[c]))
        x1_s[c] = x1
        at_chunk(c, early_step, 1, 2, depth + 1)
        pl.when(c == 0)(rest_arrives)
        h = norm_low(x1, inverse_rms(x1), gain(1, WIDE))
        for j in range(2):
            part = slice(j * FF // 2, (j + 1) * FF // 2)
            lifted = mul(wt_s[0, MIXW + j * FF // 2 : MIXW + (j + 1) * FF // 2, :], h)
            r_s[c, part, :] = jnp.maximum(lifted, 0.0).astype(bf16)
        x2 = x1 + mul(wn_s[0, :, MIXW + FF :], r_s[c])
        put_wide(x2_s, c, x2)
        e = norm_low(x2, inverse_rms(x2), gain(2, WIDE))
        for j in range(2):
            part = slice(j * WIDTH, (j + 1) * WIDTH)
            mem_s[c, part, :] = mul(
                wt_s[0, 4 * WIDTH + j * WIDTH : 4 * WIDTH + (j + 1) * WIDTH, :], e
            ).astype(bf16)
        return carry

    def put_wide(ref, c, value):
        for i in range(COLUMNS):
            ref[pl.ds(pl.multiple_of((COLUMNS * c + i) * D, D), D), :] = value[
                :, i * LANES : (i + 1) * LANES
            ]

    def get_wide(ref, c):
        return jnp.concatenate(
            [ref[pl.ds(pl.multiple_of((COLUMNS * c + i) * D, D), D), :] for i in range(COLUMNS)], 1
        )

    lax.fori_loop(0, chunks, encode, 0)
    for j in range(2 * chunks, depth + 1):
        early_step(j)
    out_stat_ref[...] = stat_s[depth, :8, :]

    def put_blocks(first, value):
        for index in range(value.shape[1] // LANES):
            block = first + index
            part = value[:, index * LANES : (index + 1) * LANES].astype(bf16)
            if block < FIRST // LANES:
                first_s[1, block * D : (block + 1) * D, :] = part
            else:
                block -= FIRST // LANES
                rest_s[1, block * D : (block + 1) * D, :] = part

    def add_blocks(first, value):
        for index in range(value.shape[1] // LANES):
            g0_s[first + index] += value[:, index * LANES : (index + 1) * LANES]

    start = onehot(start_ids, CODES)
    both = mul(ext_s[:, :CODES], start)
    y0 = both[:D] + both[D:]
    inverse0 = inverse_rms(y0)
    h0 = norm_low(y0, inverse0, gain(3, LANES))
    dz_s[:, :LANES] = mul(wt_s[1, : 3 * WIDTH, :], h0).astype(bf16)
    both = mul(mul_t(eye, h0).astype(bf16), wn_s[1, :, WIDTH : 3 * WIDTH]).astype(bf16)
    self_chance = []
    mixed_parts = []
    for j in range(PAIRS):
        part = slice(j * LANES, (j + 1) * LANES)
        chance, mixed = attend(
            both[:, part],
            dz_s[part, :LANES],
            dz_s[2 * WIDTH + j * LANES : 2 * WIDTH + (j + 1) * LANES, :LANES],
            dbias_s[j],
        )
        self_chance.append(chance)
        mixed_parts.append(mixed)
    self_values = both[:, WIDTH:]
    self_mixed = jnp.concatenate(mixed_parts, 0)
    y1 = y0 + mul(wn_s[1, :, 3 * WIDTH : 4 * WIDTH], self_mixed)
    inverse1 = inverse_rms(y1)
    h1 = norm_low(y1, inverse1, gain(4, LANES))
    cross_s[...] = mul(wt_s[1, 4 * WIDTH : 5 * WIDTH, :], h1).astype(bf16)

    def spreader(g, turned):
        shape = (LANES, 32 * GROUP) if turned else (32 * GROUP, LANES)
        row, token = iota(shape, 1 if turned else 0), iota(shape, 0 if turned else 1)
        hit = token == 4 * GROUP * g + 4 * (row >> 5) + (row & 3)
        return jnp.where(hit, 1.0, 0.0).astype(bf16)

    def rows_of(g, table):
        rows = mul_t(spreader(g, False), table)
        mask = (iota(rows.shape, 1) >> 6) == ((iota(rows.shape, 0) & 31) >> 2)
        return jnp.where(mask, rows, 0.0).astype(bf16)

    def head_mask(shape):
        return (iota(shape, 0) >> 6) == ((iota(shape, 1) & 31) >> 2)

    def rows_t_of(g, table):
        rows = mul(table, spreader(g, True))
        return jnp.where(head_mask(rows.shape), rows, 0.0).astype(bf16)

    def gather_rows(ref):
        total = jnp.zeros((WIDTH, LANES), f32)
        for g in range(chunks):
            total = total + mul(ref[g], spreader(g, False))
        return total.astype(bf16)

    def blocks_of(table):
        rows = []
        for i in range(GROUP):
            part = table[32 * i : 32 * i + 32]
            column, shift = divmod(PACK * i, LANES)
            part = turn(part, shift)
            lane = iota(part.shape, 1)
            zero = jnp.zeros_like(part)
            columns = [zero] * COLUMNS
            columns[column] = jnp.where(lane >= shift, part, 0.0)
            if shift > LANES - PACK:
                columns[column + 1] = jnp.where(lane < shift, part, 0.0)
            rows.append(jnp.concatenate(columns, 1))
        return jnp.concatenate(rows, 0).astype(bf16)

    def row_products(rows, ref, g, first):
        both = mul(rows, ref[g, first : first + WIDTH, :])
        parts = []
        for i in range(GROUP):
            own = both[32 * i : 32 * i + 32]
            column, shift = divmod(PACK * i, LANES)
            part = turn(own[:, column * LANES : (column + 1) * LANES], -shift)
            if shift > LANES - PACK:
                after = turn(own[:, (column + 1) * LANES : (column + 2) * LANES], -shift)
                part = jnp.where(iota(part.shape, 1) < LANES - shift, part, after)
            parts.append(part)
        return jnp.concatenate(parts, 0)

    def cross(g, carry):
        queries = rows_of(g, cross_s[...])
        scores = row_products(queries, mem_s, g, 0)
        scores = jnp.where(iota(scores.shape, 1) < HIST_LEN, scores, -1e30)
        chance = jnp.exp(scores - jnp.max(scores, axis=1, keepdims=True))
        chance = chance * (1.0 / jnp.sum(chance, axis=1, keepdims=True))
        pc_s[g] = chance
        mixed = mul_t(mem_s[g, WIDTH:, :], blocks_of(chance))
        oc_s[g] = jnp.where(head_mask(mixed.shape), mixed, 0.0).astype(bf16)
        return carry

    lax.fori_loop(0, chunks, cross, 0)
    cross_mixed = gather_rows(oc_s)
    y2 = y1 + mul(wn_s[1, :, 5 * WIDTH : 6 * WIDTH], cross_mixed)
    inverse2 = inverse_rms(y2)
    h2 = norm_low(y2, inverse2, gain(5, LANES))
    lifted = mul(wt_s[1, MIXW : MIXW + FF, :], h2)
    active = jnp.maximum(lifted, 0.0).astype(bf16)
    y3 = y2 + mul(wn_s[1, :, MIXW + FF :], active)
    inverse3 = inverse_rms(y3)
    final = norm_low(y3, inverse3, gain(6, LANES))
    logits = mul(codes_s[...], final)
    top = jnp.max(logits, axis=0, keepdims=True)
    log_total = top + jnp.log(jnp.sum(jnp.exp(logits - top), axis=0, keepdims=True))
    match = iota(logits.shape, 0) == goal
    picked = jnp.sum(jnp.where(match, logits, 0.0), axis=0, keepdims=True)
    weight = jnp.zeros((1, LANES), f32)
    for d in range(DOMAINS):
        share = 1.0 / (DOMAINS * jnp.maximum(stat_s[depth, 8 + d : 9 + d, :], 1.0))
        weight = weight + jnp.where(domain == d, share, 0.0)
    loss = jnp.sum(weight * (log_total - picked), axis=1, keepdims=True)
    back_logits = (
        weight * (jnp.exp(logits - log_total) - jnp.where(match, 1.0, 0.0))
    ).astype(bf16)
    back_final = mul(ext_s[:D, :CODES], back_logits)
    table_grad = mul_t(back_logits, final)
    back, gain_grad = norm_back(y3, inverse3, gain(6, LANES), back_final)
    ggain_s[6] = gain_grad
    low = back.astype(bf16)
    put_blocks(26, mul_t(low, active))
    back_lifted = jnp.where(lifted > 0, mul(wt_s[1, MIXW + FF :, :], low), 0.0).astype(bf16)
    put_blocks(18, mul_t(h2, back_lifted))
    more, gain_grad = norm_back(
        y2, inverse2, gain(5, LANES), mul(wn_s[1, :, MIXW : MIXW + FF], back_lifted)
    )
    ggain_s[5] = gain_grad
    back = back + more
    low = back.astype(bf16)
    put_blocks(15, mul_t(low, cross_mixed))
    cross_back_s[...] = mul(wt_s[1, 5 * WIDTH : 6 * WIDTH, :], low).astype(bf16)

    def cross_back(g, carry):
        mixed_rows = rows_of(g, cross_back_s[...])
        back_chance = row_products(mixed_rows, mem_s, g, WIDTH)
        back_chance = jnp.where(iota(back_chance.shape, 1) < HIST_LEN, back_chance, 0.0)
        chance = pc_s[g]
        inner = jnp.sum(back_chance * chance, axis=1, keepdims=True)
        spread = blocks_of(chance * (back_chance - inner))
        total = mul_t(mem_s[g, :WIDTH, :], spread)
        mem_s[g, :WIDTH, :] = mul(rows_t_of(g, cross_s[...]), spread).astype(bf16)
        mem_s[g, WIDTH:, :] = mul(rows_t_of(g, cross_back_s[...]), blocks_of(chance)).astype(bf16)
        oc_s[g] = jnp.where(head_mask(total.shape), total, 0.0).astype(bf16)
        return carry

    lax.fori_loop(0, chunks, cross_back, 0)
    back_query = gather_rows(oc_s)
    put_blocks(12, mul_t(h1, back_query) * HEAD_DIM**-0.5)
    more, gain_grad = norm_back(
        y1, inverse1, gain(4, LANES), mul(wn_s[1, :, 4 * WIDTH : 5 * WIDTH], back_query)
    )
    ggain_s[4] = gain_grad
    back = back + more
    low = back.astype(bf16)
    put_blocks(9, mul_t(low, self_mixed))
    back_mixed = mul(wt_s[1, 3 * WIDTH : 4 * WIDTH, :], low).astype(bf16)
    self_scores = []
    for j in range(PAIRS):
        part = slice(j * LANES, (j + 1) * LANES)
        keys = slice(WIDTH + j * LANES, WIDTH + (j + 1) * LANES)
        values = slice(2 * WIDTH + j * LANES, 2 * WIDTH + (j + 1) * LANES)
        one, two, three, scores = attend_back(
            dz_s[keys, :LANES],
            dz_s[part, :LANES],
            self_values[:, part],
            back_mixed[part],
            self_chance[j],
        )
        dz_s[part, LANES : 2 * LANES] = one
        dz_s[keys, LANES : 2 * LANES] = two
        dz_s[values, LANES : 2 * LANES] = three
        self_scores.append(scores)
    put_blocks(0, mul_t(h0, dz_s[:WIDTH, LANES : 2 * LANES]) * HEAD_DIM**-0.5)
    put_blocks(3, mul_t(h0, dz_s[WIDTH:, LANES : 2 * LANES]))
    more, gain_grad = norm_back(
        y0, inverse0, gain(3, LANES), mul(wn_s[1, :, : 3 * WIDTH], dz_s[:, LANES : 2 * LANES])
    )
    ggain_s[3] = gain_grad
    back = back + more
    spread = mul_t(start, split_low(back))
    ge_s[:CODES, :] = table_grad + spread[:, :D] + spread[:, D:]
    ge_s[CODES:, :] = jnp.zeros((n, D), f32)
    rows_s[...] = jnp.zeros_like(rows_s)
    for head in range(HEADS):
        lanes = slice((head % 2) * LANES, (head % 2 + 1) * LANES)
        for b in range(LEVELS):
            hit = jnp.where(offset == b, self_scores[head // 2][:, lanes], 0.0)
            rows_s[head, BUCKETS + b : BUCKETS + b + 1, :] = jnp.sum(hit, axis=0, keepdims=True)

    def reducing(buffer, kept, held, upto):
        steps, at = [], 0
        for k, stage in enumerate(order[:upto]):
            rows, left = held[k], held[k + 1]
            side = side_of(stage)
            if left < rows:
                source = buffer.at[span(at + (1 - side) * left, left)]
                at = at + side * left
            else:
                source = buffer.at[span(at, rows)]
            steps.append((remote(source, kept[k], stage), at, left))
        return steps, at, held

    def begin(steps, k):
        steps[k][0].start()

    def finish(steps, buffer, kept, k):
        copy, at, left = steps[k]
        copy.wait()
        place = span(at, left)
        total = buffer[place, :].astype(f32) + kept[k][...].astype(f32)
        buffer[place, :] = total.astype(bf16)

    flat_depth = depth - 1
    held_rest, held_first, held_codes = shares(dp, REST), shares(dp, FIRST), shares(dp, CODES, 1)
    land, rest = {}, lands
    for name, number in (
        ("rest0", flat_depth),
        ("rest1", flat_depth),
        ("first1", flat_depth),
        ("first0", len(far)),
        ("codes", len(far)),
    ):
        land[name], rest = rest[:number], rest[number:]
    land_rest, land_first = rest
    rest1 = reducing(rest_s.at[1], land["rest1"], held_rest, flat_depth)
    first1 = reducing(first_s.at[1], land["first1"], held_first, flat_depth)
    rest0 = reducing(rest_s.at[0], land["rest0"], held_rest, flat_depth)
    first0 = reducing(first_s.at[0], land["first0"], held_first, len(far))
    codes = reducing(codes_s, land["codes"], held_codes, len(far))

    def step1(k):
        if k > 0:
            finish(rest1[0], rest_s.at[1], land["rest1"], k - 1)
            finish(first1[0], first_s.at[1], land["first1"], k - 1)
        if k < flat_depth:
            begin(rest1[0], k)
            begin(first1[0], k)

    def crossing(buffer, target, at, rows):
        source = buffer.at[1 - section, span(at, rows)]
        return remote(source, target, across)

    cross_rest = crossing(rest_s, land_rest, rest1[1], rest1[2][-1])
    cross_first = crossing(first_s, land_first, first1[1], first1[2][-1])

    def settle(copy, buffer, landed, at, rows, base):
        copy.wait()
        value = (buffer[section, span(at, rows), :].astype(f32) + landed[...].astype(f32)).astype(
            bf16
        )
        out_ref[span(base + at, rows), :] = value
        value = value.astype(f32)
        return jnp.sum(value * value, axis=0, keepdims=True)

    def gathering(base, at, held):
        steps = []
        for k in reversed(range(flat_depth)):
            rows, left = held[k], held[k + 1]
            if left < rows:
                place = out_ref.at[span(base + at, left)]
                steps.append(remote(place, place, order[k]))
                at = at - side_of(order[k]) * left
            else:
                steps.append(None)
        return steps

    gather_rest = gathering(0, rest1[1], rest1[2])

    def step0(k):
        if k > 0 and k <= flat_depth:
            finish(rest0[0], rest_s.at[0], land["rest0"], k - 1)
        if k < flat_depth:
            begin(rest0[0], k)
        if k == flat_depth:
            cross_rest.start()
        if k == flat_depth + 1:
            squares = settle(cross_rest, rest_s, land_rest, rest1[1], rest1[2][-1], 0)
            own_slot_s[16:17, :] = squares / (dp * rest1[2][-1] // REST)
        if k > flat_depth + 1 and gather_rest[k - flat_depth - 2] is not None:
            gather_rest[k - flat_depth - 2].wait()
        if flat_depth < k < 2 * flat_depth + 1 and gather_rest[k - flat_depth - 1] is not None:
            gather_rest[k - flat_depth - 1].start()

    g0_s[...] = jnp.zeros_like(g0_s)
    gbias_s[...] = jnp.zeros_like(gbias_s)
    for g in range(3):
        ggain_s[g] = jnp.zeros((D, LANES), f32)

    def fold(x):
        return sum(x[:, i * LANES : (i + 1) * LANES] for i in range(COLUMNS))

    def back_rest(c, carry):
        at_chunk(c, step1, 0, 2, flat_depth + 1)
        x2 = get_wide(x2_s, c)
        inverse = inverse_rms(x2)
        back_memory = mem_s[c]
        add_blocks(12, mul_t(norm_low(x2, inverse, gain(2, WIDE)), back_memory))
        back, gain_grad = norm_back(
            x2, inverse, gain(2, WIDE), mul(wn_s[0, :, 4 * WIDTH : 6 * WIDTH], back_memory)
        )
        ggain_s[2] += fold(gain_grad)
        low = back.astype(bf16)
        add_blocks(26, mul_t(low, r_s[c]))
        for j in range(4):
            part = slice(j * FF // 4, (j + 1) * FF // 4)
            back_active = mul(wt_s[0, MIXW + FF + part.start : MIXW + FF + part.stop, :], low)
            live = r_s[c, part, :].astype(f32) > 0
            r_s[c, part, :] = jnp.where(live, back_active, 0.0).astype(bf16)
        at_chunk(c, step1, 1, 2, flat_depth + 1)
        x1 = x1_s[c]
        inverse = inverse_rms(x1)
        add_blocks(18, mul_t(norm_low(x1, inverse, gain(1, WIDE)), r_s[c]))
        more, gain_grad = norm_back(
            x1, inverse, gain(1, WIDE), mul(wn_s[0, :, MIXW : MIXW + FF], r_s[c])
        )
        ggain_s[1] += fold(gain_grad)
        put_wide(x2_s, c, back + more)
        return carry

    lax.fori_loop(0, chunks, back_rest, 0)
    for j in range(2 * chunks, flat_depth + 1):
        step1(j)
    for block in range(REST // D):
        rest_s[0, block * D : (block + 1) * D, :] = g0_s[FIRST // D + block].astype(bf16)

    steps0 = 2 * flat_depth + 2

    def back_first(c, carry):
        at_chunk(c, step0, 0, 3, steps0)
        back = get_wide(x2_s, c)
        lane = iota((D, LANES), 1)
        low = [jnp.where(lane < PACK, part, 0.0).astype(bf16) for part in unpack(back)]
        low = jnp.concatenate(low, 1)
        add_blocks(9, mul_t(low, o_s[c]))
        o_s[c] = mul(wt_s[0, 3 * WIDTH : 4 * WIDTH, :], low).astype(bf16)
        for i in range(GROUP):
            if i == GROUP // 2:
                at_chunk(c, step0, 1, 3, steps0)
            lanes = slice(i * LANES, (i + 1) * LANES)
            for j in range(PAIRS):
                part = slice(j * LANES, (j + 1) * LANES)
                keys = slice(WIDTH + j * LANES, WIDTH + (j + 1) * LANES)
                values = slice(2 * WIDTH + j * LANES, 2 * WIDTH + (j + 1) * LANES)
                one, two, three, scores = attend_back(
                    qkv_s[c, keys, lanes],
                    qkv_s[c, part, lanes],
                    qkv_s[c, values, lanes].T[:KEYS],
                    o_s[c, part, lanes],
                    p_s[GROUP * c + i, j],
                )
                qkv_s[c, part, lanes] = one
                qkv_s[c, keys, lanes] = two
                qkv_s[c, values, lanes] = three
                gbias_s[j] += scores
        at_chunk(c, step0, 2, 3, steps0)
        x0 = x0_s[c]
        inverse = inverse_rms(x0)
        add_blocks(0, mul_t(spread_low(x0 * inverse * gain(0, WIDE)), qkv_s[c]))
        back_normed = packed(mul(wn_s[0, :, : 3 * WIDTH], qkv_s[c]))
        more, gain_grad = norm_back(x0, inverse, gain(0, WIDE), back_normed)
        ggain_s[0] += fold(gain_grad)
        find(c)
        spread = mul_t(hot_s[...], split_low(back + more))
        ge_s[...] += spread[:, :D] + spread[:, D:]
        return carry

    lax.fori_loop(0, chunks, back_first, 0)

    for block in range(FIRST // D):
        value = g0_s[block]
        if block < 3:
            value = value * HEAD_DIM**-0.5
        first_s[0, block * D : (block + 1) * D, :] = value.astype(bf16)
    codes_s[...] = ge_s[:CODES, :].astype(bf16)
    begin(first0[0], 0)
    begin(codes[0], 0)
    user_low_s[...] = ge_s[CODES:, :].astype(bf16)
    store_users = pltpu.make_async_copy(
        user_low_s, out_user_ref.at[span(slot * n, n)], local_sems.at[BLOCKS + 2]
    )
    store_users.start()
    late = list(range(min(3 * chunks, steps0), steps0))
    if late:
        step0(late.pop(0))

    ones = jnp.ones((8, LANES), f32)
    own_slot_s[8:16, :] = jnp.zeros((8, LANES), f32)
    for g in range(7):
        own_slot_s[g : g + 1, :] = mul_exact_t(ones, ggain_s[g])[:1]
    own_slot_s[7:8, :] = jnp.broadcast_to(loss, (1, LANES))

    def bucket_sums(b, carry):
        for head in range(HEADS):
            lanes = slice((head % 2) * LANES, (head % 2 + 1) * LANES)
            hit = jnp.where(buckets == b, gbias_s[head // 2, :, lanes], 0.0)
            rows_s[head, pl.ds(b, 1), :] = jnp.sum(hit, axis=0, keepdims=True)
        return carry

    lax.fori_loop(0, BUCKETS, bucket_sums, 0)
    for head in range(HEADS):
        sums = mul_exact_t(ones, rows_s[head])
        own_slot_s[8 + head : 9 + head, : 2 * BUCKETS] = sums[:1]
    own_slot_s[19:, :] = jnp.zeros((5, LANES), f32)

    for k in range(len(far)):
        finish(first0[0], first_s.at[0], land["first0"], k)
        finish(codes[0], codes_s, land["codes"], k)
        if k + 1 < len(far):
            begin(first0[0], k + 1)
            begin(codes[0], k + 1)

    first_at, first_left = first0[1], held_first[len(far) + 1 :]
    codes_at, codes_left = codes[1], held_codes[len(far) + 1 :]
    size, code_size = first_left[-1], codes_left[-1]
    mine_first = first_at + shift_of(0, first_left)
    mine_codes = codes_at + shift_of(0, codes_left)
    inside, crossing_first, everyone = [], [], []
    for mask in masks:
        source = first_s.at[0, span(first_at + shift_of(mask, first_left), size)]
        copy = remote_to(source, near_first.at[mask], device_of(mask))
        (crossing_first if mask >> 3 else inside).append(copy)
    for mask in masks:
        source = codes_s.at[span(codes_at + shift_of(mask, codes_left), code_size)]
        everyone.append(remote_to(source, near_codes.at[mask], device_of(mask)))
    store_users.wait()
    held = out_user_ref.at[span(slot * n, n)]
    users_out = [remote_to(held, held, device_of(mask)) for mask in masks]

    @pl.when(section == 0)
    def _():
        for copy in inside:
            copy.start()
        cross_first.start()

    @pl.when(section == 1)
    def _():
        for copy in crossing_first:
            copy.start()

    for copy in everyone + users_out:
        copy.start()
    for step in late:
        step0(step)

    def keep_first(value):
        value = value.astype(bf16)
        out_ref[span(REST + mine_first, size), :] = value
        value = value.astype(f32)
        squares = jnp.sum(value * value, axis=0, keepdims=True)
        own_slot_s[17:18, :] = squares / (dp * size // FIRST)

    @pl.when(section == 0)
    def _():
        for copy in inside:
            copy.wait()
        for copy in crossing_first:
            copy.wait_recv()
        cross_first.wait_send()
        value = first_s[0, span(mine_first, size), :].astype(f32)
        for mask in masks:
            value = value + near_first[mask].astype(f32)
        keep_first(value)

    @pl.when(section == 1)
    def _():
        for copy in crossing_first:
            copy.wait_send()
        cross_first.wait_recv()
        value = first_s[1, span(mine_first, size), :].astype(f32)
        keep_first(value + land_first[...].astype(f32))

    for copy in everyone:
        copy.wait()
    value = codes_s[span(mine_codes, code_size), :].astype(f32)
    for mask in masks:
        value = value + near_codes[mask].astype(f32)
    value = value.astype(bf16)
    out_ref[span(COLS + mine_codes, code_size), :] = value
    value = value.astype(f32)
    squares = jnp.sum(value * value, axis=0, keepdims=True)
    own_slot_s[18:19, :] = squares / (2 * dp * code_size // CODES)

    store_slot = pltpu.make_async_copy(
        own_slot_s, out_slot_ref.at[slot], local_sems.at[BLOCKS + 3]
    )
    store_slot.start()

    copies = []
    place = out_ref.at[span(REST + mine_first, size)]
    code_place = out_ref.at[span(COLS + mine_codes, code_size)]
    for mask in masks:
        device = device_of(mask)
        if not mask >> 3:
            copies.append(remote_to(place, place, device))
        copies.append(remote_to(code_place, code_place, device))
    for copy in copies:
        copy.start()
    store_slot.wait()
    held = out_slot_ref.at[slot]
    slots_out = [remote_to(held, held, device_of(mask)) for mask in masks]
    for copy in slots_out:
        copy.start()
    copies += slots_out
    for copy in copies + users_out:
        copy.wait()
    for j, k in enumerate(reversed(range(len(far)))):
        stage = far[k]
        copies = []
        if held_first[k + 1] < held_first[k]:
            place = out_ref.at[span(REST + first_at, held_first[k + 1])]
            copies.append(remote(place, place, stage))
            first_at = first_at - side_of(stage) * held_first[k + 1]
        if held_codes[k + 1] < held_codes[k]:
            place = out_ref.at[span(COLS + codes_at, held_codes[k + 1])]
            copies.append(remote(place, place, stage))
            codes_at = codes_at - side_of(stage) * held_codes[k + 1]
        slots = 16 * 2**j
        first_slot = lax.div(slot, slots) * slots
        held = out_slot_ref.at[pl.ds(first_slot, slots)]
        copies.append(remote(held, held, stage))
        held = out_user_ref.at[span(first_slot * n, slots * n)]
        copies.append(remote(held, held, stage))
        for copy in copies:
            copy.start()
        for copy in copies:
            copy.wait()


def gradients(codes, users, targets, domains, bias, gains, mixer, feed, embedding, dp):
    n = users.shape[0] // 2
    chunks = n // GROUP
    order = stages(dp)
    depth = len(order)
    devices = 2 * dp
    vmem = pl.BlockSpec(memory_space=pltpu.VMEM)
    smem = pl.BlockSpec(memory_space=pltpu.SMEM)
    hbm = pl.BlockSpec(memory_space=pl.ANY)
    stat = (16, LANES)
    held_rest, held_first, held_codes = shares(dp, REST), shares(dp, FIRST), shares(dp, CODES, 1)
    plane, far = depth - 1, depth - 4
    sizes = [*held_rest[1:] * 2, *held_first[1:]]
    sizes += [*held_first[1 : far + 1], *held_codes[1 : far + 1], held_rest[-1], held_first[-1]]
    lands = [pltpu.VMEM((rows, D), bf16) for rows in sizes]
    copies = 128 + 16 * depth
    return pl.pallas_call(
        functools.partial(step_kernel, n, dp),
        out_shape=(
            jax.ShapeDtypeStruct((COLS + CODES, D), bf16),
            jax.ShapeDtypeStruct((devices * n, D), bf16),
            jax.ShapeDtypeStruct((devices, 8, LANES), jnp.int32),
            jax.ShapeDtypeStruct((devices, 24, LANES), f32),
            jax.ShapeDtypeStruct((8, LANES), f32),
        ),
        in_specs=[vmem, smem, vmem, vmem, vmem, smem, vmem, hbm, hbm, hbm],
        out_specs=(vmem, hbm, hbm, hbm, vmem),
        scratch_shapes=[
            pltpu.VMEM((chunks, D, WIDE), f32),
            pltpu.VMEM((chunks, D, WIDE), f32),
            pltpu.VMEM((chunks * COLUMNS * D, LANES), f32),
            pltpu.VMEM((chunks, 3 * WIDTH, SPAN), bf16),
            pltpu.VMEM((n, PAIRS, KEYS, 2 * LANES), bf16),
            pltpu.VMEM((chunks, WIDTH, SPAN), bf16),
            pltpu.VMEM((chunks, FF, WIDE), bf16),
            pltpu.VMEM((chunks, 2 * WIDTH, WIDE), bf16),
            pltpu.VMEM((3 * WIDTH, 2 * LANES), bf16),
            pltpu.VMEM((2, D, COLS), bf16),
            pltpu.VMEM((2, COLS, D), bf16),
            pltpu.VMEM((2 * D, CODES + n), bf16),
            pltpu.VMEM((7, D, LANES), f32),
            pltpu.VMEM((PAIRS, KEYS, 2 * LANES), f32),
            pltpu.VMEM((PAIRS, LANES, 2 * LANES), f32),
            pltpu.VMEM((BLOCKS, D, LANES), f32),
            pltpu.VMEM((CODES + n, D), f32),
            pltpu.VMEM((PAIRS, KEYS, 2 * LANES), f32),
            pltpu.VMEM((7, D, LANES), f32),
            pltpu.VMEM((HEADS, 2 * BUCKETS, LANES), f32),
            pltpu.VMEM((n, D), f32),
            pltpu.VMEM((n, LANES), jnp.int32),
            pltpu.VMEM((WIDTH, LANES), bf16),
            pltpu.VMEM((WIDTH, LANES), bf16),
            pltpu.VMEM((chunks, 32 * GROUP, LANES), f32),
            pltpu.VMEM((chunks, WIDTH, 32 * GROUP), bf16),
            pltpu.VMEM((2, REST, D), bf16),
            pltpu.VMEM((2, FIRST, D), bf16),
            pltpu.VMEM((CODES, D), bf16),
            pltpu.VMEM((8, LANES), jnp.int32),
            pltpu.VMEM((n, D), bf16),
            pltpu.VMEM((24, LANES), f32),
            pltpu.VMEM((8, WIDE), jnp.int32),
            pltpu.VMEM((CODES + n, WIDE), bf16),
            pltpu.VMEM((depth + 1,) + stat, f32),
            pltpu.VMEM((depth,) + stat, f32),
            pltpu.VMEM((16, held_first[-1], D), bf16),
            pltpu.VMEM((16, held_codes[-1], D), bf16),
            pltpu.SemaphoreType.DMA((BLOCKS + 4,)),
            pltpu.SemaphoreType.DMA((copies,)),
            pltpu.SemaphoreType.DMA((copies,)),
        ]
        + lands,
        compiler_params=pltpu.CompilerParams(
            collective_id=0, has_side_effects=True, vmem_limit_bytes=63 * 2**20
        ),
        name="gradients",
    )(codes, users, users.reshape(1, -1), targets, domains, bias, gains, mixer, feed, embedding)


def adam(weight, moment, square, slope, rate, decay):
    moment = beta_one * moment + (1 - beta_one) * slope
    square = beta_two * square + (1 - beta_two) * slope * slope
    unbiased_moment = moment * (1 / (1 - beta_one**STEP))
    unbiased_square = square * (1 / (1 - beta_two**STEP))
    root = unbiased_square * lax.rsqrt(unbiased_square)
    step = unbiased_moment / (root + adam_eps) + decay * weight
    return weight - rate * step, moment, square


def update_kernel(*refs):
    parts_in, big_in, small_in, refs = refs[:5], refs[5:14], refs[14:20], refs[20:]
    loss_ref, norm_ref, section_ref, hist_ref = refs[:4]
    big_out, small_out, low_out, refs = refs[4:13], refs[13:19], refs[19:22], refs[22:]
    parts, hold, low_hold = refs[:5], refs[5:14], refs[14:17]
    user_grad, part_sems, in_sems, out_sems = refs[17:]
    grad_ref, user_ref, ids_ref, slot_ref, stat_ref = parts
    arrivals = [pltpu.make_async_copy(parts_in[i], parts[i], part_sems.at[i]) for i in range(5)]
    loads = [pltpu.make_async_copy(big_in[i], hold[i], in_sems.at[i]) for i in range(9)]
    for load in arrivals[1:] + arrivals[:1] + loads:
        load.start()
    for arrival in arrivals:
        arrival.wait()

    users = user_grad.shape[0]
    span = min(1024, user_ref.shape[0])
    slots = span // LANES * (ids_ref.shape[0] * LANES // user_ref.shape[0])
    fit = ids_ref.shape[0] * LANES // user_ref.shape[0]
    user_grad[...] = jnp.zeros_like(user_grad)

    def scatter(part, carry):
        rows = user_ref[pl.ds(pl.multiple_of(part * span, span), span), :]
        lanes = []
        for group in range(span // LANES):
            total = ids_ref[part * slots + group * fit, :1, :]
            for other in range(1, fit):
                total = total + ids_ref[part * slots + group * fit + other, :1, :]
            lanes.append(total)
        ids = jnp.concatenate(lanes, 1)
        for block in range(users // USER_ROWS):
            place = slice(block * USER_ROWS, (block + 1) * USER_ROWS)
            hit = iota((USER_ROWS, span), 0) + block * USER_ROWS == ids
            user_grad[place, :] += mul(jnp.where(hit, 1.0, 0.0).astype(bf16), rows)
        return carry

    lax.fori_loop(0, user_ref.shape[0] // span, scatter, 0)

    def total(x):
        return jnp.sum(jnp.sum(x, axis=0, keepdims=True), axis=1, keepdims=True)

    def slot_sum(first):
        def add(i, value):
            return value + slot_ref[2 * i + first]

        zero = jnp.zeros(slot_ref.shape[1:], f32)
        return lax.fori_loop(0, slot_ref.shape[0] // 2, add, zero)

    even, odd = slot_sum(0), slot_sum(1)
    section_squares = [total(x[16:17] + x[17:18]) for x in (even, odd)]
    small = even[:16] + odd[:16]
    rest = total(even[18:19] + odd[18:19])
    user_values = user_grad[...]
    rest = rest + total(user_values * user_values)
    lane, line = iota(small.shape, 1), iota(small.shape, 0)
    counted = (line < 7) | ((line > 7) & (lane < 2 * BUCKETS))
    small_kept = jnp.where(counted, small, 0.0)
    rest = rest + total(small_kept * small_kept)
    norm = jnp.sqrt(section_squares[0] + section_squares[1] + rest)
    factor = jnp.minimum(1.0, clip_norm / (norm + 1e-06))
    loss_ref[0] = small[7, 0]
    norm_ref[0] = norm[0, 0]
    for s in range(2):
        section_ref[s] = jnp.sqrt(section_squares[s])[0, 0]
    for row in range(8):
        lanes = slice((row % 2) * LANES, (row % 2 + 1) * LANES)
        hist_ref[row // 2 : row // 2 + 1, lanes] = stat_ref[row : row + 1, :]

    outs = adam(
        small_in[0][...], small_in[1][...], small_in[2][...], factor * small[:7], rate_gain, 0.0
    )
    for ref, value in zip(small_out[:3], outs):
        ref[...] = value
    for head in range(HEADS):
        for s in range(2):
            slope = factor * small[8 + head : 9 + head, s * BUCKETS : (s + 1) * BUCKETS]
            one = slice(s, s + 1)
            outs = adam(
                small_in[3][head, one, :],
                small_in[4][head, one, :],
                small_in[5][head, one, :],
                slope,
                rate_small,
                0.0,
            )
            for ref, value in zip(small_out[3:], outs):
                ref[head, one, :] = value

    stores = []

    def store(kind, place):
        first = 3 * kind
        pieces = [(hold[first + i], big_out[first + i]) for i in range(3)]
        pieces.append((low_hold[kind], low_out[kind]))
        for source, target in pieces:
            copy = pltpu.make_async_copy(
                source.at[place], target.at[place], out_sems.at[len(stores)]
            )
            copy.start()
            stores.append(copy)

    def step(kind, place, slope):
        first = 3 * kind
        outs = adam(
            hold[first][place],
            hold[first + 1][place],
            hold[first + 2][place],
            factor * slope,
            rate_matrix,
            decay_matrix,
        )
        for i in range(3):
            hold[first + i][place] = outs[i]
        low_hold[kind][place] = outs[0].astype(bf16)

    def block_of(block):
        first = FIRST // D
        place = block - first if block >= first else REST // D + block
        return grad_ref[place * D : (place + 1) * D, :].astype(f32)

    for i in range(3):
        loads[i].wait()
    for part in range(6):
        for block in range(3 * part, 3 * part + 3):
            lanes = slice(block * LANES, (block + 1) * LANES)
            step(0, (0, slice(None), lanes), block_of(block))
        store(0, (0, slice(None), slice(3 * part * LANES, 3 * (part + 1) * LANES)))
    for i in range(3, 6):
        loads[i].wait()
    for part in range(4):
        for block in range(4 * part, 4 * part + 4):
            lanes = slice(block * LANES, (block + 1) * LANES)
            step(1, (0, slice(None), lanes), block_of(MIXW // LANES + block))
        store(1, (0, slice(None), slice(4 * part * LANES, 4 * (part + 1) * LANES)))
    for i in range(6, 9):
        loads[i].wait()
    for part in range(4):
        rows = slice(part * CODEBOOK, (part + 1) * CODEBOOK)
        step(2, (rows, slice(None)), grad_ref[COLS + rows.start : COLS + rows.stop, :].astype(f32))
        store(2, (rows, slice(None)))
    for part in range(users // USER_ROWS):
        rows = slice(part * USER_ROWS, (part + 1) * USER_ROWS)
        place = (slice(CODES + part * USER_ROWS, CODES + (part + 1) * USER_ROWS), slice(None))
        step(2, place, user_grad[rows, :])
        store(2, place)
    for copy in stores:
        copy.wait()


def update(reduced, mixers, feeds, embeds, gains, biases):
    vmem = pl.BlockSpec(memory_space=pltpu.VMEM)
    smem = pl.BlockSpec(memory_space=pltpu.SMEM)
    hbm = pl.BlockSpec(memory_space=pl.ANY)
    big = [*mixers, *feeds, *embeds]
    small = [*gains, *biases]
    low = [jax.ShapeDtypeStruct(x[0].shape, bf16) for x in (mixers, feeds, embeds)]
    users = embeds[0].shape[0] - CODES
    pieces = 4 * (6 + 4 + 4 + users // USER_ROWS)
    return pl.pallas_call(
        update_kernel,
        out_shape=[
            jax.ShapeDtypeStruct((1,), f32),
            jax.ShapeDtypeStruct((1,), f32),
            jax.ShapeDtypeStruct((2,), f32),
            jax.ShapeDtypeStruct((LEVELS, CODEBOOK), f32),
        ]
        + [jax.ShapeDtypeStruct(x.shape, f32) for x in big + small]
        + low,
        in_specs=[hbm] * 14 + [vmem] * 6,
        out_specs=[smem] * 3 + [vmem] + [hbm] * 9 + [vmem] * 6 + [hbm] * 3,
        scratch_shapes=[pltpu.VMEM(x.shape, x.dtype) for x in reduced]
        + [pltpu.VMEM(x.shape, f32) for x in big]
        + [pltpu.VMEM(x.shape, bf16) for x in low]
        + [
            pltpu.VMEM((users, D), f32),
            pltpu.SemaphoreType.DMA((5,)),
            pltpu.SemaphoreType.DMA((9,)),
            pltpu.SemaphoreType.DMA((pieces,)),
        ],
        compiler_params=pltpu.CompilerParams(vmem_limit_bytes=62 * 2**20),
        name="update",
    )(*reduced, *big, *small)


def shards(
    history_codes,
    user_ids,
    targets,
    domains,
    mixer,
    mixer_moment,
    mixer_square,
    feed,
    feed_moment,
    feed_square,
    embedding,
    embedding_moment,
    embedding_square,
    gains,
    gains_moment,
    gains_square,
    position_bias,
    bias_moment,
    bias_square,
):
    def turned(table):
        return jnp.transpose(table, (2, 0, 1))

    biases = [turned(x) for x in (position_bias, bias_moment, bias_square)]
    reduced = gradients(
        history_codes,
        user_ids,
        targets.T,
        domains.reshape(1, -1),
        biases[0],
        gains,
        mixer,
        feed,
        embedding,
        lax.axis_size("dp"),
    )
    outs = update(
        reduced,
        (mixer, mixer_moment, mixer_square),
        (feed, feed_moment, feed_square),
        (embedding, embedding_moment, embedding_square),
        (gains, gains_moment, gains_square),
        biases,
    )
    loss, norm, sections, histograms = outs[:4]
    back = [jnp.transpose(x, (1, 2, 0)) for x in outs[16:19]]
    return (
        loss.reshape(()),
        norm.reshape(()),
        sections,
        histograms,
        *outs[4:16],
        *back,
        *outs[19:],
    )


def solution(mesh):
    by_dp, by_pipe, copied = P("dp"), P("pipe"), P()
    return jax.shard_map(
        shards,
        mesh=mesh,
        in_specs=(by_dp,) * 4 + (by_pipe,) * 6 + (copied,) * 9,
        out_specs=(copied,) * 4 + (by_pipe,) * 6 + (copied,) * 9 + (by_pipe,) * 2 + (copied,),
        check_vma=False,
    )
```

```python
import functools

import jax
import jax.numpy as jnp
from jax import lax
from jax.experimental import pallas as pl
from jax.experimental.pallas import tpu as pltpu
from jax.sharding import PartitionSpec as P

D = 128
HEADS = 6
HEAD_DIM = 64
FF = 1024
CODEBOOK = 256
LEVELS = 4
BUCKETS = 32
DOMAINS = 3
HIST_LEN = 81
STEP = 5
CODES = 1024
LANES = 128
WIDTH = HEADS * HEAD_DIM
MIXW = 6 * WIDTH
COLS = MIXW + 2 * FF
BLOCKS = COLS // LANES
KEYS = 96
GROUP = 8
BATCH = 2
PACK = 96
WIDE = GROUP * PACK
SPAN = GROUP * LANES
COLUMNS = WIDE // LANES
PAIRS = HEADS // 2
FIRST = 4 * WIDTH
REST = COLS - FIRST
USER_ROWS = 400
MESH = pl.DeviceIdType.MESH

norm_eps = 1e-06
beta_one = 0.9
beta_two = 0.999
adam_eps = 1e-08
clip_norm = 0.5
rate_matrix = 0.04
rate_gain = 0.8
rate_small = 0.3
decay_matrix = 0.01

f32 = jnp.float32
bf16 = jnp.bfloat16


def iota(shape, axis):
    return lax.broadcasted_iota(jnp.int32, shape, axis)


def mul(left, right):
    return jnp.dot(left, right, preferred_element_type=f32)


def mul_t(left, right):
    return lax.dot_general(left, right, (((1,), (1,)), ((), ())), preferred_element_type=f32)


def mul_exact(left, right):
    return jnp.dot(left, right, preferred_element_type=f32, precision=lax.Precision.HIGHEST)


def mul_exact_t(left, right):
    return lax.dot_general(
        left,
        right,
        (((1,), (1,)), ((), ())),
        preferred_element_type=f32,
        precision=lax.Precision.HIGHEST,
    )


def onehot(ids, rows):
    return jnp.where(iota((rows, ids.shape[1]), 0) == ids, 1.0, 0.0).astype(bf16)


def inverse_rms(x):
    return lax.rsqrt(jnp.mean(x * x, axis=0, keepdims=True) + norm_eps)


def norm_low(x, inverse, gain):
    return (x * inverse * gain).astype(bf16)


def norm_back(x, inverse, gain, upstream):
    scaled = x * inverse
    inner = upstream * gain
    back = inverse * (inner - scaled * jnp.mean(inner * scaled, axis=0, keepdims=True))
    return back, upstream * scaled


def block_diag(pair):
    zero = jnp.zeros((HEAD_DIM, LANES), pair.dtype)
    left = jnp.concatenate([pair[:HEAD_DIM], zero], 0)
    right = jnp.concatenate([zero, pair[HEAD_DIM:]], 0)
    return jnp.concatenate([left, right], 1)


def diagonal(both):
    return jnp.concatenate([both[:HEAD_DIM, :LANES], both[HEAD_DIM:, LANES:]], 0)


def turn(x, shift):
    return x if shift % LANES == 0 else pltpu.roll(x, shift % LANES, 1)


def pack(tables):
    lane = iota(tables[0].shape, 1)
    columns = []
    for first in range(0, len(tables), 4):
        turned = [turn(tables[first + i], PACK * i) for i in range(4)]
        for i in range(3):
            columns.append(jnp.where(lane < PACK - 32 * i, turned[i], turned[i + 1]))
    return jnp.concatenate(columns, 1)


def unpack(x):
    lane = iota((x.shape[0], LANES), 1)
    tables = []
    for first in range(0, x.shape[1] // LANES, 3):
        a, b, c = [x[:, (first + i) * LANES : (first + i + 1) * LANES] for i in range(3)]
        tables.append(a)
        tables.append(jnp.where(lane < 32, turn(a, 32), turn(b, 32)))
        tables.append(jnp.where(lane < 64, turn(b, 64), turn(c, 64)))
        tables.append(turn(c, 96))
    return tables


def stack(both):
    return jnp.concatenate([both[:, :LANES], both[:, LANES:]], 0)


def pad_keys(table):
    if table.shape[0] == LANES:
        return table
    zero = jnp.zeros((LANES - table.shape[0], table.shape[1]), table.dtype)
    return jnp.concatenate([table, zero], 0)


def columns_of(table, i):
    return table[:, 2 * i * LANES : 2 * (i + 1) * LANES]


def attend(keys, queries, values, bias):
    scores = [mul(key, block_diag(query)) for key, query in zip(keys, queries)]
    scores = jnp.concatenate(scores, 1) + bias
    top = jnp.max(scores, axis=0, keepdims=True)
    chance = jnp.exp(scores - top)
    total = jnp.sum(chance, axis=0, keepdims=True)
    chance = (chance * (1.0 / total)).astype(bf16)
    full = pad_keys(chance)
    mixed = [mul(value, columns_of(full, i)) for i, value in enumerate(values)]
    return chance, [diagonal(both).astype(bf16) for both in mixed]


def attend_back(keys_t, queries, values, back_mixed, chance):
    exact = chance.astype(f32)
    back_chance = [mul(value, block_diag(back)) for value, back in zip(values, back_mixed)]
    back_chance = jnp.concatenate(back_chance, 1)
    inner = jnp.sum(back_chance * exact, axis=0, keepdims=True)
    back_scores = exact * (back_chance - inner)
    low = pad_keys(back_scores.astype(bf16))
    full = pad_keys(chance)
    count = range(len(queries))
    back_query = [mul(keys_t[i], columns_of(low, i)) for i in count]
    back_keys = [mul_t(queries[i], stack(columns_of(low, i))) for i in count]
    back_values = [mul_t(back_mixed[i], stack(columns_of(full, i))) for i in count]
    results = [
        [diagonal(both).astype(bf16) for both in part]
        for part in (back_query, back_keys, back_values)
    ]
    return *results, back_scores


def split_low(x):
    high = x.astype(bf16)
    return jnp.concatenate([high, (x - high.astype(f32)).astype(bf16)], 0)


def stages(dp):
    bits = [2**k for k in range(dp.bit_length() - 1)]
    near = bits[1:4]
    return [("dp", bit) for bit in bits[:1] + bits[4:] + near] + [("pipe", 1)]


def side_of(stage):
    axis, bit = stage
    return lax.rem(lax.div(lax.axis_index(axis), bit), 2)


def partner_of(stage):
    axis, bit = stage
    return {axis: lax.axis_index(axis) + bit * (1 - 2 * side_of(stage))}


def shares(dp, rows, across=0):
    held = [rows]
    depth = len(stages(dp)) - 1
    for k in range(depth + across):
        later = min(3, depth - 1 - k) + across if k < depth else 0
        half = held[-1] // 2
        held.append(half if half % (16 * 2**later) == 0 else held[-1])
    return held


def span(start, size):
    return pl.ds(pl.multiple_of(start, 16), size)


def step_kernel(n, dp, *refs):
    codes_ref, users_ref, user_row_ref, targets_ref, domains_ref, bias_ref, gains_ref = refs[:7]
    mixer_ref, feed_ref, embed_ref = refs[7:10]
    out_ref, out_user_ref, out_ids_ref, out_slot_ref, out_stat_ref = refs[10:15]
    x0_s, x1_s, x2_s, qkv_s, p_s, o_s, r_s, mem_s, dz_s, wn_s, wt_s, ext_s = refs[15:27]
    gain_s, ebias_s, dbias_s, g0_s, ge_s, gbias_s, ggain_s, rows_s, user_s, ids_s = refs[27:37]
    cross_s, cross_back_s, pc_s, oc_s, rest_s, first_s, codes_s, slot_s, user_low_s, own_slot_s, id_rows_s, hot_s, dqkv_s = refs[37:50]
    stat_s, stat_land, near_first, near_codes, local_sems, sends, recvs = refs[50:57]
    lands = refs[57:]
    order = stages(dp)
    across = order[-1]
    depth = len(order)
    chunks = n // GROUP
    section = lax.axis_index("pipe")
    used = [0]

    def remote_to(source, target, device):
        index = used[0]
        used[0] += 1
        return pltpu.make_async_remote_copy(
            src_ref=source,
            dst_ref=target,
            send_sem=sends.at[index],
            recv_sem=recvs.at[index],
            device_id=device,
            device_id_type=MESH,
        )

    def remote(source, target, stage):
        return remote_to(source, target, partner_of(stage))

    near, far = order[-4:], order[:-4]
    masks = range(1, 2 ** len(near))

    def device_of(mask):
        place = {"dp": lax.axis_index("dp"), "pipe": lax.axis_index("pipe")}
        for i, (axis, bit) in enumerate(near):
            if mask >> i & 1:
                place[axis] = place[axis] + bit * (1 - 2 * side_of((axis, bit)))
        return place

    def shift_of(mask, lefts):
        total = 0
        for i, left in enumerate(lefts):
            side = side_of(near[i])
            total = total + (1 - side if mask >> i & 1 else side) * left
        return total

    locals_in = []
    for block in range(BLOCKS):
        lanes = slice(block * LANES, (block + 1) * LANES)
        if block < MIXW // LANES:
            source = mixer_ref.at[0, :, lanes]
        else:
            source = feed_ref.at[0, :, slice(lanes.start - MIXW, lanes.stop - MIXW)]
        locals_in.append(pltpu.make_async_copy(source, g0_s.at[block], local_sems.at[block]))
    vocabulary = embed_ref.shape[0]
    flat = x2_s.at[pl.ds(0, vocabulary)]
    load_embed = pltpu.make_async_copy(embed_ref, flat, local_sems.at[BLOCKS])
    for copy in locals_in:
        copy.start()
    load_embed.start()

    barrier = pltpu.get_barrier_semaphore()
    for stage in far:
        pl.semaphore_signal(barrier, inc=1, device_id=partner_of(stage), device_id_type=MESH)
    for mask in masks:
        pl.semaphore_signal(barrier, inc=1, device_id=device_of(mask), device_id_type=MESH)
    pl.semaphore_wait(barrier, len(far) + len(masks))

    scale = HEAD_DIM**-0.5
    cross_scale = jnp.where(section == 1, scale, 1.0).astype(f32)
    for copy in locals_in:
        copy.wait()
    for block in range(BLOCKS):
        value = g0_s[block]
        if block < 3:
            value = value * scale
        elif 12 <= block < 15:
            value = value * cross_scale
        wn_s[section, :, block * LANES : (block + 1) * LANES] = value.astype(bf16)
    half = D // 2
    mine = span(side_of(order[0]) * half, half)
    pieces = (slice(0, FIRST), slice(FIRST, COLS))
    over = [
        remote(wn_s.at[section, mine, piece], wn_s.at[section, mine, piece], across)
        for piece in pieces
    ]
    for copy in over:
        copy.start()

    ids_s[:, : HIST_LEN - 1] = codes_ref[pl.ds(pl.multiple_of(section * n, 8), n), :]
    lane, row = iota((n, LANES), 1), iota((n, LANES), 0)
    ids = ids_s[...] + ((lane & 3) << 8)
    ids = jnp.where(lane < HIST_LEN - 1, ids, jnp.where(lane == HIST_LEN - 1, CODES + row, -1))
    ids_s[...] = ids
    packed = []
    for i in range(GROUP):
        rows = [ids_s[c * GROUP + i : c * GROUP + i + 1, :] for c in range(chunks)]
        rows += [jnp.zeros((8 - chunks, LANES), jnp.int32)]
        packed.append(jnp.concatenate(rows, 0))
    id_rows_s[...] = pack(packed)
    count = targets_ref.shape[1]
    history, token = iota((count, LANES), 0), iota((count, LANES), 1)
    pick = jnp.where((token >> 2) + section * n == history, 1.0, 0.0)
    level, place = iota((LEVELS, LANES), 0), iota((LEVELS, LANES), 1) & 3
    target = mul(targets_ref[...].astype(f32), pick) + (level * CODEBOOK).astype(f32)
    goal = jnp.sum(jnp.where(level == place, target, 0.0), axis=0, keepdims=True).astype(jnp.int32)
    start_ids = jnp.sum(
        jnp.where(level == place - 1, target, 0.0), axis=0, keepdims=True
    ).astype(jnp.int32)
    domain = mul(domains_ref[...].astype(f32), pick)
    pick = jnp.where(lax.rem(token, n) + section * n == history, 1.0, 0.0)
    own_users = mul_exact(user_row_ref[...].astype(f32), pick)

    counts = [
        jnp.sum(jnp.where(domain == d, 1.0, 0.0), axis=1, keepdims=True) for d in range(DOMAINS)
    ]
    counts += [jnp.zeros((1, 1), f32)] * (8 - DOMAINS)
    stat_s[0, 8:, :] = jnp.broadcast_to(jnp.concatenate(counts, 0), (8, LANES))
    histogram = mul_t(jnp.ones((8, LANES), bf16), onehot(goal, CODES))
    for r in range(8):
        stat_s[0, r : r + 1, :] = histogram[:1, r * LANES : (r + 1) * LANES]
    slot = 0
    for k, stage in enumerate(order):
        slot = slot + side_of(stage) * 2 ** (depth - 1 - k)
    owner = iota((8, LANES), 1) // n
    own_users = jnp.broadcast_to(own_users, (8, LANES)).astype(jnp.int32)
    slot_s[...] = jnp.where(owner == lax.rem(slot, LANES // n), own_users, 0)
    store_ids = pltpu.make_async_copy(slot_s, out_ids_ref.at[slot], local_sems.at[BLOCKS + 1])
    store_ids.start()
    store_ids.wait()

    def slots_of(j):
        return pl.ds(lax.div(slot, 2**j) * 2**j, 2**j)

    early = []
    for j, stage in enumerate(reversed(order)):
        held = out_ids_ref.at[slots_of(j)]
        early.append(
            (
                remote(stat_s.at[j], stat_land.at[j], stage),
                remote(held, held, stage),
            )
        )

    def early_step(j):
        if j > 0:
            for copy in early[j - 1]:
                copy.wait()
            stat_s[j] = stat_s[j - 1] + stat_land[j - 1]
        if j < depth:
            for copy in early[j]:
                copy.start()

    eye = jnp.where(iota((LANES, LANES), 0) == iota((LANES, LANES), 1), 1.0, 0.0).astype(bf16)
    load_embed.wait()

    def fetch(i, carry):
        user_s[pl.ds(i, 1), :] = x2_s[pl.ds(CODES + users_ref[section * n + i], 1), :]
        return carry

    lax.fori_loop(0, n, fetch, 0)
    for block in range(CODES // LANES + 1):
        if block < CODES // LANES:
            rows = x2_s[block * LANES : (block + 1) * LANES, :]
            codes_s[block * LANES : (block + 1) * LANES, :] = rows.astype(bf16)
            width = LANES
        else:
            rows = user_s[...]
            width = n
        high = rows.astype(bf16)
        low = (rows - high.astype(f32)).astype(bf16)
        lanes = slice(block * LANES, block * LANES + width)
        ext_s[:D, lanes] = mul_t(eye, high).astype(bf16)
        ext_s[D:, lanes] = mul_t(eye, low).astype(bf16)

    def find(c):
        ids = id_rows_s[pl.ds(c, 1), :]
        for first in range(0, CODES + n, LANES):
            rows = min(LANES, CODES + n - first)
            hot_s[first : first + rows, :] = onehot(ids - first, rows)

    def lookup(c, carry):
        find(c)
        both = mul(ext_s[...], hot_s[...])
        x0_s[c] = both[:D] + both[D:]
        return carry

    lax.fori_loop(0, chunks, lookup, 0)

    for g in range(7):
        gain_s[g] = jnp.broadcast_to(gains_ref[g : g + 1, :], (LANES, LANES)).T

    def positions(axis):
        index = iota((KEYS, LANES), axis)
        return jnp.where(index == HIST_LEN - 1, 0, index + 1)

    key, query = positions(0), positions(1)
    distance = jnp.abs(query - key)
    remoteness = jnp.zeros_like(distance)
    for edge in (12, 16, 23, 32, 46, 64, 91):
        remoteness = remoteness + (distance >= edge).astype(jnp.int32)
    nearby = jnp.minimum(jnp.where(distance < 8, distance, 8 + remoteness), 15)
    buckets = nearby + jnp.where(key > query, 16, 0)
    real = iota((KEYS, LANES), 0) < HIST_LEN
    for head in range(HEADS):
        lanes = slice(head * LANES, (head + 1) * LANES)

        def choose(b, table):
            return jnp.where(buckets == b, bias_ref[head, 0, b], table)

        table = lax.fori_loop(0, BUCKETS, choose, jnp.zeros((KEYS, LANES), f32))
        ebias_s[:, lanes] = jnp.where(real, table, -1e30)
    key, query = iota((LANES, LANES), 0), iota((LANES, LANES), 1)
    offset = query - key
    seen = ((key >> 2) == (query >> 2)) & (offset >= 0)
    for head in range(HEADS):
        lanes = slice(head * LANES, (head + 1) * LANES)
        table = jnp.full((LANES, LANES), -1e30, f32)
        for b in range(LEVELS):
            table = jnp.where(seen & (offset == b), bias_ref[head, 1, b], table)
        dbias_s[:, lanes] = table

    def transpose_weights(which, first, last):
        for block in range(first, last):
            place = slice(block * LANES, (block + 1) * LANES)
            wt_s[which, place, :] = wn_s[which, :, place].T

    beside = []
    for piece in pieces:
        came = wn_s.at[1 - section, mine, piece]
        beside.append(remote(came, came, order[0]))
    over[0].wait()
    beside[0].start()
    transpose_weights(section, 0, BLOCKS)
    beside[0].wait()
    transpose_weights(1 - section, 0, FIRST // LANES)

    def rest_arrives():
        over[1].wait()
        beside[1].start()
        beside[1].wait()
        transpose_weights(1 - section, FIRST // LANES, BLOCKS)

    def gain(g, width):
        column = gain_s[g]
        return column if width == LANES else jnp.concatenate([column] * (width // LANES), 1)

    def at_chunk(c, step, point, points, count):
        for j in range(point, count, points):
            pl.when(c == j // points)(functools.partial(step, j))

    def spread_low(x):
        return jnp.concatenate([part.astype(bf16) for part in unpack(x)], 1)

    def packed(x):
        return pack([x[:, i * LANES : (i + 1) * LANES] for i in range(GROUP)])

    def part_of(j):
        return slice(j * LANES, (j + 1) * LANES)

    def encode(c, carry):
        at_chunk(c, early_step, 0, 2, depth + 1)
        x0 = x0_s[c]
        h = spread_low(x0 * inverse_rms(x0) * gain(0, WIDE))
        for j in range(3):
            part = slice(j * WIDTH, (j + 1) * WIDTH)
            qkv_s[c, part, :] = mul(wt_s[0, part, :], h).astype(bf16)
        for first in range(0, GROUP, BATCH):
            queries, keys, values = [], [], []
            for i in range(first, first + BATCH):
                lanes = slice(i * LANES, (i + 1) * LANES)
                queries += [qkv_s[c, part_of(j), lanes] for j in range(PAIRS)]
                keys += [qkv_s[c, part_of(PAIRS + j), lanes].T[:KEYS] for j in range(PAIRS)]
                values += [qkv_s[c, part_of(2 * PAIRS + j), lanes] for j in range(PAIRS)]
            bias = jnp.concatenate([ebias_s[...]] * BATCH, 1)
            chance, mixed = attend(keys, queries, values, bias)
            for i in range(BATCH):
                lanes = slice((first + i) * LANES, (first + i + 1) * LANES)
                p_s[GROUP * c + first + i] = chance[:, i * HEADS * LANES : (i + 1) * HEADS * LANES]
                o_s[c, :, lanes] = jnp.concatenate(mixed[i * PAIRS : (i + 1) * PAIRS], 0)
        x1 = x0 + packed(mul(wn_s[0, :, 3 * WIDTH : 4 * WIDTH], o_s[c]))
        x1_s[c] = x1
        at_chunk(c, early_step, 1, 2, depth + 1)
        pl.when(c == 0)(rest_arrives)
        h = norm_low(x1, inverse_rms(x1), gain(1, WIDE))
        for j in range(2):
            part = slice(j * FF // 2, (j + 1) * FF // 2)
            lifted = mul(wt_s[0, MIXW + j * FF // 2 : MIXW + (j + 1) * FF // 2, :], h)
            r_s[c, part, :] = jnp.maximum(lifted, 0.0).astype(bf16)
        x2 = x1 + mul(wn_s[0, :, MIXW + FF :], r_s[c])
        put_wide(x2_s, c, x2)
        e = norm_low(x2, inverse_rms(x2), gain(2, WIDE))
        for j in range(2):
            part = slice(j * WIDTH, (j + 1) * WIDTH)
            mem_s[c, part, :] = mul(
                wt_s[0, 4 * WIDTH + j * WIDTH : 4 * WIDTH + (j + 1) * WIDTH, :], e
            ).astype(bf16)
        return carry

    def put_wide(ref, c, value):
        for i in range(COLUMNS):
            ref[pl.ds(pl.multiple_of((COLUMNS * c + i) * D, D), D), :] = value[
                :, i * LANES : (i + 1) * LANES
            ]

    def get_wide(ref, c):
        return jnp.concatenate(
            [ref[pl.ds(pl.multiple_of((COLUMNS * c + i) * D, D), D), :] for i in range(COLUMNS)], 1
        )

    lax.fori_loop(0, chunks, encode, 0)
    for j in range(2 * chunks, depth + 1):
        early_step(j)
    out_stat_ref[...] = stat_s[depth, :8, :]

    def put_blocks(first, value):
        for index in range(value.shape[1] // LANES):
            block = first + index
            part = value[:, index * LANES : (index + 1) * LANES].astype(bf16)
            if block < FIRST // LANES:
                first_s[1, block * D : (block + 1) * D, :] = part
            else:
                block -= FIRST // LANES
                rest_s[1, block * D : (block + 1) * D, :] = part

    def add_blocks(first, value):
        for index in range(value.shape[1] // LANES):
            g0_s[first + index] += value[:, index * LANES : (index + 1) * LANES]

    start = onehot(start_ids, CODES)
    both = mul(ext_s[:, :CODES], start)
    y0 = both[:D] + both[D:]
    inverse0 = inverse_rms(y0)
    h0 = norm_low(y0, inverse0, gain(3, LANES))
    dz_s[:, :LANES] = mul(wt_s[1, : 3 * WIDTH, :], h0).astype(bf16)
    both = mul(mul_t(eye, h0).astype(bf16), wn_s[1, :, WIDTH : 3 * WIDTH]).astype(bf16)
    self_chance, mixed = attend(
        [both[:, part_of(j)] for j in range(PAIRS)],
        [dz_s[part_of(j), :LANES] for j in range(PAIRS)],
        [dz_s[part_of(2 * PAIRS + j), :LANES] for j in range(PAIRS)],
        dbias_s[...],
    )
    self_values = both[:, WIDTH:]
    self_mixed = jnp.concatenate(mixed, 0)
    y1 = y0 + mul(wn_s[1, :, 3 * WIDTH : 4 * WIDTH], self_mixed)
    inverse1 = inverse_rms(y1)
    h1 = norm_low(y1, inverse1, gain(4, LANES))
    cross_s[...] = mul(wt_s[1, 4 * WIDTH : 5 * WIDTH, :], h1).astype(bf16)

    def spreader(g, turned):
        shape = (LANES, 32 * GROUP) if turned else (32 * GROUP, LANES)
        row, token = iota(shape, 1 if turned else 0), iota(shape, 0 if turned else 1)
        hit = token == 4 * GROUP * g + 4 * (row >> 5) + (row & 3)
        return jnp.where(hit, 1.0, 0.0).astype(bf16)

    def rows_of(g, table):
        rows = mul_t(spreader(g, False), table)
        mask = (iota(rows.shape, 1) >> 6) == ((iota(rows.shape, 0) & 31) >> 2)
        return jnp.where(mask, rows, 0.0).astype(bf16)

    def head_mask(shape):
        return (iota(shape, 0) >> 6) == ((iota(shape, 1) & 31) >> 2)

    def rows_t_of(g, table):
        rows = mul(table, spreader(g, True))
        return jnp.where(head_mask(rows.shape), rows, 0.0).astype(bf16)

    def gather_rows(ref):
        total = jnp.zeros((WIDTH, LANES), f32)
        for g in range(chunks):
            total = total + mul(ref[g], spreader(g, False))
        return total.astype(bf16)

    def blocks_of(table):
        rows = []
        for i in range(GROUP):
            part = table[32 * i : 32 * i + 32]
            column, shift = divmod(PACK * i, LANES)
            part = turn(part, shift)
            lane = iota(part.shape, 1)
            zero = jnp.zeros_like(part)
            columns = [zero] * COLUMNS
            columns[column] = jnp.where(lane >= shift, part, 0.0)
            if shift > LANES - PACK:
                columns[column + 1] = jnp.where(lane < shift, part, 0.0)
            rows.append(jnp.concatenate(columns, 1))
        return jnp.concatenate(rows, 0).astype(bf16)

    def row_products(rows, ref, g, first):
        both = mul(rows, ref[g, first : first + WIDTH, :])
        parts = []
        for i in range(GROUP):
            own = both[32 * i : 32 * i + 32]
            column, shift = divmod(PACK * i, LANES)
            part = turn(own[:, column * LANES : (column + 1) * LANES], -shift)
            if shift > LANES - PACK:
                after = turn(own[:, (column + 1) * LANES : (column + 2) * LANES], -shift)
                part = jnp.where(iota(part.shape, 1) < LANES - shift, part, after)
            parts.append(part)
        return jnp.concatenate(parts, 0)

    def cross(g, carry):
        queries = rows_of(g, cross_s[...])
        scores = row_products(queries, mem_s, g, 0)
        scores = jnp.where(iota(scores.shape, 1) < HIST_LEN, scores, -1e30)
        chance = jnp.exp(scores - jnp.max(scores, axis=1, keepdims=True))
        chance = chance * (1.0 / jnp.sum(chance, axis=1, keepdims=True))
        pc_s[g] = chance
        mixed = mul_t(mem_s[g, WIDTH:, :], blocks_of(chance))
        oc_s[g] = jnp.where(head_mask(mixed.shape), mixed, 0.0).astype(bf16)
        return carry

    lax.fori_loop(0, chunks, cross, 0)
    cross_mixed = gather_rows(oc_s)
    y2 = y1 + mul(wn_s[1, :, 5 * WIDTH : 6 * WIDTH], cross_mixed)
    inverse2 = inverse_rms(y2)
    h2 = norm_low(y2, inverse2, gain(5, LANES))
    lifted = mul(wt_s[1, MIXW : MIXW + FF, :], h2)
    active = jnp.maximum(lifted, 0.0).astype(bf16)
    y3 = y2 + mul(wn_s[1, :, MIXW + FF :], active)
    inverse3 = inverse_rms(y3)
    final = norm_low(y3, inverse3, gain(6, LANES))
    logits = mul(codes_s[...], final)
    top = jnp.max(logits, axis=0, keepdims=True)
    log_total = top + jnp.log(jnp.sum(jnp.exp(logits - top), axis=0, keepdims=True))
    match = iota(logits.shape, 0) == goal
    picked = jnp.sum(jnp.where(match, logits, 0.0), axis=0, keepdims=True)
    weight = jnp.zeros((1, LANES), f32)
    for d in range(DOMAINS):
        share = 1.0 / (DOMAINS * jnp.maximum(stat_s[depth, 8 + d : 9 + d, :], 1.0))
        weight = weight + jnp.where(domain == d, share, 0.0)
    loss = jnp.sum(weight * (log_total - picked), axis=1, keepdims=True)
    back_logits = (
        weight * (jnp.exp(logits - log_total) - jnp.where(match, 1.0, 0.0))
    ).astype(bf16)
    back_final = mul(ext_s[:D, :CODES], back_logits)
    table_grad = mul_t(back_logits, final)
    back, gain_grad = norm_back(y3, inverse3, gain(6, LANES), back_final)
    ggain_s[6] = gain_grad
    low = back.astype(bf16)
    put_blocks(26, mul_t(low, active))
    back_lifted = jnp.where(lifted > 0, mul(wt_s[1, MIXW + FF :, :], low), 0.0).astype(bf16)
    put_blocks(18, mul_t(h2, back_lifted))
    more, gain_grad = norm_back(
        y2, inverse2, gain(5, LANES), mul(wn_s[1, :, MIXW : MIXW + FF], back_lifted)
    )
    ggain_s[5] = gain_grad
    back = back + more
    low = back.astype(bf16)
    put_blocks(15, mul_t(low, cross_mixed))
    cross_back_s[...] = mul(wt_s[1, 5 * WIDTH : 6 * WIDTH, :], low).astype(bf16)

    def cross_back(g, carry):
        mixed_rows = rows_of(g, cross_back_s[...])
        back_chance = row_products(mixed_rows, mem_s, g, WIDTH)
        back_chance = jnp.where(iota(back_chance.shape, 1) < HIST_LEN, back_chance, 0.0)
        chance = pc_s[g]
        inner = jnp.sum(back_chance * chance, axis=1, keepdims=True)
        spread = blocks_of(chance * (back_chance - inner))
        total = mul_t(mem_s[g, :WIDTH, :], spread)
        mem_s[g, :WIDTH, :] = mul(rows_t_of(g, cross_s[...]), spread).astype(bf16)
        mem_s[g, WIDTH:, :] = mul(rows_t_of(g, cross_back_s[...]), blocks_of(chance)).astype(bf16)
        oc_s[g] = jnp.where(head_mask(total.shape), total, 0.0).astype(bf16)
        return carry

    lax.fori_loop(0, chunks, cross_back, 0)
    back_query = gather_rows(oc_s)
    put_blocks(12, mul_t(h1, back_query) * HEAD_DIM**-0.5)
    more, gain_grad = norm_back(
        y1, inverse1, gain(4, LANES), mul(wn_s[1, :, 4 * WIDTH : 5 * WIDTH], back_query)
    )
    ggain_s[4] = gain_grad
    back = back + more
    low = back.astype(bf16)
    put_blocks(9, mul_t(low, self_mixed))
    back_mixed = mul(wt_s[1, 3 * WIDTH : 4 * WIDTH, :], low).astype(bf16)
    *back_parts, self_scores = attend_back(
        [dz_s[part_of(PAIRS + j), :LANES] for j in range(PAIRS)],
        [dz_s[part_of(j), :LANES] for j in range(PAIRS)],
        [self_values[:, part_of(j)] for j in range(PAIRS)],
        [back_mixed[part_of(j)] for j in range(PAIRS)],
        self_chance,
    )
    dz_s[:, LANES:] = jnp.concatenate([x for part in back_parts for x in part], 0)
    put_blocks(0, mul_t(h0, dz_s[:WIDTH, LANES : 2 * LANES]) * HEAD_DIM**-0.5)
    put_blocks(3, mul_t(h0, dz_s[WIDTH:, LANES : 2 * LANES]))
    more, gain_grad = norm_back(
        y0, inverse0, gain(3, LANES), mul(wn_s[1, :, : 3 * WIDTH], dz_s[:, LANES : 2 * LANES])
    )
    ggain_s[3] = gain_grad
    back = back + more
    spread = mul_t(start, split_low(back))
    ge_s[:CODES, :] = table_grad + spread[:, :D] + spread[:, D:]
    ge_s[CODES:, :] = jnp.zeros((n, D), f32)
    rows_s[...] = jnp.zeros_like(rows_s)
    for head in range(HEADS):
        lanes = slice(head * LANES, (head + 1) * LANES)
        for b in range(LEVELS):
            hit = jnp.where(offset == b, self_scores[:, lanes], 0.0)
            rows_s[head, BUCKETS + b : BUCKETS + b + 1, :] = jnp.sum(hit, axis=0, keepdims=True)

    def reducing(buffer, kept, held, upto):
        steps, at = [], 0
        for k, stage in enumerate(order[:upto]):
            rows, left = held[k], held[k + 1]
            side = side_of(stage)
            if left < rows:
                source = buffer.at[span(at + (1 - side) * left, left)]
                at = at + side * left
            else:
                source = buffer.at[span(at, rows)]
            steps.append((remote(source, kept[k], stage), at, left))
        return steps, at, held

    def begin(steps, k):
        steps[k][0].start()

    def finish(steps, buffer, kept, k):
        copy, at, left = steps[k]
        copy.wait()
        place = span(at, left)
        total = buffer[place, :].astype(f32) + kept[k][...].astype(f32)
        buffer[place, :] = total.astype(bf16)

    flat_depth = depth - 1
    held_rest, held_first, held_codes = shares(dp, REST), shares(dp, FIRST), shares(dp, CODES, 1)
    land, rest = {}, lands
    for name, number in (
        ("rest0", flat_depth),
        ("rest1", flat_depth),
        ("first1", flat_depth),
        ("first0", len(far)),
        ("codes", len(far)),
    ):
        land[name], rest = rest[:number], rest[number:]
    land_rest, land_first = rest
    rest1 = reducing(rest_s.at[1], land["rest1"], held_rest, flat_depth)
    first1 = reducing(first_s.at[1], land["first1"], held_first, flat_depth)
    rest0 = reducing(rest_s.at[0], land["rest0"], held_rest, flat_depth)
    first0 = reducing(first_s.at[0], land["first0"], held_first, len(far))
    codes = reducing(codes_s, land["codes"], held_codes, len(far))

    def step1(k):
        if k > 0:
            finish(rest1[0], rest_s.at[1], land["rest1"], k - 1)
            finish(first1[0], first_s.at[1], land["first1"], k - 1)
        if k < flat_depth:
            begin(rest1[0], k)
            begin(first1[0], k)

    def crossing(buffer, target, at, rows):
        source = buffer.at[1 - section, span(at, rows)]
        return remote(source, target, across)

    cross_rest = crossing(rest_s, land_rest, rest1[1], rest1[2][-1])
    cross_first = crossing(first_s, land_first, first1[1], first1[2][-1])

    def settle(copy, buffer, landed, at, rows, base):
        copy.wait()
        value = (buffer[section, span(at, rows), :].astype(f32) + landed[...].astype(f32)).astype(
            bf16
        )
        out_ref[span(base + at, rows), :] = value
        value = value.astype(f32)
        return jnp.sum(value * value, axis=0, keepdims=True)

    def gathering(base, at, held):
        steps = []
        for k in reversed(range(flat_depth)):
            rows, left = held[k], held[k + 1]
            if left < rows:
                place = out_ref.at[span(base + at, left)]
                steps.append(remote(place, place, order[k]))
                at = at - side_of(order[k]) * left
            else:
                steps.append(None)
        return steps

    gather_rest = gathering(0, rest1[1], rest1[2])

    def step0(k):
        if k > 0 and k <= flat_depth:
            finish(rest0[0], rest_s.at[0], land["rest0"], k - 1)
        if k < flat_depth:
            begin(rest0[0], k)
        if k == flat_depth:
            cross_rest.start()
        if k == flat_depth + 1:
            squares = settle(cross_rest, rest_s, land_rest, rest1[1], rest1[2][-1], 0)
            own_slot_s[16:17, :] = squares / (dp * rest1[2][-1] // REST)
        if k > flat_depth + 1 and gather_rest[k - flat_depth - 2] is not None:
            gather_rest[k - flat_depth - 2].wait()
        if flat_depth < k < 2 * flat_depth + 1 and gather_rest[k - flat_depth - 1] is not None:
            gather_rest[k - flat_depth - 1].start()

    g0_s[...] = jnp.zeros_like(g0_s)
    gbias_s[...] = jnp.zeros_like(gbias_s)
    for g in range(3):
        ggain_s[g] = jnp.zeros((D, LANES), f32)

    def fold(x):
        return sum(x[:, i * LANES : (i + 1) * LANES] for i in range(COLUMNS))

    def back_rest(c, carry):
        at_chunk(c, step1, 0, 2, flat_depth + 1)
        x2 = get_wide(x2_s, c)
        inverse = inverse_rms(x2)
        back_memory = mem_s[c]
        add_blocks(12, mul_t(norm_low(x2, inverse, gain(2, WIDE)), back_memory))
        back, gain_grad = norm_back(
            x2, inverse, gain(2, WIDE), mul(wn_s[0, :, 4 * WIDTH : 6 * WIDTH], back_memory)
        )
        ggain_s[2] += fold(gain_grad)
        low = back.astype(bf16)
        add_blocks(26, mul_t(low, r_s[c]))
        for j in range(4):
            part = slice(j * FF // 4, (j + 1) * FF // 4)
            back_active = mul(wt_s[0, MIXW + FF + part.start : MIXW + FF + part.stop, :], low)
            live = r_s[c, part, :].astype(f32) > 0
            r_s[c, part, :] = jnp.where(live, back_active, 0.0).astype(bf16)
        at_chunk(c, step1, 1, 2, flat_depth + 1)
        x1 = x1_s[c]
        inverse = inverse_rms(x1)
        add_blocks(18, mul_t(norm_low(x1, inverse, gain(1, WIDE)), r_s[c]))
        more, gain_grad = norm_back(
            x1, inverse, gain(1, WIDE), mul(wn_s[0, :, MIXW : MIXW + FF], r_s[c])
        )
        ggain_s[1] += fold(gain_grad)
        put_wide(x2_s, c, back + more)
        return carry

    lax.fori_loop(0, chunks, back_rest, 0)
    for j in range(2 * chunks, flat_depth + 1):
        step1(j)
    for block in range(REST // D):
        rest_s[0, block * D : (block + 1) * D, :] = g0_s[FIRST // D + block].astype(bf16)

    steps0 = 2 * flat_depth + 2

    def back_first(c, carry):
        at_chunk(c, step0, 0, 3, steps0)
        back = get_wide(x2_s, c)
        lane = iota((D, LANES), 1)
        low = [jnp.where(lane < PACK, part, 0.0).astype(bf16) for part in unpack(back)]
        low = jnp.concatenate(low, 1)
        add_blocks(9, mul_t(low, o_s[c]))
        o_s[c] = mul(wt_s[0, 3 * WIDTH : 4 * WIDTH, :], low).astype(bf16)
        for first in range(0, GROUP, BATCH):
            if first == GROUP // 2:
                at_chunk(c, step0, 1, 3, steps0)
            queries, keys, values, backs = [], [], [], []
            for i in range(first, first + BATCH):
                lanes = slice(i * LANES, (i + 1) * LANES)
                queries += [qkv_s[c, part_of(j), lanes] for j in range(PAIRS)]
                keys += [qkv_s[c, part_of(PAIRS + j), lanes] for j in range(PAIRS)]
                values += [qkv_s[c, part_of(2 * PAIRS + j), lanes].T[:KEYS] for j in range(PAIRS)]
                backs += [o_s[c, part_of(j), lanes] for j in range(PAIRS)]
            chance = [p_s[GROUP * c + first + i] for i in range(BATCH)]
            *results, scores = attend_back(
                keys, queries, values, backs, jnp.concatenate(chance, 1)
            )
            for i in range(BATCH):
                lanes = slice((first + i) * LANES, (first + i + 1) * LANES)
                own = slice(i * PAIRS, (i + 1) * PAIRS)
                dqkv_s[:, lanes] = jnp.concatenate([x for part in results for x in part[own]], 0)
            width = HEADS * LANES
            gbias_s[...] += sum(scores[:, i * width : (i + 1) * width] for i in range(BATCH))
        at_chunk(c, step0, 2, 3, steps0)
        x0 = x0_s[c]
        inverse = inverse_rms(x0)
        add_blocks(0, mul_t(spread_low(x0 * inverse * gain(0, WIDE)), dqkv_s[...]))
        back_normed = packed(mul(wn_s[0, :, : 3 * WIDTH], dqkv_s[...]))
        more, gain_grad = norm_back(x0, inverse, gain(0, WIDE), back_normed)
        ggain_s[0] += fold(gain_grad)
        find(c)
        spread = mul_t(hot_s[...], split_low(back + more))
        ge_s[...] += spread[:, :D] + spread[:, D:]
        return carry

    lax.fori_loop(0, chunks, back_first, 0)

    for block in range(FIRST // D):
        value = g0_s[block]
        if block < 3:
            value = value * HEAD_DIM**-0.5
        first_s[0, block * D : (block + 1) * D, :] = value.astype(bf16)
    codes_s[...] = ge_s[:CODES, :].astype(bf16)
    begin(first0[0], 0)
    begin(codes[0], 0)
    user_low_s[...] = ge_s[CODES:, :].astype(bf16)
    store_users = pltpu.make_async_copy(
        user_low_s, out_user_ref.at[span(slot * n, n)], local_sems.at[BLOCKS + 2]
    )
    store_users.start()
    late = list(range(min(3 * chunks, steps0), steps0))
    if late:
        step0(late.pop(0))

    ones = jnp.ones((8, LANES), f32)
    own_slot_s[8:16, :] = jnp.zeros((8, LANES), f32)
    for g in range(7):
        own_slot_s[g : g + 1, :] = mul_exact_t(ones, ggain_s[g])[:1]
    own_slot_s[7:8, :] = jnp.broadcast_to(loss, (1, LANES))

    def bucket_sums(b, carry):
        for head in range(HEADS):
            lanes = slice(head * LANES, (head + 1) * LANES)
            hit = jnp.where(buckets == b, gbias_s[:, lanes], 0.0)
            rows_s[head, pl.ds(b, 1), :] = jnp.sum(hit, axis=0, keepdims=True)
        return carry

    lax.fori_loop(0, BUCKETS, bucket_sums, 0)
    for head in range(HEADS):
        sums = mul_exact_t(ones, rows_s[head])
        own_slot_s[8 + head : 9 + head, : 2 * BUCKETS] = sums[:1]
    own_slot_s[19:, :] = jnp.zeros((5, LANES), f32)

    for k in range(len(far)):
        finish(first0[0], first_s.at[0], land["first0"], k)
        finish(codes[0], codes_s, land["codes"], k)
        if k + 1 < len(far):
            begin(first0[0], k + 1)
            begin(codes[0], k + 1)

    first_at, first_left = first0[1], held_first[len(far) + 1 :]
    codes_at, codes_left = codes[1], held_codes[len(far) + 1 :]
    size, code_size = first_left[-1], codes_left[-1]
    mine_first = first_at + shift_of(0, first_left)
    mine_codes = codes_at + shift_of(0, codes_left)
    inside, crossing_first, everyone = [], [], []
    for mask in masks:
        source = first_s.at[0, span(first_at + shift_of(mask, first_left), size)]
        copy = remote_to(source, near_first.at[mask], device_of(mask))
        (crossing_first if mask >> 3 else inside).append(copy)
    for mask in masks:
        source = codes_s.at[span(codes_at + shift_of(mask, codes_left), code_size)]
        everyone.append(remote_to(source, near_codes.at[mask], device_of(mask)))
    store_users.wait()
    held = out_user_ref.at[span(slot * n, n)]
    users_out = [remote_to(held, held, device_of(mask)) for mask in masks]

    @pl.when(section == 0)
    def _():
        for copy in inside:
            copy.start()
        cross_first.start()

    @pl.when(section == 1)
    def _():
        for copy in crossing_first:
            copy.start()

    for copy in everyone + users_out:
        copy.start()
    for step in late:
        step0(step)

    def keep_first(value):
        value = value.astype(bf16)
        out_ref[span(REST + mine_first, size), :] = value
        value = value.astype(f32)
        squares = jnp.sum(value * value, axis=0, keepdims=True)
        own_slot_s[17:18, :] = squares / (dp * size // FIRST)

    @pl.when(section == 0)
    def _():
        for copy in inside:
            copy.wait()
        for copy in crossing_first:
            copy.wait_recv()
        cross_first.wait_send()
        value = first_s[0, span(mine_first, size), :].astype(f32)
        for mask in masks:
            value = value + near_first[mask].astype(f32)
        keep_first(value)

    @pl.when(section == 1)
    def _():
        for copy in crossing_first:
            copy.wait_send()
        cross_first.wait_recv()
        value = first_s[1, span(mine_first, size), :].astype(f32)
        keep_first(value + land_first[...].astype(f32))

    for copy in everyone:
        copy.wait()
    value = codes_s[span(mine_codes, code_size), :].astype(f32)
    for mask in masks:
        value = value + near_codes[mask].astype(f32)
    value = value.astype(bf16)
    out_ref[span(COLS + mine_codes, code_size), :] = value
    value = value.astype(f32)
    squares = jnp.sum(value * value, axis=0, keepdims=True)
    own_slot_s[18:19, :] = squares / (2 * dp * code_size // CODES)

    store_slot = pltpu.make_async_copy(
        own_slot_s, out_slot_ref.at[slot], local_sems.at[BLOCKS + 3]
    )
    store_slot.start()

    copies = []
    place = out_ref.at[span(REST + mine_first, size)]
    code_place = out_ref.at[span(COLS + mine_codes, code_size)]
    for mask in masks:
        device = device_of(mask)
        if not mask >> 3:
            copies.append(remote_to(place, place, device))
        copies.append(remote_to(code_place, code_place, device))
    for copy in copies:
        copy.start()
    store_slot.wait()
    held = out_slot_ref.at[slot]
    slots_out = [remote_to(held, held, device_of(mask)) for mask in masks]
    for copy in slots_out:
        copy.start()
    copies += slots_out
    for copy in copies + users_out:
        copy.wait()
    for j, k in enumerate(reversed(range(len(far)))):
        stage = far[k]
        copies = []
        if held_first[k + 1] < held_first[k]:
            place = out_ref.at[span(REST + first_at, held_first[k + 1])]
            copies.append(remote(place, place, stage))
            first_at = first_at - side_of(stage) * held_first[k + 1]
        if held_codes[k + 1] < held_codes[k]:
            place = out_ref.at[span(COLS + codes_at, held_codes[k + 1])]
            copies.append(remote(place, place, stage))
            codes_at = codes_at - side_of(stage) * held_codes[k + 1]
        slots = 16 * 2**j
        first_slot = lax.div(slot, slots) * slots
        held = out_slot_ref.at[pl.ds(first_slot, slots)]
        copies.append(remote(held, held, stage))
        held = out_user_ref.at[span(first_slot * n, slots * n)]
        copies.append(remote(held, held, stage))
        for copy in copies:
            copy.start()
        for copy in copies:
            copy.wait()


def gradients(codes, users, targets, domains, bias, gains, mixer, feed, embedding, dp):
    n = users.shape[0] // 2
    chunks = n // GROUP
    order = stages(dp)
    depth = len(order)
    devices = 2 * dp
    vmem = pl.BlockSpec(memory_space=pltpu.VMEM)
    smem = pl.BlockSpec(memory_space=pltpu.SMEM)
    hbm = pl.BlockSpec(memory_space=pl.ANY)
    stat = (16, LANES)
    held_rest, held_first, held_codes = shares(dp, REST), shares(dp, FIRST), shares(dp, CODES, 1)
    plane, far = depth - 1, depth - 4
    sizes = [*held_rest[1:] * 2, *held_first[1:]]
    sizes += [*held_first[1 : far + 1], *held_codes[1 : far + 1], held_rest[-1], held_first[-1]]
    lands = [pltpu.VMEM((rows, D), bf16) for rows in sizes]
    copies = 128 + 16 * depth
    return pl.pallas_call(
        functools.partial(step_kernel, n, dp),
        out_shape=(
            jax.ShapeDtypeStruct((COLS + CODES, D), bf16),
            jax.ShapeDtypeStruct((devices * n, D), bf16),
            jax.ShapeDtypeStruct((devices, 8, LANES), jnp.int32),
            jax.ShapeDtypeStruct((devices, 24, LANES), f32),
            jax.ShapeDtypeStruct((8, LANES), f32),
        ),
        in_specs=[vmem, smem, vmem, vmem, vmem, smem, vmem, hbm, hbm, hbm],
        out_specs=(vmem, hbm, hbm, hbm, vmem),
        scratch_shapes=[
            pltpu.VMEM((chunks, D, WIDE), f32),
            pltpu.VMEM((chunks, D, WIDE), f32),
            pltpu.VMEM((chunks * COLUMNS * D, LANES), f32),
            pltpu.VMEM((chunks, 3 * WIDTH, SPAN), bf16),
            pltpu.VMEM((n, KEYS, HEADS * LANES), bf16),
            pltpu.VMEM((chunks, WIDTH, SPAN), bf16),
            pltpu.VMEM((chunks, FF, WIDE), bf16),
            pltpu.VMEM((chunks, 2 * WIDTH, WIDE), bf16),
            pltpu.VMEM((3 * WIDTH, 2 * LANES), bf16),
            pltpu.VMEM((2, D, COLS), bf16),
            pltpu.VMEM((2, COLS, D), bf16),
            pltpu.VMEM((2 * D, CODES + n), bf16),
            pltpu.VMEM((7, D, LANES), f32),
            pltpu.VMEM((KEYS, HEADS * LANES), f32),
            pltpu.VMEM((LANES, HEADS * LANES), f32),
            pltpu.VMEM((BLOCKS, D, LANES), f32),
            pltpu.VMEM((CODES + n, D), f32),
            pltpu.VMEM((KEYS, HEADS * LANES), f32),
            pltpu.VMEM((7, D, LANES), f32),
            pltpu.VMEM((HEADS, 2 * BUCKETS, LANES), f32),
            pltpu.VMEM((n, D), f32),
            pltpu.VMEM((n, LANES), jnp.int32),
            pltpu.VMEM((WIDTH, LANES), bf16),
            pltpu.VMEM((WIDTH, LANES), bf16),
            pltpu.VMEM((chunks, 32 * GROUP, LANES), f32),
            pltpu.VMEM((chunks, WIDTH, 32 * GROUP), bf16),
            pltpu.VMEM((2, REST, D), bf16),
            pltpu.VMEM((2, FIRST, D), bf16),
            pltpu.VMEM((CODES, D), bf16),
            pltpu.VMEM((8, LANES), jnp.int32),
            pltpu.VMEM((n, D), bf16),
            pltpu.VMEM((24, LANES), f32),
            pltpu.VMEM((8, WIDE), jnp.int32),
            pltpu.VMEM((CODES + n, WIDE), bf16),
            pltpu.VMEM((3 * WIDTH, SPAN), bf16),
            pltpu.VMEM((depth + 1,) + stat, f32),
            pltpu.VMEM((depth,) + stat, f32),
            pltpu.VMEM((16, held_first[-1], D), bf16),
            pltpu.VMEM((16, held_codes[-1], D), bf16),
            pltpu.SemaphoreType.DMA((BLOCKS + 4,)),
            pltpu.SemaphoreType.DMA((copies,)),
            pltpu.SemaphoreType.DMA((copies,)),
        ]
        + lands,
        compiler_params=pltpu.CompilerParams(
            collective_id=0, has_side_effects=True, vmem_limit_bytes=63 * 2**20
        ),
        name="gradients",
    )(codes, users, users.reshape(1, -1), targets, domains, bias, gains, mixer, feed, embedding)


def adam(weight, moment, square, slope, rate, decay):
    moment = beta_one * moment + (1 - beta_one) * slope
    square = beta_two * square + (1 - beta_two) * slope * slope
    unbiased_moment = moment * (1 / (1 - beta_one**STEP))
    unbiased_square = square * (1 / (1 - beta_two**STEP))
    root = unbiased_square * lax.rsqrt(unbiased_square)
    step = unbiased_moment / (root + adam_eps) + decay * weight
    return weight - rate * step, moment, square


def update_kernel(*refs):
    parts_in, big_in, small_in, refs = refs[:5], refs[5:14], refs[14:20], refs[20:]
    loss_ref, norm_ref, section_ref, hist_ref = refs[:4]
    big_out, small_out, low_out, refs = refs[4:13], refs[13:19], refs[19:22], refs[22:]
    parts, hold, low_hold = refs[:5], refs[5:14], refs[14:17]
    user_grad, part_sems, in_sems, out_sems = refs[17:]
    grad_ref, user_ref, ids_ref, slot_ref, stat_ref = parts
    arrivals = [pltpu.make_async_copy(parts_in[i], parts[i], part_sems.at[i]) for i in range(5)]
    loads = [pltpu.make_async_copy(big_in[i], hold[i], in_sems.at[i]) for i in range(9)]
    for load in arrivals[1:] + arrivals[:1] + loads:
        load.start()
    for arrival in arrivals:
        arrival.wait()

    users = user_grad.shape[0]
    span = min(1024, user_ref.shape[0])
    slots = span // LANES * (ids_ref.shape[0] * LANES // user_ref.shape[0])
    fit = ids_ref.shape[0] * LANES // user_ref.shape[0]
    user_grad[...] = jnp.zeros_like(user_grad)

    def scatter(part, carry):
        rows = user_ref[pl.ds(pl.multiple_of(part * span, span), span), :]
        lanes = []
        for group in range(span // LANES):
            total = ids_ref[part * slots + group * fit, :1, :]
            for other in range(1, fit):
                total = total + ids_ref[part * slots + group * fit + other, :1, :]
            lanes.append(total)
        ids = jnp.concatenate(lanes, 1)
        for block in range(users // USER_ROWS):
            place = slice(block * USER_ROWS, (block + 1) * USER_ROWS)
            hit = iota((USER_ROWS, span), 0) + block * USER_ROWS == ids
            user_grad[place, :] += mul(jnp.where(hit, 1.0, 0.0).astype(bf16), rows)
        return carry

    lax.fori_loop(0, user_ref.shape[0] // span, scatter, 0)

    def total(x):
        return jnp.sum(jnp.sum(x, axis=0, keepdims=True), axis=1, keepdims=True)

    def slot_sum(first):
        def add(i, value):
            return value + slot_ref[2 * i + first]

        zero = jnp.zeros(slot_ref.shape[1:], f32)
        return lax.fori_loop(0, slot_ref.shape[0] // 2, add, zero)

    even, odd = slot_sum(0), slot_sum(1)
    section_squares = [total(x[16:17] + x[17:18]) for x in (even, odd)]
    small = even[:16] + odd[:16]
    rest = total(even[18:19] + odd[18:19])
    user_values = user_grad[...]
    rest = rest + total(user_values * user_values)
    lane, line = iota(small.shape, 1), iota(small.shape, 0)
    counted = (line < 7) | ((line > 7) & (lane < 2 * BUCKETS))
    small_kept = jnp.where(counted, small, 0.0)
    rest = rest + total(small_kept * small_kept)
    norm = jnp.sqrt(section_squares[0] + section_squares[1] + rest)
    factor = jnp.minimum(1.0, clip_norm / (norm + 1e-06))
    loss_ref[0] = small[7, 0]
    norm_ref[0] = norm[0, 0]
    for s in range(2):
        section_ref[s] = jnp.sqrt(section_squares[s])[0, 0]
    for row in range(8):
        lanes = slice((row % 2) * LANES, (row % 2 + 1) * LANES)
        hist_ref[row // 2 : row // 2 + 1, lanes] = stat_ref[row : row + 1, :]

    outs = adam(
        small_in[0][...], small_in[1][...], small_in[2][...], factor * small[:7], rate_gain, 0.0
    )
    for ref, value in zip(small_out[:3], outs):
        ref[...] = value
    for head in range(HEADS):
        for s in range(2):
            slope = factor * small[8 + head : 9 + head, s * BUCKETS : (s + 1) * BUCKETS]
            one = slice(s, s + 1)
            outs = adam(
                small_in[3][head, one, :],
                small_in[4][head, one, :],
                small_in[5][head, one, :],
                slope,
                rate_small,
                0.0,
            )
            for ref, value in zip(small_out[3:], outs):
                ref[head, one, :] = value

    stores = []

    def store(kind, place):
        first = 3 * kind
        pieces = [(hold[first + i], big_out[first + i]) for i in range(3)]
        pieces.append((low_hold[kind], low_out[kind]))
        for source, target in pieces:
            copy = pltpu.make_async_copy(
                source.at[place], target.at[place], out_sems.at[len(stores)]
            )
            copy.start()
            stores.append(copy)

    def step(kind, place, slope):
        first = 3 * kind
        outs = adam(
            hold[first][place],
            hold[first + 1][place],
            hold[first + 2][place],
            factor * slope,
            rate_matrix,
            decay_matrix,
        )
        for i in range(3):
            hold[first + i][place] = outs[i]
        low_hold[kind][place] = outs[0].astype(bf16)

    def block_of(block):
        first = FIRST // D
        place = block - first if block >= first else REST // D + block
        return grad_ref[place * D : (place + 1) * D, :].astype(f32)

    for i in range(3):
        loads[i].wait()
    for part in range(6):
        for block in range(3 * part, 3 * part + 3):
            lanes = slice(block * LANES, (block + 1) * LANES)
            step(0, (0, slice(None), lanes), block_of(block))
        store(0, (0, slice(None), slice(3 * part * LANES, 3 * (part + 1) * LANES)))
    for i in range(3, 6):
        loads[i].wait()
    for part in range(4):
        for block in range(4 * part, 4 * part + 4):
            lanes = slice(block * LANES, (block + 1) * LANES)
            step(1, (0, slice(None), lanes), block_of(MIXW // LANES + block))
        store(1, (0, slice(None), slice(4 * part * LANES, 4 * (part + 1) * LANES)))
    for i in range(6, 9):
        loads[i].wait()
    for part in range(4):
        rows = slice(part * CODEBOOK, (part + 1) * CODEBOOK)
        step(2, (rows, slice(None)), grad_ref[COLS + rows.start : COLS + rows.stop, :].astype(f32))
        store(2, (rows, slice(None)))
    for part in range(users // USER_ROWS):
        rows = slice(part * USER_ROWS, (part + 1) * USER_ROWS)
        place = (slice(CODES + part * USER_ROWS, CODES + (part + 1) * USER_ROWS), slice(None))
        step(2, place, user_grad[rows, :])
        store(2, place)
    for copy in stores:
        copy.wait()


def update(reduced, mixers, feeds, embeds, gains, biases):
    vmem = pl.BlockSpec(memory_space=pltpu.VMEM)
    smem = pl.BlockSpec(memory_space=pltpu.SMEM)
    hbm = pl.BlockSpec(memory_space=pl.ANY)
    big = [*mixers, *feeds, *embeds]
    small = [*gains, *biases]
    low = [jax.ShapeDtypeStruct(x[0].shape, bf16) for x in (mixers, feeds, embeds)]
    users = embeds[0].shape[0] - CODES
    pieces = 4 * (6 + 4 + 4 + users // USER_ROWS)
    return pl.pallas_call(
        update_kernel,
        out_shape=[
            jax.ShapeDtypeStruct((1,), f32),
            jax.ShapeDtypeStruct((1,), f32),
            jax.ShapeDtypeStruct((2,), f32),
            jax.ShapeDtypeStruct((LEVELS, CODEBOOK), f32),
        ]
        + [jax.ShapeDtypeStruct(x.shape, f32) for x in big + small]
        + low,
        in_specs=[hbm] * 14 + [vmem] * 6,
        out_specs=[smem] * 3 + [vmem] + [hbm] * 9 + [vmem] * 6 + [hbm] * 3,
        scratch_shapes=[pltpu.VMEM(x.shape, x.dtype) for x in reduced]
        + [pltpu.VMEM(x.shape, f32) for x in big]
        + [pltpu.VMEM(x.shape, bf16) for x in low]
        + [
            pltpu.VMEM((users, D), f32),
            pltpu.SemaphoreType.DMA((5,)),
            pltpu.SemaphoreType.DMA((9,)),
            pltpu.SemaphoreType.DMA((pieces,)),
        ],
        compiler_params=pltpu.CompilerParams(vmem_limit_bytes=62 * 2**20),
        name="update",
    )(*reduced, *big, *small)


def shards(
    history_codes,
    user_ids,
    targets,
    domains,
    mixer,
    mixer_moment,
    mixer_square,
    feed,
    feed_moment,
    feed_square,
    embedding,
    embedding_moment,
    embedding_square,
    gains,
    gains_moment,
    gains_square,
    position_bias,
    bias_moment,
    bias_square,
):
    def turned(table):
        return jnp.transpose(table, (2, 0, 1))

    biases = [turned(x) for x in (position_bias, bias_moment, bias_square)]
    reduced = gradients(
        history_codes,
        user_ids,
        targets.T,
        domains.reshape(1, -1),
        biases[0],
        gains,
        mixer,
        feed,
        embedding,
        lax.axis_size("dp"),
    )
    outs = update(
        reduced,
        (mixer, mixer_moment, mixer_square),
        (feed, feed_moment, feed_square),
        (embedding, embedding_moment, embedding_square),
        (gains, gains_moment, gains_square),
        biases,
    )
    loss, norm, sections, histograms = outs[:4]
    back = [jnp.transpose(x, (1, 2, 0)) for x in outs[16:19]]
    return (
        loss.reshape(()),
        norm.reshape(()),
        sections,
        histograms,
        *outs[4:16],
        *back,
        *outs[19:],
    )


def solution(mesh):
    by_dp, by_pipe, copied = P("dp"), P("pipe"), P()
    return jax.shard_map(
        shards,
        mesh=mesh,
        in_specs=(by_dp,) * 4 + (by_pipe,) * 6 + (copied,) * 9,
        out_specs=(copied,) * 4 + (by_pipe,) * 6 + (copied,) * 9 + (by_pipe,) * 2 + (copied,),
        check_vma=False,
    )
```

```python
import functools

import jax
import jax.numpy as jnp
from jax import lax
from jax.experimental import pallas as pl
from jax.experimental.pallas import tpu as pltpu
from jax.sharding import PartitionSpec as P

D = 128
HEADS = 6
HEAD_DIM = 64
FF = 1024
CODEBOOK = 256
LEVELS = 4
BUCKETS = 32
DOMAINS = 3
HIST_LEN = 81
STEP = 5
CODES = 1024
LANES = 128
WIDTH = HEADS * HEAD_DIM
MIXW = 6 * WIDTH
COLS = MIXW + 2 * FF
BLOCKS = COLS // LANES
KEYS = 96
GROUP = 8
BATCH = 2
NEAR = 3
PACK = 96
WIDE = GROUP * PACK
SPAN = GROUP * LANES
COLUMNS = WIDE // LANES
PAIRS = HEADS // 2
FIRST = 4 * WIDTH
REST = COLS - FIRST
USER_ROWS = 400
MESH = pl.DeviceIdType.MESH

norm_eps = 1e-06
beta_one = 0.9
beta_two = 0.999
adam_eps = 1e-08
clip_norm = 0.5
rate_matrix = 0.04
rate_gain = 0.8
rate_small = 0.3
decay_matrix = 0.01

f32 = jnp.float32
bf16 = jnp.bfloat16


def iota(shape, axis):
    return lax.broadcasted_iota(jnp.int32, shape, axis)


def mul(left, right):
    return jnp.dot(left, right, preferred_element_type=f32)


def mul_t(left, right):
    return lax.dot_general(left, right, (((1,), (1,)), ((), ())), preferred_element_type=f32)


def mul_exact(left, right):
    return jnp.dot(left, right, preferred_element_type=f32, precision=lax.Precision.HIGHEST)


def mul_exact_t(left, right):
    return lax.dot_general(
        left,
        right,
        (((1,), (1,)), ((), ())),
        preferred_element_type=f32,
        precision=lax.Precision.HIGHEST,
    )


def onehot(ids, rows):
    return jnp.where(iota((rows, ids.shape[1]), 0) == ids, 1.0, 0.0).astype(bf16)


def inverse_rms(x):
    return lax.rsqrt(jnp.mean(x * x, axis=0, keepdims=True) + norm_eps)


def norm_low(x, inverse, gain):
    return (x * inverse * gain).astype(bf16)


def norm_back(x, inverse, gain, upstream):
    scaled = x * inverse
    inner = upstream * gain
    back = inverse * (inner - scaled * jnp.mean(inner * scaled, axis=0, keepdims=True))
    return back, upstream * scaled


def block_diag(pair):
    zero = jnp.zeros((HEAD_DIM, LANES), pair.dtype)
    left = jnp.concatenate([pair[:HEAD_DIM], zero], 0)
    right = jnp.concatenate([zero, pair[HEAD_DIM:]], 0)
    return jnp.concatenate([left, right], 1)


def diagonal(both):
    return jnp.concatenate([both[:HEAD_DIM, :LANES], both[HEAD_DIM:, LANES:]], 0)


def turn(x, shift):
    return x if shift % LANES == 0 else pltpu.roll(x, shift % LANES, 1)


def pack(tables):
    lane = iota(tables[0].shape, 1)
    columns = []
    for first in range(0, len(tables), 4):
        turned = [turn(tables[first + i], PACK * i) for i in range(4)]
        for i in range(3):
            columns.append(jnp.where(lane < PACK - 32 * i, turned[i], turned[i + 1]))
    return jnp.concatenate(columns, 1)


def unpack(x):
    lane = iota((x.shape[0], LANES), 1)
    tables = []
    for first in range(0, x.shape[1] // LANES, 3):
        a, b, c = [x[:, (first + i) * LANES : (first + i + 1) * LANES] for i in range(3)]
        tables.append(a)
        tables.append(jnp.where(lane < 32, turn(a, 32), turn(b, 32)))
        tables.append(jnp.where(lane < 64, turn(b, 64), turn(c, 64)))
        tables.append(turn(c, 96))
    return tables


def stack(both):
    return jnp.concatenate([both[:, :LANES], both[:, LANES:]], 0)


def pad_keys(table):
    if table.shape[0] == LANES:
        return table
    zero = jnp.zeros((LANES - table.shape[0], table.shape[1]), table.dtype)
    return jnp.concatenate([table, zero], 0)


def columns_of(table, i):
    return table[:, 2 * i * LANES : 2 * (i + 1) * LANES]


def attend(keys, queries, values, bias):
    scores = [mul(key, block_diag(query)) for key, query in zip(keys, queries)]
    scores = jnp.concatenate(scores, 1) + bias
    top = jnp.max(scores, axis=0, keepdims=True)
    chance = jnp.exp(scores - top)
    total = jnp.sum(chance, axis=0, keepdims=True)
    chance = (chance * (1.0 / total)).astype(bf16)
    full = pad_keys(chance)
    mixed = [mul(value, columns_of(full, i)) for i, value in enumerate(values)]
    return chance, [diagonal(both).astype(bf16) for both in mixed]


def attend_back(keys_t, queries, values, back_mixed, chance):
    exact = chance.astype(f32)
    back_chance = [mul(value, block_diag(back)) for value, back in zip(values, back_mixed)]
    back_chance = jnp.concatenate(back_chance, 1)
    inner = jnp.sum(back_chance * exact, axis=0, keepdims=True)
    back_scores = exact * (back_chance - inner)
    low = pad_keys(back_scores.astype(bf16))
    full = pad_keys(chance)
    count = range(len(queries))
    back_query = [mul(keys_t[i], columns_of(low, i)) for i in count]
    back_keys = [mul_t(queries[i], stack(columns_of(low, i))) for i in count]
    back_values = [mul_t(back_mixed[i], stack(columns_of(full, i))) for i in count]
    results = [
        [diagonal(both).astype(bf16) for both in part]
        for part in (back_query, back_keys, back_values)
    ]
    return *results, back_scores


def split_low(x):
    high = x.astype(bf16)
    return jnp.concatenate([high, (x - high.astype(f32)).astype(bf16)], 0)


def stages(dp):
    bits = [2**k for k in range(dp.bit_length() - 1)]
    return [("dp", bit) for bit in bits[:2] + bits[4:] + bits[2:4]] + [("pipe", 1)]


def side_of(stage):
    axis, bit = stage
    return lax.rem(lax.div(lax.axis_index(axis), bit), 2)


def partner_of(stage):
    axis, bit = stage
    return {axis: lax.axis_index(axis) + bit * (1 - 2 * side_of(stage))}


def shares(dp, rows, across=0):
    held = [rows]
    depth = len(stages(dp)) - 1
    for k in range(depth + across):
        later = min(NEAR - 1, depth - 1 - k) + across if k < depth else 0
        half = held[-1] // 2
        held.append(half if half % (16 * 2**later) == 0 else held[-1])
    return held


def span(start, size):
    return pl.ds(pl.multiple_of(start, 16), size)


def step_kernel(n, dp, *refs):
    codes_ref, users_ref, user_row_ref, targets_ref, domains_ref, bias_ref, gains_ref = refs[:7]
    mixer_ref, feed_ref, embed_ref = refs[7:10]
    out_ref, out_user_ref, out_ids_ref, out_slot_ref, out_stat_ref = refs[10:15]
    x0_s, x1_s, x2_s, qkv_s, p_s, o_s, r_s, mem_s, dz_s, wn_s, wt_s, ext_s = refs[15:27]
    gain_s, ebias_s, dbias_s, g0_s, ge_s, gbias_s, ggain_s, rows_s, user_s, ids_s = refs[27:37]
    cross_s, cross_back_s, pc_s, oc_s, rest_s, first_s, codes_s, slot_s, user_low_s, own_slot_s, id_rows_s, hot_s, dqkv_s = refs[37:50]
    stat_s, stat_land, near_first, near_codes, local_sems, sends, recvs = refs[50:57]
    lands = refs[57:]
    order = stages(dp)
    across = order[-1]
    depth = len(order)
    chunks = n // GROUP
    section = lax.axis_index("pipe")
    used = [0]

    def remote_to(source, target, device):
        index = used[0]
        used[0] += 1
        return pltpu.make_async_remote_copy(
            src_ref=source,
            dst_ref=target,
            send_sem=sends.at[index],
            recv_sem=recvs.at[index],
            device_id=device,
            device_id_type=MESH,
        )

    def remote(source, target, stage):
        return remote_to(source, target, partner_of(stage))

    near, far = order[-NEAR:], order[:-NEAR]
    masks = range(1, 2 ** len(near))

    def device_of(mask):
        place = {"dp": lax.axis_index("dp"), "pipe": lax.axis_index("pipe")}
        for i, (axis, bit) in enumerate(near):
            if mask >> i & 1:
                place[axis] = place[axis] + bit * (1 - 2 * side_of((axis, bit)))
        return place

    def shift_of(mask, lefts):
        total = 0
        for i, left in enumerate(lefts):
            side = side_of(near[i])
            total = total + (1 - side if mask >> i & 1 else side) * left
        return total

    locals_in = []
    for block in range(BLOCKS):
        lanes = slice(block * LANES, (block + 1) * LANES)
        if block < MIXW // LANES:
            source = mixer_ref.at[0, :, lanes]
        else:
            source = feed_ref.at[0, :, slice(lanes.start - MIXW, lanes.stop - MIXW)]
        locals_in.append(pltpu.make_async_copy(source, g0_s.at[block], local_sems.at[block]))
    vocabulary = embed_ref.shape[0]
    flat = x2_s.at[pl.ds(0, vocabulary)]
    load_embed = pltpu.make_async_copy(embed_ref, flat, local_sems.at[BLOCKS])
    for copy in locals_in:
        copy.start()
    load_embed.start()

    barrier = pltpu.get_barrier_semaphore()
    for stage in far:
        pl.semaphore_signal(barrier, inc=1, device_id=partner_of(stage), device_id_type=MESH)
    for mask in masks:
        pl.semaphore_signal(barrier, inc=1, device_id=device_of(mask), device_id_type=MESH)

    scale = HEAD_DIM**-0.5
    cross_scale = jnp.where(section == 1, scale, 1.0).astype(f32)
    for copy in locals_in:
        copy.wait()
    for block in range(BLOCKS):
        value = g0_s[block]
        if block < 3:
            value = value * scale
        elif 12 <= block < 15:
            value = value * cross_scale
        wn_s[section, :, block * LANES : (block + 1) * LANES] = value.astype(bf16)
    pl.semaphore_wait(barrier, len(far) + len(masks))
    half = D // 2
    mine = span(side_of(order[0]) * half, half)
    pieces = (slice(0, FIRST), slice(FIRST, COLS))
    over = [
        remote(wn_s.at[section, mine, piece], wn_s.at[section, mine, piece], across)
        for piece in pieces
    ]
    for copy in over:
        copy.start()

    ids_s[:, : HIST_LEN - 1] = codes_ref[pl.ds(pl.multiple_of(section * n, 8), n), :]
    lane, row = iota((n, LANES), 1), iota((n, LANES), 0)
    ids = ids_s[...] + ((lane & 3) << 8)
    ids = jnp.where(lane < HIST_LEN - 1, ids, jnp.where(lane == HIST_LEN - 1, CODES + row, -1))
    ids_s[...] = ids
    packed = []
    for i in range(GROUP):
        rows = [ids_s[c * GROUP + i : c * GROUP + i + 1, :] for c in range(chunks)]
        rows += [jnp.zeros((8 - chunks, LANES), jnp.int32)]
        packed.append(jnp.concatenate(rows, 0))
    id_rows_s[...] = pack(packed)
    count = targets_ref.shape[1]
    history, token = iota((count, LANES), 0), iota((count, LANES), 1)
    pick = jnp.where((token >> 2) + section * n == history, 1.0, 0.0)
    level, place = iota((LEVELS, LANES), 0), iota((LEVELS, LANES), 1) & 3
    target = mul(targets_ref[...].astype(f32), pick) + (level * CODEBOOK).astype(f32)
    goal = jnp.sum(jnp.where(level == place, target, 0.0), axis=0, keepdims=True).astype(jnp.int32)
    start_ids = jnp.sum(
        jnp.where(level == place - 1, target, 0.0), axis=0, keepdims=True
    ).astype(jnp.int32)
    domain = mul(domains_ref[...].astype(f32), pick)
    pick = jnp.where(lax.rem(token, n) + section * n == history, 1.0, 0.0)
    own_users = mul_exact(user_row_ref[...].astype(f32), pick)

    counts = [
        jnp.sum(jnp.where(domain == d, 1.0, 0.0), axis=1, keepdims=True) for d in range(DOMAINS)
    ]
    counts += [jnp.zeros((1, 1), f32)] * (8 - DOMAINS)
    stat_s[0, 8:, :] = jnp.broadcast_to(jnp.concatenate(counts, 0), (8, LANES))
    histogram = mul_t(jnp.ones((8, LANES), bf16), onehot(goal, CODES))
    for r in range(8):
        stat_s[0, r : r + 1, :] = histogram[:1, r * LANES : (r + 1) * LANES]
    slot = 0
    for k, stage in enumerate(order):
        slot = slot + side_of(stage) * 2 ** (depth - 1 - k)
    owner = iota((8, LANES), 1) // n
    own_users = jnp.broadcast_to(own_users, (8, LANES)).astype(jnp.int32)
    slot_s[...] = jnp.where(owner == lax.rem(slot, LANES // n), own_users, 0)
    store_ids = pltpu.make_async_copy(slot_s, out_ids_ref.at[slot], local_sems.at[BLOCKS + 1])
    store_ids.start()
    store_ids.wait()

    def slots_of(j):
        return pl.ds(lax.div(slot, 2**j) * 2**j, 2**j)

    early = []
    for j, stage in enumerate(reversed(order)):
        held = out_ids_ref.at[slots_of(j)]
        early.append(
            (
                remote(stat_s.at[j], stat_land.at[j], stage),
                remote(held, held, stage),
            )
        )

    def early_step(j):
        if j > 0:
            for copy in early[j - 1]:
                copy.wait()
            stat_s[j] = stat_s[j - 1] + stat_land[j - 1]
        if j < depth:
            for copy in early[j]:
                copy.start()

    eye = jnp.where(iota((LANES, LANES), 0) == iota((LANES, LANES), 1), 1.0, 0.0).astype(bf16)
    load_embed.wait()

    def fetch(i, carry):
        user_s[pl.ds(i, 1), :] = x2_s[pl.ds(CODES + users_ref[section * n + i], 1), :]
        return carry

    lax.fori_loop(0, n, fetch, 0, unroll=8)
    for block in range(CODES // LANES + 1):
        if block < CODES // LANES:
            rows = x2_s[block * LANES : (block + 1) * LANES, :]
            codes_s[block * LANES : (block + 1) * LANES, :] = rows.astype(bf16)
            width = LANES
        else:
            rows = user_s[...]
            width = n
        high = rows.astype(bf16)
        low = (rows - high.astype(f32)).astype(bf16)
        lanes = slice(block * LANES, block * LANES + width)
        ext_s[:D, lanes] = mul_t(eye, high).astype(bf16)
        ext_s[D:, lanes] = mul_t(eye, low).astype(bf16)

    def find(c):
        ids = id_rows_s[pl.ds(c, 1), :]
        for first in range(0, CODES + n, LANES):
            rows = min(LANES, CODES + n - first)
            hot_s[first : first + rows, :] = onehot(ids - first, rows)

    def lookup(c, carry):
        find(c)
        both = mul(ext_s[...], hot_s[...])
        x0_s[c] = both[:D] + both[D:]
        return carry

    lax.fori_loop(0, chunks, lookup, 0)

    beside = []
    for piece in pieces:
        came = wn_s.at[1 - section, mine, piece]
        beside.append(remote(came, came, order[0]))
    over[0].wait()
    beside[0].start()

    for g in range(7):
        gain_s[g] = jnp.broadcast_to(gains_ref[g : g + 1, :], (LANES, LANES)).T

    def positions(axis):
        index = iota((KEYS, LANES), axis)
        return jnp.where(index == HIST_LEN - 1, 0, index + 1)

    key, query = positions(0), positions(1)
    distance = jnp.abs(query - key)
    remoteness = jnp.zeros_like(distance)
    for edge in (12, 16, 23, 32, 46, 64, 91):
        remoteness = remoteness + (distance >= edge).astype(jnp.int32)
    nearby = jnp.minimum(jnp.where(distance < 8, distance, 8 + remoteness), 15)
    buckets = nearby + jnp.where(key > query, 16, 0)
    real = iota((KEYS, LANES), 0) < HIST_LEN
    for head in range(HEADS):
        lanes = slice(head * LANES, (head + 1) * LANES)

        def choose(b, table):
            return jnp.where(buckets == b, bias_ref[head, 0, b], table)

        table = lax.fori_loop(0, BUCKETS, choose, jnp.zeros((KEYS, LANES), f32), unroll=True)
        ebias_s[:, lanes] = jnp.where(real, table, -1e30)
    key, query = iota((LANES, LANES), 0), iota((LANES, LANES), 1)
    offset = query - key
    seen = ((key >> 2) == (query >> 2)) & (offset >= 0)
    for head in range(HEADS):
        lanes = slice(head * LANES, (head + 1) * LANES)
        table = jnp.full((LANES, LANES), -1e30, f32)
        for b in range(LEVELS):
            table = jnp.where(seen & (offset == b), bias_ref[head, 1, b], table)
        dbias_s[:, lanes] = table

    def transpose_weights(which, first, last):
        for block in range(first, last):
            place = slice(block * LANES, (block + 1) * LANES)
            wt_s[which, place, :] = wn_s[which, :, place].T

    transpose_weights(section, 0, BLOCKS)
    beside[0].wait()
    transpose_weights(1 - section, 0, FIRST // LANES)

    def rest_arrives():
        over[1].wait()
        beside[1].start()
        beside[1].wait()
        transpose_weights(1 - section, FIRST // LANES, BLOCKS)

    def gain(g, width):
        column = gain_s[g]
        return column if width == LANES else jnp.concatenate([column] * (width // LANES), 1)

    def at_chunk(c, step, point, points, count):
        for j in range(point, count, points):
            pl.when(c == j // points)(functools.partial(step, j))

    def spread_low(x):
        return jnp.concatenate([part.astype(bf16) for part in unpack(x)], 1)

    def packed(x):
        return pack([x[:, i * LANES : (i + 1) * LANES] for i in range(GROUP)])

    def part_of(j):
        return slice(j * LANES, (j + 1) * LANES)

    def encode(c, carry):
        at_chunk(c, early_step, 0, 2, depth + 1)
        x0 = x0_s[c]
        h = spread_low(x0 * inverse_rms(x0) * gain(0, WIDE))
        for j in range(3):
            part = slice(j * WIDTH, (j + 1) * WIDTH)
            qkv_s[c, part, :] = mul(wt_s[0, part, :], h).astype(bf16)
        for first in range(0, GROUP, BATCH):
            queries, keys, values = [], [], []
            for i in range(first, first + BATCH):
                lanes = slice(i * LANES, (i + 1) * LANES)
                queries += [qkv_s[c, part_of(j), lanes] for j in range(PAIRS)]
                keys += [qkv_s[c, part_of(PAIRS + j), lanes].T[:KEYS] for j in range(PAIRS)]
                values += [qkv_s[c, part_of(2 * PAIRS + j), lanes] for j in range(PAIRS)]
            bias = jnp.concatenate([ebias_s[...]] * BATCH, 1)
            chance, mixed = attend(keys, queries, values, bias)
            for i in range(BATCH):
                lanes = slice((first + i) * LANES, (first + i + 1) * LANES)
                p_s[GROUP * c + first + i] = chance[:, i * HEADS * LANES : (i + 1) * HEADS * LANES]
                o_s[c, :, lanes] = jnp.concatenate(mixed[i * PAIRS : (i + 1) * PAIRS], 0)
        x1 = x0 + packed(mul(wn_s[0, :, 3 * WIDTH : 4 * WIDTH], o_s[c]))
        x1_s[c] = x1
        at_chunk(c, early_step, 1, 2, depth + 1)
        pl.when(c == 0)(rest_arrives)
        h = norm_low(x1, inverse_rms(x1), gain(1, WIDE))
        for j in range(2):
            part = slice(j * FF // 2, (j + 1) * FF // 2)
            lifted = mul(wt_s[0, MIXW + j * FF // 2 : MIXW + (j + 1) * FF // 2, :], h)
            r_s[c, part, :] = jnp.maximum(lifted, 0.0).astype(bf16)
        x2 = x1 + mul(wn_s[0, :, MIXW + FF :], r_s[c])
        put_wide(x2_s, c, x2)
        e = norm_low(x2, inverse_rms(x2), gain(2, WIDE))
        for j in range(2):
            part = slice(j * WIDTH, (j + 1) * WIDTH)
            mem_s[c, part, :] = mul(
                wt_s[0, 4 * WIDTH + j * WIDTH : 4 * WIDTH + (j + 1) * WIDTH, :], e
            ).astype(bf16)
        return carry

    def put_wide(ref, c, value):
        for i in range(COLUMNS):
            ref[pl.ds(pl.multiple_of((COLUMNS * c + i) * D, D), D), :] = value[
                :, i * LANES : (i + 1) * LANES
            ]

    def get_wide(ref, c):
        return jnp.concatenate(
            [ref[pl.ds(pl.multiple_of((COLUMNS * c + i) * D, D), D), :] for i in range(COLUMNS)], 1
        )

    lax.fori_loop(0, chunks, encode, 0)
    for j in range(2 * chunks, depth + 1):
        early_step(j)
    out_stat_ref[...] = stat_s[depth, :8, :]

    def put_blocks(first, value):
        for index in range(value.shape[1] // LANES):
            block = first + index
            part = value[:, index * LANES : (index + 1) * LANES].astype(bf16)
            if block < FIRST // LANES:
                first_s[1, block * D : (block + 1) * D, :] = part
            else:
                block -= FIRST // LANES
                rest_s[1, block * D : (block + 1) * D, :] = part

    def add_blocks(first, value):
        for index in range(value.shape[1] // LANES):
            g0_s[first + index] += value[:, index * LANES : (index + 1) * LANES]

    start = onehot(start_ids, CODES)
    both = mul(ext_s[:, :CODES], start)
    y0 = both[:D] + both[D:]
    inverse0 = inverse_rms(y0)
    h0 = norm_low(y0, inverse0, gain(3, LANES))
    dz_s[:, :LANES] = mul(wt_s[1, : 3 * WIDTH, :], h0).astype(bf16)
    both = mul(mul_t(eye, h0).astype(bf16), wn_s[1, :, WIDTH : 3 * WIDTH]).astype(bf16)
    self_chance, mixed = attend(
        [both[:, part_of(j)] for j in range(PAIRS)],
        [dz_s[part_of(j), :LANES] for j in range(PAIRS)],
        [dz_s[part_of(2 * PAIRS + j), :LANES] for j in range(PAIRS)],
        dbias_s[...],
    )
    self_values = both[:, WIDTH:]
    self_mixed = jnp.concatenate(mixed, 0)
    y1 = y0 + mul(wn_s[1, :, 3 * WIDTH : 4 * WIDTH], self_mixed)
    inverse1 = inverse_rms(y1)
    h1 = norm_low(y1, inverse1, gain(4, LANES))
    cross_s[...] = mul(wt_s[1, 4 * WIDTH : 5 * WIDTH, :], h1).astype(bf16)

    def spreader(g, turned):
        shape = (LANES, 32 * GROUP) if turned else (32 * GROUP, LANES)
        row, token = iota(shape, 1 if turned else 0), iota(shape, 0 if turned else 1)
        hit = token == 4 * GROUP * g + 4 * (row >> 5) + (row & 3)
        return jnp.where(hit, 1.0, 0.0).astype(bf16)

    def rows_of(g, table):
        rows = mul_t(spreader(g, False), table)
        mask = (iota(rows.shape, 1) >> 6) == ((iota(rows.shape, 0) & 31) >> 2)
        return jnp.where(mask, rows, 0.0).astype(bf16)

    def head_mask(shape):
        return (iota(shape, 0) >> 6) == ((iota(shape, 1) & 31) >> 2)

    def rows_t_of(g, table):
        rows = mul(table, spreader(g, True))
        return jnp.where(head_mask(rows.shape), rows, 0.0).astype(bf16)

    def gather_rows(ref):
        total = jnp.zeros((WIDTH, LANES), f32)
        for g in range(chunks):
            total = total + mul(ref[g], spreader(g, False))
        return total.astype(bf16)

    def blocks_of(table):
        rows = []
        for i in range(GROUP):
            part = table[32 * i : 32 * i + 32]
            column, shift = divmod(PACK * i, LANES)
            part = turn(part, shift)
            lane = iota(part.shape, 1)
            zero = jnp.zeros_like(part)
            columns = [zero] * COLUMNS
            columns[column] = jnp.where(lane >= shift, part, 0.0)
            if shift > LANES - PACK:
                columns[column + 1] = jnp.where(lane < shift, part, 0.0)
            rows.append(jnp.concatenate(columns, 1))
        return jnp.concatenate(rows, 0).astype(bf16)

    def row_products(rows, ref, g, first):
        both = mul(rows, ref[g, first : first + WIDTH, :])
        parts = []
        for i in range(GROUP):
            own = both[32 * i : 32 * i + 32]
            column, shift = divmod(PACK * i, LANES)
            part = turn(own[:, column * LANES : (column + 1) * LANES], -shift)
            if shift > LANES - PACK:
                after = turn(own[:, (column + 1) * LANES : (column + 2) * LANES], -shift)
                part = jnp.where(iota(part.shape, 1) < LANES - shift, part, after)
            parts.append(part)
        return jnp.concatenate(parts, 0)

    def cross(g, carry):
        queries = rows_of(g, cross_s[...])
        scores = row_products(queries, mem_s, g, 0)
        scores = jnp.where(iota(scores.shape, 1) < HIST_LEN, scores, -1e30)
        chance = jnp.exp(scores - jnp.max(scores, axis=1, keepdims=True))
        chance = chance * (1.0 / jnp.sum(chance, axis=1, keepdims=True))
        pc_s[g] = chance
        mixed = mul_t(mem_s[g, WIDTH:, :], blocks_of(chance))
        oc_s[g] = jnp.where(head_mask(mixed.shape), mixed, 0.0).astype(bf16)
        return carry

    lax.fori_loop(0, chunks, cross, 0, unroll=True)
    cross_mixed = gather_rows(oc_s)
    y2 = y1 + mul(wn_s[1, :, 5 * WIDTH : 6 * WIDTH], cross_mixed)
    inverse2 = inverse_rms(y2)
    h2 = norm_low(y2, inverse2, gain(5, LANES))
    lifted = mul(wt_s[1, MIXW : MIXW + FF, :], h2)
    active = jnp.maximum(lifted, 0.0).astype(bf16)
    y3 = y2 + mul(wn_s[1, :, MIXW + FF :], active)
    inverse3 = inverse_rms(y3)
    final = norm_low(y3, inverse3, gain(6, LANES))
    logits = mul(codes_s[...], final)
    top = jnp.max(logits, axis=0, keepdims=True)
    log_total = top + jnp.log(jnp.sum(jnp.exp(logits - top), axis=0, keepdims=True))
    match = iota(logits.shape, 0) == goal
    picked = jnp.sum(jnp.where(match, logits, 0.0), axis=0, keepdims=True)
    weight = jnp.zeros((1, LANES), f32)
    for d in range(DOMAINS):
        share = 1.0 / (DOMAINS * jnp.maximum(stat_s[depth, 8 + d : 9 + d, :], 1.0))
        weight = weight + jnp.where(domain == d, share, 0.0)
    loss = jnp.sum(weight * (log_total - picked), axis=1, keepdims=True)
    back_logits = (
        weight * (jnp.exp(logits - log_total) - jnp.where(match, 1.0, 0.0))
    ).astype(bf16)
    back_final = mul(ext_s[:D, :CODES], back_logits)
    table_grad = mul_t(back_logits, final)
    back, gain_grad = norm_back(y3, inverse3, gain(6, LANES), back_final)
    ggain_s[6] = gain_grad
    low = back.astype(bf16)
    put_blocks(26, mul_t(low, active))
    back_lifted = jnp.where(lifted > 0, mul(wt_s[1, MIXW + FF :, :], low), 0.0).astype(bf16)
    put_blocks(18, mul_t(h2, back_lifted))
    more, gain_grad = norm_back(
        y2, inverse2, gain(5, LANES), mul(wn_s[1, :, MIXW : MIXW + FF], back_lifted)
    )
    ggain_s[5] = gain_grad
    back = back + more
    low = back.astype(bf16)
    put_blocks(15, mul_t(low, cross_mixed))
    cross_back_s[...] = mul(wt_s[1, 5 * WIDTH : 6 * WIDTH, :], low).astype(bf16)

    def cross_back(g, carry):
        mixed_rows = rows_of(g, cross_back_s[...])
        back_chance = row_products(mixed_rows, mem_s, g, WIDTH)
        back_chance = jnp.where(iota(back_chance.shape, 1) < HIST_LEN, back_chance, 0.0)
        chance = pc_s[g]
        inner = jnp.sum(back_chance * chance, axis=1, keepdims=True)
        spread = blocks_of(chance * (back_chance - inner))
        total = mul_t(mem_s[g, :WIDTH, :], spread)
        mem_s[g, :WIDTH, :] = mul(rows_t_of(g, cross_s[...]), spread).astype(bf16)
        mem_s[g, WIDTH:, :] = mul(rows_t_of(g, cross_back_s[...]), blocks_of(chance)).astype(bf16)
        oc_s[g] = jnp.where(head_mask(total.shape), total, 0.0).astype(bf16)
        return carry

    lax.fori_loop(0, chunks, cross_back, 0, unroll=True)
    back_query = gather_rows(oc_s)
    put_blocks(12, mul_t(h1, back_query) * HEAD_DIM**-0.5)
    more, gain_grad = norm_back(
        y1, inverse1, gain(4, LANES), mul(wn_s[1, :, 4 * WIDTH : 5 * WIDTH], back_query)
    )
    ggain_s[4] = gain_grad
    back = back + more
    low = back.astype(bf16)
    put_blocks(9, mul_t(low, self_mixed))
    back_mixed = mul(wt_s[1, 3 * WIDTH : 4 * WIDTH, :], low).astype(bf16)
    *back_parts, self_scores = attend_back(
        [dz_s[part_of(PAIRS + j), :LANES] for j in range(PAIRS)],
        [dz_s[part_of(j), :LANES] for j in range(PAIRS)],
        [self_values[:, part_of(j)] for j in range(PAIRS)],
        [back_mixed[part_of(j)] for j in range(PAIRS)],
        self_chance,
    )
    dz_s[:, LANES:] = jnp.concatenate([x for part in back_parts for x in part], 0)
    put_blocks(0, mul_t(h0, dz_s[:WIDTH, LANES : 2 * LANES]) * HEAD_DIM**-0.5)
    put_blocks(3, mul_t(h0, dz_s[WIDTH:, LANES : 2 * LANES]))
    more, gain_grad = norm_back(
        y0, inverse0, gain(3, LANES), mul(wn_s[1, :, : 3 * WIDTH], dz_s[:, LANES : 2 * LANES])
    )
    ggain_s[3] = gain_grad
    back = back + more
    spread = mul_t(start, split_low(back))
    ge_s[:CODES, :] = table_grad + spread[:, :D] + spread[:, D:]
    ge_s[CODES:, :] = jnp.zeros((n, D), f32)
    rows_s[...] = jnp.zeros_like(rows_s)
    for head in range(HEADS):
        lanes = slice(head * LANES, (head + 1) * LANES)
        for b in range(LEVELS):
            hit = jnp.where(offset == b, self_scores[:, lanes], 0.0)
            rows_s[head, BUCKETS + b : BUCKETS + b + 1, :] = jnp.sum(hit, axis=0, keepdims=True)

    def reducing(buffer, kept, held, upto):
        steps, at = [], 0
        for k, stage in enumerate(order[:upto]):
            rows, left = held[k], held[k + 1]
            side = side_of(stage)
            if left < rows:
                source = buffer.at[span(at + (1 - side) * left, left)]
                at = at + side * left
            else:
                source = buffer.at[span(at, rows)]
            steps.append((remote(source, kept[k], stage), at, left))
        return steps, at, held

    def begin(steps, k):
        steps[k][0].start()

    def finish(steps, buffer, kept, k):
        copy, at, left = steps[k]
        copy.wait()
        place = span(at, left)
        total = buffer[place, :].astype(f32) + kept[k][...].astype(f32)
        buffer[place, :] = total.astype(bf16)

    flat_depth = depth - 1
    held_rest, held_first, held_codes = shares(dp, REST), shares(dp, FIRST), shares(dp, CODES, 1)
    land, rest = {}, lands
    for name, number in (
        ("rest0", flat_depth),
        ("rest1", flat_depth),
        ("first1", flat_depth),
        ("first0", len(far)),
        ("codes", len(far)),
    ):
        land[name], rest = rest[:number], rest[number:]
    land_rest, land_first = rest
    rest1 = reducing(rest_s.at[1], land["rest1"], held_rest, flat_depth)
    first1 = reducing(first_s.at[1], land["first1"], held_first, flat_depth)
    rest0 = reducing(rest_s.at[0], land["rest0"], held_rest, flat_depth)
    first0 = reducing(first_s.at[0], land["first0"], held_first, len(far))
    codes = reducing(codes_s, land["codes"], held_codes, len(far))

    def step1(k):
        if k > 0:
            finish(rest1[0], rest_s.at[1], land["rest1"], k - 1)
            finish(first1[0], first_s.at[1], land["first1"], k - 1)
        if k < flat_depth:
            begin(rest1[0], k)
            begin(first1[0], k)

    def crossing(buffer, target, at, rows):
        source = buffer.at[1 - section, span(at, rows)]
        return remote(source, target, across)

    cross_rest = crossing(rest_s, land_rest, rest1[1], rest1[2][-1])
    cross_first = crossing(first_s, land_first, first1[1], first1[2][-1])

    def settle(copy, buffer, landed, at, rows, base):
        copy.wait()
        value = (buffer[section, span(at, rows), :].astype(f32) + landed[...].astype(f32)).astype(
            bf16
        )
        out_ref[span(base + at, rows), :] = value
        value = value.astype(f32)
        return jnp.sum(value * value, axis=0, keepdims=True)

    def gathering(base, at, held):
        steps = []
        for k in reversed(range(flat_depth)):
            rows, left = held[k], held[k + 1]
            if left < rows:
                place = out_ref.at[span(base + at, left)]
                steps.append(remote(place, place, order[k]))
                at = at - side_of(order[k]) * left
            else:
                steps.append(None)
        return steps

    gather_rest = gathering(0, rest1[1], rest1[2])

    def step0(k):
        if k > 0 and k <= flat_depth:
            finish(rest0[0], rest_s.at[0], land["rest0"], k - 1)
        if k < flat_depth:
            begin(rest0[0], k)
        if k == flat_depth:
            cross_rest.start()
        if k == flat_depth + 1:
            squares = settle(cross_rest, rest_s, land_rest, rest1[1], rest1[2][-1], 0)
            own_slot_s[16:17, :] = squares / (dp * rest1[2][-1] // REST)
        if k > flat_depth + 1 and gather_rest[k - flat_depth - 2] is not None:
            gather_rest[k - flat_depth - 2].wait()
        if flat_depth < k < 2 * flat_depth + 1 and gather_rest[k - flat_depth - 1] is not None:
            gather_rest[k - flat_depth - 1].start()

    g0_s[...] = jnp.zeros_like(g0_s)
    gbias_s[...] = jnp.zeros_like(gbias_s)
    for g in range(3):
        ggain_s[g] = jnp.zeros((D, LANES), f32)

    def fold(x):
        return sum(x[:, i * LANES : (i + 1) * LANES] for i in range(COLUMNS))

    def back_rest(c, carry):
        at_chunk(c, step1, 0, 2, flat_depth + 1)
        x2 = get_wide(x2_s, c)
        inverse = inverse_rms(x2)
        back_memory = mem_s[c]
        add_blocks(12, mul_t(norm_low(x2, inverse, gain(2, WIDE)), back_memory))
        back, gain_grad = norm_back(
            x2, inverse, gain(2, WIDE), mul(wn_s[0, :, 4 * WIDTH : 6 * WIDTH], back_memory)
        )
        ggain_s[2] += fold(gain_grad)
        low = back.astype(bf16)
        add_blocks(26, mul_t(low, r_s[c]))
        for j in range(4):
            part = slice(j * FF // 4, (j + 1) * FF // 4)
            back_active = mul(wt_s[0, MIXW + FF + part.start : MIXW + FF + part.stop, :], low)
            live = r_s[c, part, :].astype(f32) > 0
            r_s[c, part, :] = jnp.where(live, back_active, 0.0).astype(bf16)
        at_chunk(c, step1, 1, 2, flat_depth + 1)
        x1 = x1_s[c]
        inverse = inverse_rms(x1)
        add_blocks(18, mul_t(norm_low(x1, inverse, gain(1, WIDE)), r_s[c]))
        more, gain_grad = norm_back(
            x1, inverse, gain(1, WIDE), mul(wn_s[0, :, MIXW : MIXW + FF], r_s[c])
        )
        ggain_s[1] += fold(gain_grad)
        put_wide(x2_s, c, back + more)
        return carry

    lax.fori_loop(0, chunks, back_rest, 0)
    for j in range(2 * chunks, flat_depth + 1):
        step1(j)
    for block in range(REST // D):
        rest_s[0, block * D : (block + 1) * D, :] = g0_s[FIRST // D + block].astype(bf16)

    steps0 = 2 * flat_depth + 2

    def back_first(c, carry):
        at_chunk(c, step0, 0, 3, steps0)
        back = get_wide(x2_s, c)
        lane = iota((D, LANES), 1)
        low = [jnp.where(lane < PACK, part, 0.0).astype(bf16) for part in unpack(back)]
        low = jnp.concatenate(low, 1)
        add_blocks(9, mul_t(low, o_s[c]))
        o_s[c] = mul(wt_s[0, 3 * WIDTH : 4 * WIDTH, :], low).astype(bf16)
        for first in range(0, GROUP, BATCH):
            if first == GROUP // 2:
                at_chunk(c, step0, 1, 3, steps0)
            queries, keys, values, backs = [], [], [], []
            for i in range(first, first + BATCH):
                lanes = slice(i * LANES, (i + 1) * LANES)
                queries += [qkv_s[c, part_of(j), lanes] for j in range(PAIRS)]
                keys += [qkv_s[c, part_of(PAIRS + j), lanes] for j in range(PAIRS)]
                values += [qkv_s[c, part_of(2 * PAIRS + j), lanes].T[:KEYS] for j in range(PAIRS)]
                backs += [o_s[c, part_of(j), lanes] for j in range(PAIRS)]
            chance = [p_s[GROUP * c + first + i] for i in range(BATCH)]
            *results, scores = attend_back(
                keys, queries, values, backs, jnp.concatenate(chance, 1)
            )
            for i in range(BATCH):
                lanes = slice((first + i) * LANES, (first + i + 1) * LANES)
                own = slice(i * PAIRS, (i + 1) * PAIRS)
                dqkv_s[:, lanes] = jnp.concatenate([x for part in results for x in part[own]], 0)
            width = HEADS * LANES
            gbias_s[...] += sum(scores[:, i * width : (i + 1) * width] for i in range(BATCH))
        at_chunk(c, step0, 2, 3, steps0)
        x0 = x0_s[c]
        inverse = inverse_rms(x0)
        add_blocks(0, mul_t(spread_low(x0 * inverse * gain(0, WIDE)), dqkv_s[...]))
        back_normed = packed(mul(wn_s[0, :, : 3 * WIDTH], dqkv_s[...]))
        more, gain_grad = norm_back(x0, inverse, gain(0, WIDE), back_normed)
        ggain_s[0] += fold(gain_grad)
        find(c)
        spread = mul_t(hot_s[...], split_low(back + more))
        ge_s[...] += spread[:, :D] + spread[:, D:]
        return carry

    lax.fori_loop(0, chunks, back_first, 0)

    for block in range(FIRST // D):
        value = g0_s[block]
        if block < 3:
            value = value * HEAD_DIM**-0.5
        first_s[0, block * D : (block + 1) * D, :] = value.astype(bf16)
    codes_s[...] = ge_s[:CODES, :].astype(bf16)
    begin(first0[0], 0)
    begin(codes[0], 0)
    user_low_s[...] = ge_s[CODES:, :].astype(bf16)
    store_users = pltpu.make_async_copy(
        user_low_s, out_user_ref.at[span(slot * n, n)], local_sems.at[BLOCKS + 2]
    )
    store_users.start()
    late = list(range(min(3 * chunks, steps0), steps0))
    if late:
        step0(late.pop(0))

    ones = jnp.ones((8, LANES), f32)
    own_slot_s[8:16, :] = jnp.zeros((8, LANES), f32)
    for g in range(7):
        own_slot_s[g : g + 1, :] = mul_exact_t(ones, ggain_s[g])[:1]
    own_slot_s[7:8, :] = jnp.broadcast_to(loss, (1, LANES))

    def bucket_sums(b, carry):
        for head in range(HEADS):
            lanes = slice(head * LANES, (head + 1) * LANES)
            hit = jnp.where(buckets == b, gbias_s[:, lanes], 0.0)
            rows_s[head, pl.ds(b, 1), :] = jnp.sum(hit, axis=0, keepdims=True)
        return carry

    lax.fori_loop(0, BUCKETS, bucket_sums, 0, unroll=4)
    for head in range(HEADS):
        sums = mul_exact_t(ones, rows_s[head])
        own_slot_s[8 + head : 9 + head, : 2 * BUCKETS] = sums[:1]
    own_slot_s[19:, :] = jnp.zeros((5, LANES), f32)

    for k in range(len(far)):
        finish(first0[0], first_s.at[0], land["first0"], k)
        finish(codes[0], codes_s, land["codes"], k)
        if k + 1 < len(far):
            begin(first0[0], k + 1)
            begin(codes[0], k + 1)

    first_at, first_left = first0[1], held_first[len(far) + 1 :]
    codes_at, codes_left = codes[1], held_codes[len(far) + 1 :]
    size, code_size = first_left[-1], codes_left[-1]
    mine_first = first_at + shift_of(0, first_left)
    mine_codes = codes_at + shift_of(0, codes_left)
    inside, crossing_first, everyone = [], [], []
    for mask in masks:
        source = first_s.at[0, span(first_at + shift_of(mask, first_left), size)]
        copy = remote_to(source, near_first.at[mask], device_of(mask))
        (crossing_first if mask >> (NEAR - 1) else inside).append(copy)
    for mask in masks:
        source = codes_s.at[span(codes_at + shift_of(mask, codes_left), code_size)]
        everyone.append(remote_to(source, near_codes.at[mask], device_of(mask)))
    store_users.wait()
    held = out_user_ref.at[span(slot * n, n)]
    users_out = [remote_to(held, held, device_of(mask)) for mask in masks]

    @pl.when(section == 0)
    def _():
        for copy in inside:
            copy.start()
        cross_first.start()

    @pl.when(section == 1)
    def _():
        for copy in crossing_first:
            copy.start()

    for copy in everyone + users_out:
        copy.start()
    for step in late:
        step0(step)

    def keep_first(value):
        value = value.astype(bf16)
        out_ref[span(REST + mine_first, size), :] = value
        value = value.astype(f32)
        squares = jnp.sum(value * value, axis=0, keepdims=True)
        own_slot_s[17:18, :] = squares / (dp * size // FIRST)

    @pl.when(section == 0)
    def _():
        for copy in inside:
            copy.wait()
        for copy in crossing_first:
            copy.wait_recv()
        cross_first.wait_send()
        value = first_s[0, span(mine_first, size), :].astype(f32)
        for mask in masks:
            value = value + near_first[mask].astype(f32)
        keep_first(value)

    @pl.when(section == 1)
    def _():
        for copy in crossing_first:
            copy.wait_send()
        cross_first.wait_recv()
        value = first_s[1, span(mine_first, size), :].astype(f32)
        keep_first(value + land_first[...].astype(f32))

    for copy in everyone:
        copy.wait()
    value = codes_s[span(mine_codes, code_size), :].astype(f32)
    for mask in masks:
        value = value + near_codes[mask].astype(f32)
    value = value.astype(bf16)
    out_ref[span(COLS + mine_codes, code_size), :] = value
    value = value.astype(f32)
    squares = jnp.sum(value * value, axis=0, keepdims=True)
    own_slot_s[18:19, :] = squares / (2 * dp * code_size // CODES)

    store_slot = pltpu.make_async_copy(
        own_slot_s, out_slot_ref.at[slot], local_sems.at[BLOCKS + 3]
    )
    store_slot.start()

    copies = []
    place = out_ref.at[span(REST + mine_first, size)]
    code_place = out_ref.at[span(COLS + mine_codes, code_size)]
    for mask in masks:
        device = device_of(mask)
        if not mask >> (NEAR - 1):
            copies.append(remote_to(place, place, device))
        copies.append(remote_to(code_place, code_place, device))
    for copy in copies:
        copy.start()
    store_slot.wait()
    held = out_slot_ref.at[slot]
    slots_out = [remote_to(held, held, device_of(mask)) for mask in masks]
    for copy in slots_out:
        copy.start()
    copies += slots_out
    for copy in copies + users_out:
        copy.wait()
    for j, k in enumerate(reversed(range(len(far)))):
        stage = far[k]
        copies = []
        if held_first[k + 1] < held_first[k]:
            place = out_ref.at[span(REST + first_at, held_first[k + 1])]
            copies.append(remote(place, place, stage))
            first_at = first_at - side_of(stage) * held_first[k + 1]
        if held_codes[k + 1] < held_codes[k]:
            place = out_ref.at[span(COLS + codes_at, held_codes[k + 1])]
            copies.append(remote(place, place, stage))
            codes_at = codes_at - side_of(stage) * held_codes[k + 1]
        slots = 2 ** (NEAR + j)
        first_slot = lax.div(slot, slots) * slots
        held = out_slot_ref.at[pl.ds(first_slot, slots)]
        copies.append(remote(held, held, stage))
        held = out_user_ref.at[span(first_slot * n, slots * n)]
        copies.append(remote(held, held, stage))
        for copy in copies:
            copy.start()
        for copy in copies:
            copy.wait()


def gradients(codes, users, targets, domains, bias, gains, mixer, feed, embedding, dp):
    n = users.shape[0] // 2
    chunks = n // GROUP
    order = stages(dp)
    depth = len(order)
    devices = 2 * dp
    vmem = pl.BlockSpec(memory_space=pltpu.VMEM)
    smem = pl.BlockSpec(memory_space=pltpu.SMEM)
    hbm = pl.BlockSpec(memory_space=pl.ANY)
    stat = (16, LANES)
    held_rest, held_first, held_codes = shares(dp, REST), shares(dp, FIRST), shares(dp, CODES, 1)
    plane, far = depth - 1, depth - NEAR
    sizes = [*held_rest[1:] * 2, *held_first[1:]]
    sizes += [*held_first[1 : far + 1], *held_codes[1 : far + 1], held_rest[-1], held_first[-1]]
    lands = [pltpu.VMEM((rows, D), bf16) for rows in sizes]
    copies = 128 + 16 * depth
    return pl.pallas_call(
        functools.partial(step_kernel, n, dp),
        out_shape=(
            jax.ShapeDtypeStruct((COLS + CODES, D), bf16),
            jax.ShapeDtypeStruct((devices * n, D), bf16),
            jax.ShapeDtypeStruct((devices, 8, LANES), jnp.int32),
            jax.ShapeDtypeStruct((devices, 24, LANES), f32),
            jax.ShapeDtypeStruct((8, LANES), f32),
        ),
        in_specs=[vmem, smem, vmem, vmem, vmem, smem, vmem, hbm, hbm, hbm],
        out_specs=(vmem, hbm, hbm, hbm, vmem),
        scratch_shapes=[
            pltpu.VMEM((chunks, D, WIDE), f32),
            pltpu.VMEM((chunks, D, WIDE), f32),
            pltpu.VMEM((chunks * COLUMNS * D, LANES), f32),
            pltpu.VMEM((chunks, 3 * WIDTH, SPAN), bf16),
            pltpu.VMEM((n, KEYS, HEADS * LANES), bf16),
            pltpu.VMEM((chunks, WIDTH, SPAN), bf16),
            pltpu.VMEM((chunks, FF, WIDE), bf16),
            pltpu.VMEM((chunks, 2 * WIDTH, WIDE), bf16),
            pltpu.VMEM((3 * WIDTH, 2 * LANES), bf16),
            pltpu.VMEM((2, D, COLS), bf16),
            pltpu.VMEM((2, COLS, D), bf16),
            pltpu.VMEM((2 * D, CODES + n), bf16),
            pltpu.VMEM((7, D, LANES), f32),
            pltpu.VMEM((KEYS, HEADS * LANES), f32),
            pltpu.VMEM((LANES, HEADS * LANES), f32),
            pltpu.VMEM((BLOCKS, D, LANES), f32),
            pltpu.VMEM((CODES + n, D), f32),
            pltpu.VMEM((KEYS, HEADS * LANES), f32),
            pltpu.VMEM((7, D, LANES), f32),
            pltpu.VMEM((HEADS, 2 * BUCKETS, LANES), f32),
            pltpu.VMEM((n, D), f32),
            pltpu.VMEM((n, LANES), jnp.int32),
            pltpu.VMEM((WIDTH, LANES), bf16),
            pltpu.VMEM((WIDTH, LANES), bf16),
            pltpu.VMEM((chunks, 32 * GROUP, LANES), f32),
            pltpu.VMEM((chunks, WIDTH, 32 * GROUP), bf16),
            pltpu.VMEM((2, REST, D), bf16),
            pltpu.VMEM((2, FIRST, D), bf16),
            pltpu.VMEM((CODES, D), bf16),
            pltpu.VMEM((8, LANES), jnp.int32),
            pltpu.VMEM((n, D), bf16),
            pltpu.VMEM((24, LANES), f32),
            pltpu.VMEM((8, WIDE), jnp.int32),
            pltpu.VMEM((CODES + n, WIDE), bf16),
            pltpu.VMEM((3 * WIDTH, SPAN), bf16),
            pltpu.VMEM((depth + 1,) + stat, f32),
            pltpu.VMEM((depth,) + stat, f32),
            pltpu.VMEM((2**NEAR, held_first[-1], D), bf16),
            pltpu.VMEM((2**NEAR, held_codes[-1], D), bf16),
            pltpu.SemaphoreType.DMA((BLOCKS + 4,)),
            pltpu.SemaphoreType.DMA((copies,)),
            pltpu.SemaphoreType.DMA((copies,)),
        ]
        + lands,
        compiler_params=pltpu.CompilerParams(
            collective_id=0, has_side_effects=True, vmem_limit_bytes=63 * 2**20
        ),
        name="gradients",
    )(codes, users, users.reshape(1, -1), targets, domains, bias, gains, mixer, feed, embedding)


def adam(weight, moment, square, slope, rate, decay):
    moment = beta_one * moment + (1 - beta_one) * slope
    square = beta_two * square + (1 - beta_two) * slope * slope
    unbiased_moment = moment * (1 / (1 - beta_one**STEP))
    unbiased_square = square * (1 / (1 - beta_two**STEP))
    root = unbiased_square * lax.rsqrt(unbiased_square)
    divisor = root + adam_eps
    inverse = pl.reciprocal(divisor, approx=True)
    inverse = inverse * (2.0 - divisor * inverse)
    step = unbiased_moment * inverse + decay * weight
    return weight - rate * step, moment, square


def update_kernel(*refs):
    parts_in, big_in, small_in, refs = refs[:5], refs[5:14], refs[14:20], refs[20:]
    loss_ref, norm_ref, section_ref, hist_ref = refs[:4]
    big_out, small_out, low_out, refs = refs[4:13], refs[13:19], refs[19:22], refs[22:]
    parts, hold, low_hold = refs[:5], refs[5:14], refs[14:17]
    user_grad, part_sems, in_sems, out_sems = refs[17:]
    grad_ref, user_ref, ids_ref, slot_ref, stat_ref = parts
    arrivals = [pltpu.make_async_copy(parts_in[i], parts[i], part_sems.at[i]) for i in range(5)]
    loads = [pltpu.make_async_copy(big_in[i], hold[i], in_sems.at[i]) for i in range(9)]
    for load in arrivals[1:] + arrivals[:1] + loads:
        load.start()
    for arrival in arrivals:
        arrival.wait()

    users = user_grad.shape[0]
    span = min(1024, user_ref.shape[0])
    slots = span // LANES * (ids_ref.shape[0] * LANES // user_ref.shape[0])
    fit = ids_ref.shape[0] * LANES // user_ref.shape[0]
    user_grad[...] = jnp.zeros_like(user_grad)

    def scatter(part, carry):
        rows = user_ref[pl.ds(pl.multiple_of(part * span, span), span), :]
        lanes = []
        for group in range(span // LANES):
            total = ids_ref[part * slots + group * fit, :1, :]
            for other in range(1, fit):
                total = total + ids_ref[part * slots + group * fit + other, :1, :]
            lanes.append(total)
        ids = jnp.concatenate(lanes, 1)
        for block in range(users // USER_ROWS):
            place = slice(block * USER_ROWS, (block + 1) * USER_ROWS)
            hit = iota((USER_ROWS, span), 0) + block * USER_ROWS == ids
            user_grad[place, :] += mul(jnp.where(hit, 1.0, 0.0).astype(bf16), rows)
        return carry

    lax.fori_loop(0, user_ref.shape[0] // span, scatter, 0)

    def total(x):
        return jnp.sum(jnp.sum(x, axis=0, keepdims=True), axis=1, keepdims=True)

    def slot_sum(first):
        def add(i, value):
            return value + slot_ref[2 * i + first]

        zero = jnp.zeros(slot_ref.shape[1:], f32)
        return lax.fori_loop(0, slot_ref.shape[0] // 2, add, zero)

    even, odd = slot_sum(0), slot_sum(1)
    section_squares = [total(x[16:17] + x[17:18]) for x in (even, odd)]
    small = even[:16] + odd[:16]
    rest = total(even[18:19] + odd[18:19])
    user_values = user_grad[...]
    rest = rest + total(user_values * user_values)
    lane, line = iota(small.shape, 1), iota(small.shape, 0)
    counted = (line < 7) | ((line > 7) & (lane < 2 * BUCKETS))
    small_kept = jnp.where(counted, small, 0.0)
    rest = rest + total(small_kept * small_kept)
    norm = jnp.sqrt(section_squares[0] + section_squares[1] + rest)
    factor = jnp.minimum(1.0, clip_norm / (norm + 1e-06))
    loss_ref[0] = small[7, 0]
    norm_ref[0] = norm[0, 0]
    for s in range(2):
        section_ref[s] = jnp.sqrt(section_squares[s])[0, 0]
    for row in range(8):
        lanes = slice((row % 2) * LANES, (row % 2 + 1) * LANES)
        hist_ref[row // 2 : row // 2 + 1, lanes] = stat_ref[row : row + 1, :]

    outs = adam(
        small_in[0][...], small_in[1][...], small_in[2][...], factor * small[:7], rate_gain, 0.0
    )
    for ref, value in zip(small_out[:3], outs):
        ref[...] = value
    for head in range(HEADS):
        for s in range(2):
            slope = factor * small[8 + head : 9 + head, s * BUCKETS : (s + 1) * BUCKETS]
            one = slice(s, s + 1)
            outs = adam(
                small_in[3][head, one, :],
                small_in[4][head, one, :],
                small_in[5][head, one, :],
                slope,
                rate_small,
                0.0,
            )
            for ref, value in zip(small_out[3:], outs):
                ref[head, one, :] = value

    stores = []

    def store(kind, place):
        first = 3 * kind
        pieces = [(hold[first + i], big_out[first + i]) for i in range(3)]
        pieces.append((low_hold[kind], low_out[kind]))
        for source, target in pieces:
            copy = pltpu.make_async_copy(
                source.at[place], target.at[place], out_sems.at[len(stores)]
            )
            copy.start()
            stores.append(copy)

    def step(kind, place, slope):
        first = 3 * kind
        outs = adam(
            hold[first][place],
            hold[first + 1][place],
            hold[first + 2][place],
            factor * slope,
            rate_matrix,
            decay_matrix,
        )
        for i in range(3):
            hold[first + i][place] = outs[i]
        low_hold[kind][place] = outs[0].astype(bf16)

    def block_of(block):
        first = FIRST // D
        place = block - first if block >= first else REST // D + block
        return grad_ref[place * D : (place + 1) * D, :].astype(f32)

    for i in range(3):
        loads[i].wait()
    for part in range(6):
        for block in range(3 * part, 3 * part + 3):
            lanes = slice(block * LANES, (block + 1) * LANES)
            step(0, (0, slice(None), lanes), block_of(block))
        store(0, (0, slice(None), slice(3 * part * LANES, 3 * (part + 1) * LANES)))
    for i in range(3, 6):
        loads[i].wait()
    for part in range(4):
        for block in range(4 * part, 4 * part + 4):
            lanes = slice(block * LANES, (block + 1) * LANES)
            step(1, (0, slice(None), lanes), block_of(MIXW // LANES + block))
        store(1, (0, slice(None), slice(4 * part * LANES, 4 * (part + 1) * LANES)))
    for i in range(6, 9):
        loads[i].wait()
    for part in range(4):
        rows = slice(part * CODEBOOK, (part + 1) * CODEBOOK)
        step(2, (rows, slice(None)), grad_ref[COLS + rows.start : COLS + rows.stop, :].astype(f32))
        store(2, (rows, slice(None)))
    for part in range(users // USER_ROWS):
        rows = slice(part * USER_ROWS, (part + 1) * USER_ROWS)
        place = (slice(CODES + part * USER_ROWS, CODES + (part + 1) * USER_ROWS), slice(None))
        step(2, place, user_grad[rows, :])
        store(2, place)
    for copy in stores:
        copy.wait()


def update(reduced, mixers, feeds, embeds, gains, biases):
    vmem = pl.BlockSpec(memory_space=pltpu.VMEM)
    smem = pl.BlockSpec(memory_space=pltpu.SMEM)
    hbm = pl.BlockSpec(memory_space=pl.ANY)
    big = [*mixers, *feeds, *embeds]
    small = [*gains, *biases]
    low = [jax.ShapeDtypeStruct(x[0].shape, bf16) for x in (mixers, feeds, embeds)]
    users = embeds[0].shape[0] - CODES
    pieces = 4 * (6 + 4 + 4 + users // USER_ROWS)
    return pl.pallas_call(
        update_kernel,
        out_shape=[
            jax.ShapeDtypeStruct((1,), f32),
            jax.ShapeDtypeStruct((1,), f32),
            jax.ShapeDtypeStruct((2,), f32),
            jax.ShapeDtypeStruct((LEVELS, CODEBOOK), f32),
        ]
        + [jax.ShapeDtypeStruct(x.shape, f32) for x in big + small]
        + low,
        in_specs=[hbm] * 14 + [vmem] * 6,
        out_specs=[smem] * 3 + [vmem] + [hbm] * 9 + [vmem] * 6 + [hbm] * 3,
        scratch_shapes=[pltpu.VMEM(x.shape, x.dtype) for x in reduced]
        + [pltpu.VMEM(x.shape, f32) for x in big]
        + [pltpu.VMEM(x.shape, bf16) for x in low]
        + [
            pltpu.VMEM((users, D), f32),
            pltpu.SemaphoreType.DMA((5,)),
            pltpu.SemaphoreType.DMA((9,)),
            pltpu.SemaphoreType.DMA((pieces,)),
        ],
        compiler_params=pltpu.CompilerParams(vmem_limit_bytes=62 * 2**20),
        name="update",
    )(*reduced, *big, *small)


def shards(
    history_codes,
    user_ids,
    targets,
    domains,
    mixer,
    mixer_moment,
    mixer_square,
    feed,
    feed_moment,
    feed_square,
    embedding,
    embedding_moment,
    embedding_square,
    gains,
    gains_moment,
    gains_square,
    position_bias,
    bias_moment,
    bias_square,
):
    def turned(table):
        return jnp.transpose(table, (2, 0, 1))

    biases = [turned(x) for x in (position_bias, bias_moment, bias_square)]
    reduced = gradients(
        history_codes,
        user_ids,
        targets.T,
        domains.reshape(1, -1),
        biases[0],
        gains,
        mixer,
        feed,
        embedding,
        lax.axis_size("dp"),
    )
    outs = update(
        reduced,
        (mixer, mixer_moment, mixer_square),
        (feed, feed_moment, feed_square),
        (embedding, embedding_moment, embedding_square),
        (gains, gains_moment, gains_square),
        biases,
    )
    loss, norm, sections, histograms = outs[:4]
    back = [jnp.transpose(x, (1, 2, 0)) for x in outs[16:19]]
    return (
        loss.reshape(()),
        norm.reshape(()),
        sections,
        histograms,
        *outs[4:16],
        *back,
        *outs[19:],
    )


def solution(mesh):
    by_dp, by_pipe, copied = P("dp"), P("pipe"), P()
    return jax.shard_map(
        shards,
        mesh=mesh,
        in_specs=(by_dp,) * 4 + (by_pipe,) * 6 + (copied,) * 9,
        out_specs=(copied,) * 4 + (by_pipe,) * 6 + (copied,) * 9 + (by_pipe,) * 2 + (copied,),
        check_vma=False,
    )
```

```python
import functools

import jax
import jax.numpy as jnp
from jax import lax
from jax.experimental import pallas as pl
from jax.experimental.pallas import tpu as pltpu
from jax.sharding import PartitionSpec as P

D = 128
HEADS = 6
HEAD_DIM = 64
FF = 1024
CODEBOOK = 256
LEVELS = 4
BUCKETS = 32
DOMAINS = 3
HIST_LEN = 81
STEP = 5
CODES = 1024
LANES = 128
WIDTH = HEADS * HEAD_DIM
MIXW = 6 * WIDTH
COLS = MIXW + 2 * FF
BLOCKS = COLS // LANES
KEYS = 96
GROUP = 8
BATCH = 2
NEAR = 3
PACK = 96
WIDE = GROUP * PACK
SPAN = GROUP * LANES
COLUMNS = WIDE // LANES
PAIRS = HEADS // 2
FIRST = 4 * WIDTH
REST = COLS - FIRST
USER_ROWS = 400
MESH = pl.DeviceIdType.MESH

norm_eps = 1e-06
beta_one = 0.9
beta_two = 0.999
adam_eps = 1e-08
clip_norm = 0.5
rate_matrix = 0.04
rate_gain = 0.8
rate_small = 0.3
decay_matrix = 0.01

f32 = jnp.float32
bf16 = jnp.bfloat16


def iota(shape, axis):
    return lax.broadcasted_iota(jnp.int32, shape, axis)


def mul(left, right):
    return jnp.dot(left, right, preferred_element_type=f32)


def mul_t(left, right):
    return lax.dot_general(left, right, (((1,), (1,)), ((), ())), preferred_element_type=f32)


def mul_exact(left, right):
    return jnp.dot(left, right, preferred_element_type=f32, precision=lax.Precision.HIGHEST)


def mul_exact_t(left, right):
    return lax.dot_general(
        left,
        right,
        (((1,), (1,)), ((), ())),
        preferred_element_type=f32,
        precision=lax.Precision.HIGHEST,
    )


def onehot(ids, rows):
    return jnp.where(iota((rows, ids.shape[1]), 0) == ids, 1.0, 0.0).astype(bf16)


def inverse_rms(x):
    return lax.rsqrt(jnp.mean(x * x, axis=0, keepdims=True) + norm_eps)


def norm_low(x, inverse, gain):
    return (x * inverse * gain).astype(bf16)


def norm_back(x, inverse, gain, upstream):
    scaled = x * inverse
    inner = upstream * gain
    back = inverse * (inner - scaled * jnp.mean(inner * scaled, axis=0, keepdims=True))
    return back, upstream * scaled


def block_diag(pair):
    zero = jnp.zeros((HEAD_DIM, LANES), pair.dtype)
    left = jnp.concatenate([pair[:HEAD_DIM], zero], 0)
    right = jnp.concatenate([zero, pair[HEAD_DIM:]], 0)
    return jnp.concatenate([left, right], 1)


def diagonal(both):
    return jnp.concatenate([both[:HEAD_DIM, :LANES], both[HEAD_DIM:, LANES:]], 0)


def turn(x, shift):
    return x if shift % LANES == 0 else pltpu.roll(x, shift % LANES, 1)


def pack(tables):
    lane = iota(tables[0].shape, 1)
    columns = []
    for first in range(0, len(tables), 4):
        turned = [turn(tables[first + i], PACK * i) for i in range(4)]
        for i in range(3):
            columns.append(jnp.where(lane < PACK - 32 * i, turned[i], turned[i + 1]))
    return jnp.concatenate(columns, 1)


def unpack(x):
    lane = iota((x.shape[0], LANES), 1)
    tables = []
    for first in range(0, x.shape[1] // LANES, 3):
        a, b, c = [x[:, (first + i) * LANES : (first + i + 1) * LANES] for i in range(3)]
        tables.append(a)
        tables.append(jnp.where(lane < 32, turn(a, 32), turn(b, 32)))
        tables.append(jnp.where(lane < 64, turn(b, 64), turn(c, 64)))
        tables.append(turn(c, 96))
    return tables


def stack(both):
    return jnp.concatenate([both[:, :LANES], both[:, LANES:]], 0)


def pad_keys(table):
    if table.shape[0] == LANES:
        return table
    zero = jnp.zeros((LANES - table.shape[0], table.shape[1]), table.dtype)
    return jnp.concatenate([table, zero], 0)


def columns_of(table, i):
    return table[:, 2 * i * LANES : 2 * (i + 1) * LANES]


def attend(keys, queries, values, bias):
    scores = [mul(key, block_diag(query)) for key, query in zip(keys, queries)]
    scores = jnp.concatenate(scores, 1) + bias
    top = jnp.max(scores, axis=0, keepdims=True)
    chance = jnp.exp(scores - top)
    total = jnp.sum(chance, axis=0, keepdims=True)
    chance = (chance * (1.0 / total)).astype(bf16)
    full = pad_keys(chance)
    mixed = [mul(value, columns_of(full, i)) for i, value in enumerate(values)]
    return chance, [diagonal(both).astype(bf16) for both in mixed]


def attend_back(keys_t, queries, values, back_mixed, chance):
    exact = chance.astype(f32)
    back_chance = [mul(value, block_diag(back)) for value, back in zip(values, back_mixed)]
    back_chance = jnp.concatenate(back_chance, 1)
    inner = jnp.sum(back_chance * exact, axis=0, keepdims=True)
    back_scores = exact * (back_chance - inner)
    low = pad_keys(back_scores.astype(bf16))
    full = pad_keys(chance)
    count = range(len(queries))
    back_query = [mul(keys_t[i], columns_of(low, i)) for i in count]
    back_keys = [mul_t(queries[i], stack(columns_of(low, i))) for i in count]
    back_values = [mul_t(back_mixed[i], stack(columns_of(full, i))) for i in count]
    results = [
        [diagonal(both).astype(bf16) for both in part]
        for part in (back_query, back_keys, back_values)
    ]
    return *results, back_scores


def split_low(x):
    high = x.astype(bf16)
    return jnp.concatenate([high, (x - high.astype(f32)).astype(bf16)], 0)


def stages(dp):
    bits = [2**k for k in range(dp.bit_length() - 1)]
    return [("dp", bit) for bit in bits[:2] + bits[4:] + bits[2:4]] + [("pipe", 1)]


def side_of(stage):
    axis, bit = stage
    return lax.rem(lax.div(lax.axis_index(axis), bit), 2)


def partner_of(stage):
    axis, bit = stage
    return {axis: lax.axis_index(axis) + bit * (1 - 2 * side_of(stage))}


def shares(dp, rows, across=0):
    held = [rows]
    depth = len(stages(dp)) - 1
    for k in range(depth + across):
        later = min(NEAR - 1, depth - 1 - k) + across if k < depth else 0
        half = held[-1] // 2
        held.append(half if half % (16 * 2**later) == 0 else held[-1])
    return held


def span(start, size):
    return pl.ds(pl.multiple_of(start, 16), size)


def step_kernel(n, dp, *refs):
    codes_ref, users_ref, user_row_ref, targets_ref, domains_ref, bias_ref, gains_ref = refs[:7]
    mixer_ref, feed_ref, embed_ref = refs[7:10]
    out_ref, out_user_ref, out_ids_ref, out_slot_ref, out_stat_ref = refs[10:15]
    x0_s, x1_s, x2_s, qkv_s, p_s, o_s, r_s, mem_s, dz_s, wn_s, wt_s, ext_s = refs[15:27]
    gain_s, ebias_s, dbias_s, g0_s, ge_s, gbias_s, ggain_s, rows_s, user_s, ids_s = refs[27:37]
    cross_s, cross_back_s, pc_s, oc_s, rest_s, first_s, codes_s, slot_s, user_low_s, own_slot_s, id_rows_s, hot_s, dqkv_s = refs[37:50]
    stat_s, stat_land, near_first, near_codes, local_sems, sends, recvs = refs[50:57]
    lands = refs[57:]
    order = stages(dp)
    across = order[-1]
    depth = len(order)
    chunks = n // GROUP
    section = lax.axis_index("pipe")
    used = [0]

    def remote_to(source, target, device):
        index = used[0]
        used[0] += 1
        return pltpu.make_async_remote_copy(
            src_ref=source,
            dst_ref=target,
            send_sem=sends.at[index],
            recv_sem=recvs.at[index],
            device_id=device,
            device_id_type=MESH,
        )

    def remote(source, target, stage):
        return remote_to(source, target, partner_of(stage))

    near, far = order[-NEAR:], order[:-NEAR]
    masks = range(1, 2 ** len(near))

    def device_of(mask):
        place = {"dp": lax.axis_index("dp"), "pipe": lax.axis_index("pipe")}
        for i, (axis, bit) in enumerate(near):
            if mask >> i & 1:
                place[axis] = place[axis] + bit * (1 - 2 * side_of((axis, bit)))
        return place

    def shift_of(mask, lefts):
        total = 0
        for i, left in enumerate(lefts):
            side = side_of(near[i])
            total = total + (1 - side if mask >> i & 1 else side) * left
        return total

    locals_in = []
    for block in range(BLOCKS):
        lanes = slice(block * LANES, (block + 1) * LANES)
        if block < MIXW // LANES:
            source = mixer_ref.at[0, :, lanes]
        else:
            source = feed_ref.at[0, :, slice(lanes.start - MIXW, lanes.stop - MIXW)]
        locals_in.append(pltpu.make_async_copy(source, g0_s.at[block], local_sems.at[block]))
    vocabulary = embed_ref.shape[0]
    flat = x2_s.at[pl.ds(0, vocabulary)]
    load_embed = pltpu.make_async_copy(embed_ref, flat, local_sems.at[BLOCKS])
    for copy in locals_in:
        copy.start()
    load_embed.start()

    barrier = pltpu.get_barrier_semaphore()
    for stage in far:
        pl.semaphore_signal(barrier, inc=1, device_id=partner_of(stage), device_id_type=MESH)
    for mask in masks:
        pl.semaphore_signal(barrier, inc=1, device_id=device_of(mask), device_id_type=MESH)

    scale = HEAD_DIM**-0.5
    cross_scale = jnp.where(section == 1, scale, 1.0).astype(f32)
    for copy in locals_in:
        copy.wait()
    for block in range(BLOCKS):
        value = g0_s[block]
        if block < 3:
            value = value * scale
        elif 12 <= block < 15:
            value = value * cross_scale
        wn_s[section, :, block * LANES : (block + 1) * LANES] = value.astype(bf16)
    pl.semaphore_wait(barrier, len(far) + len(masks))
    half = D // 2
    mine = span(side_of(order[0]) * half, half)
    pieces = (slice(0, FIRST), slice(FIRST, COLS))
    over = [
        remote(wn_s.at[section, mine, piece], wn_s.at[section, mine, piece], across)
        for piece in pieces
    ]
    for copy in over:
        copy.start()

    ids_s[:, : HIST_LEN - 1] = codes_ref[pl.ds(pl.multiple_of(section * n, 8), n), :]
    lane, row = iota((n, LANES), 1), iota((n, LANES), 0)
    ids = ids_s[...] + ((lane & 3) << 8)
    ids = jnp.where(lane < HIST_LEN - 1, ids, jnp.where(lane == HIST_LEN - 1, CODES + row, -1))
    ids_s[...] = ids
    packed = []
    for i in range(GROUP):
        rows = [ids_s[c * GROUP + i : c * GROUP + i + 1, :] for c in range(chunks)]
        rows += [jnp.zeros((8 - chunks, LANES), jnp.int32)]
        packed.append(jnp.concatenate(rows, 0))
    id_rows_s[...] = pack(packed)
    count = targets_ref.shape[1]
    history, token = iota((count, LANES), 0), iota((count, LANES), 1)
    pick = jnp.where((token >> 2) + section * n == history, 1.0, 0.0)
    level, place = iota((LEVELS, LANES), 0), iota((LEVELS, LANES), 1) & 3
    target = mul(targets_ref[...].astype(f32), pick) + (level * CODEBOOK).astype(f32)
    goal = jnp.sum(jnp.where(level == place, target, 0.0), axis=0, keepdims=True).astype(jnp.int32)
    start_ids = jnp.sum(
        jnp.where(level == place - 1, target, 0.0), axis=0, keepdims=True
    ).astype(jnp.int32)
    domain = mul(domains_ref[...].astype(f32), pick)
    pick = jnp.where(lax.rem(token, n) + section * n == history, 1.0, 0.0)
    own_users = mul_exact(user_row_ref[...].astype(f32), pick)

    counts = [
        jnp.sum(jnp.where(domain == d, 1.0, 0.0), axis=1, keepdims=True) for d in range(DOMAINS)
    ]
    counts += [jnp.zeros((1, 1), f32)] * (8 - DOMAINS)
    stat_s[0, 8:, :] = jnp.broadcast_to(jnp.concatenate(counts, 0), (8, LANES))
    histogram = mul_t(jnp.ones((8, LANES), bf16), onehot(goal, CODES))
    for r in range(8):
        stat_s[0, r : r + 1, :] = histogram[:1, r * LANES : (r + 1) * LANES]
    slot = 0
    for k, stage in enumerate(order):
        slot = slot + side_of(stage) * 2 ** (depth - 1 - k)
    owner = iota((8, LANES), 1) // n
    own_users = jnp.broadcast_to(own_users, (8, LANES)).astype(jnp.int32)
    slot_s[...] = jnp.where(owner == lax.rem(slot, LANES // n), own_users, 0)
    store_ids = pltpu.make_async_copy(slot_s, out_ids_ref.at[slot], local_sems.at[BLOCKS + 1])
    store_ids.start()
    store_ids.wait()

    def slots_of(j):
        return pl.ds(lax.div(slot, 2**j) * 2**j, 2**j)

    early = []
    for j, stage in enumerate(reversed(order)):
        held = out_ids_ref.at[slots_of(j)]
        early.append(
            (
                remote(stat_s.at[j], stat_land.at[j], stage),
                remote(held, held, stage),
            )
        )

    def early_step(j):
        if j > 0:
            for copy in early[j - 1]:
                copy.wait()
            stat_s[j] = stat_s[j - 1] + stat_land[j - 1]
        if j < depth:
            for copy in early[j]:
                copy.start()

    eye = jnp.where(iota((LANES, LANES), 0) == iota((LANES, LANES), 1), 1.0, 0.0).astype(bf16)
    load_embed.wait()

    def fetch(i, carry):
        user_s[pl.ds(i, 1), :] = x2_s[pl.ds(CODES + users_ref[section * n + i], 1), :]
        return carry

    lax.fori_loop(0, n, fetch, 0, unroll=8)
    for block in range(CODES // LANES + 1):
        if block < CODES // LANES:
            rows = x2_s[block * LANES : (block + 1) * LANES, :]
            codes_s[block * LANES : (block + 1) * LANES, :] = rows.astype(bf16)
            width = LANES
        else:
            rows = user_s[...]
            width = n
        high = rows.astype(bf16)
        low = (rows - high.astype(f32)).astype(bf16)
        lanes = slice(block * LANES, block * LANES + width)
        ext_s[:D, lanes] = mul_t(eye, high).astype(bf16)
        ext_s[D:, lanes] = mul_t(eye, low).astype(bf16)

    def find(c):
        ids = id_rows_s[pl.ds(c, 1), :]
        for first in range(0, CODES + n, LANES):
            rows = min(LANES, CODES + n - first)
            hot_s[first : first + rows, :] = onehot(ids - first, rows)

    def lookup(c, carry):
        find(c)
        both = mul(ext_s[...], hot_s[...])
        x0_s[c] = both[:D] + both[D:]
        return carry

    lax.fori_loop(0, chunks, lookup, 0)

    beside = []
    for piece in pieces:
        came = wn_s.at[1 - section, mine, piece]
        beside.append(remote(came, came, order[0]))
    over[0].wait()
    beside[0].start()

    for g in range(7):
        gain_s[g] = jnp.broadcast_to(gains_ref[g : g + 1, :], (LANES, LANES)).T

    def positions(axis):
        index = iota((KEYS, LANES), axis)
        return jnp.where(index == HIST_LEN - 1, 0, index + 1)

    key, query = positions(0), positions(1)
    distance = jnp.abs(query - key)
    remoteness = jnp.zeros_like(distance)
    for edge in (12, 16, 23, 32, 46, 64, 91):
        remoteness = remoteness + (distance >= edge).astype(jnp.int32)
    nearby = jnp.minimum(jnp.where(distance < 8, distance, 8 + remoteness), 15)
    buckets = nearby + jnp.where(key > query, 16, 0)
    real = iota((KEYS, LANES), 0) < HIST_LEN
    for head in range(HEADS):
        lanes = slice(head * LANES, (head + 1) * LANES)

        def choose(b, table):
            return jnp.where(buckets == b, bias_ref[head, 0, b], table)

        table = lax.fori_loop(0, BUCKETS, choose, jnp.zeros((KEYS, LANES), f32), unroll=True)
        ebias_s[:, lanes] = jnp.where(real, table, -1e30)
    key, query = iota((LANES, LANES), 0), iota((LANES, LANES), 1)
    offset = query - key
    seen = ((key >> 2) == (query >> 2)) & (offset >= 0)
    for head in range(HEADS):
        lanes = slice(head * LANES, (head + 1) * LANES)
        table = jnp.full((LANES, LANES), -1e30, f32)
        for b in range(LEVELS):
            table = jnp.where(seen & (offset == b), bias_ref[head, 1, b], table)
        dbias_s[:, lanes] = table

    def transpose_weights(which, first, last):
        for block in range(first, last):
            place = slice(block * LANES, (block + 1) * LANES)
            wt_s[which, place, :] = wn_s[which, :, place].T

    transpose_weights(section, 0, BLOCKS)
    beside[0].wait()
    transpose_weights(1 - section, 0, FIRST // LANES)

    def rest_arrives():
        over[1].wait()
        beside[1].start()
        beside[1].wait()
        transpose_weights(1 - section, FIRST // LANES, BLOCKS)

    def gain(g, width):
        column = gain_s[g]
        return column if width == LANES else jnp.concatenate([column] * (width // LANES), 1)

    def at_chunk(c, step, point, points, count):
        for j in range(point, count, points):
            pl.when(c == j // points)(functools.partial(step, j))

    def spread_low(x):
        return jnp.concatenate([part.astype(bf16) for part in unpack(x)], 1)

    def packed(x):
        return pack([x[:, i * LANES : (i + 1) * LANES] for i in range(GROUP)])

    def lanes_of(i):
        return pl.ds(pl.multiple_of(i * LANES, LANES), LANES)

    def part_of(j):
        return slice(j * LANES, (j + 1) * LANES)

    def encode(c, carry):
        at_chunk(c, early_step, 0, 2, depth + 1)
        x0 = x0_s[c]
        h = spread_low(x0 * inverse_rms(x0) * gain(0, WIDE))
        for j in range(3):
            part = slice(j * WIDTH, (j + 1) * WIDTH)
            qkv_s[c, part, :] = mul(wt_s[0, part, :], h).astype(bf16)
        def attention(b, carry):
            queries, keys, values = [], [], []
            for i in range(BATCH):
                lanes = lanes_of(b * BATCH + i)
                queries += [qkv_s[c, part_of(j), lanes] for j in range(PAIRS)]
                keys += [qkv_s[c, part_of(PAIRS + j), lanes].T[:KEYS] for j in range(PAIRS)]
                values += [qkv_s[c, part_of(2 * PAIRS + j), lanes] for j in range(PAIRS)]
            bias = jnp.concatenate([ebias_s[...]] * BATCH, 1)
            chance, mixed = attend(keys, queries, values, bias)
            for i in range(BATCH):
                own = slice(i * HEADS * LANES, (i + 1) * HEADS * LANES)
                p_s[GROUP * c + b * BATCH + i] = chance[:, own]
                both = jnp.concatenate(mixed[i * PAIRS : (i + 1) * PAIRS], 0)
                o_s[c, :, lanes_of(b * BATCH + i)] = both
            return carry

        lax.fori_loop(0, GROUP // BATCH, attention, 0)
        x1 = x0 + packed(mul(wn_s[0, :, 3 * WIDTH : 4 * WIDTH], o_s[c]))
        x1_s[c] = x1
        at_chunk(c, early_step, 1, 2, depth + 1)
        pl.when(c == 0)(rest_arrives)
        h = norm_low(x1, inverse_rms(x1), gain(1, WIDE))
        for j in range(2):
            part = slice(j * FF // 2, (j + 1) * FF // 2)
            lifted = mul(wt_s[0, MIXW + j * FF // 2 : MIXW + (j + 1) * FF // 2, :], h)
            r_s[c, part, :] = jnp.maximum(lifted, 0.0).astype(bf16)
        x2 = x1 + mul(wn_s[0, :, MIXW + FF :], r_s[c])
        put_wide(x2_s, c, x2)
        e = norm_low(x2, inverse_rms(x2), gain(2, WIDE))
        for j in range(2):
            part = slice(j * WIDTH, (j + 1) * WIDTH)
            mem_s[c, part, :] = mul(
                wt_s[0, 4 * WIDTH + j * WIDTH : 4 * WIDTH + (j + 1) * WIDTH, :], e
            ).astype(bf16)
        return carry

    def put_wide(ref, c, value):
        for i in range(COLUMNS):
            ref[pl.ds(pl.multiple_of((COLUMNS * c + i) * D, D), D), :] = value[
                :, i * LANES : (i + 1) * LANES
            ]

    def get_wide(ref, c):
        return jnp.concatenate(
            [ref[pl.ds(pl.multiple_of((COLUMNS * c + i) * D, D), D), :] for i in range(COLUMNS)], 1
        )

    lax.fori_loop(0, chunks, encode, 0)
    for j in range(2 * chunks, depth + 1):
        early_step(j)
    out_stat_ref[...] = stat_s[depth, :8, :]

    def put_blocks(first, value):
        for index in range(value.shape[1] // LANES):
            block = first + index
            part = value[:, index * LANES : (index + 1) * LANES].astype(bf16)
            if block < FIRST // LANES:
                first_s[1, block * D : (block + 1) * D, :] = part
            else:
                block -= FIRST // LANES
                rest_s[1, block * D : (block + 1) * D, :] = part

    def add_blocks(first, value):
        for index in range(value.shape[1] // LANES):
            g0_s[first + index] += value[:, index * LANES : (index + 1) * LANES]

    start = onehot(start_ids, CODES)
    both = mul(ext_s[:, :CODES], start)
    y0 = both[:D] + both[D:]
    inverse0 = inverse_rms(y0)
    h0 = norm_low(y0, inverse0, gain(3, LANES))
    dz_s[:, :LANES] = mul(wt_s[1, : 3 * WIDTH, :], h0).astype(bf16)
    both = mul(mul_t(eye, h0).astype(bf16), wn_s[1, :, WIDTH : 3 * WIDTH]).astype(bf16)
    self_chance, mixed = attend(
        [both[:, part_of(j)] for j in range(PAIRS)],
        [dz_s[part_of(j), :LANES] for j in range(PAIRS)],
        [dz_s[part_of(2 * PAIRS + j), :LANES] for j in range(PAIRS)],
        dbias_s[...],
    )
    self_values = both[:, WIDTH:]
    self_mixed = jnp.concatenate(mixed, 0)
    y1 = y0 + mul(wn_s[1, :, 3 * WIDTH : 4 * WIDTH], self_mixed)
    inverse1 = inverse_rms(y1)
    h1 = norm_low(y1, inverse1, gain(4, LANES))
    cross_s[...] = mul(wt_s[1, 4 * WIDTH : 5 * WIDTH, :], h1).astype(bf16)

    def spreader(g, turned):
        shape = (LANES, 32 * GROUP) if turned else (32 * GROUP, LANES)
        row, token = iota(shape, 1 if turned else 0), iota(shape, 0 if turned else 1)
        hit = token == 4 * GROUP * g + 4 * (row >> 5) + (row & 3)
        return jnp.where(hit, 1.0, 0.0).astype(bf16)

    def rows_of(g, table):
        rows = mul_t(spreader(g, False), table)
        mask = (iota(rows.shape, 1) >> 6) == ((iota(rows.shape, 0) & 31) >> 2)
        return jnp.where(mask, rows, 0.0).astype(bf16)

    def head_mask(shape):
        return (iota(shape, 0) >> 6) == ((iota(shape, 1) & 31) >> 2)

    def rows_t_of(g, table):
        rows = mul(table, spreader(g, True))
        return jnp.where(head_mask(rows.shape), rows, 0.0).astype(bf16)

    def gather_rows(ref):
        total = jnp.zeros((WIDTH, LANES), f32)
        for g in range(chunks):
            total = total + mul(ref[g], spreader(g, False))
        return total.astype(bf16)

    def blocks_of(table):
        rows = []
        for i in range(GROUP):
            part = table[32 * i : 32 * i + 32]
            column, shift = divmod(PACK * i, LANES)
            part = turn(part, shift)
            lane = iota(part.shape, 1)
            zero = jnp.zeros_like(part)
            columns = [zero] * COLUMNS
            columns[column] = jnp.where(lane >= shift, part, 0.0)
            if shift > LANES - PACK:
                columns[column + 1] = jnp.where(lane < shift, part, 0.0)
            rows.append(jnp.concatenate(columns, 1))
        return jnp.concatenate(rows, 0).astype(bf16)

    def row_products(rows, ref, g, first):
        both = mul(rows, ref[g, first : first + WIDTH, :])
        parts = []
        for i in range(GROUP):
            own = both[32 * i : 32 * i + 32]
            column, shift = divmod(PACK * i, LANES)
            part = turn(own[:, column * LANES : (column + 1) * LANES], -shift)
            if shift > LANES - PACK:
                after = turn(own[:, (column + 1) * LANES : (column + 2) * LANES], -shift)
                part = jnp.where(iota(part.shape, 1) < LANES - shift, part, after)
            parts.append(part)
        return jnp.concatenate(parts, 0)

    def cross(g, carry):
        queries = rows_of(g, cross_s[...])
        scores = row_products(queries, mem_s, g, 0)
        scores = jnp.where(iota(scores.shape, 1) < HIST_LEN, scores, -1e30)
        chance = jnp.exp(scores - jnp.max(scores, axis=1, keepdims=True))
        chance = chance * (1.0 / jnp.sum(chance, axis=1, keepdims=True))
        pc_s[g] = chance
        mixed = mul_t(mem_s[g, WIDTH:, :], blocks_of(chance))
        oc_s[g] = jnp.where(head_mask(mixed.shape), mixed, 0.0).astype(bf16)
        return carry

    lax.fori_loop(0, chunks, cross, 0, unroll=True)
    cross_mixed = gather_rows(oc_s)
    y2 = y1 + mul(wn_s[1, :, 5 * WIDTH : 6 * WIDTH], cross_mixed)
    inverse2 = inverse_rms(y2)
    h2 = norm_low(y2, inverse2, gain(5, LANES))
    lifted = mul(wt_s[1, MIXW : MIXW + FF, :], h2)
    active = jnp.maximum(lifted, 0.0).astype(bf16)
    y3 = y2 + mul(wn_s[1, :, MIXW + FF :], active)
    inverse3 = inverse_rms(y3)
    final = norm_low(y3, inverse3, gain(6, LANES))
    logits = mul(codes_s[...], final)
    top = jnp.max(logits, axis=0, keepdims=True)
    log_total = top + jnp.log(jnp.sum(jnp.exp(logits - top), axis=0, keepdims=True))
    match = iota(logits.shape, 0) == goal
    picked = jnp.sum(jnp.where(match, logits, 0.0), axis=0, keepdims=True)
    weight = jnp.zeros((1, LANES), f32)
    for d in range(DOMAINS):
        share = 1.0 / (DOMAINS * jnp.maximum(stat_s[depth, 8 + d : 9 + d, :], 1.0))
        weight = weight + jnp.where(domain == d, share, 0.0)
    loss = jnp.sum(weight * (log_total - picked), axis=1, keepdims=True)
    back_logits = (
        weight * (jnp.exp(logits - log_total) - jnp.where(match, 1.0, 0.0))
    ).astype(bf16)
    back_final = mul(ext_s[:D, :CODES], back_logits)
    table_grad = mul_t(back_logits, final)
    back, gain_grad = norm_back(y3, inverse3, gain(6, LANES), back_final)
    ggain_s[6] = gain_grad
    low = back.astype(bf16)
    put_blocks(26, mul_t(low, active))
    back_lifted = jnp.where(lifted > 0, mul(wt_s[1, MIXW + FF :, :], low), 0.0).astype(bf16)
    put_blocks(18, mul_t(h2, back_lifted))
    more, gain_grad = norm_back(
        y2, inverse2, gain(5, LANES), mul(wn_s[1, :, MIXW : MIXW + FF], back_lifted)
    )
    ggain_s[5] = gain_grad
    back = back + more
    low = back.astype(bf16)
    put_blocks(15, mul_t(low, cross_mixed))
    cross_back_s[...] = mul(wt_s[1, 5 * WIDTH : 6 * WIDTH, :], low).astype(bf16)

    def cross_back(g, carry):
        mixed_rows = rows_of(g, cross_back_s[...])
        back_chance = row_products(mixed_rows, mem_s, g, WIDTH)
        back_chance = jnp.where(iota(back_chance.shape, 1) < HIST_LEN, back_chance, 0.0)
        chance = pc_s[g]
        inner = jnp.sum(back_chance * chance, axis=1, keepdims=True)
        spread = blocks_of(chance * (back_chance - inner))
        total = mul_t(mem_s[g, :WIDTH, :], spread)
        mem_s[g, :WIDTH, :] = mul(rows_t_of(g, cross_s[...]), spread).astype(bf16)
        mem_s[g, WIDTH:, :] = mul(rows_t_of(g, cross_back_s[...]), blocks_of(chance)).astype(bf16)
        oc_s[g] = jnp.where(head_mask(total.shape), total, 0.0).astype(bf16)
        return carry

    lax.fori_loop(0, chunks, cross_back, 0, unroll=True)
    back_query = gather_rows(oc_s)
    put_blocks(12, mul_t(h1, back_query) * HEAD_DIM**-0.5)
    more, gain_grad = norm_back(
        y1, inverse1, gain(4, LANES), mul(wn_s[1, :, 4 * WIDTH : 5 * WIDTH], back_query)
    )
    ggain_s[4] = gain_grad
    back = back + more
    low = back.astype(bf16)
    put_blocks(9, mul_t(low, self_mixed))
    back_mixed = mul(wt_s[1, 3 * WIDTH : 4 * WIDTH, :], low).astype(bf16)
    *back_parts, self_scores = attend_back(
        [dz_s[part_of(PAIRS + j), :LANES] for j in range(PAIRS)],
        [dz_s[part_of(j), :LANES] for j in range(PAIRS)],
        [self_values[:, part_of(j)] for j in range(PAIRS)],
        [back_mixed[part_of(j)] for j in range(PAIRS)],
        self_chance,
    )
    dz_s[:, LANES:] = jnp.concatenate([x for part in back_parts for x in part], 0)
    put_blocks(0, mul_t(h0, dz_s[:WIDTH, LANES : 2 * LANES]) * HEAD_DIM**-0.5)
    put_blocks(3, mul_t(h0, dz_s[WIDTH:, LANES : 2 * LANES]))
    more, gain_grad = norm_back(
        y0, inverse0, gain(3, LANES), mul(wn_s[1, :, : 3 * WIDTH], dz_s[:, LANES : 2 * LANES])
    )
    ggain_s[3] = gain_grad
    back = back + more
    spread = mul_t(start, split_low(back))
    ge_s[:CODES, :] = table_grad + spread[:, :D] + spread[:, D:]
    ge_s[CODES:, :] = jnp.zeros((n, D), f32)
    rows_s[...] = jnp.zeros_like(rows_s)
    for head in range(HEADS):
        lanes = slice(head * LANES, (head + 1) * LANES)
        for b in range(LEVELS):
            hit = jnp.where(offset == b, self_scores[:, lanes], 0.0)
            rows_s[head, BUCKETS + b : BUCKETS + b + 1, :] = jnp.sum(hit, axis=0, keepdims=True)

    def reducing(buffer, kept, held, upto):
        steps, at = [], 0
        for k, stage in enumerate(order[:upto]):
            rows, left = held[k], held[k + 1]
            side = side_of(stage)
            if left < rows:
                source = buffer.at[span(at + (1 - side) * left, left)]
                at = at + side * left
            else:
                source = buffer.at[span(at, rows)]
            steps.append((remote(source, kept[k], stage), at, left))
        return steps, at, held

    def begin(steps, k):
        steps[k][0].start()

    def finish(steps, buffer, kept, k):
        copy, at, left = steps[k]
        copy.wait()
        place = span(at, left)
        total = buffer[place, :].astype(f32) + kept[k][...].astype(f32)
        buffer[place, :] = total.astype(bf16)

    flat_depth = depth - 1
    held_rest, held_first, held_codes = shares(dp, REST), shares(dp, FIRST), shares(dp, CODES, 1)
    land, rest = {}, lands
    for name, number in (
        ("rest0", flat_depth),
        ("rest1", flat_depth),
        ("first1", flat_depth),
        ("first0", len(far)),
        ("codes", len(far)),
    ):
        land[name], rest = rest[:number], rest[number:]
    land_rest, land_first = rest
    rest1 = reducing(rest_s.at[1], land["rest1"], held_rest, flat_depth)
    first1 = reducing(first_s.at[1], land["first1"], held_first, flat_depth)
    rest0 = reducing(rest_s.at[0], land["rest0"], held_rest, flat_depth)
    first0 = reducing(first_s.at[0], land["first0"], held_first, len(far))
    codes = reducing(codes_s, land["codes"], held_codes, len(far))

    def step1(k):
        if k > 0:
            finish(rest1[0], rest_s.at[1], land["rest1"], k - 1)
            finish(first1[0], first_s.at[1], land["first1"], k - 1)
        if k < flat_depth:
            begin(rest1[0], k)
            begin(first1[0], k)

    def crossing(buffer, target, at, rows):
        source = buffer.at[1 - section, span(at, rows)]
        return remote(source, target, across)

    cross_rest = crossing(rest_s, land_rest, rest1[1], rest1[2][-1])
    cross_first = crossing(first_s, land_first, first1[1], first1[2][-1])

    def settle(copy, buffer, landed, at, rows, base):
        copy.wait()
        value = (buffer[section, span(at, rows), :].astype(f32) + landed[...].astype(f32)).astype(
            bf16
        )
        out_ref[span(base + at, rows), :] = value
        value = value.astype(f32)
        return jnp.sum(value * value, axis=0, keepdims=True)

    def gathering(base, at, held):
        steps = []
        for k in reversed(range(flat_depth)):
            rows, left = held[k], held[k + 1]
            if left < rows:
                place = out_ref.at[span(base + at, left)]
                steps.append(remote(place, place, order[k]))
                at = at - side_of(order[k]) * left
            else:
                steps.append(None)
        return steps

    gather_rest = gathering(0, rest1[1], rest1[2])

    def step0(k):
        if k > 0 and k <= flat_depth:
            finish(rest0[0], rest_s.at[0], land["rest0"], k - 1)
        if k < flat_depth:
            begin(rest0[0], k)
        if k == flat_depth:
            cross_rest.start()
        if k == flat_depth + 1:
            squares = settle(cross_rest, rest_s, land_rest, rest1[1], rest1[2][-1], 0)
            own_slot_s[16:17, :] = squares / (dp * rest1[2][-1] // REST)
        if k > flat_depth + 1 and gather_rest[k - flat_depth - 2] is not None:
            gather_rest[k - flat_depth - 2].wait()
        if flat_depth < k < 2 * flat_depth + 1 and gather_rest[k - flat_depth - 1] is not None:
            gather_rest[k - flat_depth - 1].start()

    g0_s[...] = jnp.zeros_like(g0_s)
    gbias_s[...] = jnp.zeros_like(gbias_s)
    for g in range(3):
        ggain_s[g] = jnp.zeros((D, LANES), f32)

    def fold(x):
        return sum(x[:, i * LANES : (i + 1) * LANES] for i in range(COLUMNS))

    def back_rest(c, carry):
        at_chunk(c, step1, 0, 2, flat_depth + 1)
        x2 = get_wide(x2_s, c)
        inverse = inverse_rms(x2)
        back_memory = mem_s[c]
        add_blocks(12, mul_t(norm_low(x2, inverse, gain(2, WIDE)), back_memory))
        back, gain_grad = norm_back(
            x2, inverse, gain(2, WIDE), mul(wn_s[0, :, 4 * WIDTH : 6 * WIDTH], back_memory)
        )
        ggain_s[2] += fold(gain_grad)
        low = back.astype(bf16)
        add_blocks(26, mul_t(low, r_s[c]))
        for j in range(4):
            part = slice(j * FF // 4, (j + 1) * FF // 4)
            back_active = mul(wt_s[0, MIXW + FF + part.start : MIXW + FF + part.stop, :], low)
            live = r_s[c, part, :].astype(f32) > 0
            r_s[c, part, :] = jnp.where(live, back_active, 0.0).astype(bf16)
        at_chunk(c, step1, 1, 2, flat_depth + 1)
        x1 = x1_s[c]
        inverse = inverse_rms(x1)
        add_blocks(18, mul_t(norm_low(x1, inverse, gain(1, WIDE)), r_s[c]))
        more, gain_grad = norm_back(
            x1, inverse, gain(1, WIDE), mul(wn_s[0, :, MIXW : MIXW + FF], r_s[c])
        )
        ggain_s[1] += fold(gain_grad)
        put_wide(x2_s, c, back + more)
        return carry

    lax.fori_loop(0, chunks, back_rest, 0)
    for j in range(2 * chunks, flat_depth + 1):
        step1(j)
    for block in range(REST // D):
        rest_s[0, block * D : (block + 1) * D, :] = g0_s[FIRST // D + block].astype(bf16)

    steps0 = 2 * flat_depth + 2

    def back_first(c, carry):
        at_chunk(c, step0, 0, 3, steps0)
        back = get_wide(x2_s, c)
        lane = iota((D, LANES), 1)
        low = [jnp.where(lane < PACK, part, 0.0).astype(bf16) for part in unpack(back)]
        low = jnp.concatenate(low, 1)
        add_blocks(9, mul_t(low, o_s[c]))
        o_s[c] = mul(wt_s[0, 3 * WIDTH : 4 * WIDTH, :], low).astype(bf16)
        def attention(b, carry):
            for j in range(1, steps0, 3):
                now = (c == j // 3) & (b == GROUP // BATCH // 2)
                pl.when(now)(functools.partial(step0, j))
            queries, keys, values, backs = [], [], [], []
            for i in range(BATCH):
                lanes = lanes_of(b * BATCH + i)
                queries += [qkv_s[c, part_of(j), lanes] for j in range(PAIRS)]
                keys += [qkv_s[c, part_of(PAIRS + j), lanes] for j in range(PAIRS)]
                values += [qkv_s[c, part_of(2 * PAIRS + j), lanes].T[:KEYS] for j in range(PAIRS)]
                backs += [o_s[c, part_of(j), lanes] for j in range(PAIRS)]
            chance = [p_s[GROUP * c + b * BATCH + i] for i in range(BATCH)]
            *results, scores = attend_back(
                keys, queries, values, backs, jnp.concatenate(chance, 1)
            )
            for i in range(BATCH):
                own = slice(i * PAIRS, (i + 1) * PAIRS)
                both = jnp.concatenate([x for part in results for x in part[own]], 0)
                dqkv_s[:, lanes_of(b * BATCH + i)] = both
            width = HEADS * LANES
            gbias_s[...] += sum(scores[:, i * width : (i + 1) * width] for i in range(BATCH))
            return carry

        lax.fori_loop(0, GROUP // BATCH, attention, 0)
        at_chunk(c, step0, 2, 3, steps0)
        x0 = x0_s[c]
        inverse = inverse_rms(x0)
        add_blocks(0, mul_t(spread_low(x0 * inverse * gain(0, WIDE)), dqkv_s[...]))
        back_normed = packed(mul(wn_s[0, :, : 3 * WIDTH], dqkv_s[...]))
        more, gain_grad = norm_back(x0, inverse, gain(0, WIDE), back_normed)
        ggain_s[0] += fold(gain_grad)
        find(c)
        spread = mul_t(hot_s[...], split_low(back + more))
        ge_s[...] += spread[:, :D] + spread[:, D:]
        return carry

    lax.fori_loop(0, chunks, back_first, 0)

    for block in range(FIRST // D):
        value = g0_s[block]
        if block < 3:
            value = value * HEAD_DIM**-0.5
        first_s[0, block * D : (block + 1) * D, :] = value.astype(bf16)
    codes_s[...] = ge_s[:CODES, :].astype(bf16)
    begin(first0[0], 0)
    begin(codes[0], 0)
    user_low_s[...] = ge_s[CODES:, :].astype(bf16)
    store_users = pltpu.make_async_copy(
        user_low_s, out_user_ref.at[span(slot * n, n)], local_sems.at[BLOCKS + 2]
    )
    store_users.start()
    late = list(range(min(3 * chunks, steps0), steps0))
    if late:
        step0(late.pop(0))

    ones = jnp.ones((8, LANES), f32)
    own_slot_s[8:16, :] = jnp.zeros((8, LANES), f32)
    for g in range(7):
        own_slot_s[g : g + 1, :] = mul_exact_t(ones, ggain_s[g])[:1]
    own_slot_s[7:8, :] = jnp.broadcast_to(loss, (1, LANES))

    def bucket_sums(b, carry):
        for head in range(HEADS):
            lanes = slice(head * LANES, (head + 1) * LANES)
            hit = jnp.where(buckets == b, gbias_s[:, lanes], 0.0)
            rows_s[head, pl.ds(b, 1), :] = jnp.sum(hit, axis=0, keepdims=True)
        return carry

    lax.fori_loop(0, BUCKETS, bucket_sums, 0, unroll=4)
    for head in range(HEADS):
        sums = mul_exact_t(ones, rows_s[head])
        own_slot_s[8 + head : 9 + head, : 2 * BUCKETS] = sums[:1]
    own_slot_s[19:, :] = jnp.zeros((5, LANES), f32)

    for k in range(len(far)):
        finish(first0[0], first_s.at[0], land["first0"], k)
        finish(codes[0], codes_s, land["codes"], k)
        if k + 1 < len(far):
            begin(first0[0], k + 1)
            begin(codes[0], k + 1)

    first_at, first_left = first0[1], held_first[len(far) + 1 :]
    codes_at, codes_left = codes[1], held_codes[len(far) + 1 :]
    size, code_size = first_left[-1], codes_left[-1]
    mine_first = first_at + shift_of(0, first_left)
    mine_codes = codes_at + shift_of(0, codes_left)
    inside, crossing_first, everyone = [], [], []
    for mask in masks:
        source = first_s.at[0, span(first_at + shift_of(mask, first_left), size)]
        copy = remote_to(source, near_first.at[mask], device_of(mask))
        (crossing_first if mask >> (NEAR - 1) else inside).append(copy)
    for mask in masks:
        source = codes_s.at[span(codes_at + shift_of(mask, codes_left), code_size)]
        everyone.append(remote_to(source, near_codes.at[mask], device_of(mask)))
    store_users.wait()
    held = out_user_ref.at[span(slot * n, n)]
    users_out = [remote_to(held, held, device_of(mask)) for mask in masks]

    @pl.when(section == 0)
    def _():
        for copy in inside:
            copy.start()
        cross_first.start()

    @pl.when(section == 1)
    def _():
        for copy in crossing_first:
            copy.start()

    for copy in everyone + users_out:
        copy.start()
    for step in late:
        step0(step)

    def keep_first(value):
        value = value.astype(bf16)
        out_ref[span(REST + mine_first, size), :] = value
        value = value.astype(f32)
        squares = jnp.sum(value * value, axis=0, keepdims=True)
        own_slot_s[17:18, :] = squares / (dp * size // FIRST)

    @pl.when(section == 0)
    def _():
        for copy in inside:
            copy.wait()
        for copy in crossing_first:
            copy.wait_recv()
        cross_first.wait_send()
        value = first_s[0, span(mine_first, size), :].astype(f32)
        for mask in masks:
            value = value + near_first[mask].astype(f32)
        keep_first(value)

    @pl.when(section == 1)
    def _():
        for copy in crossing_first:
            copy.wait_send()
        cross_first.wait_recv()
        value = first_s[1, span(mine_first, size), :].astype(f32)
        keep_first(value + land_first[...].astype(f32))

    for copy in everyone:
        copy.wait()
    value = codes_s[span(mine_codes, code_size), :].astype(f32)
    for mask in masks:
        value = value + near_codes[mask].astype(f32)
    value = value.astype(bf16)
    out_ref[span(COLS + mine_codes, code_size), :] = value
    value = value.astype(f32)
    squares = jnp.sum(value * value, axis=0, keepdims=True)
    own_slot_s[18:19, :] = squares / (2 * dp * code_size // CODES)

    store_slot = pltpu.make_async_copy(
        own_slot_s, out_slot_ref.at[slot], local_sems.at[BLOCKS + 3]
    )
    store_slot.start()

    copies = []
    place = out_ref.at[span(REST + mine_first, size)]
    code_place = out_ref.at[span(COLS + mine_codes, code_size)]
    for mask in masks:
        device = device_of(mask)
        if not mask >> (NEAR - 1):
            copies.append(remote_to(place, place, device))
        copies.append(remote_to(code_place, code_place, device))
    for copy in copies:
        copy.start()
    store_slot.wait()
    held = out_slot_ref.at[slot]
    slots_out = [remote_to(held, held, device_of(mask)) for mask in masks]
    for copy in slots_out:
        copy.start()
    copies += slots_out
    for copy in copies + users_out:
        copy.wait()
    for j, k in enumerate(reversed(range(len(far)))):
        stage = far[k]
        copies = []
        if held_first[k + 1] < held_first[k]:
            place = out_ref.at[span(REST + first_at, held_first[k + 1])]
            copies.append(remote(place, place, stage))
            first_at = first_at - side_of(stage) * held_first[k + 1]
        if held_codes[k + 1] < held_codes[k]:
            place = out_ref.at[span(COLS + codes_at, held_codes[k + 1])]
            copies.append(remote(place, place, stage))
            codes_at = codes_at - side_of(stage) * held_codes[k + 1]
        slots = 2 ** (NEAR + j)
        first_slot = lax.div(slot, slots) * slots
        held = out_slot_ref.at[pl.ds(first_slot, slots)]
        copies.append(remote(held, held, stage))
        held = out_user_ref.at[span(first_slot * n, slots * n)]
        copies.append(remote(held, held, stage))
        for copy in copies:
            copy.start()
        for copy in copies:
            copy.wait()


def gradients(codes, users, targets, domains, bias, gains, mixer, feed, embedding, dp):
    n = users.shape[0] // 2
    chunks = n // GROUP
    order = stages(dp)
    depth = len(order)
    devices = 2 * dp
    vmem = pl.BlockSpec(memory_space=pltpu.VMEM)
    smem = pl.BlockSpec(memory_space=pltpu.SMEM)
    hbm = pl.BlockSpec(memory_space=pl.ANY)
    stat = (16, LANES)
    held_rest, held_first, held_codes = shares(dp, REST), shares(dp, FIRST), shares(dp, CODES, 1)
    plane, far = depth - 1, depth - NEAR
    sizes = [*held_rest[1:] * 2, *held_first[1:]]
    sizes += [*held_first[1 : far + 1], *held_codes[1 : far + 1], held_rest[-1], held_first[-1]]
    lands = [pltpu.VMEM((rows, D), bf16) for rows in sizes]
    copies = 128 + 16 * depth
    return pl.pallas_call(
        functools.partial(step_kernel, n, dp),
        out_shape=(
            jax.ShapeDtypeStruct((COLS + CODES, D), bf16),
            jax.ShapeDtypeStruct((devices * n, D), bf16),
            jax.ShapeDtypeStruct((devices, 8, LANES), jnp.int32),
            jax.ShapeDtypeStruct((devices, 24, LANES), f32),
            jax.ShapeDtypeStruct((8, LANES), f32),
        ),
        in_specs=[vmem, smem, vmem, vmem, vmem, smem, vmem, hbm, hbm, hbm],
        out_specs=(vmem, hbm, hbm, hbm, vmem),
        scratch_shapes=[
            pltpu.VMEM((chunks, D, WIDE), f32),
            pltpu.VMEM((chunks, D, WIDE), f32),
            pltpu.VMEM((chunks * COLUMNS * D, LANES), f32),
            pltpu.VMEM((chunks, 3 * WIDTH, SPAN), bf16),
            pltpu.VMEM((n, KEYS, HEADS * LANES), bf16),
            pltpu.VMEM((chunks, WIDTH, SPAN), bf16),
            pltpu.VMEM((chunks, FF, WIDE), bf16),
            pltpu.VMEM((chunks, 2 * WIDTH, WIDE), bf16),
            pltpu.VMEM((3 * WIDTH, 2 * LANES), bf16),
            pltpu.VMEM((2, D, COLS), bf16),
            pltpu.VMEM((2, COLS, D), bf16),
            pltpu.VMEM((2 * D, CODES + n), bf16),
            pltpu.VMEM((7, D, LANES), f32),
            pltpu.VMEM((KEYS, HEADS * LANES), f32),
            pltpu.VMEM((LANES, HEADS * LANES), f32),
            pltpu.VMEM((BLOCKS, D, LANES), f32),
            pltpu.VMEM((CODES + n, D), f32),
            pltpu.VMEM((KEYS, HEADS * LANES), f32),
            pltpu.VMEM((7, D, LANES), f32),
            pltpu.VMEM((HEADS, 2 * BUCKETS, LANES), f32),
            pltpu.VMEM((n, D), f32),
            pltpu.VMEM((n, LANES), jnp.int32),
            pltpu.VMEM((WIDTH, LANES), bf16),
            pltpu.VMEM((WIDTH, LANES), bf16),
            pltpu.VMEM((chunks, 32 * GROUP, LANES), f32),
            pltpu.VMEM((chunks, WIDTH, 32 * GROUP), bf16),
            pltpu.VMEM((2, REST, D), bf16),
            pltpu.VMEM((2, FIRST, D), bf16),
            pltpu.VMEM((CODES, D), bf16),
            pltpu.VMEM((8, LANES), jnp.int32),
            pltpu.VMEM((n, D), bf16),
            pltpu.VMEM((24, LANES), f32),
            pltpu.VMEM((8, WIDE), jnp.int32),
            pltpu.VMEM((CODES + n, WIDE), bf16),
            pltpu.VMEM((3 * WIDTH, SPAN), bf16),
            pltpu.VMEM((depth + 1,) + stat, f32),
            pltpu.VMEM((depth,) + stat, f32),
            pltpu.VMEM((2**NEAR, held_first[-1], D), bf16),
            pltpu.VMEM((2**NEAR, held_codes[-1], D), bf16),
            pltpu.SemaphoreType.DMA((BLOCKS + 4,)),
            pltpu.SemaphoreType.DMA((copies,)),
            pltpu.SemaphoreType.DMA((copies,)),
        ]
        + lands,
        compiler_params=pltpu.CompilerParams(
            collective_id=0, has_side_effects=True, vmem_limit_bytes=63 * 2**20
        ),
        name="gradients",
    )(codes, users, users.reshape(1, -1), targets, domains, bias, gains, mixer, feed, embedding)


def adam(weight, moment, square, slope, rate, decay):
    moment = beta_one * moment + (1 - beta_one) * slope
    square = beta_two * square + (1 - beta_two) * slope * slope
    unbiased_moment = moment * (1 / (1 - beta_one**STEP))
    unbiased_square = square * (1 / (1 - beta_two**STEP))
    root = unbiased_square * lax.rsqrt(unbiased_square)
    divisor = root + adam_eps
    inverse = pl.reciprocal(divisor, approx=True)
    inverse = inverse * (2.0 - divisor * inverse)
    step = unbiased_moment * inverse + decay * weight
    return weight - rate * step, moment, square


def update_kernel(*refs):
    parts_in, big_in, small_in, refs = refs[:5], refs[5:14], refs[14:20], refs[20:]
    loss_ref, norm_ref, section_ref, hist_ref = refs[:4]
    big_out, small_out, low_out, refs = refs[4:13], refs[13:19], refs[19:22], refs[22:]
    parts, hold, low_hold = refs[:5], refs[5:14], refs[14:17]
    user_grad, part_sems, in_sems, out_sems = refs[17:]
    grad_ref, user_ref, ids_ref, slot_ref, stat_ref = parts
    arrivals = [pltpu.make_async_copy(parts_in[i], parts[i], part_sems.at[i]) for i in range(5)]
    loads = [pltpu.make_async_copy(big_in[i], hold[i], in_sems.at[i]) for i in range(9)]
    for load in arrivals[1:] + arrivals[:1] + loads:
        load.start()
    for arrival in arrivals:
        arrival.wait()

    users = user_grad.shape[0]
    span = min(1024, user_ref.shape[0])
    slots = span // LANES * (ids_ref.shape[0] * LANES // user_ref.shape[0])
    fit = ids_ref.shape[0] * LANES // user_ref.shape[0]
    user_grad[...] = jnp.zeros_like(user_grad)

    def scatter(part, carry):
        rows = user_ref[pl.ds(pl.multiple_of(part * span, span), span), :]
        lanes = []
        for group in range(span // LANES):
            total = ids_ref[part * slots + group * fit, :1, :]
            for other in range(1, fit):
                total = total + ids_ref[part * slots + group * fit + other, :1, :]
            lanes.append(total)
        ids = jnp.concatenate(lanes, 1)
        for block in range(users // USER_ROWS):
            place = slice(block * USER_ROWS, (block + 1) * USER_ROWS)
            hit = iota((USER_ROWS, span), 0) + block * USER_ROWS == ids
            user_grad[place, :] += mul(jnp.where(hit, 1.0, 0.0).astype(bf16), rows)
        return carry

    lax.fori_loop(0, user_ref.shape[0] // span, scatter, 0)

    def total(x):
        return jnp.sum(jnp.sum(x, axis=0, keepdims=True), axis=1, keepdims=True)

    def slot_sum(first):
        def add(i, value):
            return value + slot_ref[2 * i + first]

        zero = jnp.zeros(slot_ref.shape[1:], f32)
        return lax.fori_loop(0, slot_ref.shape[0] // 2, add, zero)

    even, odd = slot_sum(0), slot_sum(1)
    section_squares = [total(x[16:17] + x[17:18]) for x in (even, odd)]
    small = even[:16] + odd[:16]
    rest = total(even[18:19] + odd[18:19])
    user_values = user_grad[...]
    rest = rest + total(user_values * user_values)
    lane, line = iota(small.shape, 1), iota(small.shape, 0)
    counted = (line < 7) | ((line > 7) & (lane < 2 * BUCKETS))
    small_kept = jnp.where(counted, small, 0.0)
    rest = rest + total(small_kept * small_kept)
    norm = jnp.sqrt(section_squares[0] + section_squares[1] + rest)
    factor = jnp.minimum(1.0, clip_norm / (norm + 1e-06))
    loss_ref[0] = small[7, 0]
    norm_ref[0] = norm[0, 0]
    for s in range(2):
        section_ref[s] = jnp.sqrt(section_squares[s])[0, 0]
    for row in range(8):
        lanes = slice((row % 2) * LANES, (row % 2 + 1) * LANES)
        hist_ref[row // 2 : row // 2 + 1, lanes] = stat_ref[row : row + 1, :]

    outs = adam(
        small_in[0][...], small_in[1][...], small_in[2][...], factor * small[:7], rate_gain, 0.0
    )
    for ref, value in zip(small_out[:3], outs):
        ref[...] = value
    for head in range(HEADS):
        for s in range(2):
            slope = factor * small[8 + head : 9 + head, s * BUCKETS : (s + 1) * BUCKETS]
            one = slice(s, s + 1)
            outs = adam(
                small_in[3][head, one, :],
                small_in[4][head, one, :],
                small_in[5][head, one, :],
                slope,
                rate_small,
                0.0,
            )
            for ref, value in zip(small_out[3:], outs):
                ref[head, one, :] = value

    stores = []

    def store(kind, place):
        first = 3 * kind
        pieces = [(hold[first + i], big_out[first + i]) for i in range(3)]
        pieces.append((low_hold[kind], low_out[kind]))
        for source, target in pieces:
            copy = pltpu.make_async_copy(
                source.at[place], target.at[place], out_sems.at[len(stores)]
            )
            copy.start()
            stores.append(copy)

    def step(kind, place, slope):
        first = 3 * kind
        outs = adam(
            hold[first][place],
            hold[first + 1][place],
            hold[first + 2][place],
            factor * slope,
            rate_matrix,
            decay_matrix,
        )
        for i in range(3):
            hold[first + i][place] = outs[i]
        low_hold[kind][place] = outs[0].astype(bf16)

    def block_of(block):
        first = FIRST // D
        place = block - first if block >= first else REST // D + block
        return grad_ref[place * D : (place + 1) * D, :].astype(f32)

    for i in range(3):
        loads[i].wait()
    for part in range(6):
        for block in range(3 * part, 3 * part + 3):
            lanes = slice(block * LANES, (block + 1) * LANES)
            step(0, (0, slice(None), lanes), block_of(block))
        store(0, (0, slice(None), slice(3 * part * LANES, 3 * (part + 1) * LANES)))
    for i in range(3, 6):
        loads[i].wait()
    for part in range(4):
        for block in range(4 * part, 4 * part + 4):
            lanes = slice(block * LANES, (block + 1) * LANES)
            step(1, (0, slice(None), lanes), block_of(MIXW // LANES + block))
        store(1, (0, slice(None), slice(4 * part * LANES, 4 * (part + 1) * LANES)))
    for i in range(6, 9):
        loads[i].wait()
    for part in range(4):
        rows = slice(part * CODEBOOK, (part + 1) * CODEBOOK)
        step(2, (rows, slice(None)), grad_ref[COLS + rows.start : COLS + rows.stop, :].astype(f32))
        store(2, (rows, slice(None)))
    for part in range(users // USER_ROWS):
        rows = slice(part * USER_ROWS, (part + 1) * USER_ROWS)
        place = (slice(CODES + part * USER_ROWS, CODES + (part + 1) * USER_ROWS), slice(None))
        step(2, place, user_grad[rows, :])
        store(2, place)
    for copy in stores:
        copy.wait()


def update(reduced, mixers, feeds, embeds, gains, biases):
    vmem = pl.BlockSpec(memory_space=pltpu.VMEM)
    smem = pl.BlockSpec(memory_space=pltpu.SMEM)
    hbm = pl.BlockSpec(memory_space=pl.ANY)
    big = [*mixers, *feeds, *embeds]
    small = [*gains, *biases]
    low = [jax.ShapeDtypeStruct(x[0].shape, bf16) for x in (mixers, feeds, embeds)]
    users = embeds[0].shape[0] - CODES
    pieces = 4 * (6 + 4 + 4 + users // USER_ROWS)
    return pl.pallas_call(
        update_kernel,
        out_shape=[
            jax.ShapeDtypeStruct((1,), f32),
            jax.ShapeDtypeStruct((1,), f32),
            jax.ShapeDtypeStruct((2,), f32),
            jax.ShapeDtypeStruct((LEVELS, CODEBOOK), f32),
        ]
        + [jax.ShapeDtypeStruct(x.shape, f32) for x in big + small]
        + low,
        in_specs=[hbm] * 14 + [vmem] * 6,
        out_specs=[smem] * 3 + [vmem] + [hbm] * 9 + [vmem] * 6 + [hbm] * 3,
        scratch_shapes=[pltpu.VMEM(x.shape, x.dtype) for x in reduced]
        + [pltpu.VMEM(x.shape, f32) for x in big]
        + [pltpu.VMEM(x.shape, bf16) for x in low]
        + [
            pltpu.VMEM((users, D), f32),
            pltpu.SemaphoreType.DMA((5,)),
            pltpu.SemaphoreType.DMA((9,)),
            pltpu.SemaphoreType.DMA((pieces,)),
        ],
        compiler_params=pltpu.CompilerParams(vmem_limit_bytes=62 * 2**20),
        name="update",
    )(*reduced, *big, *small)


def shards(
    history_codes,
    user_ids,
    targets,
    domains,
    mixer,
    mixer_moment,
    mixer_square,
    feed,
    feed_moment,
    feed_square,
    embedding,
    embedding_moment,
    embedding_square,
    gains,
    gains_moment,
    gains_square,
    position_bias,
    bias_moment,
    bias_square,
):
    def turned(table):
        return jnp.transpose(table, (2, 0, 1))

    biases = [turned(x) for x in (position_bias, bias_moment, bias_square)]
    reduced = gradients(
        history_codes,
        user_ids,
        targets.T,
        domains.reshape(1, -1),
        biases[0],
        gains,
        mixer,
        feed,
        embedding,
        lax.axis_size("dp"),
    )
    outs = update(
        reduced,
        (mixer, mixer_moment, mixer_square),
        (feed, feed_moment, feed_square),
        (embedding, embedding_moment, embedding_square),
        (gains, gains_moment, gains_square),
        biases,
    )
    loss, norm, sections, histograms = outs[:4]
    back = [jnp.transpose(x, (1, 2, 0)) for x in outs[16:19]]
    return (
        loss.reshape(()),
        norm.reshape(()),
        sections,
        histograms,
        *outs[4:16],
        *back,
        *outs[19:],
    )


def solution(mesh):
    by_dp, by_pipe, copied = P("dp"), P("pipe"), P()
    return jax.shard_map(
        shards,
        mesh=mesh,
        in_specs=(by_dp,) * 4 + (by_pipe,) * 6 + (copied,) * 9,
        out_specs=(copied,) * 4 + (by_pipe,) * 6 + (copied,) * 9 + (by_pipe,) * 2 + (copied,),
        check_vma=False,
    )
```

```python
import functools

import jax
import jax.numpy as jnp
from jax import lax
from jax.experimental import pallas as pl
from jax.experimental.pallas import tpu as pltpu
from jax.sharding import PartitionSpec as P

D = 128
HEADS = 6
HEAD_DIM = 64
FF = 1024
CODEBOOK = 256
LEVELS = 4
BUCKETS = 32
DOMAINS = 3
HIST_LEN = 81
STEP = 5
CODES = 1024
LANES = 128
WIDTH = HEADS * HEAD_DIM
MIXW = 6 * WIDTH
COLS = MIXW + 2 * FF
BLOCKS = COLS // LANES
KEYS = 96
GROUP = 8
BATCH = 2
NEAR = 3
PACK = 96
WIDE = GROUP * PACK
SPAN = GROUP * LANES
COLUMNS = WIDE // LANES
PAIRS = HEADS // 2
FIRST = 4 * WIDTH
REST = COLS - FIRST
USER_ROWS = 400
MESH = pl.DeviceIdType.MESH

norm_eps = 1e-06
beta_one = 0.9
beta_two = 0.999
adam_eps = 1e-08
clip_norm = 0.5
rate_matrix = 0.04
rate_gain = 0.8
rate_small = 0.3
decay_matrix = 0.01

f32 = jnp.float32
bf16 = jnp.bfloat16


def iota(shape, axis):
    return lax.broadcasted_iota(jnp.int32, shape, axis)


def mul(left, right):
    return jnp.dot(left, right, preferred_element_type=f32)


def mul_t(left, right):
    return lax.dot_general(left, right, (((1,), (1,)), ((), ())), preferred_element_type=f32)


def mul_exact(left, right):
    return jnp.dot(left, right, preferred_element_type=f32, precision=lax.Precision.HIGHEST)


def mul_exact_t(left, right):
    return lax.dot_general(
        left,
        right,
        (((1,), (1,)), ((), ())),
        preferred_element_type=f32,
        precision=lax.Precision.HIGHEST,
    )


def onehot(ids, rows):
    return jnp.where(iota((rows, ids.shape[1]), 0) == ids, 1.0, 0.0).astype(bf16)


def inverse_rms(x):
    return lax.rsqrt(jnp.mean(x * x, axis=0, keepdims=True) + norm_eps)


def norm_low(x, inverse, gain):
    return (x * inverse * gain).astype(bf16)


def norm_back(x, inverse, gain, upstream):
    scaled = x * inverse
    inner = upstream * gain
    back = inverse * (inner - scaled * jnp.mean(inner * scaled, axis=0, keepdims=True))
    return back, upstream * scaled


def block_diag(pair):
    zero = jnp.zeros((HEAD_DIM, LANES), pair.dtype)
    left = jnp.concatenate([pair[:HEAD_DIM], zero], 0)
    right = jnp.concatenate([zero, pair[HEAD_DIM:]], 0)
    return jnp.concatenate([left, right], 1)


def diagonal(both):
    return jnp.concatenate([both[:HEAD_DIM, :LANES], both[HEAD_DIM:, LANES:]], 0)


def turn(x, shift):
    return x if shift % LANES == 0 else pltpu.roll(x, shift % LANES, 1)


def pack(tables):
    lane = iota(tables[0].shape, 1)
    columns = []
    for first in range(0, len(tables), 4):
        turned = [turn(tables[first + i], PACK * i) for i in range(4)]
        for i in range(3):
            columns.append(jnp.where(lane < PACK - 32 * i, turned[i], turned[i + 1]))
    return jnp.concatenate(columns, 1)


def unpack(x):
    lane = iota((x.shape[0], LANES), 1)
    tables = []
    for first in range(0, x.shape[1] // LANES, 3):
        a, b, c = [x[:, (first + i) * LANES : (first + i + 1) * LANES] for i in range(3)]
        tables.append(a)
        tables.append(jnp.where(lane < 32, turn(a, 32), turn(b, 32)))
        tables.append(jnp.where(lane < 64, turn(b, 64), turn(c, 64)))
        tables.append(turn(c, 96))
    return tables


def stack(both):
    return jnp.concatenate([both[:, :LANES], both[:, LANES:]], 0)


def pad_keys(table):
    if table.shape[0] == LANES:
        return table
    zero = jnp.zeros((LANES - table.shape[0], table.shape[1]), table.dtype)
    return jnp.concatenate([table, zero], 0)


def columns_of(table, i):
    return table[:, 2 * i * LANES : 2 * (i + 1) * LANES]


def attend(keys, queries, values, bias):
    scores = [mul(key, block_diag(query)) for key, query in zip(keys, queries)]
    scores = jnp.concatenate(scores, 1) + bias
    top = jnp.max(scores, axis=0, keepdims=True)
    chance = jnp.exp(scores - top)
    total = jnp.sum(chance, axis=0, keepdims=True)
    chance = (chance * (1.0 / total)).astype(bf16)
    full = pad_keys(chance)
    mixed = [mul(value, columns_of(full, i)) for i, value in enumerate(values)]
    return chance, [diagonal(both).astype(bf16) for both in mixed]


def attend_back(keys_t, queries, values, back_mixed, chance):
    exact = chance.astype(f32)
    back_chance = [mul(value, block_diag(back)) for value, back in zip(values, back_mixed)]
    back_chance = jnp.concatenate(back_chance, 1)
    inner = jnp.sum(back_chance * exact, axis=0, keepdims=True)
    back_scores = exact * (back_chance - inner)
    low = pad_keys(back_scores.astype(bf16))
    full = pad_keys(chance)
    count = range(len(queries))
    back_query = [mul(keys_t[i], columns_of(low, i)) for i in count]
    back_keys = [mul_t(queries[i], stack(columns_of(low, i))) for i in count]
    back_values = [mul_t(back_mixed[i], stack(columns_of(full, i))) for i in count]
    results = [
        [diagonal(both).astype(bf16) for both in part]
        for part in (back_query, back_keys, back_values)
    ]
    return *results, back_scores


def split_low(x):
    high = x.astype(bf16)
    return jnp.concatenate([high, (x - high.astype(f32)).astype(bf16)], 0)


def stages(dp):
    bits = [2**k for k in range(dp.bit_length() - 1)]
    return [("dp", bit) for bit in bits[:2] + bits[4:] + bits[2:4]] + [("pipe", 1)]


def side_of(stage):
    axis, bit = stage
    return lax.rem(lax.div(lax.axis_index(axis), bit), 2)


def partner_of(stage):
    axis, bit = stage
    return {axis: lax.axis_index(axis) + bit * (1 - 2 * side_of(stage))}


def shares(dp, rows, across=0):
    held = [rows]
    depth = len(stages(dp)) - 1
    for k in range(depth + across):
        later = min(NEAR - 1, depth - 1 - k) + across if k < depth else 0
        half = held[-1] // 2
        held.append(half if half % (16 * 2**later) == 0 else held[-1])
    return held


def span(start, size):
    return pl.ds(pl.multiple_of(start, 16), size)


def step_kernel(n, dp, *refs):
    codes_ref, users_ref, user_row_ref, targets_ref, domains_ref, bias_ref, gains_ref = refs[:7]
    mixer_ref, feed_ref, embed_ref = refs[7:10]
    out_ref, out_user_ref, out_ids_ref, out_slot_ref, out_stat_ref = refs[10:15]
    x0_s, x1_s, qkv_s, p_s, o_s, r_s, mem_s, dqkv_s = [refs[15 + 2 * i : 17 + 2 * i] for i in range(8)]
    refs = refs[31:]
    x2_s, dz_s, wn_s, wt_s, ext_s = refs[:5]
    gain_s, ebias_s, dbias_s, g0_s, ge_s, gbias_s, ggain_s, rows_s, user_s, ids_s = refs[5:15]
    cross_s, cross_back_s, pc_s, oc_s, rest_s, first_s, codes_s, slot_s, user_low_s, own_slot_s, id_rows_s, hot_s = refs[15:27]
    stat_s, stat_land, near_first, near_codes, local_sems, sends, recvs = refs[27:34]
    lands = refs[34:]
    order = stages(dp)
    across = order[-1]
    depth = len(order)
    chunks = n // GROUP
    section = lax.axis_index("pipe")
    used = [0]

    def remote_to(source, target, device):
        index = used[0]
        used[0] += 1
        return pltpu.make_async_remote_copy(
            src_ref=source,
            dst_ref=target,
            send_sem=sends.at[index],
            recv_sem=recvs.at[index],
            device_id=device,
            device_id_type=MESH,
        )

    def remote(source, target, stage):
        return remote_to(source, target, partner_of(stage))

    near, far = order[-NEAR:], order[:-NEAR]
    masks = range(1, 2 ** len(near))

    def device_of(mask):
        place = {"dp": lax.axis_index("dp"), "pipe": lax.axis_index("pipe")}
        for i, (axis, bit) in enumerate(near):
            if mask >> i & 1:
                place[axis] = place[axis] + bit * (1 - 2 * side_of((axis, bit)))
        return place

    def shift_of(mask, lefts):
        total = 0
        for i, left in enumerate(lefts):
            side = side_of(near[i])
            total = total + (1 - side if mask >> i & 1 else side) * left
        return total

    locals_in = []
    for block in range(BLOCKS):
        lanes = slice(block * LANES, (block + 1) * LANES)
        if block < MIXW // LANES:
            source = mixer_ref.at[0, :, lanes]
        else:
            source = feed_ref.at[0, :, slice(lanes.start - MIXW, lanes.stop - MIXW)]
        locals_in.append(pltpu.make_async_copy(source, g0_s.at[block], local_sems.at[block]))
    vocabulary = embed_ref.shape[0]
    flat = x2_s.at[pl.ds(0, vocabulary)]
    load_embed = pltpu.make_async_copy(embed_ref, flat, local_sems.at[BLOCKS])
    for copy in locals_in:
        copy.start()
    load_embed.start()

    barrier = pltpu.get_barrier_semaphore()
    for stage in far:
        pl.semaphore_signal(barrier, inc=1, device_id=partner_of(stage), device_id_type=MESH)
    for mask in masks:
        pl.semaphore_signal(barrier, inc=1, device_id=device_of(mask), device_id_type=MESH)

    scale = HEAD_DIM**-0.5
    cross_scale = jnp.where(section == 1, scale, 1.0).astype(f32)
    for copy in locals_in:
        copy.wait()
    for block in range(BLOCKS):
        value = g0_s[block]
        if block < 3:
            value = value * scale
        elif 12 <= block < 15:
            value = value * cross_scale
        wn_s[section, :, block * LANES : (block + 1) * LANES] = value.astype(bf16)
    pl.semaphore_wait(barrier, len(far) + len(masks))
    half = D // 2
    mine = span(side_of(order[0]) * half, half)
    pieces = (slice(0, FIRST), slice(FIRST, COLS))
    over = [
        remote(wn_s.at[section, mine, piece], wn_s.at[section, mine, piece], across)
        for piece in pieces
    ]
    for copy in over:
        copy.start()

    ids_s[:, : HIST_LEN - 1] = codes_ref[pl.ds(pl.multiple_of(section * n, 8), n), :]
    lane, row = iota((n, LANES), 1), iota((n, LANES), 0)
    ids = ids_s[...] + ((lane & 3) << 8)
    ids = jnp.where(lane < HIST_LEN - 1, ids, jnp.where(lane == HIST_LEN - 1, CODES + row, -1))
    ids_s[...] = ids
    packed = []
    for i in range(GROUP):
        rows = [ids_s[c * GROUP + i : c * GROUP + i + 1, :] for c in range(chunks)]
        rows += [jnp.zeros((8 - chunks, LANES), jnp.int32)]
        packed.append(jnp.concatenate(rows, 0))
    id_rows_s[...] = pack(packed)
    count = targets_ref.shape[1]
    history, token = iota((count, LANES), 0), iota((count, LANES), 1)
    pick = jnp.where((token >> 2) + section * n == history, 1.0, 0.0)
    level, place = iota((LEVELS, LANES), 0), iota((LEVELS, LANES), 1) & 3
    target = mul(targets_ref[...].astype(f32), pick) + (level * CODEBOOK).astype(f32)
    goal = jnp.sum(jnp.where(level == place, target, 0.0), axis=0, keepdims=True).astype(jnp.int32)
    start_ids = jnp.sum(
        jnp.where(level == place - 1, target, 0.0), axis=0, keepdims=True
    ).astype(jnp.int32)
    domain = mul(domains_ref[...].astype(f32), pick)
    pick = jnp.where(lax.rem(token, n) + section * n == history, 1.0, 0.0)
    own_users = mul_exact(user_row_ref[...].astype(f32), pick)

    counts = [
        jnp.sum(jnp.where(domain == d, 1.0, 0.0), axis=1, keepdims=True) for d in range(DOMAINS)
    ]
    counts += [jnp.zeros((1, 1), f32)] * (8 - DOMAINS)
    stat_s[0, 8:, :] = jnp.broadcast_to(jnp.concatenate(counts, 0), (8, LANES))
    histogram = mul_t(jnp.ones((8, LANES), bf16), onehot(goal, CODES))
    for r in range(8):
        stat_s[0, r : r + 1, :] = histogram[:1, r * LANES : (r + 1) * LANES]
    slot = 0
    for k, stage in enumerate(order):
        slot = slot + side_of(stage) * 2 ** (depth - 1 - k)
    owner = iota((8, LANES), 1) // n
    own_users = jnp.broadcast_to(own_users, (8, LANES)).astype(jnp.int32)
    slot_s[...] = jnp.where(owner == lax.rem(slot, LANES // n), own_users, 0)
    store_ids = pltpu.make_async_copy(slot_s, out_ids_ref.at[slot], local_sems.at[BLOCKS + 1])
    store_ids.start()
    store_ids.wait()

    def slots_of(j):
        return pl.ds(lax.div(slot, 2**j) * 2**j, 2**j)

    early = []
    for j, stage in enumerate(reversed(order)):
        held = out_ids_ref.at[slots_of(j)]
        early.append(
            (
                remote(stat_s.at[j], stat_land.at[j], stage),
                remote(held, held, stage),
            )
        )

    def early_step(j):
        if j > 0:
            for copy in early[j - 1]:
                copy.wait()
            stat_s[j] = stat_s[j - 1] + stat_land[j - 1]
        if j < depth:
            for copy in early[j]:
                copy.start()

    eye = jnp.where(iota((LANES, LANES), 0) == iota((LANES, LANES), 1), 1.0, 0.0).astype(bf16)
    load_embed.wait()

    def fetch(i, carry):
        user_s[pl.ds(i, 1), :] = x2_s[pl.ds(CODES + users_ref[section * n + i], 1), :]
        return carry

    lax.fori_loop(0, n, fetch, 0, unroll=8)
    for block in range(CODES // LANES + 1):
        if block < CODES // LANES:
            rows = x2_s[block * LANES : (block + 1) * LANES, :]
            codes_s[block * LANES : (block + 1) * LANES, :] = rows.astype(bf16)
            width = LANES
        else:
            rows = user_s[...]
            width = n
        high = rows.astype(bf16)
        low = (rows - high.astype(f32)).astype(bf16)
        lanes = slice(block * LANES, block * LANES + width)
        ext_s[:D, lanes] = mul_t(eye, high).astype(bf16)
        ext_s[D:, lanes] = mul_t(eye, low).astype(bf16)

    def find(c):
        ids = id_rows_s[pl.ds(c, 1), :]
        for first in range(0, CODES + n, LANES):
            rows = min(LANES, CODES + n - first)
            hot_s[first : first + rows, :] = onehot(ids - first, rows)

    def lookup(c):
        find(c)
        both = mul(ext_s[...], hot_s[...])
        x0_s[c % 2][c // 2] = both[:D] + both[D:]

    for c in range(chunks):
        lookup(c)

    beside = []
    for piece in pieces:
        came = wn_s.at[1 - section, mine, piece]
        beside.append(remote(came, came, order[0]))
    over[0].wait()
    beside[0].start()

    for g in range(7):
        gain_s[g] = jnp.broadcast_to(gains_ref[g : g + 1, :], (LANES, LANES)).T

    def positions(axis):
        index = iota((KEYS, LANES), axis)
        return jnp.where(index == HIST_LEN - 1, 0, index + 1)

    key, query = positions(0), positions(1)
    distance = jnp.abs(query - key)
    remoteness = jnp.zeros_like(distance)
    for edge in (12, 16, 23, 32, 46, 64, 91):
        remoteness = remoteness + (distance >= edge).astype(jnp.int32)
    nearby = jnp.minimum(jnp.where(distance < 8, distance, 8 + remoteness), 15)
    buckets = nearby + jnp.where(key > query, 16, 0)
    real = iota((KEYS, LANES), 0) < HIST_LEN
    for head in range(HEADS):
        lanes = slice(head * LANES, (head + 1) * LANES)

        def choose(b, table):
            return jnp.where(buckets == b, bias_ref[head, 0, b], table)

        table = lax.fori_loop(0, BUCKETS, choose, jnp.zeros((KEYS, LANES), f32), unroll=True)
        ebias_s[:, lanes] = jnp.where(real, table, -1e30)
    key, query = iota((LANES, LANES), 0), iota((LANES, LANES), 1)
    offset = query - key
    seen = ((key >> 2) == (query >> 2)) & (offset >= 0)
    for head in range(HEADS):
        lanes = slice(head * LANES, (head + 1) * LANES)
        table = jnp.full((LANES, LANES), -1e30, f32)
        for b in range(LEVELS):
            table = jnp.where(seen & (offset == b), bias_ref[head, 1, b], table)
        dbias_s[:, lanes] = table

    def transpose_weights(which, first, last):
        for block in range(first, last):
            place = slice(block * LANES, (block + 1) * LANES)
            wt_s[which, place, :] = wn_s[which, :, place].T

    transpose_weights(section, 0, BLOCKS)
    beside[0].wait()
    transpose_weights(1 - section, 0, FIRST // LANES)

    def rest_arrives():
        over[1].wait()
        beside[1].start()
        beside[1].wait()
        transpose_weights(1 - section, FIRST // LANES, BLOCKS)

    def gain(g, width):
        column = gain_s[g]
        return column if width == LANES else jnp.concatenate([column] * (width // LANES), 1)

    def lockstep(steps, point=None):
        for number, _ in enumerate(zip(*steps)):
            if point is not None:
                point(number)

    def at_time(t, steps):
        for time, step in enumerate(steps):
            if step is not None:
                pl.when(t == time)(step)

    def spread_low(x):
        return jnp.concatenate([part.astype(bf16) for part in unpack(x)], 1)

    def packed(x):
        return pack([x[:, i * LANES : (i + 1) * LANES] for i in range(GROUP)])

    def part_of(j):
        return slice(j * LANES, (j + 1) * LANES)

    def encode_steps(t, half):
        c = 2 * t + half
        qkv, o, r = qkv_s[half], o_s[half], r_s[half]
        x0 = x0_s[half][t]
        h = spread_low(x0 * inverse_rms(x0) * gain(0, WIDE))
        yield
        for j in range(3):
            part = slice(j * WIDTH, (j + 1) * WIDTH)
            qkv[t, part, :] = mul(wt_s[0, part, :], h).astype(bf16)
        yield
        for first in range(0, GROUP, BATCH):
            queries, keys, values = [], [], []
            for i in range(first, first + BATCH):
                lanes = slice(i * LANES, (i + 1) * LANES)
                queries += [qkv[t, part_of(j), lanes] for j in range(PAIRS)]
                keys += [qkv[t, part_of(PAIRS + j), lanes].T[:KEYS] for j in range(PAIRS)]
                values += [qkv[t, part_of(2 * PAIRS + j), lanes] for j in range(PAIRS)]
            bias = jnp.concatenate([ebias_s[...]] * BATCH, 1)
            chance, mixed = attend(keys, queries, values, bias)
            for i in range(BATCH):
                lanes = slice((first + i) * LANES, (first + i + 1) * LANES)
                own = slice(i * HEADS * LANES, (i + 1) * HEADS * LANES)
                p_s[half][t, first + i] = chance[:, own]
                o[t, :, lanes] = jnp.concatenate(mixed[i * PAIRS : (i + 1) * PAIRS], 0)
            yield
        x1 = x0 + packed(mul(wn_s[0, :, 3 * WIDTH : 4 * WIDTH], o[t]))
        x1_s[half][t] = x1
        yield
        h = norm_low(x1, inverse_rms(x1), gain(1, WIDE))
        for j in range(2):
            part = slice(j * FF // 2, (j + 1) * FF // 2)
            lifted = mul(wt_s[0, MIXW + j * FF // 2 : MIXW + (j + 1) * FF // 2, :], h)
            r[t, part, :] = jnp.maximum(lifted, 0.0).astype(bf16)
        yield
        x2 = x1 + mul(wn_s[0, :, MIXW + FF :], r[t])
        put_wide(x2_s, c, x2)
        e = norm_low(x2, inverse_rms(x2), gain(2, WIDE))
        yield
        for j in range(2):
            part = slice(j * WIDTH, (j + 1) * WIDTH)
            mem_s[half][t, part, :] = mul(
                wt_s[0, 4 * WIDTH + j * WIDTH : 4 * WIDTH + (j + 1) * WIDTH, :], e
            ).astype(bf16)
        yield

    attention = GROUP // BATCH
    pairs = chunks // 2

    def early_at(place, places):
        return [
            functools.partial(early_step, place + places * t)
            if place + places * t <= depth
            else None
            for t in range(pairs)
        ]

    def encode(t, carry):
        at_time(t, early_at(0, 3))

        def point(number):
            if number == attention // 2:
                at_time(t, early_at(1, 3))
            if number == attention + 2:
                pl.when(t == 0)(rest_arrives)
                at_time(t, early_at(2, 3))

        lockstep([encode_steps(t, 0), encode_steps(t, 1)], point)
        return carry

    def put_wide(ref, c, value):
        for i in range(COLUMNS):
            ref[pl.ds(pl.multiple_of((COLUMNS * c + i) * D, D), D), :] = value[
                :, i * LANES : (i + 1) * LANES
            ]

    def get_wide(ref, c):
        return jnp.concatenate(
            [ref[pl.ds(pl.multiple_of((COLUMNS * c + i) * D, D), D), :] for i in range(COLUMNS)], 1
        )

    lax.fori_loop(0, pairs, encode, 0)
    for j in range(3 * pairs, depth + 1):
        early_step(j)
    out_stat_ref[...] = stat_s[depth, :8, :]

    def put_blocks(first, value):
        for index in range(value.shape[1] // LANES):
            block = first + index
            part = value[:, index * LANES : (index + 1) * LANES].astype(bf16)
            if block < FIRST // LANES:
                first_s[1, block * D : (block + 1) * D, :] = part
            else:
                block -= FIRST // LANES
                rest_s[1, block * D : (block + 1) * D, :] = part

    def add_blocks(first, value):
        for index in range(value.shape[1] // LANES):
            g0_s[first + index] += value[:, index * LANES : (index + 1) * LANES]

    start = onehot(start_ids, CODES)
    both = mul(ext_s[:, :CODES], start)
    y0 = both[:D] + both[D:]
    inverse0 = inverse_rms(y0)
    h0 = norm_low(y0, inverse0, gain(3, LANES))
    dz_s[:, :LANES] = mul(wt_s[1, : 3 * WIDTH, :], h0).astype(bf16)
    both = mul(mul_t(eye, h0).astype(bf16), wn_s[1, :, WIDTH : 3 * WIDTH]).astype(bf16)
    self_chance, mixed = attend(
        [both[:, part_of(j)] for j in range(PAIRS)],
        [dz_s[part_of(j), :LANES] for j in range(PAIRS)],
        [dz_s[part_of(2 * PAIRS + j), :LANES] for j in range(PAIRS)],
        dbias_s[...],
    )
    self_values = both[:, WIDTH:]
    self_mixed = jnp.concatenate(mixed, 0)
    y1 = y0 + mul(wn_s[1, :, 3 * WIDTH : 4 * WIDTH], self_mixed)
    inverse1 = inverse_rms(y1)
    h1 = norm_low(y1, inverse1, gain(4, LANES))
    cross_s[...] = mul(wt_s[1, 4 * WIDTH : 5 * WIDTH, :], h1).astype(bf16)

    def spreader(g, turned):
        shape = (LANES, 32 * GROUP) if turned else (32 * GROUP, LANES)
        row, token = iota(shape, 1 if turned else 0), iota(shape, 0 if turned else 1)
        hit = token == 4 * GROUP * g + 4 * (row >> 5) + (row & 3)
        return jnp.where(hit, 1.0, 0.0).astype(bf16)

    def rows_of(g, table):
        rows = mul_t(spreader(g, False), table)
        mask = (iota(rows.shape, 1) >> 6) == ((iota(rows.shape, 0) & 31) >> 2)
        return jnp.where(mask, rows, 0.0).astype(bf16)

    def head_mask(shape):
        return (iota(shape, 0) >> 6) == ((iota(shape, 1) & 31) >> 2)

    def rows_t_of(g, table):
        rows = mul(table, spreader(g, True))
        return jnp.where(head_mask(rows.shape), rows, 0.0).astype(bf16)

    def gather_rows(ref):
        total = jnp.zeros((WIDTH, LANES), f32)
        for g in range(chunks):
            total = total + mul(ref[g], spreader(g, False))
        return total.astype(bf16)

    def blocks_of(table):
        rows = []
        for i in range(GROUP):
            part = table[32 * i : 32 * i + 32]
            column, shift = divmod(PACK * i, LANES)
            part = turn(part, shift)
            lane = iota(part.shape, 1)
            zero = jnp.zeros_like(part)
            columns = [zero] * COLUMNS
            columns[column] = jnp.where(lane >= shift, part, 0.0)
            if shift > LANES - PACK:
                columns[column + 1] = jnp.where(lane < shift, part, 0.0)
            rows.append(jnp.concatenate(columns, 1))
        return jnp.concatenate(rows, 0).astype(bf16)

    def row_products(rows, g, first):
        both = mul(rows, mem_s[g % 2][g // 2, first : first + WIDTH, :])
        parts = []
        for i in range(GROUP):
            own = both[32 * i : 32 * i + 32]
            column, shift = divmod(PACK * i, LANES)
            part = turn(own[:, column * LANES : (column + 1) * LANES], -shift)
            if shift > LANES - PACK:
                after = turn(own[:, (column + 1) * LANES : (column + 2) * LANES], -shift)
                part = jnp.where(iota(part.shape, 1) < LANES - shift, part, after)
            parts.append(part)
        return jnp.concatenate(parts, 0)

    def cross(g):
        queries = rows_of(g, cross_s[...])
        scores = row_products(queries, g, 0)
        scores = jnp.where(iota(scores.shape, 1) < HIST_LEN, scores, -1e30)
        chance = jnp.exp(scores - jnp.max(scores, axis=1, keepdims=True))
        chance = chance * (1.0 / jnp.sum(chance, axis=1, keepdims=True))
        pc_s[g] = chance
        mixed = mul_t(mem_s[g % 2][g // 2, WIDTH:, :], blocks_of(chance))
        oc_s[g] = jnp.where(head_mask(mixed.shape), mixed, 0.0).astype(bf16)

    for g in range(chunks):
        cross(g)
    cross_mixed = gather_rows(oc_s)
    y2 = y1 + mul(wn_s[1, :, 5 * WIDTH : 6 * WIDTH], cross_mixed)
    inverse2 = inverse_rms(y2)
    h2 = norm_low(y2, inverse2, gain(5, LANES))
    lifted = mul(wt_s[1, MIXW : MIXW + FF, :], h2)
    active = jnp.maximum(lifted, 0.0).astype(bf16)
    y3 = y2 + mul(wn_s[1, :, MIXW + FF :], active)
    inverse3 = inverse_rms(y3)
    final = norm_low(y3, inverse3, gain(6, LANES))
    logits = mul(codes_s[...], final)
    top = jnp.max(logits, axis=0, keepdims=True)
    log_total = top + jnp.log(jnp.sum(jnp.exp(logits - top), axis=0, keepdims=True))
    match = iota(logits.shape, 0) == goal
    picked = jnp.sum(jnp.where(match, logits, 0.0), axis=0, keepdims=True)
    weight = jnp.zeros((1, LANES), f32)
    for d in range(DOMAINS):
        share = 1.0 / (DOMAINS * jnp.maximum(stat_s[depth, 8 + d : 9 + d, :], 1.0))
        weight = weight + jnp.where(domain == d, share, 0.0)
    loss = jnp.sum(weight * (log_total - picked), axis=1, keepdims=True)
    back_logits = (
        weight * (jnp.exp(logits - log_total) - jnp.where(match, 1.0, 0.0))
    ).astype(bf16)
    back_final = mul(ext_s[:D, :CODES], back_logits)
    table_grad = mul_t(back_logits, final)
    back, gain_grad = norm_back(y3, inverse3, gain(6, LANES), back_final)
    ggain_s[6] = gain_grad
    low = back.astype(bf16)
    put_blocks(26, mul_t(low, active))
    back_lifted = jnp.where(lifted > 0, mul(wt_s[1, MIXW + FF :, :], low), 0.0).astype(bf16)
    put_blocks(18, mul_t(h2, back_lifted))
    more, gain_grad = norm_back(
        y2, inverse2, gain(5, LANES), mul(wn_s[1, :, MIXW : MIXW + FF], back_lifted)
    )
    ggain_s[5] = gain_grad
    back = back + more
    low = back.astype(bf16)
    put_blocks(15, mul_t(low, cross_mixed))
    cross_back_s[...] = mul(wt_s[1, 5 * WIDTH : 6 * WIDTH, :], low).astype(bf16)

    def cross_back(g):
        mixed_rows = rows_of(g, cross_back_s[...])
        back_chance = row_products(mixed_rows, g, WIDTH)
        back_chance = jnp.where(iota(back_chance.shape, 1) < HIST_LEN, back_chance, 0.0)
        chance = pc_s[g]
        inner = jnp.sum(back_chance * chance, axis=1, keepdims=True)
        spread = blocks_of(chance * (back_chance - inner))
        total = mul_t(mem_s[g % 2][g // 2, :WIDTH, :], spread)
        mem_s[g % 2][g // 2, :WIDTH, :] = mul(rows_t_of(g, cross_s[...]), spread).astype(bf16)
        mem_s[g % 2][g // 2, WIDTH:, :] = mul(rows_t_of(g, cross_back_s[...]), blocks_of(chance)).astype(bf16)
        oc_s[g] = jnp.where(head_mask(total.shape), total, 0.0).astype(bf16)

    for g in range(chunks):
        cross_back(g)
    back_query = gather_rows(oc_s)
    put_blocks(12, mul_t(h1, back_query) * HEAD_DIM**-0.5)
    more, gain_grad = norm_back(
        y1, inverse1, gain(4, LANES), mul(wn_s[1, :, 4 * WIDTH : 5 * WIDTH], back_query)
    )
    ggain_s[4] = gain_grad
    back = back + more
    low = back.astype(bf16)
    put_blocks(9, mul_t(low, self_mixed))
    back_mixed = mul(wt_s[1, 3 * WIDTH : 4 * WIDTH, :], low).astype(bf16)
    *back_parts, self_scores = attend_back(
        [dz_s[part_of(PAIRS + j), :LANES] for j in range(PAIRS)],
        [dz_s[part_of(j), :LANES] for j in range(PAIRS)],
        [self_values[:, part_of(j)] for j in range(PAIRS)],
        [back_mixed[part_of(j)] for j in range(PAIRS)],
        self_chance,
    )
    dz_s[:, LANES:] = jnp.concatenate([x for part in back_parts for x in part], 0)
    put_blocks(0, mul_t(h0, dz_s[:WIDTH, LANES : 2 * LANES]) * HEAD_DIM**-0.5)
    put_blocks(3, mul_t(h0, dz_s[WIDTH:, LANES : 2 * LANES]))
    more, gain_grad = norm_back(
        y0, inverse0, gain(3, LANES), mul(wn_s[1, :, : 3 * WIDTH], dz_s[:, LANES : 2 * LANES])
    )
    ggain_s[3] = gain_grad
    back = back + more
    spread = mul_t(start, split_low(back))
    ge_s[:CODES, :] = table_grad + spread[:, :D] + spread[:, D:]
    ge_s[CODES:, :] = jnp.zeros((n, D), f32)
    rows_s[...] = jnp.zeros_like(rows_s)
    for head in range(HEADS):
        lanes = slice(head * LANES, (head + 1) * LANES)
        for b in range(LEVELS):
            hit = jnp.where(offset == b, self_scores[:, lanes], 0.0)
            rows_s[head, BUCKETS + b : BUCKETS + b + 1, :] = jnp.sum(hit, axis=0, keepdims=True)

    def reducing(buffer, kept, held, upto):
        steps, at = [], 0
        for k, stage in enumerate(order[:upto]):
            rows, left = held[k], held[k + 1]
            side = side_of(stage)
            if left < rows:
                source = buffer.at[span(at + (1 - side) * left, left)]
                at = at + side * left
            else:
                source = buffer.at[span(at, rows)]
            steps.append((remote(source, kept[k], stage), at, left))
        return steps, at, held

    def begin(steps, k):
        steps[k][0].start()

    def finish(steps, buffer, kept, k):
        copy, at, left = steps[k]
        copy.wait()
        place = span(at, left)
        total = buffer[place, :].astype(f32) + kept[k][...].astype(f32)
        buffer[place, :] = total.astype(bf16)

    flat_depth = depth - 1
    held_rest, held_first, held_codes = shares(dp, REST), shares(dp, FIRST), shares(dp, CODES, 1)
    land, rest = {}, lands
    for name, number in (
        ("rest0", flat_depth),
        ("rest1", flat_depth),
        ("first1", flat_depth),
        ("first0", len(far)),
        ("codes", len(far)),
    ):
        land[name], rest = rest[:number], rest[number:]
    land_rest, land_first = rest
    rest1 = reducing(rest_s.at[1], land["rest1"], held_rest, flat_depth)
    first1 = reducing(first_s.at[1], land["first1"], held_first, flat_depth)
    rest0 = reducing(rest_s.at[0], land["rest0"], held_rest, flat_depth)
    first0 = reducing(first_s.at[0], land["first0"], held_first, len(far))
    codes = reducing(codes_s, land["codes"], held_codes, len(far))

    def step1(k):
        if k > 0:
            finish(rest1[0], rest_s.at[1], land["rest1"], k - 1)
            finish(first1[0], first_s.at[1], land["first1"], k - 1)
        if k < flat_depth:
            begin(rest1[0], k)
            begin(first1[0], k)

    def crossing(buffer, target, at, rows):
        source = buffer.at[1 - section, span(at, rows)]
        return remote(source, target, across)

    cross_rest = crossing(rest_s, land_rest, rest1[1], rest1[2][-1])
    cross_first = crossing(first_s, land_first, first1[1], first1[2][-1])

    def settle(copy, buffer, landed, at, rows, base):
        copy.wait()
        value = (buffer[section, span(at, rows), :].astype(f32) + landed[...].astype(f32)).astype(
            bf16
        )
        out_ref[span(base + at, rows), :] = value
        value = value.astype(f32)
        return jnp.sum(value * value, axis=0, keepdims=True)

    def gathering(base, at, held):
        steps = []
        for k in reversed(range(flat_depth)):
            rows, left = held[k], held[k + 1]
            if left < rows:
                place = out_ref.at[span(base + at, left)]
                steps.append(remote(place, place, order[k]))
                at = at - side_of(order[k]) * left
            else:
                steps.append(None)
        return steps

    gather_rest = gathering(0, rest1[1], rest1[2])

    def step0(k):
        if k > 0 and k <= flat_depth:
            finish(rest0[0], rest_s.at[0], land["rest0"], k - 1)
        if k < flat_depth:
            begin(rest0[0], k)
        if k == flat_depth:
            cross_rest.start()
        if k == flat_depth + 1:
            squares = settle(cross_rest, rest_s, land_rest, rest1[1], rest1[2][-1], 0)
            own_slot_s[16:17, :] = squares / (dp * rest1[2][-1] // REST)
        if k > flat_depth + 1 and gather_rest[k - flat_depth - 2] is not None:
            gather_rest[k - flat_depth - 2].wait()
        if flat_depth < k < 2 * flat_depth + 1 and gather_rest[k - flat_depth - 1] is not None:
            gather_rest[k - flat_depth - 1].start()

    g0_s[...] = jnp.zeros_like(g0_s)
    gbias_s[...] = jnp.zeros_like(gbias_s)
    for g in range(3):
        ggain_s[g] = jnp.zeros((D, LANES), f32)

    def fold(x):
        return sum(x[:, i * LANES : (i + 1) * LANES] for i in range(COLUMNS))

    def rest_steps(t, half):
        c = 2 * t + half
        r = r_s[half]
        x2 = get_wide(x2_s, c)
        inverse = inverse_rms(x2)
        back_memory = mem_s[half][t]
        add_blocks(12, mul_t(norm_low(x2, inverse, gain(2, WIDE)), back_memory))
        back_normed = mul(wn_s[0, :, 4 * WIDTH : 6 * WIDTH], back_memory)
        yield
        back, gain_grad = norm_back(x2, inverse, gain(2, WIDE), back_normed)
        ggain_s[2] += fold(gain_grad)
        low = back.astype(bf16)
        yield
        add_blocks(26, mul_t(low, r[t]))
        for j in range(4):
            part = slice(j * FF // 4, (j + 1) * FF // 4)
            back_active = mul(wt_s[0, MIXW + FF + part.start : MIXW + FF + part.stop, :], low)
            live = r[t, part, :].astype(f32) > 0
            r[t, part, :] = jnp.where(live, back_active, 0.0).astype(bf16)
        yield
        x1 = x1_s[half][t]
        inverse = inverse_rms(x1)
        add_blocks(18, mul_t(norm_low(x1, inverse, gain(1, WIDE)), r[t]))
        back_normed = mul(wn_s[0, :, MIXW : MIXW + FF], r[t])
        yield
        more, gain_grad = norm_back(x1, inverse, gain(1, WIDE), back_normed)
        ggain_s[1] += fold(gain_grad)
        put_wide(x2_s, c, back + more)
        yield

    places1 = {0: 0, 1: 1, 3: 2, 5: 3}
    places0 = {0: 0, 1: 1, 2: 2, 3: 3, 4: 4, 5: 5, 6: 6, 7: 7, 9: 8}
    steps0 = 2 * flat_depth + 2

    def placed(places, step, place, each):
        return [
            functools.partial(step, places[place + each * t])
            if place + each * t in places
            else None
            for t in range(pairs)
        ]

    def back_rest(t, carry):
        at_time(t, placed(places1, step1, 0, 3))

        def point(number):
            if number in (1, 3):
                at_time(t, placed(places1, step1, (number + 1) // 2, 3))

        lockstep([rest_steps(t, 0), rest_steps(t, 1)], point)
        return carry

    lax.fori_loop(0, pairs, back_rest, 0)
    for block in range(REST // D):
        rest_s[0, block * D : (block + 1) * D, :] = g0_s[FIRST // D + block].astype(bf16)

    for j in range(4, flat_depth + 1):
        step1(j)

    def first_steps(t, half):
        c = 2 * t + half
        qkv, o, dqkv = qkv_s[half], o_s[half], dqkv_s[half]
        back = get_wide(x2_s, c)
        lane = iota((D, LANES), 1)
        low = [jnp.where(lane < PACK, part, 0.0).astype(bf16) for part in unpack(back)]
        low = jnp.concatenate(low, 1)
        yield
        add_blocks(9, mul_t(low, o[t]))
        o[t] = mul(wt_s[0, 3 * WIDTH : 4 * WIDTH, :], low).astype(bf16)
        yield
        for first in range(0, GROUP, BATCH):
            queries, keys, values, backs = [], [], [], []
            for i in range(first, first + BATCH):
                lanes = slice(i * LANES, (i + 1) * LANES)
                queries += [qkv[t, part_of(j), lanes] for j in range(PAIRS)]
                keys += [qkv[t, part_of(PAIRS + j), lanes] for j in range(PAIRS)]
                values += [qkv[t, part_of(2 * PAIRS + j), lanes].T[:KEYS] for j in range(PAIRS)]
                backs += [o[t, part_of(j), lanes] for j in range(PAIRS)]
            chance = [p_s[half][t, first + i] for i in range(BATCH)]
            *results, scores = attend_back(
                keys, queries, values, backs, jnp.concatenate(chance, 1)
            )
            for i in range(BATCH):
                lanes = slice((first + i) * LANES, (first + i + 1) * LANES)
                own = slice(i * PAIRS, (i + 1) * PAIRS)
                dqkv[:, lanes] = jnp.concatenate([x for part in results for x in part[own]], 0)
            width = HEADS * LANES
            gbias_s[...] += sum(scores[:, i * width : (i + 1) * width] for i in range(BATCH))
            yield
        x0 = x0_s[half][t]
        inverse = inverse_rms(x0)
        add_blocks(0, mul_t(spread_low(x0 * inverse * gain(0, WIDE)), dqkv[...]))
        back_normed = packed(mul(wn_s[0, :, : 3 * WIDTH], dqkv[...]))
        yield
        more, gain_grad = norm_back(x0, inverse, gain(0, WIDE), back_normed)
        ggain_s[0] += fold(gain_grad)
        find(c)
        spread = mul_t(hot_s[...], split_low(back + more))
        ge_s[...] += spread[:, :D] + spread[:, D:]
        yield

    def back_first(t, carry):
        at_time(t, placed(places0, step0, 0, 5))

        def point(number):
            place = {1: 1, attention // 2 + 1: 2, attention + 1: 3, attention + 2: 4}.get(number)
            if place is not None:
                at_time(t, placed(places0, step0, place, 5))

        lockstep([first_steps(t, 0), first_steps(t, 1)], point)
        return carry

    lax.fori_loop(0, pairs, back_first, 0)

    for block in range(FIRST // D):
        value = g0_s[block]
        if block < 3:
            value = value * HEAD_DIM**-0.5
        first_s[0, block * D : (block + 1) * D, :] = value.astype(bf16)
    codes_s[...] = ge_s[:CODES, :].astype(bf16)
    begin(first0[0], 0)
    begin(codes[0], 0)
    user_low_s[...] = ge_s[CODES:, :].astype(bf16)
    store_users = pltpu.make_async_copy(
        user_low_s, out_user_ref.at[span(slot * n, n)], local_sems.at[BLOCKS + 2]
    )
    store_users.start()
    late = list(range(9, steps0))
    if late:
        step0(late.pop(0))

    ones = jnp.ones((8, LANES), f32)
    own_slot_s[8:16, :] = jnp.zeros((8, LANES), f32)
    for g in range(7):
        own_slot_s[g : g + 1, :] = mul_exact_t(ones, ggain_s[g])[:1]
    own_slot_s[7:8, :] = jnp.broadcast_to(loss, (1, LANES))

    def bucket_sums(b, carry):
        for head in range(HEADS):
            lanes = slice(head * LANES, (head + 1) * LANES)
            hit = jnp.where(buckets == b, gbias_s[:, lanes], 0.0)
            rows_s[head, pl.ds(b, 1), :] = jnp.sum(hit, axis=0, keepdims=True)
        return carry

    lax.fori_loop(0, BUCKETS, bucket_sums, 0, unroll=4)
    for head in range(HEADS):
        sums = mul_exact_t(ones, rows_s[head])
        own_slot_s[8 + head : 9 + head, : 2 * BUCKETS] = sums[:1]
    own_slot_s[19:, :] = jnp.zeros((5, LANES), f32)

    for k in range(len(far)):
        finish(first0[0], first_s.at[0], land["first0"], k)
        finish(codes[0], codes_s, land["codes"], k)
        if k + 1 < len(far):
            begin(first0[0], k + 1)
            begin(codes[0], k + 1)

    first_at, first_left = first0[1], held_first[len(far) + 1 :]
    codes_at, codes_left = codes[1], held_codes[len(far) + 1 :]
    size, code_size = first_left[-1], codes_left[-1]
    mine_first = first_at + shift_of(0, first_left)
    mine_codes = codes_at + shift_of(0, codes_left)
    inside, crossing_first, everyone = [], [], []
    for mask in masks:
        source = first_s.at[0, span(first_at + shift_of(mask, first_left), size)]
        copy = remote_to(source, near_first.at[mask], device_of(mask))
        (crossing_first if mask >> (NEAR - 1) else inside).append(copy)
    for mask in masks:
        source = codes_s.at[span(codes_at + shift_of(mask, codes_left), code_size)]
        everyone.append(remote_to(source, near_codes.at[mask], device_of(mask)))
    store_users.wait()
    held = out_user_ref.at[span(slot * n, n)]
    users_out = [remote_to(held, held, device_of(mask)) for mask in masks]

    @pl.when(section == 0)
    def _():
        for copy in inside:
            copy.start()
        cross_first.start()

    @pl.when(section == 1)
    def _():
        for copy in crossing_first:
            copy.start()

    for copy in everyone + users_out:
        copy.start()
    for step in late:
        step0(step)

    def keep_first(value):
        value = value.astype(bf16)
        out_ref[span(REST + mine_first, size), :] = value
        value = value.astype(f32)
        squares = jnp.sum(value * value, axis=0, keepdims=True)
        own_slot_s[17:18, :] = squares / (dp * size // FIRST)

    @pl.when(section == 0)
    def _():
        for copy in inside:
            copy.wait()
        for copy in crossing_first:
            copy.wait_recv()
        cross_first.wait_send()
        value = first_s[0, span(mine_first, size), :].astype(f32)
        for mask in masks:
            value = value + near_first[mask].astype(f32)
        keep_first(value)

    @pl.when(section == 1)
    def _():
        for copy in crossing_first:
            copy.wait_send()
        cross_first.wait_recv()
        value = first_s[1, span(mine_first, size), :].astype(f32)
        keep_first(value + land_first[...].astype(f32))

    for copy in everyone:
        copy.wait()
    value = codes_s[span(mine_codes, code_size), :].astype(f32)
    for mask in masks:
        value = value + near_codes[mask].astype(f32)
    value = value.astype(bf16)
    out_ref[span(COLS + mine_codes, code_size), :] = value
    value = value.astype(f32)
    squares = jnp.sum(value * value, axis=0, keepdims=True)
    own_slot_s[18:19, :] = squares / (2 * dp * code_size // CODES)

    store_slot = pltpu.make_async_copy(
        own_slot_s, out_slot_ref.at[slot], local_sems.at[BLOCKS + 3]
    )
    store_slot.start()

    copies = []
    place = out_ref.at[span(REST + mine_first, size)]
    code_place = out_ref.at[span(COLS + mine_codes, code_size)]
    for mask in masks:
        device = device_of(mask)
        if not mask >> (NEAR - 1):
            copies.append(remote_to(place, place, device))
        copies.append(remote_to(code_place, code_place, device))
    for copy in copies:
        copy.start()
    store_slot.wait()
    held = out_slot_ref.at[slot]
    slots_out = [remote_to(held, held, device_of(mask)) for mask in masks]
    for copy in slots_out:
        copy.start()
    copies += slots_out
    for copy in copies + users_out:
        copy.wait()
    for j, k in enumerate(reversed(range(len(far)))):
        stage = far[k]
        copies = []
        if held_first[k + 1] < held_first[k]:
            place = out_ref.at[span(REST + first_at, held_first[k + 1])]
            copies.append(remote(place, place, stage))
            first_at = first_at - side_of(stage) * held_first[k + 1]
        if held_codes[k + 1] < held_codes[k]:
            place = out_ref.at[span(COLS + codes_at, held_codes[k + 1])]
            copies.append(remote(place, place, stage))
            codes_at = codes_at - side_of(stage) * held_codes[k + 1]
        slots = 2 ** (NEAR + j)
        first_slot = lax.div(slot, slots) * slots
        held = out_slot_ref.at[pl.ds(first_slot, slots)]
        copies.append(remote(held, held, stage))
        held = out_user_ref.at[span(first_slot * n, slots * n)]
        copies.append(remote(held, held, stage))
        for copy in copies:
            copy.start()
        for copy in copies:
            copy.wait()


def gradients(codes, users, targets, domains, bias, gains, mixer, feed, embedding, dp):
    n = users.shape[0] // 2
    chunks = n // GROUP
    order = stages(dp)
    depth = len(order)
    devices = 2 * dp
    vmem = pl.BlockSpec(memory_space=pltpu.VMEM)
    smem = pl.BlockSpec(memory_space=pltpu.SMEM)
    hbm = pl.BlockSpec(memory_space=pl.ANY)
    stat = (16, LANES)
    held_rest, held_first, held_codes = shares(dp, REST), shares(dp, FIRST), shares(dp, CODES, 1)
    plane, far = depth - 1, depth - NEAR
    sizes = [*held_rest[1:] * 2, *held_first[1:]]
    sizes += [*held_first[1 : far + 1], *held_codes[1 : far + 1], held_rest[-1], held_first[-1]]
    lands = [pltpu.VMEM((rows, D), bf16) for rows in sizes]
    copies = 128 + 16 * depth
    return pl.pallas_call(
        functools.partial(step_kernel, n, dp),
        out_shape=(
            jax.ShapeDtypeStruct((COLS + CODES, D), bf16),
            jax.ShapeDtypeStruct((devices * n, D), bf16),
            jax.ShapeDtypeStruct((devices, 8, LANES), jnp.int32),
            jax.ShapeDtypeStruct((devices, 24, LANES), f32),
            jax.ShapeDtypeStruct((8, LANES), f32),
        ),
        in_specs=[vmem, smem, vmem, vmem, vmem, smem, vmem, hbm, hbm, hbm],
        out_specs=(vmem, hbm, hbm, hbm, vmem),
        scratch_shapes=[
            pltpu.VMEM(shape, dtype)
            for shape, dtype in (
                ((chunks // 2, D, WIDE), f32),
                ((chunks // 2, D, WIDE), f32),
                ((chunks // 2, 3 * WIDTH, SPAN), bf16),
                ((chunks // 2, GROUP, KEYS, HEADS * LANES), bf16),
                ((chunks // 2, WIDTH, SPAN), bf16),
                ((chunks // 2, FF, WIDE), bf16),
                ((chunks // 2, 2 * WIDTH, WIDE), bf16),
                ((3 * WIDTH, SPAN), bf16),
            )
            for _ in range(2)
        ]
        + [
            pltpu.VMEM((chunks * COLUMNS * D, LANES), f32),
            pltpu.VMEM((3 * WIDTH, 2 * LANES), bf16),
            pltpu.VMEM((2, D, COLS), bf16),
            pltpu.VMEM((2, COLS, D), bf16),
            pltpu.VMEM((2 * D, CODES + n), bf16),
            pltpu.VMEM((7, D, LANES), f32),
            pltpu.VMEM((KEYS, HEADS * LANES), f32),
            pltpu.VMEM((LANES, HEADS * LANES), f32),
            pltpu.VMEM((BLOCKS, D, LANES), f32),
            pltpu.VMEM((CODES + n, D), f32),
            pltpu.VMEM((KEYS, HEADS * LANES), f32),
            pltpu.VMEM((7, D, LANES), f32),
            pltpu.VMEM((HEADS, 2 * BUCKETS, LANES), f32),
            pltpu.VMEM((n, D), f32),
            pltpu.VMEM((n, LANES), jnp.int32),
            pltpu.VMEM((WIDTH, LANES), bf16),
            pltpu.VMEM((WIDTH, LANES), bf16),
            pltpu.VMEM((chunks, 32 * GROUP, LANES), f32),
            pltpu.VMEM((chunks, WIDTH, 32 * GROUP), bf16),
            pltpu.VMEM((2, REST, D), bf16),
            pltpu.VMEM((2, FIRST, D), bf16),
            pltpu.VMEM((CODES, D), bf16),
            pltpu.VMEM((8, LANES), jnp.int32),
            pltpu.VMEM((n, D), bf16),
            pltpu.VMEM((24, LANES), f32),
            pltpu.VMEM((8, WIDE), jnp.int32),
            pltpu.VMEM((CODES + n, WIDE), bf16),
            pltpu.VMEM((depth + 1,) + stat, f32),
            pltpu.VMEM((depth,) + stat, f32),
            pltpu.VMEM((2**NEAR, held_first[-1], D), bf16),
            pltpu.VMEM((2**NEAR, held_codes[-1], D), bf16),
            pltpu.SemaphoreType.DMA((BLOCKS + 4,)),
            pltpu.SemaphoreType.DMA((copies,)),
            pltpu.SemaphoreType.DMA((copies,)),
        ]
        + lands,
        compiler_params=pltpu.CompilerParams(
            collective_id=0, has_side_effects=True, vmem_limit_bytes=63 * 2**20
        ),
        name="gradients",
    )(codes, users, users.reshape(1, -1), targets, domains, bias, gains, mixer, feed, embedding)


def adam(weight, moment, square, slope, rate, decay):
    moment = beta_one * moment + (1 - beta_one) * slope
    square = beta_two * square + (1 - beta_two) * slope * slope
    unbiased_moment = moment * (1 / (1 - beta_one**STEP))
    unbiased_square = square * (1 / (1 - beta_two**STEP))
    root = unbiased_square * lax.rsqrt(unbiased_square)
    divisor = root + adam_eps
    inverse = pl.reciprocal(divisor, approx=True)
    inverse = inverse * (2.0 - divisor * inverse)
    step = unbiased_moment * inverse + decay * weight
    return weight - rate * step, moment, square


def update_kernel(*refs):
    parts_in, big_in, small_in, refs = refs[:5], refs[5:14], refs[14:20], refs[20:]
    loss_ref, norm_ref, section_ref, hist_ref = refs[:4]
    big_out, small_out, low_out, refs = refs[4:13], refs[13:19], refs[19:22], refs[22:]
    parts, hold, low_hold = refs[:5], refs[5:14], refs[14:17]
    user_grad, part_sems, in_sems, out_sems = refs[17:]
    grad_ref, user_ref, ids_ref, slot_ref, stat_ref = parts
    arrivals = [pltpu.make_async_copy(parts_in[i], parts[i], part_sems.at[i]) for i in range(5)]
    loads = [pltpu.make_async_copy(big_in[i], hold[i], in_sems.at[i]) for i in range(9)]
    for load in arrivals[1:] + arrivals[:1] + loads:
        load.start()
    for arrival in arrivals:
        arrival.wait()

    users = user_grad.shape[0]
    span = min(1024, user_ref.shape[0])
    slots = span // LANES * (ids_ref.shape[0] * LANES // user_ref.shape[0])
    fit = ids_ref.shape[0] * LANES // user_ref.shape[0]
    user_grad[...] = jnp.zeros_like(user_grad)

    def scatter(part, carry):
        rows = user_ref[pl.ds(pl.multiple_of(part * span, span), span), :]
        lanes = []
        for group in range(span // LANES):
            total = ids_ref[part * slots + group * fit, :1, :]
            for other in range(1, fit):
                total = total + ids_ref[part * slots + group * fit + other, :1, :]
            lanes.append(total)
        ids = jnp.concatenate(lanes, 1)
        for block in range(users // USER_ROWS):
            place = slice(block * USER_ROWS, (block + 1) * USER_ROWS)
            hit = iota((USER_ROWS, span), 0) + block * USER_ROWS == ids
            user_grad[place, :] += mul(jnp.where(hit, 1.0, 0.0).astype(bf16), rows)
        return carry

    lax.fori_loop(0, user_ref.shape[0] // span, scatter, 0)

    def total(x):
        return jnp.sum(jnp.sum(x, axis=0, keepdims=True), axis=1, keepdims=True)

    def slot_sum(first):
        def add(i, value):
            return value + slot_ref[2 * i + first]

        zero = jnp.zeros(slot_ref.shape[1:], f32)
        return lax.fori_loop(0, slot_ref.shape[0] // 2, add, zero)

    even, odd = slot_sum(0), slot_sum(1)
    section_squares = [total(x[16:17] + x[17:18]) for x in (even, odd)]
    small = even[:16] + odd[:16]
    rest = total(even[18:19] + odd[18:19])
    user_values = user_grad[...]
    rest = rest + total(user_values * user_values)
    lane, line = iota(small.shape, 1), iota(small.shape, 0)
    counted = (line < 7) | ((line > 7) & (lane < 2 * BUCKETS))
    small_kept = jnp.where(counted, small, 0.0)
    rest = rest + total(small_kept * small_kept)
    norm = jnp.sqrt(section_squares[0] + section_squares[1] + rest)
    factor = jnp.minimum(1.0, clip_norm / (norm + 1e-06))
    loss_ref[0] = small[7, 0]
    norm_ref[0] = norm[0, 0]
    for s in range(2):
        section_ref[s] = jnp.sqrt(section_squares[s])[0, 0]
    for row in range(8):
        lanes = slice((row % 2) * LANES, (row % 2 + 1) * LANES)
        hist_ref[row // 2 : row // 2 + 1, lanes] = stat_ref[row : row + 1, :]

    outs = adam(
        small_in[0][...], small_in[1][...], small_in[2][...], factor * small[:7], rate_gain, 0.0
    )
    for ref, value in zip(small_out[:3], outs):
        ref[...] = value
    for head in range(HEADS):
        for s in range(2):
            slope = factor * small[8 + head : 9 + head, s * BUCKETS : (s + 1) * BUCKETS]
            one = slice(s, s + 1)
            outs = adam(
                small_in[3][head, one, :],
                small_in[4][head, one, :],
                small_in[5][head, one, :],
                slope,
                rate_small,
                0.0,
            )
            for ref, value in zip(small_out[3:], outs):
                ref[head, one, :] = value

    stores = []

    def store(kind, place):
        first = 3 * kind
        pieces = [(hold[first + i], big_out[first + i]) for i in range(3)]
        pieces.append((low_hold[kind], low_out[kind]))
        for source, target in pieces:
            copy = pltpu.make_async_copy(
                source.at[place], target.at[place], out_sems.at[len(stores)]
            )
            copy.start()
            stores.append(copy)

    def step(kind, place, slope):
        first = 3 * kind
        outs = adam(
            hold[first][place],
            hold[first + 1][place],
            hold[first + 2][place],
            factor * slope,
            rate_matrix,
            decay_matrix,
        )
        for i in range(3):
            hold[first + i][place] = outs[i]
        low_hold[kind][place] = outs[0].astype(bf16)

    def block_of(block):
        first = FIRST // D
        place = block - first if block >= first else REST // D + block
        return grad_ref[place * D : (place + 1) * D, :].astype(f32)

    for i in range(3):
        loads[i].wait()
    for part in range(6):
        for block in range(3 * part, 3 * part + 3):
            lanes = slice(block * LANES, (block + 1) * LANES)
            step(0, (0, slice(None), lanes), block_of(block))
        store(0, (0, slice(None), slice(3 * part * LANES, 3 * (part + 1) * LANES)))
    for i in range(3, 6):
        loads[i].wait()
    for part in range(4):
        for block in range(4 * part, 4 * part + 4):
            lanes = slice(block * LANES, (block + 1) * LANES)
            step(1, (0, slice(None), lanes), block_of(MIXW // LANES + block))
        store(1, (0, slice(None), slice(4 * part * LANES, 4 * (part + 1) * LANES)))
    for i in range(6, 9):
        loads[i].wait()
    for part in range(4):
        rows = slice(part * CODEBOOK, (part + 1) * CODEBOOK)
        step(2, (rows, slice(None)), grad_ref[COLS + rows.start : COLS + rows.stop, :].astype(f32))
        store(2, (rows, slice(None)))
    for part in range(users // USER_ROWS):
        rows = slice(part * USER_ROWS, (part + 1) * USER_ROWS)
        place = (slice(CODES + part * USER_ROWS, CODES + (part + 1) * USER_ROWS), slice(None))
        step(2, place, user_grad[rows, :])
        store(2, place)
    for copy in stores:
        copy.wait()


def update(reduced, mixers, feeds, embeds, gains, biases):
    vmem = pl.BlockSpec(memory_space=pltpu.VMEM)
    smem = pl.BlockSpec(memory_space=pltpu.SMEM)
    hbm = pl.BlockSpec(memory_space=pl.ANY)
    big = [*mixers, *feeds, *embeds]
    small = [*gains, *biases]
    low = [jax.ShapeDtypeStruct(x[0].shape, bf16) for x in (mixers, feeds, embeds)]
    users = embeds[0].shape[0] - CODES
    pieces = 4 * (6 + 4 + 4 + users // USER_ROWS)
    return pl.pallas_call(
        update_kernel,
        out_shape=[
            jax.ShapeDtypeStruct((1,), f32),
            jax.ShapeDtypeStruct((1,), f32),
            jax.ShapeDtypeStruct((2,), f32),
            jax.ShapeDtypeStruct((LEVELS, CODEBOOK), f32),
        ]
        + [jax.ShapeDtypeStruct(x.shape, f32) for x in big + small]
        + low,
        in_specs=[hbm] * 14 + [vmem] * 6,
        out_specs=[smem] * 3 + [vmem] + [hbm] * 9 + [vmem] * 6 + [hbm] * 3,
        scratch_shapes=[pltpu.VMEM(x.shape, x.dtype) for x in reduced]
        + [pltpu.VMEM(x.shape, f32) for x in big]
        + [pltpu.VMEM(x.shape, bf16) for x in low]
        + [
            pltpu.VMEM((users, D), f32),
            pltpu.SemaphoreType.DMA((5,)),
            pltpu.SemaphoreType.DMA((9,)),
            pltpu.SemaphoreType.DMA((pieces,)),
        ],
        compiler_params=pltpu.CompilerParams(vmem_limit_bytes=62 * 2**20),
        name="update",
    )(*reduced, *big, *small)


def shards(
    history_codes,
    user_ids,
    targets,
    domains,
    mixer,
    mixer_moment,
    mixer_square,
    feed,
    feed_moment,
    feed_square,
    embedding,
    embedding_moment,
    embedding_square,
    gains,
    gains_moment,
    gains_square,
    position_bias,
    bias_moment,
    bias_square,
):
    def turned(table):
        return jnp.transpose(table, (2, 0, 1))

    biases = [turned(x) for x in (position_bias, bias_moment, bias_square)]
    reduced = gradients(
        history_codes,
        user_ids,
        targets.T,
        domains.reshape(1, -1),
        biases[0],
        gains,
        mixer,
        feed,
        embedding,
        lax.axis_size("dp"),
    )
    outs = update(
        reduced,
        (mixer, mixer_moment, mixer_square),
        (feed, feed_moment, feed_square),
        (embedding, embedding_moment, embedding_square),
        (gains, gains_moment, gains_square),
        biases,
    )
    loss, norm, sections, histograms = outs[:4]
    back = [jnp.transpose(x, (1, 2, 0)) for x in outs[16:19]]
    return (
        loss.reshape(()),
        norm.reshape(()),
        sections,
        histograms,
        *outs[4:16],
        *back,
        *outs[19:],
    )


def solution(mesh):
    by_dp, by_pipe, copied = P("dp"), P("pipe"), P()
    return jax.shard_map(
        shards,
        mesh=mesh,
        in_specs=(by_dp,) * 4 + (by_pipe,) * 6 + (copied,) * 9,
        out_specs=(copied,) * 4 + (by_pipe,) * 6 + (copied,) * 9 + (by_pipe,) * 2 + (copied,),
        check_vma=False,
    )
```

```python
import functools

import jax
import jax.numpy as jnp
from jax import lax
from jax.experimental import pallas as pl
from jax.experimental.pallas import tpu as pltpu
from jax.sharding import PartitionSpec as P

D = 128
HEADS = 6
HEAD_DIM = 64
FF = 1024
CODEBOOK = 256
LEVELS = 4
BUCKETS = 32
DOMAINS = 3
HIST_LEN = 81
STEP = 5
CODES = 1024
LANES = 128
WIDTH = HEADS * HEAD_DIM
MIXW = 6 * WIDTH
COLS = MIXW + 2 * FF
BLOCKS = COLS // LANES
KEYS = 96
GROUP = 8
BATCH = 2
NEAR = 3
PACK = 96
WIDE = GROUP * PACK
SPAN = GROUP * LANES
COLUMNS = WIDE // LANES
PAIRS = HEADS // 2
FIRST = 4 * WIDTH
REST = COLS - FIRST
USER_ROWS = 400
MESH = pl.DeviceIdType.MESH

norm_eps = 1e-06
beta_one = 0.9
beta_two = 0.999
adam_eps = 1e-08
clip_norm = 0.5
rate_matrix = 0.04
rate_gain = 0.8
rate_small = 0.3
decay_matrix = 0.01

f32 = jnp.float32
bf16 = jnp.bfloat16


def iota(shape, axis):
    return lax.broadcasted_iota(jnp.int32, shape, axis)


def mul(left, right):
    return jnp.dot(left, right, preferred_element_type=f32)


def mul_t(left, right):
    return lax.dot_general(left, right, (((1,), (1,)), ((), ())), preferred_element_type=f32)


def mul_exact(left, right):
    return jnp.dot(left, right, preferred_element_type=f32, precision=lax.Precision.HIGHEST)


def mul_exact_t(left, right):
    return lax.dot_general(
        left,
        right,
        (((1,), (1,)), ((), ())),
        preferred_element_type=f32,
        precision=lax.Precision.HIGHEST,
    )


def onehot(ids, rows):
    return jnp.where(iota((rows, ids.shape[1]), 0) == ids, 1.0, 0.0).astype(bf16)


def inverse_rms(x):
    return lax.rsqrt(jnp.mean(x * x, axis=0, keepdims=True) + norm_eps)


def norm_low(x, inverse, gain):
    return (x * inverse * gain).astype(bf16)


def norm_back(x, inverse, gain, upstream):
    scaled = x * inverse
    inner = upstream * gain
    back = inverse * (inner - scaled * jnp.mean(inner * scaled, axis=0, keepdims=True))
    return back, upstream * scaled


def block_diag(pair):
    zero = jnp.zeros((HEAD_DIM, LANES), pair.dtype)
    left = jnp.concatenate([pair[:HEAD_DIM], zero], 0)
    right = jnp.concatenate([zero, pair[HEAD_DIM:]], 0)
    return jnp.concatenate([left, right], 1)


def diagonal(both):
    return jnp.concatenate([both[:HEAD_DIM, :LANES], both[HEAD_DIM:, LANES:]], 0)


def turn(x, shift):
    return x if shift % LANES == 0 else pltpu.roll(x, shift % LANES, 1)


def pack(tables):
    lane = iota(tables[0].shape, 1)
    columns = []
    for first in range(0, len(tables), 4):
        turned = [turn(tables[first + i], PACK * i) for i in range(4)]
        for i in range(3):
            columns.append(jnp.where(lane < PACK - 32 * i, turned[i], turned[i + 1]))
    return jnp.concatenate(columns, 1)


def unpack(x):
    lane = iota((x.shape[0], LANES), 1)
    tables = []
    for first in range(0, x.shape[1] // LANES, 3):
        a, b, c = [x[:, (first + i) * LANES : (first + i + 1) * LANES] for i in range(3)]
        tables.append(a)
        tables.append(jnp.where(lane < 32, turn(a, 32), turn(b, 32)))
        tables.append(jnp.where(lane < 64, turn(b, 64), turn(c, 64)))
        tables.append(turn(c, 96))
    return tables


def stack(both):
    return jnp.concatenate([both[:, :LANES], both[:, LANES:]], 0)


def pad_keys(table):
    if table.shape[0] == LANES:
        return table
    zero = jnp.zeros((LANES - table.shape[0], table.shape[1]), table.dtype)
    return jnp.concatenate([table, zero], 0)


def columns_of(table, i):
    return table[:, 2 * i * LANES : 2 * (i + 1) * LANES]


def attend(keys, queries, values, bias):
    scores = [mul(key, block_diag(query)) for key, query in zip(keys, queries)]
    scores = jnp.concatenate(scores, 1) + bias
    top = jnp.max(scores, axis=0, keepdims=True)
    chance = jnp.exp(scores - top)
    total = jnp.sum(chance, axis=0, keepdims=True)
    chance = (chance * (1.0 / total)).astype(bf16)
    full = pad_keys(chance)
    mixed = [mul(value, columns_of(full, i)) for i, value in enumerate(values)]
    return chance, [diagonal(both).astype(bf16) for both in mixed]


def attend_back(keys_t, queries, values, back_mixed, chance):
    exact = chance.astype(f32)
    back_chance = [mul(value, block_diag(back)) for value, back in zip(values, back_mixed)]
    back_chance = jnp.concatenate(back_chance, 1)
    inner = jnp.sum(back_chance * exact, axis=0, keepdims=True)
    back_scores = exact * (back_chance - inner)
    low = pad_keys(back_scores.astype(bf16))
    full = pad_keys(chance)
    count = range(len(queries))
    back_query = [mul(keys_t[i], columns_of(low, i)) for i in count]
    back_keys = [mul_t(queries[i], stack(columns_of(low, i))) for i in count]
    back_values = [mul_t(back_mixed[i], stack(columns_of(full, i))) for i in count]
    results = [
        [diagonal(both).astype(bf16) for both in part]
        for part in (back_query, back_keys, back_values)
    ]
    return *results, back_scores


def split_low(x):
    high = x.astype(bf16)
    return jnp.concatenate([high, (x - high.astype(f32)).astype(bf16)], 0)


def stages(dp):
    bits = [2**k for k in range(dp.bit_length() - 1)]
    return [("dp", bit) for bit in bits[:2] + bits[4:] + bits[2:4]] + [("pipe", 1)]


def side_of(stage):
    axis, bit = stage
    return lax.rem(lax.div(lax.axis_index(axis), bit), 2)


def partner_of(stage):
    axis, bit = stage
    return {axis: lax.axis_index(axis) + bit * (1 - 2 * side_of(stage))}


def shares(dp, rows, across=0):
    held = [rows]
    depth = len(stages(dp)) - 1
    for k in range(depth + across):
        later = min(NEAR - 1, depth - 1 - k) + across if k < depth else 0
        half = held[-1] // 2
        held.append(half if half % (16 * 2**later) == 0 else held[-1])
    return held


def span(start, size):
    return pl.ds(pl.multiple_of(start, 16), size)


def step_kernel(n, dp, *refs):
    codes_ref, users_ref, user_row_ref, targets_ref, domains_ref, bias_ref, gains_ref = refs[:7]
    mixer_ref, feed_ref, embed_ref = refs[7:10]
    out_ref, out_user_ref, out_ids_ref, out_slot_ref, out_stat_ref = refs[10:15]
    x0_s, *doubles = refs[15], *[refs[16 + 2 * i : 18 + 2 * i] for i in range(9)]
    x1_s, qkv_s, p_s, o_s, r_s, mem_s, dqkv_s, pc_s, oc_s = doubles
    refs = refs[34:]
    x2_s, dz_s, wn_s, wt_s, ext_s = refs[:5]
    gain_s, ebias_s, dbias_s, g0_s, ge_s, gbias_s, ggain_s, rows_s, user_s, ids_s = refs[5:15]
    cross_s, cross_back_s, rest_s, first_s, codes_s, slot_s, user_low_s, own_slot_s, id_rows_s, hot_s = refs[15:25]
    stat_s, stat_land, near_first, near_codes, local_sems, sends, recvs = refs[25:32]
    lands = refs[32:]
    order = stages(dp)
    across = order[-1]
    depth = len(order)
    chunks = n // GROUP
    section = lax.axis_index("pipe")
    used = [0]

    def remote_to(source, target, device):
        index = used[0]
        used[0] += 1
        return pltpu.make_async_remote_copy(
            src_ref=source,
            dst_ref=target,
            send_sem=sends.at[index],
            recv_sem=recvs.at[index],
            device_id=device,
            device_id_type=MESH,
        )

    def remote(source, target, stage):
        return remote_to(source, target, partner_of(stage))

    near, far = order[-NEAR:], order[:-NEAR]
    masks = range(1, 2 ** len(near))

    def device_of(mask):
        place = {"dp": lax.axis_index("dp"), "pipe": lax.axis_index("pipe")}
        for i, (axis, bit) in enumerate(near):
            if mask >> i & 1:
                place[axis] = place[axis] + bit * (1 - 2 * side_of((axis, bit)))
        return place

    def shift_of(mask, lefts):
        total = 0
        for i, left in enumerate(lefts):
            side = side_of(near[i])
            total = total + (1 - side if mask >> i & 1 else side) * left
        return total

    locals_in = []
    for block in range(BLOCKS):
        lanes = slice(block * LANES, (block + 1) * LANES)
        if block < MIXW // LANES:
            source = mixer_ref.at[0, :, lanes]
        else:
            source = feed_ref.at[0, :, slice(lanes.start - MIXW, lanes.stop - MIXW)]
        locals_in.append(pltpu.make_async_copy(source, g0_s.at[block], local_sems.at[block]))
    vocabulary = embed_ref.shape[0]
    flat = x2_s.at[pl.ds(0, vocabulary)]
    load_embed = pltpu.make_async_copy(embed_ref, flat, local_sems.at[BLOCKS])
    for copy in locals_in:
        copy.start()
    load_embed.start()

    barrier = pltpu.get_barrier_semaphore()
    for stage in far:
        pl.semaphore_signal(barrier, inc=1, device_id=partner_of(stage), device_id_type=MESH)
    for mask in masks:
        pl.semaphore_signal(barrier, inc=1, device_id=device_of(mask), device_id_type=MESH)

    scale = HEAD_DIM**-0.5
    cross_scale = jnp.where(section == 1, scale, 1.0).astype(f32)
    for copy in locals_in:
        copy.wait()
    def cast_weights(block, carry):
        factor = jnp.where((block >= 12) & (block < 15), cross_scale, 1.0)
        factor = jnp.where(block < 3, scale, factor)
        lanes = pl.ds(pl.multiple_of(block * LANES, LANES), LANES)
        wn_s[section, :, lanes] = (g0_s[block] * factor).astype(bf16)
        return carry

    lax.fori_loop(0, BLOCKS, cast_weights, 0, unroll=2)
    pl.semaphore_wait(barrier, len(far) + len(masks))
    half = D // 2
    mine = span(side_of(order[0]) * half, half)
    pieces = (slice(0, FIRST), slice(FIRST, COLS))
    over = [
        remote(wn_s.at[section, mine, piece], wn_s.at[section, mine, piece], across)
        for piece in pieces
    ]
    for copy in over:
        copy.start()

    ids_s[:, : HIST_LEN - 1] = codes_ref[pl.ds(pl.multiple_of(section * n, 8), n), :]
    lane, row = iota((n, LANES), 1), iota((n, LANES), 0)
    ids = ids_s[...] + ((lane & 3) << 8)
    ids = jnp.where(lane < HIST_LEN - 1, ids, jnp.where(lane == HIST_LEN - 1, CODES + row, -1))
    ids_s[...] = ids
    packed = []
    for i in range(GROUP):
        rows = [ids_s[c * GROUP + i : c * GROUP + i + 1, :] for c in range(chunks)]
        rows += [jnp.zeros((8 - chunks, LANES), jnp.int32)]
        packed.append(jnp.concatenate(rows, 0))
    id_rows_s[...] = pack(packed)
    count = targets_ref.shape[1]
    history, token = iota((count, LANES), 0), iota((count, LANES), 1)
    pick = jnp.where((token >> 2) + section * n == history, 1.0, 0.0)
    level, place = iota((LEVELS, LANES), 0), iota((LEVELS, LANES), 1) & 3
    target = mul(targets_ref[...].astype(f32), pick) + (level * CODEBOOK).astype(f32)
    goal = jnp.sum(jnp.where(level == place, target, 0.0), axis=0, keepdims=True).astype(jnp.int32)
    start_ids = jnp.sum(
        jnp.where(level == place - 1, target, 0.0), axis=0, keepdims=True
    ).astype(jnp.int32)
    domain = mul(domains_ref[...].astype(f32), pick)
    pick = jnp.where(lax.rem(token, n) + section * n == history, 1.0, 0.0)
    own_users = mul_exact(user_row_ref[...].astype(f32), pick)

    counts = [
        jnp.sum(jnp.where(domain == d, 1.0, 0.0), axis=1, keepdims=True) for d in range(DOMAINS)
    ]
    counts += [jnp.zeros((1, 1), f32)] * (8 - DOMAINS)
    stat_s[0, 8:, :] = jnp.broadcast_to(jnp.concatenate(counts, 0), (8, LANES))
    histogram = mul_t(jnp.ones((8, LANES), bf16), onehot(goal, CODES))
    for r in range(8):
        stat_s[0, r : r + 1, :] = histogram[:1, r * LANES : (r + 1) * LANES]
    slot = 0
    for k, stage in enumerate(order):
        slot = slot + side_of(stage) * 2 ** (depth - 1 - k)
    owner = iota((8, LANES), 1) // n
    own_users = jnp.broadcast_to(own_users, (8, LANES)).astype(jnp.int32)
    slot_s[...] = jnp.where(owner == lax.rem(slot, LANES // n), own_users, 0)
    store_ids = pltpu.make_async_copy(slot_s, out_ids_ref.at[slot], local_sems.at[BLOCKS + 1])
    store_ids.start()
    store_ids.wait()

    def slots_of(j):
        return pl.ds(lax.div(slot, 2**j) * 2**j, 2**j)

    early = []
    for j, stage in enumerate(reversed(order)):
        held = out_ids_ref.at[slots_of(j)]
        early.append(
            (
                remote(stat_s.at[j], stat_land.at[j], stage),
                remote(held, held, stage),
            )
        )

    def early_step(j):
        if j > 0:
            for copy in early[j - 1]:
                copy.wait()
            stat_s[j] = stat_s[j - 1] + stat_land[j - 1]
        if j < depth:
            for copy in early[j]:
                copy.start()

    eye = jnp.where(iota((LANES, LANES), 0) == iota((LANES, LANES), 1), 1.0, 0.0).astype(bf16)
    load_embed.wait()

    def fetch(i, carry):
        user_s[pl.ds(i, 1), :] = x2_s[pl.ds(CODES + users_ref[section * n + i], 1), :]
        return carry

    lax.fori_loop(0, n, fetch, 0, unroll=4)
    for block in range(CODES // LANES + 1):
        if block < CODES // LANES:
            rows = x2_s[block * LANES : (block + 1) * LANES, :]
            codes_s[block * LANES : (block + 1) * LANES, :] = rows.astype(bf16)
            width = LANES
        else:
            rows = user_s[...]
            width = n
        high = rows.astype(bf16)
        low = (rows - high.astype(f32)).astype(bf16)
        lanes = slice(block * LANES, block * LANES + width)
        ext_s[:D, lanes] = mul_t(eye, high).astype(bf16)
        ext_s[D:, lanes] = mul_t(eye, low).astype(bf16)

    def find(c):
        ids = id_rows_s[pl.ds(c, 1), :]
        for first in range(0, CODES + n, LANES):
            rows = min(LANES, CODES + n - first)
            hot_s[first : first + rows, :] = onehot(ids - first, rows)

    def lookup(c, carry):
        find(c)
        both = mul(ext_s[...], hot_s[...])
        x0_s[c] = both[:D] + both[D:]
        return carry

    lax.fori_loop(0, chunks, lookup, 0)

    beside = []
    for piece in pieces:
        came = wn_s.at[1 - section, mine, piece]
        beside.append(remote(came, came, order[0]))
    over[0].wait()
    beside[0].start()

    for g in range(7):
        gain_s[g] = jnp.broadcast_to(gains_ref[g : g + 1, :], (LANES, LANES)).T

    def positions(axis):
        index = iota((KEYS, LANES), axis)
        return jnp.where(index == HIST_LEN - 1, 0, index + 1)

    key, query = positions(0), positions(1)
    distance = jnp.abs(query - key)
    remoteness = jnp.zeros_like(distance)
    for edge in (12, 16, 23, 32, 46, 64, 91):
        remoteness = remoteness + (distance >= edge).astype(jnp.int32)
    nearby = jnp.minimum(jnp.where(distance < 8, distance, 8 + remoteness), 15)
    buckets = nearby + jnp.where(key > query, 16, 0)
    real = iota((KEYS, LANES), 0) < HIST_LEN
    for head in range(HEADS):
        lanes = slice(head * LANES, (head + 1) * LANES)

        def choose(b, table):
            return jnp.where(buckets == b, bias_ref[head, 0, b], table)

        table = lax.fori_loop(0, BUCKETS, choose, jnp.zeros((KEYS, LANES), f32), unroll=8)
        ebias_s[:, lanes] = jnp.where(real, table, -1e30)
    key, query = iota((LANES, LANES), 0), iota((LANES, LANES), 1)
    offset = query - key
    seen = ((key >> 2) == (query >> 2)) & (offset >= 0)
    for head in range(HEADS):
        lanes = slice(head * LANES, (head + 1) * LANES)
        table = jnp.full((LANES, LANES), -1e30, f32)
        for b in range(LEVELS):
            table = jnp.where(seen & (offset == b), bias_ref[head, 1, b], table)
        dbias_s[:, lanes] = table

    def transpose_weights(which, first, last):
        def one(block, carry):
            place = pl.ds(pl.multiple_of(block * LANES, LANES), LANES)
            wt_s[which, place, :] = wn_s[which, :, place].T
            return carry

        lax.fori_loop(first, last, one, 0, unroll=2)

    transpose_weights(section, 0, BLOCKS)
    beside[0].wait()
    transpose_weights(1 - section, 0, FIRST // LANES)

    def rest_arrives():
        over[1].wait()
        beside[1].start()
        beside[1].wait()
        transpose_weights(1 - section, FIRST // LANES, BLOCKS)

    def gain(g, width):
        column = gain_s[g]
        return column if width == LANES else jnp.concatenate([column] * (width // LANES), 1)

    def lockstep(steps, point=None):
        for number, _ in enumerate(zip(*steps)):
            if point is not None:
                point(number)

    def at_time(t, steps):
        for time, step in enumerate(steps):
            if step is not None:
                pl.when(t == time)(step)

    def spread_low(x):
        return jnp.concatenate([part.astype(bf16) for part in unpack(x)], 1)

    def packed(x):
        return pack([x[:, i * LANES : (i + 1) * LANES] for i in range(GROUP)])

    def part_of(j):
        return slice(j * LANES, (j + 1) * LANES)

    def encode_steps(t, half):
        c = 2 * t + half
        qkv, o, r = qkv_s[half], o_s[half], r_s[half]
        x0 = x0_s[c]
        h = spread_low(x0 * inverse_rms(x0) * gain(0, WIDE))
        yield
        for j in range(3):
            part = slice(j * WIDTH, (j + 1) * WIDTH)
            qkv[t, part, :] = mul(wt_s[0, part, :], h).astype(bf16)
        yield
        for first in range(0, GROUP, BATCH):
            queries, keys, values = [], [], []
            for i in range(first, first + BATCH):
                lanes = slice(i * LANES, (i + 1) * LANES)
                queries += [qkv[t, part_of(j), lanes] for j in range(PAIRS)]
                keys += [qkv[t, part_of(PAIRS + j), lanes].T[:KEYS] for j in range(PAIRS)]
                values += [qkv[t, part_of(2 * PAIRS + j), lanes] for j in range(PAIRS)]
            bias = jnp.concatenate([ebias_s[...]] * BATCH, 1)
            chance, mixed = attend(keys, queries, values, bias)
            for i in range(BATCH):
                lanes = slice((first + i) * LANES, (first + i + 1) * LANES)
                own = slice(i * HEADS * LANES, (i + 1) * HEADS * LANES)
                p_s[half][t, first + i] = chance[:, own]
                o[t, :, lanes] = jnp.concatenate(mixed[i * PAIRS : (i + 1) * PAIRS], 0)
            yield
        x1 = x0 + packed(mul(wn_s[0, :, 3 * WIDTH : 4 * WIDTH], o[t]))
        x1_s[half][t] = x1
        yield
        h = norm_low(x1, inverse_rms(x1), gain(1, WIDE))
        for j in range(2):
            part = slice(j * FF // 2, (j + 1) * FF // 2)
            lifted = mul(wt_s[0, MIXW + j * FF // 2 : MIXW + (j + 1) * FF // 2, :], h)
            r[t, part, :] = jnp.maximum(lifted, 0.0).astype(bf16)
        yield
        x2 = x1 + mul(wn_s[0, :, MIXW + FF :], r[t])
        put_wide(x2_s, c, x2)
        e = norm_low(x2, inverse_rms(x2), gain(2, WIDE))
        yield
        for j in range(2):
            part = slice(j * WIDTH, (j + 1) * WIDTH)
            mem_s[half][t, part, :] = mul(
                wt_s[0, 4 * WIDTH + j * WIDTH : 4 * WIDTH + (j + 1) * WIDTH, :], e
            ).astype(bf16)
        yield

    attention = GROUP // BATCH
    pairs = chunks // 2

    def early_at(place, places):
        return [
            functools.partial(early_step, place + places * t)
            if place + places * t <= depth
            else None
            for t in range(pairs)
        ]

    def encode(t, carry):
        at_time(t, early_at(0, 3))

        def point(number):
            if number == attention // 2:
                at_time(t, early_at(1, 3))
            if number == attention + 2:
                pl.when(t == 0)(rest_arrives)
                at_time(t, early_at(2, 3))

        lockstep([encode_steps(t, 0), encode_steps(t, 1)], point)
        return carry

    def put_wide(ref, c, value):
        for i in range(COLUMNS):
            ref[pl.ds(pl.multiple_of((COLUMNS * c + i) * D, D), D), :] = value[
                :, i * LANES : (i + 1) * LANES
            ]

    def get_wide(ref, c):
        return jnp.concatenate(
            [ref[pl.ds(pl.multiple_of((COLUMNS * c + i) * D, D), D), :] for i in range(COLUMNS)], 1
        )

    lax.fori_loop(0, pairs, encode, 0)
    for j in range(3 * pairs, depth + 1):
        early_step(j)
    out_stat_ref[...] = stat_s[depth, :8, :]

    def put_blocks(first, value):
        for index in range(value.shape[1] // LANES):
            block = first + index
            part = value[:, index * LANES : (index + 1) * LANES].astype(bf16)
            if block < FIRST // LANES:
                first_s[1, block * D : (block + 1) * D, :] = part
            else:
                block -= FIRST // LANES
                rest_s[1, block * D : (block + 1) * D, :] = part

    def add_blocks(first, value):
        for index in range(value.shape[1] // LANES):
            g0_s[first + index] += value[:, index * LANES : (index + 1) * LANES]

    start = onehot(start_ids, CODES)
    both = mul(ext_s[:, :CODES], start)
    y0 = both[:D] + both[D:]
    inverse0 = inverse_rms(y0)
    h0 = norm_low(y0, inverse0, gain(3, LANES))
    dz_s[:, :LANES] = mul(wt_s[1, : 3 * WIDTH, :], h0).astype(bf16)
    both = mul(mul_t(eye, h0).astype(bf16), wn_s[1, :, WIDTH : 3 * WIDTH]).astype(bf16)
    self_chance, mixed = attend(
        [both[:, part_of(j)] for j in range(PAIRS)],
        [dz_s[part_of(j), :LANES] for j in range(PAIRS)],
        [dz_s[part_of(2 * PAIRS + j), :LANES] for j in range(PAIRS)],
        dbias_s[...],
    )
    self_values = both[:, WIDTH:]
    self_mixed = jnp.concatenate(mixed, 0)
    y1 = y0 + mul(wn_s[1, :, 3 * WIDTH : 4 * WIDTH], self_mixed)
    inverse1 = inverse_rms(y1)
    h1 = norm_low(y1, inverse1, gain(4, LANES))
    cross_s[...] = mul(wt_s[1, 4 * WIDTH : 5 * WIDTH, :], h1).astype(bf16)

    def spreader(g, turned):
        shape = (LANES, 32 * GROUP) if turned else (32 * GROUP, LANES)
        row, token = iota(shape, 1 if turned else 0), iota(shape, 0 if turned else 1)
        hit = token == 4 * GROUP * g + 4 * (row >> 5) + (row & 3)
        return jnp.where(hit, 1.0, 0.0).astype(bf16)

    def rows_of(g, table):
        rows = mul_t(spreader(g, False), table)
        mask = (iota(rows.shape, 1) >> 6) == ((iota(rows.shape, 0) & 31) >> 2)
        return jnp.where(mask, rows, 0.0).astype(bf16)

    def head_mask(shape):
        return (iota(shape, 0) >> 6) == ((iota(shape, 1) & 31) >> 2)

    def rows_t_of(g, table):
        rows = mul(table, spreader(g, True))
        return jnp.where(head_mask(rows.shape), rows, 0.0).astype(bf16)

    def gather_rows(ref):
        total = jnp.zeros((WIDTH, LANES), f32)
        for g in range(chunks):
            total = total + mul(ref[g % 2][g // 2], spreader(g, False))
        return total.astype(bf16)

    def blocks_of(table):
        rows = []
        for i in range(GROUP):
            part = table[32 * i : 32 * i + 32]
            column, shift = divmod(PACK * i, LANES)
            part = turn(part, shift)
            lane = iota(part.shape, 1)
            zero = jnp.zeros_like(part)
            columns = [zero] * COLUMNS
            columns[column] = jnp.where(lane >= shift, part, 0.0)
            if shift > LANES - PACK:
                columns[column + 1] = jnp.where(lane < shift, part, 0.0)
            rows.append(jnp.concatenate(columns, 1))
        return jnp.concatenate(rows, 0).astype(bf16)

    def row_products(rows, keys):
        both = mul(rows, keys)
        parts = []
        for i in range(GROUP):
            own = both[32 * i : 32 * i + 32]
            column, shift = divmod(PACK * i, LANES)
            part = turn(own[:, column * LANES : (column + 1) * LANES], -shift)
            if shift > LANES - PACK:
                after = turn(own[:, (column + 1) * LANES : (column + 2) * LANES], -shift)
                part = jnp.where(iota(part.shape, 1) < LANES - shift, part, after)
            parts.append(part)
        return jnp.concatenate(parts, 0)

    def cross_steps(t, half):
        g = 2 * t + half
        queries = rows_of(g, cross_s[...])
        yield
        scores = row_products(queries, mem_s[half][t, :WIDTH, :])
        scores = jnp.where(iota(scores.shape, 1) < HIST_LEN, scores, -1e30)
        chance = jnp.exp(scores - jnp.max(scores, axis=1, keepdims=True))
        chance = chance * (1.0 / jnp.sum(chance, axis=1, keepdims=True))
        pc_s[half][t] = chance
        yield
        mixed = mul_t(mem_s[half][t, WIDTH:, :], blocks_of(chance))
        oc_s[half][t] = jnp.where(head_mask(mixed.shape), mixed, 0.0).astype(bf16)
        yield

    def cross(t, carry):
        lockstep([cross_steps(t, 0), cross_steps(t, 1)])
        return carry

    lax.fori_loop(0, pairs, cross, 0)
    cross_mixed = gather_rows(oc_s)
    y2 = y1 + mul(wn_s[1, :, 5 * WIDTH : 6 * WIDTH], cross_mixed)
    inverse2 = inverse_rms(y2)
    h2 = norm_low(y2, inverse2, gain(5, LANES))
    lifted = mul(wt_s[1, MIXW : MIXW + FF, :], h2)
    active = jnp.maximum(lifted, 0.0).astype(bf16)
    y3 = y2 + mul(wn_s[1, :, MIXW + FF :], active)
    inverse3 = inverse_rms(y3)
    final = norm_low(y3, inverse3, gain(6, LANES))
    logits = mul(codes_s[...], final)
    top = jnp.max(logits, axis=0, keepdims=True)
    log_total = top + jnp.log(jnp.sum(jnp.exp(logits - top), axis=0, keepdims=True))
    match = iota(logits.shape, 0) == goal
    picked = jnp.sum(jnp.where(match, logits, 0.0), axis=0, keepdims=True)
    weight = jnp.zeros((1, LANES), f32)
    for d in range(DOMAINS):
        share = 1.0 / (DOMAINS * jnp.maximum(stat_s[depth, 8 + d : 9 + d, :], 1.0))
        weight = weight + jnp.where(domain == d, share, 0.0)
    loss = jnp.sum(weight * (log_total - picked), axis=1, keepdims=True)
    back_logits = (
        weight * (jnp.exp(logits - log_total) - jnp.where(match, 1.0, 0.0))
    ).astype(bf16)
    back_final = mul(ext_s[:D, :CODES], back_logits)
    table_grad = mul_t(back_logits, final)
    back, gain_grad = norm_back(y3, inverse3, gain(6, LANES), back_final)
    ggain_s[6] = gain_grad
    low = back.astype(bf16)
    put_blocks(26, mul_t(low, active))
    back_lifted = jnp.where(lifted > 0, mul(wt_s[1, MIXW + FF :, :], low), 0.0).astype(bf16)
    put_blocks(18, mul_t(h2, back_lifted))
    more, gain_grad = norm_back(
        y2, inverse2, gain(5, LANES), mul(wn_s[1, :, MIXW : MIXW + FF], back_lifted)
    )
    ggain_s[5] = gain_grad
    back = back + more
    low = back.astype(bf16)
    put_blocks(15, mul_t(low, cross_mixed))
    cross_back_s[...] = mul(wt_s[1, 5 * WIDTH : 6 * WIDTH, :], low).astype(bf16)

    def cross_back_steps(t, half):
        g = 2 * t + half
        memory = mem_s[half]
        mixed_rows = rows_of(g, cross_back_s[...])
        queries_t = rows_t_of(g, cross_s[...])
        mixed_t = rows_t_of(g, cross_back_s[...])
        yield
        back_chance = row_products(mixed_rows, memory[t, WIDTH:, :])
        back_chance = jnp.where(iota(back_chance.shape, 1) < HIST_LEN, back_chance, 0.0)
        chance = pc_s[half][t]
        inner = jnp.sum(back_chance * chance, axis=1, keepdims=True)
        yield
        spread = blocks_of(chance * (back_chance - inner))
        total = mul_t(memory[t, :WIDTH, :], spread)
        oc_s[half][t] = jnp.where(head_mask(total.shape), total, 0.0).astype(bf16)
        yield
        memory[t, :WIDTH, :] = mul(queries_t, spread).astype(bf16)
        memory[t, WIDTH:, :] = mul(mixed_t, blocks_of(chance)).astype(bf16)
        yield

    def cross_back(t, carry):
        lockstep([cross_back_steps(t, 0), cross_back_steps(t, 1)])
        return carry

    lax.fori_loop(0, pairs, cross_back, 0)
    back_query = gather_rows(oc_s)
    put_blocks(12, mul_t(h1, back_query) * HEAD_DIM**-0.5)
    more, gain_grad = norm_back(
        y1, inverse1, gain(4, LANES), mul(wn_s[1, :, 4 * WIDTH : 5 * WIDTH], back_query)
    )
    ggain_s[4] = gain_grad
    back = back + more
    low = back.astype(bf16)
    put_blocks(9, mul_t(low, self_mixed))
    back_mixed = mul(wt_s[1, 3 * WIDTH : 4 * WIDTH, :], low).astype(bf16)
    *back_parts, self_scores = attend_back(
        [dz_s[part_of(PAIRS + j), :LANES] for j in range(PAIRS)],
        [dz_s[part_of(j), :LANES] for j in range(PAIRS)],
        [self_values[:, part_of(j)] for j in range(PAIRS)],
        [back_mixed[part_of(j)] for j in range(PAIRS)],
        self_chance,
    )
    dz_s[:, LANES:] = jnp.concatenate([x for part in back_parts for x in part], 0)
    put_blocks(0, mul_t(h0, dz_s[:WIDTH, LANES : 2 * LANES]) * HEAD_DIM**-0.5)
    put_blocks(3, mul_t(h0, dz_s[WIDTH:, LANES : 2 * LANES]))
    more, gain_grad = norm_back(
        y0, inverse0, gain(3, LANES), mul(wn_s[1, :, : 3 * WIDTH], dz_s[:, LANES : 2 * LANES])
    )
    ggain_s[3] = gain_grad
    back = back + more
    spread = mul_t(start, split_low(back))
    ge_s[:CODES, :] = table_grad + spread[:, :D] + spread[:, D:]
    ge_s[CODES:, :] = jnp.zeros((n, D), f32)
    rows_s[...] = jnp.zeros_like(rows_s)
    for head in range(HEADS):
        lanes = slice(head * LANES, (head + 1) * LANES)
        for b in range(LEVELS):
            hit = jnp.where(offset == b, self_scores[:, lanes], 0.0)
            rows_s[head, BUCKETS + b : BUCKETS + b + 1, :] = jnp.sum(hit, axis=0, keepdims=True)

    def reducing(buffer, kept, held, upto):
        steps, at = [], 0
        for k, stage in enumerate(order[:upto]):
            rows, left = held[k], held[k + 1]
            side = side_of(stage)
            if left < rows:
                source = buffer.at[span(at + (1 - side) * left, left)]
                at = at + side * left
            else:
                source = buffer.at[span(at, rows)]
            steps.append((remote(source, kept[k], stage), at, left))
        return steps, at, held

    def begin(steps, k):
        steps[k][0].start()

    def finish(steps, buffer, kept, k):
        copy, at, left = steps[k]
        copy.wait()
        place = span(at, left)
        total = buffer[place, :].astype(f32) + kept[k][...].astype(f32)
        buffer[place, :] = total.astype(bf16)

    flat_depth = depth - 1
    held_rest, held_first, held_codes = shares(dp, REST), shares(dp, FIRST), shares(dp, CODES, 1)
    land, rest = {}, lands
    for name, number in (
        ("rest0", flat_depth),
        ("rest1", flat_depth),
        ("first1", flat_depth),
        ("first0", len(far)),
        ("codes", len(far)),
    ):
        land[name], rest = rest[:number], rest[number:]
    land_rest, land_first = rest
    rest1 = reducing(rest_s.at[1], land["rest1"], held_rest, flat_depth)
    first1 = reducing(first_s.at[1], land["first1"], held_first, flat_depth)
    rest0 = reducing(rest_s.at[0], land["rest0"], held_rest, flat_depth)
    first0 = reducing(first_s.at[0], land["first0"], held_first, len(far))
    codes = reducing(codes_s, land["codes"], held_codes, len(far))

    def step1(k):
        if k > 0:
            finish(rest1[0], rest_s.at[1], land["rest1"], k - 1)
            finish(first1[0], first_s.at[1], land["first1"], k - 1)
        if k < flat_depth:
            begin(rest1[0], k)
            begin(first1[0], k)

    def crossing(buffer, target, at, rows):
        source = buffer.at[1 - section, span(at, rows)]
        return remote(source, target, across)

    cross_rest = crossing(rest_s, land_rest, rest1[1], rest1[2][-1])
    cross_first = crossing(first_s, land_first, first1[1], first1[2][-1])

    def settle(copy, buffer, landed, at, rows, base):
        copy.wait()
        value = (buffer[section, span(at, rows), :].astype(f32) + landed[...].astype(f32)).astype(
            bf16
        )
        out_ref[span(base + at, rows), :] = value
        value = value.astype(f32)
        return jnp.sum(value * value, axis=0, keepdims=True)

    def gathering(base, at, held):
        steps = []
        for k in reversed(range(flat_depth)):
            rows, left = held[k], held[k + 1]
            if left < rows:
                place = out_ref.at[span(base + at, left)]
                steps.append(remote(place, place, order[k]))
                at = at - side_of(order[k]) * left
            else:
                steps.append(None)
        return steps

    gather_rest = gathering(0, rest1[1], rest1[2])

    def step0(k):
        if k > 0 and k <= flat_depth:
            finish(rest0[0], rest_s.at[0], land["rest0"], k - 1)
        if k < flat_depth:
            begin(rest0[0], k)
        if k == flat_depth:
            cross_rest.start()
        if k == flat_depth + 1:
            squares = settle(cross_rest, rest_s, land_rest, rest1[1], rest1[2][-1], 0)
            own_slot_s[16:17, :] = squares / (dp * rest1[2][-1] // REST)
        if k > flat_depth + 1 and gather_rest[k - flat_depth - 2] is not None:
            gather_rest[k - flat_depth - 2].wait()
        if flat_depth < k < 2 * flat_depth + 1 and gather_rest[k - flat_depth - 1] is not None:
            gather_rest[k - flat_depth - 1].start()

    g0_s[...] = jnp.zeros_like(g0_s)
    gbias_s[...] = jnp.zeros_like(gbias_s)
    for g in range(3):
        ggain_s[g] = jnp.zeros((D, LANES), f32)

    def fold(x):
        return sum(x[:, i * LANES : (i + 1) * LANES] for i in range(COLUMNS))

    def rest_steps(t, half):
        c = 2 * t + half
        r = r_s[half]
        x2 = get_wide(x2_s, c)
        inverse = inverse_rms(x2)
        back_memory = mem_s[half][t]
        add_blocks(12, mul_t(norm_low(x2, inverse, gain(2, WIDE)), back_memory))
        back_normed = mul(wn_s[0, :, 4 * WIDTH : 6 * WIDTH], back_memory)
        yield
        back, gain_grad = norm_back(x2, inverse, gain(2, WIDE), back_normed)
        ggain_s[2] += fold(gain_grad)
        low = back.astype(bf16)
        yield
        add_blocks(26, mul_t(low, r[t]))
        for j in range(4):
            part = slice(j * FF // 4, (j + 1) * FF // 4)
            back_active = mul(wt_s[0, MIXW + FF + part.start : MIXW + FF + part.stop, :], low)
            live = r[t, part, :].astype(f32) > 0
            r[t, part, :] = jnp.where(live, back_active, 0.0).astype(bf16)
        yield
        x1 = x1_s[half][t]
        inverse = inverse_rms(x1)
        add_blocks(18, mul_t(norm_low(x1, inverse, gain(1, WIDE)), r[t]))
        back_normed = mul(wn_s[0, :, MIXW : MIXW + FF], r[t])
        yield
        more, gain_grad = norm_back(x1, inverse, gain(1, WIDE), back_normed)
        ggain_s[1] += fold(gain_grad)
        put_wide(x2_s, c, back + more)
        yield

    places1 = {0: 0, 1: 1, 3: 2, 5: 3}
    places0 = {0: 0, 1: 1, 2: 2, 3: 3, 4: 4, 5: 5, 6: 6, 7: 7, 9: 8}
    steps0 = 2 * flat_depth + 2

    def placed(places, step, place, each):
        return [
            functools.partial(step, places[place + each * t])
            if place + each * t in places
            else None
            for t in range(pairs)
        ]

    def back_rest(t, carry):
        at_time(t, placed(places1, step1, 0, 3))

        def point(number):
            if number in (1, 3):
                at_time(t, placed(places1, step1, (number + 1) // 2, 3))

        lockstep([rest_steps(t, 0), rest_steps(t, 1)], point)
        return carry

    lax.fori_loop(0, pairs, back_rest, 0)
    def cast_rest(block, carry):
        place = pl.ds(pl.multiple_of(block * D, D), D)
        rest_s[0, place, :] = g0_s[FIRST // D + block].astype(bf16)
        return carry

    lax.fori_loop(0, REST // D, cast_rest, 0, unroll=2)
    for j in range(4, flat_depth + 1):
        step1(j)

    def first_steps(t, half):
        c = 2 * t + half
        qkv, o, dqkv = qkv_s[half], o_s[half], dqkv_s[half]
        back = get_wide(x2_s, c)
        lane = iota((D, LANES), 1)
        low = [jnp.where(lane < PACK, part, 0.0).astype(bf16) for part in unpack(back)]
        low = jnp.concatenate(low, 1)
        yield
        add_blocks(9, mul_t(low, o[t]))
        o[t] = mul(wt_s[0, 3 * WIDTH : 4 * WIDTH, :], low).astype(bf16)
        yield
        for first in range(0, GROUP, BATCH):
            queries, keys, values, backs = [], [], [], []
            for i in range(first, first + BATCH):
                lanes = slice(i * LANES, (i + 1) * LANES)
                queries += [qkv[t, part_of(j), lanes] for j in range(PAIRS)]
                keys += [qkv[t, part_of(PAIRS + j), lanes] for j in range(PAIRS)]
                values += [qkv[t, part_of(2 * PAIRS + j), lanes].T[:KEYS] for j in range(PAIRS)]
                backs += [o[t, part_of(j), lanes] for j in range(PAIRS)]
            chance = [p_s[half][t, first + i] for i in range(BATCH)]
            *results, scores = attend_back(
                keys, queries, values, backs, jnp.concatenate(chance, 1)
            )
            for i in range(BATCH):
                lanes = slice((first + i) * LANES, (first + i + 1) * LANES)
                own = slice(i * PAIRS, (i + 1) * PAIRS)
                dqkv[:, lanes] = jnp.concatenate([x for part in results for x in part[own]], 0)
            width = HEADS * LANES
            gbias_s[...] += sum(scores[:, i * width : (i + 1) * width] for i in range(BATCH))
            yield
        x0 = x0_s[c]
        inverse = inverse_rms(x0)
        add_blocks(0, mul_t(spread_low(x0 * inverse * gain(0, WIDE)), dqkv[...]))
        back_normed = packed(mul(wn_s[0, :, : 3 * WIDTH], dqkv[...]))
        yield
        more, gain_grad = norm_back(x0, inverse, gain(0, WIDE), back_normed)
        ggain_s[0] += fold(gain_grad)
        find(c)
        spread = mul_t(hot_s[...], split_low(back + more))
        ge_s[...] += spread[:, :D] + spread[:, D:]
        yield

    def back_first(t, carry):
        at_time(t, placed(places0, step0, 0, 5))

        def point(number):
            place = {1: 1, attention // 2 + 1: 2, attention + 1: 3, attention + 2: 4}.get(number)
            if place is not None:
                at_time(t, placed(places0, step0, place, 5))

        lockstep([first_steps(t, 0), first_steps(t, 1)], point)
        return carry

    lax.fori_loop(0, pairs, back_first, 0)

    def cast_first(block, carry):
        place = pl.ds(pl.multiple_of(block * D, D), D)
        factor = jnp.where(block < 3, scale, 1.0)
        first_s[0, place, :] = (g0_s[block] * factor).astype(bf16)
        return carry

    lax.fori_loop(0, FIRST // D, cast_first, 0, unroll=2)
    codes_s[...] = ge_s[:CODES, :].astype(bf16)
    begin(first0[0], 0)
    begin(codes[0], 0)
    user_low_s[...] = ge_s[CODES:, :].astype(bf16)
    store_users = pltpu.make_async_copy(
        user_low_s, out_user_ref.at[span(slot * n, n)], local_sems.at[BLOCKS + 2]
    )
    store_users.start()
    late = list(range(9, steps0))
    if late:
        step0(late.pop(0))

    ones = jnp.ones((8, LANES), f32)
    own_slot_s[8:16, :] = jnp.zeros((8, LANES), f32)
    for g in range(7):
        own_slot_s[g : g + 1, :] = mul_exact_t(ones, ggain_s[g])[:1]
    own_slot_s[7:8, :] = jnp.broadcast_to(loss, (1, LANES))

    def bucket_sums(b, carry):
        for head in range(HEADS):
            lanes = slice(head * LANES, (head + 1) * LANES)
            hit = jnp.where(buckets == b, gbias_s[:, lanes], 0.0)
            rows_s[head, pl.ds(b, 1), :] = jnp.sum(hit, axis=0, keepdims=True)
        return carry

    lax.fori_loop(0, BUCKETS, bucket_sums, 0, unroll=2)
    for head in range(HEADS):
        sums = mul_exact_t(ones, rows_s[head])
        own_slot_s[8 + head : 9 + head, : 2 * BUCKETS] = sums[:1]
    own_slot_s[19:, :] = jnp.zeros((5, LANES), f32)

    for k in range(len(far)):
        finish(first0[0], first_s.at[0], land["first0"], k)
        finish(codes[0], codes_s, land["codes"], k)
        if k + 1 < len(far):
            begin(first0[0], k + 1)
            begin(codes[0], k + 1)

    first_at, first_left = first0[1], held_first[len(far) + 1 :]
    codes_at, codes_left = codes[1], held_codes[len(far) + 1 :]
    size, code_size = first_left[-1], codes_left[-1]
    mine_first = first_at + shift_of(0, first_left)
    mine_codes = codes_at + shift_of(0, codes_left)
    inside, crossing_first, everyone = [], [], []
    for mask in masks:
        source = first_s.at[0, span(first_at + shift_of(mask, first_left), size)]
        copy = remote_to(source, near_first.at[mask], device_of(mask))
        (crossing_first if mask >> (NEAR - 1) else inside).append(copy)
    for mask in masks:
        source = codes_s.at[span(codes_at + shift_of(mask, codes_left), code_size)]
        everyone.append(remote_to(source, near_codes.at[mask], device_of(mask)))
    store_users.wait()
    held = out_user_ref.at[span(slot * n, n)]
    users_out = [remote_to(held, held, device_of(mask)) for mask in masks]

    @pl.when(section == 0)
    def _():
        for copy in inside:
            copy.start()
        cross_first.start()

    @pl.when(section == 1)
    def _():
        for copy in crossing_first:
            copy.start()

    for copy in everyone + users_out:
        copy.start()
    for step in late:
        step0(step)

    def keep_first(value):
        value = value.astype(bf16)
        out_ref[span(REST + mine_first, size), :] = value
        value = value.astype(f32)
        squares = jnp.sum(value * value, axis=0, keepdims=True)
        own_slot_s[17:18, :] = squares / (dp * size // FIRST)

    @pl.when(section == 0)
    def _():
        for copy in inside:
            copy.wait()
        for copy in crossing_first:
            copy.wait_recv()
        cross_first.wait_send()
        value = first_s[0, span(mine_first, size), :].astype(f32)
        for mask in masks:
            value = value + near_first[mask].astype(f32)
        keep_first(value)

    @pl.when(section == 1)
    def _():
        for copy in crossing_first:
            copy.wait_send()
        cross_first.wait_recv()
        value = first_s[1, span(mine_first, size), :].astype(f32)
        keep_first(value + land_first[...].astype(f32))

    for copy in everyone:
        copy.wait()
    value = codes_s[span(mine_codes, code_size), :].astype(f32)
    for mask in masks:
        value = value + near_codes[mask].astype(f32)
    value = value.astype(bf16)
    out_ref[span(COLS + mine_codes, code_size), :] = value
    value = value.astype(f32)
    squares = jnp.sum(value * value, axis=0, keepdims=True)
    own_slot_s[18:19, :] = squares / (2 * dp * code_size // CODES)

    store_slot = pltpu.make_async_copy(
        own_slot_s, out_slot_ref.at[slot], local_sems.at[BLOCKS + 3]
    )
    store_slot.start()

    copies = []
    place = out_ref.at[span(REST + mine_first, size)]
    code_place = out_ref.at[span(COLS + mine_codes, code_size)]
    for mask in masks:
        device = device_of(mask)
        if not mask >> (NEAR - 1):
            copies.append(remote_to(place, place, device))
        copies.append(remote_to(code_place, code_place, device))
    for copy in copies:
        copy.start()
    store_slot.wait()
    held = out_slot_ref.at[slot]
    slots_out = [remote_to(held, held, device_of(mask)) for mask in masks]
    for copy in slots_out:
        copy.start()
    copies += slots_out
    for copy in copies + users_out:
        copy.wait()
    for j, k in enumerate(reversed(range(len(far)))):
        stage = far[k]
        copies = []
        if held_first[k + 1] < held_first[k]:
            place = out_ref.at[span(REST + first_at, held_first[k + 1])]
            copies.append(remote(place, place, stage))
            first_at = first_at - side_of(stage) * held_first[k + 1]
        if held_codes[k + 1] < held_codes[k]:
            place = out_ref.at[span(COLS + codes_at, held_codes[k + 1])]
            copies.append(remote(place, place, stage))
            codes_at = codes_at - side_of(stage) * held_codes[k + 1]
        slots = 2 ** (NEAR + j)
        first_slot = lax.div(slot, slots) * slots
        held = out_slot_ref.at[pl.ds(first_slot, slots)]
        copies.append(remote(held, held, stage))
        held = out_user_ref.at[span(first_slot * n, slots * n)]
        copies.append(remote(held, held, stage))
        for copy in copies:
            copy.start()
        for copy in copies:
            copy.wait()


def gradients(codes, users, targets, domains, bias, gains, mixer, feed, embedding, dp):
    n = users.shape[0] // 2
    chunks = n // GROUP
    order = stages(dp)
    depth = len(order)
    devices = 2 * dp
    vmem = pl.BlockSpec(memory_space=pltpu.VMEM)
    smem = pl.BlockSpec(memory_space=pltpu.SMEM)
    hbm = pl.BlockSpec(memory_space=pl.ANY)
    stat = (16, LANES)
    held_rest, held_first, held_codes = shares(dp, REST), shares(dp, FIRST), shares(dp, CODES, 1)
    plane, far = depth - 1, depth - NEAR
    sizes = [*held_rest[1:] * 2, *held_first[1:]]
    sizes += [*held_first[1 : far + 1], *held_codes[1 : far + 1], held_rest[-1], held_first[-1]]
    lands = [pltpu.VMEM((rows, D), bf16) for rows in sizes]
    copies = 128 + 16 * depth
    return pl.pallas_call(
        functools.partial(step_kernel, n, dp),
        out_shape=(
            jax.ShapeDtypeStruct((COLS + CODES, D), bf16),
            jax.ShapeDtypeStruct((devices * n, D), bf16),
            jax.ShapeDtypeStruct((devices, 8, LANES), jnp.int32),
            jax.ShapeDtypeStruct((devices, 24, LANES), f32),
            jax.ShapeDtypeStruct((8, LANES), f32),
        ),
        in_specs=[vmem, smem, vmem, vmem, vmem, smem, vmem, hbm, hbm, hbm],
        out_specs=(vmem, hbm, hbm, hbm, vmem),
        scratch_shapes=[pltpu.VMEM((chunks, D, WIDE), f32)]
        + [
            pltpu.VMEM(shape, dtype)
            for shape, dtype in (
                ((chunks // 2, D, WIDE), f32),
                ((chunks // 2, 3 * WIDTH, SPAN), bf16),
                ((chunks // 2, GROUP, KEYS, HEADS * LANES), bf16),
                ((chunks // 2, WIDTH, SPAN), bf16),
                ((chunks // 2, FF, WIDE), bf16),
                ((chunks // 2, 2 * WIDTH, WIDE), bf16),
                ((3 * WIDTH, SPAN), bf16),
                ((chunks // 2, 32 * GROUP, LANES), f32),
                ((chunks // 2, WIDTH, 32 * GROUP), bf16),
            )
            for _ in range(2)
        ]
        + [
            pltpu.VMEM((chunks * COLUMNS * D, LANES), f32),
            pltpu.VMEM((3 * WIDTH, 2 * LANES), bf16),
            pltpu.VMEM((2, D, COLS), bf16),
            pltpu.VMEM((2, COLS, D), bf16),
            pltpu.VMEM((2 * D, CODES + n), bf16),
            pltpu.VMEM((7, D, LANES), f32),
            pltpu.VMEM((KEYS, HEADS * LANES), f32),
            pltpu.VMEM((LANES, HEADS * LANES), f32),
            pltpu.VMEM((BLOCKS, D, LANES), f32),
            pltpu.VMEM((CODES + n, D), f32),
            pltpu.VMEM((KEYS, HEADS * LANES), f32),
            pltpu.VMEM((7, D, LANES), f32),
            pltpu.VMEM((HEADS, 2 * BUCKETS, LANES), f32),
            pltpu.VMEM((n, D), f32),
            pltpu.VMEM((n, LANES), jnp.int32),
            pltpu.VMEM((WIDTH, LANES), bf16),
            pltpu.VMEM((WIDTH, LANES), bf16),
            pltpu.VMEM((2, REST, D), bf16),
            pltpu.VMEM((2, FIRST, D), bf16),
            pltpu.VMEM((CODES, D), bf16),
            pltpu.VMEM((8, LANES), jnp.int32),
            pltpu.VMEM((n, D), bf16),
            pltpu.VMEM((24, LANES), f32),
            pltpu.VMEM((8, WIDE), jnp.int32),
            pltpu.VMEM((CODES + n, WIDE), bf16),
            pltpu.VMEM((depth + 1,) + stat, f32),
            pltpu.VMEM((depth,) + stat, f32),
            pltpu.VMEM((2**NEAR, held_first[-1], D), bf16),
            pltpu.VMEM((2**NEAR, held_codes[-1], D), bf16),
            pltpu.SemaphoreType.DMA((BLOCKS + 4,)),
            pltpu.SemaphoreType.DMA((copies,)),
            pltpu.SemaphoreType.DMA((copies,)),
        ]
        + lands,
        compiler_params=pltpu.CompilerParams(
            collective_id=0, has_side_effects=True, vmem_limit_bytes=127 * 2**19
        ),
        name="gradients",
    )(codes, users, users.reshape(1, -1), targets, domains, bias, gains, mixer, feed, embedding)


def adam(weight, moment, square, slope, rate, decay):
    moment = beta_one * moment + (1 - beta_one) * slope
    square = beta_two * square + (1 - beta_two) * slope * slope
    unbiased_moment = moment * (1 / (1 - beta_one**STEP))
    unbiased_square = square * (1 / (1 - beta_two**STEP))
    root = unbiased_square * lax.rsqrt(unbiased_square)
    divisor = root + adam_eps
    inverse = pl.reciprocal(divisor, approx=True)
    inverse = inverse * (2.0 - divisor * inverse)
    step = unbiased_moment * inverse + decay * weight
    return weight - rate * step, moment, square


def update_kernel(*refs):
    parts_in, big_in, small_in, refs = refs[:5], refs[5:14], refs[14:20], refs[20:]
    loss_ref, norm_ref, section_ref, hist_ref = refs[:4]
    big_out, small_out, low_out, refs = refs[4:13], refs[13:19], refs[19:22], refs[22:]
    parts, hold, low_hold = refs[:5], refs[5:14], refs[14:17]
    user_grad, part_sems, in_sems, out_sems = refs[17:]
    grad_ref, user_ref, ids_ref, slot_ref, stat_ref = parts
    arrivals = [pltpu.make_async_copy(parts_in[i], parts[i], part_sems.at[i]) for i in range(5)]
    loads = [pltpu.make_async_copy(big_in[i], hold[i], in_sems.at[i]) for i in range(9)]
    for load in arrivals[1:] + arrivals[:1] + loads:
        load.start()
    for arrival in arrivals:
        arrival.wait()

    users = user_grad.shape[0]
    span = min(1024, user_ref.shape[0])
    slots = span // LANES * (ids_ref.shape[0] * LANES // user_ref.shape[0])
    fit = ids_ref.shape[0] * LANES // user_ref.shape[0]
    user_grad[...] = jnp.zeros_like(user_grad)

    def scatter(part, carry):
        rows = user_ref[pl.ds(pl.multiple_of(part * span, span), span), :]
        lanes = []
        for group in range(span // LANES):
            total = ids_ref[part * slots + group * fit, :1, :]
            for other in range(1, fit):
                total = total + ids_ref[part * slots + group * fit + other, :1, :]
            lanes.append(total)
        ids = jnp.concatenate(lanes, 1)
        def block_rows(block, carry):
            place = pl.ds(pl.multiple_of(block * USER_ROWS, 8), USER_ROWS)
            hit = iota((USER_ROWS, span), 0) + block * USER_ROWS == ids
            user_grad[place, :] += mul(jnp.where(hit, 1.0, 0.0).astype(bf16), rows)
            return carry

        lax.fori_loop(0, users // USER_ROWS, block_rows, 0)
        return carry

    lax.fori_loop(0, user_ref.shape[0] // span, scatter, 0)

    def total(x):
        return jnp.sum(jnp.sum(x, axis=0, keepdims=True), axis=1, keepdims=True)

    def slot_sum(first):
        def add(i, value):
            return value + slot_ref[2 * i + first]

        zero = jnp.zeros(slot_ref.shape[1:], f32)
        return lax.fori_loop(0, slot_ref.shape[0] // 2, add, zero)

    even, odd = slot_sum(0), slot_sum(1)
    section_squares = [total(x[16:17] + x[17:18]) for x in (even, odd)]
    small = even[:16] + odd[:16]
    rest = total(even[18:19] + odd[18:19])
    user_values = user_grad[...]
    rest = rest + total(user_values * user_values)
    lane, line = iota(small.shape, 1), iota(small.shape, 0)
    counted = (line < 7) | ((line > 7) & (lane < 2 * BUCKETS))
    small_kept = jnp.where(counted, small, 0.0)
    rest = rest + total(small_kept * small_kept)
    norm = jnp.sqrt(section_squares[0] + section_squares[1] + rest)
    factor = jnp.minimum(1.0, clip_norm / (norm + 1e-06))
    loss_ref[0] = small[7, 0]
    norm_ref[0] = norm[0, 0]
    for s in range(2):
        section_ref[s] = jnp.sqrt(section_squares[s])[0, 0]
    for row in range(8):
        lanes = slice((row % 2) * LANES, (row % 2 + 1) * LANES)
        hist_ref[row // 2 : row // 2 + 1, lanes] = stat_ref[row : row + 1, :]

    outs = adam(
        small_in[0][...], small_in[1][...], small_in[2][...], factor * small[:7], rate_gain, 0.0
    )
    for ref, value in zip(small_out[:3], outs):
        ref[...] = value
    for head in range(HEADS):
        for s in range(2):
            slope = factor * small[8 + head : 9 + head, s * BUCKETS : (s + 1) * BUCKETS]
            one = slice(s, s + 1)
            outs = adam(
                small_in[3][head, one, :],
                small_in[4][head, one, :],
                small_in[5][head, one, :],
                slope,
                rate_small,
                0.0,
            )
            for ref, value in zip(small_out[3:], outs):
                ref[head, one, :] = value

    stores = []

    def store(kind, place):
        first = 3 * kind
        pieces = [(hold[first + i], big_out[first + i]) for i in range(3)]
        pieces.append((low_hold[kind], low_out[kind]))
        for source, target in pieces:
            copy = pltpu.make_async_copy(
                source.at[place], target.at[place], out_sems.at[len(stores)]
            )
            copy.start()
            stores.append(copy)

    def step(kind, place, slope):
        first = 3 * kind
        outs = adam(
            hold[first][place],
            hold[first + 1][place],
            hold[first + 2][place],
            factor * slope.astype(f32),
            rate_matrix,
            decay_matrix,
        )
        for i in range(3):
            hold[first + i][place] = outs[i]
        low_hold[kind][place] = outs[0].astype(bf16)

    def rows_from(start, count):
        return pl.ds(pl.multiple_of(start, 16), count)

    def columns(kind, first, count, row):
        def one(i, carry):
            lanes = pl.ds(pl.multiple_of((first + i) * LANES, LANES), LANES)
            step(kind, (0, slice(None), lanes), grad_ref[rows_from(row + i * D, D), :])
            return carry

        lax.fori_loop(0, count, one, 0)
        store(kind, (0, slice(None), slice(first * LANES, (first + count) * LANES)))

    def lines(first, count, size, source, row):
        def one(i, carry):
            place = (rows_from(first + i * size, size), slice(None))
            step(2, place, source[rows_from(row + i * size, size), :])
            return carry

        lax.fori_loop(0, count, one, 0)
        store(2, (slice(first, first + count * size), slice(None)))

    skip = FIRST // LANES
    for i in range(3):
        loads[i].wait()
    columns(0, 0, skip // 2, REST)
    columns(0, skip // 2, skip // 2, REST + skip // 2 * D)
    columns(0, skip, MIXW // LANES - skip, 0)
    for i in range(3, 6):
        loads[i].wait()
    for part in range(2):
        first = part * FF // LANES
        columns(1, first, FF // LANES, (MIXW // LANES - skip + first) * D)
    for i in range(6, 9):
        loads[i].wait()
    for part in range(2):
        lines(part * CODES // 2, 4, LANES, grad_ref, COLS + part * CODES // 2)
    parts = users // USER_ROWS
    lines(CODES, parts // 2, USER_ROWS, user_grad, 0)
    done = parts // 2 * USER_ROWS
    lines(CODES + done, parts - parts // 2, USER_ROWS, user_grad, done)
    for copy in stores:
        copy.wait()


def update(reduced, mixers, feeds, embeds, gains, biases):
    vmem = pl.BlockSpec(memory_space=pltpu.VMEM)
    smem = pl.BlockSpec(memory_space=pltpu.SMEM)
    hbm = pl.BlockSpec(memory_space=pl.ANY)
    big = [*mixers, *feeds, *embeds]
    small = [*gains, *biases]
    low = [jax.ShapeDtypeStruct(x[0].shape, bf16) for x in (mixers, feeds, embeds)]
    users = embeds[0].shape[0] - CODES
    pieces = 4 * (6 + 4 + 4 + users // USER_ROWS)
    return pl.pallas_call(
        update_kernel,
        out_shape=[
            jax.ShapeDtypeStruct((1,), f32),
            jax.ShapeDtypeStruct((1,), f32),
            jax.ShapeDtypeStruct((2,), f32),
            jax.ShapeDtypeStruct((LEVELS, CODEBOOK), f32),
        ]
        + [jax.ShapeDtypeStruct(x.shape, f32) for x in big + small]
        + low,
        in_specs=[hbm] * 14 + [vmem] * 6,
        out_specs=[smem] * 3 + [vmem] + [hbm] * 9 + [vmem] * 6 + [hbm] * 3,
        scratch_shapes=[pltpu.VMEM(x.shape, x.dtype) for x in reduced]
        + [pltpu.VMEM(x.shape, f32) for x in big]
        + [pltpu.VMEM(x.shape, bf16) for x in low]
        + [
            pltpu.VMEM((users, D), f32),
            pltpu.SemaphoreType.DMA((5,)),
            pltpu.SemaphoreType.DMA((9,)),
            pltpu.SemaphoreType.DMA((pieces,)),
        ],
        compiler_params=pltpu.CompilerParams(vmem_limit_bytes=62 * 2**20),
        name="update",
    )(*reduced, *big, *small)


def shards(
    history_codes,
    user_ids,
    targets,
    domains,
    mixer,
    mixer_moment,
    mixer_square,
    feed,
    feed_moment,
    feed_square,
    embedding,
    embedding_moment,
    embedding_square,
    gains,
    gains_moment,
    gains_square,
    position_bias,
    bias_moment,
    bias_square,
):
    def turned(table):
        return jnp.transpose(table, (2, 0, 1))

    biases = [turned(x) for x in (position_bias, bias_moment, bias_square)]
    reduced = gradients(
        history_codes,
        user_ids,
        targets.T,
        domains.reshape(1, -1),
        biases[0],
        gains,
        mixer,
        feed,
        embedding,
        lax.axis_size("dp"),
    )
    outs = update(
        reduced,
        (mixer, mixer_moment, mixer_square),
        (feed, feed_moment, feed_square),
        (embedding, embedding_moment, embedding_square),
        (gains, gains_moment, gains_square),
        biases,
    )
    loss, norm, sections, histograms = outs[:4]
    back = [jnp.transpose(x, (1, 2, 0)) for x in outs[16:19]]
    return (
        loss.reshape(()),
        norm.reshape(()),
        sections,
        histograms,
        *outs[4:16],
        *back,
        *outs[19:],
    )


def solution(mesh):
    by_dp, by_pipe, copied = P("dp"), P("pipe"), P()
    return jax.shard_map(
        shards,
        mesh=mesh,
        in_specs=(by_dp,) * 4 + (by_pipe,) * 6 + (copied,) * 9,
        out_specs=(copied,) * 4 + (by_pipe,) * 6 + (copied,) * 9 + (by_pipe,) * 2 + (copied,),
        check_vma=False,
    )
```

```python
import functools

import jax
import jax.numpy as jnp
from jax import lax
from jax.experimental import pallas as pl
from jax.experimental.pallas import tpu as pltpu
from jax.sharding import PartitionSpec as P

D = 128
HEADS = 6
HEAD_DIM = 64
FF = 1024
CODEBOOK = 256
LEVELS = 4
BUCKETS = 32
DOMAINS = 3
HIST_LEN = 81
STEP = 5
CODES = 1024
LANES = 128
WIDTH = HEADS * HEAD_DIM
MIXW = 6 * WIDTH
COLS = MIXW + 2 * FF
BLOCKS = COLS // LANES
KEYS = 96
GROUP = 8
BATCH = 2
NEAR = 3
PACK = 96
WIDE = GROUP * PACK
SPAN = GROUP * LANES
COLUMNS = WIDE // LANES
PAIRS = HEADS // 2
FIRST = 4 * WIDTH
REST = COLS - FIRST
USER_ROWS = 400
MESH = pl.DeviceIdType.MESH

norm_eps = 1e-06
beta_one = 0.9
beta_two = 0.999
adam_eps = 1e-08
clip_norm = 0.5
rate_matrix = 0.04
rate_gain = 0.8
rate_small = 0.3
decay_matrix = 0.01

f32 = jnp.float32
bf16 = jnp.bfloat16


def iota(shape, axis):
    return lax.broadcasted_iota(jnp.int32, shape, axis)


def mul(left, right):
    return jnp.dot(left, right, preferred_element_type=f32)


def mul_t(left, right):
    return lax.dot_general(left, right, (((1,), (1,)), ((), ())), preferred_element_type=f32)


def mul_exact(left, right):
    return jnp.dot(left, right, preferred_element_type=f32, precision=lax.Precision.HIGHEST)


def mul_exact_t(left, right):
    return lax.dot_general(
        left,
        right,
        (((1,), (1,)), ((), ())),
        preferred_element_type=f32,
        precision=lax.Precision.HIGHEST,
    )


def onehot(ids, rows):
    return jnp.where(iota((rows, ids.shape[1]), 0) == ids, 1.0, 0.0).astype(bf16)


def inverse_rms(x):
    return lax.rsqrt(jnp.mean(x * x, axis=0, keepdims=True) + norm_eps)


def norm_low(x, inverse, gain):
    return (x * inverse * gain).astype(bf16)


def norm_back(x, inverse, gain, upstream):
    scaled = x * inverse
    inner = upstream * gain
    back = inverse * (inner - scaled * jnp.mean(inner * scaled, axis=0, keepdims=True))
    return back, upstream * scaled


def block_diag(pair):
    zero = jnp.zeros((HEAD_DIM, LANES), pair.dtype)
    left = jnp.concatenate([pair[:HEAD_DIM], zero], 0)
    right = jnp.concatenate([zero, pair[HEAD_DIM:]], 0)
    return jnp.concatenate([left, right], 1)


def diagonal(both):
    return jnp.concatenate([both[:HEAD_DIM, :LANES], both[HEAD_DIM:, LANES:]], 0)


def turn(x, shift):
    return x if shift % LANES == 0 else pltpu.roll(x, shift % LANES, 1)


def pack(tables):
    lane = iota(tables[0].shape, 1)
    columns = []
    for first in range(0, len(tables), 4):
        turned = [turn(tables[first + i], PACK * i) for i in range(4)]
        for i in range(3):
            columns.append(jnp.where(lane < PACK - 32 * i, turned[i], turned[i + 1]))
    return jnp.concatenate(columns, 1)


def unpack(x):
    lane = iota((x.shape[0], LANES), 1)
    tables = []
    for first in range(0, x.shape[1] // LANES, 3):
        a, b, c = [x[:, (first + i) * LANES : (first + i + 1) * LANES] for i in range(3)]
        tables.append(a)
        tables.append(jnp.where(lane < 32, turn(a, 32), turn(b, 32)))
        tables.append(jnp.where(lane < 64, turn(b, 64), turn(c, 64)))
        tables.append(turn(c, 96))
    return tables


def stack(both):
    return jnp.concatenate([both[:, :LANES], both[:, LANES:]], 0)


def pad_keys(table):
    if table.shape[0] == LANES:
        return table
    zero = jnp.zeros((LANES - table.shape[0], table.shape[1]), table.dtype)
    return jnp.concatenate([table, zero], 0)


def columns_of(table, i):
    return table[:, 2 * i * LANES : 2 * (i + 1) * LANES]


def attend(keys, queries, values, bias):
    scores = [mul(key, block_diag(query)) for key, query in zip(keys, queries)]
    scores = jnp.concatenate(scores, 1) + bias
    top = jnp.max(scores, axis=0, keepdims=True)
    chance = jnp.exp(scores - top)
    total = jnp.sum(chance, axis=0, keepdims=True)
    chance = (chance * (1.0 / total)).astype(bf16)
    full = pad_keys(chance)
    mixed = [mul(value, columns_of(full, i)) for i, value in enumerate(values)]
    return chance, [diagonal(both).astype(bf16) for both in mixed]


def attend_back(keys_t, queries, values, back_mixed, chance):
    exact = chance.astype(f32)
    back_chance = [mul(value, block_diag(back)) for value, back in zip(values, back_mixed)]
    back_chance = jnp.concatenate(back_chance, 1)
    inner = jnp.sum(back_chance * exact, axis=0, keepdims=True)
    back_scores = exact * (back_chance - inner)
    low = pad_keys(back_scores.astype(bf16))
    full = pad_keys(chance)
    count = range(len(queries))
    back_query = [mul(keys_t[i], columns_of(low, i)) for i in count]
    back_keys = [mul_t(queries[i], stack(columns_of(low, i))) for i in count]
    back_values = [mul_t(back_mixed[i], stack(columns_of(full, i))) for i in count]
    results = [
        [diagonal(both).astype(bf16) for both in part]
        for part in (back_query, back_keys, back_values)
    ]
    return *results, back_scores


def split_low(x):
    high = x.astype(bf16)
    return jnp.concatenate([high, (x - high.astype(f32)).astype(bf16)], 0)


def stages(dp):
    bits = [2**k for k in range(dp.bit_length() - 1)]
    return [("dp", bit) for bit in bits[:2] + bits[4:] + bits[2:4]] + [("pipe", 1)]


def code_stages(dp):
    order = stages(dp)
    return order[:1] + order[2:-NEAR] + order[-1:] + order[1:2] + order[-NEAR:-1]


def high_low(x, parts):
    rows = []
    for _ in range(parts):
        rows.append(x.astype(bf16))
        x = x - rows[-1].astype(f32)
    return jnp.concatenate(rows, 0)


def side_of(stage):
    axis, bit = stage
    return lax.rem(lax.div(lax.axis_index(axis), bit), 2)


def partner_of(stage):
    axis, bit = stage
    return {axis: lax.axis_index(axis) + bit * (1 - 2 * side_of(stage))}


def shares(dp, rows, across=0):
    held = [rows]
    depth = len(stages(dp)) - 1
    for k in range(depth + across):
        later = min(NEAR - 1, depth - 1 - k) + across if k < depth else 0
        half = held[-1] // 2
        held.append(half if half % (16 * 2**later) == 0 else held[-1])
    return held


def span(start, size):
    return pl.ds(pl.multiple_of(start, 16), size)


def step_kernel(n, dp, *refs):
    codes_ref, users_ref, user_row_ref, targets_ref, domains_ref, bias_ref, gains_ref = refs[:7]
    mixer_ref, feed_ref, embed_ref = refs[7:10]
    out_ref, out_ids_ref, out_slot_ref, out_stat_ref = refs[10:14]
    refs = refs[14:]
    x0_s, *doubles = refs[0], *[refs[1 + 2 * i : 3 + 2 * i] for i in range(9)]
    x1_s, qkv_s, p_s, o_s, r_s, mem_s, dqkv_s, pc_s, oc_s = doubles
    refs = refs[19:]
    x2_s, dz_s, wn_s, wt_s, ext_s = refs[:5]
    gain_s, ebias_s, dbias_s, g0_s, ge_s, gbias_s, ggain_s, rows_s, user_s, ids_s = refs[5:15]
    cross_s, cross_back_s, rest_s, first_s, codes_s, slot_s, own_slot_s, squares_s, id_rows_s, hot_s = refs[15:25]
    stat_s, stat_land, small_s, small_land, near_first, near_codes = refs[25:31]
    local_sems, sends, recvs = refs[31:34]
    lands = refs[34:]
    order = stages(dp)
    across = order[-1]
    depth = len(order)
    chunks = n // GROUP
    section = lax.axis_index("pipe")
    used = [0]

    def remote_to(source, target, device):
        index = used[0]
        used[0] += 1
        return pltpu.make_async_remote_copy(
            src_ref=source,
            dst_ref=target,
            send_sem=sends.at[index],
            recv_sem=recvs.at[index],
            device_id=device,
            device_id_type=MESH,
        )

    def remote(source, target, stage):
        return remote_to(source, target, partner_of(stage))

    near, far = order[-NEAR:], order[:-NEAR]
    route = code_stages(dp)
    code_near, code_far = route[-NEAR:], route[:-NEAR]
    masks = range(1, 2**NEAR)

    def device_of(mask, near=near):
        place = {"dp": lax.axis_index("dp"), "pipe": lax.axis_index("pipe")}
        for i, (axis, bit) in enumerate(near):
            if mask >> i & 1:
                place[axis] = place[axis] + bit * (1 - 2 * side_of((axis, bit)))
        return place

    def shift_of(mask, lefts, near=near):
        total = 0
        for i, left in enumerate(lefts):
            side = side_of(near[i])
            total = total + (1 - side if mask >> i & 1 else side) * left
        return total

    locals_in = []
    for block in range(BLOCKS):
        lanes = slice(block * LANES, (block + 1) * LANES)
        if block < MIXW // LANES:
            source = mixer_ref.at[0, :, lanes]
        else:
            source = feed_ref.at[0, :, slice(lanes.start - MIXW, lanes.stop - MIXW)]
        locals_in.append(pltpu.make_async_copy(source, g0_s.at[block], local_sems.at[block]))
    vocabulary = embed_ref.shape[0]
    flat = x2_s.at[pl.ds(0, vocabulary)]
    load_embed = pltpu.make_async_copy(embed_ref, flat, local_sems.at[BLOCKS])
    for copy in locals_in:
        copy.start()
    load_embed.start()

    barrier = pltpu.get_barrier_semaphore()
    greeted = [partner_of(stage) for stage in far if stage != code_near[0]]
    greeted += [device_of(mask) for mask in masks]
    greeted += [device_of(mask, code_near) for mask in masks if mask & 1]
    for device in greeted:
        pl.semaphore_signal(barrier, inc=1, device_id=device, device_id_type=MESH)

    scale = HEAD_DIM**-0.5
    cross_scale = jnp.where(section == 1, scale, 1.0).astype(f32)
    for copy in locals_in:
        copy.wait()
    def cast_weights(block, carry):
        factor = jnp.where((block >= 12) & (block < 15), cross_scale, 1.0)
        factor = jnp.where(block < 3, scale, factor)
        lanes = pl.ds(pl.multiple_of(block * LANES, LANES), LANES)
        wn_s[section, :, lanes] = (g0_s[block] * factor).astype(bf16)
        return carry

    lax.fori_loop(0, BLOCKS, cast_weights, 0, unroll=2)
    pl.semaphore_wait(barrier, len(greeted))
    half = D // 2
    mine = span(side_of(order[0]) * half, half)
    pieces = (slice(0, FIRST), slice(FIRST, COLS))
    over = [
        remote(wn_s.at[section, mine, piece], wn_s.at[section, mine, piece], across)
        for piece in pieces
    ]
    for copy in over:
        copy.start()

    ids_s[:, : HIST_LEN - 1] = codes_ref[pl.ds(pl.multiple_of(section * n, 8), n), :]
    lane, row = iota((n, LANES), 1), iota((n, LANES), 0)
    ids = ids_s[...] + ((lane & 3) << 8)
    ids = jnp.where(lane < HIST_LEN - 1, ids, jnp.where(lane == HIST_LEN - 1, CODES + row, -1))
    ids_s[...] = ids
    packed = []
    for i in range(GROUP):
        rows = [ids_s[c * GROUP + i : c * GROUP + i + 1, :] for c in range(chunks)]
        rows += [jnp.zeros((8 - chunks, LANES), jnp.int32)]
        packed.append(jnp.concatenate(rows, 0))
    id_rows_s[...] = pack(packed)
    count = targets_ref.shape[1]
    history, token = iota((count, LANES), 0), iota((count, LANES), 1)
    pick = jnp.where((token >> 2) + section * n == history, 1.0, 0.0)
    level, place = iota((LEVELS, LANES), 0), iota((LEVELS, LANES), 1) & 3
    target = mul(targets_ref[...].astype(f32), pick) + (level * CODEBOOK).astype(f32)
    goal = jnp.sum(jnp.where(level == place, target, 0.0), axis=0, keepdims=True).astype(jnp.int32)
    start_ids = jnp.sum(
        jnp.where(level == place - 1, target, 0.0), axis=0, keepdims=True
    ).astype(jnp.int32)
    domain = mul(domains_ref[...].astype(f32), pick)
    pick = jnp.where(lax.rem(token, n) + section * n == history, 1.0, 0.0)
    own_users = mul_exact(user_row_ref[...].astype(f32), pick)

    counts = [
        jnp.sum(jnp.where(domain == d, 1.0, 0.0), axis=1, keepdims=True) for d in range(DOMAINS)
    ]
    counts += [jnp.zeros((1, 1), f32)] * (8 - DOMAINS)
    stat_s[0, 8:, :] = jnp.broadcast_to(jnp.concatenate(counts, 0), (8, LANES))
    histogram = mul_t(jnp.ones((8, LANES), bf16), onehot(goal, CODES))
    for r in range(8):
        stat_s[0, r : r + 1, :] = histogram[:1, r * LANES : (r + 1) * LANES]
    slot = 0
    for k, stage in enumerate(route):
        slot = slot + side_of(stage) * 2 ** (depth - 1 - k)
    owner = iota((8, LANES), 1) // n
    own_users = jnp.broadcast_to(own_users, (8, LANES)).astype(jnp.int32)
    slot_s[...] = jnp.where(owner == lax.rem(slot, LANES // n), own_users, 0)
    store_ids = pltpu.make_async_copy(slot_s, out_ids_ref.at[slot], local_sems.at[BLOCKS + 1])
    store_ids.start()
    store_ids.wait()

    def slots_of(j):
        return pl.ds(lax.div(slot, 2**j) * 2**j, 2**j)

    early = []
    for j, stage in enumerate(reversed(route)):
        held = out_ids_ref.at[slots_of(j)]
        early.append(
            (
                remote(stat_s.at[j], stat_land.at[j], stage),
                remote(held, held, stage),
            )
        )

    def early_step(j):
        if j > 0:
            for copy in early[j - 1]:
                copy.wait()
            stat_s[j] = stat_s[j - 1] + stat_land[j - 1]
        if j < depth:
            for copy in early[j]:
                copy.start()

    eye = jnp.where(iota((LANES, LANES), 0) == iota((LANES, LANES), 1), 1.0, 0.0).astype(bf16)
    load_embed.wait()

    def fetch(i, carry):
        user_s[pl.ds(i, 1), :] = x2_s[pl.ds(CODES + users_ref[section * n + i], 1), :]
        return carry

    lax.fori_loop(0, n, fetch, 0, unroll=4)
    for block in range(CODES // LANES + 1):
        if block < CODES // LANES:
            rows = x2_s[block * LANES : (block + 1) * LANES, :]
            codes_s[block * LANES : (block + 1) * LANES, :] = rows.astype(bf16)
            width = LANES
        else:
            rows = user_s[...]
            width = n
        high = rows.astype(bf16)
        low = (rows - high.astype(f32)).astype(bf16)
        lanes = slice(block * LANES, block * LANES + width)
        ext_s[:D, lanes] = mul_t(eye, high).astype(bf16)
        ext_s[D:, lanes] = mul_t(eye, low).astype(bf16)

    def find(c):
        ids = id_rows_s[pl.ds(c, 1), :]
        for first in range(0, CODES + n, LANES):
            rows = min(LANES, CODES + n - first)
            hot_s[first : first + rows, :] = onehot(ids - first, rows)

    def lookup(c, carry):
        find(c)
        both = mul(ext_s[...], hot_s[...])
        x0_s[c] = both[:D] + both[D:]
        return carry

    lax.fori_loop(0, chunks, lookup, 0)

    beside = []
    for piece in pieces:
        came = wn_s.at[1 - section, mine, piece]
        beside.append(remote(came, came, order[0]))
    over[0].wait()
    beside[0].start()

    for g in range(7):
        gain_s[g] = jnp.broadcast_to(gains_ref[g : g + 1, :], (LANES, LANES)).T

    def positions(axis):
        index = iota((KEYS, LANES), axis)
        return jnp.where(index == HIST_LEN - 1, 0, index + 1)

    key, query = positions(0), positions(1)
    distance = jnp.abs(query - key)
    remoteness = jnp.zeros_like(distance)
    for edge in (12, 16, 23, 32, 46, 64, 91):
        remoteness = remoteness + (distance >= edge).astype(jnp.int32)
    nearby = jnp.minimum(jnp.where(distance < 8, distance, 8 + remoteness), 15)
    buckets = nearby + jnp.where(key > query, 16, 0)
    real = iota((KEYS, LANES), 0) < HIST_LEN
    for head in range(HEADS):
        lanes = slice(head * LANES, (head + 1) * LANES)

        def choose(b, table):
            return jnp.where(buckets == b, bias_ref[head, 0, b], table)

        table = lax.fori_loop(0, BUCKETS, choose, jnp.zeros((KEYS, LANES), f32), unroll=8)
        ebias_s[:, lanes] = jnp.where(real, table, -1e30)
    key, query = iota((LANES, LANES), 0), iota((LANES, LANES), 1)
    offset = query - key
    seen = ((key >> 2) == (query >> 2)) & (offset >= 0)
    for head in range(HEADS):
        lanes = slice(head * LANES, (head + 1) * LANES)
        table = jnp.full((LANES, LANES), -1e30, f32)
        for b in range(LEVELS):
            table = jnp.where(seen & (offset == b), bias_ref[head, 1, b], table)
        dbias_s[:, lanes] = table

    def transpose_weights(which, first, last):
        def one(block, carry):
            place = pl.ds(pl.multiple_of(block * LANES, LANES), LANES)
            wt_s[which, place, :] = wn_s[which, :, place].T
            return carry

        lax.fori_loop(first, last, one, 0, unroll=2)

    transpose_weights(section, 0, BLOCKS)
    beside[0].wait()
    transpose_weights(1 - section, 0, FIRST // LANES)

    def rest_arrives():
        over[1].wait()
        beside[1].start()
        beside[1].wait()
        transpose_weights(1 - section, FIRST // LANES, BLOCKS)

    def gain(g, width):
        column = gain_s[g]
        return column if width == LANES else jnp.concatenate([column] * (width // LANES), 1)

    def lockstep(steps, point=None):
        for number, _ in enumerate(zip(*steps)):
            if point is not None:
                point(number)

    def at_time(t, steps):
        for time, step in enumerate(steps):
            if step is not None:
                pl.when(t == time)(step)

    def spread_low(x):
        return jnp.concatenate([part.astype(bf16) for part in unpack(x)], 1)

    def packed(x):
        return pack([x[:, i * LANES : (i + 1) * LANES] for i in range(GROUP)])

    def part_of(j):
        return slice(j * LANES, (j + 1) * LANES)

    def encode_steps(t, half):
        c = 2 * t + half
        qkv, o, r = qkv_s[half], o_s[half], r_s[half]
        x0 = x0_s[c]
        h = spread_low(x0 * inverse_rms(x0) * gain(0, WIDE))
        yield
        for j in range(3):
            part = slice(j * WIDTH, (j + 1) * WIDTH)
            qkv[t, part, :] = mul(wt_s[0, part, :], h).astype(bf16)
        yield
        for first in range(0, GROUP, BATCH):
            queries, keys, values = [], [], []
            for i in range(first, first + BATCH):
                lanes = slice(i * LANES, (i + 1) * LANES)
                queries += [qkv[t, part_of(j), lanes] for j in range(PAIRS)]
                keys += [qkv[t, part_of(PAIRS + j), lanes].T[:KEYS] for j in range(PAIRS)]
                values += [qkv[t, part_of(2 * PAIRS + j), lanes] for j in range(PAIRS)]
            bias = jnp.concatenate([ebias_s[...]] * BATCH, 1)
            chance, mixed = attend(keys, queries, values, bias)
            for i in range(BATCH):
                lanes = slice((first + i) * LANES, (first + i + 1) * LANES)
                own = slice(i * HEADS * LANES, (i + 1) * HEADS * LANES)
                p_s[half][t, first + i] = chance[:, own]
                o[t, :, lanes] = jnp.concatenate(mixed[i * PAIRS : (i + 1) * PAIRS], 0)
            yield
        x1 = x0 + packed(mul(wn_s[0, :, 3 * WIDTH : 4 * WIDTH], o[t]))
        x1_s[half][t] = x1
        yield
        h = norm_low(x1, inverse_rms(x1), gain(1, WIDE))
        for j in range(2):
            part = slice(j * FF // 2, (j + 1) * FF // 2)
            lifted = mul(wt_s[0, MIXW + j * FF // 2 : MIXW + (j + 1) * FF // 2, :], h)
            r[t, part, :] = jnp.maximum(lifted, 0.0).astype(bf16)
        yield
        x2 = x1 + mul(wn_s[0, :, MIXW + FF :], r[t])
        put_wide(x2_s, c, x2)
        e = norm_low(x2, inverse_rms(x2), gain(2, WIDE))
        yield
        for j in range(2):
            part = slice(j * WIDTH, (j + 1) * WIDTH)
            mem_s[half][t, part, :] = mul(
                wt_s[0, 4 * WIDTH + j * WIDTH : 4 * WIDTH + (j + 1) * WIDTH, :], e
            ).astype(bf16)
        yield

    attention = GROUP // BATCH
    pairs = chunks // 2

    def early_at(place, places):
        return [
            functools.partial(early_step, place + places * t)
            if place + places * t <= depth
            else None
            for t in range(pairs)
        ]

    def encode(t, carry):
        at_time(t, early_at(0, 3))

        def point(number):
            if number == attention // 2:
                at_time(t, early_at(1, 3))
            if number == attention + 2:
                pl.when(t == 0)(rest_arrives)
                at_time(t, early_at(2, 3))

        lockstep([encode_steps(t, 0), encode_steps(t, 1)], point)
        return carry

    def put_wide(ref, c, value):
        for i in range(COLUMNS):
            ref[pl.ds(pl.multiple_of((COLUMNS * c + i) * D, D), D), :] = value[
                :, i * LANES : (i + 1) * LANES
            ]

    def get_wide(ref, c):
        return jnp.concatenate(
            [ref[pl.ds(pl.multiple_of((COLUMNS * c + i) * D, D), D), :] for i in range(COLUMNS)], 1
        )

    lax.fori_loop(0, pairs, encode, 0)
    for j in range(3 * pairs, depth + 1):
        early_step(j)
    out_stat_ref[...] = stat_s[depth, :8, :]

    def put_blocks(first, value):
        for index in range(value.shape[1] // LANES):
            block = first + index
            part = value[:, index * LANES : (index + 1) * LANES].astype(bf16)
            if block < FIRST // LANES:
                first_s[1, block * D : (block + 1) * D, :] = part
            else:
                block -= FIRST // LANES
                rest_s[1, block * D : (block + 1) * D, :] = part

    def add_blocks(first, value):
        for index in range(value.shape[1] // LANES):
            g0_s[first + index] += value[:, index * LANES : (index + 1) * LANES]

    start = onehot(start_ids, CODES)
    both = mul(ext_s[:, :CODES], start)
    y0 = both[:D] + both[D:]
    inverse0 = inverse_rms(y0)
    h0 = norm_low(y0, inverse0, gain(3, LANES))
    dz_s[:, :LANES] = mul(wt_s[1, : 3 * WIDTH, :], h0).astype(bf16)
    both = mul(mul_t(eye, h0).astype(bf16), wn_s[1, :, WIDTH : 3 * WIDTH]).astype(bf16)
    self_chance, mixed = attend(
        [both[:, part_of(j)] for j in range(PAIRS)],
        [dz_s[part_of(j), :LANES] for j in range(PAIRS)],
        [dz_s[part_of(2 * PAIRS + j), :LANES] for j in range(PAIRS)],
        dbias_s[...],
    )
    self_values = both[:, WIDTH:]
    self_mixed = jnp.concatenate(mixed, 0)
    y1 = y0 + mul(wn_s[1, :, 3 * WIDTH : 4 * WIDTH], self_mixed)
    inverse1 = inverse_rms(y1)
    h1 = norm_low(y1, inverse1, gain(4, LANES))
    cross_s[...] = mul(wt_s[1, 4 * WIDTH : 5 * WIDTH, :], h1).astype(bf16)

    def spreader(g, turned):
        shape = (LANES, 32 * GROUP) if turned else (32 * GROUP, LANES)
        row, token = iota(shape, 1 if turned else 0), iota(shape, 0 if turned else 1)
        hit = token == 4 * GROUP * g + 4 * (row >> 5) + (row & 3)
        return jnp.where(hit, 1.0, 0.0).astype(bf16)

    def rows_of(g, table):
        rows = mul_t(spreader(g, False), table)
        mask = (iota(rows.shape, 1) >> 6) == ((iota(rows.shape, 0) & 31) >> 2)
        return jnp.where(mask, rows, 0.0).astype(bf16)

    def head_mask(shape):
        return (iota(shape, 0) >> 6) == ((iota(shape, 1) & 31) >> 2)

    def rows_t_of(g, table):
        rows = mul(table, spreader(g, True))
        return jnp.where(head_mask(rows.shape), rows, 0.0).astype(bf16)

    def gather_rows(ref):
        total = jnp.zeros((WIDTH, LANES), f32)
        for g in range(chunks):
            total = total + mul(ref[g % 2][g // 2], spreader(g, False))
        return total.astype(bf16)

    def blocks_of(table):
        rows = []
        for i in range(GROUP):
            part = table[32 * i : 32 * i + 32]
            column, shift = divmod(PACK * i, LANES)
            part = turn(part, shift)
            lane = iota(part.shape, 1)
            zero = jnp.zeros_like(part)
            columns = [zero] * COLUMNS
            columns[column] = jnp.where(lane >= shift, part, 0.0)
            if shift > LANES - PACK:
                columns[column + 1] = jnp.where(lane < shift, part, 0.0)
            rows.append(jnp.concatenate(columns, 1))
        return jnp.concatenate(rows, 0).astype(bf16)

    def row_products(rows, keys):
        both = mul(rows, keys)
        parts = []
        for i in range(GROUP):
            own = both[32 * i : 32 * i + 32]
            column, shift = divmod(PACK * i, LANES)
            part = turn(own[:, column * LANES : (column + 1) * LANES], -shift)
            if shift > LANES - PACK:
                after = turn(own[:, (column + 1) * LANES : (column + 2) * LANES], -shift)
                part = jnp.where(iota(part.shape, 1) < LANES - shift, part, after)
            parts.append(part)
        return jnp.concatenate(parts, 0)

    def cross_steps(t, half):
        g = 2 * t + half
        queries = rows_of(g, cross_s[...])
        yield
        scores = row_products(queries, mem_s[half][t, :WIDTH, :])
        scores = jnp.where(iota(scores.shape, 1) < HIST_LEN, scores, -1e30)
        chance = jnp.exp(scores - jnp.max(scores, axis=1, keepdims=True))
        chance = chance * (1.0 / jnp.sum(chance, axis=1, keepdims=True))
        pc_s[half][t] = chance
        yield
        mixed = mul_t(mem_s[half][t, WIDTH:, :], blocks_of(chance))
        oc_s[half][t] = jnp.where(head_mask(mixed.shape), mixed, 0.0).astype(bf16)
        yield

    def cross(t, carry):
        lockstep([cross_steps(t, 0), cross_steps(t, 1)])
        return carry

    lax.fori_loop(0, pairs, cross, 0)
    cross_mixed = gather_rows(oc_s)
    y2 = y1 + mul(wn_s[1, :, 5 * WIDTH : 6 * WIDTH], cross_mixed)
    inverse2 = inverse_rms(y2)
    h2 = norm_low(y2, inverse2, gain(5, LANES))
    lifted = mul(wt_s[1, MIXW : MIXW + FF, :], h2)
    active = jnp.maximum(lifted, 0.0).astype(bf16)
    y3 = y2 + mul(wn_s[1, :, MIXW + FF :], active)
    inverse3 = inverse_rms(y3)
    final = norm_low(y3, inverse3, gain(6, LANES))
    logits = mul(codes_s[...], final)
    top = jnp.max(logits, axis=0, keepdims=True)
    log_total = top + jnp.log(jnp.sum(jnp.exp(logits - top), axis=0, keepdims=True))
    match = iota(logits.shape, 0) == goal
    picked = jnp.sum(jnp.where(match, logits, 0.0), axis=0, keepdims=True)
    weight = jnp.zeros((1, LANES), f32)
    for d in range(DOMAINS):
        share = 1.0 / (DOMAINS * jnp.maximum(stat_s[depth, 8 + d : 9 + d, :], 1.0))
        weight = weight + jnp.where(domain == d, share, 0.0)
    loss = jnp.sum(weight * (log_total - picked), axis=1, keepdims=True)
    back_logits = (
        weight * (jnp.exp(logits - log_total) - jnp.where(match, 1.0, 0.0))
    ).astype(bf16)
    back_final = mul(ext_s[:D, :CODES], back_logits)
    table_grad = mul_t(back_logits, final)
    back, gain_grad = norm_back(y3, inverse3, gain(6, LANES), back_final)
    ggain_s[6] = gain_grad
    low = back.astype(bf16)
    put_blocks(26, mul_t(low, active))
    back_lifted = jnp.where(lifted > 0, mul(wt_s[1, MIXW + FF :, :], low), 0.0).astype(bf16)
    put_blocks(18, mul_t(h2, back_lifted))
    more, gain_grad = norm_back(
        y2, inverse2, gain(5, LANES), mul(wn_s[1, :, MIXW : MIXW + FF], back_lifted)
    )
    ggain_s[5] = gain_grad
    back = back + more
    low = back.astype(bf16)
    put_blocks(15, mul_t(low, cross_mixed))
    cross_back_s[...] = mul(wt_s[1, 5 * WIDTH : 6 * WIDTH, :], low).astype(bf16)

    def cross_back_steps(t, half):
        g = 2 * t + half
        memory = mem_s[half]
        mixed_rows = rows_of(g, cross_back_s[...])
        queries_t = rows_t_of(g, cross_s[...])
        mixed_t = rows_t_of(g, cross_back_s[...])
        yield
        back_chance = row_products(mixed_rows, memory[t, WIDTH:, :])
        back_chance = jnp.where(iota(back_chance.shape, 1) < HIST_LEN, back_chance, 0.0)
        chance = pc_s[half][t]
        inner = jnp.sum(back_chance * chance, axis=1, keepdims=True)
        yield
        spread = blocks_of(chance * (back_chance - inner))
        total = mul_t(memory[t, :WIDTH, :], spread)
        oc_s[half][t] = jnp.where(head_mask(total.shape), total, 0.0).astype(bf16)
        yield
        memory[t, :WIDTH, :] = mul(queries_t, spread).astype(bf16)
        memory[t, WIDTH:, :] = mul(mixed_t, blocks_of(chance)).astype(bf16)
        yield

    def cross_back(t, carry):
        lockstep([cross_back_steps(t, 0), cross_back_steps(t, 1)])
        return carry

    lax.fori_loop(0, pairs, cross_back, 0)
    back_query = gather_rows(oc_s)
    put_blocks(12, mul_t(h1, back_query) * HEAD_DIM**-0.5)
    more, gain_grad = norm_back(
        y1, inverse1, gain(4, LANES), mul(wn_s[1, :, 4 * WIDTH : 5 * WIDTH], back_query)
    )
    ggain_s[4] = gain_grad
    back = back + more
    low = back.astype(bf16)
    put_blocks(9, mul_t(low, self_mixed))
    back_mixed = mul(wt_s[1, 3 * WIDTH : 4 * WIDTH, :], low).astype(bf16)
    *back_parts, self_scores = attend_back(
        [dz_s[part_of(PAIRS + j), :LANES] for j in range(PAIRS)],
        [dz_s[part_of(j), :LANES] for j in range(PAIRS)],
        [self_values[:, part_of(j)] for j in range(PAIRS)],
        [back_mixed[part_of(j)] for j in range(PAIRS)],
        self_chance,
    )
    dz_s[:, LANES:] = jnp.concatenate([x for part in back_parts for x in part], 0)
    put_blocks(0, mul_t(h0, dz_s[:WIDTH, LANES : 2 * LANES]) * HEAD_DIM**-0.5)
    put_blocks(3, mul_t(h0, dz_s[WIDTH:, LANES : 2 * LANES]))
    more, gain_grad = norm_back(
        y0, inverse0, gain(3, LANES), mul(wn_s[1, :, : 3 * WIDTH], dz_s[:, LANES : 2 * LANES])
    )
    ggain_s[3] = gain_grad
    back = back + more
    spread = mul_t(start, split_low(back))
    ge_s[:CODES, :] = table_grad + spread[:, :D] + spread[:, D:]
    ge_s[CODES:, :] = jnp.zeros((n, D), f32)
    rows_s[...] = jnp.zeros_like(rows_s)
    for head in range(HEADS):
        lanes = slice(head * LANES, (head + 1) * LANES)
        for b in range(LEVELS):
            hit = jnp.where(offset == b, self_scores[:, lanes], 0.0)
            rows_s[head, BUCKETS + b : BUCKETS + b + 1, :] = jnp.sum(hit, axis=0, keepdims=True)

    def reducing(buffer, kept, held, stages):
        steps, at = [], 0
        for k, stage in enumerate(stages):
            rows, left = held[k], held[k + 1]
            side = side_of(stage)
            if left < rows:
                source = buffer.at[span(at + (1 - side) * left, left)]
                at = at + side * left
            else:
                source = buffer.at[span(at, rows)]
            steps.append((remote(source, kept[k], stage), at, left))
        return steps, at, held

    def begin(steps, k):
        steps[k][0].start()

    def finish(steps, buffer, kept, k):
        copy, at, left = steps[k]
        copy.wait()
        place = span(at, left)
        total = buffer[place, :].astype(f32) + kept[k][...].astype(f32)
        buffer[place, :] = total.astype(bf16)

    flat_depth = depth - 1
    held_rest, held_first, held_codes = shares(dp, REST), shares(dp, FIRST), shares(dp, CODES, 1)
    land, rest = {}, lands
    for name, number in (
        ("rest0", flat_depth),
        ("rest1", flat_depth),
        ("first1", flat_depth),
        ("first0", len(far)),
        ("codes", len(far)),
    ):
        land[name], rest = rest[:number], rest[number:]
    land_rest, land_first = rest
    rest1 = reducing(rest_s.at[1], land["rest1"], held_rest, order[:-1])
    first1 = reducing(first_s.at[1], land["first1"], held_first, order[:-1])
    rest0 = reducing(rest_s.at[0], land["rest0"], held_rest, order[:-1])
    first0 = reducing(first_s.at[0], land["first0"], held_first, far)
    codes = reducing(codes_s, land["codes"], held_codes, code_far)

    def step1(k):
        if k > 0:
            finish(rest1[0], rest_s.at[1], land["rest1"], k - 1)
            finish(first1[0], first_s.at[1], land["first1"], k - 1)
        if k < flat_depth:
            begin(rest1[0], k)
            begin(first1[0], k)

    def crossing(buffer, target, at, rows):
        source = buffer.at[1 - section, span(at, rows)]
        return remote(source, target, across)

    cross_rest = crossing(rest_s, land_rest, rest1[1], rest1[2][-1])
    cross_first = crossing(first_s, land_first, first1[1], first1[2][-1])

    def settle(copy, buffer, landed, at, rows, base):
        copy.wait()
        value = (buffer[section, span(at, rows), :].astype(f32) + landed[...].astype(f32)).astype(
            bf16
        )
        out_ref[span(base + at, rows), :] = value
        value = value.astype(f32)
        return jnp.sum(value * value, axis=0, keepdims=True)

    def gathering(base, at, held):
        steps = []
        for k in reversed(range(flat_depth)):
            rows, left = held[k], held[k + 1]
            if left < rows:
                place = out_ref.at[span(base + at, left)]
                steps.append(remote(place, place, order[k]))
                at = at - side_of(order[k]) * left
            else:
                steps.append(None)
        return steps

    gather_rest = gathering(0, rest1[1], rest1[2])

    def step0(k):
        if k > 0 and k <= flat_depth:
            finish(rest0[0], rest_s.at[0], land["rest0"], k - 1)
        if k < flat_depth:
            begin(rest0[0], k)
        if k == flat_depth:
            cross_rest.start()
        if k == flat_depth + 1:
            squares = settle(cross_rest, rest_s, land_rest, rest1[1], rest1[2][-1], 0)
            squares_s[0:1, :] = squares / (dp * rest1[2][-1] // REST)
        if k > flat_depth + 1 and gather_rest[k - flat_depth - 2] is not None:
            gather_rest[k - flat_depth - 2].wait()
        if flat_depth < k < 2 * flat_depth + 1 and gather_rest[k - flat_depth - 1] is not None:
            gather_rest[k - flat_depth - 1].start()

    g0_s[...] = jnp.zeros_like(g0_s)
    gbias_s[...] = jnp.zeros_like(gbias_s)
    for g in range(3):
        ggain_s[g] = jnp.zeros((D, LANES), f32)

    def fold(x):
        return sum(x[:, i * LANES : (i + 1) * LANES] for i in range(COLUMNS))

    def rest_steps(t, half):
        c = 2 * t + half
        r = r_s[half]
        x2 = get_wide(x2_s, c)
        inverse = inverse_rms(x2)
        back_memory = mem_s[half][t]
        add_blocks(12, mul_t(norm_low(x2, inverse, gain(2, WIDE)), back_memory))
        back_normed = mul(wn_s[0, :, 4 * WIDTH : 6 * WIDTH], back_memory)
        yield
        back, gain_grad = norm_back(x2, inverse, gain(2, WIDE), back_normed)
        ggain_s[2] += fold(gain_grad)
        low = back.astype(bf16)
        yield
        add_blocks(26, mul_t(low, r[t]))
        for j in range(4):
            part = slice(j * FF // 4, (j + 1) * FF // 4)
            back_active = mul(wt_s[0, MIXW + FF + part.start : MIXW + FF + part.stop, :], low)
            live = r[t, part, :].astype(f32) > 0
            r[t, part, :] = jnp.where(live, back_active, 0.0).astype(bf16)
        yield
        x1 = x1_s[half][t]
        inverse = inverse_rms(x1)
        add_blocks(18, mul_t(norm_low(x1, inverse, gain(1, WIDE)), r[t]))
        back_normed = mul(wn_s[0, :, MIXW : MIXW + FF], r[t])
        yield
        more, gain_grad = norm_back(x1, inverse, gain(1, WIDE), back_normed)
        ggain_s[1] += fold(gain_grad)
        put_wide(x2_s, c, back + more)
        yield

    places1 = {0: 0, 1: 1, 3: 2, 5: 3}
    places0 = {0: 0, 1: 1, 2: 2, 3: 3, 4: 4, 5: 5, 6: 6, 7: 7, 9: 8}
    steps0 = 2 * flat_depth + 2

    def placed(places, step, place, each):
        return [
            functools.partial(step, places[place + each * t])
            if place + each * t in places
            else None
            for t in range(pairs)
        ]

    def back_rest(t, carry):
        at_time(t, placed(places1, step1, 0, 3))

        def point(number):
            if number in (1, 3):
                at_time(t, placed(places1, step1, (number + 1) // 2, 3))

        lockstep([rest_steps(t, 0), rest_steps(t, 1)], point)
        return carry

    lax.fori_loop(0, pairs, back_rest, 0)
    def cast_rest(block, carry):
        place = pl.ds(pl.multiple_of(block * D, D), D)
        rest_s[0, place, :] = g0_s[FIRST // D + block].astype(bf16)
        return carry

    lax.fori_loop(0, REST // D, cast_rest, 0, unroll=2)
    for j in range(4, flat_depth + 1):
        step1(j)

    def first_steps(t, half):
        c = 2 * t + half
        qkv, o, dqkv = qkv_s[half], o_s[half], dqkv_s[half]
        back = get_wide(x2_s, c)
        lane = iota((D, LANES), 1)
        low = [jnp.where(lane < PACK, part, 0.0).astype(bf16) for part in unpack(back)]
        low = jnp.concatenate(low, 1)
        yield
        add_blocks(9, mul_t(low, o[t]))
        o[t] = mul(wt_s[0, 3 * WIDTH : 4 * WIDTH, :], low).astype(bf16)
        yield
        for first in range(0, GROUP, BATCH):
            queries, keys, values, backs = [], [], [], []
            for i in range(first, first + BATCH):
                lanes = slice(i * LANES, (i + 1) * LANES)
                queries += [qkv[t, part_of(j), lanes] for j in range(PAIRS)]
                keys += [qkv[t, part_of(PAIRS + j), lanes] for j in range(PAIRS)]
                values += [qkv[t, part_of(2 * PAIRS + j), lanes].T[:KEYS] for j in range(PAIRS)]
                backs += [o[t, part_of(j), lanes] for j in range(PAIRS)]
            chance = [p_s[half][t, first + i] for i in range(BATCH)]
            *results, scores = attend_back(
                keys, queries, values, backs, jnp.concatenate(chance, 1)
            )
            for i in range(BATCH):
                lanes = slice((first + i) * LANES, (first + i + 1) * LANES)
                own = slice(i * PAIRS, (i + 1) * PAIRS)
                dqkv[:, lanes] = jnp.concatenate([x for part in results for x in part[own]], 0)
            width = HEADS * LANES
            gbias_s[...] += sum(scores[:, i * width : (i + 1) * width] for i in range(BATCH))
            yield
        x0 = x0_s[c]
        inverse = inverse_rms(x0)
        add_blocks(0, mul_t(spread_low(x0 * inverse * gain(0, WIDE)), dqkv[...]))
        back_normed = packed(mul(wn_s[0, :, : 3 * WIDTH], dqkv[...]))
        yield
        more, gain_grad = norm_back(x0, inverse, gain(0, WIDE), back_normed)
        ggain_s[0] += fold(gain_grad)
        find(c)
        spread = mul_t(hot_s[...], split_low(back + more))
        ge_s[...] += spread[:, :D] + spread[:, D:]
        yield

    def back_first(t, carry):
        at_time(t, placed(places0, step0, 0, 5))

        def point(number):
            place = {1: 1, attention // 2 + 1: 2, attention + 1: 3, attention + 2: 4}.get(number)
            if place is not None:
                at_time(t, placed(places0, step0, place, 5))

        lockstep([first_steps(t, 0), first_steps(t, 1)], point)
        return carry

    lax.fori_loop(0, pairs, back_first, 0)

    def cast_first(block, carry):
        place = pl.ds(pl.multiple_of(block * D, D), D)
        factor = jnp.where(block < 3, scale, 1.0)
        first_s[0, place, :] = (g0_s[block] * factor).astype(bf16)
        return carry

    lax.fori_loop(0, FIRST // D, cast_first, 0, unroll=2)
    codes_s[...] = ge_s[:CODES, :].astype(bf16)
    begin(first0[0], 0)
    begin(codes[0], 0)
    code_size = held_codes[-1]
    own_slot_s[code_size : code_size + n, :] = ge_s[CODES:, :].astype(bf16)
    late = list(range(9, steps0))
    if late:
        step0(late.pop(0))

    ones = jnp.ones((8, LANES), f32)
    small_s[0, 8:16, :] = jnp.zeros((8, LANES), f32)
    for g in range(7):
        small_s[0, g : g + 1, :] = mul_exact_t(ones, ggain_s[g])[:1]
    small_s[0, 7:8, :] = jnp.broadcast_to(loss, (1, LANES))

    def bucket_sums(b, carry):
        for head in range(HEADS):
            lanes = slice(head * LANES, (head + 1) * LANES)
            hit = jnp.where(buckets == b, gbias_s[:, lanes], 0.0)
            rows_s[head, pl.ds(b, 1), :] = jnp.sum(hit, axis=0, keepdims=True)
        return carry

    lax.fori_loop(0, BUCKETS, bucket_sums, 0, unroll=2)
    for head in range(HEADS):
        sums = mul_exact_t(ones, rows_s[head])
        small_s[0, 8 + head : 9 + head, : 2 * BUCKETS] = sums[:1]
    small_steps = [
        remote(small_s.at[k], small_land.at[k], stage) for k, stage in enumerate(code_far)
    ]
    small_steps[0].start()

    for k in range(len(far)):
        finish(first0[0], first_s.at[0], land["first0"], k)
        finish(codes[0], codes_s, land["codes"], k)
        if k + 1 < len(far):
            begin(first0[0], k + 1)
            begin(codes[0], k + 1)
        small_steps[k].wait()
        small_s[k + 1] = small_s[k] + small_land[k]
        if k + 1 < len(far):
            small_steps[k + 1].start()

    first_at, first_left = first0[1], held_first[len(far) + 1 :]
    codes_at, codes_left = codes[1], held_codes[len(far) + 1 :]
    size = first_left[-1]
    mine_first = first_at + shift_of(0, first_left)
    mine_codes = codes_at + shift_of(0, codes_left, code_near)
    inside, crossing_first, everyone = [], [], []
    for mask in masks:
        source = first_s.at[0, span(first_at + shift_of(mask, first_left), size)]
        copy = remote_to(source, near_first.at[mask], device_of(mask))
        (crossing_first if mask >> (NEAR - 1) else inside).append(copy)
    for mask in masks:
        source = codes_s.at[span(codes_at + shift_of(mask, codes_left, code_near), code_size)]
        everyone.append(remote_to(source, near_codes.at[mask], device_of(mask, code_near)))

    @pl.when(section == 0)
    def _():
        for copy in inside:
            copy.start()
        cross_first.start()

    @pl.when(section == 1)
    def _():
        for copy in crossing_first:
            copy.start()

    for copy in everyone:
        copy.start()
    for step in late:
        step0(step)
    rows = code_size + n
    own_slot_s[rows + 16 :, :] = high_low(small_s[len(far)], 2)

    def keep_first(value):
        value = value.astype(bf16)
        out_ref[span(REST + mine_first, size), :] = value
        value = value.astype(f32)
        squares = jnp.sum(value * value, axis=0, keepdims=True)
        squares_s[1:2, :] = squares / (dp * size // FIRST)

    @pl.when(section == 0)
    def _():
        for copy in inside:
            copy.wait()
        for copy in crossing_first:
            copy.wait_recv()
        cross_first.wait_send()
        value = first_s[0, span(mine_first, size), :].astype(f32)
        for mask in masks:
            value = value + near_first[mask].astype(f32)
        keep_first(value)

    @pl.when(section == 1)
    def _():
        for copy in crossing_first:
            copy.wait_send()
        cross_first.wait_recv()
        value = first_s[1, span(mine_first, size), :].astype(f32)
        keep_first(value + land_first[...].astype(f32))

    place = out_ref.at[span(REST + mine_first, size)]
    copies = [
        remote_to(place, place, device_of(mask)) for mask in masks if not mask >> (NEAR - 1)
    ]
    for copy in copies:
        copy.start()
    for copy in everyone:
        copy.wait()
    value = codes_s[span(mine_codes, code_size), :].astype(f32)
    for mask in masks:
        value = value + near_codes[mask].astype(f32)
    value = value.astype(bf16)
    own_slot_s[:code_size, :] = value
    value = value.astype(f32)
    squares = jnp.sum(value * value, axis=0, keepdims=True)
    squares_s[2:3, :] = squares / (2 * dp * code_size // CODES)
    squares_s[3:, :] = jnp.zeros((5, LANES), f32)
    own_slot_s[rows : rows + 16, :] = high_low(squares_s[...], 2)
    kept_slot = out_slot_ref.at[slot]
    store_slot = pltpu.make_async_copy(own_slot_s, kept_slot, local_sems.at[BLOCKS + 2])
    store_slot.start()
    slots_out = [remote_to(own_slot_s, kept_slot, device_of(mask, code_near)) for mask in masks]
    for copy in slots_out:
        copy.start()
    store_slot.wait()
    for copy in copies + slots_out:
        copy.wait()
    for j, k in enumerate(reversed(range(len(far)))):
        copies = []
        if held_first[k + 1] < held_first[k]:
            place = out_ref.at[span(REST + first_at, held_first[k + 1])]
            copies.append(remote(place, place, far[k]))
            first_at = first_at - side_of(far[k]) * held_first[k + 1]
        slots = 2 ** (NEAR + j)
        held = out_slot_ref.at[pl.ds(lax.div(slot, slots) * slots, slots), pl.ds(0, rows + 16)]
        copies.append(remote(held, held, code_far[k]))
        for copy in copies:
            copy.start()
        for copy in copies:
            copy.wait()


def gradients(codes, users, targets, domains, bias, gains, mixer, feed, embedding, dp):
    n = users.shape[0] // 2
    chunks = n // GROUP
    order = stages(dp)
    depth = len(order)
    devices = 2 * dp
    vmem = pl.BlockSpec(memory_space=pltpu.VMEM)
    smem = pl.BlockSpec(memory_space=pltpu.SMEM)
    hbm = pl.BlockSpec(memory_space=pl.ANY)
    stat = (16, LANES)
    held_rest, held_first, held_codes = shares(dp, REST), shares(dp, FIRST), shares(dp, CODES, 1)
    plane, far = depth - 1, depth - NEAR
    slot_rows = held_codes[-1] + n + 16 + 32
    sizes = [*held_rest[1:] * 2, *held_first[1:]]
    sizes += [*held_first[1 : far + 1], *held_codes[1 : far + 1], held_rest[-1], held_first[-1]]
    lands = [pltpu.VMEM((rows, D), bf16) for rows in sizes]
    copies = 128 + 16 * depth
    return pl.pallas_call(
        functools.partial(step_kernel, n, dp),
        out_shape=(
            jax.ShapeDtypeStruct((COLS, D), bf16),
            jax.ShapeDtypeStruct((devices, 8, LANES), jnp.int32),
            jax.ShapeDtypeStruct((devices, slot_rows, LANES), bf16),
            jax.ShapeDtypeStruct((8, LANES), f32),
        ),
        in_specs=[vmem, smem, vmem, vmem, vmem, smem, vmem, hbm, hbm, hbm],
        out_specs=(vmem, hbm, hbm, vmem),
        scratch_shapes=[pltpu.VMEM((chunks, D, WIDE), f32)]
        + [
            pltpu.VMEM(shape, dtype)
            for shape, dtype in (
                ((chunks // 2, D, WIDE), f32),
                ((chunks // 2, 3 * WIDTH, SPAN), bf16),
                ((chunks // 2, GROUP, KEYS, HEADS * LANES), bf16),
                ((chunks // 2, WIDTH, SPAN), bf16),
                ((chunks // 2, FF, WIDE), bf16),
                ((chunks // 2, 2 * WIDTH, WIDE), bf16),
                ((3 * WIDTH, SPAN), bf16),
                ((chunks // 2, 32 * GROUP, LANES), f32),
                ((chunks // 2, WIDTH, 32 * GROUP), bf16),
            )
            for _ in range(2)
        ]
        + [
            pltpu.VMEM((chunks * COLUMNS * D, LANES), f32),
            pltpu.VMEM((3 * WIDTH, 2 * LANES), bf16),
            pltpu.VMEM((2, D, COLS), bf16),
            pltpu.VMEM((2, COLS, D), bf16),
            pltpu.VMEM((2 * D, CODES + n), bf16),
            pltpu.VMEM((7, D, LANES), f32),
            pltpu.VMEM((KEYS, HEADS * LANES), f32),
            pltpu.VMEM((LANES, HEADS * LANES), f32),
            pltpu.VMEM((BLOCKS, D, LANES), f32),
            pltpu.VMEM((CODES + n, D), f32),
            pltpu.VMEM((KEYS, HEADS * LANES), f32),
            pltpu.VMEM((7, D, LANES), f32),
            pltpu.VMEM((HEADS, 2 * BUCKETS, LANES), f32),
            pltpu.VMEM((n, D), f32),
            pltpu.VMEM((n, LANES), jnp.int32),
            pltpu.VMEM((WIDTH, LANES), bf16),
            pltpu.VMEM((WIDTH, LANES), bf16),
            pltpu.VMEM((2, REST, D), bf16),
            pltpu.VMEM((2, FIRST, D), bf16),
            pltpu.VMEM((CODES, D), bf16),
            pltpu.VMEM((8, LANES), jnp.int32),
            pltpu.VMEM((slot_rows, LANES), bf16),
            pltpu.VMEM((8, LANES), f32),
            pltpu.VMEM((8, WIDE), jnp.int32),
            pltpu.VMEM((CODES + n, WIDE), bf16),
            pltpu.VMEM((depth + 1,) + stat, f32),
            pltpu.VMEM((depth,) + stat, f32),
            pltpu.VMEM((far + 1, 16, LANES), f32),
            pltpu.VMEM((far, 16, LANES), f32),
            pltpu.VMEM((2**NEAR, held_first[-1], D), bf16),
            pltpu.VMEM((2**NEAR, held_codes[-1], D), bf16),
            pltpu.SemaphoreType.DMA((BLOCKS + 3,)),
            pltpu.SemaphoreType.DMA((copies,)),
            pltpu.SemaphoreType.DMA((copies,)),
        ]
        + lands,
        compiler_params=pltpu.CompilerParams(
            collective_id=0, has_side_effects=True, vmem_limit_bytes=127 * 2**19
        ),
        name="gradients",
    )(codes, users, users.reshape(1, -1), targets, domains, bias, gains, mixer, feed, embedding)


def adam(weight, moment, square, slope, rate, decay):
    moment = beta_one * moment + (1 - beta_one) * slope
    square = beta_two * square + (1 - beta_two) * slope * slope
    unbiased_moment = moment * (1 / (1 - beta_one**STEP))
    unbiased_square = square * (1 / (1 - beta_two**STEP))
    root = unbiased_square * lax.rsqrt(unbiased_square)
    divisor = root + adam_eps
    inverse = pl.reciprocal(divisor, approx=True)
    inverse = inverse * (2.0 - divisor * inverse)
    step = unbiased_moment * inverse + decay * weight
    return weight - rate * step, moment, square


def update_kernel(n, dp, *refs):
    parts_in, big_in, small_in, refs = refs[:4], refs[4:13], refs[13:19], refs[19:]
    loss_ref, norm_ref, section_ref, hist_ref = refs[:4]
    big_out, small_out, low_out, refs = refs[4:13], refs[13:19], refs[19:22], refs[22:]
    parts, hold, low_hold = refs[:4], refs[4:13], refs[13:16]
    user_grad, code_grad, part_sems, in_sems, out_sems = refs[16:]
    grad_ref, ids_ref, slot_ref, stat_ref = parts
    arrivals = [pltpu.make_async_copy(parts_in[i], parts[i], part_sems.at[i]) for i in range(4)]
    loads = [pltpu.make_async_copy(big_in[i], hold[i], in_sems.at[i]) for i in range(9)]
    for load in arrivals[1:] + arrivals[:1] + loads:
        load.start()
    for arrival in arrivals:
        arrival.wait()
    devices = slot_ref.shape[0]
    held = shares(dp, CODES, 1)
    code_size = held[-1]

    users = user_grad.shape[0]
    fit = LANES // n
    each = min(1024 // n, devices)
    span_rows = each * n
    user_grad[...] = jnp.zeros_like(user_grad)

    def scatter(part, carry):
        first = part * each
        rows = [slot_ref[first + i, code_size : code_size + n, :] for i in range(each)]
        rows = jnp.concatenate(rows, 0)
        lanes = []
        for group in range(each // fit):
            lanes.append(
                sum(ids_ref[first + group * fit + other, :1, :] for other in range(fit))
            )
        ids = jnp.concatenate(lanes, 1)

        def block_rows(block, carry):
            place = pl.ds(pl.multiple_of(block * USER_ROWS, 8), USER_ROWS)
            hit = iota((USER_ROWS, span_rows), 0) + block * USER_ROWS == ids
            user_grad[place, :] += mul(jnp.where(hit, 1.0, 0.0).astype(bf16), rows)
            return carry

        lax.fori_loop(0, users // USER_ROWS, block_rows, 0)
        return carry

    lax.fori_loop(0, devices // each, scatter, 0)

    def total(x):
        return jnp.sum(jnp.sum(x, axis=0, keepdims=True), axis=1, keepdims=True)

    route = code_stages(dp)
    depth = len(route)
    near = 2**NEAR
    top = code_size + n

    def squares_of(slot):
        value = slot_ref[slot, top : top + 16, :].astype(f32)
        return value[:8] + value[8:]

    def add(i, sums):
        first = 2 * near * i
        return tuple(
            total + sum(squares_of(first + side * near + j) for j in range(near))
            for side, total in enumerate(sums)
        )

    zero = jnp.zeros((8, LANES), f32)
    even, odd = lax.fori_loop(0, devices // (2 * near), add, (zero, zero))
    section_squares = [total(x[0:1] + x[1:2]) for x in (even, odd)]
    rest = total(even[2:3] + odd[2:3])
    first = 0
    for k, stage in enumerate(route[:-NEAR]):
        first = first + side_of(stage) * 2 ** (depth - 1 - k)
    small = jnp.zeros((16, LANES), f32)
    for i in range(near):
        value = slot_ref[first + i, top + 16 :, :].astype(f32)
        small = small + (value[:16] + value[16:])
    for slot in range(devices):
        at, kept = 0, True
        for k in range(depth):
            if slot >> (depth - 1 - k) & 1:
                kept = kept and held[k + 1] < held[k]
                at += held[k + 1]
        if kept:
            code_grad[at : at + code_size, :] = slot_ref[slot, :code_size, :]
    user_values = user_grad[...]
    rest = rest + total(user_values * user_values)
    lane, line = iota(small.shape, 1), iota(small.shape, 0)
    counted = (line < 7) | ((line > 7) & (lane < 2 * BUCKETS))
    small_kept = jnp.where(counted, small, 0.0)
    rest = rest + total(small_kept * small_kept)
    norm = jnp.sqrt(section_squares[0] + section_squares[1] + rest)
    factor = jnp.minimum(1.0, clip_norm / (norm + 1e-06))
    loss_ref[0] = small[7, 0]
    norm_ref[0] = norm[0, 0]
    for s in range(2):
        section_ref[s] = jnp.sqrt(section_squares[s])[0, 0]
    for row in range(8):
        lanes = slice((row % 2) * LANES, (row % 2 + 1) * LANES)
        hist_ref[row // 2 : row // 2 + 1, lanes] = stat_ref[row : row + 1, :]

    outs = adam(
        small_in[0][...], small_in[1][...], small_in[2][...], factor * small[:7], rate_gain, 0.0
    )
    for ref, value in zip(small_out[:3], outs):
        ref[...] = value
    for head in range(HEADS):
        for s in range(2):
            slope = factor * small[8 + head : 9 + head, s * BUCKETS : (s + 1) * BUCKETS]
            one = slice(s, s + 1)
            outs = adam(
                small_in[3][head, one, :],
                small_in[4][head, one, :],
                small_in[5][head, one, :],
                slope,
                rate_small,
                0.0,
            )
            for ref, value in zip(small_out[3:], outs):
                ref[head, one, :] = value

    stores = []

    def store(kind, place):
        first = 3 * kind
        pieces = [(hold[first + i], big_out[first + i]) for i in range(3)]
        pieces.append((low_hold[kind], low_out[kind]))
        for source, target in pieces:
            copy = pltpu.make_async_copy(
                source.at[place], target.at[place], out_sems.at[len(stores)]
            )
            copy.start()
            stores.append(copy)

    def step(kind, place, slope):
        first = 3 * kind
        outs = adam(
            hold[first][place],
            hold[first + 1][place],
            hold[first + 2][place],
            factor * slope.astype(f32),
            rate_matrix,
            decay_matrix,
        )
        for i in range(3):
            hold[first + i][place] = outs[i]
        low_hold[kind][place] = outs[0].astype(bf16)

    def rows_from(start, count):
        return pl.ds(pl.multiple_of(start, 16), count)

    def columns(kind, first, count, row):
        def one(i, carry):
            lanes = pl.ds(pl.multiple_of((first + i) * LANES, LANES), LANES)
            step(kind, (0, slice(None), lanes), grad_ref[rows_from(row + i * D, D), :])
            return carry

        lax.fori_loop(0, count, one, 0)
        store(kind, (0, slice(None), slice(first * LANES, (first + count) * LANES)))

    def lines(first, count, size, source, row):
        def one(i, carry):
            place = (rows_from(first + i * size, size), slice(None))
            step(2, place, source[rows_from(row + i * size, size), :])
            return carry

        lax.fori_loop(0, count, one, 0)
        store(2, (slice(first, first + count * size), slice(None)))

    skip = FIRST // LANES
    for i in range(3):
        loads[i].wait()
    columns(0, 0, skip // 2, REST)
    columns(0, skip // 2, skip // 2, REST + skip // 2 * D)
    columns(0, skip, MIXW // LANES - skip, 0)
    for i in range(3, 6):
        loads[i].wait()
    for part in range(2):
        first = part * FF // LANES
        columns(1, first, FF // LANES, (MIXW // LANES - skip + first) * D)
    for i in range(6, 9):
        loads[i].wait()
    for part in range(2):
        lines(part * CODES // 2, 4, LANES, code_grad, part * CODES // 2)
    parts = users // USER_ROWS
    lines(CODES, parts // 2, USER_ROWS, user_grad, 0)
    done = parts // 2 * USER_ROWS
    lines(CODES + done, parts - parts // 2, USER_ROWS, user_grad, done)
    for copy in stores:
        copy.wait()


def update(n, dp, reduced, mixers, feeds, embeds, gains, biases):
    vmem = pl.BlockSpec(memory_space=pltpu.VMEM)
    smem = pl.BlockSpec(memory_space=pltpu.SMEM)
    hbm = pl.BlockSpec(memory_space=pl.ANY)
    big = [*mixers, *feeds, *embeds]
    small = [*gains, *biases]
    low = [jax.ShapeDtypeStruct(x[0].shape, bf16) for x in (mixers, feeds, embeds)]
    users = embeds[0].shape[0] - CODES
    pieces = 4 * (6 + 4 + 4 + users // USER_ROWS)
    return pl.pallas_call(
        functools.partial(update_kernel, n, dp),
        out_shape=[
            jax.ShapeDtypeStruct((1,), f32),
            jax.ShapeDtypeStruct((1,), f32),
            jax.ShapeDtypeStruct((2,), f32),
            jax.ShapeDtypeStruct((LEVELS, CODEBOOK), f32),
        ]
        + [jax.ShapeDtypeStruct(x.shape, f32) for x in big + small]
        + low,
        in_specs=[hbm] * 13 + [vmem] * 6,
        out_specs=[smem] * 3 + [vmem] + [hbm] * 9 + [vmem] * 6 + [hbm] * 3,
        scratch_shapes=[pltpu.VMEM(x.shape, x.dtype) for x in reduced]
        + [pltpu.VMEM(x.shape, f32) for x in big]
        + [pltpu.VMEM(x.shape, bf16) for x in low]
        + [
            pltpu.VMEM((users, D), f32),
            pltpu.VMEM((CODES, D), bf16),
            pltpu.SemaphoreType.DMA((4,)),
            pltpu.SemaphoreType.DMA((9,)),
            pltpu.SemaphoreType.DMA((pieces,)),
        ],
        compiler_params=pltpu.CompilerParams(vmem_limit_bytes=62 * 2**20),
        name="update",
    )(*reduced, *big, *small)


def shards(
    history_codes,
    user_ids,
    targets,
    domains,
    mixer,
    mixer_moment,
    mixer_square,
    feed,
    feed_moment,
    feed_square,
    embedding,
    embedding_moment,
    embedding_square,
    gains,
    gains_moment,
    gains_square,
    position_bias,
    bias_moment,
    bias_square,
):
    def turned(table):
        return jnp.transpose(table, (2, 0, 1))

    biases = [turned(x) for x in (position_bias, bias_moment, bias_square)]
    reduced = gradients(
        history_codes,
        user_ids,
        targets.T,
        domains.reshape(1, -1),
        biases[0],
        gains,
        mixer,
        feed,
        embedding,
        lax.axis_size("dp"),
    )
    outs = update(
        history_codes.shape[0] // 2,
        lax.axis_size("dp"),
        reduced,
        (mixer, mixer_moment, mixer_square),
        (feed, feed_moment, feed_square),
        (embedding, embedding_moment, embedding_square),
        (gains, gains_moment, gains_square),
        biases,
    )
    loss, norm, sections, histograms = outs[:4]
    back = [jnp.transpose(x, (1, 2, 0)) for x in outs[16:19]]
    return (
        loss.reshape(()),
        norm.reshape(()),
        sections,
        histograms,
        *outs[4:16],
        *back,
        *outs[19:],
    )


def solution(mesh):
    by_dp, by_pipe, copied = P("dp"), P("pipe"), P()
    return jax.shard_map(
        shards,
        mesh=mesh,
        in_specs=(by_dp,) * 4 + (by_pipe,) * 6 + (copied,) * 9,
        out_specs=(copied,) * 4 + (by_pipe,) * 6 + (copied,) * 9 + (by_pipe,) * 2 + (copied,),
        check_vma=False,
    )
```

```python
import functools

import jax
import jax.numpy as jnp
from jax import lax
from jax.experimental import pallas as pl
from jax.experimental.pallas import tpu as pltpu
from jax.sharding import PartitionSpec as P

D = 128
HEADS = 6
HEAD_DIM = 64
FF = 1024
CODEBOOK = 256
LEVELS = 4
BUCKETS = 32
DOMAINS = 3
HIST_LEN = 81
STEP = 5
CODES = 1024
LANES = 128
WIDTH = HEADS * HEAD_DIM
MIXW = 6 * WIDTH
COLS = MIXW + 2 * FF
BLOCKS = COLS // LANES
KEYS = 96
GROUP = 8
BATCH = 2
NEAR = 3
PACK = 96
WIDE = GROUP * PACK
SPAN = GROUP * LANES
COLUMNS = WIDE // LANES
PAIRS = HEADS // 2
FIRST = 4 * WIDTH
REST = COLS - FIRST
USER_ROWS = 400
MESH = pl.DeviceIdType.MESH

norm_eps = 1e-06
beta_one = 0.9
beta_two = 0.999
adam_eps = 1e-08
clip_norm = 0.5
rate_matrix = 0.04
rate_gain = 0.8
rate_small = 0.3
decay_matrix = 0.01

f32 = jnp.float32
bf16 = jnp.bfloat16


def iota(shape, axis):
    return lax.broadcasted_iota(jnp.int32, shape, axis)


def mul(left, right):
    return jnp.dot(left, right, preferred_element_type=f32)


def mul_t(left, right):
    return lax.dot_general(left, right, (((1,), (1,)), ((), ())), preferred_element_type=f32)


def mul_exact(left, right):
    return jnp.dot(left, right, preferred_element_type=f32, precision=lax.Precision.HIGHEST)


def mul_exact_t(left, right):
    return lax.dot_general(
        left,
        right,
        (((1,), (1,)), ((), ())),
        preferred_element_type=f32,
        precision=lax.Precision.HIGHEST,
    )


def onehot(ids, rows):
    return jnp.where(iota((rows, ids.shape[1]), 0) == ids, 1.0, 0.0).astype(bf16)


def inverse_rms(x):
    return lax.rsqrt(jnp.mean(x * x, axis=0, keepdims=True) + norm_eps)


def norm_low(x, inverse, gain):
    return (x * inverse * gain).astype(bf16)


def norm_back(x, inverse, gain, upstream):
    scaled = x * inverse
    inner = upstream * gain
    back = inverse * (inner - scaled * jnp.mean(inner * scaled, axis=0, keepdims=True))
    return back, upstream * scaled


def block_diag(pair):
    zero = jnp.zeros((HEAD_DIM, LANES), pair.dtype)
    left = jnp.concatenate([pair[:HEAD_DIM], zero], 0)
    right = jnp.concatenate([zero, pair[HEAD_DIM:]], 0)
    return jnp.concatenate([left, right], 1)


def diagonal(both):
    return jnp.concatenate([both[:HEAD_DIM, :LANES], both[HEAD_DIM:, LANES:]], 0)


def turn(x, shift):
    return x if shift % LANES == 0 else pltpu.roll(x, shift % LANES, 1)


def pack(tables):
    lane = iota(tables[0].shape, 1)
    columns = []
    for first in range(0, len(tables), 4):
        turned = [turn(tables[first + i], PACK * i) for i in range(4)]
        for i in range(3):
            columns.append(jnp.where(lane < PACK - 32 * i, turned[i], turned[i + 1]))
    return jnp.concatenate(columns, 1)


def unpack(x):
    lane = iota((x.shape[0], LANES), 1)
    tables = []
    for first in range(0, x.shape[1] // LANES, 3):
        a, b, c = [x[:, (first + i) * LANES : (first + i + 1) * LANES] for i in range(3)]
        tables.append(a)
        tables.append(jnp.where(lane < 32, turn(a, 32), turn(b, 32)))
        tables.append(jnp.where(lane < 64, turn(b, 64), turn(c, 64)))
        tables.append(turn(c, 96))
    return tables


def stack(both):
    return jnp.concatenate([both[:, :LANES], both[:, LANES:]], 0)


def pad_keys(table):
    if table.shape[0] == LANES:
        return table
    zero = jnp.zeros((LANES - table.shape[0], table.shape[1]), table.dtype)
    return jnp.concatenate([table, zero], 0)


def columns_of(table, i):
    return table[:, 2 * i * LANES : 2 * (i + 1) * LANES]


def attend(keys, queries, values, bias):
    scores = [mul(key, block_diag(query)) for key, query in zip(keys, queries)]
    scores = jnp.concatenate(scores, 1) + bias
    top = jnp.max(scores, axis=0, keepdims=True)
    chance = jnp.exp(scores - top)
    total = jnp.sum(chance, axis=0, keepdims=True)
    chance = (chance * (1.0 / total)).astype(bf16)
    full = pad_keys(chance)
    mixed = [mul(value, columns_of(full, i)) for i, value in enumerate(values)]
    return chance, [diagonal(both).astype(bf16) for both in mixed]


def attend_back(keys_t, queries, values, back_mixed, chance):
    exact = chance.astype(f32)
    back_chance = [mul(value, block_diag(back)) for value, back in zip(values, back_mixed)]
    back_chance = jnp.concatenate(back_chance, 1)
    inner = jnp.sum(back_chance * exact, axis=0, keepdims=True)
    back_scores = exact * (back_chance - inner)
    low = pad_keys(back_scores.astype(bf16))
    full = pad_keys(chance)
    count = range(len(queries))
    back_query = [mul(keys_t[i], columns_of(low, i)) for i in count]
    back_keys = [mul_t(queries[i], stack(columns_of(low, i))) for i in count]
    back_values = [mul_t(back_mixed[i], stack(columns_of(full, i))) for i in count]
    results = [
        [diagonal(both).astype(bf16) for both in part]
        for part in (back_query, back_keys, back_values)
    ]
    return *results, back_scores


def split_low(x):
    high = x.astype(bf16)
    return jnp.concatenate([high, (x - high.astype(f32)).astype(bf16)], 0)


def stages(dp):
    bits = [2**k for k in range(dp.bit_length() - 1)]
    return [("dp", bit) for bit in bits[:2] + bits[4:] + bits[2:4]] + [("pipe", 1)]


def code_stages(dp):
    order = stages(dp)
    return order[:1] + order[2:-NEAR] + order[-1:] + order[1:2] + order[-NEAR:-1]


def high_low(x, parts):
    rows = []
    for _ in range(parts):
        rows.append(x.astype(bf16))
        x = x - rows[-1].astype(f32)
    return jnp.concatenate(rows, 0)


def side_of(stage):
    axis, bit = stage
    return lax.rem(lax.div(lax.axis_index(axis), bit), 2)


def partner_of(stage):
    axis, bit = stage
    return {axis: lax.axis_index(axis) + bit * (1 - 2 * side_of(stage))}


def shares(dp, rows, across=0):
    held = [rows]
    depth = len(stages(dp)) - 1
    for k in range(depth + across):
        later = min(NEAR - 1, depth - 1 - k) + across if k < depth else 0
        half = held[-1] // 2
        held.append(half if half % (16 * 2**later) == 0 else held[-1])
    return held


def span(start, size):
    return pl.ds(pl.multiple_of(start, 16), size)


def step_kernel(n, dp, *refs):
    codes_ref, users_ref, user_row_ref, targets_ref, domains_ref, bias_ref, gains_ref = refs[:7]
    mixer_ref, feed_ref, embed_ref = refs[7:10]
    out_ref, out_ids_ref, out_slot_ref, out_stat_ref = refs[10:14]
    refs = refs[14:]
    x0_s, *doubles = refs[0], *[refs[1 + 2 * i : 3 + 2 * i] for i in range(9)]
    x1_s, qkv_s, p_s, o_s, r_s, mem_s, dqkv_s, pc_s, oc_s = doubles
    refs = refs[19:]
    x2_s, dz_s, wn_s, wt_s, ext_s = refs[:5]
    gain_s, ebias_s, dbias_s, g0_s, ge_s, gbias_s, ggain_s, rows_s, user_s, ids_s = refs[5:15]
    cross_s, cross_back_s, rest_s, first_s, codes_s, slot_s, own_slot_s, squares_s, id_rows_s, hot_s = refs[15:25]
    stat_s, stat_land, small_s, small_land, near_first, near_codes = refs[25:31]
    local_sems, sends, recvs = refs[31:34]
    lands = refs[34:]
    order = stages(dp)
    across = order[-1]
    depth = len(order)
    chunks = n // GROUP
    section = lax.axis_index("pipe")
    used = [0]

    def remote_to(source, target, device):
        index = used[0]
        used[0] += 1
        return pltpu.make_async_remote_copy(
            src_ref=source,
            dst_ref=target,
            send_sem=sends.at[index],
            recv_sem=recvs.at[index],
            device_id=device,
            device_id_type=MESH,
        )

    def remote(source, target, stage):
        return remote_to(source, target, partner_of(stage))

    near, far = order[-NEAR:], order[:-NEAR]
    route = code_stages(dp)
    code_near, code_far = route[-NEAR:], route[:-NEAR]
    masks = range(1, 2**NEAR)

    def device_of(mask, near=near):
        place = {"dp": lax.axis_index("dp"), "pipe": lax.axis_index("pipe")}
        for i, (axis, bit) in enumerate(near):
            if mask >> i & 1:
                place[axis] = place[axis] + bit * (1 - 2 * side_of((axis, bit)))
        return place

    def shift_of(mask, lefts, near=near):
        total = 0
        for i, left in enumerate(lefts):
            side = side_of(near[i])
            total = total + (1 - side if mask >> i & 1 else side) * left
        return total

    locals_in = []
    for block in range(BLOCKS):
        lanes = slice(block * LANES, (block + 1) * LANES)
        if block < MIXW // LANES:
            source = mixer_ref.at[0, :, lanes]
        else:
            source = feed_ref.at[0, :, slice(lanes.start - MIXW, lanes.stop - MIXW)]
        locals_in.append(pltpu.make_async_copy(source, g0_s.at[block], local_sems.at[block]))
    vocabulary = embed_ref.shape[0]
    flat = x2_s.at[pl.ds(0, vocabulary)]
    load_embed = pltpu.make_async_copy(embed_ref, flat, local_sems.at[BLOCKS])
    for copy in locals_in:
        copy.start()
    load_embed.start()

    barrier = pltpu.get_barrier_semaphore()
    greeted = [partner_of(stage) for stage in far if stage != code_near[0]]
    greeted += [device_of(mask) for mask in masks]
    greeted += [device_of(mask, code_near) for mask in masks if mask & 1]
    for device in greeted:
        pl.semaphore_signal(barrier, inc=1, device_id=device, device_id_type=MESH)

    ids_s[:, : HIST_LEN - 1] = codes_ref[pl.ds(pl.multiple_of(section * n, 8), n), :]
    lane, row = iota((n, LANES), 1), iota((n, LANES), 0)
    ids = ids_s[...] + ((lane & 3) << 8)
    ids = jnp.where(lane < HIST_LEN - 1, ids, jnp.where(lane == HIST_LEN - 1, CODES + row, -1))
    ids_s[...] = ids
    packed = []
    for i in range(GROUP):
        rows = [ids_s[c * GROUP + i : c * GROUP + i + 1, :] for c in range(chunks)]
        rows += [jnp.zeros((8 - chunks, LANES), jnp.int32)]
        packed.append(jnp.concatenate(rows, 0))
    id_rows_s[...] = pack(packed)
    count = targets_ref.shape[1]
    history, token = iota((count, LANES), 0), iota((count, LANES), 1)
    pick = jnp.where((token >> 2) + section * n == history, 1.0, 0.0)
    level, place = iota((LEVELS, LANES), 0), iota((LEVELS, LANES), 1) & 3
    target = mul(targets_ref[...].astype(f32), pick) + (level * CODEBOOK).astype(f32)
    goal = jnp.sum(jnp.where(level == place, target, 0.0), axis=0, keepdims=True).astype(jnp.int32)
    start_ids = jnp.sum(
        jnp.where(level == place - 1, target, 0.0), axis=0, keepdims=True
    ).astype(jnp.int32)
    domain = mul(domains_ref[...].astype(f32), pick)
    pick = jnp.where(lax.rem(token, n) + section * n == history, 1.0, 0.0)
    own_users = mul_exact(user_row_ref[...].astype(f32), pick)

    counts = [
        jnp.sum(jnp.where(domain == d, 1.0, 0.0), axis=1, keepdims=True) for d in range(DOMAINS)
    ]
    counts += [jnp.zeros((1, 1), f32)] * (8 - DOMAINS)
    stat_s[0, 8:, :] = jnp.broadcast_to(jnp.concatenate(counts, 0), (8, LANES))
    histogram = mul_t(jnp.ones((8, LANES), bf16), onehot(goal, CODES))
    for r in range(8):
        stat_s[0, r : r + 1, :] = histogram[:1, r * LANES : (r + 1) * LANES]
    slot = 0
    for k, stage in enumerate(route):
        slot = slot + side_of(stage) * 2 ** (depth - 1 - k)
    owner = iota((8, LANES), 1) // n
    own_users = jnp.broadcast_to(own_users, (8, LANES)).astype(jnp.int32)
    slot_s[...] = jnp.where(owner == lax.rem(slot, LANES // n), own_users, 0)
    store_ids = pltpu.make_async_copy(slot_s, out_ids_ref.at[slot], local_sems.at[BLOCKS + 1])
    store_ids.start()
    store_ids.wait()

    def slots_of(j):
        return pl.ds(lax.div(slot, 2**j) * 2**j, 2**j)

    for g in range(7):
        gain_s[g] = jnp.broadcast_to(gains_ref[g : g + 1, :], (LANES, LANES)).T

    def positions(axis):
        index = iota((KEYS, LANES), axis)
        return jnp.where(index == HIST_LEN - 1, 0, index + 1)

    key, query = positions(0), positions(1)
    distance = jnp.abs(query - key)
    remoteness = jnp.zeros_like(distance)
    for edge in (12, 16, 23, 32, 46, 64, 91):
        remoteness = remoteness + (distance >= edge).astype(jnp.int32)
    nearby = jnp.minimum(jnp.where(distance < 8, distance, 8 + remoteness), 15)
    buckets = nearby + jnp.where(key > query, 16, 0)
    real = iota((KEYS, LANES), 0) < HIST_LEN
    for head in range(HEADS):
        lanes = slice(head * LANES, (head + 1) * LANES)

        def choose(b, table):
            return jnp.where(buckets == b, bias_ref[head, 0, b], table)

        table = lax.fori_loop(0, BUCKETS, choose, jnp.zeros((KEYS, LANES), f32), unroll=8)
        ebias_s[:, lanes] = jnp.where(real, table, -1e30)
    key, query = iota((LANES, LANES), 0), iota((LANES, LANES), 1)
    offset = query - key
    seen = ((key >> 2) == (query >> 2)) & (offset >= 0)
    for head in range(HEADS):
        lanes = slice(head * LANES, (head + 1) * LANES)
        table = jnp.full((LANES, LANES), -1e30, f32)
        for b in range(LEVELS):
            table = jnp.where(seen & (offset == b), bias_ref[head, 1, b], table)
        dbias_s[:, lanes] = table

    scale = HEAD_DIM**-0.5
    cross_scale = jnp.where(section == 1, scale, 1.0).astype(f32)
    for copy in locals_in:
        copy.wait()
    def cast_weights(block, carry):
        factor = jnp.where((block >= 12) & (block < 15), cross_scale, 1.0)
        factor = jnp.where(block < 3, scale, factor)
        lanes = pl.ds(pl.multiple_of(block * LANES, LANES), LANES)
        wn_s[section, :, lanes] = (g0_s[block] * factor).astype(bf16)
        return carry

    lax.fori_loop(0, BLOCKS, cast_weights, 0, unroll=2)
    pl.semaphore_wait(barrier, len(greeted))
    half = D // 2
    mine = span(side_of(order[0]) * half, half)
    pieces = (slice(0, FIRST), slice(FIRST, COLS))
    over = [
        remote(wn_s.at[section, mine, piece], wn_s.at[section, mine, piece], across)
        for piece in pieces
    ]
    for copy in over:
        copy.start()

    early = []
    for j, stage in enumerate(reversed(route)):
        held = out_ids_ref.at[slots_of(j)]
        early.append(
            (
                remote(stat_s.at[j], stat_land.at[j], stage),
                remote(held, held, stage),
            )
        )

    def early_step(j):
        if j > 0:
            for copy in early[j - 1]:
                copy.wait()
            stat_s[j] = stat_s[j - 1] + stat_land[j - 1]
        if j < depth:
            for copy in early[j]:
                copy.start()

    eye = jnp.where(iota((LANES, LANES), 0) == iota((LANES, LANES), 1), 1.0, 0.0).astype(bf16)
    load_embed.wait()

    def fetch(i, carry):
        user_s[pl.ds(i, 1), :] = x2_s[pl.ds(CODES + users_ref[section * n + i], 1), :]
        return carry

    lax.fori_loop(0, n, fetch, 0, unroll=4)
    for block in range(CODES // LANES + 1):
        if block < CODES // LANES:
            rows = x2_s[block * LANES : (block + 1) * LANES, :]
            codes_s[block * LANES : (block + 1) * LANES, :] = rows.astype(bf16)
            width = LANES
        else:
            rows = user_s[...]
            width = n
        high = rows.astype(bf16)
        low = (rows - high.astype(f32)).astype(bf16)
        lanes = slice(block * LANES, block * LANES + width)
        ext_s[:D, lanes] = mul_t(eye, high).astype(bf16)
        ext_s[D:, lanes] = mul_t(eye, low).astype(bf16)

    def find(c):
        ids = id_rows_s[pl.ds(c, 1), :]
        for first in range(0, CODES + n, LANES):
            rows = min(LANES, CODES + n - first)
            hot_s[first : first + rows, :] = onehot(ids - first, rows)

    def lookup(c, carry):
        find(c)
        both = mul(ext_s[...], hot_s[...])
        x0_s[c] = both[:D] + both[D:]
        return carry

    lax.fori_loop(0, chunks, lookup, 0)

    beside = []
    for piece in pieces:
        came = wn_s.at[1 - section, mine, piece]
        beside.append(remote(came, came, order[0]))
    over[0].wait()
    beside[0].start()

    def transpose_weights(which, first, last):
        def one(block, carry):
            place = pl.ds(pl.multiple_of(block * LANES, LANES), LANES)
            wt_s[which, place, :] = wn_s[which, :, place].T
            return carry

        lax.fori_loop(first, last, one, 0, unroll=2)

    transpose_weights(section, 0, BLOCKS)
    beside[0].wait()
    transpose_weights(1 - section, 0, FIRST // LANES)

    def rest_passes():
        over[1].wait()
        beside[1].start()

    def rest_arrives():
        beside[1].wait()
        transpose_weights(1 - section, FIRST // LANES, BLOCKS)

    def gain(g, width):
        column = gain_s[g]
        return column if width == LANES else jnp.concatenate([column] * (width // LANES), 1)

    def lockstep(steps, point=None):
        for number, _ in enumerate(zip(*steps)):
            if point is not None:
                point(number)

    def at_time(t, steps):
        for time, step in enumerate(steps):
            if step is not None:
                pl.when(t == time)(step)

    def spread_low(x):
        return jnp.concatenate([part.astype(bf16) for part in unpack(x)], 1)

    def packed(x):
        return pack([x[:, i * LANES : (i + 1) * LANES] for i in range(GROUP)])

    def part_of(j):
        return slice(j * LANES, (j + 1) * LANES)

    def encode_steps(t, half):
        c = 2 * t + half
        qkv, o, r = qkv_s[half], o_s[half], r_s[half]
        x0 = x0_s[c]
        h = spread_low(x0 * inverse_rms(x0) * gain(0, WIDE))
        yield
        for j in range(3):
            part = slice(j * WIDTH, (j + 1) * WIDTH)
            qkv[t, part, :] = mul(wt_s[0, part, :], h).astype(bf16)
        yield
        for first in range(0, GROUP, BATCH):
            queries, keys, values = [], [], []
            for i in range(first, first + BATCH):
                lanes = slice(i * LANES, (i + 1) * LANES)
                queries += [qkv[t, part_of(j), lanes] for j in range(PAIRS)]
                keys += [qkv[t, part_of(PAIRS + j), lanes].T[:KEYS] for j in range(PAIRS)]
                values += [qkv[t, part_of(2 * PAIRS + j), lanes] for j in range(PAIRS)]
            bias = jnp.concatenate([ebias_s[...]] * BATCH, 1)
            chance, mixed = attend(keys, queries, values, bias)
            for i in range(BATCH):
                lanes = slice((first + i) * LANES, (first + i + 1) * LANES)
                own = slice(i * HEADS * LANES, (i + 1) * HEADS * LANES)
                p_s[half][t, first + i] = chance[:, own]
                o[t, :, lanes] = jnp.concatenate(mixed[i * PAIRS : (i + 1) * PAIRS], 0)
            yield
        x1 = x0 + packed(mul(wn_s[0, :, 3 * WIDTH : 4 * WIDTH], o[t]))
        x1_s[half][t] = x1
        yield
        h = norm_low(x1, inverse_rms(x1), gain(1, WIDE))
        for j in range(2):
            part = slice(j * FF // 2, (j + 1) * FF // 2)
            lifted = mul(wt_s[0, MIXW + j * FF // 2 : MIXW + (j + 1) * FF // 2, :], h)
            r[t, part, :] = jnp.maximum(lifted, 0.0).astype(bf16)
        yield
        x2 = x1 + mul(wn_s[0, :, MIXW + FF :], r[t])
        put_wide(x2_s, c, x2)
        e = norm_low(x2, inverse_rms(x2), gain(2, WIDE))
        yield
        for j in range(2):
            part = slice(j * WIDTH, (j + 1) * WIDTH)
            mem_s[half][t, part, :] = mul(
                wt_s[0, 4 * WIDTH + j * WIDTH : 4 * WIDTH + (j + 1) * WIDTH, :], e
            ).astype(bf16)
        yield

    attention = GROUP // BATCH
    pairs = chunks // 2

    def early_at(place, places):
        return [
            functools.partial(early_step, place + places * t)
            if place + places * t <= depth
            else None
            for t in range(pairs)
        ]

    def encode(t, carry):
        at_time(t, early_at(0, 3))

        def point(number):
            if number == attention // 2:
                pl.when(t == 0)(rest_passes)
                at_time(t, early_at(1, 3))
            if number == attention + 2:
                pl.when(t == 0)(rest_arrives)
                at_time(t, early_at(2, 3))

        lockstep([encode_steps(t, 0), encode_steps(t, 1)], point)
        return carry

    def put_wide(ref, c, value):
        for i in range(COLUMNS):
            ref[pl.ds(pl.multiple_of((COLUMNS * c + i) * D, D), D), :] = value[
                :, i * LANES : (i + 1) * LANES
            ]

    def get_wide(ref, c):
        return jnp.concatenate(
            [ref[pl.ds(pl.multiple_of((COLUMNS * c + i) * D, D), D), :] for i in range(COLUMNS)], 1
        )

    lax.fori_loop(0, pairs, encode, 0)
    for j in range(3 * pairs, depth + 1):
        early_step(j)
    out_stat_ref[...] = stat_s[depth, :8, :]

    def put_blocks(first, value):
        for index in range(value.shape[1] // LANES):
            block = first + index
            part = value[:, index * LANES : (index + 1) * LANES].astype(bf16)
            if block < FIRST // LANES:
                first_s[1, block * D : (block + 1) * D, :] = part
            else:
                block -= FIRST // LANES
                rest_s[1, block * D : (block + 1) * D, :] = part

    def add_blocks(first, value):
        for index in range(value.shape[1] // LANES):
            g0_s[first + index] += value[:, index * LANES : (index + 1) * LANES]

    start = onehot(start_ids, CODES)
    both = mul(ext_s[:, :CODES], start)
    y0 = both[:D] + both[D:]
    inverse0 = inverse_rms(y0)
    h0 = norm_low(y0, inverse0, gain(3, LANES))
    dz_s[:, :LANES] = mul(wt_s[1, : 3 * WIDTH, :], h0).astype(bf16)
    both = mul(mul_t(eye, h0).astype(bf16), wn_s[1, :, WIDTH : 3 * WIDTH]).astype(bf16)
    self_chance, mixed = attend(
        [both[:, part_of(j)] for j in range(PAIRS)],
        [dz_s[part_of(j), :LANES] for j in range(PAIRS)],
        [dz_s[part_of(2 * PAIRS + j), :LANES] for j in range(PAIRS)],
        dbias_s[...],
    )
    self_values = both[:, WIDTH:]
    self_mixed = jnp.concatenate(mixed, 0)
    y1 = y0 + mul(wn_s[1, :, 3 * WIDTH : 4 * WIDTH], self_mixed)
    inverse1 = inverse_rms(y1)
    h1 = norm_low(y1, inverse1, gain(4, LANES))
    cross_s[...] = mul(wt_s[1, 4 * WIDTH : 5 * WIDTH, :], h1).astype(bf16)

    def spreader(g, turned):
        shape = (LANES, 32 * GROUP) if turned else (32 * GROUP, LANES)
        row, token = iota(shape, 1 if turned else 0), iota(shape, 0 if turned else 1)
        hit = token == 4 * GROUP * g + 4 * (row >> 5) + (row & 3)
        return jnp.where(hit, 1.0, 0.0).astype(bf16)

    def rows_of(g, table):
        rows = mul_t(spreader(g, False), table)
        mask = (iota(rows.shape, 1) >> 6) == ((iota(rows.shape, 0) & 31) >> 2)
        return jnp.where(mask, rows, 0.0).astype(bf16)

    def head_mask(shape):
        return (iota(shape, 0) >> 6) == ((iota(shape, 1) & 31) >> 2)

    def rows_t_of(g, table):
        rows = mul(table, spreader(g, True))
        return jnp.where(head_mask(rows.shape), rows, 0.0).astype(bf16)

    def gather_rows(ref):
        total = jnp.zeros((WIDTH, LANES), f32)
        for g in range(chunks):
            total = total + mul(ref[g % 2][g // 2], spreader(g, False))
        return total.astype(bf16)

    def blocks_of(table):
        rows = []
        for i in range(GROUP):
            part = table[32 * i : 32 * i + 32]
            column, shift = divmod(PACK * i, LANES)
            part = turn(part, shift)
            lane = iota(part.shape, 1)
            zero = jnp.zeros_like(part)
            columns = [zero] * COLUMNS
            columns[column] = jnp.where(lane >= shift, part, 0.0)
            if shift > LANES - PACK:
                columns[column + 1] = jnp.where(lane < shift, part, 0.0)
            rows.append(jnp.concatenate(columns, 1))
        return jnp.concatenate(rows, 0).astype(bf16)

    def row_products(rows, keys):
        both = mul(rows, keys)
        parts = []
        for i in range(GROUP):
            own = both[32 * i : 32 * i + 32]
            column, shift = divmod(PACK * i, LANES)
            part = turn(own[:, column * LANES : (column + 1) * LANES], -shift)
            if shift > LANES - PACK:
                after = turn(own[:, (column + 1) * LANES : (column + 2) * LANES], -shift)
                part = jnp.where(iota(part.shape, 1) < LANES - shift, part, after)
            parts.append(part)
        return jnp.concatenate(parts, 0)

    def cross_steps(t, half):
        g = 2 * t + half
        queries = rows_of(g, cross_s[...])
        yield
        scores = row_products(queries, mem_s[half][t, :WIDTH, :])
        scores = jnp.where(iota(scores.shape, 1) < HIST_LEN, scores, -1e30)
        chance = jnp.exp(scores - jnp.max(scores, axis=1, keepdims=True))
        chance = chance * (1.0 / jnp.sum(chance, axis=1, keepdims=True))
        pc_s[half][t] = chance
        yield
        mixed = mul_t(mem_s[half][t, WIDTH:, :], blocks_of(chance))
        oc_s[half][t] = jnp.where(head_mask(mixed.shape), mixed, 0.0).astype(bf16)
        yield

    def cross(t, carry):
        lockstep([cross_steps(t, 0), cross_steps(t, 1)])
        return carry

    lax.fori_loop(0, pairs, cross, 0)
    cross_mixed = gather_rows(oc_s)
    y2 = y1 + mul(wn_s[1, :, 5 * WIDTH : 6 * WIDTH], cross_mixed)
    inverse2 = inverse_rms(y2)
    h2 = norm_low(y2, inverse2, gain(5, LANES))
    lifted = mul(wt_s[1, MIXW : MIXW + FF, :], h2)
    active = jnp.maximum(lifted, 0.0).astype(bf16)
    y3 = y2 + mul(wn_s[1, :, MIXW + FF :], active)
    inverse3 = inverse_rms(y3)
    final = norm_low(y3, inverse3, gain(6, LANES))
    logits = mul(codes_s[...], final)
    top = jnp.max(logits, axis=0, keepdims=True)
    log_total = top + jnp.log(jnp.sum(jnp.exp(logits - top), axis=0, keepdims=True))
    match = iota(logits.shape, 0) == goal
    picked = jnp.sum(jnp.where(match, logits, 0.0), axis=0, keepdims=True)
    weight = jnp.zeros((1, LANES), f32)
    for d in range(DOMAINS):
        share = 1.0 / (DOMAINS * jnp.maximum(stat_s[depth, 8 + d : 9 + d, :], 1.0))
        weight = weight + jnp.where(domain == d, share, 0.0)
    loss = jnp.sum(weight * (log_total - picked), axis=1, keepdims=True)
    back_logits = (
        weight * (jnp.exp(logits - log_total) - jnp.where(match, 1.0, 0.0))
    ).astype(bf16)
    back_final = mul(ext_s[:D, :CODES], back_logits)
    table_grad = mul_t(back_logits, final)
    back, gain_grad = norm_back(y3, inverse3, gain(6, LANES), back_final)
    ggain_s[6] = gain_grad
    low = back.astype(bf16)
    put_blocks(26, mul_t(low, active))
    back_lifted = jnp.where(lifted > 0, mul(wt_s[1, MIXW + FF :, :], low), 0.0).astype(bf16)
    put_blocks(18, mul_t(h2, back_lifted))
    more, gain_grad = norm_back(
        y2, inverse2, gain(5, LANES), mul(wn_s[1, :, MIXW : MIXW + FF], back_lifted)
    )
    ggain_s[5] = gain_grad
    back = back + more
    low = back.astype(bf16)
    put_blocks(15, mul_t(low, cross_mixed))
    cross_back_s[...] = mul(wt_s[1, 5 * WIDTH : 6 * WIDTH, :], low).astype(bf16)

    def cross_back_steps(t, half):
        g = 2 * t + half
        memory = mem_s[half]
        mixed_rows = rows_of(g, cross_back_s[...])
        queries_t = rows_t_of(g, cross_s[...])
        mixed_t = rows_t_of(g, cross_back_s[...])
        yield
        back_chance = row_products(mixed_rows, memory[t, WIDTH:, :])
        back_chance = jnp.where(iota(back_chance.shape, 1) < HIST_LEN, back_chance, 0.0)
        chance = pc_s[half][t]
        inner = jnp.sum(back_chance * chance, axis=1, keepdims=True)
        yield
        spread = blocks_of(chance * (back_chance - inner))
        total = mul_t(memory[t, :WIDTH, :], spread)
        oc_s[half][t] = jnp.where(head_mask(total.shape), total, 0.0).astype(bf16)
        yield
        memory[t, :WIDTH, :] = mul(queries_t, spread).astype(bf16)
        memory[t, WIDTH:, :] = mul(mixed_t, blocks_of(chance)).astype(bf16)
        yield

    def cross_back(t, carry):
        lockstep([cross_back_steps(t, 0), cross_back_steps(t, 1)])
        return carry

    lax.fori_loop(0, pairs, cross_back, 0)
    back_query = gather_rows(oc_s)
    put_blocks(12, mul_t(h1, back_query) * HEAD_DIM**-0.5)
    more, gain_grad = norm_back(
        y1, inverse1, gain(4, LANES), mul(wn_s[1, :, 4 * WIDTH : 5 * WIDTH], back_query)
    )
    ggain_s[4] = gain_grad
    back = back + more
    low = back.astype(bf16)
    put_blocks(9, mul_t(low, self_mixed))
    back_mixed = mul(wt_s[1, 3 * WIDTH : 4 * WIDTH, :], low).astype(bf16)
    *back_parts, self_scores = attend_back(
        [dz_s[part_of(PAIRS + j), :LANES] for j in range(PAIRS)],
        [dz_s[part_of(j), :LANES] for j in range(PAIRS)],
        [self_values[:, part_of(j)] for j in range(PAIRS)],
        [back_mixed[part_of(j)] for j in range(PAIRS)],
        self_chance,
    )
    dz_s[:, LANES:] = jnp.concatenate([x for part in back_parts for x in part], 0)
    put_blocks(0, mul_t(h0, dz_s[:WIDTH, LANES : 2 * LANES]) * HEAD_DIM**-0.5)
    put_blocks(3, mul_t(h0, dz_s[WIDTH:, LANES : 2 * LANES]))
    more, gain_grad = norm_back(
        y0, inverse0, gain(3, LANES), mul(wn_s[1, :, : 3 * WIDTH], dz_s[:, LANES : 2 * LANES])
    )
    ggain_s[3] = gain_grad
    back = back + more
    spread = mul_t(start, split_low(back))
    ge_s[:CODES, :] = table_grad + spread[:, :D] + spread[:, D:]
    ge_s[CODES:, :] = jnp.zeros((n, D), f32)
    rows_s[...] = jnp.zeros_like(rows_s)
    for head in range(HEADS):
        lanes = slice(head * LANES, (head + 1) * LANES)
        for b in range(LEVELS):
            hit = jnp.where(offset == b, self_scores[:, lanes], 0.0)
            rows_s[head, BUCKETS + b : BUCKETS + b + 1, :] = jnp.sum(hit, axis=0, keepdims=True)

    def reducing(buffer, kept, held, stages):
        steps, at = [], 0
        for k, stage in enumerate(stages):
            rows, left = held[k], held[k + 1]
            side = side_of(stage)
            if left < rows:
                source = buffer.at[span(at + (1 - side) * left, left)]
                at = at + side * left
            else:
                source = buffer.at[span(at, rows)]
            steps.append((remote(source, kept[k], stage), at, left))
        return steps, at, held

    def begin(steps, k):
        steps[k][0].start()

    def finish(steps, buffer, kept, k):
        copy, at, left = steps[k]
        copy.wait()
        place = span(at, left)
        total = buffer[place, :].astype(f32) + kept[k][...].astype(f32)
        buffer[place, :] = total.astype(bf16)

    flat_depth = depth - 1
    held_rest, held_first, held_codes = shares(dp, REST), shares(dp, FIRST), shares(dp, CODES, 1)
    land, rest = {}, lands
    for name, number in (
        ("rest0", flat_depth),
        ("rest1", flat_depth),
        ("first1", flat_depth),
        ("first0", len(far)),
        ("codes", len(far)),
    ):
        land[name], rest = rest[:number], rest[number:]
    land_rest, land_first = rest
    rest1 = reducing(rest_s.at[1], land["rest1"], held_rest, order[:-1])
    first1 = reducing(first_s.at[1], land["first1"], held_first, order[:-1])
    rest0 = reducing(rest_s.at[0], land["rest0"], held_rest, order[:-1])
    first0 = reducing(first_s.at[0], land["first0"], held_first, far)
    codes = reducing(codes_s, land["codes"], held_codes, code_far)

    def step1(k):
        if k > 0:
            finish(rest1[0], rest_s.at[1], land["rest1"], k - 1)
            finish(first1[0], first_s.at[1], land["first1"], k - 1)
        if k < flat_depth:
            begin(rest1[0], k)
            begin(first1[0], k)

    def crossing(buffer, target, at, rows):
        source = buffer.at[1 - section, span(at, rows)]
        return remote(source, target, across)

    cross_rest = crossing(rest_s, land_rest, rest1[1], rest1[2][-1])
    cross_first = crossing(first_s, land_first, first1[1], first1[2][-1])

    def settle(copy, buffer, landed, at, rows, base):
        copy.wait()
        value = (buffer[section, span(at, rows), :].astype(f32) + landed[...].astype(f32)).astype(
            bf16
        )
        out_ref[span(base + at, rows), :] = value
        value = value.astype(f32)
        return jnp.sum(value * value, axis=0, keepdims=True)

    def gathering(base, at, held):
        steps = []
        for k in reversed(range(flat_depth)):
            rows, left = held[k], held[k + 1]
            if left < rows:
                place = out_ref.at[span(base + at, left)]
                steps.append(remote(place, place, order[k]))
                at = at - side_of(order[k]) * left
            else:
                steps.append(None)
        return steps

    gather_rest = gathering(0, rest1[1], rest1[2])

    def step0(k):
        if k > 0 and k <= flat_depth:
            finish(rest0[0], rest_s.at[0], land["rest0"], k - 1)
        if k < flat_depth:
            begin(rest0[0], k)
        if k == flat_depth:
            cross_rest.start()
        if k == flat_depth + 1:
            squares = settle(cross_rest, rest_s, land_rest, rest1[1], rest1[2][-1], 0)
            squares_s[0:1, :] = squares / (dp * rest1[2][-1] // REST)
        if k > flat_depth + 1 and gather_rest[k - flat_depth - 2] is not None:
            gather_rest[k - flat_depth - 2].wait()
        if flat_depth < k < 2 * flat_depth + 1 and gather_rest[k - flat_depth - 1] is not None:
            gather_rest[k - flat_depth - 1].start()

    g0_s[...] = jnp.zeros_like(g0_s)
    gbias_s[...] = jnp.zeros_like(gbias_s)
    for g in range(3):
        ggain_s[g] = jnp.zeros((D, LANES), f32)

    def fold(x):
        return sum(x[:, i * LANES : (i + 1) * LANES] for i in range(COLUMNS))

    def rest_steps(t, half):
        c = 2 * t + half
        r = r_s[half]
        x2 = get_wide(x2_s, c)
        inverse = inverse_rms(x2)
        back_memory = mem_s[half][t]
        add_blocks(12, mul_t(norm_low(x2, inverse, gain(2, WIDE)), back_memory))
        back_normed = mul(wn_s[0, :, 4 * WIDTH : 6 * WIDTH], back_memory)
        yield
        back, gain_grad = norm_back(x2, inverse, gain(2, WIDE), back_normed)
        ggain_s[2] += fold(gain_grad)
        low = back.astype(bf16)
        yield
        add_blocks(26, mul_t(low, r[t]))
        for j in range(4):
            part = slice(j * FF // 4, (j + 1) * FF // 4)
            back_active = mul(wt_s[0, MIXW + FF + part.start : MIXW + FF + part.stop, :], low)
            live = r[t, part, :].astype(f32) > 0
            r[t, part, :] = jnp.where(live, back_active, 0.0).astype(bf16)
        yield
        x1 = x1_s[half][t]
        inverse = inverse_rms(x1)
        add_blocks(18, mul_t(norm_low(x1, inverse, gain(1, WIDE)), r[t]))
        back_normed = mul(wn_s[0, :, MIXW : MIXW + FF], r[t])
        yield
        more, gain_grad = norm_back(x1, inverse, gain(1, WIDE), back_normed)
        ggain_s[1] += fold(gain_grad)
        put_wide(x2_s, c, back + more)
        yield

    places1 = {0: 0, 1: 1, 4: 2}
    places0 = {0: 0, 1: 1, 3: 2, 4: 3, 5: 4, 6: 5, 7: 6, 8: 7}
    steps0 = 2 * flat_depth + 2

    def placed(places, step, place, each):
        return [
            functools.partial(step, places[place + each * t])
            if place + each * t in places
            else None
            for t in range(pairs)
        ]

    def back_rest(t, carry):
        at_time(t, placed(places1, step1, 0, 3))

        def point(number):
            if number in (1, 3):
                at_time(t, placed(places1, step1, (number + 1) // 2, 3))

        lockstep([rest_steps(t, 0), rest_steps(t, 1)], point)
        return carry

    lax.fori_loop(0, pairs, back_rest, 0)
    def cast_rest(block, carry):
        place = pl.ds(pl.multiple_of(block * D, D), D)
        rest_s[0, place, :] = g0_s[FIRST // D + block].astype(bf16)
        return carry

    lax.fori_loop(0, REST // D, cast_rest, 0, unroll=2)
    def first_steps(t, half):
        c = 2 * t + half
        qkv, o, dqkv = qkv_s[half], o_s[half], dqkv_s[half]
        back = get_wide(x2_s, c)
        lane = iota((D, LANES), 1)
        low = [jnp.where(lane < PACK, part, 0.0).astype(bf16) for part in unpack(back)]
        low = jnp.concatenate(low, 1)
        yield
        add_blocks(9, mul_t(low, o[t]))
        o[t] = mul(wt_s[0, 3 * WIDTH : 4 * WIDTH, :], low).astype(bf16)
        yield
        for first in range(0, GROUP, BATCH):
            queries, keys, values, backs = [], [], [], []
            for i in range(first, first + BATCH):
                lanes = slice(i * LANES, (i + 1) * LANES)
                queries += [qkv[t, part_of(j), lanes] for j in range(PAIRS)]
                keys += [qkv[t, part_of(PAIRS + j), lanes] for j in range(PAIRS)]
                values += [qkv[t, part_of(2 * PAIRS + j), lanes].T[:KEYS] for j in range(PAIRS)]
                backs += [o[t, part_of(j), lanes] for j in range(PAIRS)]
            chance = [p_s[half][t, first + i] for i in range(BATCH)]
            *results, scores = attend_back(
                keys, queries, values, backs, jnp.concatenate(chance, 1)
            )
            for i in range(BATCH):
                lanes = slice((first + i) * LANES, (first + i + 1) * LANES)
                own = slice(i * PAIRS, (i + 1) * PAIRS)
                dqkv[:, lanes] = jnp.concatenate([x for part in results for x in part[own]], 0)
            width = HEADS * LANES
            gbias_s[...] += sum(scores[:, i * width : (i + 1) * width] for i in range(BATCH))
            yield
        x0 = x0_s[c]
        inverse = inverse_rms(x0)
        add_blocks(0, mul_t(spread_low(x0 * inverse * gain(0, WIDE)), dqkv[...]))
        back_normed = packed(mul(wn_s[0, :, : 3 * WIDTH], dqkv[...]))
        yield
        more, gain_grad = norm_back(x0, inverse, gain(0, WIDE), back_normed)
        ggain_s[0] += fold(gain_grad)
        find(c)
        spread = mul_t(hot_s[...], split_low(back + more))
        ge_s[...] += spread[:, :D] + spread[:, D:]
        yield

    def both_steps(k):
        if k == 0:
            step1(3)
        if k == 1:
            for j in range(4, flat_depth + 1):
                step1(j)
        step0(k)

    def back_first(t, carry):
        at_time(t, placed(places0, both_steps, 0, 5))

        def point(number):
            place = {1: 1, attention // 2 + 1: 2, attention + 1: 3, attention + 2: 4}.get(number)
            if place is not None:
                at_time(t, placed(places0, both_steps, place, 5))

        lockstep([first_steps(t, 0), first_steps(t, 1)], point)
        return carry

    lax.fori_loop(0, pairs, back_first, 0)

    def cast_first(block, carry):
        place = pl.ds(pl.multiple_of(block * D, D), D)
        factor = jnp.where(block < 3, scale, 1.0)
        first_s[0, place, :] = (g0_s[block] * factor).astype(bf16)
        return carry

    lax.fori_loop(0, FIRST // D, cast_first, 0, unroll=2)
    codes_s[...] = ge_s[:CODES, :].astype(bf16)
    begin(first0[0], 0)
    begin(codes[0], 0)
    code_size = held_codes[-1]
    own_slot_s[code_size : code_size + n, :] = ge_s[CODES:, :].astype(bf16)
    late = list(range(8, steps0))
    if late:
        step0(late.pop(0))

    def sum_small():
        ones = jnp.ones((8, LANES), f32)
        small_s[0, 8:16, :] = jnp.zeros((8, LANES), f32)
        for g in range(7):
            small_s[0, g : g + 1, :] = mul_exact_t(ones, ggain_s[g])[:1]
        small_s[0, 7:8, :] = jnp.broadcast_to(loss, (1, LANES))

        def bucket_sums(b, carry):
            for head in range(HEADS):
                lanes = slice(head * LANES, (head + 1) * LANES)
                hit = jnp.where(buckets == b, gbias_s[:, lanes], 0.0)
                rows_s[head, pl.ds(b, 1), :] = jnp.sum(hit, axis=0, keepdims=True)
            return carry

        lax.fori_loop(0, BUCKETS, bucket_sums, 0, unroll=2)
        for head in range(HEADS):
            sums = mul_exact_t(ones, rows_s[head])
            small_s[0, 8 + head : 9 + head, : 2 * BUCKETS] = sums[:1]

    for k in range(len(far)):
        finish(first0[0], first_s.at[0], land["first0"], k)
        finish(codes[0], codes_s, land["codes"], k)
        if k + 1 < len(far):
            begin(first0[0], k + 1)
            begin(codes[0], k + 1)
        if k == 0:
            sum_small()

    first_at, first_left = first0[1], held_first[len(far) + 1 :]
    codes_at, codes_left = codes[1], held_codes[len(far) + 1 :]
    size = first_left[-1]
    mine_first = first_at + shift_of(0, first_left)
    mine_codes = codes_at + shift_of(0, codes_left, code_near)
    inside, crossing_first, everyone = [], [], []
    for mask in masks:
        source = first_s.at[0, span(first_at + shift_of(mask, first_left), size)]
        copy = remote_to(source, near_first.at[mask], device_of(mask))
        (crossing_first if mask >> (NEAR - 1) else inside).append(copy)
    for mask in masks:
        source = codes_s.at[span(codes_at + shift_of(mask, codes_left, code_near), code_size)]
        everyone.append(remote_to(source, near_codes.at[mask], device_of(mask, code_near)))

    @pl.when(section == 0)
    def _():
        for copy in inside:
            copy.start()
        cross_first.start()

    @pl.when(section == 1)
    def _():
        for copy in crossing_first:
            copy.start()

    for copy in everyone:
        copy.start()
    for step in late:
        step0(step)
    for k, stage in enumerate(code_far):
        copy = remote(small_s.at[k], small_land.at[k], stage)
        copy.start()
        copy.wait()
        small_s[k + 1] = small_s[k] + small_land[k]
    rows = code_size + n
    own_slot_s[rows + 16 :, :] = high_low(small_s[len(far)], 2)

    def keep_first(value):
        value = value.astype(bf16)
        out_ref[span(REST + mine_first, size), :] = value
        value = value.astype(f32)
        squares = jnp.sum(value * value, axis=0, keepdims=True)
        squares_s[1:2, :] = squares / (dp * size // FIRST)

    @pl.when(section == 0)
    def _():
        for copy in inside:
            copy.wait()
        for copy in crossing_first:
            copy.wait_recv()
        cross_first.wait_send()
        value = first_s[0, span(mine_first, size), :].astype(f32)
        for mask in masks:
            value = value + near_first[mask].astype(f32)
        keep_first(value)

    @pl.when(section == 1)
    def _():
        for copy in crossing_first:
            copy.wait_send()
        cross_first.wait_recv()
        value = first_s[1, span(mine_first, size), :].astype(f32)
        keep_first(value + land_first[...].astype(f32))

    place = out_ref.at[span(REST + mine_first, size)]
    copies = [
        remote_to(place, place, device_of(mask)) for mask in masks if not mask >> (NEAR - 1)
    ]
    for copy in copies:
        copy.start()
    for copy in everyone:
        copy.wait()
    value = codes_s[span(mine_codes, code_size), :].astype(f32)
    for mask in masks:
        value = value + near_codes[mask].astype(f32)
    value = value.astype(bf16)
    own_slot_s[:code_size, :] = value
    value = value.astype(f32)
    squares = jnp.sum(value * value, axis=0, keepdims=True)
    squares_s[2:3, :] = squares / (2 * dp * code_size // CODES)
    squares_s[3:, :] = jnp.zeros((5, LANES), f32)
    own_slot_s[rows : rows + 16, :] = high_low(squares_s[...], 2)
    kept_slot = out_slot_ref.at[slot]
    store_slot = pltpu.make_async_copy(own_slot_s, kept_slot, local_sems.at[BLOCKS + 2])
    store_slot.start()
    slots_out = [remote_to(own_slot_s, kept_slot, device_of(mask, code_near)) for mask in masks]
    for copy in slots_out:
        copy.start()
    store_slot.wait()
    for copy in copies + slots_out:
        copy.wait()
    for j, k in enumerate(reversed(range(len(far)))):
        copies = []
        if held_first[k + 1] < held_first[k]:
            place = out_ref.at[span(REST + first_at, held_first[k + 1])]
            copies.append(remote(place, place, far[k]))
            first_at = first_at - side_of(far[k]) * held_first[k + 1]
        slots = 2 ** (NEAR + j)
        held = out_slot_ref.at[pl.ds(lax.div(slot, slots) * slots, slots), pl.ds(0, rows + 16)]
        copies.append(remote(held, held, code_far[k]))
        for copy in copies:
            copy.start()
        for copy in copies:
            copy.wait()


def gradients(codes, users, targets, domains, bias, gains, mixer, feed, embedding, dp):
    n = users.shape[0] // 2
    chunks = n // GROUP
    order = stages(dp)
    depth = len(order)
    devices = 2 * dp
    vmem = pl.BlockSpec(memory_space=pltpu.VMEM)
    smem = pl.BlockSpec(memory_space=pltpu.SMEM)
    hbm = pl.BlockSpec(memory_space=pl.ANY)
    stat = (16, LANES)
    held_rest, held_first, held_codes = shares(dp, REST), shares(dp, FIRST), shares(dp, CODES, 1)
    plane, far = depth - 1, depth - NEAR
    slot_rows = held_codes[-1] + n + 16 + 32
    sizes = [*held_rest[1:] * 2, *held_first[1:]]
    sizes += [*held_first[1 : far + 1], *held_codes[1 : far + 1], held_rest[-1], held_first[-1]]
    lands = [pltpu.VMEM((rows, D), bf16) for rows in sizes]
    copies = 128 + 16 * depth
    return pl.pallas_call(
        functools.partial(step_kernel, n, dp),
        out_shape=(
            jax.ShapeDtypeStruct((COLS, D), bf16),
            jax.ShapeDtypeStruct((devices, 8, LANES), jnp.int32),
            jax.ShapeDtypeStruct((devices, slot_rows, LANES), bf16),
            jax.ShapeDtypeStruct((8, LANES), f32),
        ),
        in_specs=[vmem, smem, vmem, vmem, vmem, smem, vmem, hbm, hbm, hbm],
        out_specs=(vmem, hbm, hbm, vmem),
        scratch_shapes=[pltpu.VMEM((chunks, D, WIDE), f32)]
        + [
            pltpu.VMEM(shape, dtype)
            for shape, dtype in (
                ((chunks // 2, D, WIDE), f32),
                ((chunks // 2, 3 * WIDTH, SPAN), bf16),
                ((chunks // 2, GROUP, KEYS, HEADS * LANES), bf16),
                ((chunks // 2, WIDTH, SPAN), bf16),
                ((chunks // 2, FF, WIDE), bf16),
                ((chunks // 2, 2 * WIDTH, WIDE), bf16),
                ((3 * WIDTH, SPAN), bf16),
                ((chunks // 2, 32 * GROUP, LANES), f32),
                ((chunks // 2, WIDTH, 32 * GROUP), bf16),
            )
            for _ in range(2)
        ]
        + [
            pltpu.VMEM((chunks * COLUMNS * D, LANES), f32),
            pltpu.VMEM((3 * WIDTH, 2 * LANES), bf16),
            pltpu.VMEM((2, D, COLS), bf16),
            pltpu.VMEM((2, COLS, D), bf16),
            pltpu.VMEM((2 * D, CODES + n), bf16),
            pltpu.VMEM((7, D, LANES), f32),
            pltpu.VMEM((KEYS, HEADS * LANES), f32),
            pltpu.VMEM((LANES, HEADS * LANES), f32),
            pltpu.VMEM((BLOCKS, D, LANES), f32),
            pltpu.VMEM((CODES + n, D), f32),
            pltpu.VMEM((KEYS, HEADS * LANES), f32),
            pltpu.VMEM((7, D, LANES), f32),
            pltpu.VMEM((HEADS, 2 * BUCKETS, LANES), f32),
            pltpu.VMEM((n, D), f32),
            pltpu.VMEM((n, LANES), jnp.int32),
            pltpu.VMEM((WIDTH, LANES), bf16),
            pltpu.VMEM((WIDTH, LANES), bf16),
            pltpu.VMEM((2, REST, D), bf16),
            pltpu.VMEM((2, FIRST, D), bf16),
            pltpu.VMEM((CODES, D), bf16),
            pltpu.VMEM((8, LANES), jnp.int32),
            pltpu.VMEM((slot_rows, LANES), bf16),
            pltpu.VMEM((8, LANES), f32),
            pltpu.VMEM((8, WIDE), jnp.int32),
            pltpu.VMEM((CODES + n, WIDE), bf16),
            pltpu.VMEM((depth + 1,) + stat, f32),
            pltpu.VMEM((depth,) + stat, f32),
            pltpu.VMEM((far + 1, 16, LANES), f32),
            pltpu.VMEM((far, 16, LANES), f32),
            pltpu.VMEM((2**NEAR, held_first[-1], D), bf16),
            pltpu.VMEM((2**NEAR, held_codes[-1], D), bf16),
            pltpu.SemaphoreType.DMA((BLOCKS + 3,)),
            pltpu.SemaphoreType.DMA((copies,)),
            pltpu.SemaphoreType.DMA((copies,)),
        ]
        + lands,
        compiler_params=pltpu.CompilerParams(
            collective_id=0, has_side_effects=True, vmem_limit_bytes=127 * 2**19
        ),
        name="gradients",
    )(codes, users, users.reshape(1, -1), targets, domains, bias, gains, mixer, feed, embedding)


def adam(weight, moment, square, slope, rate, decay):
    moment = beta_one * moment + (1 - beta_one) * slope
    square = beta_two * square + (1 - beta_two) * slope * slope
    unbiased_moment = moment * (1 / (1 - beta_one**STEP))
    unbiased_square = square * (1 / (1 - beta_two**STEP))
    root = unbiased_square * lax.rsqrt(unbiased_square)
    divisor = root + adam_eps
    inverse = pl.reciprocal(divisor, approx=True)
    inverse = inverse * (2.0 - divisor * inverse)
    step = unbiased_moment * inverse + decay * weight
    return weight - rate * step, moment, square


def update_kernel(n, dp, *refs):
    parts_in, big_in, small_in, refs = refs[:4], refs[4:13], refs[13:19], refs[19:]
    loss_ref, norm_ref, section_ref, hist_ref = refs[:4]
    big_out, small_out, low_out, refs = refs[4:13], refs[13:19], refs[19:22], refs[22:]
    parts, hold, low_hold = refs[:4], refs[4:13], refs[13:16]
    user_grad, code_grad, part_sems, in_sems, out_sems = refs[16:]
    grad_ref, ids_ref, slot_ref, stat_ref = parts
    arrivals = [pltpu.make_async_copy(parts_in[i], parts[i], part_sems.at[i]) for i in range(4)]
    loads = [pltpu.make_async_copy(big_in[i], hold[i], in_sems.at[i]) for i in range(9)]
    for load in arrivals[1:] + arrivals[:1] + loads:
        load.start()
    for arrival in arrivals:
        arrival.wait()
    devices = slot_ref.shape[0]
    held = shares(dp, CODES, 1)
    code_size = held[-1]

    users = user_grad.shape[0]
    fit = LANES // n
    each = min(1024 // n, devices)
    span_rows = each * n
    user_grad[...] = jnp.zeros_like(user_grad)

    def scatter(part, carry):
        first = part * each
        rows = [slot_ref[first + i, code_size : code_size + n, :] for i in range(each)]
        rows = jnp.concatenate(rows, 0)
        lanes = []
        for group in range(each // fit):
            lanes.append(
                sum(ids_ref[first + group * fit + other, :1, :] for other in range(fit))
            )
        ids = jnp.concatenate(lanes, 1)

        def block_rows(block, carry):
            place = pl.ds(pl.multiple_of(block * USER_ROWS, 8), USER_ROWS)
            hit = iota((USER_ROWS, span_rows), 0) + block * USER_ROWS == ids
            user_grad[place, :] += mul(jnp.where(hit, 1.0, 0.0).astype(bf16), rows)
            return carry

        lax.fori_loop(0, users // USER_ROWS, block_rows, 0)
        return carry

    lax.fori_loop(0, devices // each, scatter, 0)

    def total(x):
        return jnp.sum(jnp.sum(x, axis=0, keepdims=True), axis=1, keepdims=True)

    route = code_stages(dp)
    depth = len(route)
    near = 2**NEAR
    top = code_size + n

    def squares_of(slot):
        value = slot_ref[slot, top : top + 16, :].astype(f32)
        return value[:8] + value[8:]

    def add(i, sums):
        first = 2 * near * i
        return tuple(
            total + sum(squares_of(first + side * near + j) for j in range(near))
            for side, total in enumerate(sums)
        )

    zero = jnp.zeros((8, LANES), f32)
    even, odd = lax.fori_loop(0, devices // (2 * near), add, (zero, zero))
    section_squares = [total(x[0:1] + x[1:2]) for x in (even, odd)]
    rest = total(even[2:3] + odd[2:3])
    first = 0
    for k, stage in enumerate(route[:-NEAR]):
        first = first + side_of(stage) * 2 ** (depth - 1 - k)
    small = jnp.zeros((16, LANES), f32)
    for i in range(near):
        value = slot_ref[first + i, top + 16 :, :].astype(f32)
        small = small + (value[:16] + value[16:])
    for slot in range(devices):
        at, kept = 0, True
        for k in range(depth):
            if slot >> (depth - 1 - k) & 1:
                kept = kept and held[k + 1] < held[k]
                at += held[k + 1]
        if kept:
            code_grad[at : at + code_size, :] = slot_ref[slot, :code_size, :]
    user_values = user_grad[...]
    rest = rest + total(user_values * user_values)
    lane, line = iota(small.shape, 1), iota(small.shape, 0)
    counted = (line < 7) | ((line > 7) & (lane < 2 * BUCKETS))
    small_kept = jnp.where(counted, small, 0.0)
    rest = rest + total(small_kept * small_kept)
    norm = jnp.sqrt(section_squares[0] + section_squares[1] + rest)
    factor = jnp.minimum(1.0, clip_norm / (norm + 1e-06))
    loss_ref[0] = small[7, 0]
    norm_ref[0] = norm[0, 0]
    for s in range(2):
        section_ref[s] = jnp.sqrt(section_squares[s])[0, 0]
    for row in range(8):
        lanes = slice((row % 2) * LANES, (row % 2 + 1) * LANES)
        hist_ref[row // 2 : row // 2 + 1, lanes] = stat_ref[row : row + 1, :]

    outs = adam(
        small_in[0][...], small_in[1][...], small_in[2][...], factor * small[:7], rate_gain, 0.0
    )
    for ref, value in zip(small_out[:3], outs):
        ref[...] = value
    for head in range(HEADS):
        for s in range(2):
            slope = factor * small[8 + head : 9 + head, s * BUCKETS : (s + 1) * BUCKETS]
            one = slice(s, s + 1)
            outs = adam(
                small_in[3][head, one, :],
                small_in[4][head, one, :],
                small_in[5][head, one, :],
                slope,
                rate_small,
                0.0,
            )
            for ref, value in zip(small_out[3:], outs):
                ref[head, one, :] = value

    stores = []

    def store(kind, place):
        first = 3 * kind
        pieces = [(hold[first + i], big_out[first + i]) for i in range(3)]
        pieces.append((low_hold[kind], low_out[kind]))
        for source, target in pieces:
            copy = pltpu.make_async_copy(
                source.at[place], target.at[place], out_sems.at[len(stores)]
            )
            copy.start()
            stores.append(copy)

    def step(kind, place, slope):
        first = 3 * kind
        outs = adam(
            hold[first][place],
            hold[first + 1][place],
            hold[first + 2][place],
            factor * slope.astype(f32),
            rate_matrix,
            decay_matrix,
        )
        for i in range(3):
            hold[first + i][place] = outs[i]
        low_hold[kind][place] = outs[0].astype(bf16)

    def rows_from(start, count):
        return pl.ds(pl.multiple_of(start, 16), count)

    def columns(kind, first, count, row):
        def one(i, carry):
            lanes = pl.ds(pl.multiple_of((first + i) * LANES, LANES), LANES)
            step(kind, (0, slice(None), lanes), grad_ref[rows_from(row + i * D, D), :])
            return carry

        lax.fori_loop(0, count, one, 0)
        store(kind, (0, slice(None), slice(first * LANES, (first + count) * LANES)))

    def lines(first, count, size, source, row):
        def one(i, carry):
            place = (rows_from(first + i * size, size), slice(None))
            step(2, place, source[rows_from(row + i * size, size), :])
            return carry

        lax.fori_loop(0, count, one, 0)
        store(2, (slice(first, first + count * size), slice(None)))

    skip = FIRST // LANES
    for i in range(3):
        loads[i].wait()
    columns(0, 0, skip // 2, REST)
    columns(0, skip // 2, skip // 2, REST + skip // 2 * D)
    columns(0, skip, MIXW // LANES - skip, 0)
    for i in range(3, 6):
        loads[i].wait()
    for part in range(2):
        first = part * FF // LANES
        columns(1, first, FF // LANES, (MIXW // LANES - skip + first) * D)
    for i in range(6, 9):
        loads[i].wait()
    for part in range(2):
        lines(part * CODES // 2, 4, LANES, code_grad, part * CODES // 2)
    parts = users // USER_ROWS
    lines(CODES, parts // 2, USER_ROWS, user_grad, 0)
    done = parts // 2 * USER_ROWS
    lines(CODES + done, parts - parts // 2, USER_ROWS, user_grad, done)
    for copy in stores:
        copy.wait()


def update(n, dp, reduced, mixers, feeds, embeds, gains, biases):
    vmem = pl.BlockSpec(memory_space=pltpu.VMEM)
    smem = pl.BlockSpec(memory_space=pltpu.SMEM)
    hbm = pl.BlockSpec(memory_space=pl.ANY)
    big = [*mixers, *feeds, *embeds]
    small = [*gains, *biases]
    low = [jax.ShapeDtypeStruct(x[0].shape, bf16) for x in (mixers, feeds, embeds)]
    users = embeds[0].shape[0] - CODES
    pieces = 4 * (6 + 4 + 4 + users // USER_ROWS)
    return pl.pallas_call(
        functools.partial(update_kernel, n, dp),
        out_shape=[
            jax.ShapeDtypeStruct((1,), f32),
            jax.ShapeDtypeStruct((1,), f32),
            jax.ShapeDtypeStruct((2,), f32),
            jax.ShapeDtypeStruct((LEVELS, CODEBOOK), f32),
        ]
        + [jax.ShapeDtypeStruct(x.shape, f32) for x in big + small]
        + low,
        in_specs=[hbm] * 13 + [vmem] * 6,
        out_specs=[smem] * 3 + [vmem] + [hbm] * 9 + [vmem] * 6 + [hbm] * 3,
        scratch_shapes=[pltpu.VMEM(x.shape, x.dtype) for x in reduced]
        + [pltpu.VMEM(x.shape, f32) for x in big]
        + [pltpu.VMEM(x.shape, bf16) for x in low]
        + [
            pltpu.VMEM((users, D), f32),
            pltpu.VMEM((CODES, D), bf16),
            pltpu.SemaphoreType.DMA((4,)),
            pltpu.SemaphoreType.DMA((9,)),
            pltpu.SemaphoreType.DMA((pieces,)),
        ],
        compiler_params=pltpu.CompilerParams(vmem_limit_bytes=62 * 2**20),
        name="update",
    )(*reduced, *big, *small)


def shards(
    history_codes,
    user_ids,
    targets,
    domains,
    mixer,
    mixer_moment,
    mixer_square,
    feed,
    feed_moment,
    feed_square,
    embedding,
    embedding_moment,
    embedding_square,
    gains,
    gains_moment,
    gains_square,
    position_bias,
    bias_moment,
    bias_square,
):
    def turned(table):
        return jnp.transpose(table, (2, 0, 1))

    biases = [turned(x) for x in (position_bias, bias_moment, bias_square)]
    reduced = gradients(
        history_codes,
        user_ids,
        targets.T,
        domains.reshape(1, -1),
        biases[0],
        gains,
        mixer,
        feed,
        embedding,
        lax.axis_size("dp"),
    )
    outs = update(
        history_codes.shape[0] // 2,
        lax.axis_size("dp"),
        reduced,
        (mixer, mixer_moment, mixer_square),
        (feed, feed_moment, feed_square),
        (embedding, embedding_moment, embedding_square),
        (gains, gains_moment, gains_square),
        biases,
    )
    loss, norm, sections, histograms = outs[:4]
    back = [jnp.transpose(x, (1, 2, 0)) for x in outs[16:19]]
    return (
        loss.reshape(()),
        norm.reshape(()),
        sections,
        histograms,
        *outs[4:16],
        *back,
        *outs[19:],
    )


def solution(mesh):
    by_dp, by_pipe, copied = P("dp"), P("pipe"), P()
    return jax.shard_map(
        shards,
        mesh=mesh,
        in_specs=(by_dp,) * 4 + (by_pipe,) * 6 + (copied,) * 9,
        out_specs=(copied,) * 4 + (by_pipe,) * 6 + (copied,) * 9 + (by_pipe,) * 2 + (copied,),
        check_vma=False,
    )
```

```python
import functools

import jax
import jax.numpy as jnp
from jax import lax
from jax.experimental import pallas as pl
from jax.experimental.pallas import tpu as pltpu
from jax.sharding import PartitionSpec as P

D = 128
HEADS = 6
HEAD_DIM = 64
FF = 1024
CODEBOOK = 256
LEVELS = 4
BUCKETS = 32
DOMAINS = 3
HIST_LEN = 81
STEP = 5
CODES = 1024
LANES = 128
WIDTH = HEADS * HEAD_DIM
MIXW = 6 * WIDTH
COLS = MIXW + 2 * FF
BLOCKS = COLS // LANES
KEYS = 96
GROUP = 8
BATCH = 2
NEAR = 3
PACK = 96
WIDE = GROUP * PACK
SPAN = GROUP * LANES
COLUMNS = WIDE // LANES
PAIRS = HEADS // 2
FIRST = 4 * WIDTH
REST = COLS - FIRST
USER_ROWS = 400
MESH = pl.DeviceIdType.MESH

norm_eps = 1e-06
beta_one = 0.9
beta_two = 0.999
adam_eps = 1e-08
clip_norm = 0.5
rate_matrix = 0.04
rate_gain = 0.8
rate_small = 0.3
decay_matrix = 0.01

f32 = jnp.float32
bf16 = jnp.bfloat16


def iota(shape, axis):
    return lax.broadcasted_iota(jnp.int32, shape, axis)


def mul(left, right):
    return jnp.dot(left, right, preferred_element_type=f32)


def mul_t(left, right):
    return lax.dot_general(left, right, (((1,), (1,)), ((), ())), preferred_element_type=f32)


def mul_exact(left, right):
    return jnp.dot(left, right, preferred_element_type=f32, precision=lax.Precision.HIGHEST)


def mul_exact_t(left, right):
    return lax.dot_general(
        left,
        right,
        (((1,), (1,)), ((), ())),
        preferred_element_type=f32,
        precision=lax.Precision.HIGHEST,
    )


def onehot(ids, rows):
    return jnp.where(iota((rows, ids.shape[1]), 0) == ids, 1.0, 0.0).astype(bf16)


def inverse_rms(x):
    return lax.rsqrt(jnp.mean(x * x, axis=0, keepdims=True) + norm_eps)


def norm_low(x, inverse, gain):
    return (x * inverse * gain).astype(bf16)


def norm_back(x, inverse, gain, upstream):
    scaled = x * inverse
    inner = upstream * gain
    back = inverse * (inner - scaled * jnp.mean(inner * scaled, axis=0, keepdims=True))
    return back, upstream * scaled


def block_diag(pair):
    zero = jnp.zeros((HEAD_DIM, LANES), pair.dtype)
    left = jnp.concatenate([pair[:HEAD_DIM], zero], 0)
    right = jnp.concatenate([zero, pair[HEAD_DIM:]], 0)
    return jnp.concatenate([left, right], 1)


def diagonal(both):
    return jnp.concatenate([both[:HEAD_DIM, :LANES], both[HEAD_DIM:, LANES:]], 0)


def turn(x, shift):
    return x if shift % LANES == 0 else pltpu.roll(x, shift % LANES, 1)


def pack(tables):
    lane = iota(tables[0].shape, 1)
    columns = []
    for first in range(0, len(tables), 4):
        turned = [turn(tables[first + i], PACK * i) for i in range(4)]
        for i in range(3):
            columns.append(jnp.where(lane < PACK - 32 * i, turned[i], turned[i + 1]))
    return jnp.concatenate(columns, 1)


def unpack(x):
    lane = iota((x.shape[0], LANES), 1)
    tables = []
    for first in range(0, x.shape[1] // LANES, 3):
        a, b, c = [x[:, (first + i) * LANES : (first + i + 1) * LANES] for i in range(3)]
        tables.append(a)
        tables.append(jnp.where(lane < 32, turn(a, 32), turn(b, 32)))
        tables.append(jnp.where(lane < 64, turn(b, 64), turn(c, 64)))
        tables.append(turn(c, 96))
    return tables


def stack(both):
    return jnp.concatenate([both[:, :LANES], both[:, LANES:]], 0)


def pad_keys(table):
    if table.shape[0] == LANES:
        return table
    zero = jnp.zeros((LANES - table.shape[0], table.shape[1]), table.dtype)
    return jnp.concatenate([table, zero], 0)


def columns_of(table, i):
    return table[:, 2 * i * LANES : 2 * (i + 1) * LANES]


def attend(keys, queries, values, bias):
    scores = [mul(key, block_diag(query)) for key, query in zip(keys, queries)]
    scores = jnp.concatenate(scores, 1) + bias
    top = jnp.max(scores, axis=0, keepdims=True)
    chance = jnp.exp(scores - top)
    total = jnp.sum(chance, axis=0, keepdims=True)
    chance = (chance * (1.0 / total)).astype(bf16)
    full = pad_keys(chance)
    mixed = [mul(value, columns_of(full, i)) for i, value in enumerate(values)]
    return chance, [diagonal(both).astype(bf16) for both in mixed]


def attend_back(keys_t, queries, values, back_mixed, chance):
    exact = chance.astype(f32)
    back_chance = [mul(value, block_diag(back)) for value, back in zip(values, back_mixed)]
    back_chance = jnp.concatenate(back_chance, 1)
    inner = jnp.sum(back_chance * exact, axis=0, keepdims=True)
    back_scores = exact * (back_chance - inner)
    low = pad_keys(back_scores.astype(bf16))
    full = pad_keys(chance)
    count = range(len(queries))
    back_query = [mul(keys_t[i], columns_of(low, i)) for i in count]
    back_keys = [mul_t(queries[i], stack(columns_of(low, i))) for i in count]
    back_values = [mul_t(back_mixed[i], stack(columns_of(full, i))) for i in count]
    results = [
        [diagonal(both).astype(bf16) for both in part]
        for part in (back_query, back_keys, back_values)
    ]
    return *results, back_scores


def stages(dp):
    bits = [2**k for k in range(dp.bit_length() - 1)]
    return [("dp", bit) for bit in bits[:2] + bits[4:] + bits[2:4]] + [("pipe", 1)]


def code_stages(dp):
    order = stages(dp)
    return order[:1] + order[2:-NEAR] + order[-1:] + order[1:2] + order[-NEAR:-1]


def high_low(x, parts):
    rows = []
    for _ in range(parts):
        rows.append(x.astype(bf16))
        x = x - rows[-1].astype(f32)
    return jnp.concatenate(rows, 0)


def side_of(stage):
    axis, bit = stage
    return lax.rem(lax.div(lax.axis_index(axis), bit), 2)


def partner_of(stage):
    axis, bit = stage
    return {axis: lax.axis_index(axis) + bit * (1 - 2 * side_of(stage))}


def shares(dp, rows, across=0):
    held = [rows]
    depth = len(stages(dp)) - 1
    for k in range(depth + across):
        later = min(NEAR - 1, depth - 1 - k) + across if k < depth else 0
        half = held[-1] // 2
        held.append(half if half % (16 * 2**later) == 0 else held[-1])
    return held


def span(start, size):
    return pl.ds(pl.multiple_of(start, 16), size)


def step_kernel(n, dp, *refs):
    codes_ref, users_ref, user_row_ref, targets_ref, domains_ref, bias_ref, gains_ref = refs[:7]
    mixer_ref, feed_ref, embed_ref = refs[7:10]
    out_ref, out_ids_ref, out_slot_ref, out_stat_ref = refs[10:14]
    refs = refs[14:]
    x0_s, *doubles = refs[0], *[refs[1 + 2 * i : 3 + 2 * i] for i in range(9)]
    x1_s, qkv_s, p_s, o_s, r_s, mem_s, dqkv_s, pc_s, oc_s = doubles
    refs = refs[19:]
    x2_s, dz_s, wn_s, wt_s, ext_s = refs[:5]
    gain_s, ebias_s, dbias_s, g0_s, ge_s, gbias_s, ggain_s, rows_s, user_s, ids_s = refs[5:15]
    cross_s, cross_back_s, rest_s, first_s, codes_s, slot_s, own_slot_s, squares_s, id_rows_s, hot_s = refs[15:25]
    stat_s, stat_land, small_s, small_land, near_first, near_codes = refs[25:31]
    local_sems, sends, recvs = refs[31:34]
    lands = refs[34:]
    order = stages(dp)
    across = order[-1]
    depth = len(order)
    chunks = n // GROUP
    section = lax.axis_index("pipe")
    used = [0]

    def remote_to(source, target, device):
        index = used[0]
        used[0] += 1
        return pltpu.make_async_remote_copy(
            src_ref=source,
            dst_ref=target,
            send_sem=sends.at[index],
            recv_sem=recvs.at[index],
            device_id=device,
            device_id_type=MESH,
        )

    def remote(source, target, stage):
        return remote_to(source, target, partner_of(stage))

    near, far = order[-NEAR:], order[:-NEAR]
    route = code_stages(dp)
    code_near, code_far = route[-NEAR:], route[:-NEAR]
    masks = range(1, 2**NEAR)

    def device_of(mask, near=near):
        place = {"dp": lax.axis_index("dp"), "pipe": lax.axis_index("pipe")}
        for i, (axis, bit) in enumerate(near):
            if mask >> i & 1:
                place[axis] = place[axis] + bit * (1 - 2 * side_of((axis, bit)))
        return place

    def shift_of(mask, lefts, near=near):
        total = 0
        for i, left in enumerate(lefts):
            side = side_of(near[i])
            total = total + (1 - side if mask >> i & 1 else side) * left
        return total

    locals_in = []
    for block in range(BLOCKS):
        lanes = slice(block * LANES, (block + 1) * LANES)
        if block < MIXW // LANES:
            source = mixer_ref.at[0, :, lanes]
        else:
            source = feed_ref.at[0, :, slice(lanes.start - MIXW, lanes.stop - MIXW)]
        locals_in.append(pltpu.make_async_copy(source, g0_s.at[block], local_sems.at[block]))
    vocabulary = embed_ref.shape[0]
    flat = x2_s.at[pl.ds(0, vocabulary)]
    load_embed = pltpu.make_async_copy(embed_ref, flat, local_sems.at[BLOCKS])
    for copy in locals_in:
        copy.start()
    load_embed.start()

    barrier = pltpu.get_barrier_semaphore()
    greeted = [partner_of(stage) for stage in far if stage != code_near[0]]
    greeted += [device_of(mask) for mask in masks]
    greeted += [device_of(mask, code_near) for mask in masks if mask & 1]
    for device in greeted:
        pl.semaphore_signal(barrier, inc=1, device_id=device, device_id_type=MESH)

    ids_s[:, : HIST_LEN - 1] = codes_ref[pl.ds(pl.multiple_of(section * n, 8), n), :]
    lane, row = iota((n, LANES), 1), iota((n, LANES), 0)
    ids = ids_s[...] + ((lane & 3) << 8)
    ids = jnp.where(lane < HIST_LEN - 1, ids, jnp.where(lane == HIST_LEN - 1, CODES + row, -1))
    ids_s[...] = ids
    packed = []
    for i in range(GROUP):
        rows = [ids_s[c * GROUP + i : c * GROUP + i + 1, :] for c in range(chunks)]
        rows += [jnp.zeros((8 - chunks, LANES), jnp.int32)]
        packed.append(jnp.concatenate(rows, 0))
    id_rows_s[...] = pack(packed)
    count = targets_ref.shape[1]
    history, token = iota((count, LANES), 0), iota((count, LANES), 1)
    pick = jnp.where((token >> 2) + section * n == history, 1.0, 0.0)
    level, place = iota((LEVELS, LANES), 0), iota((LEVELS, LANES), 1) & 3
    target = mul(targets_ref[...].astype(f32), pick) + (level * CODEBOOK).astype(f32)
    goal = jnp.sum(jnp.where(level == place, target, 0.0), axis=0, keepdims=True).astype(jnp.int32)
    start_ids = jnp.sum(
        jnp.where(level == place - 1, target, 0.0), axis=0, keepdims=True
    ).astype(jnp.int32)
    domain = mul(domains_ref[...].astype(f32), pick)
    pick = jnp.where(lax.rem(token, n) + section * n == history, 1.0, 0.0)
    own_users = mul_exact(user_row_ref[...].astype(f32), pick)

    counts = [
        jnp.sum(jnp.where(domain == d, 1.0, 0.0), axis=1, keepdims=True) for d in range(DOMAINS)
    ]
    counts += [jnp.zeros((1, 1), f32)] * (8 - DOMAINS)
    stat_s[0, 8:, :] = jnp.broadcast_to(jnp.concatenate(counts, 0), (8, LANES))
    histogram = mul_t(jnp.ones((8, LANES), bf16), onehot(goal, CODES))
    for r in range(8):
        stat_s[0, r : r + 1, :] = histogram[:1, r * LANES : (r + 1) * LANES]
    slot = 0
    for k, stage in enumerate(route):
        slot = slot + side_of(stage) * 2 ** (depth - 1 - k)
    owner = iota((8, LANES), 1) // n
    own_users = jnp.broadcast_to(own_users, (8, LANES)).astype(jnp.int32)
    slot_s[...] = jnp.where(owner == lax.rem(slot, LANES // n), own_users, 0)
    store_ids = pltpu.make_async_copy(slot_s, out_ids_ref.at[slot], local_sems.at[BLOCKS + 1])
    store_ids.start()
    store_ids.wait()

    def slots_of(j):
        return pl.ds(lax.div(slot, 2**j) * 2**j, 2**j)

    for g in range(7):
        gain_s[g] = jnp.broadcast_to(gains_ref[g : g + 1, :], (LANES, LANES)).T

    def positions(axis):
        index = iota((KEYS, LANES), axis)
        return jnp.where(index == HIST_LEN - 1, 0, index + 1)

    key, query = positions(0), positions(1)
    distance = jnp.abs(query - key)
    remoteness = jnp.zeros_like(distance)
    for edge in (12, 16, 23, 32, 46, 64, 91):
        remoteness = remoteness + (distance >= edge).astype(jnp.int32)
    nearby = jnp.minimum(jnp.where(distance < 8, distance, 8 + remoteness), 15)
    buckets = nearby + jnp.where(key > query, 16, 0)
    real = iota((KEYS, LANES), 0) < HIST_LEN
    for head in range(HEADS):
        lanes = slice(head * LANES, (head + 1) * LANES)

        def choose(b, table):
            return jnp.where(buckets == b, bias_ref[head, 0, b], table)

        table = lax.fori_loop(0, BUCKETS, choose, jnp.zeros((KEYS, LANES), f32), unroll=8)
        ebias_s[:, lanes] = jnp.where(real, table, -1e30)
    key, query = iota((LANES, LANES), 0), iota((LANES, LANES), 1)
    offset = query - key
    seen = ((key >> 2) == (query >> 2)) & (offset >= 0)
    for head in range(HEADS):
        lanes = slice(head * LANES, (head + 1) * LANES)
        table = jnp.full((LANES, LANES), -1e30, f32)
        for b in range(LEVELS):
            table = jnp.where(seen & (offset == b), bias_ref[head, 1, b], table)
        dbias_s[:, lanes] = table

    scale = HEAD_DIM**-0.5
    cross_scale = jnp.where(section == 1, scale, 1.0).astype(f32)
    for copy in locals_in:
        copy.wait()
    def cast_weights(block, carry):
        factor = jnp.where((block >= 12) & (block < 15), cross_scale, 1.0)
        factor = jnp.where(block < 3, scale, factor)
        lanes = pl.ds(pl.multiple_of(block * LANES, LANES), LANES)
        wn_s[section, :, lanes] = (g0_s[block] * factor).astype(bf16)
        return carry

    lax.fori_loop(0, BLOCKS, cast_weights, 0, unroll=2)
    pl.semaphore_wait(barrier, len(greeted))
    half = D // 2
    mine = span(side_of(order[0]) * half, half)
    pieces = (slice(0, FIRST), slice(FIRST, COLS))
    over = [
        remote(wn_s.at[section, mine, piece], wn_s.at[section, mine, piece], across)
        for piece in pieces
    ]
    for copy in over:
        copy.start()

    early = []
    for j, stage in enumerate(reversed(route)):
        held = out_ids_ref.at[slots_of(j)]
        early.append(
            (
                remote(stat_s.at[j], stat_land.at[j], stage),
                remote(held, held, stage),
            )
        )

    def early_step(j):
        if j > 0:
            for copy in early[j - 1]:
                copy.wait()
            stat_s[j] = stat_s[j - 1] + stat_land[j - 1]
        if j < depth:
            for copy in early[j]:
                copy.start()

    eye = jnp.where(iota((LANES, LANES), 0) == iota((LANES, LANES), 1), 1.0, 0.0).astype(bf16)
    load_embed.wait()

    def fetch(i, carry):
        user_s[pl.ds(i, 1), :] = x2_s[pl.ds(CODES + users_ref[section * n + i], 1), :]
        return carry

    lax.fori_loop(0, n, fetch, 0, unroll=4)
    for block in range(CODES // LANES + 1):
        if block < CODES // LANES:
            rows = x2_s[block * LANES : (block + 1) * LANES, :]
            codes_s[block * LANES : (block + 1) * LANES, :] = rows.astype(bf16)
            width = LANES
        else:
            rows = user_s[...]
            width = n
        high = rows.astype(bf16)
        low = (rows - high.astype(f32)).astype(bf16)
        lanes = slice(block * LANES, block * LANES + width)
        ext_s[:D, lanes] = mul_t(eye, high).astype(bf16)
        ext_s[D:, lanes] = mul_t(eye, low).astype(bf16)

    def find(c):
        ids = id_rows_s[pl.ds(c, 1), :]
        for first in range(0, CODES + n, LANES):
            rows = min(LANES, CODES + n - first)
            hot_s[first : first + rows, :] = onehot(ids - first, rows)

    def lookup(c, carry):
        find(c)
        both = mul(ext_s[...], hot_s[...])
        x0_s[c] = both[:D] + both[D:]
        return carry

    lax.fori_loop(0, chunks, lookup, 0)

    beside = []
    for piece in pieces:
        came = wn_s.at[1 - section, mine, piece]
        beside.append(remote(came, came, order[0]))
    over[0].wait()
    beside[0].start()

    def transpose_weights(which, first, last):
        def one(block, carry):
            place = pl.ds(pl.multiple_of(block * LANES, LANES), LANES)
            wt_s[which, place, :] = wn_s[which, :, place].T
            return carry

        lax.fori_loop(first, last, one, 0, unroll=2)

    transpose_weights(section, 0, BLOCKS)
    beside[0].wait()
    transpose_weights(1 - section, 0, FIRST // LANES)

    def rest_passes():
        over[1].wait()
        beside[1].start()

    def rest_arrives():
        beside[1].wait()
        transpose_weights(1 - section, FIRST // LANES, BLOCKS)

    def gain(g, width):
        column = gain_s[g]
        return column if width == LANES else jnp.concatenate([column] * (width // LANES), 1)

    def lockstep(steps, point=None):
        for number, _ in enumerate(zip(*steps)):
            if point is not None:
                point(number)

    def at_time(t, steps):
        for time, step in enumerate(steps):
            if step is not None:
                pl.when(t == time)(step)

    def spread_low(x):
        return jnp.concatenate([part.astype(bf16) for part in unpack(x)], 1)

    def packed(x):
        return pack([x[:, i * LANES : (i + 1) * LANES] for i in range(GROUP)])

    def part_of(j):
        return slice(j * LANES, (j + 1) * LANES)

    def encode_steps(t, half):
        c = 2 * t + half
        qkv, o, r = qkv_s[half], o_s[half], r_s[half]
        x0 = x0_s[c]
        h = spread_low(x0 * inverse_rms(x0) * gain(0, WIDE))
        yield
        for j in range(3):
            part = slice(j * WIDTH, (j + 1) * WIDTH)
            qkv[t, part, :] = mul(wt_s[0, part, :], h).astype(bf16)
        yield
        for first in range(0, GROUP, BATCH):
            queries, keys, values = [], [], []
            for i in range(first, first + BATCH):
                lanes = slice(i * LANES, (i + 1) * LANES)
                queries += [qkv[t, part_of(j), lanes] for j in range(PAIRS)]
                keys += [qkv[t, part_of(PAIRS + j), lanes].T[:KEYS] for j in range(PAIRS)]
                values += [qkv[t, part_of(2 * PAIRS + j), lanes] for j in range(PAIRS)]
            bias = jnp.concatenate([ebias_s[...]] * BATCH, 1)
            chance, mixed = attend(keys, queries, values, bias)
            for i in range(BATCH):
                lanes = slice((first + i) * LANES, (first + i + 1) * LANES)
                own = slice(i * HEADS * LANES, (i + 1) * HEADS * LANES)
                p_s[half][t, first + i] = chance[:, own]
                o[t, :, lanes] = jnp.concatenate(mixed[i * PAIRS : (i + 1) * PAIRS], 0)
            yield
        x1 = x0 + packed(mul(wn_s[0, :, 3 * WIDTH : 4 * WIDTH], o[t]))
        x1_s[half][t] = x1
        yield
        h = norm_low(x1, inverse_rms(x1), gain(1, WIDE))
        for j in range(2):
            part = slice(j * FF // 2, (j + 1) * FF // 2)
            lifted = mul(wt_s[0, MIXW + j * FF // 2 : MIXW + (j + 1) * FF // 2, :], h)
            r[t, part, :] = jnp.maximum(lifted, 0.0).astype(bf16)
        yield
        x2 = x1 + mul(wn_s[0, :, MIXW + FF :], r[t])
        put_wide(x2_s, c, x2)
        e = norm_low(x2, inverse_rms(x2), gain(2, WIDE))
        yield
        for j in range(2):
            part = slice(j * WIDTH, (j + 1) * WIDTH)
            mem_s[half][t, part, :] = mul(
                wt_s[0, 4 * WIDTH + j * WIDTH : 4 * WIDTH + (j + 1) * WIDTH, :], e
            ).astype(bf16)
        yield

    attention = GROUP // BATCH
    pairs = chunks // 2

    def early_at(place, places):
        return [
            functools.partial(early_step, place + places * t)
            if place + places * t <= depth
            else None
            for t in range(pairs)
        ]

    def encode(t, carry):
        at_time(t, early_at(0, 3))

        def point(number):
            if number == attention // 2:
                pl.when(t == 0)(rest_passes)
                at_time(t, early_at(1, 3))
            if number == attention + 2:
                pl.when(t == 0)(rest_arrives)
                at_time(t, early_at(2, 3))

        lockstep([encode_steps(t, 0), encode_steps(t, 1)], point)
        return carry

    def put_wide(ref, c, value):
        for i in range(COLUMNS):
            ref[pl.ds(pl.multiple_of((COLUMNS * c + i) * D, D), D), :] = value[
                :, i * LANES : (i + 1) * LANES
            ]

    def get_wide(ref, c):
        return jnp.concatenate(
            [ref[pl.ds(pl.multiple_of((COLUMNS * c + i) * D, D), D), :] for i in range(COLUMNS)], 1
        )

    lax.fori_loop(0, pairs, encode, 0)
    for j in range(3 * pairs, depth + 1):
        early_step(j)
    out_stat_ref[...] = stat_s[depth, :8, :]

    def put_blocks(first, value):
        for index in range(value.shape[1] // LANES):
            block = first + index
            part = value[:, index * LANES : (index + 1) * LANES].astype(bf16)
            if block < FIRST // LANES:
                first_s[1, block * D : (block + 1) * D, :] = part
            else:
                block -= FIRST // LANES
                rest_s[1, block * D : (block + 1) * D, :] = part

    def add_blocks(first, value):
        for index in range(value.shape[1] // LANES):
            g0_s[first + index] += value[:, index * LANES : (index + 1) * LANES]

    start = onehot(start_ids, CODES)
    both = mul(ext_s[:, :CODES], start)
    y0 = both[:D] + both[D:]
    inverse0 = inverse_rms(y0)
    h0 = norm_low(y0, inverse0, gain(3, LANES))
    dz_s[:, :LANES] = mul(wt_s[1, : 3 * WIDTH, :], h0).astype(bf16)
    both = mul(mul_t(eye, h0).astype(bf16), wn_s[1, :, WIDTH : 3 * WIDTH]).astype(bf16)
    self_chance, mixed = attend(
        [both[:, part_of(j)] for j in range(PAIRS)],
        [dz_s[part_of(j), :LANES] for j in range(PAIRS)],
        [dz_s[part_of(2 * PAIRS + j), :LANES] for j in range(PAIRS)],
        dbias_s[...],
    )
    self_values = both[:, WIDTH:]
    self_mixed = jnp.concatenate(mixed, 0)
    y1 = y0 + mul(wn_s[1, :, 3 * WIDTH : 4 * WIDTH], self_mixed)
    inverse1 = inverse_rms(y1)
    h1 = norm_low(y1, inverse1, gain(4, LANES))
    cross_s[...] = mul(wt_s[1, 4 * WIDTH : 5 * WIDTH, :], h1).astype(bf16)

    def spreader(g, turned):
        shape = (LANES, 32 * GROUP) if turned else (32 * GROUP, LANES)
        row, token = iota(shape, 1 if turned else 0), iota(shape, 0 if turned else 1)
        hit = token == 4 * GROUP * g + 4 * (row >> 5) + (row & 3)
        return jnp.where(hit, 1.0, 0.0).astype(bf16)

    def rows_of(g, table):
        rows = mul_t(spreader(g, False), table)
        mask = (iota(rows.shape, 1) >> 6) == ((iota(rows.shape, 0) & 31) >> 2)
        return jnp.where(mask, rows, 0.0).astype(bf16)

    def head_mask(shape):
        return (iota(shape, 0) >> 6) == ((iota(shape, 1) & 31) >> 2)

    def rows_t_of(g, table):
        rows = mul(table, spreader(g, True))
        return jnp.where(head_mask(rows.shape), rows, 0.0).astype(bf16)

    def gather_rows(ref):
        total = jnp.zeros((WIDTH, LANES), f32)
        for g in range(chunks):
            total = total + mul(ref[g % 2][g // 2], spreader(g, False))
        return total.astype(bf16)

    def blocks_of(table):
        rows = []
        for i in range(GROUP):
            part = table[32 * i : 32 * i + 32]
            column, shift = divmod(PACK * i, LANES)
            part = turn(part, shift)
            lane = iota(part.shape, 1)
            zero = jnp.zeros_like(part)
            columns = [zero] * COLUMNS
            columns[column] = jnp.where(lane >= shift, part, 0.0)
            if shift > LANES - PACK:
                columns[column + 1] = jnp.where(lane < shift, part, 0.0)
            rows.append(jnp.concatenate(columns, 1))
        return jnp.concatenate(rows, 0).astype(bf16)

    def row_products(rows, keys):
        both = mul(rows, keys)
        parts = []
        for i in range(GROUP):
            own = both[32 * i : 32 * i + 32]
            column, shift = divmod(PACK * i, LANES)
            part = turn(own[:, column * LANES : (column + 1) * LANES], -shift)
            if shift > LANES - PACK:
                after = turn(own[:, (column + 1) * LANES : (column + 2) * LANES], -shift)
                part = jnp.where(iota(part.shape, 1) < LANES - shift, part, after)
            parts.append(part)
        return jnp.concatenate(parts, 0)

    def cross_steps(t, half):
        g = 2 * t + half
        queries = rows_of(g, cross_s[...])
        yield
        scores = row_products(queries, mem_s[half][t, :WIDTH, :])
        scores = jnp.where(iota(scores.shape, 1) < HIST_LEN, scores, -1e30)
        chance = jnp.exp(scores - jnp.max(scores, axis=1, keepdims=True))
        chance = chance * (1.0 / jnp.sum(chance, axis=1, keepdims=True))
        pc_s[half][t] = chance
        yield
        mixed = mul_t(mem_s[half][t, WIDTH:, :], blocks_of(chance))
        oc_s[half][t] = jnp.where(head_mask(mixed.shape), mixed, 0.0).astype(bf16)
        yield

    def cross(t, carry):
        lockstep([cross_steps(t, 0), cross_steps(t, 1)])
        return carry

    lax.fori_loop(0, pairs, cross, 0)
    cross_mixed = gather_rows(oc_s)
    y2 = y1 + mul(wn_s[1, :, 5 * WIDTH : 6 * WIDTH], cross_mixed)
    inverse2 = inverse_rms(y2)
    h2 = norm_low(y2, inverse2, gain(5, LANES))
    lifted = mul(wt_s[1, MIXW : MIXW + FF, :], h2)
    active = jnp.maximum(lifted, 0.0).astype(bf16)
    y3 = y2 + mul(wn_s[1, :, MIXW + FF :], active)
    inverse3 = inverse_rms(y3)
    final = norm_low(y3, inverse3, gain(6, LANES))
    logits = mul(codes_s[...], final)
    top = jnp.max(logits, axis=0, keepdims=True)
    log_total = top + jnp.log(jnp.sum(jnp.exp(logits - top), axis=0, keepdims=True))
    match = iota(logits.shape, 0) == goal
    picked = jnp.sum(jnp.where(match, logits, 0.0), axis=0, keepdims=True)
    weight = jnp.zeros((1, LANES), f32)
    for d in range(DOMAINS):
        share = 1.0 / (DOMAINS * jnp.maximum(stat_s[depth, 8 + d : 9 + d, :], 1.0))
        weight = weight + jnp.where(domain == d, share, 0.0)
    loss = jnp.sum(weight * (log_total - picked), axis=1, keepdims=True)
    back_logits = (
        weight * (jnp.exp(logits - log_total) - jnp.where(match, 1.0, 0.0))
    ).astype(bf16)
    back_final = mul(ext_s[:D, :CODES], back_logits)
    table_grad = mul_t(back_logits, final)
    back, gain_grad = norm_back(y3, inverse3, gain(6, LANES), back_final)
    ggain_s[6] = gain_grad
    low = back.astype(bf16)
    put_blocks(26, mul_t(low, active))
    back_lifted = jnp.where(lifted > 0, mul(wt_s[1, MIXW + FF :, :], low), 0.0).astype(bf16)
    put_blocks(18, mul_t(h2, back_lifted))
    more, gain_grad = norm_back(
        y2, inverse2, gain(5, LANES), mul(wn_s[1, :, MIXW : MIXW + FF], back_lifted)
    )
    ggain_s[5] = gain_grad
    back = back + more
    low = back.astype(bf16)
    put_blocks(15, mul_t(low, cross_mixed))
    cross_back_s[...] = mul(wt_s[1, 5 * WIDTH : 6 * WIDTH, :], low).astype(bf16)

    def cross_back_steps(t, half):
        g = 2 * t + half
        memory = mem_s[half]
        mixed_rows = rows_of(g, cross_back_s[...])
        queries_t = rows_t_of(g, cross_s[...])
        mixed_t = rows_t_of(g, cross_back_s[...])
        yield
        back_chance = row_products(mixed_rows, memory[t, WIDTH:, :])
        back_chance = jnp.where(iota(back_chance.shape, 1) < HIST_LEN, back_chance, 0.0)
        chance = pc_s[half][t]
        inner = jnp.sum(back_chance * chance, axis=1, keepdims=True)
        yield
        spread = blocks_of(chance * (back_chance - inner))
        total = mul_t(memory[t, :WIDTH, :], spread)
        oc_s[half][t] = jnp.where(head_mask(total.shape), total, 0.0).astype(bf16)
        yield
        memory[t, :WIDTH, :] = mul(queries_t, spread).astype(bf16)
        memory[t, WIDTH:, :] = mul(mixed_t, blocks_of(chance)).astype(bf16)
        yield

    def cross_back(t, carry):
        lockstep([cross_back_steps(t, 0), cross_back_steps(t, 1)])
        return carry

    lax.fori_loop(0, pairs, cross_back, 0)
    back_query = gather_rows(oc_s)
    put_blocks(12, mul_t(h1, back_query) * HEAD_DIM**-0.5)
    more, gain_grad = norm_back(
        y1, inverse1, gain(4, LANES), mul(wn_s[1, :, 4 * WIDTH : 5 * WIDTH], back_query)
    )
    ggain_s[4] = gain_grad
    back = back + more
    low = back.astype(bf16)
    put_blocks(9, mul_t(low, self_mixed))
    back_mixed = mul(wt_s[1, 3 * WIDTH : 4 * WIDTH, :], low).astype(bf16)
    *back_parts, self_scores = attend_back(
        [dz_s[part_of(PAIRS + j), :LANES] for j in range(PAIRS)],
        [dz_s[part_of(j), :LANES] for j in range(PAIRS)],
        [self_values[:, part_of(j)] for j in range(PAIRS)],
        [back_mixed[part_of(j)] for j in range(PAIRS)],
        self_chance,
    )
    dz_s[:, LANES:] = jnp.concatenate([x for part in back_parts for x in part], 0)
    put_blocks(0, mul_t(h0, dz_s[:WIDTH, LANES : 2 * LANES]) * HEAD_DIM**-0.5)
    put_blocks(3, mul_t(h0, dz_s[WIDTH:, LANES : 2 * LANES]))
    more, gain_grad = norm_back(
        y0, inverse0, gain(3, LANES), mul(wn_s[1, :, : 3 * WIDTH], dz_s[:, LANES : 2 * LANES])
    )
    ggain_s[3] = gain_grad
    back = back + more
    ge_s[:CODES, :] = table_grad + mul_t(start, back.astype(bf16))
    ge_s[CODES:, :] = jnp.zeros((n, D), f32)
    rows_s[...] = jnp.zeros_like(rows_s)
    for head in range(HEADS):
        lanes = slice(head * LANES, (head + 1) * LANES)
        for b in range(LEVELS):
            hit = jnp.where(offset == b, self_scores[:, lanes], 0.0)
            rows_s[head, BUCKETS + b : BUCKETS + b + 1, :] = jnp.sum(hit, axis=0, keepdims=True)

    def reducing(buffer, kept, held, stages):
        steps, at = [], 0
        for k, stage in enumerate(stages):
            rows, left = held[k], held[k + 1]
            side = side_of(stage)
            if left < rows:
                source = buffer.at[span(at + (1 - side) * left, left)]
                at = at + side * left
            else:
                source = buffer.at[span(at, rows)]
            steps.append((remote(source, kept[k], stage), at, left))
        return steps, at, held

    def begin(steps, k):
        steps[k][0].start()

    def finish(steps, buffer, kept, k):
        copy, at, left = steps[k]
        copy.wait()
        place = span(at, left)
        total = buffer[place, :].astype(f32) + kept[k][...].astype(f32)
        buffer[place, :] = total.astype(bf16)

    flat_depth = depth - 1
    held_rest, held_first, held_codes = shares(dp, REST), shares(dp, FIRST), shares(dp, CODES, 1)
    land, rest = {}, lands
    for name, number in (
        ("rest0", flat_depth),
        ("rest1", flat_depth),
        ("first1", flat_depth),
        ("first0", len(far)),
        ("codes", len(far)),
    ):
        land[name], rest = rest[:number], rest[number:]
    land_rest, land_first = rest
    rest1 = reducing(rest_s.at[1], land["rest1"], held_rest, order[:-1])
    first1 = reducing(first_s.at[1], land["first1"], held_first, order[:-1])
    rest0 = reducing(rest_s.at[0], land["rest0"], held_rest, order[:-1])
    first0 = reducing(first_s.at[0], land["first0"], held_first, far)
    codes = reducing(codes_s, land["codes"], held_codes, code_far)

    def step1(k):
        if k > 0:
            finish(rest1[0], rest_s.at[1], land["rest1"], k - 1)
            finish(first1[0], first_s.at[1], land["first1"], k - 1)
        if k < flat_depth:
            begin(rest1[0], k)
            begin(first1[0], k)

    def crossing(buffer, target, at, rows):
        source = buffer.at[1 - section, span(at, rows)]
        return remote(source, target, across)

    cross_rest = crossing(rest_s, land_rest, rest1[1], rest1[2][-1])
    cross_first = crossing(first_s, land_first, first1[1], first1[2][-1])

    def settle(copy, buffer, landed, at, rows, base):
        copy.wait()
        value = (buffer[section, span(at, rows), :].astype(f32) + landed[...].astype(f32)).astype(
            bf16
        )
        out_ref[span(base + at, rows), :] = value
        value = value.astype(f32)
        return jnp.sum(value * value, axis=0, keepdims=True)

    def gathering(base, at, held):
        steps = []
        for k in reversed(range(flat_depth)):
            rows, left = held[k], held[k + 1]
            if left < rows:
                place = out_ref.at[span(base + at, left)]
                steps.append(remote(place, place, order[k]))
                at = at - side_of(order[k]) * left
            else:
                steps.append(None)
        return steps

    gather_rest = gathering(0, rest1[1], rest1[2])

    def step0(k):
        if k > 0 and k <= flat_depth:
            finish(rest0[0], rest_s.at[0], land["rest0"], k - 1)
        if k < flat_depth:
            begin(rest0[0], k)
        if k == flat_depth:
            cross_rest.start()
        if k == flat_depth + 1:
            squares = settle(cross_rest, rest_s, land_rest, rest1[1], rest1[2][-1], 0)
            squares_s[0:1, :] = squares / (dp * rest1[2][-1] // REST)
        if k > flat_depth + 1 and gather_rest[k - flat_depth - 2] is not None:
            gather_rest[k - flat_depth - 2].wait()
        if flat_depth < k < 2 * flat_depth + 1 and gather_rest[k - flat_depth - 1] is not None:
            gather_rest[k - flat_depth - 1].start()

    g0_s[...] = jnp.zeros_like(g0_s)
    gbias_s[...] = jnp.zeros_like(gbias_s)
    for g in range(3):
        ggain_s[g] = jnp.zeros((D, LANES), f32)

    def fold(x):
        return sum(x[:, i * LANES : (i + 1) * LANES] for i in range(COLUMNS))

    def rest_steps(t, half):
        c = 2 * t + half
        r = r_s[half]
        x2 = get_wide(x2_s, c)
        inverse = inverse_rms(x2)
        back_memory = mem_s[half][t]
        add_blocks(12, mul_t(norm_low(x2, inverse, gain(2, WIDE)), back_memory))
        back_normed = mul(wn_s[0, :, 4 * WIDTH : 6 * WIDTH], back_memory)
        yield
        back, gain_grad = norm_back(x2, inverse, gain(2, WIDE), back_normed)
        ggain_s[2] += fold(gain_grad)
        low = back.astype(bf16)
        yield
        add_blocks(26, mul_t(low, r[t]))
        for j in range(4):
            part = slice(j * FF // 4, (j + 1) * FF // 4)
            back_active = mul(wt_s[0, MIXW + FF + part.start : MIXW + FF + part.stop, :], low)
            live = r[t, part, :].astype(f32) > 0
            r[t, part, :] = jnp.where(live, back_active, 0.0).astype(bf16)
        yield
        x1 = x1_s[half][t]
        inverse = inverse_rms(x1)
        add_blocks(18, mul_t(norm_low(x1, inverse, gain(1, WIDE)), r[t]))
        back_normed = mul(wn_s[0, :, MIXW : MIXW + FF], r[t])
        yield
        more, gain_grad = norm_back(x1, inverse, gain(1, WIDE), back_normed)
        ggain_s[1] += fold(gain_grad)
        put_wide(x2_s, c, back + more)
        yield

    places1 = {0: 0, 1: 1, 4: 2}
    places0 = {0: 0, 1: 1, 3: 2, 4: 3, 5: 4, 6: 5, 7: 6, 8: 7}
    steps0 = 2 * flat_depth + 2

    def placed(places, step, place, each):
        return [
            functools.partial(step, places[place + each * t])
            if place + each * t in places
            else None
            for t in range(pairs)
        ]

    def back_rest(t, carry):
        at_time(t, placed(places1, step1, 0, 3))

        def point(number):
            if number in (1, 3):
                at_time(t, placed(places1, step1, (number + 1) // 2, 3))

        lockstep([rest_steps(t, 0), rest_steps(t, 1)], point)
        return carry

    lax.fori_loop(0, pairs, back_rest, 0)
    def cast_rest(block, carry):
        place = pl.ds(pl.multiple_of(block * D, D), D)
        rest_s[0, place, :] = g0_s[FIRST // D + block].astype(bf16)
        return carry

    lax.fori_loop(0, REST // D, cast_rest, 0, unroll=2)
    def first_steps(t, half):
        c = 2 * t + half
        qkv, o, dqkv = qkv_s[half], o_s[half], dqkv_s[half]
        back = get_wide(x2_s, c)
        lane = iota((D, LANES), 1)
        low = [jnp.where(lane < PACK, part, 0.0).astype(bf16) for part in unpack(back)]
        low = jnp.concatenate(low, 1)
        yield
        add_blocks(9, mul_t(low, o[t]))
        o[t] = mul(wt_s[0, 3 * WIDTH : 4 * WIDTH, :], low).astype(bf16)
        yield
        for first in range(0, GROUP, BATCH):
            queries, keys, values, backs = [], [], [], []
            for i in range(first, first + BATCH):
                lanes = slice(i * LANES, (i + 1) * LANES)
                queries += [qkv[t, part_of(j), lanes] for j in range(PAIRS)]
                keys += [qkv[t, part_of(PAIRS + j), lanes] for j in range(PAIRS)]
                values += [qkv[t, part_of(2 * PAIRS + j), lanes].T[:KEYS] for j in range(PAIRS)]
                backs += [o[t, part_of(j), lanes] for j in range(PAIRS)]
            chance = [p_s[half][t, first + i] for i in range(BATCH)]
            *results, scores = attend_back(
                keys, queries, values, backs, jnp.concatenate(chance, 1)
            )
            for i in range(BATCH):
                lanes = slice((first + i) * LANES, (first + i + 1) * LANES)
                own = slice(i * PAIRS, (i + 1) * PAIRS)
                dqkv[:, lanes] = jnp.concatenate([x for part in results for x in part[own]], 0)
            width = HEADS * LANES
            gbias_s[...] += sum(scores[:, i * width : (i + 1) * width] for i in range(BATCH))
            yield
        x0 = x0_s[c]
        inverse = inverse_rms(x0)
        add_blocks(0, mul_t(spread_low(x0 * inverse * gain(0, WIDE)), dqkv[...]))
        back_normed = packed(mul(wn_s[0, :, : 3 * WIDTH], dqkv[...]))
        yield
        more, gain_grad = norm_back(x0, inverse, gain(0, WIDE), back_normed)
        ggain_s[0] += fold(gain_grad)
        find(c)
        ge_s[...] += mul_t(hot_s[...], (back + more).astype(bf16))
        yield

    def both_steps(k):
        if k == 0:
            step1(3)
        if k == 1:
            for j in range(4, flat_depth + 1):
                step1(j)
        step0(k)

    def back_first(t, carry):
        at_time(t, placed(places0, both_steps, 0, 5))

        def point(number):
            place = {1: 1, attention // 2 + 1: 2, attention + 1: 3, attention + 2: 4}.get(number)
            if place is not None:
                at_time(t, placed(places0, both_steps, place, 5))

        lockstep([first_steps(t, 0), first_steps(t, 1)], point)
        return carry

    lax.fori_loop(0, pairs, back_first, 0)

    def cast_first(block, carry):
        place = pl.ds(pl.multiple_of(block * D, D), D)
        factor = jnp.where(block < 3, scale, 1.0)
        first_s[0, place, :] = (g0_s[block] * factor).astype(bf16)
        return carry

    lax.fori_loop(0, FIRST // D, cast_first, 0, unroll=2)
    codes_s[...] = ge_s[:CODES, :].astype(bf16)
    begin(first0[0], 0)
    begin(codes[0], 0)
    code_size = held_codes[-1]
    own_slot_s[code_size : code_size + n, :] = ge_s[CODES:, :].astype(bf16)
    late = list(range(8, steps0))
    if late:
        step0(late.pop(0))

    def sum_small():
        ones = jnp.ones((8, LANES), f32)
        small_s[0, 8:16, :] = jnp.zeros((8, LANES), f32)
        for g in range(7):
            small_s[0, g : g + 1, :] = mul_exact_t(ones, ggain_s[g])[:1]
        small_s[0, 7:8, :] = jnp.broadcast_to(loss, (1, LANES))

        def bucket_sums(b, carry):
            for head in range(HEADS):
                lanes = slice(head * LANES, (head + 1) * LANES)
                hit = jnp.where(buckets == b, gbias_s[:, lanes], 0.0)
                rows_s[head, pl.ds(b, 1), :] = jnp.sum(hit, axis=0, keepdims=True)
            return carry

        lax.fori_loop(0, BUCKETS, bucket_sums, 0, unroll=2)
        for head in range(HEADS):
            sums = mul_exact_t(ones, rows_s[head])
            small_s[0, 8 + head : 9 + head, : 2 * BUCKETS] = sums[:1]

    for k in range(len(far)):
        finish(first0[0], first_s.at[0], land["first0"], k)
        finish(codes[0], codes_s, land["codes"], k)
        if k + 1 < len(far):
            begin(first0[0], k + 1)
            begin(codes[0], k + 1)
        if k == 0:
            sum_small()

    first_at, first_left = first0[1], held_first[len(far) + 1 :]
    codes_at, codes_left = codes[1], held_codes[len(far) + 1 :]
    size = first_left[-1]
    mine_first = first_at + shift_of(0, first_left)
    mine_codes = codes_at + shift_of(0, codes_left, code_near)
    inside, crossing_first, everyone = [], [], []
    for mask in masks:
        source = first_s.at[0, span(first_at + shift_of(mask, first_left), size)]
        copy = remote_to(source, near_first.at[mask], device_of(mask))
        (crossing_first if mask >> (NEAR - 1) else inside).append(copy)
    for mask in masks:
        source = codes_s.at[span(codes_at + shift_of(mask, codes_left, code_near), code_size)]
        everyone.append(remote_to(source, near_codes.at[mask], device_of(mask, code_near)))

    @pl.when(section == 0)
    def _():
        for copy in inside:
            copy.start()
        cross_first.start()

    @pl.when(section == 1)
    def _():
        for copy in crossing_first:
            copy.start()

    for copy in everyone:
        copy.start()
    for step in late:
        step0(step)
    for k, stage in enumerate(code_far):
        copy = remote(small_s.at[k], small_land.at[k], stage)
        copy.start()
        copy.wait()
        small_s[k + 1] = small_s[k] + small_land[k]
    rows = code_size + n
    own_slot_s[rows + 16 :, :] = high_low(small_s[len(far)], 2)

    def keep_first(value):
        value = value.astype(bf16)
        out_ref[span(REST + mine_first, size), :] = value
        value = value.astype(f32)
        squares = jnp.sum(value * value, axis=0, keepdims=True)
        squares_s[1:2, :] = squares / (dp * size // FIRST)

    @pl.when(section == 0)
    def _():
        for copy in inside:
            copy.wait()
        for copy in crossing_first:
            copy.wait_recv()
        cross_first.wait_send()
        value = first_s[0, span(mine_first, size), :].astype(f32)
        for mask in masks:
            value = value + near_first[mask].astype(f32)
        keep_first(value)

    @pl.when(section == 1)
    def _():
        for copy in crossing_first:
            copy.wait_send()
        cross_first.wait_recv()
        value = first_s[1, span(mine_first, size), :].astype(f32)
        keep_first(value + land_first[...].astype(f32))

    place = out_ref.at[span(REST + mine_first, size)]
    copies = [
        remote_to(place, place, device_of(mask)) for mask in masks if not mask >> (NEAR - 1)
    ]
    for copy in copies:
        copy.start()
    for copy in everyone:
        copy.wait()
    value = codes_s[span(mine_codes, code_size), :].astype(f32)
    for mask in masks:
        value = value + near_codes[mask].astype(f32)
    value = value.astype(bf16)
    own_slot_s[:code_size, :] = value
    value = value.astype(f32)
    squares = jnp.sum(value * value, axis=0, keepdims=True)
    squares_s[2:3, :] = squares / (2 * dp * code_size // CODES)
    squares_s[3:, :] = jnp.zeros((5, LANES), f32)
    own_slot_s[rows : rows + 16, :] = high_low(squares_s[...], 2)
    kept_slot = out_slot_ref.at[slot]
    store_slot = pltpu.make_async_copy(own_slot_s, kept_slot, local_sems.at[BLOCKS + 2])
    store_slot.start()
    slots_out = [remote_to(own_slot_s, kept_slot, device_of(mask, code_near)) for mask in masks]
    for copy in slots_out:
        copy.start()
    store_slot.wait()
    for copy in copies + slots_out:
        copy.wait()
    for j, k in enumerate(reversed(range(len(far)))):
        copies = []
        if held_first[k + 1] < held_first[k]:
            place = out_ref.at[span(REST + first_at, held_first[k + 1])]
            copies.append(remote(place, place, far[k]))
            first_at = first_at - side_of(far[k]) * held_first[k + 1]
        slots = 2 ** (NEAR + j)
        held = out_slot_ref.at[pl.ds(lax.div(slot, slots) * slots, slots), pl.ds(0, rows + 16)]
        copies.append(remote(held, held, code_far[k]))
        for copy in copies:
            copy.start()
        for copy in copies:
            copy.wait()


def gradients(codes, users, targets, domains, bias, gains, mixer, feed, embedding, dp):
    n = users.shape[0] // 2
    chunks = n // GROUP
    order = stages(dp)
    depth = len(order)
    devices = 2 * dp
    vmem = pl.BlockSpec(memory_space=pltpu.VMEM)
    smem = pl.BlockSpec(memory_space=pltpu.SMEM)
    hbm = pl.BlockSpec(memory_space=pl.ANY)
    stat = (16, LANES)
    held_rest, held_first, held_codes = shares(dp, REST), shares(dp, FIRST), shares(dp, CODES, 1)
    plane, far = depth - 1, depth - NEAR
    slot_rows = held_codes[-1] + n + 16 + 32
    sizes = [*held_rest[1:] * 2, *held_first[1:]]
    sizes += [*held_first[1 : far + 1], *held_codes[1 : far + 1], held_rest[-1], held_first[-1]]
    lands = [pltpu.VMEM((rows, D), bf16) for rows in sizes]
    copies = 128 + 16 * depth
    return pl.pallas_call(
        functools.partial(step_kernel, n, dp),
        out_shape=(
            jax.ShapeDtypeStruct((COLS, D), bf16),
            jax.ShapeDtypeStruct((devices, 8, LANES), jnp.int32),
            jax.ShapeDtypeStruct((devices, slot_rows, LANES), bf16),
            jax.ShapeDtypeStruct((8, LANES), f32),
        ),
        in_specs=[vmem, smem, vmem, vmem, vmem, smem, vmem, hbm, hbm, hbm],
        out_specs=(vmem, hbm, hbm, vmem),
        scratch_shapes=[pltpu.VMEM((chunks, D, WIDE), f32)]
        + [
            pltpu.VMEM(shape, dtype)
            for shape, dtype in (
                ((chunks // 2, D, WIDE), f32),
                ((chunks // 2, 3 * WIDTH, SPAN), bf16),
                ((chunks // 2, GROUP, KEYS, HEADS * LANES), bf16),
                ((chunks // 2, WIDTH, SPAN), bf16),
                ((chunks // 2, FF, WIDE), bf16),
                ((chunks // 2, 2 * WIDTH, WIDE), bf16),
                ((3 * WIDTH, SPAN), bf16),
                ((chunks // 2, 32 * GROUP, LANES), f32),
                ((chunks // 2, WIDTH, 32 * GROUP), bf16),
            )
            for _ in range(2)
        ]
        + [
            pltpu.VMEM((chunks * COLUMNS * D, LANES), f32),
            pltpu.VMEM((3 * WIDTH, 2 * LANES), bf16),
            pltpu.VMEM((2, D, COLS), bf16),
            pltpu.VMEM((2, COLS, D), bf16),
            pltpu.VMEM((2 * D, CODES + n), bf16),
            pltpu.VMEM((7, D, LANES), f32),
            pltpu.VMEM((KEYS, HEADS * LANES), f32),
            pltpu.VMEM((LANES, HEADS * LANES), f32),
            pltpu.VMEM((BLOCKS, D, LANES), f32),
            pltpu.VMEM((CODES + n, D), f32),
            pltpu.VMEM((KEYS, HEADS * LANES), f32),
            pltpu.VMEM((7, D, LANES), f32),
            pltpu.VMEM((HEADS, 2 * BUCKETS, LANES), f32),
            pltpu.VMEM((n, D), f32),
            pltpu.VMEM((n, LANES), jnp.int32),
            pltpu.VMEM((WIDTH, LANES), bf16),
            pltpu.VMEM((WIDTH, LANES), bf16),
            pltpu.VMEM((2, REST, D), bf16),
            pltpu.VMEM((2, FIRST, D), bf16),
            pltpu.VMEM((CODES, D), bf16),
            pltpu.VMEM((8, LANES), jnp.int32),
            pltpu.VMEM((slot_rows, LANES), bf16),
            pltpu.VMEM((8, LANES), f32),
            pltpu.VMEM((8, WIDE), jnp.int32),
            pltpu.VMEM((CODES + n, WIDE), bf16),
            pltpu.VMEM((depth + 1,) + stat, f32),
            pltpu.VMEM((depth,) + stat, f32),
            pltpu.VMEM((far + 1, 16, LANES), f32),
            pltpu.VMEM((far, 16, LANES), f32),
            pltpu.VMEM((2**NEAR, held_first[-1], D), bf16),
            pltpu.VMEM((2**NEAR, held_codes[-1], D), bf16),
            pltpu.SemaphoreType.DMA((BLOCKS + 3,)),
            pltpu.SemaphoreType.DMA((copies,)),
            pltpu.SemaphoreType.DMA((copies,)),
        ]
        + lands,
        compiler_params=pltpu.CompilerParams(
            collective_id=0, has_side_effects=True, vmem_limit_bytes=127 * 2**19
        ),
        name="gradients",
    )(codes, users, users.reshape(1, -1), targets, domains, bias, gains, mixer, feed, embedding)


def adam(weight, moment, square, slope, rate, decay):
    moment = beta_one * moment + (1 - beta_one) * slope
    square = beta_two * square + (1 - beta_two) * slope * slope
    unbiased_moment = moment * (1 / (1 - beta_one**STEP))
    unbiased_square = square * (1 / (1 - beta_two**STEP))
    root = unbiased_square * lax.rsqrt(unbiased_square)
    divisor = root + adam_eps
    inverse = pl.reciprocal(divisor, approx=True)
    inverse = inverse * (2.0 - divisor * inverse)
    step = unbiased_moment * inverse + decay * weight
    return weight - rate * step, moment, square


def update_kernel(n, dp, *refs):
    parts_in, big_in, small_in, refs = refs[:4], refs[4:13], refs[13:19], refs[19:]
    loss_ref, norm_ref, section_ref, hist_ref = refs[:4]
    big_out, small_out, low_out, refs = refs[4:13], refs[13:19], refs[19:22], refs[22:]
    parts, hold, low_hold = refs[:4], refs[4:13], refs[13:16]
    user_grad, code_grad, part_sems, in_sems, out_sems = refs[16:]
    grad_ref, ids_ref, slot_ref, stat_ref = parts
    arrivals = [pltpu.make_async_copy(parts_in[i], parts[i], part_sems.at[i]) for i in range(4)]
    loads = [pltpu.make_async_copy(big_in[i], hold[i], in_sems.at[i]) for i in range(9)]
    for load in arrivals[1:] + arrivals[:1] + loads:
        load.start()
    for arrival in arrivals:
        arrival.wait()
    devices = slot_ref.shape[0]
    held = shares(dp, CODES, 1)
    code_size = held[-1]

    users = user_grad.shape[0]
    fit = LANES // n
    each = min(1024 // n, devices)
    span_rows = each * n
    user_grad[...] = jnp.zeros_like(user_grad)

    def scatter(part, carry):
        first = part * each
        rows = [slot_ref[first + i, code_size : code_size + n, :] for i in range(each)]
        rows = jnp.concatenate(rows, 0)
        lanes = []
        for group in range(each // fit):
            lanes.append(
                sum(ids_ref[first + group * fit + other, :1, :] for other in range(fit))
            )
        ids = jnp.concatenate(lanes, 1)

        def block_rows(block, carry):
            place = pl.ds(pl.multiple_of(block * USER_ROWS, 8), USER_ROWS)
            hit = iota((USER_ROWS, span_rows), 0) + block * USER_ROWS == ids
            user_grad[place, :] += mul(jnp.where(hit, 1.0, 0.0).astype(bf16), rows)
            return carry

        lax.fori_loop(0, users // USER_ROWS, block_rows, 0)
        return carry

    lax.fori_loop(0, devices // each, scatter, 0)

    def total(x):
        return jnp.sum(jnp.sum(x, axis=0, keepdims=True), axis=1, keepdims=True)

    route = code_stages(dp)
    depth = len(route)
    near = 2**NEAR
    top = code_size + n

    def squares_of(slot):
        value = slot_ref[slot, top : top + 16, :].astype(f32)
        return value[:8] + value[8:]

    def add(i, sums):
        first = 2 * near * i
        return tuple(
            total + sum(squares_of(first + side * near + j) for j in range(near))
            for side, total in enumerate(sums)
        )

    zero = jnp.zeros((8, LANES), f32)
    even, odd = lax.fori_loop(0, devices // (2 * near), add, (zero, zero))
    section_squares = [total(x[0:1] + x[1:2]) for x in (even, odd)]
    rest = total(even[2:3] + odd[2:3])
    first = 0
    for k, stage in enumerate(route[:-NEAR]):
        first = first + side_of(stage) * 2 ** (depth - 1 - k)
    small = jnp.zeros((16, LANES), f32)
    for i in range(near):
        value = slot_ref[first + i, top + 16 :, :].astype(f32)
        small = small + (value[:16] + value[16:])
    for slot in range(devices):
        at, kept = 0, True
        for k in range(depth):
            if slot >> (depth - 1 - k) & 1:
                kept = kept and held[k + 1] < held[k]
                at += held[k + 1]
        if kept:
            code_grad[at : at + code_size, :] = slot_ref[slot, :code_size, :]
    user_values = user_grad[...]
    rest = rest + total(user_values * user_values)
    lane, line = iota(small.shape, 1), iota(small.shape, 0)
    counted = (line < 7) | ((line > 7) & (lane < 2 * BUCKETS))
    small_kept = jnp.where(counted, small, 0.0)
    rest = rest + total(small_kept * small_kept)
    norm = jnp.sqrt(section_squares[0] + section_squares[1] + rest)
    factor = jnp.minimum(1.0, clip_norm / (norm + 1e-06))
    loss_ref[0] = small[7, 0]
    norm_ref[0] = norm[0, 0]
    for s in range(2):
        section_ref[s] = jnp.sqrt(section_squares[s])[0, 0]
    for row in range(8):
        lanes = slice((row % 2) * LANES, (row % 2 + 1) * LANES)
        hist_ref[row // 2 : row // 2 + 1, lanes] = stat_ref[row : row + 1, :]

    stores = []

    def store(kind, place):
        first = 3 * kind
        pieces = [(hold[first + i], big_out[first + i]) for i in range(3)]
        pieces.append((low_hold[kind], low_out[kind]))
        for source, target in pieces:
            copy = pltpu.make_async_copy(
                source.at[place], target.at[place], out_sems.at[len(stores)]
            )
            copy.start()
            stores.append(copy)

    def step(kind, place, slope):
        first = 3 * kind
        outs = adam(
            hold[first][place],
            hold[first + 1][place],
            hold[first + 2][place],
            factor * slope.astype(f32),
            rate_matrix,
            decay_matrix,
        )
        for i in range(3):
            hold[first + i][place] = outs[i]
        low_hold[kind][place] = outs[0].astype(bf16)

    def rows_from(start, count):
        return pl.ds(pl.multiple_of(start, 16), count)

    def columns(kind, first, count, row):
        def one(i, carry):
            lanes = pl.ds(pl.multiple_of((first + i) * LANES, LANES), LANES)
            step(kind, (0, slice(None), lanes), grad_ref[rows_from(row + i * D, D), :])
            return carry

        lax.fori_loop(0, count, one, 0)
        store(kind, (0, slice(None), slice(first * LANES, (first + count) * LANES)))

    def lines(first, count, size, source, row):
        def one(i, carry):
            place = (rows_from(first + i * size, size), slice(None))
            step(2, place, source[rows_from(row + i * size, size), :])
            return carry

        lax.fori_loop(0, count, one, 0)
        store(2, (slice(first, first + count * size), slice(None)))

    skip = FIRST // LANES
    for i in range(3):
        loads[i].wait()
    columns(0, 0, skip // 2, REST)
    columns(0, skip // 2, skip // 2, REST + skip // 2 * D)
    columns(0, skip, MIXW // LANES - skip, 0)
    for i in range(3, 6):
        loads[i].wait()
    for part in range(2):
        first = part * FF // LANES
        columns(1, first, FF // LANES, (MIXW // LANES - skip + first) * D)
    for i in range(6, 9):
        loads[i].wait()
    for part in range(2):
        lines(part * CODES // 2, 4, LANES, code_grad, part * CODES // 2)
    parts = users // USER_ROWS
    lines(CODES, parts // 2, USER_ROWS, user_grad, 0)
    done = parts // 2 * USER_ROWS
    lines(CODES + done, parts - parts // 2, USER_ROWS, user_grad, done)
    outs = adam(
        small_in[0][...], small_in[1][...], small_in[2][...], factor * small[:7], rate_gain, 0.0
    )
    for ref, value in zip(small_out[:3], outs):
        ref[...] = value
    for head in range(HEADS):
        for s in range(2):
            slope = factor * small[8 + head : 9 + head, s * BUCKETS : (s + 1) * BUCKETS]
            one = slice(s, s + 1)
            outs = adam(
                small_in[3][head, one, :],
                small_in[4][head, one, :],
                small_in[5][head, one, :],
                slope,
                rate_small,
                0.0,
            )
            for ref, value in zip(small_out[3:], outs):
                ref[head, one, :] = value

    for copy in stores:
        copy.wait()


def update(n, dp, reduced, mixers, feeds, embeds, gains, biases):
    vmem = pl.BlockSpec(memory_space=pltpu.VMEM)
    smem = pl.BlockSpec(memory_space=pltpu.SMEM)
    hbm = pl.BlockSpec(memory_space=pl.ANY)
    big = [*mixers, *feeds, *embeds]
    small = [*gains, *biases]
    low = [jax.ShapeDtypeStruct(x[0].shape, bf16) for x in (mixers, feeds, embeds)]
    users = embeds[0].shape[0] - CODES
    pieces = 4 * (6 + 4 + 4 + users // USER_ROWS)
    return pl.pallas_call(
        functools.partial(update_kernel, n, dp),
        out_shape=[
            jax.ShapeDtypeStruct((1,), f32),
            jax.ShapeDtypeStruct((1,), f32),
            jax.ShapeDtypeStruct((2,), f32),
            jax.ShapeDtypeStruct((LEVELS, CODEBOOK), f32),
        ]
        + [jax.ShapeDtypeStruct(x.shape, f32) for x in big + small]
        + low,
        in_specs=[hbm] * 13 + [vmem] * 6,
        out_specs=[smem] * 3 + [vmem] + [hbm] * 9 + [vmem] * 6 + [hbm] * 3,
        scratch_shapes=[pltpu.VMEM(x.shape, x.dtype) for x in reduced]
        + [pltpu.VMEM(x.shape, f32) for x in big]
        + [pltpu.VMEM(x.shape, bf16) for x in low]
        + [
            pltpu.VMEM((users, D), f32),
            pltpu.VMEM((CODES, D), bf16),
            pltpu.SemaphoreType.DMA((4,)),
            pltpu.SemaphoreType.DMA((9,)),
            pltpu.SemaphoreType.DMA((pieces,)),
        ],
        compiler_params=pltpu.CompilerParams(vmem_limit_bytes=62 * 2**20),
        name="update",
    )(*reduced, *big, *small)


def shards(
    history_codes,
    user_ids,
    targets,
    domains,
    mixer,
    mixer_moment,
    mixer_square,
    feed,
    feed_moment,
    feed_square,
    embedding,
    embedding_moment,
    embedding_square,
    gains,
    gains_moment,
    gains_square,
    position_bias,
    bias_moment,
    bias_square,
):
    def turned(table):
        return jnp.transpose(table, (2, 0, 1))

    biases = [turned(x) for x in (position_bias, bias_moment, bias_square)]
    reduced = gradients(
        history_codes,
        user_ids,
        targets.T,
        domains.reshape(1, -1),
        biases[0],
        gains,
        mixer,
        feed,
        embedding,
        lax.axis_size("dp"),
    )
    outs = update(
        history_codes.shape[0] // 2,
        lax.axis_size("dp"),
        reduced,
        (mixer, mixer_moment, mixer_square),
        (feed, feed_moment, feed_square),
        (embedding, embedding_moment, embedding_square),
        (gains, gains_moment, gains_square),
        biases,
    )
    loss, norm, sections, histograms = outs[:4]
    back = [jnp.transpose(x, (1, 2, 0)) for x in outs[16:19]]
    return (
        loss.reshape(()),
        norm.reshape(()),
        sections,
        histograms,
        *outs[4:16],
        *back,
        *outs[19:],
    )


def solution(mesh):
    by_dp, by_pipe, copied = P("dp"), P("pipe"), P()
    return jax.shard_map(
        shards,
        mesh=mesh,
        in_specs=(by_dp,) * 4 + (by_pipe,) * 6 + (copied,) * 9,
        out_specs=(copied,) * 4 + (by_pipe,) * 6 + (copied,) * 9 + (by_pipe,) * 2 + (copied,),
        check_vma=False,
    )
```
